32 devices in a mesh: pipe: 4 (over x, core), dp: 8 (over z, y).
Axes of the slice: x: 2, y: 2, z: 4, core: 2. Of those that a mesh axis runs over, the one named last changes fastest.
Arguments:
- series: bfloat16 [32, 336, 512], P(('pipe', 'dp')), may hold values from -6 to 6
- groups: int32 [32], P(('pipe', 'dp')), may hold values from 0 to 2
- cotangent: bfloat16 [32, 512, 512], P(('pipe', 'dp')), may hold values from -6 to 6
- embed_weight: float32 [624, 512], P(None, 'dp'), may hold values from -0.4375 to 0.4375
- embed_bias: float32 [3, 512], P(None, 'dp'), may hold values from -3 to 3
- qkv_weight: float32 [4, 1536, 512], P('pipe', 'dp'), may hold values from -0.25 to 0.25
- out_weight: float32 [4, 512, 512], P('pipe', 'dp'), may hold values from -2 to 2
- up_weight: float32 [4, 2048, 512], P('pipe', 'dp'), may hold values from -0.25 to 0.25
- down_weight: float32 [4, 512, 2048], P('pipe', 'dp'), may hold values from -0.125 to 0.125
- gains: float32 [4, 1024], P('pipe', 'dp'), may hold values from 0.25 to 1.75
- biases: float32 [4, 5120], P('pipe', 'dp'), may hold values from -2 to 2
Outputs:
- block_output: bfloat16 [32, 512, 512], P(('pipe', 'dp'))
- series_grad: float32 [32, 336, 512], P(('pipe', 'dp'))
- embed_weight_grad: float32 [624, 512], P(None, ('pipe', 'dp'))
- embed_bias_grad: float32 [3, 512], P(None, ('pipe', 'dp'))
- qkv_grad: float32 [4, 1536, 512], P('pipe', 'dp')
- out_grad: float32 [4, 512, 512], P('pipe', 'dp')
- up_grad: float32 [4, 2048, 512], P('pipe', 'dp')
- down_grad: float32 [4, 512, 2048], P('pipe', 'dp')
- gains_grad: float32 [4, 1024], P('pipe', 'dp')
- biases_grad: float32 [4, 5120], P('pipe', 'dp')
The draws below stay inside these ranges and needn't reach their ends.
All inputs are finite; a program needn't handle non-finite values.
Results may differ from the reference program's by a relative error of at most 0.019.
The reference program's roundings to bfloat16 on the way count: a program that leaves them out, or rounds other values in their place, can miss the bound.
Values may be sent and summed in bfloat16 or wider, within the bound.
A program may use at most 384 MiB of HBM per device.

```python
import math
import jax
import jax.numpy as jnp
from jax import lax

HEAD = 64
D = 512
FF = 2048
V = 512
L1 = 96
L2 = 192
L3 = 336
GROUPS = 3
WPD = 1
HIST = 336
LSUM = 624
SECTIONS = 4
WINDOWS = 32


def plant(drawn, stream_key, low, top_value):
    longest = drawn.shape.index(max(drawn.shape))
    spots = []
    for shift in (0, 1):
        where = [jax.random.randint(jax.random.fold_in(stream_key, axis), (), 0, length) for axis, length in enumerate(drawn.shape)]
        where[longest] = (where[longest] + shift) % drawn.shape[longest]
        spots.append(tuple(where))
    return drawn.at[spots[0]].set(low).at[spots[1]].set(top_value)


def shard_levels(rng, shape, shards, least, high):
    gain = 1.0
    for axis_at, parts in shards:
        steps = jax.random.uniform(jax.random.fold_in(jax.random.fold_in(rng, 6), axis_at), (parts,), jnp.float32, least / len(shards), high / len(shards))
        gain = gain * jnp.repeat(jnp.exp(steps), shape[axis_at] // parts).reshape((-1,) + (1,) * (len(shape) - 1 - axis_at))
    return gain


def scatter_about(own_key, extent, scale, bound, shards=(), kind=jnp.bfloat16):
    drawn = jax.random.normal(own_key, extent, jnp.float32) * scale
    if len(shards) > 0:
        drawn = shard_levels(own_key, extent, shards, -0.22, 0.18) * drawn
    return jnp.clip(drawn, min=-bound, max=bound).astype(kind)


def setup_inputs(seed: int = 0) -> dict:
    keys = jax.random.split(jax.random.key(seed), 12)
    return {
        "series": scatter_about(keys[0], (WINDOWS, HIST, V), 1.0, 6.0, ((0, 32),)),
        "groups": plant(jax.random.randint(keys[1], (WINDOWS,), 0, GROUPS), jax.random.fold_in(keys[1], 1), 0, GROUPS - 1).astype(jnp.int32),
        "cotangent": scatter_about(keys[2], (WINDOWS, V, D), 1.0, 6.0, ((0, 32),)),
        "embed_weight": scatter_about(keys[3], (LSUM, D), L2 ** -0.5, 0.4375, ((1, 8),), jnp.float32),
        "embed_bias": scatter_about(keys[4], (GROUPS, D), 0.5, 3.0, ((1, 8),), jnp.float32),
        "qkv_weight": scatter_about(keys[5], (SECTIONS, 3 * D, D), D ** -0.5, 0.25, ((0, 4), (1, 8)), jnp.float32),
        "out_weight": scatter_about(keys[6], (SECTIONS, D, D), (D // 64) ** -0.5, 2.0, ((0, 4), (1, 8)), jnp.float32),
        "up_weight": scatter_about(keys[7], (SECTIONS, FF, D), D ** -0.5, 0.25, ((0, 4), (1, 8)), jnp.float32),
        "down_weight": scatter_about(keys[8], (SECTIONS, D, FF), FF ** -0.5, 0.125, ((0, 4), (1, 8)), jnp.float32),
        "gains": jnp.clip(1.0 + 0.15 * jax.random.normal(keys[9], (SECTIONS, 2 * D), jnp.float32), 0.25, 1.75),
        "biases": scatter_about(keys[10], (SECTIONS, 6 * D + FF), 0.3, 2.0, ((0, 4), (1, 8)), jnp.float32),
    }


EXACT_PRECISION = lax.Precision.HIGHEST
NORM_EPS = 1e-05

@jax.custom_vjp
def low(v):
    return lax.optimization_barrier(v.astype(jnp.bfloat16)).astype(jnp.float32)

@jax.custom_vjp
def low_back(v):
    return v

def low_keep(v):
    return (low(v), None)

def low_pass(kept, grad):
    return (grad,)

def back_keep(v):
    return (v, None)

def back_low(kept, grad):
    return (low(grad),)
low.defvjp(low_keep, low_pass)
low_back.defvjp(back_keep, back_low)

def layer_norm(values, gain_vec, shift_vec):
    mean_val = lax.optimization_barrier(jnp.mean(values, axis=-1, keepdims=True))
    centred = values - mean_val
    variance = lax.optimization_barrier(jnp.mean(centred * centred, axis=-1, keepdims=True))
    return centred * lax.rsqrt(variance + NORM_EPS) * gain_vec + shift_vec

def project(values, matrix):
    return jnp.einsum('nvi,oi->nvo', values, matrix, precision=EXACT_PRECISION)

def unpack(gain_vec, bias_vec, model_width, hidden_width):
    middle = 4 * model_width + hidden_width
    return (bias_vec[:model_width], bias_vec[model_width:2 * model_width], bias_vec[2 * model_width:3 * model_width], gain_vec[:model_width], bias_vec[3 * model_width:4 * model_width], bias_vec[4 * model_width:middle], bias_vec[middle:middle + model_width], gain_vec[model_width:], bias_vec[middle + model_width:])

def embed_windows(block_series, group_row, embedding_matrix, embed_b):
    hist_len = block_series.shape[1]
    pieces = [block_series[:, hist_len - span_len:, :] for span_len in (L1, L2, L3)]
    expanded_hidden = jnp.concatenate(pieces, axis=1)
    segment = jnp.concatenate([jnp.full((span_len,), group_id, jnp.int32) for group_id, span_len in enumerate((L1, L2, L3))])
    chosen = (group_row[:, None] == segment[None, :]).astype(jnp.float32)
    expanded_hidden = expanded_hidden * chosen[:, :, None]
    group_pick = (group_row[:, None] == jnp.arange(GROUPS, dtype=jnp.int32)[None, :]).astype(jnp.float32)
    final_result = jnp.einsum('jiu,iz->juz', expanded_hidden, embedding_matrix, precision=EXACT_PRECISION)
    final_result = final_result + jnp.dot(group_pick, embed_b, precision=EXACT_PRECISION)[:, None, :]
    return low_back(low(final_result))

def encoder_section(inputs, qkv_w, out_w, up_w, down_w, gain_vec, bias_vec):
    num_windows, num_tokens, model_width = inputs.shape
    bias_q, bias_v, bias_o, gain_one, shift_one, bias_up, bias_down, gain_two, shift_two = unpack(gain_vec, bias_vec, model_width, up_w.shape[0])
    score_scale = 1.0 / math.sqrt(HEAD)
    mixed_qkv = low_back(project(inputs, qkv_w))
    queries = low(mixed_qkv[..., :model_width] + bias_q).reshape(num_windows, num_tokens, -1, HEAD)
    key_rows = low(mixed_qkv[..., model_width:2 * model_width]).reshape(num_windows, num_tokens, -1, HEAD)
    value_rows = low(mixed_qkv[..., 2 * model_width:] + bias_v).reshape(num_windows, num_tokens, -1, HEAD)
    scores = low_back(jnp.einsum('nqhe,nkhe->nhqk', queries, key_rows, precision=EXACT_PRECISION) * score_scale)
    attn_probs = low(jax.nn.softmax(scores, axis=-1))
    attended = jnp.einsum('nhqk,nkhe->nqhe', attn_probs, value_rows, precision=EXACT_PRECISION)
    attended = low(low_back(attended.reshape(num_windows, num_tokens, model_width)))
    first_sum = inputs + (low_back(project(attended, out_w)) + bias_o)
    normed = low(layer_norm(first_sum, gain_one, shift_one))
    upper_pre = low_back(project(normed, up_w)) + bias_up
    hidden = low(jax.nn.gelu(upper_pre, approximate=False))
    second_sum = normed + (low_back(project(hidden, down_w)) + bias_down)
    return low_back(low(layer_norm(second_sum, gain_two, shift_two)))

def reference(series, groups, cotangent, embed_weight, embed_bias, qkv_weight, out_weight, up_weight, down_weight, gains, biases):
    num_windows = series.shape[0]
    blocks = num_windows // WPD
    block_groups = groups.reshape(blocks, WPD)

    def forward(series_wide, embedding_matrix, embed_b, qkv_all, out_all, up_all, down_all, gain_all, bias_all):
        params = [low(member) for member in (embedding_matrix, embed_b, qkv_all, out_all, up_all, down_all, gain_all, bias_all)]

        def encode_block(carried, inputs):
            block_series, group_row = inputs
            activation = embed_windows(block_series, group_row, params[0], params[1])
            for section_num in range(SECTIONS):
                activation = encoder_section(activation, params[2][section_num], params[3][section_num], params[4][section_num], params[5][section_num], params[6][section_num], params[7][section_num])
            return (carried, activation)
        blocked = series_wide.reshape(blocks, WPD, series_wide.shape[1], series_wide.shape[2])
        _, layer_outputs = lax.scan(jax.checkpoint(encode_block), jnp.zeros((), jnp.float32), (blocked, block_groups))
        return layer_outputs.reshape(num_windows, layer_outputs.shape[2], layer_outputs.shape[3])
    primals = (series.astype(jnp.float32), embed_weight, embed_bias, qkv_weight, out_weight, up_weight, down_weight, gains, biases)
    block_output, pullback = jax.vjp(forward, *primals)
    gradients = pullback(cotangent.astype(jnp.float32))
    return (block_output.astype(jnp.bfloat16), gradients[0], gradients[1], gradients[2], gradients[3], gradients[4], gradients[5], gradients[6], gradients[7], gradients[8])
```

```python
from functools import partial
import math

import jax
import jax.numpy as jnp
from jax import lax
from jax.experimental import pallas as pl
from jax.experimental.pallas import tpu as pltpu
from jax.sharding import PartitionSpec as P

HEAD = 64
L1 = 96
L2 = 192
L3 = 336
GROUPS = 3


NORM_EPS = 1e-05
EXACT_PRECISION = lax.Precision.HIGHEST


def layer_norm(values, gain_vec, shift_vec):
    mean_val = jnp.mean(values, axis=-1, keepdims=True)
    centred = values - mean_val
    variance = jnp.mean(centred * centred, axis=-1, keepdims=True)
    return centred * lax.rsqrt(variance + NORM_EPS) * gain_vec + shift_vec


def gelu_exact(values):
    return jax.nn.gelu(values, approximate=False)


def project(values, matrix):
    return jnp.einsum("nvi,oi->nvo", values, matrix, preferred_element_type=jnp.float32)


def project_back(grad_in, matrix):
    return jnp.einsum("nvo,oi->nvi", grad_in, matrix, preferred_element_type=jnp.float32)


def outer_sum(grad_in, values):
    return jnp.einsum("nvo,nvi->oi", grad_in, values, preferred_element_type=jnp.float32)


def split_heads(values):
    return values.reshape(values.shape[0], values.shape[1], -1, HEAD)


def unpack(gain_vec, bias_vec, model_width, hidden_width):
    gain_wide = gain_vec.astype(jnp.float32)
    bias_wide = bias_vec.astype(jnp.float32)
    middle = 4 * model_width + hidden_width
    return (
        bias_wide[:model_width],
        bias_wide[model_width : 2 * model_width],
        bias_wide[2 * model_width : 3 * model_width],
        gain_wide[:model_width],
        bias_wide[3 * model_width : 4 * model_width],
        bias_wide[4 * model_width : middle],
        bias_wide[middle : middle + model_width],
        gain_wide[model_width:],
        bias_wide[middle + model_width :],
    )


def section_forward(inputs, weights):
    qkv_w, out_w, up_w, down_w, gain_vec, bias_vec = weights
    model_width = inputs.shape[-1]
    vectors = unpack(gain_vec, bias_vec, model_width, up_w.shape[0])
    score_scale = 1.0 / math.sqrt(HEAD)
    mixed_qkv = project(inputs, qkv_w)
    queries = (mixed_qkv[..., :model_width] + vectors[0]).astype(jnp.bfloat16)
    key_rows = mixed_qkv[..., model_width : 2 * model_width].astype(jnp.bfloat16)
    value_rows = (mixed_qkv[..., 2 * model_width :] + vectors[1]).astype(jnp.bfloat16)
    scores = (
        jnp.einsum(
            "nqhe,nkhe->nhqk",
            split_heads(queries),
            split_heads(key_rows),
            preferred_element_type=jnp.float32,
        )
        * score_scale
    )
    top_val = jnp.max(scores, axis=-1, keepdims=True)
    exp_scores = jnp.exp(scores - top_val)
    totals = jnp.sum(exp_scores, axis=-1, keepdims=True)
    attn_probs = (exp_scores / totals).astype(jnp.bfloat16)
    log_total = top_val + jnp.log(totals)
    attended = jnp.einsum(
        "nhqk,nkhe->nqhe", attn_probs, split_heads(value_rows), preferred_element_type=jnp.float32
    )
    attended = attended.reshape(inputs.shape).astype(jnp.bfloat16)
    first_sum = inputs.astype(jnp.float32) + (project(attended, out_w) + vectors[2])
    normed = layer_norm(first_sum, vectors[3], vectors[4]).astype(jnp.bfloat16)
    upper_pre = project(normed, up_w) + vectors[5]
    hidden = gelu_exact(upper_pre).astype(jnp.bfloat16)
    second_sum = normed.astype(jnp.float32) + (project(hidden, down_w) + vectors[6])
    final_result = layer_norm(second_sum, vectors[7], vectors[8]).astype(jnp.bfloat16)
    saved_set = (
        inputs,
        queries,
        key_rows,
        value_rows,
        log_total,
        attended,
        first_sum,
        normed,
        upper_pre,
        hidden,
        second_sum,
    )
    return (final_result, saved_set)


def dense_backward(grad_out, saved_set, weights):
    qkv_w, out_w, up_w, down_w, gain_vec, bias_vec = weights
    normed, upper_pre, hidden, second_sum = (
        saved_set[7],
        saved_set[8],
        saved_set[9],
        saved_set[10],
    )
    vectors = unpack(gain_vec, bias_vec, normed.shape[-1], up_w.shape[0])
    _, norm_back = jax.vjp(layer_norm, second_sum, vectors[7], vectors[8])
    grad_second, grad_gain_two, grad_shift_two = norm_back(grad_out.astype(jnp.float32))
    grad_lower = grad_second.astype(jnp.bfloat16)
    grad_bias_down = jnp.sum(grad_second, axis=(0, 1))
    grad_hidden = project_back(grad_lower, down_w)
    _, gelu_derivative = jax.vjp(gelu_exact, upper_pre)
    (grad_upper,) = gelu_derivative(grad_hidden)
    grad_bias_up = jnp.sum(grad_upper, axis=(0, 1))
    upper_low = grad_upper.astype(jnp.bfloat16)
    grad_normed = project_back(upper_low, up_w) + grad_second
    return (
        grad_normed,
        (grad_lower, upper_low),
        (grad_gain_two, grad_shift_two, grad_bias_up, grad_bias_down),
    )


def attend_backward(grad_normed, saved_set, weights):
    qkv_w, out_w, up_w, down_w, gain_vec, bias_vec = weights
    inputs, queries, key_rows, value_rows, log_total, attended, first_sum = saved_set[:7]
    vectors = unpack(gain_vec, bias_vec, inputs.shape[-1], up_w.shape[0])
    score_scale = 1.0 / math.sqrt(HEAD)
    _, norm_back = jax.vjp(layer_norm, first_sum, vectors[3], vectors[4])
    grad_first, grad_gain_one, grad_shift_one = norm_back(grad_normed)
    grad_bias_o = jnp.sum(grad_first, axis=(0, 1))
    branch_low = grad_first.astype(jnp.bfloat16)
    grad_attended = split_heads(project_back(branch_low, out_w).astype(jnp.bfloat16))
    query_heads = split_heads(queries)
    key_heads = split_heads(key_rows)
    value_heads = split_heads(value_rows)
    scores = (
        jnp.einsum("nqhe,nkhe->nhqk", query_heads, key_heads, preferred_element_type=jnp.float32)
        * score_scale
    )
    attn_probs = jnp.exp(scores - log_total)
    grad_probs = jnp.einsum(
        "nqhe,nkhe->nhqk", grad_attended, value_heads, preferred_element_type=jnp.float32
    )
    grad_values = jnp.einsum(
        "nhqk,nqhe->nkhe",
        attn_probs.astype(jnp.bfloat16),
        grad_attended,
        preferred_element_type=jnp.float32,
    )
    grad_scores = attn_probs * (
        grad_probs - jnp.sum(attn_probs * grad_probs, axis=-1, keepdims=True)
    )
    grad_scores = grad_scores.astype(jnp.bfloat16)
    grad_queries = (
        jnp.einsum("nhqk,nkhe->nqhe", grad_scores, key_heads, preferred_element_type=jnp.float32)
        * score_scale
    )
    grad_keys = (
        jnp.einsum("nhqk,nqhe->nkhe", grad_scores, query_heads, preferred_element_type=jnp.float32)
        * score_scale
    )
    grad_queries = grad_queries.reshape(inputs.shape)
    grad_keys = grad_keys.reshape(inputs.shape)
    grad_values = grad_values.reshape(inputs.shape)
    grad_bias_q = jnp.sum(grad_queries, axis=(0, 1))
    grad_bias_v = jnp.sum(grad_values, axis=(0, 1))
    mixed_low = jnp.concatenate([grad_queries, grad_keys, grad_values], axis=-1).astype(
        jnp.bfloat16
    )
    grad_input = (project_back(mixed_low, qkv_w) + grad_first).astype(jnp.bfloat16)
    return (
        grad_input,
        (mixed_low, branch_low),
        (grad_gain_one, grad_shift_one, grad_bias_q, grad_bias_v, grad_bias_o),
    )


MESH = pl.DeviceIdType.MESH
LANES = 128
ZS = 4
SECT = 4


class Place:
    def __init__(self, dps):
        self.bs = dps // ZS
        pipe = lax.axis_index("pipe")
        dp = lax.axis_index("dp")
        self.pipe, self.dp = pipe, dp
        self.x, self.c = pipe // 2, pipe % 2
        self.z, self.b = dp // self.bs, dp % self.bs
        self.block = self.c * 2 + self.x
        self.x_peer = ((1 - self.x) * 2 + self.c, dp)
        self.core_peer = (self.x * 2 + 1 - self.c, dp)

    def block_of(self, pipe):
        return (pipe % 2) * 2 + pipe // 2

    def pipe_at(self, step):
        return (self.pipe + step) % SECT

    def z_at(self, step):
        return (self.z + step) % ZS

    def b_at(self, step):
        return (self.b + step) % self.bs

    def z_peer(self, step):
        return (self.pipe, self.z_at(step) * self.bs + self.b)

    def b_peer(self, step):
        return (self.pipe, self.z * self.bs + self.b_at(step))

    def greet(self):
        barrier = pltpu.get_barrier_semaphore()
        peers = [(self.pipe_at(k), self.dp) for k in range(1, SECT)]
        peers += [self.z_peer(k) for k in range(1, ZS)]
        peers += [self.b_peer(k) for k in range(1, self.bs)]
        for peer in peers:
            pl.semaphore_signal(barrier, inc=1, device_id=peer, device_id_type=MESH)
        pl.semaphore_wait(barrier, len(peers))


def remote(src, dst, send, recv, peer):
    return pltpu.make_async_remote_copy(
        src_ref=src, dst_ref=dst, send_sem=send, recv_sem=recv, device_id=peer, device_id_type=MESH
    )


class Spread:
    def __init__(self, at, out, send, recv):
        self.at, self.out, self.send, self.recv = at, out, send, recv
        nb = at.bs - 1
        self.slot_z = 0
        self.slot_b1 = ZS - 1
        self.slot_x1 = self.slot_b1 + nb
        self.slot_x2 = self.slot_x1 + 1
        self.slot_b2 = self.slot_x2 + 1
        self.slot_c = self.slot_b2 + nb
        self.half = ZS // 2

    @staticmethod
    def slots(bs):
        return ZS - 1 + 2 * (bs - 1) + 3

    def copy(self, region, slot, peer):
        return remote(region, region, self.send.at[slot], self.recv.at[slot], peer)

    def z_copies(self, back):
        at, out = self.at, self.out
        return [
            self.copy(
                out.at[at.block, at.z_at(-k + ZS) if back else at.z, at.b],
                self.slot_z + k - 1,
                at.z_peer(k),
            )
            for k in range(1, ZS)
        ]

    def first_copies(self, back):
        at, out, half = self.at, self.out, self.half
        copies = [
            self.copy(
                out.at[at.block, pl.ds(0, half), at.b_at(at.bs - k) if back else at.b],
                self.slot_b1 + k - 1,
                at.b_peer(k),
            )
            for k in range(1, at.bs)
        ]
        block = at.c * 2 + 1 - at.x if back else at.block
        copies.append(self.copy(out.at[block, pl.ds(half, half), at.b], self.slot_x1, at.x_peer))
        return copies

    def second_copies(self, back):
        at, out, half = self.at, self.out, self.half
        block = at.c * 2 + 1 - at.x if back else at.block
        copies = [self.copy(out.at[block, pl.ds(0, half)], self.slot_x2, at.x_peer)]
        copies += [
            self.copy(
                out.at[
                    pl.ds(at.c * 2, 2), pl.ds(half, half), at.b_at(at.bs - k) if back else at.b
                ],
                self.slot_b2 + k - 1,
                at.b_peer(k),
            )
            for k in range(1, at.bs)
        ]
        return copies

    def core_copies(self, back):
        at, out = self.at, self.out
        core = 1 - at.c if back else at.c
        return [self.copy(out.at[pl.ds(core * 2, 2)], self.slot_c, at.core_peer)]

    def groups(self):
        return (self.z_copies, self.first_copies, self.second_copies, self.core_copies)

    def start(self, stage):
        for copy in self.groups()[stage](False):
            copy.start()

    def land(self, stage):
        for copy in self.groups()[stage](True):
            copy.wait_recv()

    def drain(self):
        for group in self.groups():
            for copy in group(False):
                copy.wait_send()


def gather_kernel(
    dps, att_in, ffn_in, emb_in, att, ffn, emb, p_send, p_recv, own_sem, send, recv
):
    at = Place(dps)
    own = [
        pltpu.make_async_copy(
            emb_in.at[at.block], emb.at[at.block, at.z, at.b], own_sem.at[0]
        ),
        pltpu.make_async_copy(
            att_in.at[at.block], att.at[at.pipe, at.block, at.z, at.b], own_sem.at[1]
        ),
        pltpu.make_async_copy(
            ffn_in.at[at.block], ffn.at[at.pipe, at.block, at.z, at.b], own_sem.at[2]
        ),
    ]
    for copy in own:
        copy.start()

    def split_copies(kind, piece, out, back):
        copies = []
        for k in range(1, SECT):
            other = at.pipe_at(SECT - k) if back else at.pipe_at(k)
            if back:
                region = out.at[other, at.block, at.z, at.b]
                src = region
            else:
                block = at.block_of(other)
                region = out.at[at.pipe, block, at.z, at.b]
                src = piece.at[block]
            copies.append(
                remote(
                    src,
                    region,
                    p_send.at[kind, k - 1],
                    p_recv.at[kind, k - 1],
                    (at.pipe_at(k), at.dp),
                )
            )
        return copies

    at.greet()
    for kind, (piece, out) in enumerate(((att_in, att), (ffn_in, ffn))):
        for copy in split_copies(kind, piece, out, False):
            copy.start()
    chunks = [Spread(at, emb, send.at[0], recv.at[0])]
    for section in range(SECT):
        for kind, out in enumerate((att, ffn)):
            number = 1 + 2 * section + kind
            chunks.append(Spread(at, out.at[section], send.at[number], recv.at[number]))
    for copy in own:
        copy.wait()
    stages = 4
    for tick in range(len(chunks) + stages):
        for stage in reversed(range(stages + 1)):
            number = tick - stage
            if 0 <= number < len(chunks):
                if stage == 0:
                    if number in (1, 2):
                        kind = number - 1
                        piece, out = ((att_in, att), (ffn_in, ffn))[kind]
                        for copy in split_copies(kind, piece, out, True):
                            copy.wait_recv()
                else:
                    chunks[number].land(stage - 1)
                if stage < stages:
                    chunks[number].start(stage)
    for kind, (piece, out) in enumerate(((att_in, att), (ffn_in, ffn))):
        for copy in split_copies(kind, piece, out, False):
            copy.wait_send()
    for chunk in chunks:
        chunk.drain()


def gather_all(att_in, ffn_in, emb_in, dps):
    bs = dps // ZS

    def whole(piece, *lead):
        return jax.ShapeDtypeStruct(lead + (SECT, ZS, bs) + piece.shape[1:], piece.dtype)

    slots = Spread.slots(bs)
    anywhere = pl.BlockSpec(memory_space=pl.ANY)
    return pl.pallas_call(
        partial(gather_kernel, dps),
        out_shape=(whole(att_in, SECT), whole(ffn_in, SECT), whole(emb_in)),
        in_specs=[anywhere] * 3,
        out_specs=(anywhere,) * 3,
        scratch_shapes=[
            pltpu.SemaphoreType.DMA((2, SECT - 1)),
            pltpu.SemaphoreType.DMA((2, SECT - 1)),
            pltpu.SemaphoreType.DMA((3,)),
            pltpu.SemaphoreType.DMA((1 + 2 * SECT, slots)),
            pltpu.SemaphoreType.DMA((1 + 2 * SECT, slots)),
        ],
        compiler_params=pltpu.CompilerParams(collective_id=0, has_side_effects=True),
        name="gather_parameters",
    )(att_in, ffn_in, emb_in)


class Fold:
    def __init__(self, at, source, bufs, final, local, send, recv):
        self.at, self.source, self.bufs, self.final = at, source, bufs, final
        self.local, self.send, self.recv = local, send, recv
        self.half = ZS // 2
        nb = at.bs - 1
        self.slot_c = 0
        self.slot_x1 = 1
        self.slot_b1 = 2
        self.slot_x2 = 2 + nb
        self.slot_b2 = 3 + nb
        self.slot_z = 3 + 2 * nb

    @staticmethod
    def slots(bs):
        return 3 + 2 * (bs - 1) + ZS - 1

    @staticmethod
    def scratch(bs, rows):
        half = ZS // 2
        nb = max(bs - 1, 1)
        shapes = [
            (2, ZS, bs, rows, LANES),
            (2, ZS, bs, rows, LANES),
            (half, bs, rows, LANES),
            (nb, 2, half, rows, LANES),
            (half, rows, LANES),
            (nb, half, rows, LANES),
            (ZS - 1, rows, LANES),
        ]
        return [pltpu.VMEM(shape, jnp.bfloat16) for shape in shapes]

    def copy(self, src, dst, slot, peer):
        return remote(src, dst, self.send.at[slot], self.recv.at[slot], peer)

    def core_copies(self):
        at = self.at
        other = self.source.at[pl.ds((1 - at.c) * 2, 2)]
        return [self.copy(other, self.bufs[1], self.slot_c, at.core_peer)]

    def first_copies(self):
        at, half = self.at, self.half
        total = self.bufs[0]
        copies = [
            self.copy(total.at[1 - at.x, pl.ds(0, half)], self.bufs[2], self.slot_x1, at.x_peer)
        ]
        copies += [
            self.copy(
                total.at[:, pl.ds(half, half), at.b_at(k)],
                self.bufs[3].at[k - 1],
                self.slot_b1 + k - 1,
                at.b_peer(k),
            )
            for k in range(1, at.bs)
        ]
        return copies

    def second_copies(self):
        at, half = self.at, self.half
        total = self.bufs[0]
        copies = [
            self.copy(
                total.at[1 - at.x, pl.ds(half, half), at.b], self.bufs[4], self.slot_x2, at.x_peer
            )
        ]
        copies += [
            self.copy(
                total.at[at.x, pl.ds(0, half), at.b_at(k)],
                self.bufs[5].at[k - 1],
                self.slot_b2 + k - 1,
                at.b_peer(k),
            )
            for k in range(1, at.bs)
        ]
        return copies

    def z_copies(self):
        at = self.at
        return [
            self.copy(
                self.bufs[0].at[at.x, at.z_at(k), at.b],
                self.bufs[6].at[k - 1],
                self.slot_z + k - 1,
                at.z_peer(k),
            )
            for k in range(1, ZS)
        ]

    def groups(self):
        return (self.core_copies, self.first_copies, self.second_copies, self.z_copies)

    def own_copy(self):
        return pltpu.make_async_copy(
            self.source.at[pl.ds(self.at.c * 2, 2)], self.bufs[0], self.local
        )

    def begin(self):
        self.own_copy().start()
        for copy in self.core_copies():
            copy.start()

    def step(self, stage):
        at, half = self.at, self.half
        total = self.bufs[0]
        for copy in self.groups()[stage]():
            copy.wait_recv()
        if stage == 0:
            self.own_copy().wait()
            bs = at.bs

            @pl.loop(0, 2 * ZS * bs)
            def _(i):
                place = (i // (ZS * bs), i // bs % ZS, i % bs)
                total[place] = total[place] + self.bufs[1][place]

        elif stage == 1:

            @pl.loop(0, half * at.bs)
            def _(i):
                z, b = i // at.bs, i % at.bs
                total[at.x, z, b] = total[at.x, z, b] + self.bufs[2][z, b]

            @pl.loop(0, 2 * half)
            def _(i):
                x, z = i // half, i % half
                for k in range(at.bs - 1):
                    total[x, half + z, at.b] = total[x, half + z, at.b] + self.bufs[3][k, x, z]

        elif stage == 2:

            @pl.loop(0, half)
            def _(z):
                total[at.x, half + z, at.b] = total[at.x, half + z, at.b] + self.bufs[4][z]
                for k in range(at.bs - 1):
                    total[at.x, z, at.b] = total[at.x, z, at.b] + self.bufs[5][k, z]

        else:
            done = total[at.x, at.z, at.b].astype(jnp.float32)
            for k in range(ZS - 1):
                done = done + self.bufs[6][k].astype(jnp.float32)
            self.final[...] = done.astype(self.final.dtype)
        if stage < 3:
            for copy in self.groups()[stage + 1]():
                copy.start()

    def drain(self):
        for group in self.groups():
            for copy in group():
                copy.wait_send()


def fold_kernel(dps, *refs):
    at = Place(dps)
    att_in, ffn_in, emb_in, att_out, ffn_out, emb_out = refs[:6]
    refs = refs[6:]
    number_of = 1 + 2 * SECT
    bufs = [refs[7 * i : 7 * i + 7] for i in range(number_of)]
    finals = refs[7 * number_of : 8 * number_of]
    local, send, recv, p_send, p_recv = refs[8 * number_of :]
    chunks = []
    owners = []
    for section in reversed(range(SECT)):
        for kind, source in ((1, ffn_in), (0, att_in)):
            number = len(chunks)
            chunks.append(
                Fold(
                    at,
                    source.at[section],
                    bufs[number],
                    finals[number],
                    local.at[number],
                    send.at[number],
                    recv.at[number],
                )
            )
            owners.append((section, kind))
    last = number_of - 1
    chunks.append(
        Fold(at, emb_in, bufs[last], finals[last], local.at[last], send.at[last], recv.at[last])
    )
    owners.append(None)

    def hand_over(number):
        section, kind = owners[number]
        out = (att_out, ffn_out)[kind]
        landing = out.at[at.block]
        return (
            pltpu.make_async_copy(finals[number], landing, local.at[number]),
            remote(
                finals[number],
                landing,
                p_send.at[number],
                p_recv.at[kind, at.pipe],
                (section, at.dp),
            ),
        )

    at.greet()
    stages = 5
    for tick in range(len(chunks) + stages):
        for stage in reversed(range(stages)):
            number = tick - stage
            if 0 <= number < len(chunks):
                if stage == 0:
                    chunks[number].begin()
                else:
                    chunks[number].step(stage - 1)
                if stage == 4:
                    if owners[number] is None:
                        emb_out[...] = finals[number][...]
                    else:
                        here, away = hand_over(number)
                        section = owners[number][0]

                        @pl.when(at.pipe == section)
                        def _():
                            here.start()

                        @pl.when(at.pipe != section)
                        def _():
                            away.start()

    for number, owner in enumerate(owners):
        if owner is not None:
            here, away = hand_over(number)

            @pl.when(at.pipe == owner[0])
            def _():
                here.wait()

            @pl.when(at.pipe != owner[0])
            def _():
                away.wait_send()

    for kind, out in enumerate((att_out, ffn_out)):
        for k in range(1, SECT):
            other = at.pipe_at(k)
            landing = out.at[at.block_of(other)]
            remote(
                landing, landing, p_send.at[0], p_recv.at[kind, other], (other, at.dp)
            ).wait_recv()
    for chunk in chunks:
        chunk.drain()


def fold_all(att, ffn, emb, dps):
    bs = dps // ZS
    number_of = 1 + 2 * SECT
    rows_att, rows_ffn, rows_emb = att.shape[-2], ffn.shape[-2], emb.shape[-2]
    rows = [rows_ffn, rows_att] * SECT + [rows_emb]
    scratch = []
    for count in rows:
        scratch += Fold.scratch(bs, count)
    scratch += [pltpu.VMEM((count, LANES), jnp.bfloat16) for count in rows]
    slots = Fold.slots(bs)
    scratch += [
        pltpu.SemaphoreType.DMA((number_of,)),
        pltpu.SemaphoreType.DMA((number_of, slots)),
        pltpu.SemaphoreType.DMA((number_of, slots)),
        pltpu.SemaphoreType.DMA((number_of,)),
        pltpu.SemaphoreType.DMA((2, SECT)),
    ]
    anywhere = pl.BlockSpec(memory_space=pl.ANY)
    return pl.pallas_call(
        partial(fold_kernel, dps),
        out_shape=(
            jax.ShapeDtypeStruct((SECT, rows_att, LANES), jnp.bfloat16),
            jax.ShapeDtypeStruct((SECT, rows_ffn, LANES), jnp.bfloat16),
            jax.ShapeDtypeStruct((rows_emb, LANES), jnp.bfloat16),
        ),
        in_specs=[anywhere] * 3,
        out_specs=(anywhere, anywhere, pl.BlockSpec(memory_space=pltpu.VMEM)),
        scratch_shapes=scratch,
        compiler_params=pltpu.CompilerParams(
            collective_id=1, has_side_effects=True, vmem_limit_bytes=56 * 1024 * 1024
        ),
        name="fold_gradients",
    )(att, ffn, emb)


def by_block(slab):
    split = slab.reshape(slab.shape[:-1] + (SECT, LANES))
    return jnp.moveaxis(split, -2, -3)


def pack_vectors(gains, biases):
    flat = jnp.concatenate([gains, biases], axis=1)
    flat = jnp.pad(flat, ((0, 0), (0, 16 * 512 - flat.shape[1])))
    return flat.reshape(flat.shape[0], 16, 512)


def pack_embedding(matrix, shift):
    wide = matrix.T
    first = jnp.pad(wide[:, L1 + L2 :], ((0, 0), (512 - L3 - GROUPS, 0)))
    return jnp.concatenate(
        [
            shift.T,
            first,
            jnp.pad(wide[:, L1 : L1 + L2], ((0, 0), (256 - L2, 0))),
            jnp.pad(wide[:, :L1], ((0, 0), (256 - L1, 0))),
        ],
        axis=1,
    )


def unpack_embedding(packed):
    matrix = jnp.concatenate(
        [packed[:, 1024 - L1 :], packed[:, 768 - L2 : 768], packed[:, 512 - L3 : 512]], axis=1
    )
    return matrix.T, packed[:, :GROUPS].T


def per_device(
    series,
    groups,
    cotangent,
    embed_weight,
    embed_bias,
    qkv_weight,
    out_weight,
    up_weight,
    down_weight,
    gains,
    biases,
):
    dps = lax.axis_size("dp")
    bs = dps // ZS
    low = jnp.bfloat16
    width = qkv_weight.shape[2]
    rows_qkv, rows_out, rows_up = qkv_weight.shape[1], out_weight.shape[1], up_weight.shape[1]
    rows_down = down_weight.shape[1] * down_weight.shape[2] // width
    n_gains, n_biases = gains.shape[1], biases.shape[1]
    down_low = down_weight[0].astype(low).reshape(-1, 4, width)
    att_in = jnp.concatenate(
        [
            qkv_weight[0].astype(low),
            out_weight[0].astype(low),
            pack_vectors(gains.astype(low), biases.astype(low))[0],
        ]
    )
    ffn_in = jnp.concatenate(
        [up_weight[0].astype(low), jnp.moveaxis(down_low, 1, 0).reshape(rows_down, width)]
    )
    emb_in = pack_embedding(embed_weight.astype(low), embed_bias.astype(low))
    emb_in = jnp.concatenate([emb_in[:, :512], emb_in[:, 512:]])
    att, ffn, emb = gather_all(by_block(att_in), by_block(ffn_in), by_block(emb_in), dps)
    att = jnp.moveaxis(att, 1, 4).reshape(SECT, dps, att.shape[4], width)
    ffn = jnp.moveaxis(ffn, 1, 4).reshape(SECT, dps, ffn.shape[4], width)
    emb = jnp.moveaxis(emb, 0, 3).reshape(dps, 2, -1, 512)
    emb = jnp.concatenate([emb[:, 0], emb[:, 1]], axis=-1).reshape(-1, 1024)
    qkv_all = att[:, :, :rows_qkv].reshape(SECT, -1, width)
    out_all = att[:, :, rows_qkv : rows_qkv + rows_out].reshape(SECT, -1, width)
    vec = att[:, :, rows_qkv + rows_out :].reshape(SECT, dps, -1)
    gains_all = vec[:, :, :n_gains].reshape(SECT, -1)
    biases_all = vec[:, :, n_gains : n_gains + n_biases].reshape(SECT, -1)
    up_all = ffn[:, :, :rows_up].reshape(SECT, -1, width)
    down_all = ffn[:, :, rows_up:].reshape(SECT, dps, 4, -1, width)
    down_all = jnp.moveaxis(down_all, 2, 3).reshape(SECT, width, -1)
    embedding_matrix, embed_b = unpack_embedding(emb)

    hist = series.shape[1]
    group = groups[0]
    lookback = jnp.where(group == 0, L1, jnp.where(group == 1, L2, L3))

    def aligned(rows):
        return jnp.pad(rows, ((hist - rows.shape[0], 0), (0, 0)))

    chosen = jnp.where(
        group == 0,
        aligned(embedding_matrix[:L1]),
        jnp.where(group == 1, aligned(embedding_matrix[L1 : L1 + L2]), embedding_matrix[L1 + L2 :]),
    )
    shift = embed_b[group].astype(jnp.float32)
    embedded = jnp.einsum("jv,jd->vd", series[0], chosen, preferred_element_type=jnp.float32)
    current = (embedded + shift).astype(low)[None]

    saved = []
    layers = []
    for section in range(SECT):
        weights = (
            qkv_all[section],
            out_all[section],
            up_all[section],
            down_all[section],
            gains_all[section],
            biases_all[section],
        )
        layers.append(weights)
        current, kept = section_forward(current, weights)
        saved.append(kept)
    block_output = current

    incoming = cotangent
    att_sums, ffn_sums = [None] * SECT, [None] * SECT
    for section in reversed(range(SECT)):
        kept = saved[section]
        grad_normed, dense_ops, dense_new = dense_backward(incoming, kept, layers[section])
        up_sum = outer_sum(dense_ops[1], kept[7])
        down_sum = outer_sum(dense_ops[0], kept[9])
        incoming, attend_ops, attend_new = attend_backward(grad_normed, kept, layers[section])
        qkv_sum = outer_sum(attend_ops[0], kept[0])
        out_sum = outer_sum(attend_ops[1], kept[5])
        gain_sum = jnp.concatenate([attend_new[0], dense_new[0]]).astype(low)
        bias_sum = jnp.concatenate(
            [
                attend_new[2],
                attend_new[3],
                attend_new[4],
                attend_new[1],
                dense_new[2],
                dense_new[3],
                dense_new[1],
            ]
        ).astype(low)
        att_sums[section] = jnp.concatenate(
            [
                qkv_sum.astype(low).reshape(dps, rows_qkv, width),
                out_sum.astype(low).reshape(dps, rows_out, width),
                pack_vectors(gain_sum.reshape(dps, -1), bias_sum.reshape(dps, -1)),
            ],
            axis=1,
        )
        down_sum = down_sum.astype(low).reshape(dps, -1, 4, width)
        ffn_sums[section] = jnp.concatenate(
            [
                up_sum.astype(low).reshape(dps, rows_up, width),
                jnp.moveaxis(down_sum, 2, 1).reshape(dps, rows_down, width),
            ],
            axis=1,
        )

    def by_place(sums):
        split = jnp.stack(sums).reshape(SECT, ZS, bs, -1, SECT, LANES)
        return jnp.moveaxis(split, 4, 1)

    grad_low = incoming[0]
    series_grad = jnp.einsum("vd,jd->jv", grad_low, chosen, preferred_element_type=jnp.float32)
    matrix_grad = jnp.einsum("jv,vd->jd", series[0], grad_low, preferred_element_type=jnp.float32)

    def placed(span, index):
        return jnp.where(group == index, matrix_grad[hist - span :], 0.0)

    matrix_sum = jnp.concatenate([placed(L1, 0), placed(L2, 1), placed(L3, 2)])
    shift_sum = jnp.sum(grad_low.astype(jnp.float32), axis=0)
    shift_sum = jnp.where((jnp.arange(GROUPS) == group)[:, None], shift_sum, 0.0)
    emb_sum = pack_embedding(matrix_sum, shift_sum).astype(low)
    emb_sum = emb_sum.reshape(2, 2, ZS, bs, -1, 8, LANES)
    emb_sum = jnp.moveaxis(jnp.swapaxes(emb_sum, 0, 1), 5, 4)
    emb_sum = emb_sum.reshape(SECT, ZS, bs, -1, LANES)

    att_out, ffn_out, emb_out = fold_all(by_place(att_sums), by_place(ffn_sums), emb_sum, dps)
    att_out = jnp.moveaxis(att_out, 0, 1).reshape(-1, width).astype(jnp.float32)
    ffn_out = jnp.moveaxis(ffn_out, 0, 1).reshape(-1, width).astype(jnp.float32)
    emb_out = jnp.moveaxis(emb_out.reshape(8, -1, LANES), 0, 1).reshape(-1, 1024)
    embed_w_grad, embed_b_grad = unpack_embedding(emb_out.astype(jnp.float32))
    vec_out = att_out[rows_qkv + rows_out :].reshape(1, -1)
    down_out = jnp.moveaxis(ffn_out[rows_up:].reshape(4, -1, width), 0, 1)
    return (
        block_output,
        series_grad[None],
        embed_w_grad,
        embed_b_grad,
        att_out[:rows_qkv][None],
        att_out[rows_qkv : rows_qkv + rows_out][None],
        ffn_out[:rows_up][None],
        down_out.reshape(1, -1, down_weight.shape[2]),
        vec_out[:, :n_gains],
        vec_out[:, n_gains : n_gains + n_biases],
    )


def solution(mesh):
    return jax.shard_map(
        per_device,
        mesh=mesh,
        in_specs=(
            P(("pipe", "dp"), None, None),
            P(("pipe", "dp")),
            P(("pipe", "dp"), None, None),
            P(None, "dp"),
            P(None, "dp"),
            P("pipe", "dp", None),
            P("pipe", "dp", None),
            P("pipe", "dp", None),
            P("pipe", "dp", None),
            P("pipe", "dp"),
            P("pipe", "dp"),
        ),
        out_specs=(
            P(("pipe", "dp"), None, None),
            P(("pipe", "dp"), None, None),
            P(None, ("pipe", "dp")),
            P(None, ("pipe", "dp")),
            P("pipe", "dp", None),
            P("pipe", "dp", None),
            P("pipe", "dp", None),
            P("pipe", "dp", None),
            P("pipe", "dp"),
            P("pipe", "dp"),
        ),
        check_vma=False,
    )
```

```python
from functools import partial
import math

import jax
import jax.numpy as jnp
from jax import lax
from jax.experimental import pallas as pl
from jax.experimental.pallas import tpu as pltpu
from jax.sharding import PartitionSpec as P

HEAD = 64
L1 = 96
L2 = 192
L3 = 336
GROUPS = 3


NORM_EPS = 1e-05


MESH = pl.DeviceIdType.MESH
LANES = 128
ZS = 4
SECT = 4


class Place:
    def __init__(self, dps):
        self.bs = dps // ZS
        pipe = lax.axis_index("pipe")
        dp = lax.axis_index("dp")
        self.pipe, self.dp = pipe, dp
        self.x, self.c = pipe // 2, pipe % 2
        self.z, self.b = dp // self.bs, dp % self.bs
        self.block = self.c * 2 + self.x
        self.x_peer = ((1 - self.x) * 2 + self.c, dp)
        self.core_peer = (self.x * 2 + 1 - self.c, dp)

    def block_of(self, pipe):
        return (pipe % 2) * 2 + pipe // 2

    def pipe_at(self, step):
        return (self.pipe + step) % SECT

    def z_at(self, step):
        return (self.z + step) % ZS

    def b_at(self, step):
        return (self.b + step) % self.bs

    def z_peer(self, step):
        return (self.pipe, self.z_at(step) * self.bs + self.b)

    def b_peer(self, step):
        return (self.pipe, self.z * self.bs + self.b_at(step))

    def greet(self):
        barrier = pltpu.get_barrier_semaphore()
        peers = [(self.pipe_at(k), self.dp) for k in range(1, SECT)]
        peers += [self.z_peer(k) for k in range(1, ZS)]
        peers += [self.b_peer(k) for k in range(1, self.bs)]
        for peer in peers:
            pl.semaphore_signal(barrier, inc=1, device_id=peer, device_id_type=MESH)
        pl.semaphore_wait(barrier, len(peers))


def remote(src, dst, send, recv, peer):
    return pltpu.make_async_remote_copy(
        src_ref=src, dst_ref=dst, send_sem=send, recv_sem=recv, device_id=peer, device_id_type=MESH
    )


class Spread:
    def __init__(self, at, out, send, recv):
        self.at, self.out, self.send, self.recv = at, out, send, recv
        nb = at.bs - 1
        self.slot_z = 0
        self.slot_b1 = ZS - 1
        self.slot_x1 = self.slot_b1 + nb
        self.slot_x2 = self.slot_x1 + 1
        self.slot_b2 = self.slot_x2 + 1
        self.slot_c = self.slot_b2 + nb
        self.half = ZS // 2

    @staticmethod
    def slots(bs):
        return ZS - 1 + 2 * (bs - 1) + 3

    def copy(self, region, slot, peer):
        return remote(region, region, self.send.at[slot], self.recv.at[slot], peer)

    def z_copies(self, back):
        at, out = self.at, self.out
        return [
            self.copy(
                out.at[at.block, at.z_at(-k + ZS) if back else at.z, at.b],
                self.slot_z + k - 1,
                at.z_peer(k),
            )
            for k in range(1, ZS)
        ]

    def first_copies(self, back):
        at, out, half = self.at, self.out, self.half
        copies = [
            self.copy(
                out.at[at.block, pl.ds(0, half), at.b_at(at.bs - k) if back else at.b],
                self.slot_b1 + k - 1,
                at.b_peer(k),
            )
            for k in range(1, at.bs)
        ]
        block = at.c * 2 + 1 - at.x if back else at.block
        copies.append(self.copy(out.at[block, pl.ds(half, half), at.b], self.slot_x1, at.x_peer))
        return copies

    def second_copies(self, back):
        at, out, half = self.at, self.out, self.half
        block = at.c * 2 + 1 - at.x if back else at.block
        copies = [self.copy(out.at[block, pl.ds(0, half)], self.slot_x2, at.x_peer)]
        copies += [
            self.copy(
                out.at[
                    pl.ds(at.c * 2, 2), pl.ds(half, half), at.b_at(at.bs - k) if back else at.b
                ],
                self.slot_b2 + k - 1,
                at.b_peer(k),
            )
            for k in range(1, at.bs)
        ]
        return copies

    def core_copies(self, back):
        at, out = self.at, self.out
        core = 1 - at.c if back else at.c
        return [self.copy(out.at[pl.ds(core * 2, 2)], self.slot_c, at.core_peer)]

    def groups(self):
        return (self.z_copies, self.first_copies, self.second_copies, self.core_copies)

    def start(self, stage):
        for copy in self.groups()[stage](False):
            copy.start()

    def land(self, stage):
        for copy in self.groups()[stage](True):
            copy.wait_recv()

    def drain(self):
        for group in self.groups():
            for copy in group(False):
                copy.wait_send()


def gather_kernel(
    dps, att_in, ffn_in, emb_in, att, ffn, emb, p_send, p_recv, own_sem, send, recv
):
    at = Place(dps)
    own = [
        pltpu.make_async_copy(
            emb_in.at[at.block], emb.at[at.block, at.z, at.b], own_sem.at[0]
        ),
        pltpu.make_async_copy(
            att_in.at[at.block], att.at[at.pipe, at.block, at.z, at.b], own_sem.at[1]
        ),
        pltpu.make_async_copy(
            ffn_in.at[at.block], ffn.at[at.pipe, at.block, at.z, at.b], own_sem.at[2]
        ),
    ]
    for copy in own:
        copy.start()

    def split_copies(kind, piece, out, back):
        copies = []
        for k in range(1, SECT):
            other = at.pipe_at(SECT - k) if back else at.pipe_at(k)
            if back:
                region = out.at[other, at.block, at.z, at.b]
                src = region
            else:
                block = at.block_of(other)
                region = out.at[at.pipe, block, at.z, at.b]
                src = piece.at[block]
            copies.append(
                remote(
                    src,
                    region,
                    p_send.at[kind, k - 1],
                    p_recv.at[kind, k - 1],
                    (at.pipe_at(k), at.dp),
                )
            )
        return copies

    at.greet()
    for kind, (piece, out) in enumerate(((att_in, att), (ffn_in, ffn))):
        for copy in split_copies(kind, piece, out, False):
            copy.start()
    chunks = [Spread(at, emb, send.at[0], recv.at[0])]
    for section in range(SECT):
        for kind, out in enumerate((att, ffn)):
            number = 1 + 2 * section + kind
            chunks.append(Spread(at, out.at[section], send.at[number], recv.at[number]))
    for copy in own:
        copy.wait()
    stages = 4
    for tick in range(len(chunks) + stages):
        for stage in reversed(range(stages + 1)):
            number = tick - stage
            if 0 <= number < len(chunks):
                if stage == 0:
                    if number in (1, 2):
                        kind = number - 1
                        piece, out = ((att_in, att), (ffn_in, ffn))[kind]
                        for copy in split_copies(kind, piece, out, True):
                            copy.wait_recv()
                else:
                    chunks[number].land(stage - 1)
                if stage < stages:
                    chunks[number].start(stage)
    for kind, (piece, out) in enumerate(((att_in, att), (ffn_in, ffn))):
        for copy in split_copies(kind, piece, out, False):
            copy.wait_send()
    for chunk in chunks:
        chunk.drain()


def gather_all(att_in, ffn_in, emb_in, dps):
    bs = dps // ZS

    def whole(piece, *lead):
        return jax.ShapeDtypeStruct(lead + (SECT, ZS, bs) + piece.shape[1:], piece.dtype)

    slots = Spread.slots(bs)
    anywhere = pl.BlockSpec(memory_space=pl.ANY)
    return pl.pallas_call(
        partial(gather_kernel, dps),
        out_shape=(whole(att_in, SECT), whole(ffn_in, SECT), whole(emb_in)),
        in_specs=[anywhere] * 3,
        out_specs=(anywhere,) * 3,
        scratch_shapes=[
            pltpu.SemaphoreType.DMA((2, SECT - 1)),
            pltpu.SemaphoreType.DMA((2, SECT - 1)),
            pltpu.SemaphoreType.DMA((3,)),
            pltpu.SemaphoreType.DMA((1 + 2 * SECT, slots)),
            pltpu.SemaphoreType.DMA((1 + 2 * SECT, slots)),
        ],
        compiler_params=pltpu.CompilerParams(collective_id=0, has_side_effects=True),
        name="gather_parameters",
    )(att_in, ffn_in, emb_in)


class Fold:
    def __init__(self, at, source, bufs, final, local, send, recv):
        self.at, self.source, self.bufs, self.final = at, source, bufs, final
        self.local, self.send, self.recv = local, send, recv
        self.half = ZS // 2
        nb = at.bs - 1
        self.slot_c = 0
        self.slot_x1 = 1
        self.slot_b1 = 2
        self.slot_x2 = 2 + nb
        self.slot_b2 = 3 + nb
        self.slot_z = 3 + 2 * nb

    @staticmethod
    def slots(bs):
        return 3 + 2 * (bs - 1) + ZS - 1

    @staticmethod
    def scratch(bs, rows):
        half = ZS // 2
        nb = max(bs - 1, 1)
        shapes = [
            (2, ZS, bs, rows, LANES),
            (2, ZS, bs, rows, LANES),
            (half, bs, rows, LANES),
            (nb, 2, half, rows, LANES),
            (half, rows, LANES),
            (nb, half, rows, LANES),
            (ZS - 1, rows, LANES),
        ]
        return [pltpu.VMEM(shape, jnp.bfloat16) for shape in shapes]

    def copy(self, src, dst, slot, peer):
        return remote(src, dst, self.send.at[slot], self.recv.at[slot], peer)

    def core_copies(self):
        at = self.at
        other = self.source.at[pl.ds((1 - at.c) * 2, 2)]
        return [self.copy(other, self.bufs[1], self.slot_c, at.core_peer)]

    def first_copies(self):
        at, half = self.at, self.half
        total = self.bufs[0]
        copies = [
            self.copy(total.at[1 - at.x, pl.ds(0, half)], self.bufs[2], self.slot_x1, at.x_peer)
        ]
        copies += [
            self.copy(
                total.at[:, pl.ds(half, half), at.b_at(k)],
                self.bufs[3].at[k - 1],
                self.slot_b1 + k - 1,
                at.b_peer(k),
            )
            for k in range(1, at.bs)
        ]
        return copies

    def second_copies(self):
        at, half = self.at, self.half
        total = self.bufs[0]
        copies = [
            self.copy(
                total.at[1 - at.x, pl.ds(half, half), at.b], self.bufs[4], self.slot_x2, at.x_peer
            )
        ]
        copies += [
            self.copy(
                total.at[at.x, pl.ds(0, half), at.b_at(k)],
                self.bufs[5].at[k - 1],
                self.slot_b2 + k - 1,
                at.b_peer(k),
            )
            for k in range(1, at.bs)
        ]
        return copies

    def z_copies(self):
        at = self.at
        return [
            self.copy(
                self.bufs[0].at[at.x, at.z_at(k), at.b],
                self.bufs[6].at[k - 1],
                self.slot_z + k - 1,
                at.z_peer(k),
            )
            for k in range(1, ZS)
        ]

    def groups(self):
        return (self.core_copies, self.first_copies, self.second_copies, self.z_copies)

    def own_copy(self):
        return pltpu.make_async_copy(
            self.source.at[pl.ds(self.at.c * 2, 2)], self.bufs[0], self.local
        )

    def begin(self):
        self.own_copy().start()
        for copy in self.core_copies():
            copy.start()

    def step(self, stage):
        at, half = self.at, self.half
        total = self.bufs[0]
        for copy in self.groups()[stage]():
            copy.wait_recv()
        if stage == 0:
            self.own_copy().wait()
            bs = at.bs

            @pl.loop(0, 2 * ZS * bs)
            def _(i):
                place = (i // (ZS * bs), i // bs % ZS, i % bs)
                total[place] = total[place] + self.bufs[1][place]

        elif stage == 1:

            @pl.loop(0, half * at.bs)
            def _(i):
                z, b = i // at.bs, i % at.bs
                total[at.x, z, b] = total[at.x, z, b] + self.bufs[2][z, b]

            @pl.loop(0, 2 * half)
            def _(i):
                x, z = i // half, i % half
                for k in range(at.bs - 1):
                    total[x, half + z, at.b] = total[x, half + z, at.b] + self.bufs[3][k, x, z]

        elif stage == 2:

            @pl.loop(0, half)
            def _(z):
                total[at.x, half + z, at.b] = total[at.x, half + z, at.b] + self.bufs[4][z]
                for k in range(at.bs - 1):
                    total[at.x, z, at.b] = total[at.x, z, at.b] + self.bufs[5][k, z]

        else:
            done = total[at.x, at.z, at.b].astype(jnp.float32)
            for k in range(ZS - 1):
                done = done + self.bufs[6][k].astype(jnp.float32)
            self.final[...] = done.astype(self.final.dtype)
        if stage < 3:
            for copy in self.groups()[stage + 1]():
                copy.start()

    def drain(self):
        for group in self.groups():
            for copy in group():
                copy.wait_send()


def fold_kernel(dps, *refs):
    at = Place(dps)
    att_in, ffn_in, emb_in, att_out, ffn_out, emb_out = refs[:6]
    refs = refs[6:]
    number_of = 1 + 2 * SECT
    bufs = [refs[7 * i : 7 * i + 7] for i in range(number_of)]
    finals = refs[7 * number_of : 8 * number_of]
    local, send, recv, p_send, p_recv = refs[8 * number_of :]
    chunks = []
    owners = []
    for section in reversed(range(SECT)):
        for kind, source in ((1, ffn_in), (0, att_in)):
            number = len(chunks)
            chunks.append(
                Fold(
                    at,
                    source.at[section],
                    bufs[number],
                    finals[number],
                    local.at[number],
                    send.at[number],
                    recv.at[number],
                )
            )
            owners.append((section, kind))
    last = number_of - 1
    chunks.append(
        Fold(at, emb_in, bufs[last], finals[last], local.at[last], send.at[last], recv.at[last])
    )
    owners.append(None)

    def hand_over(number):
        section, kind = owners[number]
        out = (att_out, ffn_out)[kind]
        landing = out.at[at.block]
        return (
            pltpu.make_async_copy(finals[number], landing, local.at[number]),
            remote(
                finals[number],
                landing,
                p_send.at[number],
                p_recv.at[kind, at.pipe],
                (section, at.dp),
            ),
        )

    at.greet()
    stages = 5
    for tick in range(len(chunks) + stages):
        for stage in reversed(range(stages)):
            number = tick - stage
            if 0 <= number < len(chunks):
                if stage == 0:
                    chunks[number].begin()
                else:
                    chunks[number].step(stage - 1)
                if stage == 4:
                    if owners[number] is None:
                        emb_out[...] = finals[number][...]
                    else:
                        here, away = hand_over(number)
                        section = owners[number][0]

                        @pl.when(at.pipe == section)
                        def _():
                            here.start()

                        @pl.when(at.pipe != section)
                        def _():
                            away.start()

    for number, owner in enumerate(owners):
        if owner is not None:
            here, away = hand_over(number)

            @pl.when(at.pipe == owner[0])
            def _():
                here.wait()

            @pl.when(at.pipe != owner[0])
            def _():
                away.wait_send()

    for kind, out in enumerate((att_out, ffn_out)):
        for k in range(1, SECT):
            other = at.pipe_at(k)
            landing = out.at[at.block_of(other)]
            remote(
                landing, landing, p_send.at[0], p_recv.at[kind, other], (other, at.dp)
            ).wait_recv()
    for chunk in chunks:
        chunk.drain()


def fold_all(att, ffn, emb, dps):
    bs = dps // ZS
    number_of = 1 + 2 * SECT
    rows_att, rows_ffn, rows_emb = att.shape[-2], ffn.shape[-2], emb.shape[-2]
    rows = [rows_ffn, rows_att] * SECT + [rows_emb]
    scratch = []
    for count in rows:
        scratch += Fold.scratch(bs, count)
    scratch += [pltpu.VMEM((count, LANES), jnp.bfloat16) for count in rows]
    slots = Fold.slots(bs)
    scratch += [
        pltpu.SemaphoreType.DMA((number_of,)),
        pltpu.SemaphoreType.DMA((number_of, slots)),
        pltpu.SemaphoreType.DMA((number_of, slots)),
        pltpu.SemaphoreType.DMA((number_of,)),
        pltpu.SemaphoreType.DMA((2, SECT)),
    ]
    anywhere = pl.BlockSpec(memory_space=pl.ANY)
    return pl.pallas_call(
        partial(fold_kernel, dps),
        out_shape=(
            jax.ShapeDtypeStruct((SECT, rows_att, LANES), jnp.bfloat16),
            jax.ShapeDtypeStruct((SECT, rows_ffn, LANES), jnp.bfloat16),
            jax.ShapeDtypeStruct((rows_emb, LANES), jnp.bfloat16),
        ),
        in_specs=[anywhere] * 3,
        out_specs=(anywhere, anywhere, pl.BlockSpec(memory_space=pltpu.VMEM)),
        scratch_shapes=scratch,
        compiler_params=pltpu.CompilerParams(
            collective_id=1, has_side_effects=True, vmem_limit_bytes=56 * 1024 * 1024
        ),
        name="fold_gradients",
    )(att, ffn, emb)


HALF = 256
WIDE = 512
QKV_TILE = 384
VEC_ROWS = 16


def dot_nt(a, b):
    return lax.dot_general(a, b, (((1,), (1,)), ((), ())), preferred_element_type=jnp.float32)


def dot_nn(a, b):
    return lax.dot_general(a, b, (((1,), (0,)), ((), ())), preferred_element_type=jnp.float32)


def dot_tn(a, b):
    return lax.dot_general(a, b, (((0,), (0,)), ((), ())), preferred_element_type=jnp.float32)


def aligned(index, unit):
    return pl.multiple_of(index, unit)


def rows_of(ref, bs, first, count, start, rows, blocks=range(SECT)):
    parts = []
    for i in range(count):
        d = first + i
        place = (d // bs, d % bs)
        parts.append(
            jnp.concatenate(
                [ref[(lb,) + place + (pl.ds(start, rows), slice(None))] for lb in blocks], axis=1
            )
        )
    return parts[0] if count == 1 else jnp.concatenate(parts, axis=0)


def put_rows(ref, bs, first, count, start, rows, value, block=0):
    value = value.astype(ref.dtype)
    for i in range(count):
        d = first + i
        place = (d // bs, d % bs)
        for lane in range(value.shape[1] // LANES):
            ref[(block + lane,) + place + (pl.ds(start, rows), slice(None))] = value[
                i * rows : (i + 1) * rows, lane * LANES : (lane + 1) * LANES
            ]


def vector_pieces(dps):
    n_gains, n_biases = 2 * WIDE // dps, 10 * WIDE // dps
    starts = [(0, 0), (0, 2), (1, 0), (1, 2), (2, 0), (2, 1), (2, 2), (2, 3), (3, 0), (3, 2)]
    pieces = []
    for d in range(dps):
        at = 0
        while at < n_gains + n_biases:
            if at < n_gains:
                index = d * n_gains + at
                row, column = (1, 3)[index // WIDE], WIDE + index % WIDE
                left = n_gains - at
            else:
                index = d * n_biases + at - n_gains
                row, part = starts[index // WIDE]
                column = part * WIDE + index % WIDE
                left = n_gains + n_biases - at
            size = min(left, LANES - at % LANES, LANES - column % LANES)
            pieces.append((d, at // WIDE, at % WIDE, row, column, size))
            at += size
    return pieces


def read_vectors(ref, table, bs, start):
    dps = ZS * bs
    tiles = {}
    for d, row, lane, to_row, to_lane, size in vector_pieces(dps):
        key = (d, lane // LANES)
        if key not in tiles:
            tile = ref[lane // LANES, d // bs, d % bs, start : start + VEC_ROWS, :]
            tiles[key] = tile.astype(jnp.float32)
        off = lane % LANES
        table[to_row : to_row + 1, to_lane : to_lane + size] = tiles[key][
            row : row + 1, off : off + size
        ]


def write_vectors(ref, table, bs, start):
    dps = ZS * bs
    found = {}
    for d, row, lane, to_row, to_lane, size in vector_pieces(dps):
        piece = table[to_row : to_row + 1, to_lane : to_lane + size]
        found.setdefault((d, lane // LANES), {}).setdefault(row, []).append(piece)
    row_id = lax.broadcasted_iota(jnp.int32, (VEC_ROWS, LANES), 0)
    for d in range(dps):
        for lb in range(SECT):
            tile = jnp.zeros((VEC_ROWS, LANES), jnp.float32)
            for row, pieces in found.get((d, lb), {}).items():
                have = sum(piece.shape[1] for piece in pieces)
                if have < LANES:
                    pieces = pieces + [jnp.zeros((1, LANES - have), jnp.float32)]
                line = pieces[0] if len(pieces) == 1 else jnp.concatenate(pieces, axis=1)
                tile = jnp.where(row_id == row, line, tile)
            ref[lb, d // bs, d % bs, start : start + VEC_ROWS, :] = tile.astype(ref.dtype)


def normalize(x, gain, shift):
    mean = jnp.mean(x, axis=1, keepdims=True)
    centred = x - mean
    scale = lax.rsqrt(jnp.mean(centred * centred, axis=1, keepdims=True) + NORM_EPS)
    return centred * scale * gain + shift


def normalize_back(x, grad, gain):
    mean = jnp.mean(x, axis=1, keepdims=True)
    centred = x - mean
    scale = lax.rsqrt(jnp.mean(centred * centred, axis=1, keepdims=True) + NORM_EPS)
    unit = centred * scale
    inner = grad * gain
    first = jnp.mean(inner, axis=1, keepdims=True)
    second = jnp.mean(inner * unit, axis=1, keepdims=True)
    out = scale * (inner - first - unit * second)
    return out, jnp.sum(grad * unit, axis=0, keepdims=True), jnp.sum(grad, axis=0, keepdims=True)


def gelu_pair(u):
    bell = jnp.exp(-0.5 * (u * u))
    t = 1.0 / (1.0 + 0.23164188824 * jnp.abs(u))
    tail = 0.5307027145 * t
    tail = (tail - 0.7265760135) * t
    tail = (tail + 0.7107068705) * t
    tail = (tail - 0.142248368) * t
    tail = (tail + 0.127414796) * t * bell
    below = jnp.where(u < 0.0, tail, 1.0 - tail)
    return u * below, below + u * (0.3989422804014327 * bell)


def head_masks(scale):
    lane = lax.broadcasted_iota(jnp.int32, (1, LANES), 1)
    first = jnp.where(lane < HEAD, scale, 0.0).astype(jnp.bfloat16)
    second = jnp.where(lane < HEAD, 0.0, scale).astype(jnp.bfloat16)
    return first, second


class Sizes:
    def __init__(self, dps):
        self.dps, self.bs = dps, dps // ZS
        self.qkv, self.out, self.up, self.down = (
            3 * WIDE // dps,
            WIDE // dps,
            4 * WIDE // dps,
            WIDE // dps,
        )
        self.vec = self.qkv + self.out
        self.att = self.vec + VEC_ROWS
        self.ffn = self.up + 4 * self.down


def forward_attention(size, w, table, h, mixed, lse, attended, first, normed):
    bs = size.bs
    per_tile = QKV_TILE // size.qkv

    @pl.loop(0, 3 * WIDE // QKV_TILE)
    def _(t):
        columns = pl.ds(aligned(t * QKV_TILE, LANES), QKV_TILE)
        matrix = rows_of(w, bs, t * per_tile, per_tile, 0, size.qkv)
        mixed[:, columns] = (dot_nt(h[...], matrix) + table[0:1, columns]).astype(mixed.dtype)

    @pl.loop(0, 8)
    def _(i):
        pair, part = i // 2, i % 2
        rows = pl.ds(aligned(part * HALF, HALF), HALF)
        lane = aligned(pair * LANES, LANES)
        queries = mixed[rows, pl.ds(lane, LANES)]
        key_rows = mixed[:, pl.ds(WIDE + lane, LANES)]
        values = mixed[:, pl.ds(2 * WIDE + lane, LANES)].T
        joined = []
        for head, mask in enumerate(head_masks(1.0 / math.sqrt(HEAD))):
            scores = dot_nt(key_rows, queries * mask)
            top = jnp.max(scores, axis=0, keepdims=True)
            probs = jnp.exp(scores - top)
            total = jnp.sum(probs, axis=0, keepdims=True)
            lse[2 * pair + head, :, rows] = top + jnp.log(total)
            probs = (probs * (1.0 / total)).astype(jnp.bfloat16)
            joined.append(dot_nn(values[head * HEAD : (head + 1) * HEAD], probs))
        joined = jnp.concatenate(joined, axis=0).T
        attended[rows, pl.ds(lane, LANES)] = joined.astype(attended.dtype)

    @pl.loop(0, 2)
    def _(part):
        rows = pl.ds(aligned(part * HALF, HALF), HALF)
        matrix = rows_of(w, bs, 0, size.dps, size.qkv, size.out)
        out = dot_nt(attended[rows, :], matrix) + table[1:2, 0:WIDE]
        total = h[rows, :].astype(jnp.float32) + out
        first[rows, :] = total
        normed[rows, :] = normalize(
            total, table[1:2, WIDE : 2 * WIDE], table[1:2, 2 * WIDE : 3 * WIDE]
        ).astype(normed.dtype)


def forward_dense(size, w, table, normed, slope, hidden, second, h):
    bs = size.bs
    per_tile = HALF // size.up

    @pl.loop(0, 4 * WIDE // HALF)
    def _(j):
        columns = pl.ds(aligned(j * HALF, HALF), HALF)
        matrix = rows_of(w, bs, j * per_tile, per_tile, 0, size.up)
        upper = dot_nt(normed[...], matrix) + table[2:3, columns]
        value, grad = gelu_pair(upper)
        hidden[:, columns] = value.astype(hidden.dtype)
        slope[:, columns] = grad.astype(slope.dtype)

    @pl.loop(0, 2)
    def _(part):
        rows = pl.ds(aligned(part * HALF, HALF), HALF)
        total = normed[rows, :].astype(jnp.float32) + table[3:4, 0:WIDE]
        for j in range(4):
            matrix = rows_of(w, bs, 0, size.dps, size.up + j * size.down, size.down)
            total = total + dot_nt(hidden[rows, j * WIDE : (j + 1) * WIDE], matrix)
        second[rows, :] = total
        h[rows, :] = normalize(
            total, table[3:4, WIDE : 2 * WIDE], table[3:4, 2 * WIDE : 3 * WIDE]
        ).astype(h.dtype)


def backward_dense(
    size, w, table, grads, dtable, dy, second, slope, hidden, normed, dnormed, dlow, dlow_t
):
    bs = size.bs
    per_tile = HALF // size.up
    dtable[...] = jnp.zeros_like(dtable)

    @pl.loop(0, 2)
    def _(part):
        rows = pl.ds(aligned(part * HALF, HALF), HALF)
        grad, gain_sum, shift_sum = normalize_back(
            second[rows, :], dy[rows, :].astype(jnp.float32), table[3:4, WIDE : 2 * WIDE]
        )
        dnormed[rows, :] = grad
        dlow[rows, :] = grad.astype(dlow.dtype)
        dtable[3:4, 0:WIDE] += jnp.sum(grad, axis=0, keepdims=True)
        dtable[3:4, WIDE : 2 * WIDE] += gain_sum
        dtable[3:4, 2 * WIDE : 3 * WIDE] += shift_sum

    dlow_t[...] = dlow[...].T

    @pl.loop(0, 4 * WIDE // HALF)
    def _(j):
        columns = pl.ds(aligned(j * HALF, HALF), HALF)
        block = 2 * (j % 2)
        start = aligned(size.up + j // 2 * size.down, 16)
        matrix = rows_of(w, bs, 0, size.dps, start, size.down, (block, block + 1))
        dupper = dot_nn(dlow[...], matrix) * slope[:, columns].astype(jnp.float32)
        dtable[2:3, columns] = jnp.sum(dupper, axis=0, keepdims=True)
        dup = dupper.astype(jnp.bfloat16)
        put_rows(
            grads, bs, 0, size.dps, start, size.down, dot_nn(dlow_t[...], hidden[:, columns]), block
        )
        put_rows(grads, bs, j * per_tile, per_tile, 0, size.up, dot_tn(dup, normed[...]))
        matrix = rows_of(w, bs, j * per_tile, per_tile, 0, size.up)
        dnormed[...] += dot_nn(dup, matrix)


def backward_attention(
    size, w, table, grads, dtable, dy, first, attended, mixed, lse, h, dnormed, dlow, dlow_t, dmixed
):
    bs = size.bs

    @pl.loop(0, 2)
    def _(part):
        rows = pl.ds(aligned(part * HALF, HALF), HALF)
        grad, gain_sum, shift_sum = normalize_back(
            first[rows, :], dnormed[rows, :], table[1:2, WIDE : 2 * WIDE]
        )
        dnormed[rows, :] = grad
        dlow[rows, :] = grad.astype(dlow.dtype)
        dtable[1:2, 0:WIDE] += jnp.sum(grad, axis=0, keepdims=True)
        dtable[1:2, WIDE : 2 * WIDE] += gain_sum
        dtable[1:2, 2 * WIDE : 3 * WIDE] += shift_sum

    dlow_t[...] = dlow[...].T
    for block in (0, 2):
        columns = slice(block * LANES, (block + 2) * LANES)
        value = dot_nn(dlow_t[...], attended[:, columns])
        put_rows(grads, bs, 0, size.dps, size.qkv, size.out, value, block)

    @pl.loop(0, 2)
    def _(part):
        rows = pl.ds(aligned(part * HALF, HALF), HALF)
        matrix = rows_of(w, bs, 0, size.dps, size.qkv, size.out)
        dlow[rows, :] = dot_nn(dlow[rows, :], matrix).astype(dlow.dtype)

    scale = 1.0 / math.sqrt(HEAD)

    @pl.loop(0, 4)
    def _(pair):
        lane = aligned(pair * LANES, LANES)
        columns = pl.ds(lane, LANES)
        key_rows = mixed[:, pl.ds(WIDE + lane, LANES)]
        keys_t = key_rows.T
        values = mixed[:, pl.ds(2 * WIDE + lane, LANES)]
        dkeys = jnp.zeros((WIDE, LANES), jnp.float32)
        dvalues = jnp.zeros((WIDE, LANES), jnp.float32)
        for part in range(2):
            rows = slice(part * HALF, (part + 1) * HALF)
            queries = mixed[rows, columns]
            grad_out = dlow[rows, columns]
            dqueries = []
            for head in range(2):
                query = queries * head_masks(scale)[head]
                grad = grad_out * head_masks(1.0)[head]
                probs = jnp.exp(dot_nt(key_rows, query) - lse[2 * pair + head, :, rows])
                dprobs = dot_nt(values, grad)
                delta = jnp.sum(probs * dprobs, axis=0, keepdims=True)
                dscores = (probs * (dprobs - delta)).astype(jnp.bfloat16)
                dvalues = dvalues + dot_nn(probs.astype(jnp.bfloat16), grad)
                dkeys = dkeys + dot_nn(dscores, query)
                dqueries.append(dot_nn(keys_t[head * HEAD : (head + 1) * HEAD], dscores))
            dquery = jnp.concatenate(dqueries, axis=0).T * scale
            dtable[0:1, columns] += jnp.sum(dquery, axis=0, keepdims=True)
            dmixed[rows, columns] = dquery.astype(dmixed.dtype)
        dmixed[:, pl.ds(WIDE + lane, LANES)] = dkeys.astype(dmixed.dtype)
        dmixed[:, pl.ds(2 * WIDE + lane, LANES)] = dvalues.astype(dmixed.dtype)
        dtable[0:1, pl.ds(2 * WIDE + lane, LANES)] = jnp.sum(dvalues, axis=0, keepdims=True)

    per_tile = QKV_TILE // size.qkv

    @pl.loop(0, 3 * WIDE // QKV_TILE)
    def _(t):
        columns = pl.ds(aligned(t * QKV_TILE, LANES), QKV_TILE)
        grad = dmixed[:, columns]
        put_rows(grads, bs, t * per_tile, per_tile, 0, size.qkv, dot_tn(grad, h[...]))
        matrix = rows_of(w, bs, t * per_tile, per_tile, 0, size.qkv)
        dnormed[...] += dot_nn(grad, matrix)

    dy[...] = dnormed[...].astype(dy.dtype)
    write_vectors(grads, dtable, bs, size.vec)


def copies_of(pairs, sems, at=0):
    return [
        pltpu.make_async_copy(src, dst, sems.at[at + i]) for i, (src, dst) in enumerate(pairs)
    ]


def start_all(copies):
    for copy in copies:
        copy.start()


def wait_all(copies):
    for copy in copies:
        copy.wait()


def saved_shapes():
    low, wide = jnp.bfloat16, jnp.float32
    return [
        ((WIDE, WIDE), low),
        ((WIDE, 3 * WIDE), low),
        ((2 * SECT, 1, WIDE), wide),
        ((WIDE, WIDE), low),
        ((WIDE, WIDE), wide),
        ((WIDE, WIDE), low),
        ((WIDE, 4 * WIDE), low),
        ((WIDE, 4 * WIDE), low),
        ((WIDE, WIDE), wide),
        ((SECT, 4 * WIDE), wide),
    ]


def weight_shapes(size):
    low = jnp.bfloat16
    return [
        ((SECT, ZS, size.bs, size.att, LANES), low),
        ((SECT, ZS, size.bs, size.ffn, LANES), low),
    ]


def forward_kernel(dps, att, ffn, h_in, out, *refs):
    size = Sizes(dps)
    kept, refs = refs[:10], refs[10:]
    local, refs = refs[:10], refs[10:]
    w_att, w_ffn, w_sem, kept_sem = refs
    h, mixed, lse, attended, first, normed, slope, hidden, second, table = local

    def weights(kind, section):
        src, dst = ((att, w_att), (ffn, w_ffn))[kind]
        return pltpu.make_async_copy(src.at[section], dst, w_sem.at[kind])

    def saves(section, early):
        which = (1, 2, 3, 4, 5, 9) if early else (6, 7, 8)
        return [
            pltpu.make_async_copy(local[i], kept[i].at[section], kept_sem.at[i]) for i in which
        ]

    weights(0, 0).start()
    weights(1, 0).start()
    h[...] = h_in[...]
    table[...] = jnp.zeros_like(table)

    @pl.loop(0, SECT)
    def _(section):
        weights(0, section).wait()
        read_vectors(w_att, table, size.bs, size.vec)
        keep_h = pltpu.make_async_copy(h, kept[0].at[section], kept_sem.at[0])
        keep_h.start()
        forward_attention(size, w_att, table, h, mixed, lse, attended, first, normed)
        start_all(saves(section, True))

        @pl.when(section + 1 < SECT)
        def _():
            weights(0, section + 1).start()

        @pl.when(section > 0)
        def _():
            wait_all(saves(section - 1, False))

        weights(1, section).wait()
        keep_h.wait()
        forward_dense(size, w_ffn, table, normed, slope, hidden, second, h)
        start_all(saves(section, False))

        @pl.when(section + 1 < SECT)
        def _():
            weights(1, section + 1).start()

        wait_all(saves(section, True))

    wait_all(saves(SECT - 1, False))
    out[...] = h[...]


def forward_all(att, ffn, h, dps):
    size = Sizes(dps)
    shapes = saved_shapes()
    anywhere = pl.BlockSpec(memory_space=pl.ANY)
    inside = pl.BlockSpec(memory_space=pltpu.VMEM)
    return pl.pallas_call(
        partial(forward_kernel, dps),
        out_shape=[jax.ShapeDtypeStruct(h.shape, h.dtype)]
        + [jax.ShapeDtypeStruct((SECT,) + shape, dtype) for shape, dtype in shapes],
        in_specs=[anywhere, anywhere, inside],
        out_specs=[inside] + [anywhere] * len(shapes),
        scratch_shapes=[pltpu.VMEM(shape, dtype) for shape, dtype in shapes + weight_shapes(size)]
        + [pltpu.SemaphoreType.DMA((2,)), pltpu.SemaphoreType.DMA((len(shapes),))],
        compiler_params=pltpu.CompilerParams(vmem_limit_bytes=48 * 1024 * 1024),
        name="forward_layers",
    )(att, ffn, h)


def backward_kernel(dps, att, ffn, cotangent, *refs):
    size = Sizes(dps)
    kept, refs = refs[:10], refs[10:]
    dh, g_att_out, g_ffn_out = refs[:3]
    refs = refs[3:]
    local, refs = refs[:9], refs[9:]
    tables, w_att, w_ffn, g_att, g_ffn, refs = *refs[:5], refs[5:]
    dtable, dy, dnormed, dlow, dlow_t, dmixed, w_sem, kept_sem, g_sem, table_sem = refs
    h, mixed, lse, attended, first, normed, slope, hidden, second = local

    def weights(kind, section):
        src, dst = ((att, w_att), (ffn, w_ffn))[kind]
        return pltpu.make_async_copy(src.at[section], dst, w_sem.at[kind])

    def loads(section, dense):
        which = (5, 6, 7, 8) if dense else (0, 1, 2, 3, 4)
        return [
            pltpu.make_async_copy(kept[i].at[section], local[i], kept_sem.at[i]) for i in which
        ]

    def results(kind, section):
        src, dst = ((g_att, g_att_out), (g_ffn, g_ffn_out))[kind]
        return pltpu.make_async_copy(src, dst.at[section], g_sem.at[kind])

    last = SECT - 1
    start_all(loads(last, True) + [weights(1, last)])
    get_tables = pltpu.make_async_copy(kept[9], tables, table_sem)
    get_tables.start()
    start_all(loads(last, False) + [weights(0, last)])
    dy[...] = cotangent[...]
    get_tables.wait()

    @pl.loop(0, SECT)
    def _(i):
        section = last - i
        table = tables.at[section]
        wait_all(loads(section, True) + [weights(1, section)])

        @pl.when(i > 0)
        def _():
            results(1, section + 1).wait()

        backward_dense(
            size, w_ffn, table, g_ffn, dtable, dy, second, slope, hidden, normed, dnormed, dlow, dlow_t
        )
        results(1, section).start()

        @pl.when(section > 0)
        def _():
            start_all(loads(section - 1, True) + [weights(1, section - 1)])

        wait_all(loads(section, False) + [weights(0, section)])

        @pl.when(i > 0)
        def _():
            results(0, section + 1).wait()

        backward_attention(
            size,
            w_att,
            table,
            g_att,
            dtable,
            dy,
            first,
            attended,
            mixed,
            lse,
            h,
            dnormed,
            dlow,
            dlow_t,
            dmixed,
        )
        results(0, section).start()

        @pl.when(section > 0)
        def _():
            start_all(loads(section - 1, False) + [weights(0, section - 1)])

    results(0, 0).wait()
    results(1, 0).wait()
    dh[...] = dy[...]


def backward_all(att, ffn, cotangent, kept, dps):
    size = Sizes(dps)
    low, wide = jnp.bfloat16, jnp.float32
    anywhere = pl.BlockSpec(memory_space=pl.ANY)
    inside = pl.BlockSpec(memory_space=pltpu.VMEM)
    weights = weight_shapes(size)
    shapes = saved_shapes()
    scratch = shapes[:9] + [((SECT,) + shapes[9][0], wide)] + weights + weights
    scratch += [
        (shapes[9][0], wide),
        ((WIDE, WIDE), low),
        ((WIDE, WIDE), wide),
        ((WIDE, WIDE), low),
        ((WIDE, WIDE), low),
        ((WIDE, 3 * WIDE), low),
    ]
    return pl.pallas_call(
        partial(backward_kernel, dps),
        out_shape=[jax.ShapeDtypeStruct(cotangent.shape, low)]
        + [jax.ShapeDtypeStruct((SECT,) + shape, dtype) for shape, dtype in weights],
        in_specs=[anywhere, anywhere, inside] + [anywhere] * len(kept),
        out_specs=[inside, anywhere, anywhere],
        scratch_shapes=[pltpu.VMEM(shape, dtype) for shape, dtype in scratch]
        + [
            pltpu.SemaphoreType.DMA((2,)),
            pltpu.SemaphoreType.DMA((9,)),
            pltpu.SemaphoreType.DMA((2,)),
            pltpu.SemaphoreType.DMA(()),
        ],
        compiler_params=pltpu.CompilerParams(vmem_limit_bytes=56 * 1024 * 1024),
        name="backward_layers",
    )(att, ffn, cotangent, *kept)


def by_block(slab):
    split = slab.reshape(slab.shape[:-1] + (SECT, LANES))
    return jnp.moveaxis(split, -2, -3)


def pack_vectors(gains, biases):
    flat = jnp.concatenate([gains, biases], axis=1)
    flat = jnp.pad(flat, ((0, 0), (0, 16 * 512 - flat.shape[1])))
    return flat.reshape(flat.shape[0], 16, 512)


def pack_embedding(matrix, shift):
    wide = matrix.T
    first = jnp.pad(wide[:, L1 + L2 :], ((0, 0), (512 - L3 - GROUPS, 0)))
    return jnp.concatenate(
        [
            shift.T,
            first,
            jnp.pad(wide[:, L1 : L1 + L2], ((0, 0), (256 - L2, 0))),
            jnp.pad(wide[:, :L1], ((0, 0), (256 - L1, 0))),
        ],
        axis=1,
    )


def unpack_embedding(packed):
    matrix = jnp.concatenate(
        [packed[:, 1024 - L1 :], packed[:, 768 - L2 : 768], packed[:, 512 - L3 : 512]], axis=1
    )
    return matrix.T, packed[:, :GROUPS].T


def per_device(
    series,
    groups,
    cotangent,
    embed_weight,
    embed_bias,
    qkv_weight,
    out_weight,
    up_weight,
    down_weight,
    gains,
    biases,
):
    dps = lax.axis_size("dp")
    bs = dps // ZS
    low = jnp.bfloat16
    width = qkv_weight.shape[2]
    rows_qkv, rows_out, rows_up = qkv_weight.shape[1], out_weight.shape[1], up_weight.shape[1]
    rows_down = down_weight.shape[1] * down_weight.shape[2] // width
    n_gains, n_biases = gains.shape[1], biases.shape[1]
    down_low = down_weight[0].astype(low).reshape(-1, 4, width)
    att_in = jnp.concatenate(
        [
            qkv_weight[0].astype(low),
            out_weight[0].astype(low),
            pack_vectors(gains.astype(low), biases.astype(low))[0],
        ]
    )
    ffn_in = jnp.concatenate(
        [up_weight[0].astype(low), jnp.moveaxis(down_low, 1, 0).reshape(rows_down, width)]
    )
    emb_in = pack_embedding(embed_weight.astype(low), embed_bias.astype(low))
    emb_in = jnp.concatenate([emb_in[:, :512], emb_in[:, 512:]])
    att, ffn, emb = gather_all(by_block(att_in), by_block(ffn_in), by_block(emb_in), dps)
    emb = jnp.moveaxis(emb, 0, 3).reshape(dps, 2, -1, 512)
    emb = jnp.concatenate([emb[:, 0], emb[:, 1]], axis=-1).reshape(-1, 1024)
    embedding_matrix, embed_b = unpack_embedding(emb)

    hist = series.shape[1]
    group = groups[0]
    lookback = jnp.where(group == 0, L1, jnp.where(group == 1, L2, L3))

    def aligned(rows):
        return jnp.pad(rows, ((hist - rows.shape[0], 0), (0, 0)))

    chosen = jnp.where(
        group == 0,
        aligned(embedding_matrix[:L1]),
        jnp.where(group == 1, aligned(embedding_matrix[L1 : L1 + L2]), embedding_matrix[L1 + L2 :]),
    )
    shift = embed_b[group].astype(jnp.float32)
    embedded = jnp.einsum("jv,jd->vd", series[0], chosen, preferred_element_type=jnp.float32)
    embedded = (embedded + shift).astype(low)

    block_output, *kept = forward_all(att, ffn, embedded, dps)
    grad_low, att_sums, ffn_sums = backward_all(att, ffn, cotangent[0], kept, dps)
    series_grad = jnp.einsum("vd,jd->jv", grad_low, chosen, preferred_element_type=jnp.float32)
    matrix_grad = jnp.einsum("jv,vd->jd", series[0], grad_low, preferred_element_type=jnp.float32)

    def placed(span, index):
        return jnp.where(group == index, matrix_grad[hist - span :], 0.0)

    matrix_sum = jnp.concatenate([placed(L1, 0), placed(L2, 1), placed(L3, 2)])
    shift_sum = jnp.sum(grad_low.astype(jnp.float32), axis=0)
    shift_sum = jnp.where((jnp.arange(GROUPS) == group)[:, None], shift_sum, 0.0)
    emb_sum = pack_embedding(matrix_sum, shift_sum).astype(low)
    emb_sum = emb_sum.reshape(2, 2, ZS, bs, -1, 8, LANES)
    emb_sum = jnp.moveaxis(jnp.swapaxes(emb_sum, 0, 1), 5, 4)
    emb_sum = emb_sum.reshape(SECT, ZS, bs, -1, LANES)

    att_out, ffn_out, emb_out = fold_all(att_sums, ffn_sums, emb_sum, dps)
    att_out = jnp.moveaxis(att_out, 0, 1).reshape(-1, width).astype(jnp.float32)
    ffn_out = jnp.moveaxis(ffn_out, 0, 1).reshape(-1, width).astype(jnp.float32)
    emb_out = jnp.moveaxis(emb_out.reshape(8, -1, LANES), 0, 1).reshape(-1, 1024)
    embed_w_grad, embed_b_grad = unpack_embedding(emb_out.astype(jnp.float32))
    vec_out = att_out[rows_qkv + rows_out :].reshape(1, -1)
    down_out = jnp.moveaxis(ffn_out[rows_up:].reshape(4, -1, width), 0, 1)
    return (
        block_output[None],
        series_grad[None],
        embed_w_grad,
        embed_b_grad,
        att_out[:rows_qkv][None],
        att_out[rows_qkv : rows_qkv + rows_out][None],
        ffn_out[:rows_up][None],
        down_out.reshape(1, -1, down_weight.shape[2]),
        vec_out[:, :n_gains],
        vec_out[:, n_gains : n_gains + n_biases],
    )


def solution(mesh):
    return jax.shard_map(
        per_device,
        mesh=mesh,
        in_specs=(
            P(("pipe", "dp"), None, None),
            P(("pipe", "dp")),
            P(("pipe", "dp"), None, None),
            P(None, "dp"),
            P(None, "dp"),
            P("pipe", "dp", None),
            P("pipe", "dp", None),
            P("pipe", "dp", None),
            P("pipe", "dp", None),
            P("pipe", "dp"),
            P("pipe", "dp"),
        ),
        out_specs=(
            P(("pipe", "dp"), None, None),
            P(("pipe", "dp"), None, None),
            P(None, ("pipe", "dp")),
            P(None, ("pipe", "dp")),
            P("pipe", "dp", None),
            P("pipe", "dp", None),
            P("pipe", "dp", None),
            P("pipe", "dp", None),
            P("pipe", "dp"),
            P("pipe", "dp"),
        ),
        check_vma=False,
    )
```

```python
from functools import partial
import math

import jax
import jax.numpy as jnp
from jax import lax
from jax.experimental import pallas as pl
from jax.experimental.pallas import tpu as pltpu
from jax.sharding import PartitionSpec as P

HEAD = 64
L1 = 96
L2 = 192
L3 = 336
GROUPS = 3


NORM_EPS = 1e-05


MESH = pl.DeviceIdType.MESH
LANES = 128
ZS = 4
SECT = 4


class Place:
    def __init__(self, dps):
        self.bs = dps // ZS
        pipe = lax.axis_index("pipe")
        dp = lax.axis_index("dp")
        self.pipe, self.dp = pipe, dp
        self.x, self.c = pipe // 2, pipe % 2
        self.z, self.b = dp // self.bs, dp % self.bs
        self.block = self.c * 2 + self.x
        self.x_peer = ((1 - self.x) * 2 + self.c, dp)
        self.core_peer = (self.x * 2 + 1 - self.c, dp)

    def block_of(self, pipe):
        return (pipe % 2) * 2 + pipe // 2

    def pipe_at(self, step):
        return (self.pipe + step) % SECT

    def z_at(self, step):
        return (self.z + step) % ZS

    def b_at(self, step):
        return (self.b + step) % self.bs

    def z_peer(self, step):
        return (self.pipe, self.z_at(step) * self.bs + self.b)

    def b_peer(self, step):
        return (self.pipe, self.z * self.bs + self.b_at(step))

    def greet(self):
        barrier = pltpu.get_barrier_semaphore()
        peers = [(self.pipe_at(k), self.dp) for k in range(1, SECT)]
        peers += [self.z_peer(k) for k in range(1, ZS)]
        peers += [self.b_peer(k) for k in range(1, self.bs)]
        for peer in peers:
            pl.semaphore_signal(barrier, inc=1, device_id=peer, device_id_type=MESH)
        pl.semaphore_wait(barrier, len(peers))


def remote(src, dst, send, recv, peer):
    return pltpu.make_async_remote_copy(
        src_ref=src, dst_ref=dst, send_sem=send, recv_sem=recv, device_id=peer, device_id_type=MESH
    )


def copies_start(copies):
    for copy in copies:
        copy.start()


def copies_wait(copies):
    for copy in copies:
        copy.wait()


class Spread:
    def __init__(self, at, out, send, recv):
        self.at, self.out, self.send, self.recv = at, out, send, recv
        nb = at.bs - 1
        self.slot_z = 0
        self.slot_b1 = ZS - 1
        self.slot_x1 = self.slot_b1 + nb
        self.slot_x2 = self.slot_x1 + 1
        self.slot_b2 = self.slot_x2 + 1
        self.slot_c = self.slot_b2 + nb
        self.half = ZS // 2

    @staticmethod
    def slots(bs):
        return ZS - 1 + 2 * (bs - 1) + 3

    def copy(self, region, slot, peer):
        return remote(region, region, self.send.at[slot], self.recv.at[slot], peer)

    def copies(self, stage, back):
        at, out, half = self.at, self.out, self.half
        x_block = at.c * 2 + 1 - at.x if back else at.block
        if stage == 0:
            return [
                self.copy(
                    out.at[at.block, at.z_at(ZS - k) if back else at.z, at.b],
                    self.slot_z + k - 1,
                    at.z_peer(k),
                )
                for k in range(1, ZS)
            ]
        if stage == 3:
            core = 1 - at.c if back else at.c
            return [self.copy(out.at[pl.ds(core * 2, 2)], self.slot_c, at.core_peer)]
        copies = []
        for k in range(1, at.bs):
            b = at.b_at(at.bs - k) if back else at.b
            if stage == 1:
                region, slot = out.at[at.block, pl.ds(0, half), b], self.slot_b1
            else:
                region, slot = out.at[pl.ds(at.c * 2, 2), pl.ds(half, half), b], self.slot_b2
            copies.append(self.copy(region, slot + k - 1, at.b_peer(k)))
        if stage == 1:
            region, slot = out.at[x_block, pl.ds(half, half), at.b], self.slot_x1
        else:
            region, slot = out.at[x_block, pl.ds(0, half)], self.slot_x2
        copies.append(self.copy(region, slot, at.x_peer))
        return copies

    def start(self, stage):
        copies_start(self.copies(stage, False))

    def land(self, stage):
        for copy in self.copies(stage, True):
            copy.wait_recv()
        for copy in self.copies(stage, False):
            copy.wait_send()

    def move(self, stage):
        self.land(stage)
        self.start(stage + 1)


class Fold:
    def __init__(self, at, grads, total, bufs, final, send, recv, credit):
        self.at, self.grads, self.total, self.bufs, self.final = at, grads, total, bufs, final
        self.send, self.recv, self.credit = send, recv, credit
        self.half = ZS // 2
        nb = at.bs - 1
        self.slot_c = 0
        self.slot_x1 = 1
        self.slot_b1 = 2
        self.slot_x2 = 2 + nb
        self.slot_b2 = 3 + nb
        self.slot_z = 3 + 2 * nb

    @staticmethod
    def slots(bs):
        return 3 + 2 * (bs - 1) + ZS - 1

    @staticmethod
    def buffers(bs, rows):
        half = ZS // 2
        nb = max(bs - 1, 1)
        return [
            (2, ZS, bs, rows, LANES),
            (half, bs, rows, LANES),
            (nb, 2, half, rows, LANES),
            (half, rows, LANES),
            (nb, half, rows, LANES),
            (ZS - 1, rows, LANES),
        ]

    def parts(self, stage):
        at, half, total, bufs = self.at, self.half, self.total, self.bufs
        if stage == 0:
            other = self.grads.at[pl.ds((1 - at.c) * 2, 2)]
            return [(other, bufs[0], self.slot_c, at.core_peer, at.core_peer)]
        if stage == 3:
            return [
                (
                    total.at[at.x, at.z_at(k), at.b],
                    bufs[5].at[k - 1],
                    self.slot_z + k - 1,
                    at.z_peer(k),
                    at.z_peer(ZS - k),
                )
                for k in range(1, ZS)
            ]
        found = []
        for k in range(1, at.bs):
            if stage == 1:
                src, buf, slot = total.at[:, pl.ds(half, half), at.b_at(k)], bufs[2], self.slot_b1
            else:
                src, buf, slot = total.at[at.x, pl.ds(0, half), at.b_at(k)], bufs[4], self.slot_b2
            found.append((src, buf.at[k - 1], slot + k - 1, at.b_peer(k), at.b_peer(at.bs - k)))
        if stage == 1:
            src, buf, slot = total.at[1 - at.x, pl.ds(0, half)], bufs[1], self.slot_x1
        else:
            src, buf, slot = total.at[1 - at.x, pl.ds(half, half), at.b], bufs[3], self.slot_x2
        found.append((src, buf, slot, at.x_peer, at.x_peer))
        return found

    def start(self, stage, again):
        for src, buf, slot, to, _ in self.parts(stage):
            if again is not False:

                @pl.when(again)
                def _():
                    pl.semaphore_wait(self.credit.at[slot], 1)

            remote(src, buf, self.send.at[slot], self.recv.at[slot], to).start()

    def land(self, stage, more):
        at, half, bs = self.at, self.half, self.at.bs
        total, bufs = self.total, self.bufs
        for src, buf, slot, to, _ in self.parts(stage):
            remote(src, buf, self.send.at[slot], self.recv.at[slot], to).wait()
        if stage == 0:

            @pl.loop(0, 2 * ZS * bs)
            def _(i):
                z, b = i // bs % ZS, i % bs
                x = i // (ZS * bs)
                total[x, z, b] = self.grads[at.c * 2 + x, z, b] + bufs[0][x, z, b]

        elif stage == 1:

            @pl.loop(0, half * bs)
            def _(i):
                z, b = i // bs, i % bs
                total[at.x, z, b] = total[at.x, z, b] + bufs[1][z, b]

            @pl.loop(0, 2 * half)
            def _(i):
                x, z = i // half, i % half
                for k in range(bs - 1):
                    total[x, half + z, at.b] = total[x, half + z, at.b] + bufs[2][k, x, z]

        elif stage == 2:

            @pl.loop(0, half)
            def _(z):
                total[at.x, half + z, at.b] = total[at.x, half + z, at.b] + bufs[3][z]
                for k in range(bs - 1):
                    total[at.x, z, at.b] = total[at.x, z, at.b] + bufs[4][k, z]

        else:
            done = total[at.x, at.z, at.b].astype(jnp.float32)
            for k in range(ZS - 1):
                done = done + bufs[5][k].astype(jnp.float32)
            self.final[...] = done.astype(self.final.dtype)
        if more is not False:

            @pl.when(more)
            def _():
                for _, _, slot, _, origin in self.parts(stage):
                    pl.semaphore_signal(
                        self.credit.at[slot], inc=1, device_id=origin, device_id_type=MESH
                    )

    def move(self, stage, again, more):
        self.land(stage, more)
        self.start(stage + 1, again)


HALF = 256
WIDE = 512
QKV_TILE = 384
VEC_ROWS = 16


def dot_nt(a, b):
    return lax.dot_general(a, b, (((1,), (1,)), ((), ())), preferred_element_type=jnp.float32)


def dot_nn(a, b):
    return lax.dot_general(a, b, (((1,), (0,)), ((), ())), preferred_element_type=jnp.float32)


def dot_tn(a, b):
    return lax.dot_general(a, b, (((0,), (0,)), ((), ())), preferred_element_type=jnp.float32)


def aligned(index, unit):
    return pl.multiple_of(index, unit)


def rows_of(ref, bs, first, count, start, rows, blocks=range(SECT)):
    parts = []
    for i in range(count):
        d = first + i
        place = (d // bs, d % bs)
        parts.append(
            jnp.concatenate(
                [ref[(lb,) + place + (pl.ds(start, rows), slice(None))] for lb in blocks], axis=1
            )
        )
    return parts[0] if count == 1 else jnp.concatenate(parts, axis=0)


def put_rows(ref, bs, first, count, start, rows, value, block=0):
    value = value.astype(ref.dtype)
    for i in range(count):
        d = first + i
        place = (d // bs, d % bs)
        for lane in range(value.shape[1] // LANES):
            ref[(block + lane,) + place + (pl.ds(start, rows), slice(None))] = value[
                i * rows : (i + 1) * rows, lane * LANES : (lane + 1) * LANES
            ]


def vector_pieces(dps):
    n_gains, n_biases = 2 * WIDE // dps, 10 * WIDE // dps
    starts = [(0, 0), (0, 2), (1, 0), (1, 2), (2, 0), (2, 1), (2, 2), (2, 3), (3, 0), (3, 2)]
    pieces = []
    for d in range(dps):
        at = 0
        while at < n_gains + n_biases:
            if at < n_gains:
                index = d * n_gains + at
                row, column = (1, 3)[index // WIDE], WIDE + index % WIDE
                left = n_gains - at
            else:
                index = d * n_biases + at - n_gains
                row, part = starts[index // WIDE]
                column = part * WIDE + index % WIDE
                left = n_gains + n_biases - at
            size = min(left, LANES - at % LANES, LANES - column % LANES)
            pieces.append((d, at // WIDE, at % WIDE, row, column, size))
            at += size
    return pieces


def read_vectors(ref, table, bs, start):
    dps = ZS * bs
    tiles = {}
    for d, row, lane, to_row, to_lane, size in vector_pieces(dps):
        key = (d, lane // LANES)
        if key not in tiles:
            tile = ref[lane // LANES, d // bs, d % bs, start : start + VEC_ROWS, :]
            tiles[key] = tile.astype(jnp.float32)
        off = lane % LANES
        table[to_row : to_row + 1, to_lane : to_lane + size] = tiles[key][
            row : row + 1, off : off + size
        ]


def write_vectors(ref, table, bs, start):
    dps = ZS * bs
    found = {}
    for d, row, lane, to_row, to_lane, size in vector_pieces(dps):
        piece = table[to_row : to_row + 1, to_lane : to_lane + size]
        found.setdefault((d, lane // LANES), {}).setdefault(row, []).append(piece)
    row_id = lax.broadcasted_iota(jnp.int32, (VEC_ROWS, LANES), 0)
    for d in range(dps):
        for lb in range(SECT):
            tile = jnp.zeros((VEC_ROWS, LANES), jnp.float32)
            for row, pieces in found.get((d, lb), {}).items():
                have = sum(piece.shape[1] for piece in pieces)
                if have < LANES:
                    pieces = pieces + [jnp.zeros((1, LANES - have), jnp.float32)]
                line = pieces[0] if len(pieces) == 1 else jnp.concatenate(pieces, axis=1)
                tile = jnp.where(row_id == row, line, tile)
            ref[lb, d // bs, d % bs, start : start + VEC_ROWS, :] = tile.astype(ref.dtype)


def normalize(x, gain, shift):
    mean = jnp.mean(x, axis=1, keepdims=True)
    centred = x - mean
    scale = lax.rsqrt(jnp.mean(centred * centred, axis=1, keepdims=True) + NORM_EPS)
    return centred * scale * gain + shift


def normalize_back(x, grad, gain):
    mean = jnp.mean(x, axis=1, keepdims=True)
    centred = x - mean
    scale = lax.rsqrt(jnp.mean(centred * centred, axis=1, keepdims=True) + NORM_EPS)
    unit = centred * scale
    inner = grad * gain
    first = jnp.mean(inner, axis=1, keepdims=True)
    second = jnp.mean(inner * unit, axis=1, keepdims=True)
    out = scale * (inner - first - unit * second)
    return out, jnp.sum(grad * unit, axis=0, keepdims=True), jnp.sum(grad, axis=0, keepdims=True)


def gelu_pair(u):
    bell = jnp.exp(-0.5 * (u * u))
    t = 1.0 / (1.0 + 0.23164188824 * jnp.abs(u))
    tail = 0.5307027145 * t
    tail = (tail - 0.7265760135) * t
    tail = (tail + 0.7107068705) * t
    tail = (tail - 0.142248368) * t
    tail = (tail + 0.127414796) * t * bell
    below = jnp.where(u < 0.0, tail, 1.0 - tail)
    return u * below, below + u * (0.3989422804014327 * bell)


def head_masks(scale):
    lane = lax.broadcasted_iota(jnp.int32, (1, LANES), 1)
    first = jnp.where(lane < HEAD, scale, 0.0).astype(jnp.bfloat16)
    second = jnp.where(lane < HEAD, 0.0, scale).astype(jnp.bfloat16)
    return first, second


class Sizes:
    def __init__(self, dps):
        self.dps, self.bs = dps, dps // ZS
        self.qkv, self.out, self.up, self.down = (
            3 * WIDE // dps,
            WIDE // dps,
            4 * WIDE // dps,
            WIDE // dps,
        )
        self.vec = self.qkv + self.out
        self.att = self.vec + VEC_ROWS
        self.ffn = self.up + 4 * self.down


def forward_attention(size, w, table, h, mixed, lse, attended, first, normed):
    bs = size.bs
    per_tile = QKV_TILE // size.qkv

    @pl.loop(0, 3 * WIDE // QKV_TILE)
    def _(t):
        columns = pl.ds(aligned(t * QKV_TILE, LANES), QKV_TILE)
        matrix = rows_of(w, bs, t * per_tile, per_tile, 0, size.qkv)
        mixed[:, columns] = (dot_nt(h[...], matrix) + table[0:1, columns]).astype(mixed.dtype)

    @pl.loop(0, 8)
    def _(i):
        pair, part = i // 2, i % 2
        rows = pl.ds(aligned(part * HALF, HALF), HALF)
        lane = aligned(pair * LANES, LANES)
        queries = mixed[rows, pl.ds(lane, LANES)]
        key_rows = mixed[:, pl.ds(WIDE + lane, LANES)]
        values = mixed[:, pl.ds(2 * WIDE + lane, LANES)].T
        joined = []
        for head, mask in enumerate(head_masks(1.0 / math.sqrt(HEAD))):
            scores = dot_nt(key_rows, queries * mask)
            top = jnp.max(scores, axis=0, keepdims=True)
            probs = jnp.exp(scores - top)
            total = jnp.sum(probs, axis=0, keepdims=True)
            lse[2 * pair + head, :, rows] = top + jnp.log(total)
            probs = (probs * (1.0 / total)).astype(jnp.bfloat16)
            joined.append(dot_nn(values[head * HEAD : (head + 1) * HEAD], probs))
        joined = jnp.concatenate(joined, axis=0).T
        attended[rows, pl.ds(lane, LANES)] = joined.astype(attended.dtype)

    @pl.loop(0, 2)
    def _(part):
        rows = pl.ds(aligned(part * HALF, HALF), HALF)
        matrix = rows_of(w, bs, 0, size.dps, size.qkv, size.out)
        out = dot_nt(attended[rows, :], matrix) + table[1:2, 0:WIDE]
        total = h[rows, :].astype(jnp.float32) + out
        first[rows, :] = total
        normed[rows, :] = normalize(
            total, table[1:2, WIDE : 2 * WIDE], table[1:2, 2 * WIDE : 3 * WIDE]
        ).astype(normed.dtype)


def forward_dense(size, w, table, normed, slope, hidden, second, h):
    bs = size.bs
    per_tile = HALF // size.up

    @pl.loop(0, 4 * WIDE // HALF)
    def _(j):
        columns = pl.ds(aligned(j * HALF, HALF), HALF)
        matrix = rows_of(w, bs, j * per_tile, per_tile, 0, size.up)
        upper = dot_nt(normed[...], matrix) + table[2:3, columns]
        value, grad = gelu_pair(upper)
        hidden[:, columns] = value.astype(hidden.dtype)
        slope[:, columns] = grad.astype(slope.dtype)

    @pl.loop(0, 2)
    def _(part):
        rows = pl.ds(aligned(part * HALF, HALF), HALF)
        total = normed[rows, :].astype(jnp.float32) + table[3:4, 0:WIDE]
        for j in range(4):
            matrix = rows_of(w, bs, 0, size.dps, size.up + j * size.down, size.down)
            total = total + dot_nt(hidden[rows, j * WIDE : (j + 1) * WIDE], matrix)
        second[rows, :] = total
        h[rows, :] = normalize(
            total, table[3:4, WIDE : 2 * WIDE], table[3:4, 2 * WIDE : 3 * WIDE]
        ).astype(h.dtype)


def backward_dense(
    size, w, table, grads, dtable, dy, second, slope, hidden, normed, dnormed, dlow, dlow_t, between
):
    bs = size.bs
    per_tile = HALF // size.up
    dtable[...] = jnp.zeros_like(dtable)

    @pl.loop(0, 2)
    def _(part):
        rows = pl.ds(aligned(part * HALF, HALF), HALF)
        grad, gain_sum, shift_sum = normalize_back(
            second[rows, :], dy[rows, :].astype(jnp.float32), table[3:4, WIDE : 2 * WIDE]
        )
        dnormed[rows, :] = grad
        dlow[rows, :] = grad.astype(dlow.dtype)
        dtable[3:4, 0:WIDE] += jnp.sum(grad, axis=0, keepdims=True)
        dtable[3:4, WIDE : 2 * WIDE] += gain_sum
        dtable[3:4, 2 * WIDE : 3 * WIDE] += shift_sum

    dlow_t[...] = dlow[...].T

    def step(j):
        columns = pl.ds(aligned(j * HALF, HALF), HALF)
        block = 2 * (j % 2)
        start = aligned(size.up + j // 2 * size.down, 16)
        matrix = rows_of(w, bs, 0, size.dps, start, size.down, (block, block + 1))
        dupper = dot_nn(dlow[...], matrix) * slope[:, columns].astype(jnp.float32)
        dtable[2:3, columns] = jnp.sum(dupper, axis=0, keepdims=True)
        dup = dupper.astype(jnp.bfloat16)
        put_rows(
            grads, bs, 0, size.dps, start, size.down, dot_nn(dlow_t[...], hidden[:, columns]), block
        )
        put_rows(grads, bs, j * per_tile, per_tile, 0, size.up, dot_tn(dup, normed[...]))
        matrix = rows_of(w, bs, j * per_tile, per_tile, 0, size.up)
        dnormed[...] += dot_nn(dup, matrix)

    steps = 4 * WIDE // HALF
    pl.loop(0, steps // 2)(step)
    between()
    pl.loop(steps // 2, steps)(step)


def backward_attention(
    size,
    w,
    table,
    grads,
    dtable,
    dy,
    first,
    attended,
    mixed,
    lse,
    h,
    dnormed,
    dlow,
    dlow_t,
    dmixed,
    between,
):
    bs = size.bs

    @pl.loop(0, 2)
    def _(part):
        rows = pl.ds(aligned(part * HALF, HALF), HALF)
        grad, gain_sum, shift_sum = normalize_back(
            first[rows, :], dnormed[rows, :], table[1:2, WIDE : 2 * WIDE]
        )
        dnormed[rows, :] = grad
        dlow[rows, :] = grad.astype(dlow.dtype)
        dtable[1:2, 0:WIDE] += jnp.sum(grad, axis=0, keepdims=True)
        dtable[1:2, WIDE : 2 * WIDE] += gain_sum
        dtable[1:2, 2 * WIDE : 3 * WIDE] += shift_sum

    dlow_t[...] = dlow[...].T
    for block in (0, 2):
        columns = slice(block * LANES, (block + 2) * LANES)
        value = dot_nn(dlow_t[...], attended[:, columns])
        put_rows(grads, bs, 0, size.dps, size.qkv, size.out, value, block)

    @pl.loop(0, 2)
    def _(part):
        rows = pl.ds(aligned(part * HALF, HALF), HALF)
        matrix = rows_of(w, bs, 0, size.dps, size.qkv, size.out)
        dlow[rows, :] = dot_nn(dlow[rows, :], matrix).astype(dlow.dtype)

    scale = 1.0 / math.sqrt(HEAD)

    def step(pair):
        lane = aligned(pair * LANES, LANES)
        columns = pl.ds(lane, LANES)
        key_rows = mixed[:, pl.ds(WIDE + lane, LANES)]
        keys_t = key_rows.T
        values = mixed[:, pl.ds(2 * WIDE + lane, LANES)]
        dkeys = jnp.zeros((WIDE, LANES), jnp.float32)
        dvalues = jnp.zeros((WIDE, LANES), jnp.float32)
        for part in range(2):
            rows = slice(part * HALF, (part + 1) * HALF)
            queries = mixed[rows, columns]
            grad_out = dlow[rows, columns]
            dqueries = []
            for head in range(2):
                query = queries * head_masks(scale)[head]
                grad = grad_out * head_masks(1.0)[head]
                probs = jnp.exp(dot_nt(key_rows, query) - lse[2 * pair + head, :, rows])
                dprobs = dot_nt(values, grad)
                delta = jnp.sum(probs * dprobs, axis=0, keepdims=True)
                dscores = (probs * (dprobs - delta)).astype(jnp.bfloat16)
                dvalues = dvalues + dot_nn(probs.astype(jnp.bfloat16), grad)
                dkeys = dkeys + dot_nn(dscores, query)
                dqueries.append(dot_nn(keys_t[head * HEAD : (head + 1) * HEAD], dscores))
            dquery = jnp.concatenate(dqueries, axis=0).T * scale
            dtable[0:1, columns] += jnp.sum(dquery, axis=0, keepdims=True)
            dmixed[rows, columns] = dquery.astype(dmixed.dtype)
        dmixed[:, pl.ds(WIDE + lane, LANES)] = dkeys.astype(dmixed.dtype)
        dmixed[:, pl.ds(2 * WIDE + lane, LANES)] = dvalues.astype(dmixed.dtype)
        dtable[0:1, pl.ds(2 * WIDE + lane, LANES)] = jnp.sum(dvalues, axis=0, keepdims=True)

    pl.loop(0, 2)(step)
    between()
    pl.loop(2, 4)(step)
    per_tile = QKV_TILE // size.qkv

    @pl.loop(0, 3 * WIDE // QKV_TILE)
    def _(t):
        columns = pl.ds(aligned(t * QKV_TILE, LANES), QKV_TILE)
        grad = dmixed[:, columns]
        put_rows(grads, bs, t * per_tile, per_tile, 0, size.qkv, dot_tn(grad, h[...]))
        matrix = rows_of(w, bs, t * per_tile, per_tile, 0, size.qkv)
        dnormed[...] += dot_nn(grad, matrix)

    dy[...] = dnormed[...].astype(dy.dtype)
    write_vectors(grads, dtable, bs, size.vec)


WINDOW = 384


def embed(size, emb, pick, x, wsel, h):
    rows = WIDE // size.dps
    first = rows_of(emb, size.bs, 0, size.dps, 0, rows)
    second = rows_of(emb, size.bs, 0, size.dps, rows, rows)
    long, middle, short = (pick[g : g + 1, :] for g in (2, 1, 0))
    wide = jnp.concatenate(
        [
            first[:, LANES : 2 * LANES] * long,
            first[:, 2 * LANES : 3 * LANES] * long + second[:, :LANES] * middle,
            first[:, 3 * LANES :] * long
            + second[:, LANES : 2 * LANES] * middle
            + second[:, 3 * LANES :] * short,
        ],
        axis=1,
    )
    wsel[...] = wide.T
    matrix = jnp.concatenate([wide, first[:, :LANES]], axis=1)
    h[...] = dot_nt(x[...], matrix).astype(h.dtype)


def embed_back(size, pick, x, wsel, dh, grads, series_grad):
    history = series_grad.shape[0]
    series_grad[...] = dot_nt(wsel[...], dh[...])[WINDOW - history :]
    sums = dot_tn(dh[...], x[...])
    long, middle, short = (pick[g : g + 1, :].astype(jnp.float32) for g in (2, 1, 0))
    parts = [sums[:, i * LANES : (i + 1) * LANES] for i in range(4)]
    parts = [
        parts[3],
        parts[0] * long,
        parts[1] * long,
        parts[2] * long,
        parts[1] * middle,
        parts[2] * middle,
        jnp.zeros_like(parts[0]),
        parts[2] * short,
    ]
    rows = WIDE // (SECT * size.dps)
    for pipe in range(SECT):
        block = (pipe % 2) * 2 + pipe // 2
        for dp in range(size.dps):
            start = (pipe * size.dps + dp) * rows
            piece = jnp.concatenate([part[start : start + rows] for part in parts], axis=0)
            grads[block, dp // size.bs, dp % size.bs] = piece.astype(grads.dtype)


def saved_shapes():
    low, wide = jnp.bfloat16, jnp.float32
    return [
        ((WIDE, WIDE), low),
        ((WIDE, 3 * WIDE), low),
        ((2 * SECT, 1, WIDE), wide),
        ((WIDE, WIDE), low),
        ((WIDE, WIDE), wide),
        ((WIDE, WIDE), low),
        ((WIDE, 4 * WIDE), low),
        ((WIDE, 4 * WIDE), low),
        ((WIDE, WIDE), wide),
        ((SECT, 4 * WIDE), wide),
    ]


def chunk_shape(size, rows):
    return ((SECT, ZS, size.bs, rows, LANES), jnp.bfloat16)


def forward_kernel(dps, att_in, ffn_in, emb_in, x, pick, *refs):
    size = Sizes(dps)
    out, att, ffn, emb, wsel = refs[:5]
    kept, local, refs = refs[5:15], refs[15:25], refs[25:]
    w_att, w_ffn, w_emb, w_sem, kept_sem, own_sem, p_send, p_recv, send, recv = refs
    h, mixed, lse, attended, first, normed, slope, hidden, second, table = local
    at = Place(dps)
    pieces, wholes, buffers = (att_in, ffn_in), (att, ffn), (w_att, w_ffn)

    own = [
        pltpu.make_async_copy(
            emb_in.at[at.block], emb.at[at.block, at.z, at.b], own_sem.at[2]
        ),
    ] + [
        pltpu.make_async_copy(
            pieces[kind].at[at.block],
            wholes[kind].at[at.pipe, at.block, at.z, at.b],
            own_sem.at[kind],
        )
        for kind in range(2)
    ]
    copies_start(own)

    def split(kind, back):
        copies = []
        for k in range(1, SECT):
            if back:
                region = wholes[kind].at[at.pipe_at(SECT - k), at.block, at.z, at.b]
                src = region
            else:
                block = at.block_of(at.pipe_at(k))
                region = wholes[kind].at[at.pipe, block, at.z, at.b]
                src = pieces[kind].at[block]
            sems = p_send.at[kind, k - 1], p_recv.at[kind, k - 1]
            copies.append(remote(src, region, *sems, (at.pipe_at(k), at.dp)))
        return copies

    def split_land(kind):
        for copy in split(kind, True):
            copy.wait_recv()
        for copy in split(kind, False):
            copy.wait_send()

    def chunk(kind, section):
        number = 1 + 2 * section + kind
        return Spread(at, wholes[kind].at[section], send.at[number], recv.at[number])

    def weights(kind, section, core):
        blocks = pl.ds(core * 2, 2)
        return pltpu.make_async_copy(
            wholes[kind].at[section, blocks], buffers[kind].at[blocks], w_sem.at[kind, core]
        )

    def saves(section, early):
        which = (1, 2, 3, 4, 5, 9) if early else (6, 7, 8)
        return [
            pltpu.make_async_copy(local[i], kept[i].at[section], kept_sem.at[i]) for i in which
        ]

    at.greet()
    copies_start(split(0, False) + split(1, False))
    start = Spread(at, emb, send.at[0], recv.at[0])
    own[0].wait()
    start.start(0)
    own[1].wait()
    split_land(0)
    chunk(0, 0).start(0)
    table[...] = jnp.zeros_like(table)

    start.move(0)
    chunk(0, 0).move(0)
    own[2].wait()
    split_land(1)
    chunk(1, 0).start(0)

    start.move(1)
    chunk(0, 0).move(1)
    chunk(1, 0).move(0)
    chunk(0, 1).start(0)

    start.move(2)

    @pl.loop(0, SECT)
    def _(section):
        chunk(0, section).move(2)
        weights(0, section, at.c).start()
        chunk(1, section).move(1)

        @pl.when(section + 1 < SECT)
        def _():
            chunk(0, section + 1).move(0)
            chunk(1, section + 1).start(0)

        @pl.when(section == 0)
        def _():
            start.land(3)
            get = pltpu.make_async_copy(emb, w_emb, own_sem.at[2])
            get.start()
            get.wait()
            embed(size, w_emb, pick, x, wsel, h)

        chunk(0, section).land(3)
        weights(0, section, 1 - at.c).start()
        keep_h = pltpu.make_async_copy(h, kept[0].at[section], kept_sem.at[0])
        keep_h.start()
        weights(0, section, at.c).wait()
        weights(0, section, 1 - at.c).wait()
        read_vectors(w_att, table, size.bs, size.vec)
        forward_attention(size, w_att, table, h, mixed, lse, attended, first, normed)
        copies_start(saves(section, True))

        chunk(1, section).move(2)
        weights(1, section, at.c).start()

        @pl.when(section + 1 < SECT)
        def _():
            chunk(0, section + 1).move(1)
            chunk(1, section + 1).move(0)

        @pl.when(section + 2 < SECT)
        def _():
            chunk(0, section + 2).start(0)

        @pl.when(section > 0)
        def _():
            copies_wait(saves(section - 1, False))

        chunk(1, section).land(3)
        weights(1, section, 1 - at.c).start()
        keep_h.wait()
        weights(1, section, at.c).wait()
        weights(1, section, 1 - at.c).wait()
        forward_dense(size, w_ffn, table, normed, slope, hidden, second, h)
        copies_start(saves(section, False))
        copies_wait(saves(section, True))

    copies_wait(saves(SECT - 1, False))
    out[...] = h[...]


def forward_all(att_in, ffn_in, emb_in, x, pick, dps):
    size = Sizes(dps)
    low = jnp.bfloat16
    shapes = saved_shapes()
    chunks = [chunk_shape(size, piece.shape[1]) for piece in (att_in, ffn_in, emb_in)]
    anywhere = pl.BlockSpec(memory_space=pl.ANY)
    inside = pl.BlockSpec(memory_space=pltpu.VMEM)
    outs = [((WIDE, WIDE), low)]
    outs += [((SECT,) + shape, dtype) for shape, dtype in chunks[:2]] + [chunks[2]]
    outs += [((WINDOW, WIDE), low)]
    outs += [((SECT,) + shape, dtype) for shape, dtype in shapes]
    slots = Spread.slots(size.bs)
    dma = pltpu.SemaphoreType.DMA
    return pl.pallas_call(
        partial(forward_kernel, dps),
        out_shape=[jax.ShapeDtypeStruct(shape, dtype) for shape, dtype in outs],
        in_specs=[anywhere] * 3 + [inside] * 2,
        out_specs=[inside] + [anywhere] * 3 + [inside] + [anywhere] * len(shapes),
        scratch_shapes=[pltpu.VMEM(shape, dtype) for shape, dtype in shapes + chunks]
        + [
            dma((2, 2)),
            dma((len(shapes),)),
            dma((3,)),
            dma((2, SECT - 1)),
            dma((2, SECT - 1)),
            dma((1 + 2 * SECT, slots)),
            dma((1 + 2 * SECT, slots)),
        ],
        compiler_params=pltpu.CompilerParams(
            collective_id=0, has_side_effects=True, vmem_limit_bytes=48 * 1024 * 1024
        ),
        name="gather_forward",
    )(att_in, ffn_in, emb_in, x, pick)


def backward_kernel(dps, att, ffn, cotangent, x, pick, wsel, *refs):
    size = Sizes(dps)
    kept, refs = refs[:10], refs[10:]
    series_grad, att_out, ffn_out, emb_out = refs[:4]
    refs = refs[4:]
    local, refs = refs[:9], refs[9:]
    tables, w_att, w_ffn, dtable, dy, dnormed, dlow, dlow_t, dmixed = refs[:9]
    refs = refs[9:]
    kinds = [(refs[9 * k], refs[9 * k + 1], refs[9 * k + 2 : 9 * k + 8], refs[9 * k + 8]) for k in range(3)]
    refs = refs[27:]
    w_sem, kept_sem, table_sem, out_sem, p_send, p_recv, send, recv, credit = refs
    h, mixed, lse, attended, first, normed, slope, hidden, second = local
    at = Place(dps)
    last = SECT - 1

    def weights(kind, section):
        src, dst = ((att, w_att), (ffn, w_ffn))[kind]
        return pltpu.make_async_copy(src.at[section], dst, w_sem.at[kind])

    def loads(section, dense):
        which = (5, 6, 7, 8) if dense else (0, 1, 2, 3, 4)
        return [
            pltpu.make_async_copy(kept[i].at[section], local[i], kept_sem.at[i]) for i in which
        ]

    def chunk(kind, i):
        grads, totals, bufs, finals = kinds[kind]
        return Fold(
            at, grads, totals.at[i % 2], bufs, finals.at[i], send.at[kind], recv.at[kind], credit.at[kind]
        )

    def begin(kind, i):
        chunk(kind, i).start(0, i > 0)

    def move(kind, i, stage):
        chunk(kind, i).move(stage, i > 0, i < last)

    def hand_over(kind, i):
        landing = (att_out, ffn_out)[kind].at[at.block]
        final = kinds[kind][3].at[i]
        return (
            pltpu.make_async_copy(final, landing, out_sem.at[kind]),
            remote(final, landing, p_send.at[kind, i], p_recv.at[kind, at.pipe], (last - i, at.dp)),
        )

    def finish(kind, i):
        chunk(kind, i).land(3, i < last)
        here, away = hand_over(kind, i)

        @pl.when(at.pipe == last - i)
        def _():
            here.start()

        @pl.when(at.pipe != last - i)
        def _():
            away.start()

    copies_start(loads(last, True) + [weights(1, last)])
    get_tables = pltpu.make_async_copy(kept[9], tables, table_sem)
    get_tables.start()
    copies_start(loads(last, False) + [weights(0, last)])
    dy[...] = cotangent[...]
    at.greet()
    get_tables.wait()

    @pl.loop(0, SECT)
    def _(i):
        section = last - i
        table = tables.at[section]

        def between_dense():
            @pl.when(i > 1)
            def _():
                finish(1, i - 2)
                move(0, i - 2, 2)

            @pl.when(i > 0)
            def _():
                move(1, i - 1, 1)
                move(0, i - 1, 0)

        def between_attention():
            @pl.when(i > 1)
            def _():
                finish(0, i - 2)

            @pl.when(i > 0)
            def _():
                move(1, i - 1, 2)
                move(0, i - 1, 1)

            move(1, i, 0)

        copies_wait(loads(section, True) + [weights(1, section)])
        backward_dense(
            size,
            w_ffn,
            table,
            kinds[1][0],
            dtable,
            dy,
            second,
            slope,
            hidden,
            normed,
            dnormed,
            dlow,
            dlow_t,
            between_dense,
        )
        begin(1, i)

        @pl.when(section > 0)
        def _():
            copies_start(loads(section - 1, True) + [weights(1, section - 1)])

        copies_wait(loads(section, False) + [weights(0, section)])
        backward_attention(
            size,
            w_att,
            table,
            kinds[0][0],
            dtable,
            dy,
            first,
            attended,
            mixed,
            lse,
            h,
            dnormed,
            dlow,
            dlow_t,
            dmixed,
            between_attention,
        )
        begin(0, i)

        @pl.when(section > 0)
        def _():
            copies_start(loads(section - 1, False) + [weights(0, section - 1)])

    end = Fold(
        at,
        kinds[2][0],
        kinds[2][1].at[0],
        kinds[2][2],
        kinds[2][3].at[0],
        send.at[2],
        recv.at[2],
        credit.at[2],
    )
    finish(1, last - 1)
    move(0, last - 1, 2)
    move(1, last, 1)
    move(0, last, 0)
    embed_back(size, pick, x, wsel, dy, kinds[2][0], series_grad)
    end.start(0, False)
    finish(0, last - 1)
    move(1, last, 2)
    move(0, last, 1)
    end.move(0, False, False)
    finish(1, last)
    move(0, last, 2)
    end.move(1, False, False)
    finish(0, last)
    end.move(2, False, False)
    end.land(3, False)
    emb_out[...] = kinds[2][3][0]

    for kind, out in enumerate((att_out, ffn_out)):
        for i in range(SECT):
            here, away = hand_over(kind, i)

            @pl.when(at.pipe == last - i)
            def _():
                here.wait()

            @pl.when(at.pipe != last - i)
            def _():
                away.wait_send()

        for k in range(1, SECT):
            other = at.pipe_at(k)
            landing = out.at[at.block_of(other)]
            sems = p_send.at[kind, 0], p_recv.at[kind, other]
            remote(landing, landing, *sems, (other, at.dp)).wait_recv()


def backward_all(att, ffn, cotangent, x, pick, wsel, kept, history, dps):
    size = Sizes(dps)
    low, wide = jnp.bfloat16, jnp.float32
    anywhere = pl.BlockSpec(memory_space=pl.ANY)
    inside = pl.BlockSpec(memory_space=pltpu.VMEM)
    shapes = saved_shapes()
    rows_emb = 8 * WIDE // (SECT * dps)
    scratch = shapes[:9] + [((SECT,) + shapes[9][0], wide)]
    scratch += [chunk_shape(size, size.att), chunk_shape(size, size.ffn)]
    scratch += [
        (shapes[9][0], wide),
        ((WIDE, WIDE), low),
        ((WIDE, WIDE), wide),
        ((WIDE, WIDE), low),
        ((WIDE, WIDE), low),
        ((WIDE, 3 * WIDE), low),
    ]
    for rows, sets, results in ((size.att, 2, SECT), (size.ffn, 2, SECT), (rows_emb, 1, 1)):
        scratch += [
            chunk_shape(size, rows),
            ((sets, 2, ZS, size.bs, rows, LANES), low),
        ]
        scratch += [(shape, low) for shape in Fold.buffers(size.bs, rows)]
        scratch += [((results, rows, LANES), low)]
    slots = Fold.slots(size.bs)
    dma = pltpu.SemaphoreType.DMA
    return pl.pallas_call(
        partial(backward_kernel, dps),
        out_shape=[
            jax.ShapeDtypeStruct((history, WIDE), wide),
            jax.ShapeDtypeStruct((SECT, size.att, LANES), low),
            jax.ShapeDtypeStruct((SECT, size.ffn, LANES), low),
            jax.ShapeDtypeStruct((rows_emb, LANES), low),
        ],
        in_specs=[anywhere, anywhere] + [inside] * 4 + [anywhere] * len(kept),
        out_specs=[inside, anywhere, anywhere, inside],
        scratch_shapes=[pltpu.VMEM(shape, dtype) for shape, dtype in scratch]
        + [
            dma((2,)),
            dma((9,)),
            dma(()),
            dma((2,)),
            dma((2, SECT)),
            dma((2, SECT)),
            dma((3, slots)),
            dma((3, slots)),
            pltpu.SemaphoreType.REGULAR((3, slots)),
        ],
        compiler_params=pltpu.CompilerParams(
            collective_id=1, has_side_effects=True, vmem_limit_bytes=60 * 1024 * 1024
        ),
        name="backward_fold",
    )(att, ffn, cotangent, x, pick, wsel, *kept)


def by_block(slab):
    split = slab.reshape(slab.shape[:-1] + (SECT, LANES))
    return jnp.moveaxis(split, -2, -3)


def pack_vectors(gains, biases):
    flat = jnp.concatenate([gains, biases], axis=1)
    flat = jnp.pad(flat, ((0, 0), (0, 16 * 512 - flat.shape[1])))
    return flat.reshape(flat.shape[0], 16, 512)


def pack_embedding(matrix, shift):
    wide = matrix.T
    first = jnp.pad(wide[:, L1 + L2 :], ((0, 0), (512 - L3 - GROUPS, 0)))
    return jnp.concatenate(
        [
            shift.T,
            first,
            jnp.pad(wide[:, L1 : L1 + L2], ((0, 0), (256 - L2, 0))),
            jnp.pad(wide[:, :L1], ((0, 0), (256 - L1, 0))),
        ],
        axis=1,
    )


def unpack_embedding(packed):
    matrix = jnp.concatenate(
        [packed[:, 1024 - L1 :], packed[:, 768 - L2 : 768], packed[:, 512 - L3 : 512]], axis=1
    )
    return matrix.T, packed[:, :GROUPS].T


def per_device(
    series,
    groups,
    cotangent,
    embed_weight,
    embed_bias,
    qkv_weight,
    out_weight,
    up_weight,
    down_weight,
    gains,
    biases,
):
    dps = lax.axis_size("dp")
    low = jnp.bfloat16
    width = qkv_weight.shape[2]
    rows_qkv, rows_out, rows_up = qkv_weight.shape[1], out_weight.shape[1], up_weight.shape[1]
    rows_down = down_weight.shape[1] * down_weight.shape[2] // width
    n_gains, n_biases = gains.shape[1], biases.shape[1]
    down_low = down_weight[0].astype(low).reshape(-1, 4, width)
    att_in = jnp.concatenate(
        [
            qkv_weight[0].astype(low),
            out_weight[0].astype(low),
            pack_vectors(gains.astype(low), biases.astype(low))[0],
        ]
    )
    ffn_in = jnp.concatenate(
        [up_weight[0].astype(low), jnp.moveaxis(down_low, 1, 0).reshape(rows_down, width)]
    )
    emb_in = pack_embedding(embed_weight.astype(low), embed_bias.astype(low))
    emb_in = jnp.concatenate([emb_in[:, :512], emb_in[:, 512:]])
    hist = series.shape[1]
    pick = (jnp.arange(GROUPS, dtype=jnp.int32) == groups[0]).astype(low)
    x = jnp.concatenate(
        [
            jnp.pad(series[0].T, ((0, 0), (WINDOW - hist, 0))),
            jnp.broadcast_to(jnp.pad(pick, (0, LANES - GROUPS)), (series.shape[2], LANES)),
        ],
        axis=1,
    )
    pick = jnp.broadcast_to(pick[:, None], (GROUPS, LANES))
    block_output, att, ffn, _, wsel, *kept = forward_all(
        by_block(att_in), by_block(ffn_in), by_block(emb_in), x, pick, dps
    )
    series_grad, att_out, ffn_out, emb_out = backward_all(
        att, ffn, cotangent[0], x, pick, wsel, kept, hist, dps
    )
    att_out = jnp.moveaxis(att_out, 0, 1).reshape(-1, width).astype(jnp.float32)
    ffn_out = jnp.moveaxis(ffn_out, 0, 1).reshape(-1, width).astype(jnp.float32)
    emb_out = jnp.moveaxis(emb_out.reshape(8, -1, LANES), 0, 1).reshape(-1, 1024)
    embed_w_grad, embed_b_grad = unpack_embedding(emb_out.astype(jnp.float32))
    vec_out = att_out[rows_qkv + rows_out :].reshape(1, -1)
    down_out = jnp.moveaxis(ffn_out[rows_up:].reshape(4, -1, width), 0, 1)
    return (
        block_output[None],
        series_grad[None],
        embed_w_grad,
        embed_b_grad,
        att_out[:rows_qkv][None],
        att_out[rows_qkv : rows_qkv + rows_out][None],
        ffn_out[:rows_up][None],
        down_out.reshape(1, -1, down_weight.shape[2]),
        vec_out[:, :n_gains],
        vec_out[:, n_gains : n_gains + n_biases],
    )


def solution(mesh):
    return jax.shard_map(
        per_device,
        mesh=mesh,
        in_specs=(
            P(("pipe", "dp"), None, None),
            P(("pipe", "dp")),
            P(("pipe", "dp"), None, None),
            P(None, "dp"),
            P(None, "dp"),
            P("pipe", "dp", None),
            P("pipe", "dp", None),
            P("pipe", "dp", None),
            P("pipe", "dp", None),
            P("pipe", "dp"),
            P("pipe", "dp"),
        ),
        out_specs=(
            P(("pipe", "dp"), None, None),
            P(("pipe", "dp"), None, None),
            P(None, ("pipe", "dp")),
            P(None, ("pipe", "dp")),
            P("pipe", "dp", None),
            P("pipe", "dp", None),
            P("pipe", "dp", None),
            P("pipe", "dp", None),
            P("pipe", "dp"),
            P("pipe", "dp"),
        ),
        check_vma=False,
    )
```

```python
from functools import partial
import math

import jax
import jax.numpy as jnp
from jax import lax
from jax.experimental import pallas as pl
from jax.experimental.pallas import tpu as pltpu
from jax.sharding import PartitionSpec as P

HEAD = 64
L1 = 96
L2 = 192
L3 = 336
GROUPS = 3


NORM_EPS = 1e-05


MESH = pl.DeviceIdType.MESH
LANES = 128
ZS = 4
SECT = 4
EMB = 3


class Place:
    def __init__(self, dps):
        self.bs = dps // ZS
        pipe = lax.axis_index("pipe")
        dp = lax.axis_index("dp")
        self.pipe, self.dp = pipe, dp
        self.x, self.c = pipe // 2, pipe % 2
        self.z, self.b = dp // self.bs, dp % self.bs
        self.block = self.c * 2 + self.x
        self.x_peer = ((1 - self.x) * 2 + self.c, dp)
        self.core_peer = (self.x * 2 + 1 - self.c, dp)

    def block_of(self, pipe):
        return (pipe % 2) * 2 + pipe // 2

    def pipe_at(self, step):
        return (self.pipe + step) % SECT

    def z_at(self, step):
        return (self.z + step) % ZS

    def b_at(self, step):
        return (self.b + step) % self.bs

    def z_peer(self, step):
        return (self.pipe, self.z_at(step) * self.bs + self.b)

    def b_peer(self, step):
        return (self.pipe, self.z * self.bs + self.b_at(step))

    def greet(self):
        barrier = pltpu.get_barrier_semaphore()
        peers = [(self.pipe_at(k), self.dp) for k in range(1, SECT)]
        peers += [self.z_peer(k) for k in range(1, ZS)]
        peers += [self.b_peer(k) for k in range(1, self.bs)]
        for peer in peers:
            pl.semaphore_signal(barrier, inc=1, device_id=peer, device_id_type=MESH)
        pl.semaphore_wait(barrier, len(peers))


def remote(src, dst, send, recv, peer):
    return pltpu.make_async_remote_copy(
        src_ref=src, dst_ref=dst, send_sem=send, recv_sem=recv, device_id=peer, device_id_type=MESH
    )


FORWARD_START = (
    (0, 3, 0),
    (0, 0, 0),
    (1, 3, 0),
    (2, 3, 0),
    (1, 0, 0),
    (3, 3, 0),
    (0, 1, 0),
    (2, 0, 0),
    (0, 2, 0),
    (1, 1, 0),
    (3, 0, 0),
    (1, 2, 0),
    (0, 0, 1),
    (2, 1, 0),
    (4, 0, 0),
    (4, 3, 0),
    ('embed',),
)
FORWARD_PERIOD = (
    ('mix',),
    (1, 0, 1),
    ('mix',),
    ('attend',),
    (2, 2, 0),
    (0, 1, 1),
    (3, 1, 0),
    ('attend',),
    ('attend',),
    (2, 0, 1),
    (0, 2, 1),
    ('attend',),
    (4, 1, 0),
    ('project',),
    ('up',),
    (3, 2, 0),
    ('up',),
    (1, 1, 1),
    ('up',),
    (3, 0, 1),
    (4, 2, 0),
    (1, 2, 1),
    (0, 0, 2),
    ('up',),
    (2, 1, 1),
    ('down',),
    (4, 0, 1),
    ('down',),
)
BACKWARD_PERIOD = (
    ('norm2',),
    (4, 2, -2),
    ('down',),
    (1, 0, -1),
    (4, 1, -2),
    ('down',),
    (3, 2, -1),
    (0, 2, 0),
    ('up',),
    ('up',),
    (3, 1, -1),
    (1, 2, 0),
    (4, 0, -2),
    ('up',),
    ('up',),
    (0, 1, 0),
    ('norm1',),
    (2, 0, -1),
    ('attend',),
    ('attend',),
    (1, 1, 0),
    ('attend',),
    ('attend',),
    ('mix',),
    (2, 2, 0),
    ('mix',),
    (0, 0, 0),
    (2, 1, 0),
    (3, 0, -1),
)
BACKWARD_END = (
    (4, 2, 2),
    (1, 0, 3),
    (4, 1, 2),
    (3, 2, 3),
    (3, 1, 3),
    ('embed',),
    (4, 0, 2),
    (2, 0, 3),
    (0, 3, 0),
    (1, 3, 0),
    (3, 0, 3),
    (2, 3, 0),
    (3, 3, 0),
    (4, 2, 3),
    (4, 1, 3),
    (4, 0, 3),
    (4, 3, 0),
)


def copies_start(copies):
    for copy in copies:
        copy.start()


def copies_wait(copies):
    for copy in copies:
        copy.wait()


class Spread:
    def __init__(self, at, out, send, recv):
        self.at, self.out, self.send, self.recv = at, out, send, recv
        nb = at.bs - 1
        self.slot_z = 0
        self.slot_b1 = ZS - 1
        self.slot_x1 = self.slot_b1 + nb
        self.slot_x2 = self.slot_x1 + 1
        self.slot_b2 = self.slot_x2 + 1
        self.slot_c = self.slot_b2 + nb
        self.half = ZS // 2

    @staticmethod
    def slots(bs):
        return ZS - 1 + 2 * (bs - 1) + 3

    def copy(self, region, slot, peer):
        return remote(region, region, self.send.at[slot], self.recv.at[slot], peer)

    def copies(self, stage, back):
        at, out, half = self.at, self.out, self.half
        x_block = at.c * 2 + 1 - at.x if back else at.block
        if stage == 0:
            return [
                self.copy(
                    out.at[at.block, at.z_at(ZS - k) if back else at.z, at.b],
                    self.slot_z + k - 1,
                    at.z_peer(k),
                )
                for k in range(1, ZS)
            ]
        if stage == 3:
            core = 1 - at.c if back else at.c
            return [self.copy(out.at[pl.ds(core * 2, 2)], self.slot_c, at.core_peer)]
        copies = []
        for k in range(1, at.bs):
            b = at.b_at(at.bs - k) if back else at.b
            if stage == 1:
                region, slot = out.at[at.block, pl.ds(0, half), b], self.slot_b1
            else:
                region, slot = out.at[pl.ds(at.c * 2, 2), pl.ds(half, half), b], self.slot_b2
            copies.append(self.copy(region, slot + k - 1, at.b_peer(k)))
        if stage == 1:
            region, slot = out.at[x_block, pl.ds(half, half), at.b], self.slot_x1
        else:
            region, slot = out.at[x_block, pl.ds(0, half)], self.slot_x2
        copies.append(self.copy(region, slot, at.x_peer))
        return copies

    def start(self, stage):
        copies_start(self.copies(stage, False))

    def land(self, stage):
        for copy in self.copies(stage, True):
            copy.wait_recv()
        for copy in self.copies(stage, False):
            copy.wait_send()

    def move(self, stage):
        self.land(stage)
        self.start(stage + 1)


class Fold:
    def __init__(self, at, grads, total, bufs, final, send, recv, credit):
        self.at, self.grads, self.total, self.bufs, self.final = at, grads, total, bufs, final
        self.send, self.recv, self.credit = send, recv, credit
        self.half = ZS // 2
        nb = at.bs - 1
        self.slot_c = 0
        self.slot_x1 = 1
        self.slot_b1 = 2
        self.slot_x2 = 2 + nb
        self.slot_b2 = 3 + nb
        self.slot_z = 3 + 2 * nb

    @staticmethod
    def slots(bs):
        return 3 + 2 * (bs - 1) + ZS - 1

    @staticmethod
    def buffers(bs, rows):
        half = ZS // 2
        nb = max(bs - 1, 1)
        return [
            (2, ZS, bs, rows, LANES),
            (half, bs, rows, LANES),
            (nb, 2, half, rows, LANES),
            (half, rows, LANES),
            (nb, half, rows, LANES),
            (ZS - 1, rows, LANES),
        ]

    def parts(self, stage):
        at, half, total, bufs = self.at, self.half, self.total, self.bufs
        if stage == 0:
            other = self.grads.at[pl.ds((1 - at.c) * 2, 2)]
            return [(other, bufs[0], self.slot_c, at.core_peer, at.core_peer)]
        if stage == 3:
            return [
                (
                    total.at[at.x, at.z_at(k), at.b],
                    bufs[5].at[k - 1],
                    self.slot_z + k - 1,
                    at.z_peer(k),
                    at.z_peer(ZS - k),
                )
                for k in range(1, ZS)
            ]
        found = []
        for k in range(1, at.bs):
            if stage == 1:
                src, buf, slot = total.at[:, pl.ds(half, half), at.b_at(k)], bufs[2], self.slot_b1
            else:
                src, buf, slot = total.at[at.x, pl.ds(0, half), at.b_at(k)], bufs[4], self.slot_b2
            found.append((src, buf.at[k - 1], slot + k - 1, at.b_peer(k), at.b_peer(at.bs - k)))
        if stage == 1:
            src, buf, slot = total.at[1 - at.x, pl.ds(0, half)], bufs[1], self.slot_x1
        else:
            src, buf, slot = total.at[1 - at.x, pl.ds(half, half), at.b], bufs[3], self.slot_x2
        found.append((src, buf, slot, at.x_peer, at.x_peer))
        return found

    def start(self, stage, again):
        for src, buf, slot, to, _ in self.parts(stage):
            if again is not False:

                @pl.when(again)
                def _():
                    pl.semaphore_wait(self.credit.at[slot], 1)

            remote(src, buf, self.send.at[slot], self.recv.at[slot], to).start()

    def land(self, stage, more):
        at, half, bs = self.at, self.half, self.at.bs
        total, bufs = self.total, self.bufs
        for src, buf, slot, to, _ in self.parts(stage):
            remote(src, buf, self.send.at[slot], self.recv.at[slot], to).wait()
        if stage == 0:

            @pl.loop(0, 2 * ZS * bs)
            def _(i):
                z, b = i // bs % ZS, i % bs
                x = i // (ZS * bs)
                total[x, z, b] = self.grads[at.c * 2 + x, z, b] + bufs[0][x, z, b]

        elif stage == 1:

            @pl.loop(0, half * bs)
            def _(i):
                z, b = i // bs, i % bs
                total[at.x, z, b] = total[at.x, z, b] + bufs[1][z, b]

            @pl.loop(0, 2 * half)
            def _(i):
                x, z = i // half, i % half
                for k in range(bs - 1):
                    total[x, half + z, at.b] = total[x, half + z, at.b] + bufs[2][k, x, z]

        elif stage == 2:

            @pl.loop(0, half)
            def _(z):
                total[at.x, half + z, at.b] = total[at.x, half + z, at.b] + bufs[3][z]
                for k in range(bs - 1):
                    total[at.x, z, at.b] = total[at.x, z, at.b] + bufs[4][k, z]

        else:
            done = total[at.x, at.z, at.b].astype(jnp.float32)
            for k in range(ZS - 1):
                done = done + bufs[5][k].astype(jnp.float32)
            self.final[...] = done.astype(self.final.dtype)
        if more is not False:

            @pl.when(more)
            def _():
                for _, _, slot, _, origin in self.parts(stage):
                    pl.semaphore_signal(
                        self.credit.at[slot], inc=1, device_id=origin, device_id_type=MESH
                    )

    def move(self, stage, again, more):
        self.land(stage, more)
        self.start(stage + 1, again)


HALF = 256
WIDE = 512
QKV_TILE = 384
VEC_ROWS = 16


def dot_nt(a, b):
    return lax.dot_general(a, b, (((1,), (1,)), ((), ())), preferred_element_type=jnp.float32)


def dot_nn(a, b):
    return lax.dot_general(a, b, (((1,), (0,)), ((), ())), preferred_element_type=jnp.float32)


def dot_tn(a, b):
    return lax.dot_general(a, b, (((0,), (0,)), ((), ())), preferred_element_type=jnp.float32)


def aligned(index, unit):
    return pl.multiple_of(index, unit)


def rows_of(ref, bs, first, count, start, rows, blocks=range(SECT)):
    parts = []
    for i in range(count):
        d = first + i
        place = (d // bs, d % bs)
        parts.append(
            jnp.concatenate(
                [ref[(lb,) + place + (pl.ds(start, rows), slice(None))] for lb in blocks], axis=1
            )
        )
    return parts[0] if count == 1 else jnp.concatenate(parts, axis=0)


def put_rows(ref, bs, first, count, start, rows, value, block=0):
    value = value.astype(ref.dtype)
    for i in range(count):
        d = first + i
        place = (d // bs, d % bs)
        for lane in range(value.shape[1] // LANES):
            ref[(block + lane,) + place + (pl.ds(start, rows), slice(None))] = value[
                i * rows : (i + 1) * rows, lane * LANES : (lane + 1) * LANES
            ]


def vector_pieces(dps):
    n_gains, n_biases = 2 * WIDE // dps, 10 * WIDE // dps
    starts = [(0, 0), (0, 2), (1, 0), (1, 2), (2, 0), (2, 1), (2, 2), (2, 3), (3, 0), (3, 2)]
    pieces = []
    for d in range(dps):
        at = 0
        while at < n_gains + n_biases:
            if at < n_gains:
                index = d * n_gains + at
                row, column = (1, 3)[index // WIDE], WIDE + index % WIDE
                left = n_gains - at
            else:
                index = d * n_biases + at - n_gains
                row, part = starts[index // WIDE]
                column = part * WIDE + index % WIDE
                left = n_gains + n_biases - at
            size = min(left, LANES - at % LANES, LANES - column % LANES)
            pieces.append((d, at // WIDE, at % WIDE, row, column, size))
            at += size
    return pieces


def read_vectors(ref, table, bs, start):
    dps = ZS * bs
    tiles = {}
    for d, row, lane, to_row, to_lane, size in vector_pieces(dps):
        key = (d, lane // LANES)
        if key not in tiles:
            tile = ref[lane // LANES, d // bs, d % bs, start : start + VEC_ROWS, :]
            tiles[key] = tile.astype(jnp.float32)
        off = lane % LANES
        table[to_row : to_row + 1, to_lane : to_lane + size] = tiles[key][
            row : row + 1, off : off + size
        ]


def write_vectors(ref, table, bs, start):
    dps = ZS * bs
    found = {}
    for d, row, lane, to_row, to_lane, size in vector_pieces(dps):
        piece = table[to_row : to_row + 1, to_lane : to_lane + size]
        found.setdefault((d, lane // LANES), {}).setdefault(row, []).append(piece)
    row_id = lax.broadcasted_iota(jnp.int32, (VEC_ROWS, LANES), 0)
    for d in range(dps):
        for lb in range(SECT):
            tile = jnp.zeros((VEC_ROWS, LANES), jnp.float32)
            for row, pieces in found.get((d, lb), {}).items():
                have = sum(piece.shape[1] for piece in pieces)
                if have < LANES:
                    pieces = pieces + [jnp.zeros((1, LANES - have), jnp.float32)]
                line = pieces[0] if len(pieces) == 1 else jnp.concatenate(pieces, axis=1)
                tile = jnp.where(row_id == row, line, tile)
            ref[lb, d // bs, d % bs, start : start + VEC_ROWS, :] = tile.astype(ref.dtype)


def normalize(x, gain, shift):
    mean = jnp.mean(x, axis=1, keepdims=True)
    centred = x - mean
    scale = lax.rsqrt(jnp.mean(centred * centred, axis=1, keepdims=True) + NORM_EPS)
    return centred * scale * gain + shift


def normalize_back(x, grad, gain):
    mean = jnp.mean(x, axis=1, keepdims=True)
    centred = x - mean
    scale = lax.rsqrt(jnp.mean(centred * centred, axis=1, keepdims=True) + NORM_EPS)
    unit = centred * scale
    inner = grad * gain
    first = jnp.mean(inner, axis=1, keepdims=True)
    second = jnp.mean(inner * unit, axis=1, keepdims=True)
    out = scale * (inner - first - unit * second)
    return out, jnp.sum(grad * unit, axis=0, keepdims=True), jnp.sum(grad, axis=0, keepdims=True)


def gelu_pair(u):
    bell = jnp.exp(-0.5 * (u * u))
    t = 1.0 / (1.0 + 0.23164188824 * jnp.abs(u))
    tail = 0.5307027145 * t
    tail = (tail - 0.7265760135) * t
    tail = (tail + 0.7107068705) * t
    tail = (tail - 0.142248368) * t
    tail = (tail + 0.127414796) * t * bell
    below = jnp.where(u < 0.0, tail, 1.0 - tail)
    return u * below, below + u * (0.3989422804014327 * bell)


def head_masks(scale):
    lane = lax.broadcasted_iota(jnp.int32, (1, LANES), 1)
    first = jnp.where(lane < HEAD, scale, 0.0).astype(jnp.bfloat16)
    second = jnp.where(lane < HEAD, 0.0, scale).astype(jnp.bfloat16)
    return first, second


class Sizes:
    def __init__(self, dps):
        self.dps, self.bs = dps, dps // ZS
        self.qkv, self.out, self.up, self.down = (
            3 * WIDE // dps,
            WIDE // dps,
            4 * WIDE // dps,
            WIDE // dps,
        )
        self.vec = self.qkv + self.out
        self.att = self.vec + VEC_ROWS
        self.wide = 4 * self.down


def forward_mix(size, w, table, h, mixed, piece):
    per_tile = QKV_TILE // size.qkv

    @pl.loop(2 * piece, 2 * piece + 2)
    def _(t):
        columns = pl.ds(aligned(t * QKV_TILE, LANES), QKV_TILE)
        matrix = rows_of(w, size.bs, t * per_tile, per_tile, 0, size.qkv)
        mixed[:, columns] = (dot_nt(h[...], matrix) + table[0:1, columns]).astype(mixed.dtype)


def forward_attend(mixed, lse, attended, pair):
    lane = pair * LANES
    key_rows = mixed[:, WIDE + lane : WIDE + lane + LANES]
    values = mixed[:, 2 * WIDE + lane : 2 * WIDE + lane + LANES].T

    for part in range(2):
        rows = slice(part * HALF, (part + 1) * HALF)
        queries = mixed[rows, lane : lane + LANES]
        joined = []
        for head, mask in enumerate(head_masks(1.0 / math.sqrt(HEAD))):
            scores = dot_nt(key_rows, queries * mask)
            top = jnp.max(scores, axis=0, keepdims=True)
            probs = jnp.exp(scores - top)
            total = jnp.sum(probs, axis=0, keepdims=True)
            lse[2 * pair + head, :, rows] = top + jnp.log(total)
            probs = (probs * (1.0 / total)).astype(jnp.bfloat16)
            joined.append(dot_nn(values[head * HEAD : (head + 1) * HEAD], probs))
        joined = jnp.concatenate(joined, axis=0).T
        attended[rows, lane : lane + LANES] = joined.astype(attended.dtype)


def forward_project(size, w, table, h, attended, first, normed):
    for part in range(2):
        rows = slice(part * HALF, (part + 1) * HALF)
        matrix = rows_of(w, size.bs, 0, size.dps, size.qkv, size.out)
        out = dot_nt(attended[rows, :], matrix) + table[1:2, 0:WIDE]
        total = h[rows, :].astype(jnp.float32) + out
        first[rows, :] = total
        normed[rows, :] = normalize(
            total, table[1:2, WIDE : 2 * WIDE], table[1:2, 2 * WIDE : 3 * WIDE]
        ).astype(normed.dtype)


def forward_up(size, w, table, normed, slope, hidden, piece):
    per_tile = HALF // size.up

    @pl.loop(2 * piece, 2 * piece + 2)
    def _(j):
        columns = pl.ds(aligned(j * HALF, HALF), HALF)
        matrix = rows_of(w, size.bs, j * per_tile, per_tile, 0, size.up)
        upper = dot_nt(normed[...], matrix) + table[2:3, columns]
        value, grad = gelu_pair(upper)
        hidden[:, columns] = value.astype(hidden.dtype)
        slope[:, columns] = grad.astype(slope.dtype)


def forward_down(size, w, table, normed, hidden, second, h, part):
    rows = slice(part * HALF, (part + 1) * HALF)
    total = normed[rows, :].astype(jnp.float32) + table[3:4, 0:WIDE]
    for j in range(4):
        matrix = rows_of(w, size.bs, 0, size.dps, j * size.down, size.down)
        total = total + dot_nt(hidden[rows, j * WIDE : (j + 1) * WIDE], matrix)
    second[rows, :] = total
    h[rows, :] = normalize(
        total, table[3:4, WIDE : 2 * WIDE], table[3:4, 2 * WIDE : 3 * WIDE]
    ).astype(h.dtype)


def backward_norm_two(table, dtable, dy, second, dnormed, dlow, dlow_t):
    dtable[...] = jnp.zeros_like(dtable)
    for part in range(2):
        rows = slice(part * HALF, (part + 1) * HALF)
        grad, gain_sum, shift_sum = normalize_back(
            second[rows, :], dy[rows, :].astype(jnp.float32), table[3:4, WIDE : 2 * WIDE]
        )
        dnormed[rows, :] = grad
        dlow[rows, :] = grad.astype(dlow.dtype)
        dtable[3:4, 0:WIDE] += jnp.sum(grad, axis=0, keepdims=True)
        dtable[3:4, WIDE : 2 * WIDE] += gain_sum
        dtable[3:4, 2 * WIDE : 3 * WIDE] += shift_sum
    dlow_t[...] = dlow[...].T


def backward_down(size, grads, hidden, dlow_t, piece):
    @pl.loop(4 * piece, 4 * piece + 4)
    def _(j):
        columns = pl.ds(aligned(j * HALF, HALF), HALF)
        start = aligned(j // 2 * size.down, 16)
        value = dot_nn(dlow_t[...], hidden[:, columns])
        put_rows(grads, size.bs, 0, size.dps, start, size.down, value, 2 * (j % 2))


def backward_up(size, w_up, w_down, grads, dtable, slope, normed, dnormed, dlow, piece):
    per_tile = HALF // size.up

    @pl.loop(2 * piece, 2 * piece + 2)
    def _(j):
        columns = pl.ds(aligned(j * HALF, HALF), HALF)
        block = 2 * (j % 2)
        start = aligned(j // 2 * size.down, 16)
        matrix = rows_of(w_down, size.bs, 0, size.dps, start, size.down, (block, block + 1))
        dupper = dot_nn(dlow[...], matrix) * slope[:, columns].astype(jnp.float32)
        dtable[2:3, columns] = jnp.sum(dupper, axis=0, keepdims=True)
        dup = dupper.astype(jnp.bfloat16)
        first = j * per_tile
        put_rows(grads, size.bs, first, per_tile, 0, size.up, dot_tn(dup, normed[...]))
        matrix = rows_of(w_up, size.bs, first, per_tile, 0, size.up)
        dnormed[...] += dot_nn(dup, matrix)


def backward_norm_one(size, w, table, grads, dtable, first, attended, dnormed, dlow, dlow_t):
    for part in range(2):
        rows = slice(part * HALF, (part + 1) * HALF)
        grad, gain_sum, shift_sum = normalize_back(
            first[rows, :], dnormed[rows, :], table[1:2, WIDE : 2 * WIDE]
        )
        dnormed[rows, :] = grad
        dlow[rows, :] = grad.astype(dlow.dtype)
        dtable[1:2, 0:WIDE] += jnp.sum(grad, axis=0, keepdims=True)
        dtable[1:2, WIDE : 2 * WIDE] += gain_sum
        dtable[1:2, 2 * WIDE : 3 * WIDE] += shift_sum
    dlow_t[...] = dlow[...].T
    for block in (0, 2):
        columns = slice(block * LANES, (block + 2) * LANES)
        value = dot_nn(dlow_t[...], attended[:, columns])
        put_rows(grads, size.bs, 0, size.dps, size.qkv, size.out, value, block)
    for part in range(2):
        rows = slice(part * HALF, (part + 1) * HALF)
        matrix = rows_of(w, size.bs, 0, size.dps, size.qkv, size.out)
        dlow[rows, :] = dot_nn(dlow[rows, :], matrix).astype(dlow.dtype)


def backward_attend(mixed, lse, dtable, dlow, dmixed, pair):
    scale = 1.0 / math.sqrt(HEAD)
    lane = pair * LANES
    columns = slice(lane, lane + LANES)
    key_columns = slice(WIDE + lane, WIDE + lane + LANES)
    value_columns = slice(2 * WIDE + lane, 2 * WIDE + lane + LANES)
    key_rows = mixed[:, key_columns]
    keys_t = key_rows.T
    values = mixed[:, value_columns]
    dkeys = jnp.zeros((WIDE, LANES), jnp.float32)
    dvalues = jnp.zeros((WIDE, LANES), jnp.float32)
    for part in range(2):
        rows = slice(part * HALF, (part + 1) * HALF)
        queries = mixed[rows, columns]
        grad_out = dlow[rows, columns]
        dqueries = []
        for head in range(2):
            query = queries * head_masks(scale)[head]
            grad = grad_out * head_masks(1.0)[head]
            probs = jnp.exp(dot_nt(key_rows, query) - lse[2 * pair + head, :, rows])
            dprobs = dot_nt(values, grad)
            delta = jnp.sum(probs * dprobs, axis=0, keepdims=True)
            dscores = (probs * (dprobs - delta)).astype(jnp.bfloat16)
            dvalues = dvalues + dot_nn(probs.astype(jnp.bfloat16), grad)
            dkeys = dkeys + dot_nn(dscores, query)
            dqueries.append(dot_nn(keys_t[head * HEAD : (head + 1) * HEAD], dscores))
        dquery = jnp.concatenate(dqueries, axis=0).T * scale
        dtable[0:1, columns] += jnp.sum(dquery, axis=0, keepdims=True)
        dmixed[rows, columns] = dquery.astype(dmixed.dtype)
    dmixed[:, key_columns] = dkeys.astype(dmixed.dtype)
    dmixed[:, value_columns] = dvalues.astype(dmixed.dtype)
    dtable[0:1, value_columns] = jnp.sum(dvalues, axis=0, keepdims=True)


def backward_mix(size, w, grads, h, dnormed, dmixed, piece):
    per_tile = QKV_TILE // size.qkv

    @pl.loop(2 * piece, 2 * piece + 2)
    def _(t):
        columns = pl.ds(aligned(t * QKV_TILE, LANES), QKV_TILE)
        grad = dmixed[:, columns]
        put_rows(grads, size.bs, t * per_tile, per_tile, 0, size.qkv, dot_tn(grad, h[...]))
        matrix = rows_of(w, size.bs, t * per_tile, per_tile, 0, size.qkv)
        dnormed[...] += dot_nn(grad, matrix)


WINDOW = 384


def embed(size, emb, pick, x, wsel, h):
    rows = WIDE // size.dps
    first = rows_of(emb, size.bs, 0, size.dps, 0, rows)
    second = rows_of(emb, size.bs, 0, size.dps, rows, rows)
    long, middle, short = (pick[g : g + 1, :] for g in (2, 1, 0))
    wide = jnp.concatenate(
        [
            first[:, LANES : 2 * LANES] * long,
            first[:, 2 * LANES : 3 * LANES] * long + second[:, :LANES] * middle,
            first[:, 3 * LANES :] * long
            + second[:, LANES : 2 * LANES] * middle
            + second[:, 3 * LANES :] * short,
        ],
        axis=1,
    )
    wsel[...] = wide.T
    matrix = jnp.concatenate([wide, first[:, :LANES]], axis=1)
    h[...] = dot_nt(x[...], matrix).astype(h.dtype)


def embed_back(size, pick, x, wsel, dh, grads, series_grad):
    history = series_grad.shape[0]
    series_grad[...] = dot_nt(wsel[...], dh[...])[WINDOW - history :]
    sums = dot_tn(dh[...], x[...])
    long, middle, short = (pick[g : g + 1, :].astype(jnp.float32) for g in (2, 1, 0))
    parts = [sums[:, i * LANES : (i + 1) * LANES] for i in range(4)]
    parts = [
        parts[3],
        parts[0] * long,
        parts[1] * long,
        parts[2] * long,
        parts[1] * middle,
        parts[2] * middle,
        jnp.zeros_like(parts[0]),
        parts[2] * short,
    ]
    rows = WIDE // (SECT * size.dps)
    for pipe in range(SECT):
        block = (pipe % 2) * 2 + pipe // 2
        for dp in range(size.dps):
            start = (pipe * size.dps + dp) * rows
            piece = jnp.concatenate([part[start : start + rows] for part in parts], axis=0)
            grads[block, dp // size.bs, dp % size.bs] = piece.astype(grads.dtype)


def saved_shapes():
    low, wide = jnp.bfloat16, jnp.float32
    return [
        ((WIDE, WIDE), low),
        ((WIDE, 3 * WIDE), low),
        ((2 * SECT, 1, WIDE), wide),
        ((WIDE, WIDE), low),
        ((WIDE, WIDE), wide),
        ((WIDE, WIDE), low),
        ((WIDE, 4 * WIDE), low),
        ((WIDE, 4 * WIDE), low),
        ((WIDE, WIDE), wide),
        ((SECT, 4 * WIDE), wide),
    ]


def chunk_shape(size, rows):
    return (SECT, ZS, size.bs, rows, LANES)


def follow(plan, section, act, compute):
    seen = {}
    for step in plan:
        if len(step) == 1:
            piece = seen.get(step[0], 0)
            seen[step[0]] = piece + 1
            compute(step[0], piece)
            continue
        op, kind, offset = step
        where = section + offset
        if isinstance(where, int):
            if 0 <= where < SECT:
                act(op, kind, where)
        elif offset == 0:
            act(op, kind, where)
        else:
            inside = where < SECT if offset > 0 else where >= 0

            @pl.when(inside)
            def _():
                act(op, kind, where)


def forward_kernel(dps, *refs):
    size = Sizes(dps)
    pieces, x, pick, refs = refs[:4], refs[4], refs[5], refs[6:]
    out, wholes, wsel = refs[0], refs[1:5], refs[5]
    kept, local, refs = refs[6:16], refs[16:26], refs[26:]
    buffers, refs = refs[:4], refs[4:]
    w_sem, kept_sem, own_sem, p_send, p_recv, send, recv = refs
    h, mixed, lse, attended, first, normed, slope, hidden, second, table = local
    w_att, w_up, w_down, w_emb = buffers
    at = Place(dps)

    own = [
        pltpu.make_async_copy(
            pieces[kind].at[at.block],
            wholes[kind].at[at.pipe, at.block, at.z, at.b]
            if kind < EMB
            else wholes[kind].at[at.block, at.z, at.b],
            own_sem.at[kind],
        )
        for kind in range(4)
    ]
    copies_start(own)

    def split(kind, back):
        copies = []
        for k in range(1, SECT):
            if back:
                region = wholes[kind].at[at.pipe_at(SECT - k), at.block, at.z, at.b]
                src = region
            else:
                block = at.block_of(at.pipe_at(k))
                region = wholes[kind].at[at.pipe, block, at.z, at.b]
                src = pieces[kind].at[block]
            sems = p_send.at[kind, k - 1], p_recv.at[kind, k - 1]
            copies.append(remote(src, region, *sems, (at.pipe_at(k), at.dp)))
        return copies

    def chunk(kind, section):
        if kind == EMB:
            return Spread(at, wholes[kind], send.at[3 * SECT], recv.at[3 * SECT])
        number = 3 * section + kind
        return Spread(at, wholes[kind].at[section], send.at[number], recv.at[number])

    def load(kind, section, core):
        blocks = pl.ds(core * 2, 2)
        src, dst = wholes[kind], buffers[kind]
        if kind != EMB:
            src, dst = src.at[section], dst.at[section % 2]
        return pltpu.make_async_copy(src.at[blocks], dst.at[blocks], w_sem.at[kind, core])

    def loaded(kind, section):
        load(kind, section, at.c).wait()
        load(kind, section, 1 - at.c).wait()

    def act(op, kind, section):
        if op == 0:
            own_now = kind == EMB or (isinstance(section, int) and section == 0)
            if own_now:
                own[kind].wait()
            if own_now and kind != EMB:
                for copy in split(kind, True):
                    copy.wait_recv()
                for copy in split(kind, False):
                    copy.wait_send()
            chunk(kind, section).start(0)
        elif op < 4:
            chunk(kind, section).move(op - 1)
            if op == 3:
                load(kind, section, at.c).start()
        else:
            chunk(kind, section).land(3)
            load(kind, section, 1 - at.c).start()

    def saves(section, early):
        which = (1, 2, 3, 4, 5, 9) if early else (6, 7, 8)
        return [
            pltpu.make_async_copy(local[i], kept[i].at[section], kept_sem.at[i]) for i in which
        ]

    at.greet()
    for kind in range(3):
        copies_start(split(kind, False))
    table[...] = jnp.zeros_like(table)

    def before(name, piece):
        loaded(EMB, 0)
        embed(size, w_emb, pick, x, wsel, h)

    follow(FORWARD_START, 0, act, before)

    @pl.loop(0, SECT)
    def _(section):
        att, up, down = (ref.at[section % 2] for ref in (w_att, w_up, w_down))
        keep_h = pltpu.make_async_copy(h, kept[0].at[section], kept_sem.at[0])

        def compute(name, piece):
            if name == "mix":
                if piece == 0:

                    @pl.when(section > 0)
                    def _():
                        copies_wait(saves(section - 1, True))

                    keep_h.start()
                    loaded(0, section)
                    read_vectors(att, table, size.bs, size.vec)
                forward_mix(size, att, table, h, mixed, piece)
            elif name == "attend":
                forward_attend(mixed, lse, attended, piece)
            elif name == "project":
                forward_project(size, att, table, h, attended, first, normed)
                copies_start(saves(section, True))
            elif name == "up":
                if piece == 0:

                    @pl.when(section > 0)
                    def _():
                        copies_wait(saves(section - 1, False))

                    loaded(1, section)
                forward_up(size, up, table, normed, slope, hidden, piece)
            else:
                if piece == 0:
                    loaded(2, section)
                    keep_h.wait()
                forward_down(size, down, table, normed, hidden, second, h, piece)
                if piece == 1:
                    copies_start(saves(section, False))

        follow(FORWARD_PERIOD, section, act, compute)

    copies_wait(saves(SECT - 1, True))
    copies_wait(saves(SECT - 1, False))
    out[...] = h[...]


def forward_all(pieces, x, pick, dps):
    size = Sizes(dps)
    low = jnp.bfloat16
    shapes = saved_shapes()
    chunks = [chunk_shape(size, piece.shape[1]) for piece in pieces]
    anywhere = pl.BlockSpec(memory_space=pl.ANY)
    inside = pl.BlockSpec(memory_space=pltpu.VMEM)
    outs = [((WIDE, WIDE), low)]
    outs += [((SECT,) + shape, low) for shape in chunks[:3]] + [(chunks[3], low)]
    outs += [((WINDOW, WIDE), low)]
    outs += [((SECT,) + shape, dtype) for shape, dtype in shapes]
    scratch = shapes + [((2,) + shape, low) for shape in chunks[:3]] + [(chunks[3], low)]
    slots = Spread.slots(size.bs)
    dma = pltpu.SemaphoreType.DMA
    return pl.pallas_call(
        partial(forward_kernel, dps),
        out_shape=[jax.ShapeDtypeStruct(shape, dtype) for shape, dtype in outs],
        in_specs=[anywhere] * 4 + [inside] * 2,
        out_specs=[inside] + [anywhere] * 4 + [inside] + [anywhere] * len(shapes),
        scratch_shapes=[pltpu.VMEM(shape, dtype) for shape, dtype in scratch]
        + [
            dma((4, 2)),
            dma((len(shapes),)),
            dma((4,)),
            dma((3, SECT - 1)),
            dma((3, SECT - 1)),
            dma((1 + 3 * SECT, slots)),
            dma((1 + 3 * SECT, slots)),
        ],
        compiler_params=pltpu.CompilerParams(
            collective_id=0, has_side_effects=True, vmem_limit_bytes=52 * 1024 * 1024
        ),
        name="gather_forward",
    )(*pieces, x, pick)


def backward_kernel(dps, att, up, down, cotangent, x, pick, wsel, *refs):
    size = Sizes(dps)
    kept, refs = refs[:10], refs[10:]
    series_grad, outs, refs = refs[0], refs[1:5], refs[5:]
    local, refs = refs[:9], refs[9:]
    tables, w_att, w_up, w_down, dtable, dy, dnormed, dlow, dlow_t, dmixed = refs[:10]
    refs = refs[10:]
    kinds = [
        (refs[9 * k], refs[9 * k + 1], refs[9 * k + 2 : 9 * k + 8], refs[9 * k + 8])
        for k in range(4)
    ]
    refs = refs[36:]
    w_sem, kept_sem, table_sem, out_sem, p_send, p_recv, send, recv, credit = refs
    h, mixed, lse, attended, first, normed, slope, hidden, second = local
    at = Place(dps)
    last = SECT - 1

    def weights(kind, section):
        src, dst = ((att, w_att), (up, w_up), (down, w_down))[kind]
        return pltpu.make_async_copy(src.at[section], dst, w_sem.at[kind])

    def loads(section, dense):
        which = (5, 6, 7, 8) if dense else (0, 1, 2, 3, 4)
        found = [
            pltpu.make_async_copy(kept[i].at[section], local[i], kept_sem.at[i]) for i in which
        ]
        return found + [weights(kind, section) for kind in ((1, 2) if dense else (0,))]

    def chunk(kind, i):
        grads, totals, bufs, finals = kinds[kind]
        return Fold(
            at,
            grads,
            totals.at[i % 2],
            bufs,
            finals.at[i],
            send.at[kind],
            recv.at[kind],
            credit.at[kind],
        )

    def hand_over(kind, i):
        landing = outs[kind].at[at.block]
        final = kinds[kind][3].at[i]
        return (
            pltpu.make_async_copy(final, landing, out_sem.at[kind]),
            remote(final, landing, p_send.at[kind, i], p_recv.at[kind, at.pipe], (last - i, at.dp)),
        )

    def act(op, kind, i):
        again, more = (False, False) if kind == EMB else (i > 0, i < last)
        if op == 0:
            chunk(kind, i).start(0, again)
        elif op < 4:
            chunk(kind, i).move(op - 1, again, more)
        else:
            chunk(kind, i).land(3, more)
            if kind == EMB:
                outs[kind][...] = kinds[kind][3][0]
            else:
                here, away = hand_over(kind, i)

                @pl.when(at.pipe == last - i)
                def _():
                    here.start()

                @pl.when(at.pipe != last - i)
                def _():
                    away.start()

    copies_start(loads(last, True))
    get_tables = pltpu.make_async_copy(kept[9], tables, table_sem)
    get_tables.start()
    copies_start(loads(last, False))
    dy[...] = cotangent[...]
    at.greet()
    get_tables.wait()

    @pl.loop(0, SECT)
    def _(i):
        section = last - i
        table = tables.at[section]

        def compute(name, piece):
            if name == "norm2":
                copies_wait(loads(section, True))
                backward_norm_two(table, dtable, dy, second, dnormed, dlow, dlow_t)
            elif name == "down":
                backward_down(size, kinds[2][0], hidden, dlow_t, piece)
            elif name == "up":
                backward_up(
                    size, w_up, w_down, kinds[1][0], dtable, slope, normed, dnormed, dlow, piece
                )
                if piece == 3:

                    @pl.when(section > 0)
                    def _():
                        copies_start(loads(section - 1, True))

            elif name == "norm1":
                copies_wait(loads(section, False))
                backward_norm_one(
                    size, w_att, table, kinds[0][0], dtable, first, attended, dnormed, dlow, dlow_t
                )
            elif name == "attend":
                backward_attend(mixed, lse, dtable, dlow, dmixed, piece)
            else:
                backward_mix(size, w_att, kinds[0][0], h, dnormed, dmixed, piece)
                if piece == 1:
                    dy[...] = dnormed[...].astype(dy.dtype)
                    write_vectors(kinds[0][0], dtable, size.bs, size.vec)

                    @pl.when(section > 0)
                    def _():
                        copies_start(loads(section - 1, False))

        follow(BACKWARD_PERIOD, i, act, compute)

    def after(name, piece):
        embed_back(size, pick, x, wsel, dy, kinds[EMB][0], series_grad)

    follow(BACKWARD_END, 0, act, after)

    for kind in range(3):
        for i in range(SECT):
            here, away = hand_over(kind, i)

            @pl.when(at.pipe == last - i)
            def _():
                here.wait()

            @pl.when(at.pipe != last - i)
            def _():
                away.wait_send()

        for k in range(1, SECT):
            other = at.pipe_at(k)
            landing = outs[kind].at[at.block_of(other)]
            sems = p_send.at[kind, 0], p_recv.at[kind, other]
            remote(landing, landing, *sems, (other, at.dp)).wait_recv()


def backward_all(weights, cotangent, x, pick, wsel, kept, history, dps):
    size = Sizes(dps)
    low, wide = jnp.bfloat16, jnp.float32
    anywhere = pl.BlockSpec(memory_space=pl.ANY)
    inside = pl.BlockSpec(memory_space=pltpu.VMEM)
    shapes = saved_shapes()
    rows_emb = 8 * WIDE // (SECT * dps)
    kind_rows = (size.att, size.up, size.wide, rows_emb)
    scratch = shapes[:9] + [((SECT,) + shapes[9][0], wide)]
    scratch += [(chunk_shape(size, rows), low) for rows in kind_rows[:3]]
    scratch += [
        (shapes[9][0], wide),
        ((WIDE, WIDE), low),
        ((WIDE, WIDE), wide),
        ((WIDE, WIDE), low),
        ((WIDE, WIDE), low),
        ((WIDE, 3 * WIDE), low),
    ]
    for kind, rows in enumerate(kind_rows):
        sets, results = (1, 1) if kind == EMB else (2, SECT)
        scratch += [
            (chunk_shape(size, rows), low),
            ((sets, 2, ZS, size.bs, rows, LANES), low),
        ]
        scratch += [(shape, low) for shape in Fold.buffers(size.bs, rows)]
        scratch += [((results, rows, LANES), low)]
    slots = Fold.slots(size.bs)
    dma = pltpu.SemaphoreType.DMA
    return pl.pallas_call(
        partial(backward_kernel, dps),
        out_shape=[jax.ShapeDtypeStruct((history, WIDE), wide)]
        + [jax.ShapeDtypeStruct((SECT, rows, LANES), low) for rows in kind_rows[:3]]
        + [jax.ShapeDtypeStruct((rows_emb, LANES), low)],
        in_specs=[anywhere] * 3 + [inside] * 4 + [anywhere] * len(kept),
        out_specs=[inside] + [anywhere] * 3 + [inside],
        scratch_shapes=[pltpu.VMEM(shape, dtype) for shape, dtype in scratch]
        + [
            dma((3,)),
            dma((9,)),
            dma(()),
            dma((3,)),
            dma((3, SECT)),
            dma((3, SECT)),
            dma((4, slots)),
            dma((4, slots)),
            pltpu.SemaphoreType.REGULAR((4, slots)),
        ],
        compiler_params=pltpu.CompilerParams(
            collective_id=1, has_side_effects=True, vmem_limit_bytes=60 * 1024 * 1024
        ),
        name="backward_fold",
    )(*weights, cotangent, x, pick, wsel, *kept)


def by_block(slab):
    split = slab.reshape(slab.shape[:-1] + (SECT, LANES))
    return jnp.moveaxis(split, -2, -3)


def pack_vectors(gains, biases):
    flat = jnp.concatenate([gains, biases], axis=1)
    flat = jnp.pad(flat, ((0, 0), (0, 16 * 512 - flat.shape[1])))
    return flat.reshape(flat.shape[0], 16, 512)


def pack_embedding(matrix, shift):
    wide = matrix.T
    first = jnp.pad(wide[:, L1 + L2 :], ((0, 0), (512 - L3 - GROUPS, 0)))
    return jnp.concatenate(
        [
            shift.T,
            first,
            jnp.pad(wide[:, L1 : L1 + L2], ((0, 0), (256 - L2, 0))),
            jnp.pad(wide[:, :L1], ((0, 0), (256 - L1, 0))),
        ],
        axis=1,
    )


def unpack_embedding(packed):
    matrix = jnp.concatenate(
        [packed[:, 1024 - L1 :], packed[:, 768 - L2 : 768], packed[:, 512 - L3 : 512]], axis=1
    )
    return matrix.T, packed[:, :GROUPS].T


def per_device(
    series,
    groups,
    cotangent,
    embed_weight,
    embed_bias,
    qkv_weight,
    out_weight,
    up_weight,
    down_weight,
    gains,
    biases,
):
    dps = lax.axis_size("dp")
    low = jnp.bfloat16
    width = qkv_weight.shape[2]
    rows_qkv, rows_out = qkv_weight.shape[1], out_weight.shape[1]
    rows_down = down_weight.shape[1] * down_weight.shape[2] // width
    n_gains, n_biases = gains.shape[1], biases.shape[1]
    down_low = down_weight[0].astype(low).reshape(-1, 4, width)
    att_in = jnp.concatenate(
        [
            qkv_weight[0].astype(low),
            out_weight[0].astype(low),
            pack_vectors(gains.astype(low), biases.astype(low))[0],
        ]
    )
    up_in = up_weight[0].astype(low)
    down_in = jnp.moveaxis(down_low, 1, 0).reshape(rows_down, width)
    emb_in = pack_embedding(embed_weight.astype(low), embed_bias.astype(low))
    emb_in = jnp.concatenate([emb_in[:, :512], emb_in[:, 512:]])
    hist = series.shape[1]
    pick = (jnp.arange(GROUPS, dtype=jnp.int32) == groups[0]).astype(low)
    x = jnp.concatenate(
        [
            jnp.pad(series[0].T, ((0, 0), (WINDOW - hist, 0))),
            jnp.broadcast_to(jnp.pad(pick, (0, LANES - GROUPS)), (series.shape[2], LANES)),
        ],
        axis=1,
    )
    pick = jnp.broadcast_to(pick[:, None], (GROUPS, LANES))
    pieces = [by_block(piece) for piece in (att_in, up_in, down_in, emb_in)]
    block_output, att, up, down, _, wsel, *kept = forward_all(pieces, x, pick, dps)
    series_grad, att_out, up_out, down_out, emb_out = backward_all(
        (att, up, down), cotangent[0], x, pick, wsel, kept, hist, dps
    )
    att_out = jnp.moveaxis(att_out, 0, 1).reshape(-1, width).astype(jnp.float32)
    up_out = jnp.moveaxis(up_out, 0, 1).reshape(-1, width).astype(jnp.float32)
    emb_out = jnp.moveaxis(emb_out.reshape(8, -1, LANES), 0, 1).reshape(-1, 1024)
    embed_w_grad, embed_b_grad = unpack_embedding(emb_out.astype(jnp.float32))
    vec_out = att_out[rows_qkv + rows_out :].reshape(1, -1)
    down_out = down_out.astype(jnp.float32).reshape(SECT, 4, -1, LANES)
    down_out = jnp.transpose(down_out, (2, 1, 0, 3))
    return (
        block_output[None],
        series_grad[None],
        embed_w_grad,
        embed_b_grad,
        att_out[:rows_qkv][None],
        att_out[rows_qkv : rows_qkv + rows_out][None],
        up_out[None],
        down_out.reshape(1, -1, down_weight.shape[2]),
        vec_out[:, :n_gains],
        vec_out[:, n_gains : n_gains + n_biases],
    )


def solution(mesh):
    return jax.shard_map(
        per_device,
        mesh=mesh,
        in_specs=(
            P(("pipe", "dp"), None, None),
            P(("pipe", "dp")),
            P(("pipe", "dp"), None, None),
            P(None, "dp"),
            P(None, "dp"),
            P("pipe", "dp", None),
            P("pipe", "dp", None),
            P("pipe", "dp", None),
            P("pipe", "dp", None),
            P("pipe", "dp"),
            P("pipe", "dp"),
        ),
        out_specs=(
            P(("pipe", "dp"), None, None),
            P(("pipe", "dp"), None, None),
            P(None, ("pipe", "dp")),
            P(None, ("pipe", "dp")),
            P("pipe", "dp", None),
            P("pipe", "dp", None),
            P("pipe", "dp", None),
            P("pipe", "dp", None),
            P("pipe", "dp"),
            P("pipe", "dp"),
        ),
        check_vma=False,
    )
```

```python
from functools import partial
import math

import jax
import jax.numpy as jnp
from jax import lax
from jax.experimental import pallas as pl
from jax.experimental.pallas import tpu as pltpu
from jax.sharding import PartitionSpec as P

HEAD = 64
L1 = 96
L2 = 192
L3 = 336
GROUPS = 3


NORM_EPS = 1e-05


MESH = pl.DeviceIdType.MESH
LANES = 128
ZS = 4
SECT = 4
EMB = 3


class Place:
    def __init__(self, dps):
        self.bs = dps // ZS
        pipe = lax.axis_index("pipe")
        dp = lax.axis_index("dp")
        self.pipe, self.dp = pipe, dp
        self.x, self.c = pipe // 2, pipe % 2
        self.z, self.b = dp // self.bs, dp % self.bs
        self.block = self.c * 2 + self.x
        self.x_peer = ((1 - self.x) * 2 + self.c, dp)
        self.core_peer = (self.x * 2 + 1 - self.c, dp)

    def block_of(self, pipe):
        return (pipe % 2) * 2 + pipe // 2

    def pipe_at(self, step):
        return (self.pipe + step) % SECT

    def z_at(self, step):
        return (self.z + step) % ZS

    def b_at(self, step):
        return (self.b + step) % self.bs

    def z_peer(self, step):
        return (self.pipe, self.z_at(step) * self.bs + self.b)

    def b_peer(self, step):
        return (self.pipe, self.z * self.bs + self.b_at(step))

    def greet(self):
        barrier = pltpu.get_barrier_semaphore()
        peers = [(self.pipe_at(k), self.dp) for k in range(1, SECT)]
        peers += [self.z_peer(k) for k in range(1, ZS)]
        peers += [self.b_peer(k) for k in range(1, self.bs)]
        for peer in peers:
            pl.semaphore_signal(barrier, inc=1, device_id=peer, device_id_type=MESH)
        pl.semaphore_wait(barrier, len(peers))


def remote(src, dst, send, recv, peer):
    return pltpu.make_async_remote_copy(
        src_ref=src, dst_ref=dst, send_sem=send, recv_sem=recv, device_id=peer, device_id_type=MESH
    )


FORWARD_START = (
    (0, 3, 0),
    (0, 0, 0),
    (1, 3, 0),
    (2, 3, 0),
    (0, 1, 0),
    (1, 0, 0),
    (3, 3, 0),
    (4, 3, 0),
    (0, 2, 0),
    (2, 0, 0),
    (1, 1, 0),
    (1, 2, 0),
    (3, 0, 0),
    (0, 0, 1),
    (2, 1, 0),
    (4, 0, 0),
    (0, 1, 1),
    ('embed',),
)
FORWARD_PERIOD = (
    ('mix',),
    ('mix',),
    (1, 0, 1),
    ('attend',),
    ('attend',),
    (2, 2, 0),
    (3, 1, 0),
    (0, 2, 1),
    ('attend',),
    ('attend',),
    (2, 0, 1),
    (4, 1, 0),
    ('project',),
    (3, 2, 0),
    (1, 1, 1),
    ('up',),
    ('up',),
    ('up',),
    (1, 2, 1),
    (3, 0, 1),
    (4, 2, 0),
    (0, 0, 2),
    ('up',),
    (2, 1, 1),
    ('down',),
    (4, 0, 1),
    ('down',),
    (0, 1, 2),
)
BACKWARD_PERIOD = (
    (0, 0, -1),
    ('norm2',),
    (2, 1, -1),
    (4, 2, -2),
    ('down',),
    ('down',),
    (0, 2, 0),
    (1, 0, -1),
    ('gelu',),
    ('gelu',),
    (1, 2, 0),
    ('up',),
    (3, 2, -1),
    (3, 1, -1),
    ('normed',),
    ('norm1',),
    (0, 1, 0),
    (4, 0, -2),
    (2, 0, -1),
    ('attend',),
    ('attend',),
    (1, 1, 0),
    ('attend',),
    (3, 0, -1),
    ('attend',),
    ('mix',),
    (2, 2, 0),
    ('mix',),
    (4, 1, -1),
    ('input',),
)
BACKWARD_END = (
    (0, 0, 3),
    (2, 1, 3),
    (4, 2, 2),
    (1, 0, 3),
    (3, 2, 3),
    ('embed',),
    (0, 3, 0),
    (3, 1, 3),
    (4, 0, 2),
    (2, 0, 3),
    (1, 3, 0),
    (3, 0, 3),
    (2, 3, 0),
    (3, 3, 0),
    (4, 1, 3),
    (4, 2, 3),
    (4, 0, 3),
    (4, 3, 0),
)


def copies_start(copies):
    for copy in copies:
        copy.start()


def copies_wait(copies):
    for copy in copies:
        copy.wait()


class Spread:
    def __init__(self, at, out, send, recv):
        self.at, self.out, self.send, self.recv = at, out, send, recv
        nb = at.bs - 1
        self.slot_z = 0
        self.slot_b1 = ZS - 1
        self.slot_x1 = self.slot_b1 + nb
        self.slot_x2 = self.slot_x1 + 1
        self.slot_b2 = self.slot_x2 + 1
        self.slot_c = self.slot_b2 + nb
        self.half = ZS // 2

    @staticmethod
    def slots(bs):
        return ZS - 1 + 2 * (bs - 1) + 3

    def copy(self, region, slot, peer):
        return remote(region, region, self.send.at[slot], self.recv.at[slot], peer)

    def copies(self, stage, back):
        at, out, half = self.at, self.out, self.half
        x_block = at.c * 2 + 1 - at.x if back else at.block
        if stage == 0:
            return [
                self.copy(
                    out.at[at.block, at.z_at(ZS - k) if back else at.z, at.b],
                    self.slot_z + k - 1,
                    at.z_peer(k),
                )
                for k in range(1, ZS)
            ]
        if stage == 3:
            core = 1 - at.c if back else at.c
            return [self.copy(out.at[pl.ds(core * 2, 2)], self.slot_c, at.core_peer)]
        copies = []
        for k in range(1, at.bs):
            b = at.b_at(at.bs - k) if back else at.b
            if stage == 1:
                region, slot = out.at[at.block, pl.ds(0, half), b], self.slot_b1
            else:
                region, slot = out.at[pl.ds(at.c * 2, 2), pl.ds(half, half), b], self.slot_b2
            copies.append(self.copy(region, slot + k - 1, at.b_peer(k)))
        if stage == 1:
            region, slot = out.at[x_block, pl.ds(half, half), at.b], self.slot_x1
        else:
            region, slot = out.at[x_block, pl.ds(0, half)], self.slot_x2
        copies.append(self.copy(region, slot, at.x_peer))
        return copies

    def start(self, stage):
        copies_start(self.copies(stage, False))

    def land(self, stage):
        for copy in self.copies(stage, True):
            copy.wait_recv()
        for copy in self.copies(stage, False):
            copy.wait_send()

    def move(self, stage):
        self.land(stage)
        self.start(stage + 1)


class Fold:
    def __init__(self, at, grads, total, bufs, final, send, recv, credit):
        self.at, self.grads, self.total, self.bufs, self.final = at, grads, total, bufs, final
        self.send, self.recv, self.credit = send, recv, credit
        self.half = ZS // 2
        nb = at.bs - 1
        self.slot_c = 0
        self.slot_x1 = 1
        self.slot_b1 = 2
        self.slot_x2 = 2 + nb
        self.slot_b2 = 3 + nb
        self.slot_z = 3 + 2 * nb

    @staticmethod
    def slots(bs):
        return 3 + 2 * (bs - 1) + ZS - 1

    @staticmethod
    def buffers(bs, rows):
        half = ZS // 2
        nb = max(bs - 1, 1)
        return [
            (2, ZS, bs, rows, LANES),
            (half, bs, rows, LANES),
            (nb, 2, half, rows, LANES),
            (half, rows, LANES),
            (nb, half, rows, LANES),
            (ZS - 1, rows, LANES),
        ]

    def parts(self, stage):
        at, half, total, bufs = self.at, self.half, self.total, self.bufs
        if stage == 0:
            other = self.grads.at[pl.ds((1 - at.c) * 2, 2)]
            return [(other, bufs[0], self.slot_c, at.core_peer, at.core_peer)]
        if stage == 3:
            return [
                (
                    total.at[at.x, at.z_at(k), at.b],
                    bufs[5].at[k - 1],
                    self.slot_z + k - 1,
                    at.z_peer(k),
                    at.z_peer(ZS - k),
                )
                for k in range(1, ZS)
            ]
        found = []
        for k in range(1, at.bs):
            if stage == 1:
                src, buf, slot = total.at[:, pl.ds(half, half), at.b_at(k)], bufs[2], self.slot_b1
            else:
                src, buf, slot = total.at[at.x, pl.ds(0, half), at.b_at(k)], bufs[4], self.slot_b2
            found.append((src, buf.at[k - 1], slot + k - 1, at.b_peer(k), at.b_peer(at.bs - k)))
        if stage == 1:
            src, buf, slot = total.at[1 - at.x, pl.ds(0, half)], bufs[1], self.slot_x1
        else:
            src, buf, slot = total.at[1 - at.x, pl.ds(half, half), at.b], bufs[3], self.slot_x2
        found.append((src, buf, slot, at.x_peer, at.x_peer))
        return found

    def start(self, stage, again):
        for src, buf, slot, to, _ in self.parts(stage):
            if again is not False:

                @pl.when(again)
                def _():
                    pl.semaphore_wait(self.credit.at[slot], 1)

            remote(src, buf, self.send.at[slot], self.recv.at[slot], to).start()

    def land(self, stage, more):
        at, half, bs = self.at, self.half, self.at.bs
        total, bufs = self.total, self.bufs
        for src, buf, slot, to, _ in self.parts(stage):
            remote(src, buf, self.send.at[slot], self.recv.at[slot], to).wait()
        if stage == 0:

            @pl.loop(0, 2 * ZS * bs)
            def _(i):
                z, b = i // bs % ZS, i % bs
                x = i // (ZS * bs)
                total[x, z, b] = self.grads[at.c * 2 + x, z, b] + bufs[0][x, z, b]

        elif stage == 1:

            @pl.loop(0, half * bs)
            def _(i):
                z, b = i // bs, i % bs
                total[at.x, z, b] = total[at.x, z, b] + bufs[1][z, b]

            @pl.loop(0, 2 * half)
            def _(i):
                x, z = i // half, i % half
                for k in range(bs - 1):
                    total[x, half + z, at.b] = total[x, half + z, at.b] + bufs[2][k, x, z]

        elif stage == 2:

            @pl.loop(0, half)
            def _(z):
                total[at.x, half + z, at.b] = total[at.x, half + z, at.b] + bufs[3][z]
                for k in range(bs - 1):
                    total[at.x, z, at.b] = total[at.x, z, at.b] + bufs[4][k, z]

        else:
            done = total[at.x, at.z, at.b].astype(jnp.float32)
            for k in range(ZS - 1):
                done = done + bufs[5][k].astype(jnp.float32)
            self.final[...] = done.astype(self.final.dtype)
        if more is not False:

            @pl.when(more)
            def _():
                for _, _, slot, _, origin in self.parts(stage):
                    pl.semaphore_signal(
                        self.credit.at[slot], inc=1, device_id=origin, device_id_type=MESH
                    )

    def move(self, stage, again, more):
        self.land(stage, more)
        self.start(stage + 1, again)


HALF = 256
WIDE = 512
QKV_TILE = 768
VEC_ROWS = 16


def dot_nt(a, b):
    return lax.dot_general(a, b, (((1,), (1,)), ((), ())), preferred_element_type=jnp.float32)


def dot_nn(a, b):
    return lax.dot_general(a, b, (((1,), (0,)), ((), ())), preferred_element_type=jnp.float32)


def dot_tn(a, b):
    return lax.dot_general(a, b, (((0,), (0,)), ((), ())), preferred_element_type=jnp.float32)


def aligned(index, unit):
    return pl.multiple_of(index, unit)


def rows_of(ref, bs, first, count, start, rows, blocks=range(SECT)):
    parts = []
    for i in range(count):
        d = first + i
        place = (d // bs, d % bs)
        parts.append(
            jnp.concatenate(
                [ref[(lb,) + place + (pl.ds(start, rows), slice(None))] for lb in blocks], axis=1
            )
        )
    return parts[0] if count == 1 else jnp.concatenate(parts, axis=0)


def put_rows(ref, bs, first, count, start, rows, value, block=0):
    value = value.astype(ref.dtype)
    for i in range(count):
        d = first + i
        place = (d // bs, d % bs)
        for lane in range(value.shape[1] // LANES):
            ref[(block + lane,) + place + (pl.ds(start, rows), slice(None))] = value[
                i * rows : (i + 1) * rows, lane * LANES : (lane + 1) * LANES
            ]


def vector_pieces(dps):
    n_gains, n_biases = 2 * WIDE // dps, 10 * WIDE // dps
    starts = [(0, 0), (0, 2), (1, 0), (1, 2), (2, 0), (2, 1), (2, 2), (2, 3), (3, 0), (3, 2)]
    pieces = []
    for d in range(dps):
        at = 0
        while at < n_gains + n_biases:
            if at < n_gains:
                index = d * n_gains + at
                row, column = (1, 3)[index // WIDE], WIDE + index % WIDE
                left = n_gains - at
            else:
                index = d * n_biases + at - n_gains
                row, part = starts[index // WIDE]
                column = part * WIDE + index % WIDE
                left = n_gains + n_biases - at
            size = min(left, LANES - at % LANES, LANES - column % LANES)
            pieces.append((d, at // WIDE, at % WIDE, row, column, size))
            at += size
    return pieces


def read_vectors(ref, table, bs, start):
    dps = ZS * bs
    tiles = {}
    for d, row, lane, to_row, to_lane, size in vector_pieces(dps):
        key = (d, lane // LANES)
        if key not in tiles:
            tile = ref[lane // LANES, d // bs, d % bs, start : start + VEC_ROWS, :]
            tiles[key] = tile.astype(jnp.float32)
        off = lane % LANES
        table[to_row : to_row + 1, to_lane : to_lane + size] = tiles[key][
            row : row + 1, off : off + size
        ]


def write_vectors(ref, table, bs, start):
    dps = ZS * bs
    found = {}
    for d, row, lane, to_row, to_lane, size in vector_pieces(dps):
        piece = table[to_row : to_row + 1, to_lane : to_lane + size]
        found.setdefault((d, lane // LANES), {}).setdefault(row, []).append(piece)
    row_id = lax.broadcasted_iota(jnp.int32, (VEC_ROWS, LANES), 0)
    for d in range(dps):
        for lb in range(SECT):
            tile = jnp.zeros((VEC_ROWS, LANES), jnp.float32)
            for row, pieces in found.get((d, lb), {}).items():
                have = sum(piece.shape[1] for piece in pieces)
                if have < LANES:
                    pieces = pieces + [jnp.zeros((1, LANES - have), jnp.float32)]
                line = pieces[0] if len(pieces) == 1 else jnp.concatenate(pieces, axis=1)
                tile = jnp.where(row_id == row, line, tile)
            ref[lb, d // bs, d % bs, start : start + VEC_ROWS, :] = tile.astype(ref.dtype)


def normalize(x, gain, shift):
    mean = jnp.mean(x, axis=1, keepdims=True)
    centred = x - mean
    scale = lax.rsqrt(jnp.mean(centred * centred, axis=1, keepdims=True) + NORM_EPS)
    return centred * scale * gain + shift


def normalize_back(x, grad, gain):
    mean = jnp.mean(x, axis=1, keepdims=True)
    centred = x - mean
    scale = lax.rsqrt(jnp.mean(centred * centred, axis=1, keepdims=True) + NORM_EPS)
    unit = centred * scale
    inner = grad * gain
    first = jnp.mean(inner, axis=1, keepdims=True)
    second = jnp.mean(inner * unit, axis=1, keepdims=True)
    out = scale * (inner - first - unit * second)
    return out, jnp.sum(grad * unit, axis=0, keepdims=True), jnp.sum(grad, axis=0, keepdims=True)


def gelu_pair(u):
    bell = jnp.exp(-0.5 * (u * u))
    t = 1.0 / (1.0 + 0.23164188824 * jnp.abs(u))
    tail = 0.5307027145 * t
    tail = (tail - 0.7265760135) * t
    tail = (tail + 0.7107068705) * t
    tail = (tail - 0.142248368) * t
    tail = (tail + 0.127414796) * t * bell
    below = jnp.where(u < 0.0, tail, 1.0 - tail)
    return u * below, below + u * (0.3989422804014327 * bell)


def head_masks(scale):
    lane = lax.broadcasted_iota(jnp.int32, (1, LANES), 1)
    first = jnp.where(lane < HEAD, scale, 0.0).astype(jnp.bfloat16)
    second = jnp.where(lane < HEAD, 0.0, scale).astype(jnp.bfloat16)
    return first, second


class Sizes:
    def __init__(self, dps):
        self.dps, self.bs = dps, dps // ZS
        self.qkv, self.out, self.up, self.down = (
            3 * WIDE // dps,
            WIDE // dps,
            4 * WIDE // dps,
            WIDE // dps,
        )
        self.att = self.qkv + VEC_ROWS
        self.dense = self.out + self.up
        self.wide = 4 * self.down


def qkv_rows(size, w, tile):
    count = QKV_TILE // size.qkv
    return rows_of(w, size.bs, tile * count, count, 0, size.qkv)


def out_rows(size, w):
    return rows_of(w, size.bs, 0, size.dps, 0, size.out)


def up_rows(size, w, tile):
    count = HALF // size.up
    return rows_of(w, size.bs, tile * count, count, size.out, size.up)


def forward_mix(size, w, table, h, mixed, piece):
    columns = slice(piece * QKV_TILE, (piece + 1) * QKV_TILE)
    mixed[:, columns] = (
        dot_nt(h[...], qkv_rows(size, w, piece)) + table[0:1, columns]
    ).astype(mixed.dtype)


def forward_attend(mixed, lse, attended, pair):
    lane = pair * LANES
    key_rows = mixed[:, WIDE + lane : WIDE + lane + LANES]
    values = mixed[:, 2 * WIDE + lane : 2 * WIDE + lane + LANES].T

    for part in range(2):
        rows = slice(part * HALF, (part + 1) * HALF)
        queries = mixed[rows, lane : lane + LANES]
        joined = []
        for head, mask in enumerate(head_masks(1.0 / math.sqrt(HEAD))):
            scores = dot_nt(key_rows, queries * mask)
            top = jnp.max(scores, axis=0, keepdims=True)
            probs = jnp.exp(scores - top)
            total = jnp.sum(probs, axis=0, keepdims=True)
            lse[2 * pair + head, :, rows] = top + jnp.log(total)
            probs = (probs * (1.0 / total)).astype(jnp.bfloat16)
            joined.append(dot_nn(values[head * HEAD : (head + 1) * HEAD], probs))
        joined = jnp.concatenate(joined, axis=0).T
        attended[rows, lane : lane + LANES] = joined.astype(attended.dtype)


def forward_project(size, w, table, h, attended, first, normed):
    out = dot_nt(attended[...], out_rows(size, w))
    for part in range(2):
        rows = slice(part * HALF, (part + 1) * HALF)
        total = h[rows, :].astype(jnp.float32) + (out[rows] + table[1:2, 0:WIDE])
        first[rows, :] = total
        normed[rows, :] = normalize(
            total, table[1:2, WIDE : 2 * WIDE], table[1:2, 2 * WIDE : 3 * WIDE]
        ).astype(normed.dtype)


def forward_up(size, w, table, normed, slope, hidden, piece):
    for j in (2 * piece, 2 * piece + 1):
        columns = slice(j * HALF, (j + 1) * HALF)
        upper = dot_nt(normed[...], up_rows(size, w, j)) + table[2:3, columns]
        value, grad = gelu_pair(upper)
        hidden[:, columns] = value.astype(hidden.dtype)
        slope[:, columns] = grad.astype(slope.dtype)


def forward_down(size, w, table, normed, hidden, second, h, piece):
    columns = slice(piece * HALF, (piece + 1) * HALF)
    count = size.dps // 2
    matrix = jnp.concatenate(
        [
            rows_of(w, size.bs, piece * count, count, j * size.down, size.down)
            for j in range(4)
        ],
        axis=1,
    )
    out = dot_nt(hidden[...], matrix)
    second[:, columns] = normed[:, columns].astype(jnp.float32) + (out + table[3:4, columns])
    if piece == 1:
        for part in range(2):
            rows = slice(part * HALF, (part + 1) * HALF)
            h[rows, :] = normalize(
                second[rows, :], table[3:4, WIDE : 2 * WIDE], table[3:4, 2 * WIDE : 3 * WIDE]
            ).astype(h.dtype)


def backward_norm_two(table, dtable, dy, second, dnormed, dlow, dlow_t):
    dtable[...] = jnp.zeros_like(dtable)
    for part in range(2):
        rows = slice(part * HALF, (part + 1) * HALF)
        grad, gain_sum, shift_sum = normalize_back(
            second[rows, :], dy[rows, :].astype(jnp.float32), table[3:4, WIDE : 2 * WIDE]
        )
        dnormed[rows, :] = grad
        dlow[rows, :] = grad.astype(dlow.dtype)
        dtable[3:4, 0:WIDE] += jnp.sum(grad, axis=0, keepdims=True)
        dtable[3:4, WIDE : 2 * WIDE] += gain_sum
        dtable[3:4, 2 * WIDE : 3 * WIDE] += shift_sum
    dlow_t[...] = dlow[...].T


def backward_down(size, grads, hidden, dlow_t, piece):
    @pl.loop(2 * piece, 2 * piece + 2)
    def _(i):
        start = aligned(i * size.down, 16)
        for half in range(2):
            columns = pl.ds(aligned(i * WIDE, WIDE) + half * HALF, HALF)
            value = dot_nn(dlow_t[...], hidden[:, columns])
            put_rows(grads, size.bs, 0, size.dps, start, size.down, value, 2 * half)


def backward_gelu(size, w, dtable, slope, dlow, dup, piece):
    @pl.loop(2 * piece, 2 * piece + 2)
    def _(i):
        start = aligned(i * size.down, 16)
        for half in range(2):
            columns = pl.ds(aligned(i * WIDE, WIDE) + half * HALF, HALF)
            blocks = (2 * half, 2 * half + 1)
            matrix = rows_of(w, size.bs, 0, size.dps, start, size.down, blocks)
            dupper = dot_nn(dlow[...], matrix) * slope[:, columns].astype(jnp.float32)
            dtable[2:3, columns] = jnp.sum(dupper, axis=0, keepdims=True)
            dup[:, columns] = dupper.astype(dup.dtype)


def backward_up(size, grads, normed, dup):
    count = HALF // size.up

    @pl.loop(0, 4)
    def _(i):
        for half in range(2):
            columns = pl.ds(aligned(i * WIDE, WIDE) + half * HALF, HALF)
            value = dot_tn(dup[:, columns], normed[...])
            first = (2 * i + half) * count
            put_rows(grads, size.bs, first, count, size.out, size.up, value)


def backward_normed(size, w, dnormed, dup):
    for half in range(2):
        columns = slice(half * HALF, (half + 1) * HALF)
        blocks = (2 * half, 2 * half + 1)
        matrix = rows_of(w, size.bs, 0, size.dps, size.out, size.up, blocks)
        dnormed[:, columns] = dnormed[:, columns] + dot_nn(dup[...], matrix)


def backward_norm_one(size, w, table, grads, dtable, first, attended, dnormed, dlow, dlow_t):
    for part in range(2):
        rows = slice(part * HALF, (part + 1) * HALF)
        grad, gain_sum, shift_sum = normalize_back(
            first[rows, :], dnormed[rows, :], table[1:2, WIDE : 2 * WIDE]
        )
        dnormed[rows, :] = grad
        dlow[rows, :] = grad.astype(dlow.dtype)
        dtable[1:2, 0:WIDE] += jnp.sum(grad, axis=0, keepdims=True)
        dtable[1:2, WIDE : 2 * WIDE] += gain_sum
        dtable[1:2, 2 * WIDE : 3 * WIDE] += shift_sum
    dlow_t[...] = dlow[...].T
    for block in (0, 2):
        columns = slice(block * LANES, (block + 2) * LANES)
        value = dot_nn(dlow_t[...], attended[:, columns])
        put_rows(grads, size.bs, 0, size.dps, 0, size.out, value, block)
    dlow[...] = dot_nn(dlow[...], out_rows(size, w)).astype(dlow.dtype)


def backward_attend(mixed, lse, dtable, dlow, dmixed, pair):
    scale = 1.0 / math.sqrt(HEAD)
    lane = pair * LANES
    columns = slice(lane, lane + LANES)
    key_columns = slice(WIDE + lane, WIDE + lane + LANES)
    value_columns = slice(2 * WIDE + lane, 2 * WIDE + lane + LANES)
    key_rows = mixed[:, key_columns]
    keys_t = key_rows.T
    values = mixed[:, value_columns]
    dkeys = jnp.zeros((WIDE, LANES), jnp.float32)
    dvalues = jnp.zeros((WIDE, LANES), jnp.float32)
    for part in range(2):
        rows = slice(part * HALF, (part + 1) * HALF)
        queries = mixed[rows, columns]
        grad_out = dlow[rows, columns]
        dqueries = []
        for head in range(2):
            query = queries * head_masks(scale)[head]
            grad = grad_out * head_masks(1.0)[head]
            probs = jnp.exp(dot_nt(key_rows, query) - lse[2 * pair + head, :, rows])
            dprobs = dot_nt(values, grad)
            delta = jnp.sum(probs * dprobs, axis=0, keepdims=True)
            dscores = (probs * (dprobs - delta)).astype(jnp.bfloat16)
            dvalues = dvalues + dot_nn(probs.astype(jnp.bfloat16), grad)
            dkeys = dkeys + dot_nn(dscores, query)
            dqueries.append(dot_nn(keys_t[head * HEAD : (head + 1) * HEAD], dscores))
        dquery = jnp.concatenate(dqueries, axis=0).T * scale
        dtable[0:1, columns] += jnp.sum(dquery, axis=0, keepdims=True)
        dmixed[rows, columns] = dquery.astype(dmixed.dtype)
    dmixed[:, key_columns] = dkeys.astype(dmixed.dtype)
    dmixed[:, value_columns] = dvalues.astype(dmixed.dtype)
    dtable[0:1, value_columns] = jnp.sum(dvalues, axis=0, keepdims=True)


def backward_mix(size, grads, h, dmixed, piece):
    count = QKV_TILE // size.qkv
    grad = dmixed[:, piece * QKV_TILE : (piece + 1) * QKV_TILE]
    put_rows(grads, size.bs, piece * count, count, 0, size.qkv, dot_tn(grad, h[...]))


def backward_input(size, w, dnormed, dmixed, dy):
    for half in range(2):
        columns = slice(half * HALF, (half + 1) * HALF)
        blocks = (2 * half, 2 * half + 1)
        matrix = rows_of(w, size.bs, 0, size.dps, 0, size.qkv, blocks)
        dy[:, columns] = (dnormed[:, columns] + dot_nn(dmixed[...], matrix)).astype(dy.dtype)


WINDOW = 384


def embed(size, emb, pick, x, wsel, h):
    rows = WIDE // size.dps
    first = rows_of(emb, size.bs, 0, size.dps, 0, rows)
    second = rows_of(emb, size.bs, 0, size.dps, rows, rows)
    long, middle, short = (pick[g : g + 1, :] for g in (2, 1, 0))
    wide = jnp.concatenate(
        [
            first[:, LANES : 2 * LANES] * long,
            first[:, 2 * LANES : 3 * LANES] * long + second[:, :LANES] * middle,
            first[:, 3 * LANES :] * long
            + second[:, LANES : 2 * LANES] * middle
            + second[:, 3 * LANES :] * short,
        ],
        axis=1,
    )
    wsel[...] = wide.T
    matrix = jnp.concatenate([wide, first[:, :LANES]], axis=1)
    h[...] = dot_nt(x[...], matrix).astype(h.dtype)


def embed_back(size, pick, x, wsel, dh, grads, series_grad):
    history = series_grad.shape[0]
    series_grad[...] = dot_nt(wsel[...], dh[...])[WINDOW - history :]
    sums = dot_tn(dh[...], x[...])
    long, middle, short = (pick[g : g + 1, :].astype(jnp.float32) for g in (2, 1, 0))
    parts = [sums[:, i * LANES : (i + 1) * LANES] for i in range(4)]
    parts = [
        parts[3],
        parts[0] * long,
        parts[1] * long,
        parts[2] * long,
        parts[1] * middle,
        parts[2] * middle,
        jnp.zeros_like(parts[0]),
        parts[2] * short,
    ]
    rows = WIDE // (SECT * size.dps)
    for pipe in range(SECT):
        block = (pipe % 2) * 2 + pipe // 2
        for dp in range(size.dps):
            start = (pipe * size.dps + dp) * rows
            piece = jnp.concatenate([part[start : start + rows] for part in parts], axis=0)
            grads[block, dp // size.bs, dp % size.bs] = piece.astype(grads.dtype)


def saved_shapes():
    low, wide = jnp.bfloat16, jnp.float32
    return [
        ((WIDE, WIDE), low),
        ((WIDE, 3 * WIDE), low),
        ((2 * SECT, 1, WIDE), wide),
        ((WIDE, WIDE), low),
        ((WIDE, WIDE), wide),
        ((WIDE, WIDE), low),
        ((WIDE, 4 * WIDE), low),
        ((WIDE, 4 * WIDE), low),
        ((WIDE, WIDE), wide),
        ((SECT, 4 * WIDE), wide),
    ]


def chunk_shape(size, rows):
    return (SECT, ZS, size.bs, rows, LANES)


def follow(plan, section, act, compute):
    seen = {}
    for step in plan:
        if len(step) == 1:
            piece = seen.get(step[0], 0)
            seen[step[0]] = piece + 1
            compute(step[0], piece)
            continue
        op, kind, offset = step
        where = section + offset
        if isinstance(where, int):
            if 0 <= where < SECT:
                act(op, kind, where)
        elif offset == 0:
            act(op, kind, where)
        else:
            inside = where < SECT if offset > 0 else where >= 0

            @pl.when(inside)
            def _():
                act(op, kind, where)


def forward_kernel(dps, *refs):
    size = Sizes(dps)
    pieces, x, pick, refs = refs[:4], refs[4], refs[5], refs[6:]
    out, wholes, wsel = refs[0], refs[1:5], refs[5]
    kept, local, refs = refs[6:16], refs[16:26], refs[26:]
    buffers, refs = refs[:4], refs[4:]
    w_sem, kept_sem, own_sem, p_send, p_recv, send, recv = refs
    h, mixed, lse, attended, first, normed, slope, hidden, second, table = local
    w_att, w_up, w_down, w_emb = buffers
    at = Place(dps)

    own = [
        pltpu.make_async_copy(
            pieces[kind].at[at.block],
            wholes[kind].at[at.pipe, at.block, at.z, at.b]
            if kind < EMB
            else wholes[kind].at[at.block, at.z, at.b],
            own_sem.at[kind],
        )
        for kind in range(4)
    ]
    copies_start(own)

    def split(kind, back):
        copies = []
        for k in range(1, SECT):
            if back:
                region = wholes[kind].at[at.pipe_at(SECT - k), at.block, at.z, at.b]
                src = region
            else:
                block = at.block_of(at.pipe_at(k))
                region = wholes[kind].at[at.pipe, block, at.z, at.b]
                src = pieces[kind].at[block]
            sems = p_send.at[kind, k - 1], p_recv.at[kind, k - 1]
            copies.append(remote(src, region, *sems, (at.pipe_at(k), at.dp)))
        return copies

    def chunk(kind, section):
        if kind == EMB:
            return Spread(at, wholes[kind], send.at[3 * SECT], recv.at[3 * SECT])
        number = 3 * section + kind
        return Spread(at, wholes[kind].at[section], send.at[number], recv.at[number])

    def load(kind, section, core):
        blocks = pl.ds(core * 2, 2)
        src, dst = wholes[kind], buffers[kind]
        if kind != EMB:
            src, dst = src.at[section], dst.at[section % 2]
        return pltpu.make_async_copy(src.at[blocks], dst.at[blocks], w_sem.at[kind, core])

    def loaded(kind, section):
        load(kind, section, at.c).wait()
        load(kind, section, 1 - at.c).wait()

    def act(op, kind, section):
        if op == 0:
            own_now = kind == EMB or (isinstance(section, int) and section == 0)
            if own_now:
                own[kind].wait()
            if own_now and kind != EMB:
                for copy in split(kind, True):
                    copy.wait_recv()
                for copy in split(kind, False):
                    copy.wait_send()
            chunk(kind, section).start(0)
        elif op < 4:
            chunk(kind, section).move(op - 1)
            if op == 3:
                load(kind, section, at.c).start()
        else:
            chunk(kind, section).land(3)
            load(kind, section, 1 - at.c).start()

    def saves(section, early):
        which = (1, 2, 3, 4, 5, 9) if early else (6, 7, 8)
        return [
            pltpu.make_async_copy(local[i], kept[i].at[section], kept_sem.at[i]) for i in which
        ]

    at.greet()
    for kind in range(3):
        copies_start(split(kind, False))
    table[...] = jnp.zeros_like(table)

    def before(name, piece):
        loaded(EMB, 0)
        embed(size, w_emb, pick, x, wsel, h)

    follow(FORWARD_START, 0, act, before)

    @pl.loop(0, SECT)
    def _(section):
        att, up, down = (ref.at[section % 2] for ref in (w_att, w_up, w_down))
        keep_h = pltpu.make_async_copy(h, kept[0].at[section], kept_sem.at[0])

        def compute(name, piece):
            if name == "mix":
                if piece == 0:

                    @pl.when(section > 0)
                    def _():
                        copies_wait(saves(section - 1, True))

                    keep_h.start()
                    loaded(0, section)
                    read_vectors(att, table, size.bs, size.qkv)
                forward_mix(size, att, table, h, mixed, piece)
            elif name == "attend":
                forward_attend(mixed, lse, attended, piece)
            elif name == "project":
                loaded(1, section)
                forward_project(size, up, table, h, attended, first, normed)
                copies_start(saves(section, True))
            elif name == "up":
                if piece == 0:

                    @pl.when(section > 0)
                    def _():
                        copies_wait(saves(section - 1, False))

                forward_up(size, up, table, normed, slope, hidden, piece)
            else:
                if piece == 0:
                    loaded(2, section)
                    keep_h.wait()
                forward_down(size, down, table, normed, hidden, second, h, piece)
                if piece == 1:
                    copies_start(saves(section, False))

        follow(FORWARD_PERIOD, section, act, compute)

    copies_wait(saves(SECT - 1, True))
    copies_wait(saves(SECT - 1, False))
    out[...] = h[...]


def forward_all(pieces, x, pick, dps):
    size = Sizes(dps)
    low = jnp.bfloat16
    shapes = saved_shapes()
    chunks = [chunk_shape(size, piece.shape[1]) for piece in pieces]
    anywhere = pl.BlockSpec(memory_space=pl.ANY)
    inside = pl.BlockSpec(memory_space=pltpu.VMEM)
    outs = [((WIDE, WIDE), low)]
    outs += [((SECT,) + shape, low) for shape in chunks[:3]] + [(chunks[3], low)]
    outs += [((WINDOW, WIDE), low)]
    outs += [((SECT,) + shape, dtype) for shape, dtype in shapes]
    scratch = shapes + [((2,) + shape, low) for shape in chunks[:3]] + [(chunks[3], low)]
    slots = Spread.slots(size.bs)
    dma = pltpu.SemaphoreType.DMA
    return pl.pallas_call(
        partial(forward_kernel, dps),
        out_shape=[jax.ShapeDtypeStruct(shape, dtype) for shape, dtype in outs],
        in_specs=[anywhere] * 4 + [inside] * 2,
        out_specs=[inside] + [anywhere] * 4 + [inside] + [anywhere] * len(shapes),
        scratch_shapes=[pltpu.VMEM(shape, dtype) for shape, dtype in scratch]
        + [
            dma((4, 2)),
            dma((len(shapes),)),
            dma((4,)),
            dma((3, SECT - 1)),
            dma((3, SECT - 1)),
            dma((1 + 3 * SECT, slots)),
            dma((1 + 3 * SECT, slots)),
        ],
        compiler_params=pltpu.CompilerParams(
            collective_id=0, has_side_effects=True, vmem_limit_bytes=52 * 1024 * 1024
        ),
        name="gather_forward",
    )(*pieces, x, pick)


def backward_kernel(dps, att, up, down, cotangent, x, pick, wsel, *refs):
    size = Sizes(dps)
    kept, refs = refs[:10], refs[10:]
    series_grad, outs, refs = refs[0], refs[1:5], refs[5:]
    local, refs = refs[:9], refs[9:]
    tables, w_att, w_up, w_down, dtable, dy, dnormed, dlow, dlow_t, dmixed, dup = refs[:11]
    refs = refs[11:]
    kinds = [
        (refs[9 * k], refs[9 * k + 1], refs[9 * k + 2 : 9 * k + 8], refs[9 * k + 8])
        for k in range(4)
    ]
    refs = refs[36:]
    w_sem, kept_sem, table_sem, out_sem, p_send, p_recv, send, recv, credit = refs
    h, mixed, lse, attended, first, normed, slope, hidden, second = local
    at = Place(dps)
    last = SECT - 1

    def weights(kind, section):
        src, dst = ((att, w_att), (up, w_up), (down, w_down))[kind]
        return pltpu.make_async_copy(src.at[section], dst, w_sem.at[kind])

    def loads(section, dense):
        which = (5, 6, 7, 8) if dense else (0, 1, 2, 3, 4)
        found = [
            pltpu.make_async_copy(kept[i].at[section], local[i], kept_sem.at[i]) for i in which
        ]
        return found + [weights(kind, section) for kind in ((1, 2) if dense else (0,))]

    def chunk(kind, i):
        grads, totals, bufs, finals = kinds[kind]
        return Fold(
            at,
            grads,
            totals.at[i % 2],
            bufs,
            finals.at[i],
            send.at[kind],
            recv.at[kind],
            credit.at[kind],
        )

    def hand_over(kind, i):
        landing = outs[kind].at[at.block]
        final = kinds[kind][3].at[i]
        return (
            pltpu.make_async_copy(final, landing, out_sem.at[kind]),
            remote(final, landing, p_send.at[kind, i], p_recv.at[kind, at.pipe], (last - i, at.dp)),
        )

    def act(op, kind, i):
        again, more = (False, False) if kind == EMB else (i > 0, i < last)
        if op == 0:
            chunk(kind, i).start(0, again)
        elif op < 4:
            chunk(kind, i).move(op - 1, again, more)
        else:
            chunk(kind, i).land(3, more)
            if kind == EMB:
                outs[kind][...] = kinds[kind][3][0]
            else:
                here, away = hand_over(kind, i)

                @pl.when(at.pipe == last - i)
                def _():
                    here.start()

                @pl.when(at.pipe != last - i)
                def _():
                    away.start()

    copies_start(loads(last, True))
    get_tables = pltpu.make_async_copy(kept[9], tables, table_sem)
    get_tables.start()
    copies_start(loads(last, False))
    dy[...] = cotangent[...]
    at.greet()
    get_tables.wait()

    @pl.loop(0, SECT)
    def _(i):
        section = last - i
        table = tables.at[section]

        def compute(name, piece):
            if name == "norm2":
                copies_wait(loads(section, True))
                backward_norm_two(table, dtable, dy, second, dnormed, dlow, dlow_t)
            elif name == "down":
                backward_down(size, kinds[2][0], hidden, dlow_t, piece)
            elif name == "gelu":
                backward_gelu(size, w_down, dtable, slope, dlow, dup, piece)
            elif name == "up":
                backward_up(size, kinds[1][0], normed, dup)
            elif name == "normed":
                backward_normed(size, w_up, dnormed, dup)
            elif name == "norm1":
                copies_wait(loads(section, False))
                backward_norm_one(
                    size, w_up, table, kinds[1][0], dtable, first, attended, dnormed, dlow, dlow_t
                )

                @pl.when(section > 0)
                def _():
                    copies_start(loads(section - 1, True))

            elif name == "attend":
                backward_attend(mixed, lse, dtable, dlow, dmixed, piece)
            elif name == "mix":
                backward_mix(size, kinds[0][0], h, dmixed, piece)
                if piece == 1:
                    write_vectors(kinds[0][0], dtable, size.bs, size.qkv)
            else:
                backward_input(size, w_att, dnormed, dmixed, dy)

                @pl.when(section > 0)
                def _():
                    copies_start(loads(section - 1, False))

        follow(BACKWARD_PERIOD, i, act, compute)

    def after(name, piece):
        embed_back(size, pick, x, wsel, dy, kinds[EMB][0], series_grad)

    follow(BACKWARD_END, 0, act, after)

    for kind in range(3):
        for i in range(SECT):
            here, away = hand_over(kind, i)

            @pl.when(at.pipe == last - i)
            def _():
                here.wait()

            @pl.when(at.pipe != last - i)
            def _():
                away.wait_send()

        for k in range(1, SECT):
            other = at.pipe_at(k)
            landing = outs[kind].at[at.block_of(other)]
            sems = p_send.at[kind, 0], p_recv.at[kind, other]
            remote(landing, landing, *sems, (other, at.dp)).wait_recv()


def backward_all(weights, cotangent, x, pick, wsel, kept, history, dps):
    size = Sizes(dps)
    low, wide = jnp.bfloat16, jnp.float32
    anywhere = pl.BlockSpec(memory_space=pl.ANY)
    inside = pl.BlockSpec(memory_space=pltpu.VMEM)
    shapes = saved_shapes()
    rows_emb = 8 * WIDE // (SECT * dps)
    kind_rows = (size.att, size.dense, size.wide, rows_emb)
    scratch = shapes[:9] + [((SECT,) + shapes[9][0], wide)]
    scratch += [(chunk_shape(size, rows), low) for rows in kind_rows[:3]]
    scratch += [
        (shapes[9][0], wide),
        ((WIDE, WIDE), low),
        ((WIDE, WIDE), wide),
        ((WIDE, WIDE), low),
        ((WIDE, WIDE), low),
        ((WIDE, 3 * WIDE), low),
        ((WIDE, 4 * WIDE), low),
    ]
    for kind, rows in enumerate(kind_rows):
        sets, results = (1, 1) if kind == EMB else (2, SECT)
        scratch += [
            (chunk_shape(size, rows), low),
            ((sets, 2, ZS, size.bs, rows, LANES), low),
        ]
        scratch += [(shape, low) for shape in Fold.buffers(size.bs, rows)]
        scratch += [((results, rows, LANES), low)]
    slots = Fold.slots(size.bs)
    dma = pltpu.SemaphoreType.DMA
    return pl.pallas_call(
        partial(backward_kernel, dps),
        out_shape=[jax.ShapeDtypeStruct((history, WIDE), wide)]
        + [jax.ShapeDtypeStruct((SECT, rows, LANES), low) for rows in kind_rows[:3]]
        + [jax.ShapeDtypeStruct((rows_emb, LANES), low)],
        in_specs=[anywhere] * 3 + [inside] * 4 + [anywhere] * len(kept),
        out_specs=[inside] + [anywhere] * 3 + [inside],
        scratch_shapes=[pltpu.VMEM(shape, dtype) for shape, dtype in scratch]
        + [
            dma((3,)),
            dma((9,)),
            dma(()),
            dma((3,)),
            dma((3, SECT)),
            dma((3, SECT)),
            dma((4, slots)),
            dma((4, slots)),
            pltpu.SemaphoreType.REGULAR((4, slots)),
        ],
        compiler_params=pltpu.CompilerParams(
            collective_id=1, has_side_effects=True, vmem_limit_bytes=60 * 1024 * 1024
        ),
        name="backward_fold",
    )(*weights, cotangent, x, pick, wsel, *kept)


def by_block(slab):
    split = slab.reshape(slab.shape[:-1] + (SECT, LANES))
    return jnp.moveaxis(split, -2, -3)


def pack_vectors(gains, biases):
    flat = jnp.concatenate([gains, biases], axis=1)
    flat = jnp.pad(flat, ((0, 0), (0, 16 * 512 - flat.shape[1])))
    return flat.reshape(flat.shape[0], 16, 512)


def pack_embedding(matrix, shift):
    wide = matrix.T
    first = jnp.pad(wide[:, L1 + L2 :], ((0, 0), (512 - L3 - GROUPS, 0)))
    return jnp.concatenate(
        [
            shift.T,
            first,
            jnp.pad(wide[:, L1 : L1 + L2], ((0, 0), (256 - L2, 0))),
            jnp.pad(wide[:, :L1], ((0, 0), (256 - L1, 0))),
        ],
        axis=1,
    )


def unpack_embedding(packed):
    matrix = jnp.concatenate(
        [packed[:, 1024 - L1 :], packed[:, 768 - L2 : 768], packed[:, 512 - L3 : 512]], axis=1
    )
    return matrix.T, packed[:, :GROUPS].T


def per_device(
    series,
    groups,
    cotangent,
    embed_weight,
    embed_bias,
    qkv_weight,
    out_weight,
    up_weight,
    down_weight,
    gains,
    biases,
):
    dps = lax.axis_size("dp")
    low = jnp.bfloat16
    width = qkv_weight.shape[2]
    rows_qkv, rows_out = qkv_weight.shape[1], out_weight.shape[1]
    rows_down = down_weight.shape[1] * down_weight.shape[2] // width
    n_gains, n_biases = gains.shape[1], biases.shape[1]
    down_low = down_weight[0].astype(low).reshape(-1, 4, width)
    att_in = jnp.concatenate(
        [
            qkv_weight[0].astype(low),
            pack_vectors(gains.astype(low), biases.astype(low))[0],
        ]
    )
    up_in = jnp.concatenate([out_weight[0].astype(low), up_weight[0].astype(low)])
    down_in = jnp.moveaxis(down_low, 1, 0).reshape(rows_down, width)
    emb_in = pack_embedding(embed_weight.astype(low), embed_bias.astype(low))
    emb_in = jnp.concatenate([emb_in[:, :512], emb_in[:, 512:]])
    hist = series.shape[1]
    pick = (jnp.arange(GROUPS, dtype=jnp.int32) == groups[0]).astype(low)
    x = jnp.concatenate(
        [
            jnp.pad(series[0].T, ((0, 0), (WINDOW - hist, 0))),
            jnp.broadcast_to(jnp.pad(pick, (0, LANES - GROUPS)), (series.shape[2], LANES)),
        ],
        axis=1,
    )
    pick = jnp.broadcast_to(pick[:, None], (GROUPS, LANES))
    pieces = [by_block(piece) for piece in (att_in, up_in, down_in, emb_in)]
    block_output, att, up, down, _, wsel, *kept = forward_all(pieces, x, pick, dps)
    series_grad, att_out, up_out, down_out, emb_out = backward_all(
        (att, up, down), cotangent[0], x, pick, wsel, kept, hist, dps
    )
    att_out = jnp.moveaxis(att_out, 0, 1).reshape(-1, width).astype(jnp.float32)
    up_out = jnp.moveaxis(up_out, 0, 1).reshape(-1, width).astype(jnp.float32)
    emb_out = jnp.moveaxis(emb_out.reshape(8, -1, LANES), 0, 1).reshape(-1, 1024)
    embed_w_grad, embed_b_grad = unpack_embedding(emb_out.astype(jnp.float32))
    vec_out = att_out[rows_qkv:].reshape(1, -1)
    down_out = down_out.astype(jnp.float32).reshape(SECT, 4, -1, LANES)
    down_out = jnp.transpose(down_out, (2, 1, 0, 3))
    return (
        block_output[None],
        series_grad[None],
        embed_w_grad,
        embed_b_grad,
        att_out[:rows_qkv][None],
        up_out[:rows_out][None],
        up_out[rows_out:][None],
        down_out.reshape(1, -1, down_weight.shape[2]),
        vec_out[:, :n_gains],
        vec_out[:, n_gains : n_gains + n_biases],
    )


def solution(mesh):
    return jax.shard_map(
        per_device,
        mesh=mesh,
        in_specs=(
            P(("pipe", "dp"), None, None),
            P(("pipe", "dp")),
            P(("pipe", "dp"), None, None),
            P(None, "dp"),
            P(None, "dp"),
            P("pipe", "dp", None),
            P("pipe", "dp", None),
            P("pipe", "dp", None),
            P("pipe", "dp", None),
            P("pipe", "dp"),
            P("pipe", "dp"),
        ),
        out_specs=(
            P(("pipe", "dp"), None, None),
            P(("pipe", "dp"), None, None),
            P(None, ("pipe", "dp")),
            P(None, ("pipe", "dp")),
            P("pipe", "dp", None),
            P("pipe", "dp", None),
            P("pipe", "dp", None),
            P("pipe", "dp", None),
            P("pipe", "dp"),
            P("pipe", "dp"),
        ),
        check_vma=False,
    )
```

```python
from functools import partial
import math

import jax
import jax.numpy as jnp
from jax import lax
from jax.experimental import pallas as pl
from jax.experimental.pallas import tpu as pltpu
from jax.sharding import PartitionSpec as P

HEAD = 64
L1 = 96
L2 = 192
L3 = 336
GROUPS = 3


NORM_EPS = 1e-05


MESH = pl.DeviceIdType.MESH
LANES = 128
ZS = 4
SECT = 4
EMB = 3


class Place:
    def __init__(self, dps):
        self.bs = dps // ZS
        pipe = lax.axis_index("pipe")
        dp = lax.axis_index("dp")
        self.pipe, self.dp = pipe, dp
        self.x, self.c = pipe // 2, pipe % 2
        self.z, self.b = dp // self.bs, dp % self.bs
        self.block = self.c * 2 + self.x
        self.x_peer = ((1 - self.x) * 2 + self.c, dp)
        self.core_peer = (self.x * 2 + 1 - self.c, dp)

    def block_of(self, pipe):
        return (pipe % 2) * 2 + pipe // 2

    def pipe_at(self, step):
        return (self.pipe + step) % SECT

    def z_at(self, step):
        return (self.z + step) % ZS

    def b_at(self, step):
        return (self.b + step) % self.bs

    def z_peer(self, step):
        return (self.pipe, self.z_at(step) * self.bs + self.b)

    def b_peer(self, step):
        return (self.pipe, self.z * self.bs + self.b_at(step))

    def plane_steps(self):
        return [(dx, k) for dx in range(2) for k in range(self.bs) if (dx, k) != (0, 0)]

    def plane_peer(self, dx, step):
        x = self.x if dx == 0 else 1 - self.x
        return (x * 2 + self.c, self.z * self.bs + self.b_at(step))

    def greet(self):
        barrier = pltpu.get_barrier_semaphore()
        peers = [(self.pipe_at(k), self.dp) for k in range(1, SECT)]
        peers += [self.z_peer(k) for k in range(1, ZS)]
        peers += [self.b_peer(k) for k in range(1, self.bs)]
        peers += [self.plane_peer(1, k) for k in range(1, self.bs)]
        for peer in peers:
            pl.semaphore_signal(barrier, inc=1, device_id=peer, device_id_type=MESH)
        pl.semaphore_wait(barrier, len(peers))


def remote(src, dst, send, recv, peer):
    return pltpu.make_async_remote_copy(
        src_ref=src, dst_ref=dst, send_sem=send, recv_sem=recv, device_id=peer, device_id_type=MESH
    )


FORWARD_START = (
    (0, 3, 0),
    (0, 0, 0),
    (0, 2, -1, "wide"),
    (1, 3, 0),
    (0, 1, 0),
    (2, 3, 0),
    (1, 0, 0),
    (0, 2, 0),
    (3, 3, 0),
    (0, 0, -1, "wide"),
    (2, 0, 0),
    (1, 1, 0),
    (0, 0, 1),
    (0, 1, 1),
    (1, 2, 0),
    (3, 0, 0),
    (2, 1, 0),
    (4, 0, 0),
    (1, 0, 1),
    (0, 2, 1),
    (2, 2, 0),
    (2, 0, 1),
    (4, 3, 0),
    ("embed",),
    (1, 0, -1, "wide"),
)
FORWARD_PERIOD = (
    ("mix",),
    (1, 1, 1),
    ("mix",),
    (0, 0, 2),
    (3, 1, 0),
    ("attend",),
    ("attend",),
    ("attend",),
    (2, 2, 3, "wide"),
    (3, 2, 3, "wide"),
    (4, 1, 0),
    (0, 1, 2),
    ("attend",),
    (1, 2, 1),
    ("project",),
    ("up",),
    (3, 0, 1),
    (2, 0, 1, "wide"),
    (3, 0, 1, "wide"),
    (2, 1, 1),
    ("up",),
    (3, 2, 0),
    (4, 0, 1),
    ("up",),
    (4, 2, 3, "wide"),
    (1, 0, 2),
    ("up",),
    (0, 2, 2),
    (1, 2, 1, "wide"),
    (4, 2, 0),
    (4, 0, 2, "wide"),
    (2, 2, 1),
    (2, 0, 2),
    ("down",),
    ("down",),
)
BACKWARD_PERIOD = (
    (2, 2, -1),
    ("norm2",),
    (0, 0, -1),
    ("down",),
    ("down",),
    (3, 0, -2),
    (4, 2, -2),
    (2, 0, 3, "wide"),
    (0, 2, 0),
    (2, 1, -1),
    ("gelu",),
    (0, 2, 0, "wide"),
    (3, 2, 2, "wide"),
    (4, 2, 2, "wide"),
    ("gelu",),
    (1, 2, 0),
    ("up",),
    ("normed",),
    (3, 2, -1),
    (3, 0, 3, "wide"),
    (4, 0, 3, "wide"),
    (1, 0, -1),
    (4, 1, -2),
    ("norm1",),
    (0, 1, 0),
    (1, 2, 0, "wide"),
    (3, 1, -1),
    ("attend",),
    ("attend",),
    (1, 1, 0),
    (4, 0, -2),
    (0, 0, 1, "wide"),
    ("attend",),
    ("attend",),
    (2, 0, -1),
    (1, 0, 1, "wide"),
    ("mix",),
    ("mix",),
    (2, 2, 1, "wide"),
    ("input",),
)
BACKWARD_END = (
    (2, 2, 3),
    (0, 0, 3),
    (3, 0, 2),
    (4, 2, 2),
    (2, 1, 3),
    (3, 2, 3),
    (1, 0, 3),
    (4, 1, 2),
    (3, 1, 3),
    ("embed",),
    (4, 0, 2),
    (0, 3, 0),
    (2, 0, 3),
    (1, 3, 0),
    (3, 0, 3),
    (2, 3, 0),
    (3, 3, 0),
    (4, 2, 3),
    (4, 1, 3),
    (4, 0, 3),
    (4, 3, 0),
)


def copies_start(copies):
    for copy in copies:
        copy.start()


def copies_wait(copies):
    for copy in copies:
        copy.wait()


class Spread:
    def __init__(self, at, out, send, recv, half=ZS // 2):
        self.at, self.out, self.send, self.recv = at, out, send, recv
        nb = at.bs - 1
        self.slot_z = 0
        self.slot_b1 = ZS - 1
        self.slot_x1 = self.slot_b1 + nb
        self.slot_x2 = self.slot_x1 + 1
        self.slot_b2 = self.slot_x2 + 1
        self.slot_c = self.slot_b2 + nb
        self.half = half

    @staticmethod
    def slots(bs):
        return ZS - 1 + 2 * (bs - 1) + 3

    def copy(self, region, slot, peer):
        return remote(region, region, self.send.at[slot], self.recv.at[slot], peer)

    def copies(self, stage, back):
        at, out, half = self.at, self.out, self.half
        rest = pl.ds(half, ZS - half)
        x_block = at.c * 2 + 1 - at.x if back else at.block
        if stage == 0:
            return [
                self.copy(
                    out.at[at.block, at.z_at(ZS - k) if back else at.z, at.b],
                    self.slot_z + k - 1,
                    at.z_peer(k),
                )
                for k in range(1, ZS)
            ]
        if stage == 3:
            core = 1 - at.c if back else at.c
            return [self.copy(out.at[pl.ds(core * 2, 2)], self.slot_c, at.core_peer)]
        copies = []
        for k in range(1, at.bs):
            b = at.b_at(at.bs - k) if back else at.b
            if stage == 1:
                region, slot = out.at[at.block, pl.ds(0, half), b], self.slot_b1
            else:
                region, slot = out.at[pl.ds(at.c * 2, 2), rest, b], self.slot_b2
            copies.append(self.copy(region, slot + k - 1, at.b_peer(k)))
        if stage == 1:
            region, slot = out.at[x_block, rest, at.b], self.slot_x1
        else:
            region, slot = out.at[x_block, pl.ds(0, half)], self.slot_x2
        copies.append(self.copy(region, slot, at.x_peer))
        return copies

    def start(self, stage):
        copies_start(self.copies(stage, False))

    def land(self, stage):
        for copy in self.copies(stage, True):
            copy.wait_recv()
        for copy in self.copies(stage, False):
            copy.wait_send()

    def move(self, stage):
        self.land(stage)
        self.start(stage + 1)


class SpreadWide(Spread):
    @staticmethod
    def slots(bs):
        return 2 * bs - 1 + ZS

    def copies(self, stage, back):
        at, out = self.at, self.out
        if stage == 0:
            copies = []
            for i, (dx, k) in enumerate(at.plane_steps()):
                x = at.x if dx == 0 else 1 - at.x
                block = at.c * 2 + x if back else at.block
                b = at.b_at(at.bs - k) if back else at.b
                copies.append(self.copy(out.at[block, at.z, b], i, at.plane_peer(dx, k)))
            return copies
        if stage == 1:
            return [
                self.copy(
                    out.at[pl.ds(at.c * 2, 2), at.z_at(ZS - k) if back else at.z],
                    2 * at.bs - 1 + k - 1,
                    at.z_peer(k),
                )
                for k in range(1, ZS)
            ]
        if stage == 2:
            return []
        core = 1 - at.c if back else at.c
        return [self.copy(out.at[pl.ds(core * 2, 2)], 2 * at.bs + ZS - 2, at.core_peer)]


class Fold:
    def __init__(self, at, grads, total, landing, bufs, final, send, recv, credit, half):
        self.at, self.grads, self.total = at, grads, total
        self.landing, self.bufs, self.final = landing, bufs, final
        self.send, self.recv, self.credit = send, recv, credit
        self.half = half
        nb = at.bs - 1
        self.slot_x1 = 1
        self.slot_b1 = 2
        self.slot_x2 = 2 + nb
        self.slot_b2 = 3 + nb
        self.slot_z = 3 + 2 * nb

    @staticmethod
    def slots(bs):
        return 3 + 2 * (bs - 1) + ZS - 1

    @staticmethod
    def buffers(bs, rows, half):
        nb = max(bs - 1, 1)
        rest = ZS - half
        return [
            (half, bs, rows, LANES),
            (nb, 2, rest, rows, LANES),
            (rest, rows, LANES),
            (nb, half, rows, LANES),
            (ZS - 1, rows, LANES),
        ]

    def core_parts(self):
        other = self.grads.at[pl.ds((1 - self.at.c) * 2, 2)]
        return [(other, self.landing, 0, self.at.core_peer, self.at.core_peer)]

    def parts(self, stage):
        at, half, total, bufs = self.at, self.half, self.total, self.bufs
        if stage == 0:
            return self.core_parts()
        if stage == 3:
            return [
                (
                    total.at[at.x, at.z_at(k), at.b],
                    bufs[4].at[k - 1],
                    self.slot_z + k - 1,
                    at.z_peer(k),
                    at.z_peer(ZS - k),
                )
                for k in range(1, ZS)
            ]
        rest = pl.ds(half, ZS - half)
        found = []
        for k in range(1, at.bs):
            if stage == 1:
                src, buf, slot = total.at[:, rest, at.b_at(k)], bufs[1], self.slot_b1
            else:
                src, buf, slot = total.at[at.x, pl.ds(0, half), at.b_at(k)], bufs[3], self.slot_b2
            found.append((src, buf.at[k - 1], slot + k - 1, at.b_peer(k), at.b_peer(at.bs - k)))
        if stage == 1:
            src, buf, slot = total.at[1 - at.x, pl.ds(0, half)], bufs[0], self.slot_x1
        else:
            src, buf, slot = total.at[1 - at.x, rest, at.b], bufs[2], self.slot_x2
        found.append((src, buf, slot, at.x_peer, at.x_peer))
        return found

    def start(self, stage, again):
        for src, buf, slot, to, _ in self.parts(stage):
            if again is not False:

                @pl.when(again)
                def _():
                    pl.semaphore_wait(self.credit.at[slot], 1)

            remote(src, buf, self.send.at[slot], self.recv.at[slot], to).start()

    def land(self, stage, more):
        parts = self.parts(stage)
        for src, buf, slot, to, _ in parts:
            remote(src, buf, self.send.at[slot], self.recv.at[slot], to).wait()
        self.add(stage)
        if more is not False:

            @pl.when(more)
            def _():
                for _, _, slot, _, origin in parts:
                    pl.semaphore_signal(
                        self.credit.at[slot], inc=1, device_id=origin, device_id_type=MESH
                    )

    def add_core(self):
        at, bs, total = self.at, self.at.bs, self.total

        @pl.loop(0, 2 * ZS * bs)
        def _(i):
            z, b = i // bs % ZS, i % bs
            x = i // (ZS * bs)
            total[x, z, b] = self.grads[at.c * 2 + x, z, b] + self.landing[x, z, b]

    def add(self, stage):
        at, half, bs = self.at, self.half, self.at.bs
        total, bufs = self.total, self.bufs
        rest = ZS - half
        if stage == 0:
            self.add_core()
        elif stage == 1:

            @pl.loop(0, half * bs)
            def _(i):
                z, b = i // bs, i % bs
                total[at.x, z, b] = total[at.x, z, b] + bufs[0][z, b]

            @pl.loop(0, 2 * rest)
            def _(i):
                x, z = i // rest, i % rest
                for k in range(bs - 1):
                    total[x, half + z, at.b] = total[x, half + z, at.b] + bufs[1][k, x, z]

        elif stage == 2:

            @pl.loop(0, rest)
            def _(z):
                total[at.x, half + z, at.b] = total[at.x, half + z, at.b] + bufs[2][z]

            @pl.loop(0, half)
            def _(z):
                for k in range(bs - 1):
                    total[at.x, z, at.b] = total[at.x, z, at.b] + bufs[3][k, z]

        else:
            self.finish([bufs[4][k] for k in range(ZS - 1)])

    def finish(self, pieces):
        at = self.at
        done = self.total[at.x, at.z, at.b].astype(jnp.float32)
        for piece in pieces:
            done = done + piece.astype(jnp.float32)
        self.final[...] = done.astype(self.final.dtype)

    def move(self, stage, again, more):
        self.land(stage, more)
        self.start(stage + 1, again)


class FoldWide(Fold):
    @staticmethod
    def slots(bs):
        return 1 + ZS - 1 + 2 * bs - 1

    @staticmethod
    def buffers(bs, rows):
        return [(ZS - 1, 2, bs, rows, LANES), (2 * bs - 1, rows, LANES)]

    def parts(self, stage):
        at, total, bufs = self.at, self.total, self.bufs
        if stage == 0:
            return self.core_parts()
        if stage == 1:
            return [
                (total.at[:, at.z_at(k)], bufs[0].at[k - 1], k, at.z_peer(k), at.z_peer(ZS - k))
                for k in range(1, ZS)
            ]
        if stage == 3:
            return []
        found = []
        for i, (dx, k) in enumerate(at.plane_steps()):
            x = at.x if dx == 0 else 1 - at.x
            src = total.at[x, at.z, at.b_at(k)]
            found.append(
                (src, bufs[1].at[i], ZS + i, at.plane_peer(dx, k), at.plane_peer(dx, at.bs - k))
            )
        return found

    def add(self, stage):
        at, bs = self.at, self.at.bs
        total, bufs = self.total, self.bufs
        if stage == 0:
            self.add_core()
        elif stage == 1:

            @pl.loop(0, 2 * bs)
            def _(i):
                x, b = i // bs, i % bs
                for k in range(ZS - 1):
                    total[x, at.z, b] = total[x, at.z, b] + bufs[0][k, x, b]

        elif stage == 3:
            self.finish([bufs[1][i] for i in range(2 * bs - 1)])


HALF = 256
WIDE = 512
QKV_TILE = 768
VEC_ROWS = 16


def dot_nt(a, b):
    return lax.dot_general(a, b, (((1,), (1,)), ((), ())), preferred_element_type=jnp.float32)


def dot_nn(a, b):
    return lax.dot_general(a, b, (((1,), (0,)), ((), ())), preferred_element_type=jnp.float32)


def dot_tn(a, b):
    return lax.dot_general(a, b, (((0,), (0,)), ((), ())), preferred_element_type=jnp.float32)


def aligned(index, unit):
    return pl.multiple_of(index, unit)


def rows_of(ref, bs, first, count, start, rows, blocks=range(SECT)):
    parts = []
    for i in range(count):
        d = first + i
        place = (d // bs, d % bs)
        parts.append(
            jnp.concatenate(
                [ref[(lb,) + place + (pl.ds(start, rows), slice(None))] for lb in blocks], axis=1
            )
        )
    return parts[0] if count == 1 else jnp.concatenate(parts, axis=0)


def put_rows(ref, bs, first, count, start, rows, value, block=0):
    value = value.astype(ref.dtype)
    for i in range(count):
        d = first + i
        place = (d // bs, d % bs)
        for lane in range(value.shape[1] // LANES):
            ref[(block + lane,) + place + (pl.ds(start, rows), slice(None))] = value[
                i * rows : (i + 1) * rows, lane * LANES : (lane + 1) * LANES
            ]


def vector_pieces(dps):
    n_gains, n_biases = 2 * WIDE // dps, 10 * WIDE // dps
    starts = [(0, 0), (0, 2), (1, 0), (1, 2), (2, 0), (2, 1), (2, 2), (2, 3), (3, 0), (3, 2)]
    pieces = []
    for d in range(dps):
        at = 0
        while at < n_gains + n_biases:
            if at < n_gains:
                index = d * n_gains + at
                row, column = (1, 3)[index // WIDE], WIDE + index % WIDE
                left = n_gains - at
            else:
                index = d * n_biases + at - n_gains
                row, part = starts[index // WIDE]
                column = part * WIDE + index % WIDE
                left = n_gains + n_biases - at
            size = min(left, LANES - at % LANES, LANES - column % LANES)
            pieces.append((d, at // WIDE, at % WIDE, row, column, size))
            at += size
    return pieces


def read_vectors(ref, table, bs, start):
    dps = ZS * bs
    tiles = {}
    for d, row, lane, to_row, to_lane, size in vector_pieces(dps):
        key = (d, lane // LANES)
        if key not in tiles:
            tile = ref[lane // LANES, d // bs, d % bs, start : start + VEC_ROWS, :]
            tiles[key] = tile.astype(jnp.float32)
        off = lane % LANES
        table[to_row : to_row + 1, to_lane : to_lane + size] = tiles[key][
            row : row + 1, off : off + size
        ]


def write_vectors(ref, table, bs, start):
    dps = ZS * bs
    found = {}
    for d, row, lane, to_row, to_lane, size in vector_pieces(dps):
        piece = table[to_row : to_row + 1, to_lane : to_lane + size]
        found.setdefault((d, lane // LANES), {}).setdefault(row, []).append(piece)
    row_id = lax.broadcasted_iota(jnp.int32, (VEC_ROWS, LANES), 0)
    for d in range(dps):
        for lb in range(SECT):
            tile = jnp.zeros((VEC_ROWS, LANES), jnp.float32)
            for row, pieces in found.get((d, lb), {}).items():
                have = sum(piece.shape[1] for piece in pieces)
                if have < LANES:
                    pieces = pieces + [jnp.zeros((1, LANES - have), jnp.float32)]
                line = pieces[0] if len(pieces) == 1 else jnp.concatenate(pieces, axis=1)
                tile = jnp.where(row_id == row, line, tile)
            ref[lb, d // bs, d % bs, start : start + VEC_ROWS, :] = tile.astype(ref.dtype)


def normalize(x, gain, shift):
    mean = jnp.mean(x, axis=1, keepdims=True)
    centred = x - mean
    scale = lax.rsqrt(jnp.mean(centred * centred, axis=1, keepdims=True) + NORM_EPS)
    return centred * scale * gain + shift


def normalize_back(x, grad, gain):
    mean = jnp.mean(x, axis=1, keepdims=True)
    centred = x - mean
    scale = lax.rsqrt(jnp.mean(centred * centred, axis=1, keepdims=True) + NORM_EPS)
    unit = centred * scale
    inner = grad * gain
    first = jnp.mean(inner, axis=1, keepdims=True)
    second = jnp.mean(inner * unit, axis=1, keepdims=True)
    out = scale * (inner - first - unit * second)
    return out, jnp.sum(grad * unit, axis=0, keepdims=True), jnp.sum(grad, axis=0, keepdims=True)


def gelu_pair(u):
    bell = jnp.exp(-0.5 * (u * u))
    t = 1.0 / (1.0 + 0.23164188824 * jnp.abs(u))
    tail = 0.5307027145 * t
    tail = (tail - 0.7265760135) * t
    tail = (tail + 0.7107068705) * t
    tail = (tail - 0.142248368) * t
    tail = (tail + 0.127414796) * t * bell
    below = jnp.where(u < 0.0, tail, 1.0 - tail)
    return u * below, below + u * (0.3989422804014327 * bell)


def head_masks(scale):
    lane = lax.broadcasted_iota(jnp.int32, (1, LANES), 1)
    first = jnp.where(lane < HEAD, scale, 0.0).astype(jnp.bfloat16)
    second = jnp.where(lane < HEAD, 0.0, scale).astype(jnp.bfloat16)
    return first, second


class Sizes:
    def __init__(self, dps):
        self.dps, self.bs = dps, dps // ZS
        self.qkv, self.out, self.up, self.down = (
            3 * WIDE // dps,
            WIDE // dps,
            4 * WIDE // dps,
            WIDE // dps,
        )
        self.att = self.qkv + VEC_ROWS
        self.dense = self.out + self.up
        self.wide = 4 * self.down


def qkv_rows(size, w, tile):
    count = QKV_TILE // size.qkv
    return rows_of(w, size.bs, tile * count, count, 0, size.qkv)


def out_rows(size, w):
    return rows_of(w, size.bs, 0, size.dps, 0, size.out)


def up_rows(size, w, tile):
    count = HALF // size.up
    return rows_of(w, size.bs, tile * count, count, size.out, size.up)


def forward_mix(size, w, table, h, mixed, piece):
    columns = slice(piece * QKV_TILE, (piece + 1) * QKV_TILE)
    mixed[:, columns] = (
        dot_nt(h[...], qkv_rows(size, w, piece)) + table[0:1, columns]
    ).astype(mixed.dtype)


def forward_attend(mixed, lse, attended, pair):
    lane = pair * LANES
    key_rows = mixed[:, WIDE + lane : WIDE + lane + LANES]
    values = mixed[:, 2 * WIDE + lane : 2 * WIDE + lane + LANES].T

    for part in range(2):
        rows = slice(part * HALF, (part + 1) * HALF)
        queries = mixed[rows, lane : lane + LANES]
        joined = []
        for head, mask in enumerate(head_masks(1.0 / math.sqrt(HEAD))):
            scores = dot_nt(key_rows, queries * mask)
            top = jnp.max(scores, axis=0, keepdims=True)
            probs = jnp.exp(scores - top)
            total = jnp.sum(probs, axis=0, keepdims=True)
            lse[2 * pair + head, :, rows] = top + jnp.log(total)
            probs = (probs * (1.0 / total)).astype(jnp.bfloat16)
            joined.append(dot_nn(values[head * HEAD : (head + 1) * HEAD], probs))
        joined = jnp.concatenate(joined, axis=0).T
        attended[rows, lane : lane + LANES] = joined.astype(attended.dtype)


def forward_project(size, w, table, h, attended, first, normed):
    out = dot_nt(attended[...], out_rows(size, w))
    for part in range(2):
        rows = slice(part * HALF, (part + 1) * HALF)
        total = h[rows, :].astype(jnp.float32) + (out[rows] + table[1:2, 0:WIDE])
        first[rows, :] = total
        normed[rows, :] = normalize(
            total, table[1:2, WIDE : 2 * WIDE], table[1:2, 2 * WIDE : 3 * WIDE]
        ).astype(normed.dtype)


def forward_up(size, w, table, normed, slope, hidden, piece):
    for j in (2 * piece, 2 * piece + 1):
        columns = slice(j * HALF, (j + 1) * HALF)
        upper = dot_nt(normed[...], up_rows(size, w, j)) + table[2:3, columns]
        value, grad = gelu_pair(upper)
        hidden[:, columns] = value.astype(hidden.dtype)
        slope[:, columns] = grad.astype(slope.dtype)


def forward_down(size, w, table, normed, hidden, second, h, piece):
    columns = slice(piece * HALF, (piece + 1) * HALF)
    count = size.dps // 2
    matrix = jnp.concatenate(
        [
            rows_of(w, size.bs, piece * count, count, j * size.down, size.down)
            for j in range(4)
        ],
        axis=1,
    )
    out = dot_nt(hidden[...], matrix)
    second[:, columns] = normed[:, columns].astype(jnp.float32) + (out + table[3:4, columns])
    if piece == 1:
        for part in range(2):
            rows = slice(part * HALF, (part + 1) * HALF)
            h[rows, :] = normalize(
                second[rows, :], table[3:4, WIDE : 2 * WIDE], table[3:4, 2 * WIDE : 3 * WIDE]
            ).astype(h.dtype)


def backward_norm_two(table, dtable, dy, second, dnormed, dlow, dlow_t):
    dtable[...] = jnp.zeros_like(dtable)
    for part in range(2):
        rows = slice(part * HALF, (part + 1) * HALF)
        grad, gain_sum, shift_sum = normalize_back(
            second[rows, :], dy[rows, :].astype(jnp.float32), table[3:4, WIDE : 2 * WIDE]
        )
        dnormed[rows, :] = grad
        dlow[rows, :] = grad.astype(dlow.dtype)
        dtable[3:4, 0:WIDE] += jnp.sum(grad, axis=0, keepdims=True)
        dtable[3:4, WIDE : 2 * WIDE] += gain_sum
        dtable[3:4, 2 * WIDE : 3 * WIDE] += shift_sum
    dlow_t[...] = dlow[...].T


def backward_down(size, grads, hidden, dlow_t, piece):
    @pl.loop(2 * piece, 2 * piece + 2)
    def _(i):
        start = aligned(i * size.down, 16)
        for half in range(2):
            columns = pl.ds(aligned(i * WIDE, WIDE) + half * HALF, HALF)
            value = dot_nn(dlow_t[...], hidden[:, columns])
            put_rows(grads, size.bs, 0, size.dps, start, size.down, value, 2 * half)


def backward_gelu(size, w, dtable, slope, dlow, dup, piece):
    @pl.loop(2 * piece, 2 * piece + 2)
    def _(i):
        start = aligned(i * size.down, 16)
        for half in range(2):
            columns = pl.ds(aligned(i * WIDE, WIDE) + half * HALF, HALF)
            blocks = (2 * half, 2 * half + 1)
            matrix = rows_of(w, size.bs, 0, size.dps, start, size.down, blocks)
            dupper = dot_nn(dlow[...], matrix) * slope[:, columns].astype(jnp.float32)
            dtable[2:3, columns] = jnp.sum(dupper, axis=0, keepdims=True)
            dup[:, columns] = dupper.astype(dup.dtype)


def backward_up(size, grads, normed, dup):
    count = HALF // size.up

    @pl.loop(0, 4)
    def _(i):
        for half in range(2):
            columns = pl.ds(aligned(i * WIDE, WIDE) + half * HALF, HALF)
            value = dot_tn(dup[:, columns], normed[...])
            first = (2 * i + half) * count
            put_rows(grads, size.bs, first, count, size.out, size.up, value)


def backward_normed(size, w, dnormed, dup):
    for half in range(2):
        columns = slice(half * HALF, (half + 1) * HALF)
        blocks = (2 * half, 2 * half + 1)
        matrix = rows_of(w, size.bs, 0, size.dps, size.out, size.up, blocks)
        dnormed[:, columns] = dnormed[:, columns] + dot_nn(dup[...], matrix)


def backward_norm_one(size, w, table, grads, dtable, first, attended, dnormed, dlow, dlow_t):
    for part in range(2):
        rows = slice(part * HALF, (part + 1) * HALF)
        grad, gain_sum, shift_sum = normalize_back(
            first[rows, :], dnormed[rows, :], table[1:2, WIDE : 2 * WIDE]
        )
        dnormed[rows, :] = grad
        dlow[rows, :] = grad.astype(dlow.dtype)
        dtable[1:2, 0:WIDE] += jnp.sum(grad, axis=0, keepdims=True)
        dtable[1:2, WIDE : 2 * WIDE] += gain_sum
        dtable[1:2, 2 * WIDE : 3 * WIDE] += shift_sum
    dlow_t[...] = dlow[...].T
    for block in (0, 2):
        columns = slice(block * LANES, (block + 2) * LANES)
        value = dot_nn(dlow_t[...], attended[:, columns])
        put_rows(grads, size.bs, 0, size.dps, 0, size.out, value, block)
    dlow[...] = dot_nn(dlow[...], out_rows(size, w)).astype(dlow.dtype)


def backward_attend(mixed, lse, dtable, dlow, dmixed, pair):
    scale = 1.0 / math.sqrt(HEAD)
    lane = pair * LANES
    columns = slice(lane, lane + LANES)
    key_columns = slice(WIDE + lane, WIDE + lane + LANES)
    value_columns = slice(2 * WIDE + lane, 2 * WIDE + lane + LANES)
    key_rows = mixed[:, key_columns]
    keys_t = key_rows.T
    values = mixed[:, value_columns]
    dkeys = jnp.zeros((WIDE, LANES), jnp.float32)
    dvalues = jnp.zeros((WIDE, LANES), jnp.float32)
    for part in range(2):
        rows = slice(part * HALF, (part + 1) * HALF)
        queries = mixed[rows, columns]
        grad_out = dlow[rows, columns]
        dqueries = []
        for head in range(2):
            query = queries * head_masks(scale)[head]
            grad = grad_out * head_masks(1.0)[head]
            probs = jnp.exp(dot_nt(key_rows, query) - lse[2 * pair + head, :, rows])
            dprobs = dot_nt(values, grad)
            delta = jnp.sum(probs * dprobs, axis=0, keepdims=True)
            dscores = (probs * (dprobs - delta)).astype(jnp.bfloat16)
            dvalues = dvalues + dot_nn(probs.astype(jnp.bfloat16), grad)
            dkeys = dkeys + dot_nn(dscores, query)
            dqueries.append(dot_nn(keys_t[head * HEAD : (head + 1) * HEAD], dscores))
        dquery = jnp.concatenate(dqueries, axis=0).T * scale
        dtable[0:1, columns] += jnp.sum(dquery, axis=0, keepdims=True)
        dmixed[rows, columns] = dquery.astype(dmixed.dtype)
    dmixed[:, key_columns] = dkeys.astype(dmixed.dtype)
    dmixed[:, value_columns] = dvalues.astype(dmixed.dtype)
    dtable[0:1, value_columns] = jnp.sum(dvalues, axis=0, keepdims=True)


def backward_mix(size, grads, h, dmixed, piece):
    count = QKV_TILE // size.qkv
    grad = dmixed[:, piece * QKV_TILE : (piece + 1) * QKV_TILE]
    put_rows(grads, size.bs, piece * count, count, 0, size.qkv, dot_tn(grad, h[...]))


def backward_input(size, w, dnormed, dmixed, dy):
    for half in range(2):
        columns = slice(half * HALF, (half + 1) * HALF)
        blocks = (2 * half, 2 * half + 1)
        matrix = rows_of(w, size.bs, 0, size.dps, 0, size.qkv, blocks)
        dy[:, columns] = (dnormed[:, columns] + dot_nn(dmixed[...], matrix)).astype(dy.dtype)


WINDOW = 384


def group_rows(group):
    rows = lax.broadcasted_iota(jnp.int32, (16, LANES), 0)
    return jnp.where(rows == group, 1.0, 0.0).astype(jnp.bfloat16)


def pack_mix(piece, qkv, gains, biases):
    low = piece.dtype
    rows = qkv.shape[0]
    flat = jnp.concatenate([gains[...], biases[...]], axis=1)
    flat = jnp.concatenate([flat, jnp.zeros((1, 2 * WIDE - flat.shape[1]), flat.dtype)], axis=1)
    row_id = lax.broadcasted_iota(jnp.int32, (VEC_ROWS, LANES), 0)
    for lb in range(SECT):
        lane = lb * LANES
        piece[lb, :rows] = qkv[:, lane : lane + LANES].astype(low)
        tile = jnp.where(row_id == 0, flat[:, lane : lane + LANES], 0.0)
        lane += WIDE
        tile = jnp.where(row_id == 1, flat[:, lane : lane + LANES], tile)
        piece[lb, rows:] = tile.astype(low)


def pack_up(piece, out, up):
    rows = out.shape[0]
    for lb in range(SECT):
        lanes = slice(lb * LANES, (lb + 1) * LANES)
        piece[lb, :rows] = out[:, lanes].astype(piece.dtype)
        piece[lb, rows:] = up[:, lanes].astype(piece.dtype)


def pack_down(piece, down):
    rows = down.shape[0]
    for lb in range(SECT):
        for j in range(4):
            start = j * WIDE + lb * LANES
            piece[lb, j * rows : (j + 1) * rows] = down[:, start : start + LANES].astype(piece.dtype)


def pack_embedding(piece, weight, shift, rows):
    n = weight.shape[1]
    rows[...] = jnp.zeros_like(rows)
    rows[:GROUPS, :n] = shift[...]
    rows[512 - L3 : 512, :n] = weight[L1 + L2 :]
    rows[768 - L2 : 768, :n] = weight[L1 : L1 + L2]
    rows[1024 - L1 :, :n] = weight[:L1]
    columns = rows[...].T[:n].astype(piece.dtype)
    for lb in range(SECT):
        for part in range(2):
            start = part * WIDE + lb * LANES
            piece[lb, part * n : (part + 1) * n] = columns[:, start : start + LANES]


def expand(series, group, x):
    empty = jnp.zeros((WINDOW - series.shape[0], series.shape[1]), series.dtype)
    x[:, :WINDOW] = jnp.concatenate([empty, series[...]], axis=0).T
    lane = lax.broadcasted_iota(jnp.int32, (x.shape[0], LANES), 1)
    x[:, WINDOW:] = jnp.where(lane == group, 1.0, 0.0).astype(x.dtype)


def embed(size, emb, pick, x, wsel, h):
    rows = WIDE // size.dps
    first = rows_of(emb, size.bs, 0, size.dps, 0, rows)
    second = rows_of(emb, size.bs, 0, size.dps, rows, rows)
    long, middle, short = (pick[g : g + 1, :] for g in (2, 1, 0))
    wide = jnp.concatenate(
        [
            first[:, LANES : 2 * LANES] * long,
            first[:, 2 * LANES : 3 * LANES] * long + second[:, :LANES] * middle,
            first[:, 3 * LANES :] * long
            + second[:, LANES : 2 * LANES] * middle
            + second[:, 3 * LANES :] * short,
        ],
        axis=1,
    )
    wsel[...] = wide.T
    matrix = jnp.concatenate([wide, first[:, :LANES]], axis=1)
    h[...] = dot_nt(x[...], matrix).astype(h.dtype)


def embed_back(size, pick, x, wsel, dh, grads, series_grad):
    history = series_grad.shape[0]
    series_grad[...] = dot_nt(wsel[...], dh[...])[WINDOW - history :]
    sums = dot_tn(dh[...], x[...])
    long, middle, short = (pick[g : g + 1, :].astype(jnp.float32) for g in (2, 1, 0))
    parts = [sums[:, i * LANES : (i + 1) * LANES] for i in range(4)]
    parts = [
        parts[3],
        parts[0] * long,
        parts[1] * long,
        parts[2] * long,
        parts[1] * middle,
        parts[2] * middle,
        jnp.zeros_like(parts[0]),
        parts[2] * short,
    ]
    rows = WIDE // (SECT * size.dps)
    for pipe in range(SECT):
        block = (pipe % 2) * 2 + pipe // 2
        for dp in range(size.dps):
            start = (pipe * size.dps + dp) * rows
            piece = jnp.concatenate([part[start : start + rows] for part in parts], axis=0)
            grads[block, dp // size.bs, dp % size.bs] = piece.astype(grads.dtype)


def saved_shapes():
    low, wide = jnp.bfloat16, jnp.float32
    return [
        ((WIDE, WIDE), low),
        ((WIDE, 3 * WIDE), low),
        ((2 * SECT, 1, WIDE), wide),
        ((WIDE, WIDE), low),
        ((WIDE, WIDE), wide),
        ((WIDE, WIDE), low),
        ((WIDE, 4 * WIDE), low),
        ((WIDE, 4 * WIDE), low),
        ((WIDE, WIDE), wide),
        ((SECT, 4 * WIDE), wide),
    ]


def chunk_shape(size, rows):
    return (SECT, ZS, size.bs, rows, LANES)


WIDE_KINDS = (0, 2)
HALVES = (2, 2, 1, 2)


def follow(plan, section, act, compute, wide):
    seen = {}
    for step in plan:
        if len(step) == 1:
            piece = seen.get(step[0], 0)
            seen[step[0]] = piece + 1
            compute(step[0], piece)
            continue
        op, kind, offset = step[:3]
        if len(step) == 4:
            if isinstance(section, int):
                act(op, kind, wide[1])
                continue

            @pl.when(section == offset)
            def _():
                act(op, kind, wide[1])

            continue
        where = section + offset
        first, last = (0, SECT - 1) if kind not in wide[0] else wide[2]
        if isinstance(where, int):
            if first <= where <= last:
                act(op, kind, where)
            continue
        inside = None
        if offset > 0 or last < SECT - 1:
            inside = where <= last
        elif offset < 0 or first > 0:
            inside = where >= first
        if inside is None:
            act(op, kind, where)
            continue

        @pl.when(inside)
        def _():
            act(op, kind, where)


def forward_kernel(dps, groups, *refs):
    size = Sizes(dps)
    given, refs = refs[:9], refs[9:]
    out, wholes, wsel, x, refs = refs[0], refs[1:5], refs[5], refs[6], refs[7:]
    kept, local, refs = refs[:10], refs[10:20], refs[20:]
    buffers, refs = refs[:4], refs[4:]
    pieces, held, refs = refs[:4], refs[4:13], refs[13:]
    emb_rows, pick, refs = refs[0], refs[1], refs[2:]
    given_sem, w_sem, kept_sem, own_sem, p_send, p_recv, send, recv = refs
    h, mixed, lse, attended, first, normed, slope, hidden, second, table = local
    w_att, w_up, w_down, w_emb = buffers
    at = Place(dps)

    own = [
        pltpu.make_async_copy(
            pieces[kind].at[at.block],
            wholes[kind].at[at.pipe, at.block, at.z, at.b]
            if kind < EMB
            else wholes[kind].at[at.block, at.z, at.b],
            own_sem.at[kind],
        )
        for kind in range(4)
    ]
    def split(kind, back):
        copies = []
        for k in range(1, SECT):
            if back:
                region = wholes[kind].at[at.pipe_at(SECT - k), at.block, at.z, at.b]
                src = region
            else:
                block = at.block_of(at.pipe_at(k))
                region = wholes[kind].at[at.pipe, block, at.z, at.b]
                src = pieces[kind].at[block]
            sems = p_send.at[kind, k - 1], p_recv.at[kind, k - 1]
            copies.append(remote(src, region, *sems, (at.pipe_at(k), at.dp)))
        return copies

    def chunk(kind, section):
        if kind == EMB:
            return Spread(at, wholes[kind], send.at[3 * SECT], recv.at[3 * SECT])
        number = 3 * section + kind
        sort = Spread
        if isinstance(section, int) and section == SECT - 1 and kind in WIDE_KINDS:
            sort = SpreadWide
        return sort(at, wholes[kind].at[section], send.at[number], recv.at[number], HALVES[kind])

    def load(kind, section, core):
        blocks = pl.ds(core * 2, 2)
        src, dst = wholes[kind], buffers[kind]
        if kind != EMB:
            src, dst = src.at[section], dst.at[section % 2]
        sem = w_sem.at[kind, section % 2, core]
        return pltpu.make_async_copy(src.at[blocks], dst.at[blocks], sem)

    def loaded(kind, section):
        load(kind, section, at.c).wait()
        load(kind, section, 1 - at.c).wait()

    arrived = []

    def act(op, kind, section):
        if op == 0:
            if kind not in arrived:
                arrived.append(kind)
                own[kind].wait()
                if kind == EMB:
                    chunk(kind, section).start(0)
                    return
                for copy in split(kind, True):
                    copy.wait_recv()
                for copy in split(kind, False):
                    copy.wait_send()
            chunk(kind, section).start(0)
        elif op < 4:
            chunk(kind, section).move(op - 1)
            if op == 3:
                load(kind, section, at.c).start()
        else:
            chunk(kind, section).land(3)
            load(kind, section, 1 - at.c).start()

    def saves(section, early):
        which = (1, 2, 3, 4, 5, 9) if early else (6, 7, 8)
        return [
            pltpu.make_async_copy(local[i], kept[i].at[section], kept_sem.at[i]) for i in which
        ]

    series, embed_weight, embed_bias, qkv, out_w, up_w, down_w, gains, biases = held
    gets = copies_of(zip(given, held), given_sem)
    for i in (3, 7, 8, 1, 2, 4, 5, 6, 0):
        gets[i].start()
    pick[...] = group_rows(groups[0])
    copies_wait([gets[i] for i in (3, 7, 8)])
    pack_mix(pieces[0], qkv, gains, biases)
    copies_wait(gets[1:3])
    pack_embedding(pieces[EMB], embed_weight, embed_bias, emb_rows)
    own[0].start()
    own[EMB].start()
    at.greet()
    copies_start(split(0, False))
    copies_wait(gets[4:7])
    pack_up(pieces[1], out_w, up_w)
    own[1].start()
    copies_start(split(1, False))
    pack_down(pieces[2], down_w)
    own[2].start()
    copies_start(split(2, False))
    table[...] = jnp.zeros_like(table)
    gets[0].wait()
    expand(series, groups[0], x)

    def before(name, piece):
        loaded(EMB, 0)
        embed(size, w_emb, pick, x, wsel, h)

    wide = (WIDE_KINDS, SECT - 1, (0, SECT - 2))
    follow(FORWARD_START, 0, act, before, wide)

    @pl.loop(0, SECT)
    def _(section):
        att, up, down = (ref.at[section % 2] for ref in (w_att, w_up, w_down))
        keep_h = pltpu.make_async_copy(h, kept[0].at[section], kept_sem.at[0])

        def compute(name, piece):
            if name == "mix":
                if piece == 0:

                    @pl.when(section > 0)
                    def _():
                        copies_wait(saves(section - 1, True))

                    keep_h.start()
                    loaded(0, section)
                    read_vectors(att, table, size.bs, size.qkv)
                forward_mix(size, att, table, h, mixed, piece)
            elif name == "attend":
                forward_attend(mixed, lse, attended, piece)
            elif name == "project":
                loaded(1, section)
                forward_project(size, up, table, h, attended, first, normed)
                copies_start(saves(section, True))
            elif name == "up":
                if piece == 0:

                    @pl.when(section > 0)
                    def _():
                        copies_wait(saves(section - 1, False))

                forward_up(size, up, table, normed, slope, hidden, piece)
            else:
                if piece == 0:
                    loaded(2, section)
                    keep_h.wait()
                forward_down(size, down, table, normed, hidden, second, h, piece)
                if piece == 1:
                    copies_start(saves(section, False))

        follow(FORWARD_PERIOD, section, act, compute, wide)

    copies_wait(saves(SECT - 1, True))
    copies_wait(saves(SECT - 1, False))
    out[...] = h[...]


def copies_of(pairs, sems):
    return [pltpu.make_async_copy(src, dst, sems.at[i]) for i, (src, dst) in enumerate(pairs)]


def forward_all(groups, given, dps):
    size = Sizes(dps)
    low, wide = jnp.bfloat16, jnp.float32
    shapes = saved_shapes()
    rows = (size.att, size.dense, size.wide, 2 * WIDE // dps)
    chunks = [chunk_shape(size, count) for count in rows]
    anywhere = pl.BlockSpec(memory_space=pl.ANY)
    inside = pl.BlockSpec(memory_space=pltpu.VMEM)
    outs = [((WIDE, WIDE), low)]
    outs += [((SECT,) + shape, low) for shape in chunks[:3]] + [(chunks[3], low)]
    outs += [((WINDOW, WIDE), low), ((WIDE, WIDE), low)]
    outs += [((SECT,) + shape, dtype) for shape, dtype in shapes]
    scratch = shapes + [((2,) + shape, low) for shape in chunks[:3]] + [(chunks[3], low)]
    scratch += [((SECT, count, LANES), low) for count in rows]
    scratch += [(array.shape, array.dtype) for array in given]
    scratch += [((2 * WIDE, LANES), wide), ((16, LANES), low)]
    slots = max(Spread.slots(size.bs), SpreadWide.slots(size.bs))
    dma = pltpu.SemaphoreType.DMA
    return pl.pallas_call(
        partial(forward_kernel, dps),
        out_shape=[jax.ShapeDtypeStruct(shape, dtype) for shape, dtype in outs],
        in_specs=[pl.BlockSpec(memory_space=pltpu.SMEM)] + [anywhere] * len(given),
        out_specs=[inside] + [anywhere] * 4 + [inside] * 2 + [anywhere] * len(shapes),
        scratch_shapes=[pltpu.VMEM(shape, dtype) for shape, dtype in scratch]
        + [
            dma((len(given),)),
            dma((4, 2, 2)),
            dma((len(shapes),)),
            dma((4,)),
            dma((3, SECT - 1)),
            dma((3, SECT - 1)),
            dma((1 + 3 * SECT, slots)),
            dma((1 + 3 * SECT, slots)),
        ],
        compiler_params=pltpu.CompilerParams(
            collective_id=0, has_side_effects=True, vmem_limit_bytes=56 * 1024 * 1024
        ),
        name="gather_forward",
    )(groups, *given)


def backward_kernel(dps, groups, att, up, down, cotangent, x_in, wsel_in, *refs):
    size = Sizes(dps)
    kept, refs = refs[:10], refs[10:]
    series_grad, outs, refs = refs[0], refs[1:5], refs[5:]
    local, refs = refs[:9], refs[9:]
    tables, w_att, w_up, w_down, dtable, dy, dnormed, dlow, dlow_t, dmixed, dup = refs[:11]
    x, wsel, pick, refs = *refs[11:14], refs[14:]
    kinds = []
    for _ in range(4):
        kinds.append(refs[:4] + (refs[4:9],))
        refs = refs[9:]
    wides = {}
    for kind in WIDE_KINDS:
        wides[kind] = refs[:2]
        refs = refs[2:]
    w_sem, kept_sem, table_sem, late_sem, out_sem, p_send, p_recv, send, recv, credit = refs
    h, mixed, lse, attended, first, normed, slope, hidden, second = local
    at = Place(dps)
    last = SECT - 1

    def weights(kind, section):
        src, dst = ((att, w_att), (up, w_up), (down, w_down))[kind]
        return pltpu.make_async_copy(src.at[section], dst, w_sem.at[kind])

    def loads(section, dense):
        which = (5, 6, 7, 8) if dense else (0, 1, 2, 3, 4)
        found = [
            pltpu.make_async_copy(kept[i].at[section], local[i], kept_sem.at[i]) for i in which
        ]
        return found + [weights(kind, section) for kind in ((1, 2) if dense else (0,))]

    def chunk(kind, i):
        grads, totals, finals, landing, bufs = kinds[kind]
        sort, row = Fold, kind
        if isinstance(i, int) and i == 0 and kind in WIDE_KINDS:
            sort, bufs, row = FoldWide, wides[kind], 4 + WIDE_KINDS.index(kind)
        refs = (grads, totals.at[i % 2], landing, bufs, finals.at[i])
        return sort(at, *refs, send.at[row], recv.at[row], credit.at[kind], HALVES[kind])

    def hand_over(kind, i):
        landing = outs[kind].at[at.block]
        final = kinds[kind][2].at[i]
        return (
            pltpu.make_async_copy(final, landing, out_sem.at[kind]),
            remote(final, landing, p_send.at[kind, i], p_recv.at[kind, at.pipe], (last - i, at.dp)),
        )

    def act(op, kind, i):
        first = 1 if kind in WIDE_KINDS else 0
        alone = kind == EMB or (isinstance(i, int) and i < first)
        again = False if alone else i > first
        more = False if alone else i < last
        if op == 0:
            chunk(kind, i).start(0, False if kind == EMB else i > 0)
        elif op == 1:
            chunk(kind, i).move(0, again, False if kind == EMB else i < last)
        elif op < 4:
            chunk(kind, i).move(op - 1, again, more)
        else:
            chunk(kind, i).land(3, more)
            if kind == EMB:
                outs[kind][...] = kinds[kind][2][0]
            else:
                here, away = hand_over(kind, i)

                @pl.when(at.pipe == last - i)
                def _():
                    here.start()

                @pl.when(at.pipe != last - i)
                def _():
                    away.start()

    copies_start(loads(last, True))
    get_tables = pltpu.make_async_copy(kept[9], tables, table_sem)
    get_tables.start()
    copies_start(loads(last, False))
    late = copies_of(((cotangent, dy), (x_in, x), (wsel_in, wsel)), late_sem)
    copies_start(late)
    pick[...] = group_rows(groups[0])
    at.greet()
    get_tables.wait()
    late[0].wait()

    wide = (WIDE_KINDS, 0, (1, last))

    @pl.loop(0, SECT)
    def _(i):
        section = last - i
        table = tables.at[section]

        def compute(name, piece):
            if name == "norm2":
                copies_wait(loads(section, True))
                backward_norm_two(table, dtable, dy, second, dnormed, dlow, dlow_t)
            elif name == "down":
                backward_down(size, kinds[2][0], hidden, dlow_t, piece)
            elif name == "gelu":
                backward_gelu(size, w_down, dtable, slope, dlow, dup, piece)
            elif name == "up":
                backward_up(size, kinds[1][0], normed, dup)
            elif name == "normed":
                backward_normed(size, w_up, dnormed, dup)
            elif name == "norm1":
                copies_wait(loads(section, False))
                backward_norm_one(
                    size, w_up, table, kinds[1][0], dtable, first, attended, dnormed, dlow, dlow_t
                )

                @pl.when(section > 0)
                def _():
                    copies_start(loads(section - 1, True))

            elif name == "attend":
                backward_attend(mixed, lse, dtable, dlow, dmixed, piece)
            elif name == "mix":
                backward_mix(size, kinds[0][0], h, dmixed, piece)
                if piece == 1:
                    write_vectors(kinds[0][0], dtable, size.bs, size.qkv)
            else:
                backward_input(size, w_att, dnormed, dmixed, dy)

                @pl.when(section > 0)
                def _():
                    copies_start(loads(section - 1, False))

        follow(BACKWARD_PERIOD, i, act, compute, wide)

    def after(name, piece):
        copies_wait(late[1:])
        embed_back(size, pick, x, wsel, dy, kinds[EMB][0], series_grad)

    follow(BACKWARD_END, 0, act, after, wide)

    for kind in range(3):
        for i in range(SECT):
            here, away = hand_over(kind, i)

            @pl.when(at.pipe == last - i)
            def _():
                here.wait()

            @pl.when(at.pipe != last - i)
            def _():
                away.wait_send()

        for k in range(1, SECT):
            other = at.pipe_at(k)
            landing = outs[kind].at[at.block_of(other)]
            sems = p_send.at[kind, 0], p_recv.at[kind, other]
            remote(landing, landing, *sems, (other, at.dp)).wait_recv()


def backward_all(groups, weights, cotangent, x, wsel, kept, history, dps):
    size = Sizes(dps)
    low, wide = jnp.bfloat16, jnp.float32
    anywhere = pl.BlockSpec(memory_space=pl.ANY)
    inside = pl.BlockSpec(memory_space=pltpu.VMEM)
    shapes = saved_shapes()
    rows_emb = 8 * WIDE // (SECT * dps)
    kind_rows = (size.att, size.dense, size.wide, rows_emb)
    scratch = shapes[:9] + [((SECT,) + shapes[9][0], wide)]
    scratch += [(chunk_shape(size, rows), low) for rows in kind_rows[:3]]
    scratch += [
        (shapes[9][0], wide),
        ((WIDE, WIDE), low),
        ((WIDE, WIDE), wide),
        ((WIDE, WIDE), low),
        ((WIDE, WIDE), low),
        ((WIDE, 3 * WIDE), low),
        ((WIDE, 4 * WIDE), low),
        ((WIDE, WIDE), low),
        ((WINDOW, WIDE), low),
        ((16, LANES), low),
    ]
    for kind, rows in enumerate(kind_rows):
        sets, results = (1, 1) if kind == EMB else (2, SECT)
        scratch += [
            (chunk_shape(size, rows), low),
            ((sets, 2, ZS, size.bs, rows, LANES), low),
            ((results, rows, LANES), low),
            ((2, ZS, size.bs, rows, LANES), low),
        ]
        scratch += [(shape, low) for shape in Fold.buffers(size.bs, rows, HALVES[kind])]
    for kind in WIDE_KINDS:
        scratch += [(shape, low) for shape in FoldWide.buffers(size.bs, kind_rows[kind])]
    slots = max(Fold.slots(size.bs), FoldWide.slots(size.bs))
    dma = pltpu.SemaphoreType.DMA
    return pl.pallas_call(
        partial(backward_kernel, dps),
        out_shape=[jax.ShapeDtypeStruct((history, WIDE), wide)]
        + [jax.ShapeDtypeStruct((SECT, rows, LANES), low) for rows in kind_rows[:3]]
        + [jax.ShapeDtypeStruct((rows_emb, LANES), low)],
        in_specs=[pl.BlockSpec(memory_space=pltpu.SMEM)] + [anywhere] * (6 + len(kept)),
        out_specs=[inside] + [anywhere] * 3 + [inside],
        scratch_shapes=[pltpu.VMEM(shape, dtype) for shape, dtype in scratch]
        + [
            dma((3,)),
            dma((9,)),
            dma(()),
            dma((3,)),
            dma((3,)),
            dma((3, SECT)),
            dma((3, SECT)),
            dma((4 + len(WIDE_KINDS), slots)),
            dma((4 + len(WIDE_KINDS), slots)),
            pltpu.SemaphoreType.REGULAR((4, slots)),
        ],
        compiler_params=pltpu.CompilerParams(
            collective_id=1, has_side_effects=True, vmem_limit_bytes=60 * 1024 * 1024
        ),
        name="backward_fold",
    )(groups, *weights, cotangent, x, wsel, *kept)


def finish_kernel(dps, n_gains, n_biases, att, up, down, emb, block_in, series_in, *refs):
    size = Sizes(dps)
    block_out, series_out, embed_w, embed_b, qkv, out, up_out, down_out, gains, biases, sems = refs
    copies = copies_of(((block_in, block_out), (series_in, series_out)), sems)
    copies_start(copies)
    for lb in range(SECT):
        lanes = slice(lb * LANES, (lb + 1) * LANES)
        qkv[:, lanes] = att[lb, : size.qkv].astype(jnp.float32)
        out[:, lanes] = up[lb, : size.out].astype(jnp.float32)
        up_out[:, lanes] = up[lb, size.out :].astype(jnp.float32)
        for j in range(4):
            rows = slice(j * size.down, (j + 1) * size.down)
            start = j * WIDE + lb * LANES
            down_out[:, start : start + LANES] = down[lb, rows].astype(jnp.float32)
    tiles = [att[lb, size.qkv :].astype(jnp.float32) for lb in range(SECT)]
    flat = jnp.concatenate([tile[row : row + 1] for row in range(2) for tile in tiles], axis=1)
    gains[...] = flat[:, :n_gains]
    biases[...] = flat[:, n_gains : n_gains + n_biases]
    rows = emb.shape[0] // 8
    packed = emb[...].astype(jnp.float32)
    packed = jnp.concatenate([packed[i * rows : (i + 1) * rows] for i in range(8)], axis=1)
    packed = jnp.concatenate([packed, jnp.zeros((LANES - rows, 8 * LANES), jnp.float32)], axis=0)
    columns = packed.T
    embed_w[:L1] = columns[1024 - L1 :, :rows]
    embed_w[L1 : L1 + L2] = columns[768 - L2 : 768, :rows]
    embed_w[L1 + L2 :] = columns[512 - L3 : 512, :rows]
    embed_b[...] = columns[:GROUPS, :rows]
    copies_wait(copies)


def finish_all(sums, block, series, n_gains, n_biases, dps):
    size = Sizes(dps)
    wide = jnp.float32
    columns = WIDE // (SECT * dps)
    outs = [
        (block.shape, block.dtype),
        (series.shape, wide),
        ((L1 + L2 + L3, columns), wide),
        ((GROUPS, columns), wide),
        ((size.qkv, WIDE), wide),
        ((size.out, WIDE), wide),
        ((size.up, WIDE), wide),
        ((size.down, 4 * WIDE), wide),
        ((1, n_gains), wide),
        ((1, n_biases), wide),
    ]
    anywhere = pl.BlockSpec(memory_space=pl.ANY)
    inside = pl.BlockSpec(memory_space=pltpu.VMEM)
    return pl.pallas_call(
        partial(finish_kernel, dps, n_gains, n_biases),
        out_shape=[jax.ShapeDtypeStruct(shape, dtype) for shape, dtype in outs],
        in_specs=[inside] * 4 + [anywhere] * 2,
        out_specs=[anywhere] * 2 + [inside] * 8,
        scratch_shapes=[pltpu.SemaphoreType.DMA((2,))],
        compiler_params=pltpu.CompilerParams(vmem_limit_bytes=32 * 1024 * 1024),
        name="finish",
    )(*sums, block, series)


def per_device(
    series,
    groups,
    cotangent,
    embed_weight,
    embed_bias,
    qkv_weight,
    out_weight,
    up_weight,
    down_weight,
    gains,
    biases,
):
    dps = lax.axis_size("dp")
    given = (
        series[0],
        embed_weight,
        embed_bias,
        qkv_weight[0],
        out_weight[0],
        up_weight[0],
        down_weight[0],
        gains,
        biases,
    )
    block_output, att, up, down, _, wsel, x, *kept = forward_all(groups, given, dps)
    series_grad, *sums = backward_all(
        groups, (att, up, down), cotangent[0], x, wsel, kept, series.shape[1], dps
    )
    outs = finish_all(sums, block_output, series_grad, gains.shape[1], biases.shape[1], dps)
    block_output, series_grad, embed_w, embed_b, qkv, out, up, down, gain_sum, bias_sum = outs
    return (
        block_output[None],
        series_grad[None],
        embed_w,
        embed_b,
        qkv[None],
        out[None],
        up[None],
        down[None],
        gain_sum,
        bias_sum,
    )


def solution(mesh):
    return jax.shard_map(
        per_device,
        mesh=mesh,
        in_specs=(
            P(("pipe", "dp"), None, None),
            P(("pipe", "dp")),
            P(("pipe", "dp"), None, None),
            P(None, "dp"),
            P(None, "dp"),
            P("pipe", "dp", None),
            P("pipe", "dp", None),
            P("pipe", "dp", None),
            P("pipe", "dp", None),
            P("pipe", "dp"),
            P("pipe", "dp"),
        ),
        out_specs=(
            P(("pipe", "dp"), None, None),
            P(("pipe", "dp"), None, None),
            P(None, ("pipe", "dp")),
            P(None, ("pipe", "dp")),
            P("pipe", "dp", None),
            P("pipe", "dp", None),
            P("pipe", "dp", None),
            P("pipe", "dp", None),
            P("pipe", "dp"),
            P("pipe", "dp"),
        ),
        check_vma=False,
    )
```

```python
from functools import partial
import math

import jax
import jax.numpy as jnp
from jax import lax
from jax.experimental import pallas as pl
from jax.experimental.pallas import tpu as pltpu
from jax.sharding import PartitionSpec as P

HEAD = 64
L1 = 96
L2 = 192
L3 = 336
GROUPS = 3


NORM_EPS = 1e-05


MESH = pl.DeviceIdType.MESH
LANES = 128
ZS = 4
SECT = 4
EMB = 3


class Place:
    def __init__(self, dps):
        self.bs = dps // ZS
        pipe = lax.axis_index("pipe")
        dp = lax.axis_index("dp")
        self.pipe, self.dp = pipe, dp
        self.x, self.c = pipe // 2, pipe % 2
        self.z, self.b = dp // self.bs, dp % self.bs
        self.block = self.c * 2 + self.x
        self.x_peer = ((1 - self.x) * 2 + self.c, dp)
        self.core_peer = (self.x * 2 + 1 - self.c, dp)

    def block_of(self, pipe):
        return (pipe % 2) * 2 + pipe // 2

    def pipe_at(self, step):
        return (self.pipe + step) % SECT

    def z_at(self, step):
        return (self.z + step) % ZS

    def b_at(self, step):
        return (self.b + step) % self.bs

    def z_peer(self, step):
        return (self.pipe, self.z_at(step) * self.bs + self.b)

    def b_peer(self, step):
        return (self.pipe, self.z * self.bs + self.b_at(step))

    def greet(self):
        barrier = pltpu.get_barrier_semaphore()
        peers = [(self.pipe_at(k), self.dp) for k in range(1, SECT)]
        peers += [self.z_peer(k) for k in range(1, ZS)]
        peers += [self.b_peer(k) for k in range(1, self.bs)]
        for peer in peers:
            pl.semaphore_signal(barrier, inc=1, device_id=peer, device_id_type=MESH)

    def met(self):
        pl.semaphore_wait(pltpu.get_barrier_semaphore(), SECT + ZS + self.bs - 3)


def remote(src, dst, send, recv, peer):
    return pltpu.make_async_remote_copy(
        src_ref=src, dst_ref=dst, send_sem=send, recv_sem=recv, device_id=peer, device_id_type=MESH
    )


FORWARD_START = (
    (0, 3, 0),
    (0, 0, 0),
    (0, 2, 0),
    (1, 3, 0),
    (1, 0, 0),
    (0, 1, 0),
    (2, 3, 0),
    (2, 0, 0),
    (0, 0, 1),
    (1, 1, 0),
    (1, 2, 0),
    (3, 3, 0),
    (0, 2, 1),
    (1, 0, 1),
    (2, 1, 0),
    (4, 3, 0),
    (3, 0, 0),
    ("embed",),
    (4, 0, 0),
)
FORWARD_PERIOD = (
    ("mix",),
    (0, 1, 1),
    (2, 0, 1),
    ("mix",),
    ("attend",),
    (3, 1, 0),
    ("attend",),
    (2, 2, 0),
    ("attend",),
    (0, 0, 2),
    (4, 1, 0),
    ("attend",),
    ("project",),
    (1, 1, 1),
    ("up",),
    (1, 2, 1),
    (0, 2, 2),
    (3, 2, 0),
    ("up",),
    (1, 0, 2),
    ("up",),
    (2, 1, 1),
    (3, 0, 1),
    (4, 2, 0),
    ("up",),
    ("down",),
    (4, 0, 1),
    ("down",),
)
BACKWARD_PERIOD = (
    (0, 0, -1),
    ("norm2",),
    (2, 1, -1),
    ("down",),
    ("down",),
    (1, 0, -1),
    (0, 2, 0),
    ("gelu",),
    ("gelu",),
    ("up",),
    (3, 1, -1),
    (1, 2, 0),
    (4, 0, -2),
    ("normed",),
    (2, 0, -1),
    ("norm1",),
    (0, 1, 0),
    ("attend",),
    ("attend",),
    (3, 0, -1),
    (3, 2, -1),
    (1, 1, 0),
    ("attend",),
    ("attend",),
    (2, 2, 0),
    ("mix",),
    ("mix",),
    ("input",),
    (4, 2, -1),
    (4, 1, -1),
)
BACKWARD_END = (
    (0, 0, 3),
    (2, 1, 3),
    (1, 0, 3),
    (3, 1, 3),
    ("embed",),
    (4, 0, 2),
    (0, 3, 0),
    (2, 0, 3),
    (1, 3, 0),
    (3, 0, 3),
    (2, 3, 0),
    (3, 2, 3),
    (4, 2, 3),
    (4, 1, 3),
    (4, 0, 3),
    (3, 3, 0),
    (4, 3, 0),
)


def copies_start(copies):
    for copy in copies:
        copy.start()


def copies_wait(copies):
    for copy in copies:
        copy.wait()


class Spread:
    def __init__(self, at, out, send, recv, half=ZS // 2):
        self.at, self.out, self.send, self.recv = at, out, send, recv
        nb = at.bs - 1
        self.slot_z = 0
        self.slot_b1 = ZS - 1
        self.slot_x1 = self.slot_b1 + nb
        self.slot_x2 = self.slot_x1 + 1
        self.slot_b2 = self.slot_x2 + 1
        self.slot_c = self.slot_b2 + nb
        self.half = half

    @staticmethod
    def slots(bs):
        return ZS - 1 + 2 * (bs - 1) + 3

    def copy(self, region, slot, peer):
        return remote(region, region, self.send.at[slot], self.recv.at[slot], peer)

    def copies(self, stage, back):
        at, out, half = self.at, self.out, self.half
        rest = pl.ds(half, ZS - half)
        x_block = at.c * 2 + 1 - at.x if back else at.block
        if stage == 0:
            return [
                self.copy(
                    out.at[at.block, at.z_at(ZS - k) if back else at.z, at.b],
                    self.slot_z + k - 1,
                    at.z_peer(k),
                )
                for k in range(1, ZS)
            ]
        if stage == 3:
            core = 1 - at.c if back else at.c
            return [self.copy(out.at[pl.ds(core * 2, 2)], self.slot_c, at.core_peer)]
        copies = []
        for k in range(1, at.bs):
            b = at.b_at(at.bs - k) if back else at.b
            if stage == 1:
                region, slot = out.at[at.block, pl.ds(0, half), b], self.slot_b1
            else:
                region, slot = out.at[pl.ds(at.c * 2, 2), rest, b], self.slot_b2
            copies.append(self.copy(region, slot + k - 1, at.b_peer(k)))
        if stage == 1:
            region, slot = out.at[x_block, rest, at.b], self.slot_x1
        else:
            region, slot = out.at[x_block, pl.ds(0, half)], self.slot_x2
        copies.append(self.copy(region, slot, at.x_peer))
        return copies

    def start(self, stage):
        copies_start(self.copies(stage, False))

    def land(self, stage):
        for copy in self.copies(stage, True):
            copy.wait_recv()
        for copy in self.copies(stage, False):
            copy.wait_send()

    def move(self, stage):
        self.land(stage)
        self.start(stage + 1)


class SpreadCross(Spread):
    @staticmethod
    def slots(bs):
        return 2 * bs + 2 * ZS - 1

    def copies(self, stage, back):
        at, out = self.at, self.out
        rows = out.shape[-2]
        cut = rows // 32 * 16
        some, rest = pl.ds(0, cut), pl.ds(cut, rows - cut)
        core = 1 - at.c if back else at.c
        if stage == 3:
            return [self.copy(out.at[pl.ds(core * 2, 2)], 2 * at.bs + 2 * ZS - 2, at.core_peer)]
        both = pl.ds(at.c * 2, 2)
        x_block = at.c * 2 + 1 - at.x if back else at.block
        copies = []
        if stage == 1:
            for k in range(1, ZS):
                z = at.z_at(ZS - k) if back else at.z
                copies.append(self.copy(out.at[both, z, at.b, some], at.bs + k - 1, at.z_peer(k)))
                slot = at.bs + ZS + k - 2
                copies.append(self.copy(out.at[at.block, z, :, rest], slot, at.z_peer(k)))
            return copies
        base = 0 if stage == 0 else at.bs + 2 * ZS - 2
        for k in range(1, at.bs):
            b = at.b_at(at.bs - k) if back else at.b
            region = out.at[at.block, at.z, b, rest] if stage == 0 else out.at[both, :, b, some]
            copies.append(self.copy(region, base + k, at.b_peer(k)))
        if stage == 0:
            region = out.at[x_block, at.z, at.b, some]
        else:
            region = out.at[x_block, :, :, rest]
        copies.append(self.copy(region, base, at.x_peer))
        return copies


class Fold:
    def __init__(self, at, grads, total, landing, bufs, final, send, recv, credit, half):
        self.at, self.grads, self.total = at, grads, total
        self.landing, self.bufs, self.final = landing, bufs, final
        self.send, self.recv, self.credit = send, recv, credit
        self.half = half
        nb = at.bs - 1
        self.slot_x1 = 1
        self.slot_b1 = 2
        self.slot_x2 = 2 + nb
        self.slot_b2 = 3 + nb
        self.slot_z = 3 + 2 * nb

    @staticmethod
    def slots(bs):
        return 3 + 2 * (bs - 1) + ZS - 1

    @staticmethod
    def buffers(bs, rows, half):
        nb = max(bs - 1, 1)
        rest = ZS - half
        return [
            (half, bs, rows, LANES),
            (nb, 2, rest, rows, LANES),
            (rest, rows, LANES),
            (nb, half, rows, LANES),
            (ZS - 1, rows, LANES),
        ]

    def core_parts(self):
        other = self.grads.at[pl.ds((1 - self.at.c) * 2, 2)]
        return [(other, self.landing, 0, self.at.core_peer, self.at.core_peer)]

    def parts(self, stage):
        at, half, total, bufs = self.at, self.half, self.total, self.bufs
        if stage == 0:
            return self.core_parts()
        if stage == 3:
            return [
                (
                    total.at[at.x, at.z_at(k), at.b],
                    bufs[4].at[k - 1],
                    self.slot_z + k - 1,
                    at.z_peer(k),
                    at.z_peer(ZS - k),
                )
                for k in range(1, ZS)
            ]
        rest = pl.ds(half, ZS - half)
        found = []
        for k in range(1, at.bs):
            if stage == 1:
                src, buf, slot = total.at[:, rest, at.b_at(k)], bufs[1], self.slot_b1
            else:
                src, buf, slot = total.at[at.x, pl.ds(0, half), at.b_at(k)], bufs[3], self.slot_b2
            found.append((src, buf.at[k - 1], slot + k - 1, at.b_peer(k), at.b_peer(at.bs - k)))
        if stage == 1:
            src, buf, slot = total.at[1 - at.x, pl.ds(0, half)], bufs[0], self.slot_x1
        else:
            src, buf, slot = total.at[1 - at.x, rest, at.b], bufs[2], self.slot_x2
        found.append((src, buf, slot, at.x_peer, at.x_peer))
        return found

    def start(self, stage, again):
        for src, buf, slot, to, _ in self.parts(stage):
            if again is not False:

                @pl.when(again)
                def _():
                    pl.semaphore_wait(self.credit.at[slot], 1)

            remote(src, buf, self.send.at[slot], self.recv.at[slot], to).start()

    def land(self, stage, more):
        parts = self.parts(stage)
        for src, buf, slot, to, _ in parts:
            remote(src, buf, self.send.at[slot], self.recv.at[slot], to).wait()
        self.add(stage)
        if more is not False:

            @pl.when(more)
            def _():
                for _, _, slot, _, origin in parts:
                    pl.semaphore_signal(
                        self.credit.at[slot], inc=1, device_id=origin, device_id_type=MESH
                    )

    def add_core(self):
        at, bs, total = self.at, self.at.bs, self.total

        @pl.loop(0, 2 * ZS * bs)
        def _(i):
            z, b = i // bs % ZS, i % bs
            x = i // (ZS * bs)
            total[x, z, b] = self.grads[at.c * 2 + x, z, b] + self.landing[x, z, b]

    def add(self, stage):
        at, half, bs = self.at, self.half, self.at.bs
        total, bufs = self.total, self.bufs
        rest = ZS - half
        if stage == 0:
            self.add_core()
        elif stage == 1:

            @pl.loop(0, half * bs)
            def _(i):
                z, b = i // bs, i % bs
                total[at.x, z, b] = total[at.x, z, b] + bufs[0][z, b]

            @pl.loop(0, 2 * rest)
            def _(i):
                x, z = i // rest, i % rest
                for k in range(bs - 1):
                    total[x, half + z, at.b] = total[x, half + z, at.b] + bufs[1][k, x, z]

        elif stage == 2:

            @pl.loop(0, rest)
            def _(z):
                total[at.x, half + z, at.b] = total[at.x, half + z, at.b] + bufs[2][z]

            @pl.loop(0, half)
            def _(z):
                for k in range(bs - 1):
                    total[at.x, z, at.b] = total[at.x, z, at.b] + bufs[3][k, z]

        else:
            self.finish([bufs[4][k] for k in range(ZS - 1)])

    def finish(self, pieces):
        at = self.at
        done = self.total[at.x, at.z, at.b].astype(jnp.float32)
        for piece in pieces:
            done = done + piece.astype(jnp.float32)
        self.final[...] = done.astype(self.final.dtype)

    def move(self, stage, again, more):
        self.land(stage, more)
        self.start(stage + 1, again)


class FoldCross(Fold):
    @staticmethod
    def slots(bs):
        return 2 * bs + 2 * ZS - 1

    @staticmethod
    def buffers(bs, rows, half):
        nb = max(bs - 1, 1)
        cut = rows // 32 * 16
        rest = rows - cut
        return [
            (nb, 2, ZS, cut, LANES),
            (ZS, bs, rest, LANES),
            (ZS - 1, 2, cut, LANES),
            (ZS - 1, bs, rest, LANES),
            (cut, LANES),
            (nb, rest, LANES),
        ]

    def cuts(self):
        rows = self.total.shape[-2]
        cut = rows // 32 * 16
        return pl.ds(0, cut), pl.ds(cut, rows - cut)

    def parts(self, stage):
        at, total, bufs = self.at, self.total, self.bufs
        if stage == 0:
            return self.core_parts()
        some, rest = self.cuts()
        found = []
        if stage == 2:
            for k in range(1, ZS):
                pair = (at.z_peer(k), at.z_peer(ZS - k))
                z = at.z_at(k)
                found.append((total.at[:, z, at.b, some], bufs[2].at[k - 1], at.bs + k, *pair))
                slot = at.bs + ZS + k - 1
                found.append((total.at[at.x, z, :, rest], bufs[3].at[k - 1], slot, *pair))
            return found
        base = 1 if stage == 1 else at.bs + 2 * ZS - 1
        for k in range(1, at.bs):
            pair = (at.b_peer(k), at.b_peer(at.bs - k))
            if stage == 1:
                src, buf = total.at[:, :, at.b_at(k), some], bufs[0].at[k - 1]
            else:
                src, buf = total.at[at.x, at.z, at.b_at(k), rest], bufs[5].at[k - 1]
            found.append((src, buf, base + k, *pair))
        if stage == 1:
            src, buf = total.at[1 - at.x, :, :, rest], bufs[1]
        else:
            src, buf = total.at[1 - at.x, at.z, at.b, some], bufs[4]
        found.append((src, buf, base, at.x_peer, at.x_peer))
        return found

    def add(self, stage):
        at, bs = self.at, self.at.bs
        total, bufs = self.total, self.bufs
        some, rest = self.cuts()
        if stage == 0:
            self.add_core()
        elif stage == 1:

            @pl.loop(0, 2 * ZS)
            def _(i):
                x, z = i // ZS, i % ZS
                for k in range(bs - 1):
                    total[x, z, at.b, some] = total[x, z, at.b, some] + bufs[0][k, x, z]

            @pl.loop(0, ZS * bs)
            def _(i):
                z, b = i // bs, i % bs
                total[at.x, z, b, rest] = total[at.x, z, b, rest] + bufs[1][z, b]

        elif stage == 2:
            for x in range(2):
                for k in range(ZS - 1):
                    total[x, at.z, at.b, some] = total[x, at.z, at.b, some] + bufs[2][k, x]

            @pl.loop(0, bs)
            def _(b):
                for k in range(ZS - 1):
                    total[at.x, at.z, b, rest] = total[at.x, at.z, b, rest] + bufs[3][k, b]

        else:
            total[at.x, at.z, at.b, some] = total[at.x, at.z, at.b, some] + bufs[4][...]
            for k in range(bs - 1):
                total[at.x, at.z, at.b, rest] = total[at.x, at.z, at.b, rest] + bufs[5][k]
            self.final[...] = total[at.x, at.z, at.b]


HALF = 256
WIDE = 512
QKV_TILE = 768
VEC_ROWS = 16


def dot_nt(a, b):
    return lax.dot_general(a, b, (((1,), (1,)), ((), ())), preferred_element_type=jnp.float32)


def dot_nn(a, b):
    return lax.dot_general(a, b, (((1,), (0,)), ((), ())), preferred_element_type=jnp.float32)


def dot_tn(a, b):
    return lax.dot_general(a, b, (((0,), (0,)), ((), ())), preferred_element_type=jnp.float32)


def aligned(index, unit):
    return pl.multiple_of(index, unit)


def rows_of(ref, bs, first, count, start, rows, blocks=range(SECT)):
    parts = []
    for i in range(count):
        d = first + i
        place = (d // bs, d % bs)
        parts.append(
            jnp.concatenate(
                [ref[(lb,) + place + (pl.ds(start, rows), slice(None))] for lb in blocks], axis=1
            )
        )
    return parts[0] if count == 1 else jnp.concatenate(parts, axis=0)


def put_rows(ref, bs, first, count, start, rows, value, block=0):
    value = value.astype(ref.dtype)
    for i in range(count):
        d = first + i
        place = (d // bs, d % bs)
        for lane in range(value.shape[1] // LANES):
            ref[(block + lane,) + place + (pl.ds(start, rows), slice(None))] = value[
                i * rows : (i + 1) * rows, lane * LANES : (lane + 1) * LANES
            ]


def vector_pieces(dps):
    n_gains, n_biases = 2 * WIDE // dps, 10 * WIDE // dps
    starts = [(0, 0), (0, 2), (1, 0), (1, 2), (2, 0), (2, 1), (2, 2), (2, 3), (3, 0), (3, 2)]
    pieces = []
    for d in range(dps):
        at = 0
        while at < n_gains + n_biases:
            if at < n_gains:
                index = d * n_gains + at
                row, column = (1, 3)[index // WIDE], WIDE + index % WIDE
                left = n_gains - at
            else:
                index = d * n_biases + at - n_gains
                row, part = starts[index // WIDE]
                column = part * WIDE + index % WIDE
                left = n_gains + n_biases - at
            size = min(left, LANES - at % LANES, LANES - column % LANES)
            pieces.append((d, at // WIDE, at % WIDE, row, column, size))
            at += size
    return pieces


def read_vectors(ref, table, bs, start):
    dps = ZS * bs
    tiles = {}
    for d, row, lane, to_row, to_lane, size in vector_pieces(dps):
        key = (d, lane // LANES)
        if key not in tiles:
            tile = ref[lane // LANES, d // bs, d % bs, start : start + VEC_ROWS, :]
            tiles[key] = tile.astype(jnp.float32)
        off = lane % LANES
        table[to_row : to_row + 1, to_lane : to_lane + size] = tiles[key][
            row : row + 1, off : off + size
        ]


def write_vectors(ref, table, bs, start):
    dps = ZS * bs
    found = {}
    for d, row, lane, to_row, to_lane, size in vector_pieces(dps):
        piece = table[to_row : to_row + 1, to_lane : to_lane + size]
        found.setdefault((d, lane // LANES), {}).setdefault(row, []).append(piece)
    row_id = lax.broadcasted_iota(jnp.int32, (VEC_ROWS, LANES), 0)
    for d in range(dps):
        for lb in range(SECT):
            tile = jnp.zeros((VEC_ROWS, LANES), jnp.float32)
            for row, pieces in found.get((d, lb), {}).items():
                have = sum(piece.shape[1] for piece in pieces)
                if have < LANES:
                    pieces = pieces + [jnp.zeros((1, LANES - have), jnp.float32)]
                line = pieces[0] if len(pieces) == 1 else jnp.concatenate(pieces, axis=1)
                tile = jnp.where(row_id == row, line, tile)
            ref[lb, d // bs, d % bs, start : start + VEC_ROWS, :] = tile.astype(ref.dtype)


def normalize(x, gain, shift):
    mean = jnp.mean(x, axis=1, keepdims=True)
    centred = x - mean
    scale = lax.rsqrt(jnp.mean(centred * centred, axis=1, keepdims=True) + NORM_EPS)
    return centred * scale * gain + shift


def normalize_back(x, grad, gain):
    mean = jnp.mean(x, axis=1, keepdims=True)
    centred = x - mean
    scale = lax.rsqrt(jnp.mean(centred * centred, axis=1, keepdims=True) + NORM_EPS)
    unit = centred * scale
    inner = grad * gain
    first = jnp.mean(inner, axis=1, keepdims=True)
    second = jnp.mean(inner * unit, axis=1, keepdims=True)
    out = scale * (inner - first - unit * second)
    return out, jnp.sum(grad * unit, axis=0, keepdims=True), jnp.sum(grad, axis=0, keepdims=True)


def gelu_pair(u):
    below = 0.5 + 0.5 * lax.erf(u * math.sqrt(0.5))
    bell = jnp.exp2((-0.5 * math.log2(math.e)) * (u * u))
    return u * below, below + u * (bell * (1.0 / math.sqrt(2.0 * math.pi)))


def head_masks(scale):
    lane = lax.broadcasted_iota(jnp.int32, (1, LANES), 1)
    first = jnp.where(lane < HEAD, scale, 0.0).astype(jnp.bfloat16)
    second = jnp.where(lane < HEAD, 0.0, scale).astype(jnp.bfloat16)
    return first, second


class Sizes:
    def __init__(self, dps):
        self.dps, self.bs = dps, dps // ZS
        self.qkv, self.out, self.up, self.down = (
            3 * WIDE // dps,
            WIDE // dps,
            4 * WIDE // dps,
            WIDE // dps,
        )
        self.att = self.qkv + VEC_ROWS
        self.dense = self.out + self.up
        self.wide = 4 * self.down


def qkv_rows(size, w, tile):
    count = QKV_TILE // size.qkv
    return rows_of(w, size.bs, tile * count, count, 0, size.qkv)


def out_rows(size, w):
    return rows_of(w, size.bs, 0, size.dps, 0, size.out)


def up_rows(size, w, tile):
    count = HALF // size.up
    return rows_of(w, size.bs, tile * count, count, size.out, size.up)


def forward_mix(size, w, table, h, mixed, piece):
    columns = slice(piece * QKV_TILE, (piece + 1) * QKV_TILE)
    mixed[:, columns] = (
        dot_nt(h[...], qkv_rows(size, w, piece)) + table[0:1, columns]
    ).astype(mixed.dtype)


def forward_attend(mixed, lse, attended, pair):
    lane = pair * LANES
    key_rows = mixed[:, WIDE + lane : WIDE + lane + LANES]
    values = mixed[:, 2 * WIDE + lane : 2 * WIDE + lane + LANES].T

    for part in range(2):
        rows = slice(part * HALF, (part + 1) * HALF)
        queries = mixed[rows, lane : lane + LANES]
        joined = []
        for head, mask in enumerate(head_masks(1.0 / math.sqrt(HEAD))):
            scores = dot_nt(key_rows, queries * mask)
            top = jnp.max(scores, axis=0, keepdims=True)
            probs = jnp.exp(scores - top)
            total = jnp.sum(probs, axis=0, keepdims=True)
            lse[2 * pair + head, :, rows] = top + jnp.log(total)
            probs = (probs * (1.0 / total)).astype(jnp.bfloat16)
            joined.append(dot_nn(values[head * HEAD : (head + 1) * HEAD], probs))
        joined = jnp.concatenate(joined, axis=0).T
        attended[rows, lane : lane + LANES] = joined.astype(attended.dtype)


def forward_project(size, w, table, h, attended, first, normed):
    out = dot_nt(attended[...], out_rows(size, w))
    for part in range(2):
        rows = slice(part * HALF, (part + 1) * HALF)
        total = h[rows, :].astype(jnp.float32) + (out[rows] + table[1:2, 0:WIDE])
        first[rows, :] = total
        normed[rows, :] = normalize(
            total, table[1:2, WIDE : 2 * WIDE], table[1:2, 2 * WIDE : 3 * WIDE]
        ).astype(normed.dtype)


def forward_up(size, w, table, normed, slope, hidden, piece):
    for j in (2 * piece, 2 * piece + 1):
        columns = slice(j * HALF, (j + 1) * HALF)
        upper = dot_nt(normed[...], up_rows(size, w, j)) + table[2:3, columns]
        value, grad = gelu_pair(upper)
        hidden[:, columns] = value.astype(hidden.dtype)
        slope[:, columns] = grad.astype(slope.dtype)


def forward_down(size, w, table, normed, hidden, second, h, piece):
    columns = slice(piece * HALF, (piece + 1) * HALF)
    count = size.dps // 2
    matrix = jnp.concatenate(
        [
            rows_of(w, size.bs, piece * count, count, j * size.down, size.down)
            for j in range(4)
        ],
        axis=1,
    )
    out = dot_nt(hidden[...], matrix)
    second[:, columns] = normed[:, columns].astype(jnp.float32) + (out + table[3:4, columns])
    if piece == 1:
        for part in range(2):
            rows = slice(part * HALF, (part + 1) * HALF)
            h[rows, :] = normalize(
                second[rows, :], table[3:4, WIDE : 2 * WIDE], table[3:4, 2 * WIDE : 3 * WIDE]
            ).astype(h.dtype)


def backward_norm_two(table, dtable, dy, second, dnormed, dlow, dlow_t):
    dtable[...] = jnp.zeros_like(dtable)
    for part in range(2):
        rows = slice(part * HALF, (part + 1) * HALF)
        grad, gain_sum, shift_sum = normalize_back(
            second[rows, :], dy[rows, :].astype(jnp.float32), table[3:4, WIDE : 2 * WIDE]
        )
        dnormed[rows, :] = grad
        dlow[rows, :] = grad.astype(dlow.dtype)
        dtable[3:4, 0:WIDE] += jnp.sum(grad, axis=0, keepdims=True)
        dtable[3:4, WIDE : 2 * WIDE] += gain_sum
        dtable[3:4, 2 * WIDE : 3 * WIDE] += shift_sum
    dlow_t[...] = dlow[...].T


def backward_down(size, grads, hidden, dlow_t, piece):
    @pl.loop(2 * piece, 2 * piece + 2)
    def _(i):
        start = aligned(i * size.down, 16)
        for half in range(2):
            columns = pl.ds(aligned(i * WIDE, WIDE) + half * HALF, HALF)
            value = dot_nn(dlow_t[...], hidden[:, columns])
            put_rows(grads, size.bs, 0, size.dps, start, size.down, value, 2 * half)


def backward_gelu(size, w, dtable, slope, dlow, dup, piece):
    @pl.loop(2 * piece, 2 * piece + 2)
    def _(i):
        start = aligned(i * size.down, 16)
        for half in range(2):
            columns = pl.ds(aligned(i * WIDE, WIDE) + half * HALF, HALF)
            blocks = (2 * half, 2 * half + 1)
            matrix = rows_of(w, size.bs, 0, size.dps, start, size.down, blocks)
            dupper = dot_nn(dlow[...], matrix) * slope[:, columns].astype(jnp.float32)
            dtable[2:3, columns] = jnp.sum(dupper, axis=0, keepdims=True)
            dup[:, columns] = dupper.astype(dup.dtype)


def backward_up(size, grads, normed, dup):
    count = HALF // size.up

    @pl.loop(0, 4)
    def _(i):
        for half in range(2):
            columns = pl.ds(aligned(i * WIDE, WIDE) + half * HALF, HALF)
            value = dot_tn(dup[:, columns], normed[...])
            first = (2 * i + half) * count
            put_rows(grads, size.bs, first, count, size.out, size.up, value)


def backward_normed(size, w, dnormed, dup):
    for half in range(2):
        columns = slice(half * HALF, (half + 1) * HALF)
        blocks = (2 * half, 2 * half + 1)
        matrix = rows_of(w, size.bs, 0, size.dps, size.out, size.up, blocks)
        dnormed[:, columns] = dnormed[:, columns] + dot_nn(dup[...], matrix)


def backward_norm_one(size, w, table, grads, dtable, first, attended, dnormed, dlow, dlow_t):
    for part in range(2):
        rows = slice(part * HALF, (part + 1) * HALF)
        grad, gain_sum, shift_sum = normalize_back(
            first[rows, :], dnormed[rows, :], table[1:2, WIDE : 2 * WIDE]
        )
        dnormed[rows, :] = grad
        dlow[rows, :] = grad.astype(dlow.dtype)
        dtable[1:2, 0:WIDE] += jnp.sum(grad, axis=0, keepdims=True)
        dtable[1:2, WIDE : 2 * WIDE] += gain_sum
        dtable[1:2, 2 * WIDE : 3 * WIDE] += shift_sum
    dlow_t[...] = dlow[...].T
    for block in (0, 2):
        columns = slice(block * LANES, (block + 2) * LANES)
        value = dot_nn(dlow_t[...], attended[:, columns])
        put_rows(grads, size.bs, 0, size.dps, 0, size.out, value, block)
    dlow[...] = dot_nn(dlow[...], out_rows(size, w)).astype(dlow.dtype)


def backward_attend(mixed, lse, dtable, dlow, dmixed, pair):
    scale = 1.0 / math.sqrt(HEAD)
    lane = pair * LANES
    columns = slice(lane, lane + LANES)
    key_columns = slice(WIDE + lane, WIDE + lane + LANES)
    value_columns = slice(2 * WIDE + lane, 2 * WIDE + lane + LANES)
    key_rows = mixed[:, key_columns]
    keys_t = key_rows.T
    values = mixed[:, value_columns]
    dkeys = jnp.zeros((WIDE, LANES), jnp.float32)
    dvalues = jnp.zeros((WIDE, LANES), jnp.float32)
    for part in range(2):
        rows = slice(part * HALF, (part + 1) * HALF)
        queries = mixed[rows, columns]
        grad_out = dlow[rows, columns]
        dqueries = []
        for head in range(2):
            query = queries * head_masks(scale)[head]
            grad = grad_out * head_masks(1.0)[head]
            probs = jnp.exp(dot_nt(key_rows, query) - lse[2 * pair + head, :, rows])
            dprobs = dot_nt(values, grad)
            delta = jnp.sum(probs * dprobs, axis=0, keepdims=True)
            dscores = (probs * (dprobs - delta)).astype(jnp.bfloat16)
            dvalues = dvalues + dot_nn(probs.astype(jnp.bfloat16), grad)
            dkeys = dkeys + dot_nn(dscores, query)
            dqueries.append(dot_nn(keys_t[head * HEAD : (head + 1) * HEAD], dscores))
        dquery = jnp.concatenate(dqueries, axis=0).T * scale
        dtable[0:1, columns] += jnp.sum(dquery, axis=0, keepdims=True)
        dmixed[rows, columns] = dquery.astype(dmixed.dtype)
    dmixed[:, key_columns] = dkeys.astype(dmixed.dtype)
    dmixed[:, value_columns] = dvalues.astype(dmixed.dtype)
    dtable[0:1, value_columns] = jnp.sum(dvalues, axis=0, keepdims=True)


def backward_mix(size, grads, h, dmixed, piece):
    count = QKV_TILE // size.qkv
    grad = dmixed[:, piece * QKV_TILE : (piece + 1) * QKV_TILE]
    put_rows(grads, size.bs, piece * count, count, 0, size.qkv, dot_tn(grad, h[...]))


def backward_input(size, w, dnormed, dmixed, dy):
    for half in range(2):
        columns = slice(half * HALF, (half + 1) * HALF)
        blocks = (2 * half, 2 * half + 1)
        matrix = rows_of(w, size.bs, 0, size.dps, 0, size.qkv, blocks)
        dy[:, columns] = (dnormed[:, columns] + dot_nn(dmixed[...], matrix)).astype(dy.dtype)


WINDOW = 384


def group_rows(group):
    rows = lax.broadcasted_iota(jnp.int32, (16, LANES), 0)
    return jnp.where(rows == group, 1.0, 0.0).astype(jnp.bfloat16)


def pack_mix(piece, qkv, gains, biases):
    low = piece.dtype
    rows = qkv.shape[0]
    flat = jnp.concatenate([gains[...], biases[...]], axis=1)
    flat = jnp.concatenate([flat, jnp.zeros((1, 2 * WIDE - flat.shape[1]), flat.dtype)], axis=1)
    row_id = lax.broadcasted_iota(jnp.int32, (VEC_ROWS, LANES), 0)
    for lb in range(SECT):
        lane = lb * LANES
        piece[lb, :rows] = qkv[:, lane : lane + LANES].astype(low)
        tile = jnp.where(row_id == 0, flat[:, lane : lane + LANES], 0.0)
        lane += WIDE
        tile = jnp.where(row_id == 1, flat[:, lane : lane + LANES], tile)
        piece[lb, rows:] = tile.astype(low)


def pack_up(piece, out, up):
    rows = out.shape[0]
    for lb in range(SECT):
        lanes = slice(lb * LANES, (lb + 1) * LANES)
        piece[lb, :rows] = out[:, lanes].astype(piece.dtype)
        piece[lb, rows:] = up[:, lanes].astype(piece.dtype)


def pack_down(piece, down):
    rows = down.shape[0]
    for lb in range(SECT):
        for j in range(4):
            start = j * WIDE + lb * LANES
            piece[lb, j * rows : (j + 1) * rows] = down[:, start : start + LANES].astype(piece.dtype)


def pack_embedding(piece, weight, shift, rows):
    n = weight.shape[1]
    rows[...] = jnp.zeros_like(rows)
    rows[:GROUPS, :n] = shift[...]
    rows[512 - L3 : 512, :n] = weight[L1 + L2 :]
    rows[768 - L2 : 768, :n] = weight[L1 : L1 + L2]
    rows[1024 - L1 :, :n] = weight[:L1]
    columns = rows[...].T[:n].astype(piece.dtype)
    for lb in range(SECT):
        for part in range(2):
            start = part * WIDE + lb * LANES
            piece[lb, part * n : (part + 1) * n] = columns[:, start : start + LANES]


def expand(series, group, x):
    empty = jnp.zeros((WINDOW - series.shape[0], series.shape[1]), series.dtype)
    x[:, :WINDOW] = jnp.concatenate([empty, series[...]], axis=0).T
    lane = lax.broadcasted_iota(jnp.int32, (x.shape[0], LANES), 1)
    x[:, WINDOW:] = jnp.where(lane == group, 1.0, 0.0).astype(x.dtype)


def embed(size, emb, pick, x, wsel, h):
    rows = WIDE // size.dps
    first = rows_of(emb, size.bs, 0, size.dps, 0, rows)
    second = rows_of(emb, size.bs, 0, size.dps, rows, rows)
    long, middle, short = (pick[g : g + 1, :] for g in (2, 1, 0))
    wide = jnp.concatenate(
        [
            first[:, LANES : 2 * LANES] * long,
            first[:, 2 * LANES : 3 * LANES] * long + second[:, :LANES] * middle,
            first[:, 3 * LANES :] * long
            + second[:, LANES : 2 * LANES] * middle
            + second[:, 3 * LANES :] * short,
        ],
        axis=1,
    )
    wsel[...] = wide.T
    matrix = jnp.concatenate([wide, first[:, :LANES]], axis=1)
    h[...] = dot_nt(x[...], matrix).astype(h.dtype)


def embed_back(size, pick, x, wsel, dh, grads, series_grad):
    history = series_grad.shape[0]
    series_grad[...] = dot_nt(wsel[...], dh[...])[WINDOW - history :]
    sums = dot_tn(dh[...], x[...])
    long, middle, short = (pick[g : g + 1, :].astype(jnp.float32) for g in (2, 1, 0))
    parts = [sums[:, i * LANES : (i + 1) * LANES] for i in range(4)]
    parts = [
        parts[3],
        parts[0] * long,
        parts[1] * long,
        parts[2] * long,
        parts[1] * middle,
        parts[2] * middle,
        jnp.zeros_like(parts[0]),
        parts[2] * short,
    ]
    rows = WIDE // (SECT * size.dps)
    for pipe in range(SECT):
        block = (pipe % 2) * 2 + pipe // 2
        for dp in range(size.dps):
            start = (pipe * size.dps + dp) * rows
            piece = jnp.concatenate([part[start : start + rows] for part in parts], axis=0)
            grads[block, dp // size.bs, dp % size.bs] = piece.astype(grads.dtype)


def saved_shapes():
    low, wide = jnp.bfloat16, jnp.float32
    return [
        ((WIDE, WIDE), low),
        ((WIDE, 3 * WIDE), low),
        ((2 * SECT, 1, WIDE), wide),
        ((WIDE, WIDE), low),
        ((WIDE, WIDE), wide),
        ((WIDE, WIDE), low),
        ((WIDE, 4 * WIDE), low),
        ((WIDE, 4 * WIDE), low),
        ((WIDE, WIDE), wide),
        ((SECT, 4 * WIDE), wide),
    ]


def chunk_shape(size, rows):
    return (SECT, ZS, size.bs, rows, LANES)


HALVES = (2, 2, 2, 2)
CROSS = (2,)


def follow(plan, section, act, compute):
    seen = {}
    for step in plan:
        if len(step) == 1:
            piece = seen.get(step[0], 0)
            seen[step[0]] = piece + 1
            compute(step[0], piece)
            continue
        op, kind, offset = step
        where = section + offset
        if isinstance(where, int):
            if 0 <= where < SECT:
                act(op, kind, where)
        elif offset == 0:
            act(op, kind, where)
        else:
            inside = where < SECT if offset > 0 else where >= 0

            @pl.when(inside)
            def _():
                act(op, kind, where)


def forward_kernel(dps, groups, *refs):
    size = Sizes(dps)
    given, refs = refs[:9], refs[9:]
    out, wholes, wsel, x, refs = refs[0], refs[1:5], refs[5], refs[6], refs[7:]
    kept, local, refs = refs[:10], refs[10:20], refs[20:]
    buffers, refs = refs[:4], refs[4:]
    pieces, held, refs = refs[:4], refs[4:13], refs[13:]
    emb_rows, pick, refs = refs[0], refs[1], refs[2:]
    given_sem, w_sem, kept_sem, own_sem, p_send, p_recv, send, recv = refs
    h, mixed, lse, attended, first, normed, slope, hidden, second, table = local
    w_att, w_up, w_down, w_emb = buffers
    at = Place(dps)

    own = [
        pltpu.make_async_copy(
            pieces[kind].at[at.block],
            wholes[kind].at[at.pipe, at.block, at.z, at.b]
            if kind < EMB
            else wholes[kind].at[at.block, at.z, at.b],
            own_sem.at[kind],
        )
        for kind in range(4)
    ]
    def split(kind, back):
        copies = []
        for k in range(1, SECT):
            if back:
                region = wholes[kind].at[at.pipe_at(SECT - k), at.block, at.z, at.b]
                src = region
            else:
                block = at.block_of(at.pipe_at(k))
                region = wholes[kind].at[at.pipe, block, at.z, at.b]
                src = pieces[kind].at[block]
            sems = p_send.at[kind, k - 1], p_recv.at[kind, k - 1]
            copies.append(remote(src, region, *sems, (at.pipe_at(k), at.dp)))
        return copies

    def chunk(kind, section):
        if kind == EMB:
            return Spread(at, wholes[kind], send.at[3 * SECT], recv.at[3 * SECT])
        number = 3 * section + kind
        sort = SpreadCross if kind in CROSS else Spread
        return sort(at, wholes[kind].at[section], send.at[number], recv.at[number], HALVES[kind])

    def load(kind, section, core):
        blocks = pl.ds(core * 2, 2)
        src, dst = wholes[kind], buffers[kind]
        if kind != EMB:
            src, dst = src.at[section], dst.at[section % 2]
        sem = w_sem.at[kind, section % 2, core]
        return pltpu.make_async_copy(src.at[blocks], dst.at[blocks], sem)

    def loaded(kind, section):
        load(kind, section, at.c).wait()
        load(kind, section, 1 - at.c).wait()

    arrived = []

    def act(op, kind, section):
        if op == 0:
            if kind not in arrived:
                arrived.append(kind)
                own[kind].wait()
                if kind == EMB:
                    chunk(kind, section).start(0)
                    return
                for copy in split(kind, True):
                    copy.wait_recv()
                for copy in split(kind, False):
                    copy.wait_send()
                if kind == 0:
                    copies_start(split(1, False))
                    copies_start(split(2, False))
            chunk(kind, section).start(0)
        elif op < 4:
            chunk(kind, section).move(op - 1)
            if op == 3:
                load(kind, section, at.c).start()
        else:
            chunk(kind, section).land(3)
            load(kind, section, 1 - at.c).start()

    def saves(section, early):
        which = (1, 2, 3, 4, 5, 9) if early else (6, 7, 8)
        return [
            pltpu.make_async_copy(local[i], kept[i].at[section], kept_sem.at[i]) for i in which
        ]

    series, embed_weight, embed_bias, qkv, out_w, up_w, down_w, gains, biases = held
    gets = copies_of(zip(given, held), given_sem)
    for i in (3, 7, 8, 1, 2, 4, 5, 6, 0):
        gets[i].start()
    pick[...] = group_rows(groups[0])
    at.greet()
    copies_wait([gets[i] for i in (3, 7, 8)])
    pack_mix(pieces[0], qkv, gains, biases)
    own[0].start()
    at.met()
    copies_start(split(0, False))
    copies_wait(gets[1:3])
    pack_embedding(pieces[EMB], embed_weight, embed_bias, emb_rows)
    own[EMB].start()
    copies_wait(gets[4:7])
    pack_up(pieces[1], out_w, up_w)
    own[1].start()
    pack_down(pieces[2], down_w)
    own[2].start()
    table[...] = jnp.zeros_like(table)
    gets[0].wait()
    expand(series, groups[0], x)

    def before(name, piece):
        loaded(EMB, 0)
        embed(size, w_emb, pick, x, wsel, h)

    follow(FORWARD_START, 0, act, before)

    @pl.loop(0, SECT)
    def _(section):
        att, up, down = (ref.at[section % 2] for ref in (w_att, w_up, w_down))
        keep_h = pltpu.make_async_copy(h, kept[0].at[section], kept_sem.at[0])

        def compute(name, piece):
            if name == "mix":
                if piece == 0:

                    @pl.when(section > 0)
                    def _():
                        copies_wait(saves(section - 1, True))

                    keep_h.start()
                    loaded(0, section)
                    read_vectors(att, table, size.bs, size.qkv)
                forward_mix(size, att, table, h, mixed, piece)
            elif name == "attend":
                forward_attend(mixed, lse, attended, piece)
            elif name == "project":
                loaded(1, section)
                forward_project(size, up, table, h, attended, first, normed)
                copies_start(saves(section, True))
            elif name == "up":
                if piece == 0:

                    @pl.when(section > 0)
                    def _():
                        copies_wait(saves(section - 1, False))

                forward_up(size, up, table, normed, slope, hidden, piece)
            else:
                if piece == 0:
                    loaded(2, section)
                    keep_h.wait()
                forward_down(size, down, table, normed, hidden, second, h, piece)
                if piece == 1:
                    copies_start(saves(section, False))

        follow(FORWARD_PERIOD, section, act, compute)

    copies_wait(saves(SECT - 1, True))
    copies_wait(saves(SECT - 1, False))
    out[...] = h[...]


def copies_of(pairs, sems):
    return [pltpu.make_async_copy(src, dst, sems.at[i]) for i, (src, dst) in enumerate(pairs)]


def forward_all(groups, given, dps):
    size = Sizes(dps)
    low, wide = jnp.bfloat16, jnp.float32
    shapes = saved_shapes()
    rows = (size.att, size.dense, size.wide, 2 * WIDE // dps)
    chunks = [chunk_shape(size, count) for count in rows]
    anywhere = pl.BlockSpec(memory_space=pl.ANY)
    inside = pl.BlockSpec(memory_space=pltpu.VMEM)
    outs = [((WIDE, WIDE), low)]
    outs += [((SECT,) + shape, low) for shape in chunks[:3]] + [(chunks[3], low)]
    outs += [((WINDOW, WIDE), low), ((WIDE, WIDE), low)]
    outs += [((SECT,) + shape, dtype) for shape, dtype in shapes]
    scratch = shapes + [((2,) + shape, low) for shape in chunks[:3]] + [(chunks[3], low)]
    scratch += [((SECT, count, LANES), low) for count in rows]
    scratch += [(array.shape, array.dtype) for array in given]
    scratch += [((2 * WIDE, LANES), wide), ((16, LANES), low)]
    slots = max(Spread.slots(size.bs), SpreadCross.slots(size.bs))
    dma = pltpu.SemaphoreType.DMA
    return pl.pallas_call(
        partial(forward_kernel, dps),
        out_shape=[jax.ShapeDtypeStruct(shape, dtype) for shape, dtype in outs],
        in_specs=[pl.BlockSpec(memory_space=pltpu.SMEM)] + [anywhere] * len(given),
        out_specs=[inside] + [anywhere] * 4 + [inside] * 2 + [anywhere] * len(shapes),
        scratch_shapes=[pltpu.VMEM(shape, dtype) for shape, dtype in scratch]
        + [
            dma((len(given),)),
            dma((4, 2, 2)),
            dma((len(shapes),)),
            dma((4,)),
            dma((3, SECT - 1)),
            dma((3, SECT - 1)),
            dma((1 + 3 * SECT, slots)),
            dma((1 + 3 * SECT, slots)),
        ],
        compiler_params=pltpu.CompilerParams(
            collective_id=0, has_side_effects=True, vmem_limit_bytes=56 * 1024 * 1024
        ),
        name="gather_forward",
    )(groups, *given)


def backward_kernel(dps, groups, att, up, down, cotangent, x_in, wsel_in, *refs):
    size = Sizes(dps)
    kept, refs = refs[:10], refs[10:]
    series_grad, outs, refs = refs[0], refs[1:5], refs[5:]
    local, refs = refs[:9], refs[9:]
    tables, w_att, w_up, w_down, dtable, dy, dnormed, dlow, dlow_t, dmixed, dup = refs[:11]
    x, wsel, pick, refs = *refs[11:14], refs[14:]
    kinds = []
    for kind in range(4):
        count = 6 if kind in CROSS else 5
        kinds.append(refs[:4] + (refs[4 : 4 + count],))
        refs = refs[4 + count :]
    w_sem, kept_sem, table_sem, late_sem, out_sem, p_send, p_recv, send, recv, credit = refs
    h, mixed, lse, attended, first, normed, slope, hidden, second = local
    at = Place(dps)
    last = SECT - 1

    def weights(kind, section):
        src, dst = ((att, w_att), (up, w_up), (down, w_down))[kind]
        return pltpu.make_async_copy(src.at[section], dst, w_sem.at[kind])

    def loads(section, dense):
        which = (5, 6, 7, 8) if dense else (0, 1, 2, 3, 4)
        found = [
            pltpu.make_async_copy(kept[i].at[section], local[i], kept_sem.at[i]) for i in which
        ]
        return found + [weights(kind, section) for kind in ((1, 2) if dense else (0,))]

    def chunk(kind, i):
        grads, totals, finals, landing, bufs = kinds[kind]
        sort = FoldCross if kind in CROSS else Fold
        refs = (grads, totals.at[i % 2], landing, bufs, finals.at[i])
        return sort(at, *refs, send.at[kind], recv.at[kind], credit.at[kind], HALVES[kind])

    def hand_over(kind, i):
        landing = outs[kind].at[at.block]
        final = kinds[kind][2].at[i]
        return (
            pltpu.make_async_copy(final, landing, out_sem.at[kind]),
            remote(final, landing, p_send.at[kind, i], p_recv.at[kind, at.pipe], (last - i, at.dp)),
        )

    def act(op, kind, i):
        again, more = (False, False) if kind == EMB else (i > 0, i < last)
        if op == 0:
            chunk(kind, i).start(0, again)
        elif op < 4:
            chunk(kind, i).move(op - 1, again, more)
        else:
            chunk(kind, i).land(3, more)
            if kind == EMB:
                outs[kind][...] = kinds[kind][2][0]
            else:
                here, away = hand_over(kind, i)

                @pl.when(at.pipe == last - i)
                def _():
                    here.start()

                @pl.when(at.pipe != last - i)
                def _():
                    away.start()

    copies_start(loads(last, True))
    get_tables = pltpu.make_async_copy(kept[9], tables, table_sem)
    get_tables.start()
    copies_start(loads(last, False))
    late = copies_of(((cotangent, dy), (x_in, x), (wsel_in, wsel)), late_sem)
    copies_start(late)
    pick[...] = group_rows(groups[0])
    at.greet()
    at.met()
    get_tables.wait()
    late[0].wait()

    @pl.loop(0, SECT)
    def _(i):
        section = last - i
        table = tables.at[section]

        def compute(name, piece):
            if name == "norm2":
                copies_wait(loads(section, True))
                backward_norm_two(table, dtable, dy, second, dnormed, dlow, dlow_t)
            elif name == "down":
                backward_down(size, kinds[2][0], hidden, dlow_t, piece)
            elif name == "gelu":
                backward_gelu(size, w_down, dtable, slope, dlow, dup, piece)
            elif name == "up":
                backward_up(size, kinds[1][0], normed, dup)
            elif name == "normed":
                backward_normed(size, w_up, dnormed, dup)
            elif name == "norm1":
                copies_wait(loads(section, False))
                backward_norm_one(
                    size, w_up, table, kinds[1][0], dtable, first, attended, dnormed, dlow, dlow_t
                )

                @pl.when(section > 0)
                def _():
                    copies_start(loads(section - 1, True))

            elif name == "attend":
                backward_attend(mixed, lse, dtable, dlow, dmixed, piece)
            elif name == "mix":
                backward_mix(size, kinds[0][0], h, dmixed, piece)
                if piece == 1:
                    write_vectors(kinds[0][0], dtable, size.bs, size.qkv)
            else:
                backward_input(size, w_att, dnormed, dmixed, dy)

                @pl.when(section > 0)
                def _():
                    copies_start(loads(section - 1, False))

        follow(BACKWARD_PERIOD, i, act, compute)

    def after(name, piece):
        copies_wait(late[1:])
        embed_back(size, pick, x, wsel, dy, kinds[EMB][0], series_grad)

    follow(BACKWARD_END, 0, act, after)

    for kind in range(3):
        for i in range(SECT):
            here, away = hand_over(kind, i)

            @pl.when(at.pipe == last - i)
            def _():
                here.wait()

            @pl.when(at.pipe != last - i)
            def _():
                away.wait_send()

        for k in range(1, SECT):
            other = at.pipe_at(k)
            landing = outs[kind].at[at.block_of(other)]
            sems = p_send.at[kind, 0], p_recv.at[kind, other]
            remote(landing, landing, *sems, (other, at.dp)).wait_recv()


def backward_all(groups, weights, cotangent, x, wsel, kept, history, dps):
    size = Sizes(dps)
    low, wide = jnp.bfloat16, jnp.float32
    anywhere = pl.BlockSpec(memory_space=pl.ANY)
    inside = pl.BlockSpec(memory_space=pltpu.VMEM)
    shapes = saved_shapes()
    rows_emb = 8 * WIDE // (SECT * dps)
    kind_rows = (size.att, size.dense, size.wide, rows_emb)
    scratch = shapes[:9] + [((SECT,) + shapes[9][0], wide)]
    scratch += [(chunk_shape(size, rows), low) for rows in kind_rows[:3]]
    scratch += [
        (shapes[9][0], wide),
        ((WIDE, WIDE), low),
        ((WIDE, WIDE), wide),
        ((WIDE, WIDE), low),
        ((WIDE, WIDE), low),
        ((WIDE, 3 * WIDE), low),
        ((WIDE, 4 * WIDE), low),
        ((WIDE, WIDE), low),
        ((WINDOW, WIDE), low),
        ((16, LANES), low),
    ]
    for kind, rows in enumerate(kind_rows):
        sets, results = (1, 1) if kind == EMB else (2, SECT)
        scratch += [
            (chunk_shape(size, rows), low),
            ((sets, 2, ZS, size.bs, rows, LANES), low),
            ((results, rows, LANES), low),
            ((2, ZS, size.bs, rows, LANES), low),
        ]
        sort = FoldCross if kind in CROSS else Fold
        scratch += [(shape, low) for shape in sort.buffers(size.bs, rows, HALVES[kind])]
    slots = max(Fold.slots(size.bs), FoldCross.slots(size.bs))
    dma = pltpu.SemaphoreType.DMA
    return pl.pallas_call(
        partial(backward_kernel, dps),
        out_shape=[jax.ShapeDtypeStruct((history, WIDE), wide)]
        + [jax.ShapeDtypeStruct((SECT, rows, LANES), low) for rows in kind_rows[:3]]
        + [jax.ShapeDtypeStruct((rows_emb, LANES), low)],
        in_specs=[pl.BlockSpec(memory_space=pltpu.SMEM)] + [anywhere] * (6 + len(kept)),
        out_specs=[inside] + [anywhere] * 3 + [inside],
        scratch_shapes=[pltpu.VMEM(shape, dtype) for shape, dtype in scratch]
        + [
            dma((3,)),
            dma((9,)),
            dma(()),
            dma((3,)),
            dma((3,)),
            dma((3, SECT)),
            dma((3, SECT)),
            dma((4, slots)),
            dma((4, slots)),
            pltpu.SemaphoreType.REGULAR((4, slots)),
        ],
        compiler_params=pltpu.CompilerParams(
            collective_id=1, has_side_effects=True, vmem_limit_bytes=60 * 1024 * 1024
        ),
        name="backward_fold",
    )(groups, *weights, cotangent, x, wsel, *kept)


def finish_kernel(dps, n_gains, n_biases, att, up, down, emb, block_in, series_in, *refs):
    size = Sizes(dps)
    block_out, series_out, embed_w, embed_b, qkv, out, up_out, down_out, gains, biases, sems = refs
    copies = copies_of(((block_in, block_out), (series_in, series_out)), sems)
    copies_start(copies)
    for lb in range(SECT):
        lanes = slice(lb * LANES, (lb + 1) * LANES)
        qkv[:, lanes] = att[lb, : size.qkv].astype(jnp.float32)
        out[:, lanes] = up[lb, : size.out].astype(jnp.float32)
        up_out[:, lanes] = up[lb, size.out :].astype(jnp.float32)
        for j in range(4):
            rows = slice(j * size.down, (j + 1) * size.down)
            start = j * WIDE + lb * LANES
            down_out[:, start : start + LANES] = down[lb, rows].astype(jnp.float32)
    tiles = [att[lb, size.qkv :].astype(jnp.float32) for lb in range(SECT)]
    flat = jnp.concatenate([tile[row : row + 1] for row in range(2) for tile in tiles], axis=1)
    gains[...] = flat[:, :n_gains]
    biases[...] = flat[:, n_gains : n_gains + n_biases]
    rows = emb.shape[0] // 8
    packed = emb[...].astype(jnp.float32)
    packed = jnp.concatenate([packed[i * rows : (i + 1) * rows] for i in range(8)], axis=1)
    packed = jnp.concatenate([packed, jnp.zeros((LANES - rows, 8 * LANES), jnp.float32)], axis=0)
    columns = packed.T
    embed_w[:L1] = columns[1024 - L1 :, :rows]
    embed_w[L1 : L1 + L2] = columns[768 - L2 : 768, :rows]
    embed_w[L1 + L2 :] = columns[512 - L3 : 512, :rows]
    embed_b[...] = columns[:GROUPS, :rows]
    copies_wait(copies)


def finish_all(sums, block, series, n_gains, n_biases, dps):
    size = Sizes(dps)
    wide = jnp.float32
    columns = WIDE // (SECT * dps)
    outs = [
        (block.shape, block.dtype),
        (series.shape, wide),
        ((L1 + L2 + L3, columns), wide),
        ((GROUPS, columns), wide),
        ((size.qkv, WIDE), wide),
        ((size.out, WIDE), wide),
        ((size.up, WIDE), wide),
        ((size.down, 4 * WIDE), wide),
        ((1, n_gains), wide),
        ((1, n_biases), wide),
    ]
    anywhere = pl.BlockSpec(memory_space=pl.ANY)
    inside = pl.BlockSpec(memory_space=pltpu.VMEM)
    return pl.pallas_call(
        partial(finish_kernel, dps, n_gains, n_biases),
        out_shape=[jax.ShapeDtypeStruct(shape, dtype) for shape, dtype in outs],
        in_specs=[inside] * 4 + [anywhere] * 2,
        out_specs=[anywhere] * 2 + [inside] * 8,
        scratch_shapes=[pltpu.SemaphoreType.DMA((2,))],
        compiler_params=pltpu.CompilerParams(vmem_limit_bytes=32 * 1024 * 1024),
        name="finish",
    )(*sums, block, series)


def per_device(
    series,
    groups,
    cotangent,
    embed_weight,
    embed_bias,
    qkv_weight,
    out_weight,
    up_weight,
    down_weight,
    gains,
    biases,
):
    dps = lax.axis_size("dp")
    given = (
        series[0],
        embed_weight,
        embed_bias,
        qkv_weight[0],
        out_weight[0],
        up_weight[0],
        down_weight[0],
        gains,
        biases,
    )
    block_output, att, up, down, _, wsel, x, *kept = forward_all(groups, given, dps)
    series_grad, *sums = backward_all(
        groups, (att, up, down), cotangent[0], x, wsel, kept, series.shape[1], dps
    )
    outs = finish_all(sums, block_output, series_grad, gains.shape[1], biases.shape[1], dps)
    block_output, series_grad, embed_w, embed_b, qkv, out, up, down, gain_sum, bias_sum = outs
    return (
        block_output[None],
        series_grad[None],
        embed_w,
        embed_b,
        qkv[None],
        out[None],
        up[None],
        down[None],
        gain_sum,
        bias_sum,
    )


def solution(mesh):
    return jax.shard_map(
        per_device,
        mesh=mesh,
        in_specs=(
            P(("pipe", "dp"), None, None),
            P(("pipe", "dp")),
            P(("pipe", "dp"), None, None),
            P(None, "dp"),
            P(None, "dp"),
            P("pipe", "dp", None),
            P("pipe", "dp", None),
            P("pipe", "dp", None),
            P("pipe", "dp", None),
            P("pipe", "dp"),
            P("pipe", "dp"),
        ),
        out_specs=(
            P(("pipe", "dp"), None, None),
            P(("pipe", "dp"), None, None),
            P(None, ("pipe", "dp")),
            P(None, ("pipe", "dp")),
            P("pipe", "dp", None),
            P("pipe", "dp", None),
            P("pipe", "dp", None),
            P("pipe", "dp", None),
            P("pipe", "dp"),
            P("pipe", "dp"),
        ),
        check_vma=False,
    )
```

```python
from functools import partial
import math

import jax
import jax.numpy as jnp
from jax import lax
from jax.experimental import pallas as pl
from jax.experimental.pallas import tpu as pltpu
from jax.sharding import PartitionSpec as P

HEAD = 64
L1 = 96
L2 = 192
L3 = 336
GROUPS = 3


NORM_EPS = 1e-05


MESH = pl.DeviceIdType.MESH
LANES = 128
ZS = 4
SECT = 4
EMB = 3


class Place:
    def __init__(self, dps):
        self.bs = dps // ZS
        pipe = lax.axis_index("pipe")
        dp = lax.axis_index("dp")
        self.pipe, self.dp = pipe, dp
        self.x, self.c = pipe // 2, pipe % 2
        self.z, self.b = dp // self.bs, dp % self.bs
        self.block = self.c * 2 + self.x
        self.x_peer = ((1 - self.x) * 2 + self.c, dp)
        self.core_peer = (self.x * 2 + 1 - self.c, dp)

    def block_of(self, pipe):
        return (pipe % 2) * 2 + pipe // 2

    def pipe_at(self, step):
        return (self.pipe + step) % SECT

    def z_at(self, step):
        return (self.z + step) % ZS

    def b_at(self, step):
        return (self.b + step) % self.bs

    def z_peer(self, step):
        return (self.pipe, self.z_at(step) * self.bs + self.b)

    def b_peer(self, step):
        return (self.pipe, self.z * self.bs + self.b_at(step))

    def greet(self):
        barrier = pltpu.get_barrier_semaphore()
        peers = [(self.pipe_at(k), self.dp) for k in range(1, SECT)]
        peers += [self.z_peer(k) for k in range(1, ZS)]
        peers += [self.b_peer(k) for k in range(1, self.bs)]
        for peer in peers:
            pl.semaphore_signal(barrier, inc=1, device_id=peer, device_id_type=MESH)

    def met(self):
        pl.semaphore_wait(pltpu.get_barrier_semaphore(), SECT + ZS + self.bs - 3)


def remote(src, dst, send, recv, peer):
    return pltpu.make_async_remote_copy(
        src_ref=src, dst_ref=dst, send_sem=send, recv_sem=recv, device_id=peer, device_id_type=MESH
    )


FORWARD_START = (
    (0, 3, 0),
    (0, 0, 0),
    (0, 2, 0),
    (1, 3, 0),
    (1, 0, 0),
    (0, 1, 0),
    (2, 3, 0),
    (2, 0, 0),
    (0, 0, 1),
    (1, 1, 0),
    (1, 2, 0),
    (3, 3, 0),
    (0, 2, 1),
    (1, 0, 1),
    (2, 1, 0),
    (4, 3, 0),
    (3, 0, 0),
    ("embed",),
    (4, 0, 0),
)
FORWARD_PERIOD = (
    ("mix",),
    (0, 1, 1),
    (2, 0, 1),
    ("mix",),
    ("attend",),
    (3, 1, 0),
    ("attend",),
    (2, 2, 0),
    ("attend",),
    (0, 0, 2),
    (4, 1, 0),
    ("attend",),
    ("project",),
    (1, 1, 1),
    ("up",),
    (1, 2, 1),
    (0, 2, 2),
    (3, 2, 0),
    ("up",),
    (1, 0, 2),
    ("up",),
    (2, 1, 1),
    (3, 0, 1),
    (4, 2, 0),
    ("up",),
    ("down",),
    (4, 0, 1),
    ("down",),
)
BACKWARD_PERIOD = (
    (0, 0, -1),
    ("norm2",),
    (2, 1, -1),
    ("down",),
    ("down",),
    (1, 0, -1),
    (0, 2, 0),
    ("gelu",),
    ("gelu",),
    ("up",),
    (3, 1, -1),
    (1, 2, 0),
    (4, 0, -2),
    ("normed",),
    (2, 0, -1),
    ("norm1",),
    (0, 1, 0),
    ("attend",),
    ("attend",),
    (3, 0, -1),
    (3, 2, -1),
    (1, 1, 0),
    ("attend",),
    ("attend",),
    (2, 2, 0),
    ("mix",),
    ("mix",),
    ("input",),
    (4, 2, -1),
    (4, 1, -1),
)
BACKWARD_END = (
    (0, 0, 3),
    (2, 1, 3),
    (1, 0, 3),
    (3, 1, 3),
    ("embed",),
    (4, 0, 2),
    (0, 3, 0),
    (2, 0, 3),
    (1, 3, 0),
    (3, 0, 3),
    (2, 3, 0),
    (3, 2, 3),
    (4, 2, 3),
    (4, 1, 3),
    (4, 0, 3),
    (3, 3, 0),
    (4, 3, 0),
)


def copies_start(copies):
    for copy in copies:
        copy.start()


def copies_wait(copies):
    for copy in copies:
        copy.wait()


class Spread:
    def __init__(self, at, out, send, recv, half=ZS // 2):
        self.at, self.out, self.send, self.recv = at, out, send, recv
        nb = at.bs - 1
        self.slot_z = 0
        self.slot_b1 = ZS - 1
        self.slot_x1 = self.slot_b1 + nb
        self.slot_x2 = self.slot_x1 + 1
        self.slot_b2 = self.slot_x2 + 1
        self.slot_c = self.slot_b2 + nb
        self.half = half

    @staticmethod
    def slots(bs):
        return ZS - 1 + 2 * (bs - 1) + 3

    def copy(self, region, slot, peer):
        return remote(region, region, self.send.at[slot], self.recv.at[slot], peer)

    def copies(self, stage, back):
        at, out, half = self.at, self.out, self.half
        rest = pl.ds(half, ZS - half)
        x_block = at.c * 2 + 1 - at.x if back else at.block
        if stage == 0:
            return [
                self.copy(
                    out.at[at.block, at.z_at(ZS - k) if back else at.z, at.b],
                    self.slot_z + k - 1,
                    at.z_peer(k),
                )
                for k in range(1, ZS)
            ]
        if stage == 3:
            core = 1 - at.c if back else at.c
            return [self.copy(out.at[pl.ds(core * 2, 2)], self.slot_c, at.core_peer)]
        copies = []
        for k in range(1, at.bs):
            b = at.b_at(at.bs - k) if back else at.b
            if stage == 1:
                region, slot = out.at[at.block, pl.ds(0, half), b], self.slot_b1
            else:
                region, slot = out.at[pl.ds(at.c * 2, 2), rest, b], self.slot_b2
            copies.append(self.copy(region, slot + k - 1, at.b_peer(k)))
        if stage == 1:
            region, slot = out.at[x_block, rest, at.b], self.slot_x1
        else:
            region, slot = out.at[x_block, pl.ds(0, half)], self.slot_x2
        copies.append(self.copy(region, slot, at.x_peer))
        return copies

    def start(self, stage):
        copies_start(self.copies(stage, False))

    def land(self, stage):
        for copy in self.copies(stage, True):
            copy.wait_recv()
        for copy in self.copies(stage, False):
            copy.wait_send()

    def move(self, stage):
        self.land(stage)
        self.start(stage + 1)


class SpreadCross(Spread):
    @staticmethod
    def slots(bs):
        return 2 * bs + 2 * ZS - 1

    def copies(self, stage, back):
        at, out = self.at, self.out
        rows = out.shape[-2]
        cut = rows // 32 * 16
        some, rest = pl.ds(0, cut), pl.ds(cut, rows - cut)
        core = 1 - at.c if back else at.c
        if stage == 3:
            return [self.copy(out.at[pl.ds(core * 2, 2)], 2 * at.bs + 2 * ZS - 2, at.core_peer)]
        both = pl.ds(at.c * 2, 2)
        x_block = at.c * 2 + 1 - at.x if back else at.block
        copies = []
        if stage == 1:
            for k in range(1, ZS):
                z = at.z_at(ZS - k) if back else at.z
                copies.append(self.copy(out.at[both, z, at.b, some], at.bs + k - 1, at.z_peer(k)))
                slot = at.bs + ZS + k - 2
                copies.append(self.copy(out.at[at.block, z, :, rest], slot, at.z_peer(k)))
            return copies
        base = 0 if stage == 0 else at.bs + 2 * ZS - 2
        for k in range(1, at.bs):
            b = at.b_at(at.bs - k) if back else at.b
            region = out.at[at.block, at.z, b, rest] if stage == 0 else out.at[both, :, b, some]
            copies.append(self.copy(region, base + k, at.b_peer(k)))
        if stage == 0:
            region = out.at[x_block, at.z, at.b, some]
        else:
            region = out.at[x_block, :, :, rest]
        copies.append(self.copy(region, base, at.x_peer))
        return copies


class Fold:
    def __init__(self, at, grads, total, landing, bufs, final, send, recv, credit, half):
        self.at, self.grads, self.total = at, grads, total
        self.landing, self.bufs, self.final = landing, bufs, final
        self.send, self.recv, self.credit = send, recv, credit
        self.half = half
        nb = at.bs - 1
        self.slot_x1 = 1
        self.slot_b1 = 2
        self.slot_x2 = 2 + nb
        self.slot_b2 = 3 + nb
        self.slot_z = 3 + 2 * nb

    @staticmethod
    def slots(bs):
        return 3 + 2 * (bs - 1) + ZS - 1

    @staticmethod
    def buffers(bs, rows, half):
        nb = max(bs - 1, 1)
        rest = ZS - half
        return [
            (half, bs, rows, LANES),
            (nb, 2, rest, rows, LANES),
            (rest, rows, LANES),
            (nb, half, rows, LANES),
            (ZS - 1, rows, LANES),
        ]

    def core_parts(self):
        other = self.grads.at[pl.ds((1 - self.at.c) * 2, 2)]
        return [(other, self.landing, 0, self.at.core_peer, self.at.core_peer)]

    def parts(self, stage):
        at, half, total, bufs = self.at, self.half, self.total, self.bufs
        if stage == 0:
            return self.core_parts()
        if stage == 3:
            return [
                (
                    total.at[at.x, at.z_at(k), at.b],
                    bufs[4].at[k - 1],
                    self.slot_z + k - 1,
                    at.z_peer(k),
                    at.z_peer(ZS - k),
                )
                for k in range(1, ZS)
            ]
        rest = pl.ds(half, ZS - half)
        found = []
        for k in range(1, at.bs):
            if stage == 1:
                src, buf, slot = total.at[:, rest, at.b_at(k)], bufs[1], self.slot_b1
            else:
                src, buf, slot = total.at[at.x, pl.ds(0, half), at.b_at(k)], bufs[3], self.slot_b2
            found.append((src, buf.at[k - 1], slot + k - 1, at.b_peer(k), at.b_peer(at.bs - k)))
        if stage == 1:
            src, buf, slot = total.at[1 - at.x, pl.ds(0, half)], bufs[0], self.slot_x1
        else:
            src, buf, slot = total.at[1 - at.x, rest, at.b], bufs[2], self.slot_x2
        found.append((src, buf, slot, at.x_peer, at.x_peer))
        return found

    def start(self, stage, again):
        for src, buf, slot, to, _ in self.parts(stage):
            if again is not False:

                @pl.when(again)
                def _():
                    pl.semaphore_wait(self.credit.at[slot], 1)

            remote(src, buf, self.send.at[slot], self.recv.at[slot], to).start()

    def land(self, stage, more):
        parts = self.parts(stage)
        for src, buf, slot, to, _ in parts:
            remote(src, buf, self.send.at[slot], self.recv.at[slot], to).wait()
        self.add(stage)
        if more is not False:

            @pl.when(more)
            def _():
                for _, _, slot, _, origin in parts:
                    pl.semaphore_signal(
                        self.credit.at[slot], inc=1, device_id=origin, device_id_type=MESH
                    )

    def add_core(self):
        at, bs, total = self.at, self.at.bs, self.total

        @pl.loop(0, 2 * ZS * bs)
        def _(i):
            z, b = i // bs % ZS, i % bs
            x = i // (ZS * bs)
            total[x, z, b] = self.grads[at.c * 2 + x, z, b] + self.landing[x, z, b]

    def add(self, stage):
        at, half, bs = self.at, self.half, self.at.bs
        total, bufs = self.total, self.bufs
        rest = ZS - half
        if stage == 0:
            self.add_core()
        elif stage == 1:

            @pl.loop(0, half * bs)
            def _(i):
                z, b = i // bs, i % bs
                total[at.x, z, b] = total[at.x, z, b] + bufs[0][z, b]

            @pl.loop(0, 2 * rest)
            def _(i):
                x, z = i // rest, i % rest
                for k in range(bs - 1):
                    total[x, half + z, at.b] = total[x, half + z, at.b] + bufs[1][k, x, z]

        elif stage == 2:

            @pl.loop(0, rest)
            def _(z):
                total[at.x, half + z, at.b] = total[at.x, half + z, at.b] + bufs[2][z]

            @pl.loop(0, half)
            def _(z):
                for k in range(bs - 1):
                    total[at.x, z, at.b] = total[at.x, z, at.b] + bufs[3][k, z]

        else:
            self.finish([bufs[4][k] for k in range(ZS - 1)])

    def finish(self, pieces):
        at = self.at
        done = self.total[at.x, at.z, at.b].astype(jnp.float32)
        for piece in pieces:
            done = done + piece.astype(jnp.float32)
        self.final[...] = done.astype(self.final.dtype)

    def move(self, stage, again, more):
        self.land(stage, more)
        self.start(stage + 1, again)


class FoldCross(Fold):
    @staticmethod
    def slots(bs):
        return 2 * bs + 2 * ZS - 1

    @staticmethod
    def buffers(bs, rows, half):
        nb = max(bs - 1, 1)
        cut = rows // 32 * 16
        rest = rows - cut
        return [
            (nb, 2, ZS, cut, LANES),
            (ZS, bs, rest, LANES),
            (ZS - 1, 2, cut, LANES),
            (ZS - 1, bs, rest, LANES),
            (cut, LANES),
            (nb, rest, LANES),
        ]

    def cuts(self):
        rows = self.total.shape[-2]
        cut = rows // 32 * 16
        return pl.ds(0, cut), pl.ds(cut, rows - cut)

    def parts(self, stage):
        at, total, bufs = self.at, self.total, self.bufs
        if stage == 0:
            return self.core_parts()
        some, rest = self.cuts()
        found = []
        if stage == 2:
            for k in range(1, ZS):
                pair = (at.z_peer(k), at.z_peer(ZS - k))
                z = at.z_at(k)
                found.append((total.at[:, z, at.b, some], bufs[2].at[k - 1], at.bs + k, *pair))
                slot = at.bs + ZS + k - 1
                found.append((total.at[at.x, z, :, rest], bufs[3].at[k - 1], slot, *pair))
            return found
        base = 1 if stage == 1 else at.bs + 2 * ZS - 1
        for k in range(1, at.bs):
            pair = (at.b_peer(k), at.b_peer(at.bs - k))
            if stage == 1:
                src, buf = total.at[:, :, at.b_at(k), some], bufs[0].at[k - 1]
            else:
                src, buf = total.at[at.x, at.z, at.b_at(k), rest], bufs[5].at[k - 1]
            found.append((src, buf, base + k, *pair))
        if stage == 1:
            src, buf = total.at[1 - at.x, :, :, rest], bufs[1]
        else:
            src, buf = total.at[1 - at.x, at.z, at.b, some], bufs[4]
        found.append((src, buf, base, at.x_peer, at.x_peer))
        return found

    def add(self, stage):
        at, bs = self.at, self.at.bs
        total, bufs = self.total, self.bufs
        some, rest = self.cuts()
        if stage == 0:
            self.add_core()
        elif stage == 1:

            @pl.loop(0, 2 * ZS)
            def _(i):
                x, z = i // ZS, i % ZS
                for k in range(bs - 1):
                    total[x, z, at.b, some] = total[x, z, at.b, some] + bufs[0][k, x, z]

            @pl.loop(0, ZS * bs)
            def _(i):
                z, b = i // bs, i % bs
                total[at.x, z, b, rest] = total[at.x, z, b, rest] + bufs[1][z, b]

        elif stage == 2:
            for x in range(2):
                for k in range(ZS - 1):
                    total[x, at.z, at.b, some] = total[x, at.z, at.b, some] + bufs[2][k, x]

            @pl.loop(0, bs)
            def _(b):
                for k in range(ZS - 1):
                    total[at.x, at.z, b, rest] = total[at.x, at.z, b, rest] + bufs[3][k, b]

        else:
            total[at.x, at.z, at.b, some] = total[at.x, at.z, at.b, some] + bufs[4][...]
            for k in range(bs - 1):
                total[at.x, at.z, at.b, rest] = total[at.x, at.z, at.b, rest] + bufs[5][k]
            self.final[...] = total[at.x, at.z, at.b]


HALF = 256
WIDE = 512
QKV_TILE = 768
VEC_ROWS = 16


def dot_nt(a, b):
    return lax.dot_general(a, b, (((1,), (1,)), ((), ())), preferred_element_type=jnp.float32)


def dot_nn(a, b):
    return lax.dot_general(a, b, (((1,), (0,)), ((), ())), preferred_element_type=jnp.float32)


def dot_tn(a, b):
    return lax.dot_general(a, b, (((0,), (0,)), ((), ())), preferred_element_type=jnp.float32)


def aligned(index, unit):
    return pl.multiple_of(index, unit)


def rows_of(ref, bs, first, count, start, rows, blocks=range(SECT)):
    parts = []
    for i in range(count):
        d = first + i
        place = (d // bs, d % bs)
        parts.append(
            jnp.concatenate(
                [ref[(lb,) + place + (pl.ds(start, rows), slice(None))] for lb in blocks], axis=1
            )
        )
    return parts[0] if count == 1 else jnp.concatenate(parts, axis=0)


def put_rows(ref, bs, first, count, start, rows, value, block=0):
    value = value.astype(ref.dtype)
    for i in range(count):
        d = first + i
        place = (d // bs, d % bs)
        for lane in range(value.shape[1] // LANES):
            ref[(block + lane,) + place + (pl.ds(start, rows), slice(None))] = value[
                i * rows : (i + 1) * rows, lane * LANES : (lane + 1) * LANES
            ]


def vector_pieces(dps):
    n_gains, n_biases = 2 * WIDE // dps, 10 * WIDE // dps
    starts = [(0, 0), (0, 2), (1, 0), (1, 2), (2, 0), (2, 1), (2, 2), (2, 3), (3, 0), (3, 2)]
    pieces = []
    for d in range(dps):
        at = 0
        while at < n_gains + n_biases:
            if at < n_gains:
                index = d * n_gains + at
                row, column = (1, 3)[index // WIDE], WIDE + index % WIDE
                left = n_gains - at
            else:
                index = d * n_biases + at - n_gains
                row, part = starts[index // WIDE]
                column = part * WIDE + index % WIDE
                left = n_gains + n_biases - at
            size = min(left, LANES - at % LANES, LANES - column % LANES)
            pieces.append((d, at // WIDE, at % WIDE, row, column, size))
            at += size
    return pieces


def read_vectors(ref, table, bs, start):
    dps = ZS * bs
    tiles = {}
    for d, row, lane, to_row, to_lane, size in vector_pieces(dps):
        key = (d, lane // LANES)
        if key not in tiles:
            tile = ref[lane // LANES, d // bs, d % bs, start : start + VEC_ROWS, :]
            tiles[key] = tile.astype(jnp.float32)
        off = lane % LANES
        table[to_row : to_row + 1, to_lane : to_lane + size] = tiles[key][
            row : row + 1, off : off + size
        ]


def write_vectors(ref, table, bs, start):
    dps = ZS * bs
    found = {}
    for d, row, lane, to_row, to_lane, size in vector_pieces(dps):
        piece = table[to_row : to_row + 1, to_lane : to_lane + size]
        found.setdefault((d, lane // LANES), {}).setdefault(row, []).append(piece)
    row_id = lax.broadcasted_iota(jnp.int32, (VEC_ROWS, LANES), 0)
    for d in range(dps):
        for lb in range(SECT):
            tile = jnp.zeros((VEC_ROWS, LANES), jnp.float32)
            for row, pieces in found.get((d, lb), {}).items():
                have = sum(piece.shape[1] for piece in pieces)
                if have < LANES:
                    pieces = pieces + [jnp.zeros((1, LANES - have), jnp.float32)]
                line = pieces[0] if len(pieces) == 1 else jnp.concatenate(pieces, axis=1)
                tile = jnp.where(row_id == row, line, tile)
            ref[lb, d // bs, d % bs, start : start + VEC_ROWS, :] = tile.astype(ref.dtype)


def normalize(x):
    mean = jnp.mean(x, axis=1, keepdims=True)
    centred = x - mean
    scale = lax.rsqrt(jnp.mean(centred * centred, axis=1, keepdims=True) + NORM_EPS)
    return centred * scale, jnp.broadcast_to(scale, (x.shape[0], LANES))


def normalize_back(unit, scale, grad, gain):
    inner = grad * gain
    first = jnp.mean(inner, axis=1, keepdims=True)
    second = jnp.mean(inner * unit, axis=1, keepdims=True)
    out = jnp.concatenate([scale] * (WIDE // LANES), axis=1) * (inner - first - unit * second)
    return out, jnp.sum(grad * unit, axis=0, keepdims=True), jnp.sum(grad, axis=0, keepdims=True)


def gelu_pair(u):
    below = 0.5 + 0.5 * lax.erf(u * math.sqrt(0.5))
    bell = jnp.exp2((-0.5 * math.log2(math.e)) * (u * u))
    return u * below, below + u * (bell * (1.0 / math.sqrt(2.0 * math.pi)))


def head_masks(scale):
    lane = lax.broadcasted_iota(jnp.int32, (1, LANES), 1)
    first = jnp.where(lane < HEAD, scale, 0.0).astype(jnp.bfloat16)
    second = jnp.where(lane < HEAD, 0.0, scale).astype(jnp.bfloat16)
    return first, second


class Sizes:
    def __init__(self, dps):
        self.dps, self.bs = dps, dps // ZS
        self.qkv, self.out, self.up, self.down = (
            3 * WIDE // dps,
            WIDE // dps,
            4 * WIDE // dps,
            WIDE // dps,
        )
        self.att = self.qkv + VEC_ROWS
        self.dense = self.out + self.up
        self.wide = 4 * self.down


def qkv_rows(size, w, tile):
    count = QKV_TILE // size.qkv
    return rows_of(w, size.bs, tile * count, count, 0, size.qkv)


def out_rows(size, w):
    return rows_of(w, size.bs, 0, size.dps, 0, size.out)


def up_rows(size, w, tile):
    count = HALF // size.up
    return rows_of(w, size.bs, tile * count, count, size.out, size.up)


def forward_mix(size, w, table, h, mixed, piece):
    columns = slice(piece * QKV_TILE, (piece + 1) * QKV_TILE)
    mixed[:, columns] = (
        dot_nt(h[...], qkv_rows(size, w, piece)) + table[0:1, columns]
    ).astype(mixed.dtype)


def forward_attend(mixed, lse, attended, pair):
    lane = pair * LANES
    key_rows = mixed[:, WIDE + lane : WIDE + lane + LANES]
    values = mixed[:, 2 * WIDE + lane : 2 * WIDE + lane + LANES].T

    for part in range(2):
        rows = slice(part * HALF, (part + 1) * HALF)
        queries = mixed[rows, lane : lane + LANES]
        joined = []
        for head, mask in enumerate(head_masks(1.0 / math.sqrt(HEAD))):
            scores = dot_nt(key_rows, queries * mask)
            top = jnp.max(scores, axis=0, keepdims=True)
            probs = jnp.exp(scores - top)
            total = jnp.sum(probs, axis=0, keepdims=True)
            lse[2 * pair + head, :, rows] = top + jnp.log(total)
            probs = (probs * (1.0 / total)).astype(jnp.bfloat16)
            joined.append(dot_nn(values[head * HEAD : (head + 1) * HEAD], probs))
        joined = jnp.concatenate(joined, axis=0).T
        attended[rows, lane : lane + LANES] = joined.astype(attended.dtype)


def forward_project(size, w, table, h, attended, first, scale, normed):
    out = dot_nt(attended[...], out_rows(size, w))
    for part in range(2):
        rows = slice(part * HALF, (part + 1) * HALF)
        total = h[rows, :].astype(jnp.float32) + (out[rows] + table[1:2, 0:WIDE])
        unit, scale[rows, :] = normalize(total)
        first[rows, :] = unit
        normed[rows, :] = (
            unit * table[1:2, WIDE : 2 * WIDE] + table[1:2, 2 * WIDE : 3 * WIDE]
        ).astype(normed.dtype)


def forward_up(size, w, table, normed, slope, hidden, piece):
    for j in (2 * piece, 2 * piece + 1):
        columns = slice(j * HALF, (j + 1) * HALF)
        upper = dot_nt(normed[...], up_rows(size, w, j)) + table[2:3, columns]
        value, grad = gelu_pair(upper)
        hidden[:, columns] = value.astype(hidden.dtype)
        slope[:, columns] = grad.astype(slope.dtype)


def forward_down(size, w, table, normed, hidden, second, scale, h, piece):
    columns = slice(piece * HALF, (piece + 1) * HALF)
    count = size.dps // 2
    matrix = jnp.concatenate(
        [
            rows_of(w, size.bs, piece * count, count, j * size.down, size.down)
            for j in range(4)
        ],
        axis=1,
    )
    out = dot_nt(hidden[...], matrix)
    second[:, columns] = normed[:, columns].astype(jnp.float32) + (out + table[3:4, columns])
    if piece == 1:
        for part in range(2):
            rows = slice(part * HALF, (part + 1) * HALF)
            unit, scale[rows, :] = normalize(second[rows, :])
            second[rows, :] = unit
            h[rows, :] = (
                unit * table[3:4, WIDE : 2 * WIDE] + table[3:4, 2 * WIDE : 3 * WIDE]
            ).astype(h.dtype)


def backward_norm_two(table, dtable, dy, second, scale, dnormed, dlow, dlow_t):
    dtable[...] = jnp.zeros_like(dtable)
    for part in range(2):
        rows = slice(part * HALF, (part + 1) * HALF)
        grad, gain_sum, shift_sum = normalize_back(
            second[rows, :],
            scale[rows, :],
            dy[rows, :].astype(jnp.float32),
            table[3:4, WIDE : 2 * WIDE],
        )
        dnormed[rows, :] = grad
        dlow[rows, :] = grad.astype(dlow.dtype)
        dtable[3:4, 0:WIDE] += jnp.sum(grad, axis=0, keepdims=True)
        dtable[3:4, WIDE : 2 * WIDE] += gain_sum
        dtable[3:4, 2 * WIDE : 3 * WIDE] += shift_sum
    dlow_t[...] = dlow[...].T


def backward_down(size, grads, hidden, dlow_t, piece):
    @pl.loop(2 * piece, 2 * piece + 2)
    def _(i):
        start = aligned(i * size.down, 16)
        for half in range(2):
            columns = pl.ds(aligned(i * WIDE, WIDE) + half * HALF, HALF)
            value = dot_nn(dlow_t[...], hidden[:, columns])
            put_rows(grads, size.bs, 0, size.dps, start, size.down, value, 2 * half)


def backward_gelu(size, w, dtable, slope, dlow, dup, piece):
    @pl.loop(2 * piece, 2 * piece + 2)
    def _(i):
        start = aligned(i * size.down, 16)
        for half in range(2):
            columns = pl.ds(aligned(i * WIDE, WIDE) + half * HALF, HALF)
            blocks = (2 * half, 2 * half + 1)
            matrix = rows_of(w, size.bs, 0, size.dps, start, size.down, blocks)
            dupper = dot_nn(dlow[...], matrix) * slope[:, columns].astype(jnp.float32)
            dtable[2:3, columns] = jnp.sum(dupper, axis=0, keepdims=True)
            dup[:, columns] = dupper.astype(dup.dtype)


def backward_up(size, grads, normed, dup):
    count = HALF // size.up

    @pl.loop(0, 4)
    def _(i):
        for half in range(2):
            columns = pl.ds(aligned(i * WIDE, WIDE) + half * HALF, HALF)
            value = dot_tn(dup[:, columns], normed[...])
            first = (2 * i + half) * count
            put_rows(grads, size.bs, first, count, size.out, size.up, value)


def backward_normed(size, w, dnormed, dup):
    for half in range(2):
        columns = slice(half * HALF, (half + 1) * HALF)
        blocks = (2 * half, 2 * half + 1)
        matrix = rows_of(w, size.bs, 0, size.dps, size.out, size.up, blocks)
        dnormed[:, columns] = dnormed[:, columns] + dot_nn(dup[...], matrix)


def backward_norm_one(
    size, w, table, grads, dtable, first, scale, attended, dnormed, dlow, dlow_t, delta
):
    for part in range(2):
        rows = slice(part * HALF, (part + 1) * HALF)
        grad, gain_sum, shift_sum = normalize_back(
            first[rows, :], scale[rows, :], dnormed[rows, :], table[1:2, WIDE : 2 * WIDE]
        )
        dnormed[rows, :] = grad
        dlow[rows, :] = grad.astype(dlow.dtype)
        dtable[1:2, 0:WIDE] += jnp.sum(grad, axis=0, keepdims=True)
        dtable[1:2, WIDE : 2 * WIDE] += gain_sum
        dtable[1:2, 2 * WIDE : 3 * WIDE] += shift_sum
    dlow_t[...] = dlow[...].T
    for block in (0, 2):
        columns = slice(block * LANES, (block + 2) * LANES)
        value = dot_nn(dlow_t[...], attended[:, columns])
        put_rows(grads, size.bs, 0, size.dps, 0, size.out, value, block)
    grad = dot_nn(dlow[...], out_rows(size, w)).astype(dlow.dtype)
    dlow[...] = grad
    product = grad.astype(jnp.float32) * attended[...].astype(jnp.float32)
    high = product.astype(jnp.bfloat16)
    rest = (product - high.astype(jnp.float32)).astype(jnp.bfloat16)
    head = lax.broadcasted_iota(jnp.int32, delta.shape, 0)
    lane = lax.broadcasted_iota(jnp.int32, delta.shape, 1)
    inside = (lane >= head * HEAD) & (lane < (head + 1) * HEAD)
    inside = jnp.where(inside, 1.0, 0.0).astype(jnp.bfloat16)
    delta[...] = dot_nt(inside, high) + dot_nt(inside, rest)


def backward_attend(mixed, lse, delta, dtable, dlow, dmixed, pair):
    scale = 1.0 / math.sqrt(HEAD)
    lane = pair * LANES
    columns = slice(lane, lane + LANES)
    key_columns = slice(WIDE + lane, WIDE + lane + LANES)
    value_columns = slice(2 * WIDE + lane, 2 * WIDE + lane + LANES)
    key_rows = mixed[:, key_columns]
    keys_t = key_rows.T
    values = mixed[:, value_columns]
    dkeys = jnp.zeros((WIDE, LANES), jnp.float32)
    dvalues = jnp.zeros((WIDE, LANES), jnp.float32)
    for part in range(2):
        rows = slice(part * HALF, (part + 1) * HALF)
        queries = mixed[rows, columns]
        grad_out = dlow[rows, columns]
        dqueries = []
        for head in range(2):
            query = queries * head_masks(scale)[head]
            grad = grad_out * head_masks(1.0)[head]
            probs = jnp.exp(dot_nt(key_rows, query) - lse[2 * pair + head, :, rows])
            dprobs = dot_nt(values, grad)
            at = 2 * pair + head
            dscores = (probs * (dprobs - delta[at : at + 1, rows])).astype(jnp.bfloat16)
            dvalues = dvalues + dot_nn(probs.astype(jnp.bfloat16), grad)
            dkeys = dkeys + dot_nn(dscores, query)
            dqueries.append(dot_nn(keys_t[head * HEAD : (head + 1) * HEAD], dscores))
        dquery = jnp.concatenate(dqueries, axis=0).T * scale
        dtable[0:1, columns] += jnp.sum(dquery, axis=0, keepdims=True)
        dmixed[rows, columns] = dquery.astype(dmixed.dtype)
    dmixed[:, key_columns] = dkeys.astype(dmixed.dtype)
    dmixed[:, value_columns] = dvalues.astype(dmixed.dtype)
    dtable[0:1, value_columns] = jnp.sum(dvalues, axis=0, keepdims=True)


def backward_mix(size, grads, h, dmixed, piece):
    count = QKV_TILE // size.qkv
    grad = dmixed[:, piece * QKV_TILE : (piece + 1) * QKV_TILE]
    put_rows(grads, size.bs, piece * count, count, 0, size.qkv, dot_tn(grad, h[...]))


def backward_input(size, w, dnormed, dmixed, dy):
    for half in range(2):
        columns = slice(half * HALF, (half + 1) * HALF)
        blocks = (2 * half, 2 * half + 1)
        matrix = rows_of(w, size.bs, 0, size.dps, 0, size.qkv, blocks)
        dy[:, columns] = (dnormed[:, columns] + dot_nn(dmixed[...], matrix)).astype(dy.dtype)


WINDOW = 384


def group_rows(group):
    rows = lax.broadcasted_iota(jnp.int32, (16, LANES), 0)
    return jnp.where(rows == group, 1.0, 0.0).astype(jnp.bfloat16)


def pack_mix(piece, qkv, gains, biases):
    low = piece.dtype
    rows = qkv.shape[0]
    flat = jnp.concatenate([gains[...], biases[...]], axis=1)
    flat = jnp.concatenate([flat, jnp.zeros((1, 2 * WIDE - flat.shape[1]), flat.dtype)], axis=1)
    row_id = lax.broadcasted_iota(jnp.int32, (VEC_ROWS, LANES), 0)
    for lb in range(SECT):
        lane = lb * LANES
        piece[lb, :rows] = qkv[:, lane : lane + LANES].astype(low)
        tile = jnp.where(row_id == 0, flat[:, lane : lane + LANES], 0.0)
        lane += WIDE
        tile = jnp.where(row_id == 1, flat[:, lane : lane + LANES], tile)
        piece[lb, rows:] = tile.astype(low)


def pack_up(piece, out, up):
    rows = out.shape[0]
    for lb in range(SECT):
        lanes = slice(lb * LANES, (lb + 1) * LANES)
        piece[lb, :rows] = out[:, lanes].astype(piece.dtype)
        piece[lb, rows:] = up[:, lanes].astype(piece.dtype)


def pack_down(piece, down):
    rows = down.shape[0]
    for lb in range(SECT):
        for j in range(4):
            start = j * WIDE + lb * LANES
            piece[lb, j * rows : (j + 1) * rows] = down[:, start : start + LANES].astype(piece.dtype)


def pack_embedding(piece, weight, shift, square):
    n = weight.shape[0]
    square[...] = jnp.zeros_like(square)
    square[:GROUPS, :n] = shift[...]

    def ending(part, width):
        return jnp.concatenate([jnp.zeros((n, width - part.shape[1]), part.dtype), part], axis=1)

    parts = [
        square[...].T[:n],
        ending(weight[:, L1 + L2 :], 3 * LANES),
        ending(weight[:, L1 : L1 + L2], 2 * LANES),
        ending(weight[:, :L1], 2 * LANES),
    ]
    columns = jnp.concatenate(parts, axis=1).astype(piece.dtype)
    for lb in range(SECT):
        for part in range(2):
            start = part * WIDE + lb * LANES
            piece[lb, part * n : (part + 1) * n] = columns[:, start : start + LANES]


def expand(series, group, x):
    empty = jnp.zeros((WINDOW - series.shape[0], series.shape[1]), series.dtype)
    x[:, :WINDOW] = jnp.concatenate([empty, series[...]], axis=0).T
    lane = lax.broadcasted_iota(jnp.int32, (x.shape[0], LANES), 1)
    x[:, WINDOW:] = jnp.where(lane == group, 1.0, 0.0).astype(x.dtype)


def embed(size, emb, pick, x, wsel, h):
    rows = WIDE // size.dps
    first = rows_of(emb, size.bs, 0, size.dps, 0, rows)
    second = rows_of(emb, size.bs, 0, size.dps, rows, rows)
    long, middle, short = (pick[g : g + 1, :] for g in (2, 1, 0))
    wide = jnp.concatenate(
        [
            first[:, LANES : 2 * LANES] * long,
            first[:, 2 * LANES : 3 * LANES] * long + second[:, :LANES] * middle,
            first[:, 3 * LANES :] * long
            + second[:, LANES : 2 * LANES] * middle
            + second[:, 3 * LANES :] * short,
        ],
        axis=1,
    )
    wsel[...] = wide.T
    matrix = jnp.concatenate([wide, first[:, :LANES]], axis=1)
    h[...] = dot_nt(x[...], matrix).astype(h.dtype)


def embed_back(size, pick, x, wsel, dh, grads, series_grad):
    history = series_grad.shape[0]
    series_grad[...] = dot_nt(wsel[...], dh[...])[WINDOW - history :]
    sums = dot_tn(dh[...], x[...])
    long, middle, short = (pick[g : g + 1, :].astype(jnp.float32) for g in (2, 1, 0))
    parts = [sums[:, i * LANES : (i + 1) * LANES] for i in range(4)]
    parts = [
        parts[3],
        parts[0] * long,
        parts[1] * long,
        parts[2] * long,
        parts[1] * middle,
        parts[2] * middle,
        jnp.zeros_like(parts[0]),
        parts[2] * short,
    ]
    rows = WIDE // (SECT * size.dps)
    for pipe in range(SECT):
        block = (pipe % 2) * 2 + pipe // 2
        for dp in range(size.dps):
            start = (pipe * size.dps + dp) * rows
            piece = jnp.concatenate([part[start : start + rows] for part in parts], axis=0)
            grads[block, dp // size.bs, dp % size.bs] = piece.astype(grads.dtype)


def saved_shapes():
    low, wide = jnp.bfloat16, jnp.float32
    return [
        ((WIDE, WIDE), low),
        ((WIDE, 3 * WIDE), low),
        ((2 * SECT, 1, WIDE), wide),
        ((WIDE, WIDE), low),
        ((WIDE, WIDE), wide),
        ((WIDE, WIDE), low),
        ((WIDE, 4 * WIDE), low),
        ((WIDE, 4 * WIDE), low),
        ((WIDE, WIDE), wide),
        ((SECT, 4 * WIDE), wide),
        ((WIDE, LANES), wide),
        ((WIDE, LANES), wide),
    ]


def chunk_shape(size, rows):
    return (SECT, ZS, size.bs, rows, LANES)


HALVES = (2, 2, 2, 2)
CROSS = (2,)


def follow(plan, section, act, compute):
    seen = {}
    for step in plan:
        if len(step) == 1:
            piece = seen.get(step[0], 0)
            seen[step[0]] = piece + 1
            compute(step[0], piece)
            continue
        op, kind, offset = step
        where = section + offset
        if isinstance(where, int):
            if 0 <= where < SECT:
                act(op, kind, where)
        elif offset == 0:
            act(op, kind, where)
        else:
            inside = where < SECT if offset > 0 else where >= 0

            @pl.when(inside)
            def _():
                act(op, kind, where)


def forward_kernel(dps, groups, *refs):
    size = Sizes(dps)
    given, refs = refs[:9], refs[9:]
    out, copies_out, wsel, x, refs = refs[0], refs[1:4], refs[4], refs[5], refs[6:]
    kept, local, refs = refs[:12], refs[12:24], refs[24:]
    wholes, refs = refs[:4], refs[4:]
    pieces, held, refs = refs[:4], refs[4:13], refs[13:]
    emb_rows, pick, refs = refs[0], refs[1], refs[2:]
    given_sem, out_sem, kept_sem, own_sem, p_send, p_recv, send, recv = refs
    h, mixed, lse, attended, first, normed, slope, hidden, second, table, scale_1, scale_2 = local
    at = Place(dps)

    own = [
        pltpu.make_async_copy(
            pieces[kind].at[at.block],
            wholes[kind].at[at.pipe, at.block, at.z, at.b]
            if kind < EMB
            else wholes[kind].at[at.block, at.z, at.b],
            own_sem.at[kind],
        )
        for kind in range(4)
    ]
    def split(kind, back):
        copies = []
        for k in range(1, SECT):
            if back:
                region = wholes[kind].at[at.pipe_at(SECT - k), at.block, at.z, at.b]
                src = region
            else:
                block = at.block_of(at.pipe_at(k))
                region = wholes[kind].at[at.pipe, block, at.z, at.b]
                src = pieces[kind].at[block]
            sems = p_send.at[kind, k - 1], p_recv.at[kind, k - 1]
            copies.append(remote(src, region, *sems, (at.pipe_at(k), at.dp)))
        return copies

    def chunk(kind, section):
        if kind == EMB:
            return Spread(at, wholes[kind], send.at[3 * SECT], recv.at[3 * SECT])
        number = 3 * section + kind
        sort = SpreadCross if kind in CROSS else Spread
        return sort(at, wholes[kind].at[section], send.at[number], recv.at[number], HALVES[kind])

    def keep(kind, section):
        src, dst = wholes[kind].at[section], copies_out[kind].at[section]
        return pltpu.make_async_copy(src, dst, out_sem.at[kind, section])

    arrived = []

    def act(op, kind, section):
        if op == 0:
            if kind not in arrived:
                arrived.append(kind)
                own[kind].wait()
                if kind == EMB:
                    chunk(kind, section).start(0)
                    return
                for copy in split(kind, True):
                    copy.wait_recv()
                for copy in split(kind, False):
                    copy.wait_send()
                if kind == 0:
                    copies_start(split(1, False))
                    copies_start(split(2, False))
            chunk(kind, section).start(0)
        elif op < 4:
            chunk(kind, section).move(op - 1)
        else:
            chunk(kind, section).land(3)
            if kind != EMB:
                keep(kind, section).start()

    def saves(section, early):
        which = (1, 2, 3, 4, 5, 9, 10) if early else (6, 7, 8, 11)
        return [
            pltpu.make_async_copy(local[i], kept[i].at[section], kept_sem.at[i]) for i in which
        ]

    series, embed_weight, embed_bias, qkv, out_w, up_w, down_w, gains, biases = held
    gets = copies_of(zip(given, held), given_sem)
    for i in (3, 7, 8, 1, 2, 4, 5, 6, 0):
        gets[i].start()
    pick[...] = group_rows(groups[0])
    at.greet()
    copies_wait([gets[i] for i in (3, 7, 8)])
    pack_mix(pieces[0], qkv, gains, biases)
    own[0].start()
    at.met()
    copies_start(split(0, False))
    copies_wait(gets[1:3])
    pack_embedding(pieces[EMB], embed_weight, embed_bias, emb_rows)
    own[EMB].start()
    copies_wait(gets[4:7])
    pack_up(pieces[1], out_w, up_w)
    own[1].start()
    pack_down(pieces[2], down_w)
    own[2].start()
    table[...] = jnp.zeros_like(table)
    gets[0].wait()
    expand(series, groups[0], x)

    def before(name, piece):
        embed(size, wholes[EMB], pick, x, wsel, h)

    follow(FORWARD_START, 0, act, before)

    @pl.loop(0, SECT)
    def _(section):
        att, up, down = (ref.at[section] for ref in wholes[:3])
        keep_h = pltpu.make_async_copy(h, kept[0].at[section], kept_sem.at[0])

        def compute(name, piece):
            if name == "mix":
                if piece == 0:

                    @pl.when(section > 0)
                    def _():
                        copies_wait(saves(section - 1, True))

                    keep_h.start()
                    read_vectors(att, table, size.bs, size.qkv)
                forward_mix(size, att, table, h, mixed, piece)
            elif name == "attend":
                forward_attend(mixed, lse, attended, piece)
            elif name == "project":
                forward_project(size, up, table, h, attended, first, scale_1, normed)
                copies_start(saves(section, True))
            elif name == "up":
                if piece == 0:

                    @pl.when(section > 0)
                    def _():
                        copies_wait(saves(section - 1, False))

                forward_up(size, up, table, normed, slope, hidden, piece)
            else:
                if piece == 0:
                    keep_h.wait()
                forward_down(size, down, table, normed, hidden, second, scale_2, h, piece)
                if piece == 1:
                    copies_start(saves(section, False))

        follow(FORWARD_PERIOD, section, act, compute)

    out[...] = h[...]
    copies_wait(saves(SECT - 1, True))
    copies_wait(saves(SECT - 1, False))
    for kind in range(3):
        copies_wait([keep(kind, section) for section in range(SECT)])


def copies_of(pairs, sems):
    return [pltpu.make_async_copy(src, dst, sems.at[i]) for i, (src, dst) in enumerate(pairs)]


def forward_all(groups, given, dps):
    size = Sizes(dps)
    low, wide = jnp.bfloat16, jnp.float32
    shapes = saved_shapes()
    rows = (size.att, size.dense, size.wide, 2 * WIDE // dps)
    chunks = [chunk_shape(size, count) for count in rows]
    anywhere = pl.BlockSpec(memory_space=pl.ANY)
    inside = pl.BlockSpec(memory_space=pltpu.VMEM)
    outs = [((WIDE, WIDE), low)]
    outs += [((SECT,) + shape, low) for shape in chunks[:3]]
    outs += [((WINDOW, WIDE), low), ((WIDE, WIDE), low)]
    outs += [((SECT,) + shape, dtype) for shape, dtype in shapes]
    scratch = shapes + [((SECT,) + shape, low) for shape in chunks[:3]] + [(chunks[3], low)]
    scratch += [((SECT, count, LANES), low) for count in rows]
    scratch += [(array.shape, array.dtype) for array in given]
    scratch += [((LANES, LANES), wide), ((16, LANES), low)]
    slots = max(Spread.slots(size.bs), SpreadCross.slots(size.bs))
    dma = pltpu.SemaphoreType.DMA
    return pl.pallas_call(
        partial(forward_kernel, dps),
        out_shape=[jax.ShapeDtypeStruct(shape, dtype) for shape, dtype in outs],
        in_specs=[pl.BlockSpec(memory_space=pltpu.SMEM)] + [anywhere] * len(given),
        out_specs=[inside] + [anywhere] * 3 + [inside] * 2 + [anywhere] * len(shapes),
        scratch_shapes=[pltpu.VMEM(shape, dtype) for shape, dtype in scratch]
        + [
            dma((len(given),)),
            dma((3, SECT)),
            dma((len(shapes),)),
            dma((4,)),
            dma((3, SECT - 1)),
            dma((3, SECT - 1)),
            dma((1 + 3 * SECT, slots)),
            dma((1 + 3 * SECT, slots)),
        ],
        compiler_params=pltpu.CompilerParams(
            collective_id=0, has_side_effects=True, vmem_limit_bytes=60 * 1024 * 1024
        ),
        name="gather_forward",
    )(groups, *given)


def backward_kernel(dps, groups, att, up, down, cotangent, x_in, wsel_in, *refs):
    size = Sizes(dps)
    kept, refs = refs[:12], refs[12:]
    series_grad, outs, refs = refs[0], refs[1:5], refs[5:]
    local, refs = refs[:11], refs[11:]
    tables, w_att, w_up, w_down, dtable, dy, dnormed, dlow, dlow_t, dmixed, dup = refs[:11]
    x, wsel, pick, delta, refs = *refs[11:15], refs[15:]
    kinds = []
    for kind in range(4):
        count = 6 if kind in CROSS else 5
        kinds.append(refs[:4] + (refs[4 : 4 + count],))
        refs = refs[4 + count :]
    w_sem, kept_sem, table_sem, late_sem, out_sem, p_send, p_recv, send, recv, credit = refs
    h, mixed, lse, attended, first, normed, slope, hidden, second, scale_1, scale_2 = local
    at = Place(dps)
    last = SECT - 1

    def weights(kind, section):
        src, dst = ((att, w_att), (up, w_up), (down, w_down))[kind]
        return pltpu.make_async_copy(src.at[section], dst, w_sem.at[kind])

    def loads(section, dense):
        which = (5, 6, 7, 8, 11) if dense else (0, 1, 2, 3, 4, 10)
        found = []
        for i in which:
            dst = local[i] if i < 9 else local[i - 1]
            found.append(pltpu.make_async_copy(kept[i].at[section], dst, kept_sem.at[i]))
        return found + [weights(kind, section) for kind in ((1, 2) if dense else (0,))]

    def chunk(kind, i):
        grads, totals, finals, landing, bufs = kinds[kind]
        sort = FoldCross if kind in CROSS else Fold
        refs = (grads, totals.at[i % 2], landing, bufs, finals.at[i])
        return sort(at, *refs, send.at[kind], recv.at[kind], credit.at[kind], HALVES[kind])

    def hand_over(kind, i):
        landing = outs[kind].at[at.block]
        final = kinds[kind][2].at[i]
        return (
            pltpu.make_async_copy(final, landing, out_sem.at[kind]),
            remote(final, landing, p_send.at[kind, i], p_recv.at[kind, at.pipe], (last - i, at.dp)),
        )

    def act(op, kind, i):
        again, more = (False, False) if kind == EMB else (i > 0, i < last)
        if op == 0:
            chunk(kind, i).start(0, again)
        elif op < 4:
            chunk(kind, i).move(op - 1, again, more)
        else:
            chunk(kind, i).land(3, more)
            if kind == EMB:
                outs[kind][...] = kinds[kind][2][0]
            else:
                here, away = hand_over(kind, i)

                @pl.when(at.pipe == last - i)
                def _():
                    here.start()

                @pl.when(at.pipe != last - i)
                def _():
                    away.start()

    copies_start(loads(last, True))
    get_tables = pltpu.make_async_copy(kept[9], tables, table_sem)
    get_tables.start()
    copies_start(loads(last, False))
    late = copies_of(((cotangent, dy), (x_in, x), (wsel_in, wsel)), late_sem)
    copies_start(late)
    pick[...] = group_rows(groups[0])
    at.greet()
    at.met()
    get_tables.wait()
    late[0].wait()

    @pl.loop(0, SECT)
    def _(i):
        section = last - i
        table = tables.at[section]

        def compute(name, piece):
            if name == "norm2":
                copies_wait(loads(section, True))
                backward_norm_two(table, dtable, dy, second, scale_2, dnormed, dlow, dlow_t)
            elif name == "down":
                backward_down(size, kinds[2][0], hidden, dlow_t, piece)
            elif name == "gelu":
                backward_gelu(size, w_down, dtable, slope, dlow, dup, piece)
            elif name == "up":
                backward_up(size, kinds[1][0], normed, dup)
            elif name == "normed":
                backward_normed(size, w_up, dnormed, dup)
            elif name == "norm1":
                copies_wait(loads(section, False))
                backward_norm_one(
                    size,
                    w_up,
                    table,
                    kinds[1][0],
                    dtable,
                    first,
                    scale_1,
                    attended,
                    dnormed,
                    dlow,
                    dlow_t,
                    delta,
                )

                @pl.when(section > 0)
                def _():
                    copies_start(loads(section - 1, True))

            elif name == "attend":
                backward_attend(mixed, lse, delta, dtable, dlow, dmixed, piece)
            elif name == "mix":
                backward_mix(size, kinds[0][0], h, dmixed, piece)
                if piece == 1:
                    write_vectors(kinds[0][0], dtable, size.bs, size.qkv)
            else:
                backward_input(size, w_att, dnormed, dmixed, dy)

                @pl.when(section > 0)
                def _():
                    copies_start(loads(section - 1, False))

        follow(BACKWARD_PERIOD, i, act, compute)

    def after(name, piece):
        copies_wait(late[1:])
        embed_back(size, pick, x, wsel, dy, kinds[EMB][0], series_grad)

    follow(BACKWARD_END, 0, act, after)

    for kind in range(3):
        for i in range(SECT):
            here, away = hand_over(kind, i)

            @pl.when(at.pipe == last - i)
            def _():
                here.wait()

            @pl.when(at.pipe != last - i)
            def _():
                away.wait_send()

        for k in range(1, SECT):
            other = at.pipe_at(k)
            landing = outs[kind].at[at.block_of(other)]
            sems = p_send.at[kind, 0], p_recv.at[kind, other]
            remote(landing, landing, *sems, (other, at.dp)).wait_recv()


def backward_all(groups, weights, cotangent, x, wsel, kept, history, dps):
    size = Sizes(dps)
    low, wide = jnp.bfloat16, jnp.float32
    anywhere = pl.BlockSpec(memory_space=pl.ANY)
    inside = pl.BlockSpec(memory_space=pltpu.VMEM)
    shapes = saved_shapes()
    rows_emb = 8 * WIDE // (SECT * dps)
    kind_rows = (size.att, size.dense, size.wide, rows_emb)
    scratch = shapes[:9] + shapes[10:] + [((SECT,) + shapes[9][0], wide)]
    scratch += [(chunk_shape(size, rows), low) for rows in kind_rows[:3]]
    scratch += [
        (shapes[9][0], wide),
        ((WIDE, WIDE), low),
        ((WIDE, WIDE), wide),
        ((WIDE, WIDE), low),
        ((WIDE, WIDE), low),
        ((WIDE, 3 * WIDE), low),
        ((WIDE, 4 * WIDE), low),
        ((WIDE, WIDE), low),
        ((WINDOW, WIDE), low),
        ((16, LANES), low),
        ((16, WIDE), wide),
    ]
    for kind, rows in enumerate(kind_rows):
        sets, results = (1, 1) if kind == EMB else (2, SECT)
        scratch += [
            (chunk_shape(size, rows), low),
            ((sets, 2, ZS, size.bs, rows, LANES), low),
            ((results, rows, LANES), low),
            ((2, ZS, size.bs, rows, LANES), low),
        ]
        sort = FoldCross if kind in CROSS else Fold
        scratch += [(shape, low) for shape in sort.buffers(size.bs, rows, HALVES[kind])]
    slots = max(Fold.slots(size.bs), FoldCross.slots(size.bs))
    dma = pltpu.SemaphoreType.DMA
    return pl.pallas_call(
        partial(backward_kernel, dps),
        out_shape=[jax.ShapeDtypeStruct((history, WIDE), wide)]
        + [jax.ShapeDtypeStruct((SECT, rows, LANES), low) for rows in kind_rows[:3]]
        + [jax.ShapeDtypeStruct((rows_emb, LANES), low)],
        in_specs=[pl.BlockSpec(memory_space=pltpu.SMEM)] + [anywhere] * (6 + len(kept)),
        out_specs=[inside] + [anywhere] * 3 + [inside],
        scratch_shapes=[pltpu.VMEM(shape, dtype) for shape, dtype in scratch]
        + [
            dma((3,)),
            dma((12,)),
            dma(()),
            dma((3,)),
            dma((3,)),
            dma((3, SECT)),
            dma((3, SECT)),
            dma((4, slots)),
            dma((4, slots)),
            pltpu.SemaphoreType.REGULAR((4, slots)),
        ],
        compiler_params=pltpu.CompilerParams(
            collective_id=1, has_side_effects=True, vmem_limit_bytes=60 * 1024 * 1024
        ),
        name="backward_fold",
    )(groups, *weights, cotangent, x, wsel, *kept)


def finish_kernel(dps, n_gains, n_biases, *refs):
    size = Sizes(dps)
    given, refs = refs[:6], refs[6:]
    block_out, series_out, embed_w, embed_b, qkv, out, up_out, down_out, gains, biases = refs[:10]
    att, up, down, emb, sems = refs[10:]
    copies = copies_of(zip(given, (att, up, down, emb, block_out, series_out)), sems)
    copies_start(copies)
    copies_wait(copies[:4])
    for lb in range(SECT):
        lanes = slice(lb * LANES, (lb + 1) * LANES)
        qkv[:, lanes] = att[lb, : size.qkv].astype(jnp.float32)
        out[:, lanes] = up[lb, : size.out].astype(jnp.float32)
        up_out[:, lanes] = up[lb, size.out :].astype(jnp.float32)
        for j in range(4):
            rows = slice(j * size.down, (j + 1) * size.down)
            start = j * WIDE + lb * LANES
            down_out[:, start : start + LANES] = down[lb, rows].astype(jnp.float32)
    tiles = [att[lb, size.qkv :].astype(jnp.float32) for lb in range(SECT)]
    flat = jnp.concatenate([tile[row : row + 1] for row in range(2) for tile in tiles], axis=1)
    gains[...] = flat[:, :n_gains]
    biases[...] = flat[:, n_gains : n_gains + n_biases]
    rows = emb.shape[0] // 8
    packed = emb[...].astype(jnp.float32)
    packed = [packed[i * rows : (i + 1) * rows] for i in range(8)]
    square = jnp.concatenate([packed[0], jnp.zeros((LANES - rows, LANES), jnp.float32)], axis=0)
    embed_b[...] = square.T[:GROUPS, :rows]
    packed = jnp.concatenate(packed, axis=1)
    ends = ((1024, L1), (768, L2), (512, L3))
    embed_w[...] = jnp.concatenate([packed[:, end - span : end] for end, span in ends], axis=1)
    copies_wait(copies[4:])


def finish_all(sums, block, series, n_gains, n_biases, dps):
    size = Sizes(dps)
    wide = jnp.float32
    columns = WIDE // (SECT * dps)
    outs = [
        (block.shape, block.dtype),
        (series.shape, wide),
        ((columns, L1 + L2 + L3), wide),
        ((GROUPS, columns), wide),
        ((size.qkv, WIDE), wide),
        ((size.out, WIDE), wide),
        ((size.up, WIDE), wide),
        ((size.down, 4 * WIDE), wide),
        ((1, n_gains), wide),
        ((1, n_biases), wide),
    ]
    anywhere = pl.BlockSpec(memory_space=pl.ANY)
    inside = pl.BlockSpec(memory_space=pltpu.VMEM)
    return pl.pallas_call(
        partial(finish_kernel, dps, n_gains, n_biases),
        out_shape=[jax.ShapeDtypeStruct(shape, dtype) for shape, dtype in outs],
        in_specs=[anywhere] * 6,
        out_specs=[anywhere] * 2 + [inside] * 8,
        scratch_shapes=[pltpu.VMEM(array.shape, array.dtype) for array in sums]
        + [pltpu.SemaphoreType.DMA((6,))],
        compiler_params=pltpu.CompilerParams(vmem_limit_bytes=60 * 1024 * 1024),
        name="finish",
    )(*sums, block, series)


def per_device(
    series,
    groups,
    cotangent,
    embed_weight,
    embed_bias,
    qkv_weight,
    out_weight,
    up_weight,
    down_weight,
    gains,
    biases,
):
    dps = lax.axis_size("dp")
    given = (
        series[0],
        embed_weight.T,
        embed_bias,
        qkv_weight[0],
        out_weight[0],
        up_weight[0],
        down_weight[0],
        gains,
        biases,
    )
    block_output, att, up, down, wsel, x, *kept = forward_all(groups, given, dps)
    series_grad, *sums = backward_all(
        groups, (att, up, down), cotangent[0], x, wsel, kept, series.shape[1], dps
    )
    outs = finish_all(sums, block_output, series_grad, gains.shape[1], biases.shape[1], dps)
    block_output, series_grad, embed_w, embed_b, qkv, out, up, down, gain_sum, bias_sum = outs
    return (
        block_output[None],
        series_grad[None],
        embed_w.T,
        embed_b,
        qkv[None],
        out[None],
        up[None],
        down[None],
        gain_sum,
        bias_sum,
    )


def solution(mesh):
    return jax.shard_map(
        per_device,
        mesh=mesh,
        in_specs=(
            P(("pipe", "dp"), None, None),
            P(("pipe", "dp")),
            P(("pipe", "dp"), None, None),
            P(None, "dp"),
            P(None, "dp"),
            P("pipe", "dp", None),
            P("pipe", "dp", None),
            P("pipe", "dp", None),
            P("pipe", "dp", None),
            P("pipe", "dp"),
            P("pipe", "dp"),
        ),
        out_specs=(
            P(("pipe", "dp"), None, None),
            P(("pipe", "dp"), None, None),
            P(None, ("pipe", "dp")),
            P(None, ("pipe", "dp")),
            P("pipe", "dp", None),
            P("pipe", "dp", None),
            P("pipe", "dp", None),
            P("pipe", "dp", None),
            P("pipe", "dp"),
            P("pipe", "dp"),
        ),
        check_vma=False,
    )
```

```python
from functools import partial
import math

import jax
import jax.numpy as jnp
from jax import lax
from jax.experimental import pallas as pl
from jax.experimental.pallas import tpu as pltpu
from jax.sharding import PartitionSpec as P

HEAD = 64
L1 = 96
L2 = 192
L3 = 336
GROUPS = 3


NORM_EPS = 1e-05


MESH = pl.DeviceIdType.MESH
LANES = 128
ZS = 4
SECT = 4
EMB = 3


class Place:
    def __init__(self, dps):
        self.bs = dps // ZS
        pipe = lax.axis_index("pipe")
        dp = lax.axis_index("dp")
        self.pipe, self.dp = pipe, dp
        self.x, self.c = pipe // 2, pipe % 2
        self.z, self.b = dp // self.bs, dp % self.bs
        self.block = self.c * 2 + self.x
        self.x_peer = ((1 - self.x) * 2 + self.c, dp)
        self.core_peer = (self.x * 2 + 1 - self.c, dp)

    def block_of(self, pipe):
        return (pipe % 2) * 2 + pipe // 2

    def pipe_at(self, step):
        return (self.pipe + step) % SECT

    def z_at(self, step):
        return (self.z + step) % ZS

    def b_at(self, step):
        return (self.b + step) % self.bs

    def z_peer(self, step):
        return (self.pipe, self.z_at(step) * self.bs + self.b)

    def b_peer(self, step):
        return (self.pipe, self.z * self.bs + self.b_at(step))

    def greet(self):
        barrier = pltpu.get_barrier_semaphore()
        peers = [(self.pipe_at(k), self.dp) for k in range(1, SECT)]
        peers += [self.z_peer(k) for k in range(1, ZS)]
        peers += [self.b_peer(k) for k in range(1, self.bs)]
        for peer in peers:
            pl.semaphore_signal(barrier, inc=1, device_id=peer, device_id_type=MESH)

    def met(self):
        pl.semaphore_wait(pltpu.get_barrier_semaphore(), SECT + ZS + self.bs - 3)


def remote(src, dst, send, recv, peer):
    return pltpu.make_async_remote_copy(
        src_ref=src, dst_ref=dst, send_sem=send, recv_sem=recv, device_id=peer, device_id_type=MESH
    )


FORWARD_START = (
    (0, 3, 0),
    (0, 0, 0),
    (0, 2, 0),
    (1, 3, 0),
    (1, 0, 0),
    (0, 1, 0),
    (2, 3, 0),
    (2, 0, 0),
    (0, 0, 1),
    (1, 1, 0),
    (1, 2, 0),
    (3, 3, 0),
    (0, 2, 1),
    (1, 0, 1),
    (2, 1, 0),
    (4, 3, 0),
    (3, 0, 0),
    ("embed",),
    (4, 0, 0),
)
FORWARD_PERIOD = (
    ("mix",),
    (0, 1, 1),
    (2, 0, 1),
    ("mix",),
    ("attend",),
    (3, 1, 0),
    ("attend",),
    (2, 2, 0),
    ("attend",),
    (0, 0, 2),
    (4, 1, 0),
    ("attend",),
    ("project",),
    (1, 1, 1),
    ("up",),
    (1, 2, 1),
    (0, 2, 2),
    (3, 2, 0),
    ("up",),
    (1, 0, 2),
    ("up",),
    (2, 1, 1),
    (3, 0, 1),
    (4, 2, 0),
    ("up",),
    ("down",),
    (4, 0, 1),
    ("down",),
)
BACKWARD_PERIOD = (
    (0, 0, -1),
    ("norm2",),
    (2, 1, -1),
    ("down",),
    ("down",),
    (1, 0, -1),
    (0, 2, 0),
    ("gelu",),
    ("gelu",),
    ("up",),
    (3, 1, -1),
    (1, 2, 0),
    (4, 0, -2),
    ("normed",),
    (2, 0, -1),
    ("norm1",),
    (0, 1, 0),
    ("attend",),
    ("attend",),
    (3, 0, -1),
    (3, 2, -1),
    (1, 1, 0),
    ("attend",),
    ("attend",),
    (2, 2, 0),
    ("mix",),
    ("mix",),
    ("input",),
    (4, 2, -1),
    (4, 1, -1),
)
BACKWARD_END = (
    (0, 0, 3),
    (2, 1, 3),
    (1, 0, 3),
    (3, 1, 3),
    ("embed",),
    (4, 0, 2),
    (0, 3, 0),
    (2, 0, 3),
    (1, 3, 0),
    (3, 0, 3),
    (2, 3, 0),
    (3, 2, 3),
    (4, 2, 3),
    (4, 1, 3),
    (4, 0, 3),
    (3, 3, 0),
    (4, 3, 0),
)


def copies_start(copies):
    for copy in copies:
        copy.start()


def copies_wait(copies):
    for copy in copies:
        copy.wait()


class Spread:
    def __init__(self, at, out, send, recv, half=ZS // 2):
        self.at, self.out, self.send, self.recv = at, out, send, recv
        nb = at.bs - 1
        self.slot_z = 0
        self.slot_b1 = ZS - 1
        self.slot_x1 = self.slot_b1 + nb
        self.slot_x2 = self.slot_x1 + 1
        self.slot_b2 = self.slot_x2 + 1
        self.slot_c = self.slot_b2 + nb
        self.half = half

    @staticmethod
    def slots(bs):
        return ZS - 1 + 2 * (bs - 1) + 3

    def copy(self, region, slot, peer):
        return remote(region, region, self.send.at[slot], self.recv.at[slot], peer)

    def copies(self, stage, back):
        at, out, half = self.at, self.out, self.half
        rest = pl.ds(half, ZS - half)
        x_block = at.c * 2 + 1 - at.x if back else at.block
        if stage == 0:
            return [
                self.copy(
                    out.at[at.block, at.z_at(ZS - k) if back else at.z, at.b],
                    self.slot_z + k - 1,
                    at.z_peer(k),
                )
                for k in range(1, ZS)
            ]
        if stage == 3:
            core = 1 - at.c if back else at.c
            return [self.copy(out.at[pl.ds(core * 2, 2)], self.slot_c, at.core_peer)]
        copies = []
        for k in range(1, at.bs):
            b = at.b_at(at.bs - k) if back else at.b
            if stage == 1:
                region, slot = out.at[at.block, pl.ds(0, half), b], self.slot_b1
            else:
                region, slot = out.at[pl.ds(at.c * 2, 2), rest, b], self.slot_b2
            copies.append(self.copy(region, slot + k - 1, at.b_peer(k)))
        if stage == 1:
            region, slot = out.at[x_block, rest, at.b], self.slot_x1
        else:
            region, slot = out.at[x_block, pl.ds(0, half)], self.slot_x2
        copies.append(self.copy(region, slot, at.x_peer))
        return copies

    def start(self, stage):
        copies_start(self.copies(stage, False))

    def land(self, stage):
        for copy in self.copies(stage, True):
            copy.wait_recv()
        for copy in self.copies(stage, False):
            copy.wait_send()

    def move(self, stage):
        self.land(stage)
        self.start(stage + 1)


class SpreadCross(Spread):
    @staticmethod
    def slots(bs):
        return 2 * bs + 2 * ZS - 1

    def copies(self, stage, back):
        at, out = self.at, self.out
        rows = out.shape[-2]
        cut = rows // 32 * 16
        some, rest = pl.ds(0, cut), pl.ds(cut, rows - cut)
        core = 1 - at.c if back else at.c
        if stage == 3:
            return [self.copy(out.at[pl.ds(core * 2, 2)], 2 * at.bs + 2 * ZS - 2, at.core_peer)]
        both = pl.ds(at.c * 2, 2)
        x_block = at.c * 2 + 1 - at.x if back else at.block
        copies = []
        if stage == 1:
            for k in range(1, ZS):
                z = at.z_at(ZS - k) if back else at.z
                copies.append(self.copy(out.at[both, z, at.b, some], at.bs + k - 1, at.z_peer(k)))
                slot = at.bs + ZS + k - 2
                copies.append(self.copy(out.at[at.block, z, :, rest], slot, at.z_peer(k)))
            return copies
        base = 0 if stage == 0 else at.bs + 2 * ZS - 2
        for k in range(1, at.bs):
            b = at.b_at(at.bs - k) if back else at.b
            region = out.at[at.block, at.z, b, rest] if stage == 0 else out.at[both, :, b, some]
            copies.append(self.copy(region, base + k, at.b_peer(k)))
        if stage == 0:
            region = out.at[x_block, at.z, at.b, some]
        else:
            region = out.at[x_block, :, :, rest]
        copies.append(self.copy(region, base, at.x_peer))
        return copies


class Fold:
    def __init__(self, at, grads, total, landing, bufs, final, send, recv, credit, half):
        self.at, self.grads, self.total = at, grads, total
        self.landing, self.bufs, self.final = landing, bufs, final
        self.send, self.recv, self.credit = send, recv, credit
        self.half = half
        nb = at.bs - 1
        self.slot_x1 = 1
        self.slot_b1 = 2
        self.slot_x2 = 2 + nb
        self.slot_b2 = 3 + nb
        self.slot_z = 3 + 2 * nb

    @staticmethod
    def slots(bs):
        return 3 + 2 * (bs - 1) + ZS - 1

    @staticmethod
    def buffers(bs, rows, half):
        nb = max(bs - 1, 1)
        rest = ZS - half
        return [
            (half, bs, rows, LANES),
            (nb, 2, rest, rows, LANES),
            (rest, rows, LANES),
            (nb, half, rows, LANES),
            (ZS - 1, rows, LANES),
        ]

    def core_parts(self):
        other = self.grads.at[pl.ds((1 - self.at.c) * 2, 2)]
        return [(other, self.landing, 0, self.at.core_peer, self.at.core_peer)]

    def parts(self, stage):
        at, half, total, bufs = self.at, self.half, self.total, self.bufs
        if stage == 0:
            return self.core_parts()
        if stage == 3:
            return [
                (
                    total.at[at.x, at.z_at(k), at.b],
                    bufs[4].at[k - 1],
                    self.slot_z + k - 1,
                    at.z_peer(k),
                    at.z_peer(ZS - k),
                )
                for k in range(1, ZS)
            ]
        rest = pl.ds(half, ZS - half)
        found = []
        for k in range(1, at.bs):
            if stage == 1:
                src, buf, slot = total.at[:, rest, at.b_at(k)], bufs[1], self.slot_b1
            else:
                src, buf, slot = total.at[at.x, pl.ds(0, half), at.b_at(k)], bufs[3], self.slot_b2
            found.append((src, buf.at[k - 1], slot + k - 1, at.b_peer(k), at.b_peer(at.bs - k)))
        if stage == 1:
            src, buf, slot = total.at[1 - at.x, pl.ds(0, half)], bufs[0], self.slot_x1
        else:
            src, buf, slot = total.at[1 - at.x, rest, at.b], bufs[2], self.slot_x2
        found.append((src, buf, slot, at.x_peer, at.x_peer))
        return found

    def start(self, stage, again):
        for src, buf, slot, to, _ in self.parts(stage):
            if again is not False:

                @pl.when(again)
                def _():
                    pl.semaphore_wait(self.credit.at[slot], 1)

            remote(src, buf, self.send.at[slot], self.recv.at[slot], to).start()

    def land(self, stage, more):
        parts = self.parts(stage)
        for src, buf, slot, to, _ in parts:
            remote(src, buf, self.send.at[slot], self.recv.at[slot], to).wait()
        self.add(stage)
        if more is not False:

            @pl.when(more)
            def _():
                for _, _, slot, _, origin in parts:
                    pl.semaphore_signal(
                        self.credit.at[slot], inc=1, device_id=origin, device_id_type=MESH
                    )

    def add_core(self):
        at, bs, total = self.at, self.at.bs, self.total

        @pl.loop(0, 2 * ZS * bs)
        def _(i):
            z, b = i // bs % ZS, i % bs
            x = i // (ZS * bs)
            total[x, z, b] = self.grads[at.c * 2 + x, z, b] + self.landing[x, z, b]

    def add(self, stage):
        at, half, bs = self.at, self.half, self.at.bs
        total, bufs = self.total, self.bufs
        rest = ZS - half
        if stage == 0:
            self.add_core()
        elif stage == 1:

            @pl.loop(0, half * bs)
            def _(i):
                z, b = i // bs, i % bs
                total[at.x, z, b] = total[at.x, z, b] + bufs[0][z, b]

            @pl.loop(0, 2 * rest)
            def _(i):
                x, z = i // rest, i % rest
                for k in range(bs - 1):
                    total[x, half + z, at.b] = total[x, half + z, at.b] + bufs[1][k, x, z]

        elif stage == 2:

            @pl.loop(0, rest)
            def _(z):
                total[at.x, half + z, at.b] = total[at.x, half + z, at.b] + bufs[2][z]

            @pl.loop(0, half)
            def _(z):
                for k in range(bs - 1):
                    total[at.x, z, at.b] = total[at.x, z, at.b] + bufs[3][k, z]

        else:
            self.finish([bufs[4][k] for k in range(ZS - 1)])

    def finish(self, pieces):
        at = self.at
        done = self.total[at.x, at.z, at.b].astype(jnp.float32)
        for piece in pieces:
            done = done + piece.astype(jnp.float32)
        self.final[...] = done.astype(self.final.dtype)

    def move(self, stage, again, more):
        self.land(stage, more)
        self.start(stage + 1, again)


class FoldCross(Fold):
    @staticmethod
    def slots(bs):
        return 2 * bs + 2 * ZS - 1

    @staticmethod
    def buffers(bs, rows, half):
        nb = max(bs - 1, 1)
        cut = rows // 32 * 16
        rest = rows - cut
        return [
            (nb, 2, ZS, cut, LANES),
            (ZS, bs, rest, LANES),
            (ZS - 1, 2, cut, LANES),
            (ZS - 1, bs, rest, LANES),
            (cut, LANES),
            (nb, rest, LANES),
        ]

    def cuts(self):
        rows = self.total.shape[-2]
        cut = rows // 32 * 16
        return pl.ds(0, cut), pl.ds(cut, rows - cut)

    def parts(self, stage):
        at, total, bufs = self.at, self.total, self.bufs
        if stage == 0:
            return self.core_parts()
        some, rest = self.cuts()
        found = []
        if stage == 2:
            for k in range(1, ZS):
                pair = (at.z_peer(k), at.z_peer(ZS - k))
                z = at.z_at(k)
                found.append((total.at[:, z, at.b, some], bufs[2].at[k - 1], at.bs + k, *pair))
                slot = at.bs + ZS + k - 1
                found.append((total.at[at.x, z, :, rest], bufs[3].at[k - 1], slot, *pair))
            return found
        base = 1 if stage == 1 else at.bs + 2 * ZS - 1
        for k in range(1, at.bs):
            pair = (at.b_peer(k), at.b_peer(at.bs - k))
            if stage == 1:
                src, buf = total.at[:, :, at.b_at(k), some], bufs[0].at[k - 1]
            else:
                src, buf = total.at[at.x, at.z, at.b_at(k), rest], bufs[5].at[k - 1]
            found.append((src, buf, base + k, *pair))
        if stage == 1:
            src, buf = total.at[1 - at.x, :, :, rest], bufs[1]
        else:
            src, buf = total.at[1 - at.x, at.z, at.b, some], bufs[4]
        found.append((src, buf, base, at.x_peer, at.x_peer))
        return found

    def add(self, stage):
        at, bs = self.at, self.at.bs
        total, bufs = self.total, self.bufs
        some, rest = self.cuts()
        if stage == 0:
            self.add_core()
        elif stage == 1:

            @pl.loop(0, 2 * ZS)
            def _(i):
                x, z = i // ZS, i % ZS
                for k in range(bs - 1):
                    total[x, z, at.b, some] = total[x, z, at.b, some] + bufs[0][k, x, z]

            @pl.loop(0, ZS * bs)
            def _(i):
                z, b = i // bs, i % bs
                total[at.x, z, b, rest] = total[at.x, z, b, rest] + bufs[1][z, b]

        elif stage == 2:
            for x in range(2):
                for k in range(ZS - 1):
                    total[x, at.z, at.b, some] = total[x, at.z, at.b, some] + bufs[2][k, x]

            @pl.loop(0, bs)
            def _(b):
                for k in range(ZS - 1):
                    total[at.x, at.z, b, rest] = total[at.x, at.z, b, rest] + bufs[3][k, b]

        else:
            total[at.x, at.z, at.b, some] = total[at.x, at.z, at.b, some] + bufs[4][...]
            for k in range(bs - 1):
                total[at.x, at.z, at.b, rest] = total[at.x, at.z, at.b, rest] + bufs[5][k]
            self.final[...] = total[at.x, at.z, at.b]


HALF = 256
WIDE = 512
QKV_TILE = 768
VEC_ROWS = 16


def dot_nt(a, b):
    return lax.dot_general(a, b, (((1,), (1,)), ((), ())), preferred_element_type=jnp.float32)


def dot_nn(a, b):
    return lax.dot_general(a, b, (((1,), (0,)), ((), ())), preferred_element_type=jnp.float32)


def dot_tn(a, b):
    return lax.dot_general(a, b, (((0,), (0,)), ((), ())), preferred_element_type=jnp.float32)


def aligned(index, unit):
    return pl.multiple_of(index, unit)


def rows_of(ref, bs, first, count, start, rows, blocks=range(SECT)):
    parts = []
    for i in range(count):
        d = first + i
        place = (d // bs, d % bs)
        parts.append(
            jnp.concatenate(
                [ref[(lb,) + place + (pl.ds(start, rows), slice(None))] for lb in blocks], axis=1
            )
        )
    return parts[0] if count == 1 else jnp.concatenate(parts, axis=0)


def put_rows(ref, bs, first, count, start, rows, value, block=0):
    value = value.astype(ref.dtype)
    for i in range(count):
        d = first + i
        place = (d // bs, d % bs)
        for lane in range(value.shape[1] // LANES):
            ref[(block + lane,) + place + (pl.ds(start, rows), slice(None))] = value[
                i * rows : (i + 1) * rows, lane * LANES : (lane + 1) * LANES
            ]


def vector_pieces(dps):
    n_gains, n_biases = 2 * WIDE // dps, 10 * WIDE // dps
    starts = [(0, 0), (0, 2), (1, 0), (1, 2), (2, 0), (2, 1), (2, 2), (2, 3), (3, 0), (3, 2)]
    pieces = []
    for d in range(dps):
        at = 0
        while at < n_gains + n_biases:
            if at < n_gains:
                index = d * n_gains + at
                row, column = (1, 3)[index // WIDE], WIDE + index % WIDE
                left = n_gains - at
            else:
                index = d * n_biases + at - n_gains
                row, part = starts[index // WIDE]
                column = part * WIDE + index % WIDE
                left = n_gains + n_biases - at
            size = min(left, LANES - at % LANES, LANES - column % LANES)
            pieces.append((d, at // WIDE, at % WIDE, row, column, size))
            at += size
    return pieces


def read_vectors(ref, table, bs, start):
    dps = ZS * bs
    tiles = {}
    for d, row, lane, to_row, to_lane, size in vector_pieces(dps):
        key = (d, lane // LANES)
        if key not in tiles:
            tile = ref[lane // LANES, d // bs, d % bs, start : start + VEC_ROWS, :]
            tiles[key] = tile.astype(jnp.float32)
        off = lane % LANES
        table[to_row : to_row + 1, to_lane : to_lane + size] = tiles[key][
            row : row + 1, off : off + size
        ]


def write_vectors(ref, table, bs, start):
    dps = ZS * bs
    found = {}
    for d, row, lane, to_row, to_lane, size in vector_pieces(dps):
        piece = table[to_row : to_row + 1, to_lane : to_lane + size]
        found.setdefault((d, lane // LANES), {}).setdefault(row, []).append(piece)
    row_id = lax.broadcasted_iota(jnp.int32, (VEC_ROWS, LANES), 0)
    for d in range(dps):
        for lb in range(SECT):
            tile = jnp.zeros((VEC_ROWS, LANES), jnp.float32)
            for row, pieces in found.get((d, lb), {}).items():
                have = sum(piece.shape[1] for piece in pieces)
                if have < LANES:
                    pieces = pieces + [jnp.zeros((1, LANES - have), jnp.float32)]
                line = pieces[0] if len(pieces) == 1 else jnp.concatenate(pieces, axis=1)
                tile = jnp.where(row_id == row, line, tile)
            ref[lb, d // bs, d % bs, start : start + VEC_ROWS, :] = tile.astype(ref.dtype)


def normalize(x):
    mean = jnp.mean(x, axis=1, keepdims=True)
    centred = x - mean
    scale = lax.rsqrt(jnp.mean(centred * centred, axis=1, keepdims=True) + NORM_EPS)
    return centred * scale, jnp.broadcast_to(scale, (x.shape[0], LANES))


def normalize_back(unit, scale, grad, gain):
    inner = grad * gain
    first = jnp.mean(inner, axis=1, keepdims=True)
    second = jnp.mean(inner * unit, axis=1, keepdims=True)
    out = jnp.concatenate([scale] * (WIDE // LANES), axis=1) * (inner - first - unit * second)
    return out, jnp.sum(grad * unit, axis=0, keepdims=True), jnp.sum(grad, axis=0, keepdims=True)


def gelu_pair(u):
    below = 0.5 + 0.5 * lax.erf(u * math.sqrt(0.5))
    bell = jnp.exp2((-0.5 * math.log2(math.e)) * (u * u))
    return u * below, below + u * (bell * (1.0 / math.sqrt(2.0 * math.pi)))


def head_masks(scale):
    lane = lax.broadcasted_iota(jnp.int32, (1, LANES), 1)
    first = jnp.where(lane < HEAD, scale, 0.0).astype(jnp.bfloat16)
    second = jnp.where(lane < HEAD, 0.0, scale).astype(jnp.bfloat16)
    return first, second


class Sizes:
    def __init__(self, dps):
        self.dps, self.bs = dps, dps // ZS
        self.qkv, self.out, self.up, self.down = (
            3 * WIDE // dps,
            WIDE // dps,
            4 * WIDE // dps,
            WIDE // dps,
        )
        self.att = self.qkv + VEC_ROWS
        self.dense = self.out + self.up
        self.wide = 4 * self.down


def qkv_rows(size, w, tile):
    count = QKV_TILE // size.qkv
    return rows_of(w, size.bs, tile * count, count, 0, size.qkv)


def out_rows(size, w):
    return rows_of(w, size.bs, 0, size.dps, 0, size.out)


def up_rows(size, w, tile):
    count = HALF // size.up
    return rows_of(w, size.bs, tile * count, count, size.out, size.up)


def forward_mix(size, w, table, h, mixed, piece):
    columns = slice(piece * QKV_TILE, (piece + 1) * QKV_TILE)
    mixed[:, columns] = (
        dot_nt(h[...], qkv_rows(size, w, piece)) + table[0:1, columns]
    ).astype(mixed.dtype)


def forward_attend(mixed, lse, attended, pair):
    lane = pair * LANES
    key_rows = mixed[:, WIDE + lane : WIDE + lane + LANES]
    values = mixed[:, 2 * WIDE + lane : 2 * WIDE + lane + LANES].T

    for part in range(2):
        rows = slice(part * HALF, (part + 1) * HALF)
        queries = mixed[rows, lane : lane + LANES]
        joined = []
        for head, mask in enumerate(head_masks(1.0 / math.sqrt(HEAD))):
            scores = dot_nt(key_rows, queries * mask)
            top = jnp.max(scores, axis=0, keepdims=True)
            probs = jnp.exp(scores - top)
            total = jnp.sum(probs, axis=0, keepdims=True)
            lse[2 * pair + head, :, rows] = top + jnp.log(total)
            probs = (probs * (1.0 / total)).astype(jnp.bfloat16)
            joined.append(dot_nn(values[head * HEAD : (head + 1) * HEAD], probs))
        joined = jnp.concatenate(joined, axis=0).T
        attended[rows, lane : lane + LANES] = joined.astype(attended.dtype)


def forward_project(size, w, table, h, attended, first, scale, normed):
    out = dot_nt(attended[...], out_rows(size, w))
    for part in range(2):
        rows = slice(part * HALF, (part + 1) * HALF)
        total = h[rows, :].astype(jnp.float32) + (out[rows] + table[1:2, 0:WIDE])
        unit, scale[rows, :] = normalize(total)
        first[rows, :] = unit
        normed[rows, :] = (
            unit * table[1:2, WIDE : 2 * WIDE] + table[1:2, 2 * WIDE : 3 * WIDE]
        ).astype(normed.dtype)


def forward_up(size, w, table, normed, slope, hidden, piece):
    for j in (2 * piece, 2 * piece + 1):
        columns = slice(j * HALF, (j + 1) * HALF)
        upper = dot_nt(normed[...], up_rows(size, w, j)) + table[2:3, columns]
        value, grad = gelu_pair(upper)
        hidden[:, columns] = value.astype(hidden.dtype)
        slope[:, columns] = grad.astype(slope.dtype)


def forward_down(size, w, table, normed, hidden, second, scale, h, piece):
    columns = slice(piece * HALF, (piece + 1) * HALF)
    count = size.dps // 2
    matrix = jnp.concatenate(
        [
            rows_of(w, size.bs, piece * count, count, j * size.down, size.down)
            for j in range(4)
        ],
        axis=1,
    )
    out = dot_nt(hidden[...], matrix)
    second[:, columns] = normed[:, columns].astype(jnp.float32) + (out + table[3:4, columns])
    if piece == 1:
        for part in range(2):
            rows = slice(part * HALF, (part + 1) * HALF)
            unit, scale[rows, :] = normalize(second[rows, :])
            second[rows, :] = unit
            h[rows, :] = (
                unit * table[3:4, WIDE : 2 * WIDE] + table[3:4, 2 * WIDE : 3 * WIDE]
            ).astype(h.dtype)


def backward_norm_two(table, dtable, dy, second, scale, dnormed, dlow, dlow_t):
    dtable[...] = jnp.zeros_like(dtable)
    for part in range(2):
        rows = slice(part * HALF, (part + 1) * HALF)
        grad, gain_sum, shift_sum = normalize_back(
            second[rows, :],
            scale[rows, :],
            dy[rows, :].astype(jnp.float32),
            table[3:4, WIDE : 2 * WIDE],
        )
        dnormed[rows, :] = grad
        dlow[rows, :] = grad.astype(dlow.dtype)
        dtable[3:4, 0:WIDE] += jnp.sum(grad, axis=0, keepdims=True)
        dtable[3:4, WIDE : 2 * WIDE] += gain_sum
        dtable[3:4, 2 * WIDE : 3 * WIDE] += shift_sum
    dlow_t[...] = dlow[...].T


def backward_down(size, grads, hidden, dlow_t, piece):
    @pl.loop(2 * piece, 2 * piece + 2)
    def _(i):
        start = aligned(i * size.down, 16)
        for half in range(2):
            columns = pl.ds(aligned(i * WIDE, WIDE) + half * HALF, HALF)
            value = dot_nn(dlow_t[...], hidden[:, columns])
            put_rows(grads, size.bs, 0, size.dps, start, size.down, value, 2 * half)


def backward_gelu(size, w, dtable, slope, dlow, dup, piece):
    @pl.loop(2 * piece, 2 * piece + 2)
    def _(i):
        start = aligned(i * size.down, 16)
        for half in range(2):
            columns = pl.ds(aligned(i * WIDE, WIDE) + half * HALF, HALF)
            blocks = (2 * half, 2 * half + 1)
            matrix = rows_of(w, size.bs, 0, size.dps, start, size.down, blocks)
            dupper = dot_nn(dlow[...], matrix) * slope[:, columns].astype(jnp.float32)
            dtable[2:3, columns] = jnp.sum(dupper, axis=0, keepdims=True)
            dup[:, columns] = dupper.astype(dup.dtype)


def backward_up(size, grads, normed, dup):
    count = HALF // size.up

    @pl.loop(0, 4)
    def _(i):
        for half in range(2):
            columns = pl.ds(aligned(i * WIDE, WIDE) + half * HALF, HALF)
            value = dot_tn(dup[:, columns], normed[...])
            first = (2 * i + half) * count
            put_rows(grads, size.bs, first, count, size.out, size.up, value)


def backward_normed(size, w, dnormed, dup):
    for half in range(2):
        columns = slice(half * HALF, (half + 1) * HALF)
        blocks = (2 * half, 2 * half + 1)
        matrix = rows_of(w, size.bs, 0, size.dps, size.out, size.up, blocks)
        dnormed[:, columns] = dnormed[:, columns] + dot_nn(dup[...], matrix)


def backward_norm_one(
    size, w, table, grads, dtable, first, scale, attended, dnormed, dlow, dlow_t, delta
):
    for part in range(2):
        rows = slice(part * HALF, (part + 1) * HALF)
        grad, gain_sum, shift_sum = normalize_back(
            first[rows, :], scale[rows, :], dnormed[rows, :], table[1:2, WIDE : 2 * WIDE]
        )
        dnormed[rows, :] = grad
        dlow[rows, :] = grad.astype(dlow.dtype)
        dtable[1:2, 0:WIDE] += jnp.sum(grad, axis=0, keepdims=True)
        dtable[1:2, WIDE : 2 * WIDE] += gain_sum
        dtable[1:2, 2 * WIDE : 3 * WIDE] += shift_sum
    dlow_t[...] = dlow[...].T
    for block in (0, 2):
        columns = slice(block * LANES, (block + 2) * LANES)
        value = dot_nn(dlow_t[...], attended[:, columns])
        put_rows(grads, size.bs, 0, size.dps, 0, size.out, value, block)
    grad = dot_nn(dlow[...], out_rows(size, w)).astype(dlow.dtype)
    dlow[...] = grad
    product = grad.astype(jnp.float32) * attended[...].astype(jnp.float32)
    high = product.astype(jnp.bfloat16)
    rest = (product - high.astype(jnp.float32)).astype(jnp.bfloat16)
    head = lax.broadcasted_iota(jnp.int32, delta.shape, 0)
    lane = lax.broadcasted_iota(jnp.int32, delta.shape, 1)
    inside = (lane >= head * HEAD) & (lane < (head + 1) * HEAD)
    inside = jnp.where(inside, 1.0, 0.0).astype(jnp.bfloat16)
    delta[...] = dot_nt(inside, high) + dot_nt(inside, rest)


def backward_attend(mixed, lse, delta, dtable, dlow, dmixed, pair):
    scale = 1.0 / math.sqrt(HEAD)
    lane = pair * LANES
    columns = slice(lane, lane + LANES)
    key_columns = slice(WIDE + lane, WIDE + lane + LANES)
    value_columns = slice(2 * WIDE + lane, 2 * WIDE + lane + LANES)
    key_rows = mixed[:, key_columns]
    keys_t = key_rows.T
    values = mixed[:, value_columns]
    dkeys = jnp.zeros((WIDE, LANES), jnp.float32)
    dvalues = jnp.zeros((WIDE, LANES), jnp.float32)
    for part in range(2):
        rows = slice(part * HALF, (part + 1) * HALF)
        queries = mixed[rows, columns]
        grad_out = dlow[rows, columns]
        dqueries = []
        for head in range(2):
            query = queries * head_masks(scale)[head]
            grad = grad_out * head_masks(1.0)[head]
            probs = jnp.exp(dot_nt(key_rows, query) - lse[2 * pair + head, :, rows])
            dprobs = dot_nt(values, grad)
            at = 2 * pair + head
            dscores = (probs * (dprobs - delta[at : at + 1, rows])).astype(jnp.bfloat16)
            dvalues = dvalues + dot_nn(probs.astype(jnp.bfloat16), grad)
            dkeys = dkeys + dot_nn(dscores, query)
            dqueries.append(dot_nn(keys_t[head * HEAD : (head + 1) * HEAD], dscores))
        dquery = jnp.concatenate(dqueries, axis=0).T * scale
        dtable[0:1, columns] += jnp.sum(dquery, axis=0, keepdims=True)
        dmixed[rows, columns] = dquery.astype(dmixed.dtype)
    dmixed[:, key_columns] = dkeys.astype(dmixed.dtype)
    dmixed[:, value_columns] = dvalues.astype(dmixed.dtype)
    dtable[0:1, value_columns] = jnp.sum(dvalues, axis=0, keepdims=True)


def backward_mix(size, grads, h, dmixed, piece):
    count = QKV_TILE // size.qkv
    grad = dmixed[:, piece * QKV_TILE : (piece + 1) * QKV_TILE]
    put_rows(grads, size.bs, piece * count, count, 0, size.qkv, dot_tn(grad, h[...]))


def backward_input(size, w, dnormed, dmixed, dy):
    for half in range(2):
        columns = slice(half * HALF, (half + 1) * HALF)
        blocks = (2 * half, 2 * half + 1)
        matrix = rows_of(w, size.bs, 0, size.dps, 0, size.qkv, blocks)
        dy[:, columns] = (dnormed[:, columns] + dot_nn(dmixed[...], matrix)).astype(dy.dtype)


WINDOW = 384


def group_rows(group):
    rows = lax.broadcasted_iota(jnp.int32, (16, LANES), 0)
    return jnp.where(rows == group, 1.0, 0.0).astype(jnp.bfloat16)


def pack_mix(piece, qkv, gains, biases):
    low = piece.dtype
    rows = qkv.shape[0]
    flat = jnp.concatenate([gains[...], biases[...]], axis=1)
    flat = jnp.concatenate([flat, jnp.zeros((1, 2 * WIDE - flat.shape[1]), flat.dtype)], axis=1)
    row_id = lax.broadcasted_iota(jnp.int32, (VEC_ROWS, LANES), 0)
    for lb in range(SECT):
        lane = lb * LANES
        piece[lb, :rows] = qkv[:, lane : lane + LANES].astype(low)
        tile = jnp.where(row_id == 0, flat[:, lane : lane + LANES], 0.0)
        lane += WIDE
        tile = jnp.where(row_id == 1, flat[:, lane : lane + LANES], tile)
        piece[lb, rows:] = tile.astype(low)


def pack_up(piece, out, up):
    rows = out.shape[0]
    for lb in range(SECT):
        lanes = slice(lb * LANES, (lb + 1) * LANES)
        piece[lb, :rows] = out[:, lanes].astype(piece.dtype)
        piece[lb, rows:] = up[:, lanes].astype(piece.dtype)


def pack_down(piece, down):
    rows = down.shape[0]
    for lb in range(SECT):
        for j in range(4):
            start = j * WIDE + lb * LANES
            piece[lb, j * rows : (j + 1) * rows] = down[:, start : start + LANES].astype(piece.dtype)


def pack_embedding(piece, weight, shift, square):
    n = weight.shape[0]
    square[...] = jnp.zeros_like(square)
    square[:GROUPS, :n] = shift[...]

    def ending(part, width):
        return jnp.concatenate([jnp.zeros((n, width - part.shape[1]), part.dtype), part], axis=1)

    parts = [
        square[...].T[:n],
        ending(weight[:, L1 + L2 :], 3 * LANES),
        ending(weight[:, L1 : L1 + L2], 2 * LANES),
        ending(weight[:, :L1], 2 * LANES),
    ]
    columns = jnp.concatenate(parts, axis=1).astype(piece.dtype)
    for lb in range(SECT):
        for part in range(2):
            start = part * WIDE + lb * LANES
            piece[lb, part * n : (part + 1) * n] = columns[:, start : start + LANES]


def expand(series, group, x):
    empty = jnp.zeros((WINDOW - series.shape[0], series.shape[1]), series.dtype)
    x[:, :WINDOW] = jnp.concatenate([empty, series[...]], axis=0).T
    lane = lax.broadcasted_iota(jnp.int32, (x.shape[0], LANES), 1)
    x[:, WINDOW:] = jnp.where(lane == group, 1.0, 0.0).astype(x.dtype)


def embed(size, emb, pick, x, wsel, h):
    rows = WIDE // size.dps
    first = rows_of(emb, size.bs, 0, size.dps, 0, rows)
    second = rows_of(emb, size.bs, 0, size.dps, rows, rows)
    long, middle, short = (pick[g : g + 1, :] for g in (2, 1, 0))
    wide = jnp.concatenate(
        [
            first[:, LANES : 2 * LANES] * long,
            first[:, 2 * LANES : 3 * LANES] * long + second[:, :LANES] * middle,
            first[:, 3 * LANES :] * long
            + second[:, LANES : 2 * LANES] * middle
            + second[:, 3 * LANES :] * short,
        ],
        axis=1,
    )
    wsel[...] = wide.T
    matrix = jnp.concatenate([wide, first[:, :LANES]], axis=1)
    h[...] = dot_nt(x[...], matrix).astype(h.dtype)


def embed_back(size, pick, x, wsel, dh, grads, series_grad):
    history = series_grad.shape[0]
    series_grad[...] = dot_nt(wsel[...], dh[...])[WINDOW - history :]
    sums = dot_tn(dh[...], x[...])
    long, middle, short = (pick[g : g + 1, :].astype(jnp.float32) for g in (2, 1, 0))
    parts = [sums[:, i * LANES : (i + 1) * LANES] for i in range(4)]
    parts = [
        parts[3],
        parts[0] * long,
        parts[1] * long,
        parts[2] * long,
        parts[1] * middle,
        parts[2] * middle,
        jnp.zeros_like(parts[0]),
        parts[2] * short,
    ]
    rows = WIDE // (SECT * size.dps)
    for pipe in range(SECT):
        block = (pipe % 2) * 2 + pipe // 2
        for dp in range(size.dps):
            start = (pipe * size.dps + dp) * rows
            piece = jnp.concatenate([part[start : start + rows] for part in parts], axis=0)
            grads[block, dp // size.bs, dp % size.bs] = piece.astype(grads.dtype)


def saved_shapes():
    low, wide = jnp.bfloat16, jnp.float32
    return [
        ((WIDE, WIDE), low),
        ((WIDE, 3 * WIDE), low),
        ((2 * SECT, 1, WIDE), wide),
        ((WIDE, WIDE), low),
        ((WIDE, WIDE), wide),
        ((WIDE, WIDE), low),
        ((WIDE, 4 * WIDE), low),
        ((WIDE, 4 * WIDE), low),
        ((WIDE, WIDE), wide),
        ((SECT, 4 * WIDE), wide),
        ((WIDE, LANES), wide),
        ((WIDE, LANES), wide),
    ]


def chunk_shape(size, rows):
    return (SECT, ZS, size.bs, rows, LANES)


HALVES = (2, 2, 2, 2)
CROSS = (2,)


def follow(plan, section, act, compute):
    seen = {}
    for step in plan:
        if len(step) == 1:
            piece = seen.get(step[0], 0)
            seen[step[0]] = piece + 1
            compute(step[0], piece)
            continue
        op, kind, offset = step
        where = section + offset
        if isinstance(where, int):
            if 0 <= where < SECT:
                act(op, kind, where)
        elif offset == 0:
            act(op, kind, where)
        else:
            inside = where < SECT if offset > 0 else where >= 0

            @pl.when(inside)
            def _():
                act(op, kind, where)


def forward_kernel(dps, groups, *refs):
    size = Sizes(dps)
    given, refs = refs[:9], refs[9:]
    out, copies_out, wsel, x, refs = refs[0], refs[1:4], refs[4], refs[5], refs[6:]
    kept, local, refs = refs[:12], refs[12:24], refs[24:]
    wholes, refs = refs[:4], refs[4:]
    pieces, held, refs = refs[:4], refs[4:13], refs[13:]
    emb_rows, pick, refs = refs[0], refs[1], refs[2:]
    given_sem, out_sem, kept_sem, own_sem, p_send, p_recv, send, recv = refs
    h, mixed, lse, attended, first, normed, slope, hidden, second, table, scale_1, scale_2 = local
    at = Place(dps)

    own = [
        pltpu.make_async_copy(
            pieces[kind].at[at.block],
            wholes[kind].at[at.pipe, at.block, at.z, at.b]
            if kind < EMB
            else wholes[kind].at[at.block, at.z, at.b],
            own_sem.at[kind],
        )
        for kind in range(4)
    ]
    def split(kind, back):
        copies = []
        for k in range(1, SECT):
            if back:
                region = wholes[kind].at[at.pipe_at(SECT - k), at.block, at.z, at.b]
                src = region
            else:
                block = at.block_of(at.pipe_at(k))
                region = wholes[kind].at[at.pipe, block, at.z, at.b]
                src = pieces[kind].at[block]
            sems = p_send.at[kind, k - 1], p_recv.at[kind, k - 1]
            copies.append(remote(src, region, *sems, (at.pipe_at(k), at.dp)))
        return copies

    def chunk(kind, section):
        if kind == EMB:
            return Spread(at, wholes[kind], send.at[3 * SECT], recv.at[3 * SECT])
        number = 3 * section + kind
        sort = SpreadCross if kind in CROSS else Spread
        return sort(at, wholes[kind].at[section], send.at[number], recv.at[number], HALVES[kind])

    def keep(kind, section):
        src, dst = wholes[kind].at[section], copies_out[kind].at[section]
        return pltpu.make_async_copy(src, dst, out_sem.at[kind, section])

    arrived = []

    def act(op, kind, section):
        if op == 0:
            if kind not in arrived:
                arrived.append(kind)
                own[kind].wait()
                if kind == EMB:
                    chunk(kind, section).start(0)
                    return
                for copy in split(kind, True):
                    copy.wait_recv()
                for copy in split(kind, False):
                    copy.wait_send()
                if kind == 0:
                    copies_start(split(1, False))
                    copies_start(split(2, False))
            chunk(kind, section).start(0)
        elif op < 4:
            chunk(kind, section).move(op - 1)
        else:
            chunk(kind, section).land(3)
            if kind != EMB:
                keep(kind, section).start()

    def saves(section, early):
        which = (1, 2, 3, 4, 5, 9, 10) if early else (6, 7, 8, 11)
        return [
            pltpu.make_async_copy(local[i], kept[i].at[section], kept_sem.at[i]) for i in which
        ]

    series, embed_weight, embed_bias, qkv, out_w, up_w, down_w, gains, biases = held
    gets = copies_of(zip(given, held), given_sem)
    for i in (3, 7, 8, 1, 2, 4, 5, 6, 0):
        gets[i].start()
    pick[...] = group_rows(groups[0])
    at.greet()
    copies_wait([gets[i] for i in (3, 7, 8)])
    pack_mix(pieces[0], qkv, gains, biases)
    own[0].start()
    at.met()
    copies_start(split(0, False))
    copies_wait(gets[1:3])
    pack_embedding(pieces[EMB], embed_weight, embed_bias, emb_rows)
    own[EMB].start()
    copies_wait(gets[4:7])
    pack_up(pieces[1], out_w, up_w)
    own[1].start()
    pack_down(pieces[2], down_w)
    own[2].start()
    table[...] = jnp.zeros_like(table)
    gets[0].wait()
    expand(series, groups[0], x)

    def before(name, piece):
        embed(size, wholes[EMB], pick, x, wsel, h)

    follow(FORWARD_START, 0, act, before)

    @pl.loop(0, SECT)
    def _(section):
        att, up, down = (ref.at[section] for ref in wholes[:3])
        keep_h = pltpu.make_async_copy(h, kept[0].at[section], kept_sem.at[0])

        def compute(name, piece):
            if name == "mix":
                if piece == 0:

                    @pl.when(section > 0)
                    def _():
                        copies_wait(saves(section - 1, True))

                    keep_h.start()
                    read_vectors(att, table, size.bs, size.qkv)
                forward_mix(size, att, table, h, mixed, piece)
            elif name == "attend":
                forward_attend(mixed, lse, attended, piece)
            elif name == "project":
                forward_project(size, up, table, h, attended, first, scale_1, normed)
                copies_start(saves(section, True))
            elif name == "up":
                if piece == 0:

                    @pl.when(section > 0)
                    def _():
                        copies_wait(saves(section - 1, False))

                forward_up(size, up, table, normed, slope, hidden, piece)
            else:
                if piece == 0:
                    keep_h.wait()
                forward_down(size, down, table, normed, hidden, second, scale_2, h, piece)
                if piece == 1:
                    copies_start(saves(section, False))

        follow(FORWARD_PERIOD, section, act, compute)

    out[...] = h[...]
    copies_wait(saves(SECT - 1, True))
    copies_wait(saves(SECT - 1, False))
    for kind in range(3):
        copies_wait([keep(kind, section) for section in range(SECT)])


def copies_of(pairs, sems):
    return [pltpu.make_async_copy(src, dst, sems.at[i]) for i, (src, dst) in enumerate(pairs)]


def forward_all(groups, given, dps):
    size = Sizes(dps)
    low, wide = jnp.bfloat16, jnp.float32
    shapes = saved_shapes()
    rows = (size.att, size.dense, size.wide, 2 * WIDE // dps)
    chunks = [chunk_shape(size, count) for count in rows]
    anywhere = pl.BlockSpec(memory_space=pl.ANY)
    inside = pl.BlockSpec(memory_space=pltpu.VMEM)
    outs = [((WIDE, WIDE), low)]
    outs += [((SECT,) + shape, low) for shape in chunks[:3]]
    outs += [((WINDOW, WIDE), low), ((WIDE, WIDE), low)]
    outs += [((SECT,) + shape, dtype) for shape, dtype in shapes]
    scratch = shapes + [((SECT,) + shape, low) for shape in chunks[:3]] + [(chunks[3], low)]
    scratch += [((SECT, count, LANES), low) for count in rows]
    scratch += [(array.shape, array.dtype) for array in given]
    scratch += [((LANES, LANES), wide), ((16, LANES), low)]
    slots = max(Spread.slots(size.bs), SpreadCross.slots(size.bs))
    dma = pltpu.SemaphoreType.DMA
    return pl.pallas_call(
        partial(forward_kernel, dps),
        out_shape=[jax.ShapeDtypeStruct(shape, dtype) for shape, dtype in outs],
        in_specs=[pl.BlockSpec(memory_space=pltpu.SMEM)] + [anywhere] * len(given),
        out_specs=[inside] + [anywhere] * 3 + [inside] * 2 + [anywhere] * len(shapes),
        scratch_shapes=[pltpu.VMEM(shape, dtype) for shape, dtype in scratch]
        + [
            dma((len(given),)),
            dma((3, SECT)),
            dma((len(shapes),)),
            dma((4,)),
            dma((3, SECT - 1)),
            dma((3, SECT - 1)),
            dma((1 + 3 * SECT, slots)),
            dma((1 + 3 * SECT, slots)),
        ],
        compiler_params=pltpu.CompilerParams(
            collective_id=0, has_side_effects=True, vmem_limit_bytes=60 * 1024 * 1024
        ),
        name="gather_forward",
    )(groups, *given)


FETCHES = {
    ("norm2", 0): (("second", "scale_2"), ("second", "scale_2")),
    ("down", 0): (("hidden",), ()),
    ("down", 1): ((), ("hidden",)),
    ("gelu", 0): (("slope", 2), ()),
    ("gelu", 1): ((), ("slope", 2)),
    ("up", 0): (("normed",), ("normed",)),
    ("normed", 0): ((1,), ()),
    ("norm1", 0): (("first", "scale_1", "attended"), ("first", "scale_1", "attended", 1)),
    ("attend", 0): (("mixed", "lse"), ()),
    ("attend", 3): ((), ("mixed", "lse")),
    ("mix", 0): (("h",), ()),
    ("mix", 1): ((), ("h",)),
    ("input", 0): ((0,), (0,)),
}


def backward_kernel(dps, groups, att, up, down, cotangent, x_in, wsel_in, *refs):
    size = Sizes(dps)
    kept, refs = refs[:12], refs[12:]
    series_grad, outs, refs = refs[0], refs[1:5], refs[5:]
    local, refs = refs[:11], refs[11:]
    tables, w_att, w_up, w_down, dtable, dy, dnormed, dlow, dlow_t, dmixed, dup = refs[:11]
    x, wsel, pick, delta, refs = *refs[11:15], refs[15:]
    kinds = []
    for kind in range(4):
        count = 6 if kind in CROSS else 5
        kinds.append(refs[:4] + (refs[4 : 4 + count],))
        refs = refs[4 + count :]
    w_sem, kept_sem, table_sem, late_sem, out_sem, p_send, p_recv, send, recv, credit = refs
    h, mixed, lse, attended, first, normed, slope, hidden, second, scale_1, scale_2 = local
    at = Place(dps)
    last = SECT - 1

    def weights(kind, section):
        src, dst = ((att, w_att), (up, w_up), (down, w_down))[kind]
        return pltpu.make_async_copy(src.at[section], dst, w_sem.at[kind])

    names = ("h", "mixed", "lse", "attended", "first", "normed", "slope", "hidden", "second")
    names += ("table", "scale_1", "scale_2")
    held = dict(zip(names[:9] + names[10:], local))

    def fetches(section, *wanted):
        found = []
        for name in wanted:
            if isinstance(name, int):
                found.append(weights(name, section))
            else:
                i = names.index(name)
                dst = held[name]
                found.append(pltpu.make_async_copy(kept[i].at[section], dst, kept_sem.at[i]))
        return found

    def chunk(kind, i):
        grads, totals, finals, landing, bufs = kinds[kind]
        sort = FoldCross if kind in CROSS else Fold
        refs = (grads, totals.at[i % 2], landing, bufs, finals.at[i])
        return sort(at, *refs, send.at[kind], recv.at[kind], credit.at[kind], HALVES[kind])

    def hand_over(kind, i):
        landing = outs[kind].at[at.block]
        final = kinds[kind][2].at[i]
        return (
            pltpu.make_async_copy(final, landing, out_sem.at[kind]),
            remote(final, landing, p_send.at[kind, i], p_recv.at[kind, at.pipe], (last - i, at.dp)),
        )

    def act(op, kind, i):
        again, more = (False, False) if kind == EMB else (i > 0, i < last)
        if op == 0:
            chunk(kind, i).start(0, again)
        elif op < 4:
            chunk(kind, i).move(op - 1, again, more)
        else:
            chunk(kind, i).land(3, more)
            if kind == EMB:
                outs[kind][...] = kinds[kind][2][0]
            else:
                here, away = hand_over(kind, i)

                @pl.when(at.pipe == last - i)
                def _():
                    here.start()

                @pl.when(at.pipe != last - i)
                def _():
                    away.start()

    copies_start(fetches(last, "second", "scale_2", "hidden", "slope", 2, "normed", 1))
    get_tables = pltpu.make_async_copy(kept[9], tables, table_sem)
    get_tables.start()
    copies_start(fetches(last, "first", "scale_1", "attended", "mixed", "lse", "h", 0))
    late = copies_of(((cotangent, dy), (x_in, x), (wsel_in, wsel)), late_sem)
    copies_start(late)
    pick[...] = group_rows(groups[0])
    at.greet()
    at.met()
    get_tables.wait()
    late[0].wait()

    @pl.loop(0, SECT)
    def _(i):
        section = last - i
        table = tables.at[section]

        def compute(name, piece):
            need, free = FETCHES.get((name, piece), ((), ()))
            copies_wait(fetches(section, *need))
            if name == "norm2":
                backward_norm_two(table, dtable, dy, second, scale_2, dnormed, dlow, dlow_t)
            elif name == "down":
                backward_down(size, kinds[2][0], hidden, dlow_t, piece)
            elif name == "gelu":
                backward_gelu(size, w_down, dtable, slope, dlow, dup, piece)
            elif name == "up":
                backward_up(size, kinds[1][0], normed, dup)
            elif name == "normed":
                backward_normed(size, w_up, dnormed, dup)
            elif name == "norm1":
                backward_norm_one(
                    size,
                    w_up,
                    table,
                    kinds[1][0],
                    dtable,
                    first,
                    scale_1,
                    attended,
                    dnormed,
                    dlow,
                    dlow_t,
                    delta,
                )
            elif name == "attend":
                backward_attend(mixed, lse, delta, dtable, dlow, dmixed, piece)
            elif name == "mix":
                backward_mix(size, kinds[0][0], h, dmixed, piece)
                if piece == 1:
                    write_vectors(kinds[0][0], dtable, size.bs, size.qkv)
            else:
                backward_input(size, w_att, dnormed, dmixed, dy)
            if free:

                @pl.when(section > 0)
                def _():
                    copies_start(fetches(section - 1, *free))

        follow(BACKWARD_PERIOD, i, act, compute)

    def after(name, piece):
        copies_wait(late[1:])
        embed_back(size, pick, x, wsel, dy, kinds[EMB][0], series_grad)

    follow(BACKWARD_END, 0, act, after)

    for kind in range(3):
        for i in range(SECT):
            here, away = hand_over(kind, i)

            @pl.when(at.pipe == last - i)
            def _():
                here.wait()

            @pl.when(at.pipe != last - i)
            def _():
                away.wait_send()

        for k in range(1, SECT):
            other = at.pipe_at(k)
            landing = outs[kind].at[at.block_of(other)]
            sems = p_send.at[kind, 0], p_recv.at[kind, other]
            remote(landing, landing, *sems, (other, at.dp)).wait_recv()


def backward_all(groups, weights, cotangent, x, wsel, kept, history, dps):
    size = Sizes(dps)
    low, wide = jnp.bfloat16, jnp.float32
    anywhere = pl.BlockSpec(memory_space=pl.ANY)
    inside = pl.BlockSpec(memory_space=pltpu.VMEM)
    shapes = saved_shapes()
    rows_emb = 8 * WIDE // (SECT * dps)
    kind_rows = (size.att, size.dense, size.wide, rows_emb)
    scratch = shapes[:9] + shapes[10:] + [((SECT,) + shapes[9][0], wide)]
    scratch += [(chunk_shape(size, rows), low) for rows in kind_rows[:3]]
    scratch += [
        (shapes[9][0], wide),
        ((WIDE, WIDE), low),
        ((WIDE, WIDE), wide),
        ((WIDE, WIDE), low),
        ((WIDE, WIDE), low),
        ((WIDE, 3 * WIDE), low),
        ((WIDE, 4 * WIDE), low),
        ((WIDE, WIDE), low),
        ((WINDOW, WIDE), low),
        ((16, LANES), low),
        ((16, WIDE), wide),
    ]
    for kind, rows in enumerate(kind_rows):
        sets, results = (1, 1) if kind == EMB else (2, SECT)
        scratch += [
            (chunk_shape(size, rows), low),
            ((sets, 2, ZS, size.bs, rows, LANES), low),
            ((results, rows, LANES), low),
            ((2, ZS, size.bs, rows, LANES), low),
        ]
        sort = FoldCross if kind in CROSS else Fold
        scratch += [(shape, low) for shape in sort.buffers(size.bs, rows, HALVES[kind])]
    slots = max(Fold.slots(size.bs), FoldCross.slots(size.bs))
    dma = pltpu.SemaphoreType.DMA
    return pl.pallas_call(
        partial(backward_kernel, dps),
        out_shape=[jax.ShapeDtypeStruct((history, WIDE), wide)]
        + [jax.ShapeDtypeStruct((SECT, rows, LANES), low) for rows in kind_rows[:3]]
        + [jax.ShapeDtypeStruct((rows_emb, LANES), low)],
        in_specs=[pl.BlockSpec(memory_space=pltpu.SMEM)] + [anywhere] * (6 + len(kept)),
        out_specs=[inside] + [anywhere] * 3 + [inside],
        scratch_shapes=[pltpu.VMEM(shape, dtype) for shape, dtype in scratch]
        + [
            dma((3,)),
            dma((12,)),
            dma(()),
            dma((3,)),
            dma((3,)),
            dma((3, SECT)),
            dma((3, SECT)),
            dma((4, slots)),
            dma((4, slots)),
            pltpu.SemaphoreType.REGULAR((4, slots)),
        ],
        compiler_params=pltpu.CompilerParams(
            collective_id=1, has_side_effects=True, vmem_limit_bytes=60 * 1024 * 1024
        ),
        name="backward_fold",
    )(groups, *weights, cotangent, x, wsel, *kept)


def finish_kernel(dps, n_gains, n_biases, *refs):
    size = Sizes(dps)
    given, refs = refs[:6], refs[6:]
    block_out, series_out, embed_w, embed_b, qkv, out, up_out, down_out, gains, biases = refs[:10]
    att, up, down, emb, sems = refs[10:]
    copies = copies_of(zip(given, (att, up, down, emb, block_out, series_out)), sems)
    copies_start(copies)
    copies_wait(copies[:4])
    for lb in range(SECT):
        lanes = slice(lb * LANES, (lb + 1) * LANES)
        qkv[:, lanes] = att[lb, : size.qkv].astype(jnp.float32)
        out[:, lanes] = up[lb, : size.out].astype(jnp.float32)
        up_out[:, lanes] = up[lb, size.out :].astype(jnp.float32)
        for j in range(4):
            rows = slice(j * size.down, (j + 1) * size.down)
            start = j * WIDE + lb * LANES
            down_out[:, start : start + LANES] = down[lb, rows].astype(jnp.float32)
    tiles = [att[lb, size.qkv :].astype(jnp.float32) for lb in range(SECT)]
    flat = jnp.concatenate([tile[row : row + 1] for row in range(2) for tile in tiles], axis=1)
    gains[...] = flat[:, :n_gains]
    biases[...] = flat[:, n_gains : n_gains + n_biases]
    rows = emb.shape[0] // 8
    packed = emb[...].astype(jnp.float32)
    packed = [packed[i * rows : (i + 1) * rows] for i in range(8)]
    square = jnp.concatenate([packed[0], jnp.zeros((LANES - rows, LANES), jnp.float32)], axis=0)
    embed_b[...] = square.T[:GROUPS, :rows]
    packed = jnp.concatenate(packed, axis=1)
    ends = ((1024, L1), (768, L2), (512, L3))
    embed_w[...] = jnp.concatenate([packed[:, end - span : end] for end, span in ends], axis=1)
    copies_wait(copies[4:])


def finish_all(sums, block, series, n_gains, n_biases, dps):
    size = Sizes(dps)
    wide = jnp.float32
    columns = WIDE // (SECT * dps)
    outs = [
        (block.shape, block.dtype),
        (series.shape, wide),
        ((columns, L1 + L2 + L3), wide),
        ((GROUPS, columns), wide),
        ((size.qkv, WIDE), wide),
        ((size.out, WIDE), wide),
        ((size.up, WIDE), wide),
        ((size.down, 4 * WIDE), wide),
        ((1, n_gains), wide),
        ((1, n_biases), wide),
    ]
    anywhere = pl.BlockSpec(memory_space=pl.ANY)
    inside = pl.BlockSpec(memory_space=pltpu.VMEM)
    return pl.pallas_call(
        partial(finish_kernel, dps, n_gains, n_biases),
        out_shape=[jax.ShapeDtypeStruct(shape, dtype) for shape, dtype in outs],
        in_specs=[anywhere] * 6,
        out_specs=[inside] * 10,
        scratch_shapes=[pltpu.VMEM(array.shape, array.dtype) for array in sums]
        + [pltpu.SemaphoreType.DMA((6,))],
        compiler_params=pltpu.CompilerParams(vmem_limit_bytes=60 * 1024 * 1024),
        name="finish",
    )(*sums, block, series)


def per_device(
    series,
    groups,
    cotangent,
    embed_weight,
    embed_bias,
    qkv_weight,
    out_weight,
    up_weight,
    down_weight,
    gains,
    biases,
):
    dps = lax.axis_size("dp")
    given = (
        series[0],
        embed_weight.T,
        embed_bias,
        qkv_weight[0],
        out_weight[0],
        up_weight[0],
        down_weight[0],
        gains,
        biases,
    )
    block_output, att, up, down, wsel, x, *kept = forward_all(groups, given, dps)
    series_grad, *sums = backward_all(
        groups, (att, up, down), cotangent[0], x, wsel, kept, series.shape[1], dps
    )
    outs = finish_all(sums, block_output, series_grad, gains.shape[1], biases.shape[1], dps)
    block_output, series_grad, embed_w, embed_b, qkv, out, up, down, gain_sum, bias_sum = outs
    return (
        block_output[None],
        series_grad[None],
        embed_w.T,
        embed_b,
        qkv[None],
        out[None],
        up[None],
        down[None],
        gain_sum,
        bias_sum,
    )


def solution(mesh):
    return jax.shard_map(
        per_device,
        mesh=mesh,
        in_specs=(
            P(("pipe", "dp"), None, None),
            P(("pipe", "dp")),
            P(("pipe", "dp"), None, None),
            P(None, "dp"),
            P(None, "dp"),
            P("pipe", "dp", None),
            P("pipe", "dp", None),
            P("pipe", "dp", None),
            P("pipe", "dp", None),
            P("pipe", "dp"),
            P("pipe", "dp"),
        ),
        out_specs=(
            P(("pipe", "dp"), None, None),
            P(("pipe", "dp"), None, None),
            P(None, ("pipe", "dp")),
            P(None, ("pipe", "dp")),
            P("pipe", "dp", None),
            P("pipe", "dp", None),
            P("pipe", "dp", None),
            P("pipe", "dp", None),
            P("pipe", "dp"),
            P("pipe", "dp"),
        ),
        check_vma=False,
    )
```

```python
from functools import partial
import math

import jax
import jax.numpy as jnp
from jax import lax
from jax.experimental import pallas as pl
from jax.experimental.pallas import tpu as pltpu
from jax.sharding import PartitionSpec as P

HEAD = 64
L1 = 96
L2 = 192
L3 = 336
GROUPS = 3


NORM_EPS = 1e-05


MESH = pl.DeviceIdType.MESH
LANES = 128
ZS = 4
SECT = 4
EMB = 3


class Place:
    def __init__(self, dps):
        self.bs = dps // ZS
        pipe = lax.axis_index("pipe")
        dp = lax.axis_index("dp")
        self.pipe, self.dp = pipe, dp
        self.x, self.c = pipe // 2, pipe % 2
        self.z, self.b = dp // self.bs, dp % self.bs
        self.block = self.c * 2 + self.x
        self.x_peer = ((1 - self.x) * 2 + self.c, dp)
        self.core_peer = (self.x * 2 + 1 - self.c, dp)

    def block_of(self, pipe):
        return (pipe % 2) * 2 + pipe // 2

    def pipe_at(self, step):
        return (self.pipe + step) % SECT

    def z_at(self, step):
        return (self.z + step) % ZS

    def b_at(self, step):
        return (self.b + step) % self.bs

    def z_peer(self, step):
        return (self.pipe, self.z_at(step) * self.bs + self.b)

    def b_peer(self, step):
        return (self.pipe, self.z * self.bs + self.b_at(step))

    def greet(self):
        barrier = pltpu.get_barrier_semaphore()
        peers = [(self.pipe_at(k), self.dp) for k in range(1, SECT)]
        peers += [self.z_peer(k) for k in range(1, ZS)]
        peers += [self.b_peer(k) for k in range(1, self.bs)]
        for peer in peers:
            pl.semaphore_signal(barrier, inc=1, device_id=peer, device_id_type=MESH)

    def met(self):
        pl.semaphore_wait(pltpu.get_barrier_semaphore(), SECT + ZS + self.bs - 3)


def remote(src, dst, send, recv, peer):
    return pltpu.make_async_remote_copy(
        src_ref=src, dst_ref=dst, send_sem=send, recv_sem=recv, device_id=peer, device_id_type=MESH
    )


FORWARD_START = (
    (0, 3, 0),
    (0, 0, 0),
    (0, 2, 0),
    (1, 3, 0),
    (1, 0, 0),
    (0, 1, 0),
    (2, 3, 0),
    (2, 0, 0),
    (0, 0, 1),
    (1, 1, 0),
    (1, 2, 0),
    (3, 3, 0),
    (0, 2, 1),
    (1, 0, 1),
    (2, 1, 0),
    (4, 3, 0),
    (3, 0, 0),
    ("embed",),
    (4, 0, 0),
)
FORWARD_PERIOD = (
    ("mix",),
    (0, 1, 1),
    (2, 0, 1),
    ("mix",),
    ("attend",),
    (3, 1, 0),
    ("attend",),
    (2, 2, 0),
    ("attend",),
    (0, 0, 2),
    (4, 1, 0),
    ("attend",),
    ("project",),
    (1, 1, 1),
    ("up",),
    (1, 2, 1),
    (0, 2, 2),
    (3, 2, 0),
    ("up",),
    (1, 0, 2),
    ("up",),
    (2, 1, 1),
    (3, 0, 1),
    (4, 2, 0),
    ("up",),
    ("down",),
    (4, 0, 1),
    ("down",),
)
BACKWARD_PERIOD = (
    (0, 0, -1),
    ("norm2",),
    (2, 1, -1),
    ("down",),
    ("down",),
    (1, 0, -1),
    (0, 2, 0),
    ("gelu",),
    ("gelu",),
    ("up",),
    (3, 1, -1),
    (1, 2, 0),
    (4, 0, -2),
    ("normed",),
    (2, 0, -1),
    ("norm1",),
    (0, 1, 0),
    ("attend",),
    ("attend",),
    (3, 0, -1),
    (3, 2, -1),
    (1, 1, 0),
    ("attend",),
    ("attend",),
    (2, 2, 0),
    ("mix",),
    ("mix",),
    ("input",),
    (4, 2, -1),
    (4, 1, -1),
)
BACKWARD_END = (
    (0, 0, 3),
    (2, 1, 3),
    (1, 0, 3),
    (3, 1, 3),
    ("embed",),
    (4, 0, 2),
    (0, 3, 0),
    (2, 0, 3),
    (1, 3, 0),
    (3, 0, 3),
    (2, 3, 0),
    (3, 2, 3),
    (4, 2, 3),
    (4, 1, 3),
    (4, 0, 3),
    (3, 3, 0),
    (4, 3, 0),
)


def copies_start(copies):
    for copy in copies:
        copy.start()


def copies_wait(copies):
    for copy in copies:
        copy.wait()


class Spread:
    def __init__(self, at, out, send, recv, half=ZS // 2):
        self.at, self.out, self.send, self.recv = at, out, send, recv
        nb = at.bs - 1
        self.slot_z = 0
        self.slot_b1 = ZS - 1
        self.slot_x1 = self.slot_b1 + nb
        self.slot_x2 = self.slot_x1 + 1
        self.slot_b2 = self.slot_x2 + 1
        self.slot_c = self.slot_b2 + nb
        self.half = half

    @staticmethod
    def slots(bs):
        return ZS - 1 + 2 * (bs - 1) + 3

    def copy(self, region, slot, peer):
        return remote(region, region, self.send.at[slot], self.recv.at[slot], peer)

    def copies(self, stage, back):
        at, out, half = self.at, self.out, self.half
        rest = pl.ds(half, ZS - half)
        x_block = at.c * 2 + 1 - at.x if back else at.block
        if stage == 0:
            return [
                self.copy(
                    out.at[at.block, at.z_at(ZS - k) if back else at.z, at.b],
                    self.slot_z + k - 1,
                    at.z_peer(k),
                )
                for k in range(1, ZS)
            ]
        if stage == 3:
            core = 1 - at.c if back else at.c
            return [self.copy(out.at[pl.ds(core * 2, 2)], self.slot_c, at.core_peer)]
        copies = []
        for k in range(1, at.bs):
            b = at.b_at(at.bs - k) if back else at.b
            if stage == 1:
                region, slot = out.at[at.block, pl.ds(0, half), b], self.slot_b1
            else:
                region, slot = out.at[pl.ds(at.c * 2, 2), rest, b], self.slot_b2
            copies.append(self.copy(region, slot + k - 1, at.b_peer(k)))
        if stage == 1:
            region, slot = out.at[x_block, rest, at.b], self.slot_x1
        else:
            region, slot = out.at[x_block, pl.ds(0, half)], self.slot_x2
        copies.append(self.copy(region, slot, at.x_peer))
        return copies

    def start(self, stage):
        copies_start(self.copies(stage, False))

    def land(self, stage):
        for copy in self.copies(stage, True):
            copy.wait_recv()
        for copy in self.copies(stage, False):
            copy.wait_send()

    def move(self, stage):
        self.land(stage)
        self.start(stage + 1)


class SpreadCross(Spread):
    @staticmethod
    def slots(bs):
        return 2 * bs + 2 * ZS - 1

    def copies(self, stage, back):
        at, out = self.at, self.out
        rows = out.shape[-2]
        cut = rows // 32 * 16
        some, rest = pl.ds(0, cut), pl.ds(cut, rows - cut)
        core = 1 - at.c if back else at.c
        if stage == 3:
            return [self.copy(out.at[pl.ds(core * 2, 2)], 2 * at.bs + 2 * ZS - 2, at.core_peer)]
        both = pl.ds(at.c * 2, 2)
        x_block = at.c * 2 + 1 - at.x if back else at.block
        copies = []
        if stage == 1:
            for k in range(1, ZS):
                z = at.z_at(ZS - k) if back else at.z
                copies.append(self.copy(out.at[both, z, at.b, some], at.bs + k - 1, at.z_peer(k)))
                slot = at.bs + ZS + k - 2
                copies.append(self.copy(out.at[at.block, z, :, rest], slot, at.z_peer(k)))
            return copies
        base = 0 if stage == 0 else at.bs + 2 * ZS - 2
        for k in range(1, at.bs):
            b = at.b_at(at.bs - k) if back else at.b
            region = out.at[at.block, at.z, b, rest] if stage == 0 else out.at[both, :, b, some]
            copies.append(self.copy(region, base + k, at.b_peer(k)))
        if stage == 0:
            region = out.at[x_block, at.z, at.b, some]
        else:
            region = out.at[x_block, :, :, rest]
        copies.append(self.copy(region, base, at.x_peer))
        return copies


class Fold:
    def __init__(self, at, grads, total, landing, bufs, final, send, recv, credit, half):
        self.at, self.grads, self.total = at, grads, total
        self.landing, self.bufs, self.final = landing, bufs, final
        self.send, self.recv, self.credit = send, recv, credit
        self.half = half
        nb = at.bs - 1
        self.slot_x1 = 1
        self.slot_b1 = 2
        self.slot_x2 = 2 + nb
        self.slot_b2 = 3 + nb
        self.slot_z = 3 + 2 * nb

    @staticmethod
    def slots(bs):
        return 3 + 2 * (bs - 1) + ZS - 1

    @staticmethod
    def buffers(bs, rows, half):
        nb = max(bs - 1, 1)
        rest = ZS - half
        return [
            (half, bs, rows, LANES),
            (nb, 2, rest, rows, LANES),
            (rest, rows, LANES),
            (nb, half, rows, LANES),
            (ZS - 1, rows, LANES),
        ]

    def core_parts(self):
        other = self.grads.at[pl.ds((1 - self.at.c) * 2, 2)]
        return [(other, self.landing, 0, self.at.core_peer, self.at.core_peer)]

    def parts(self, stage):
        at, half, total, bufs = self.at, self.half, self.total, self.bufs
        if stage == 0:
            return self.core_parts()
        if stage == 3:
            return [
                (
                    total.at[at.x, at.z_at(k), at.b],
                    bufs[4].at[k - 1],
                    self.slot_z + k - 1,
                    at.z_peer(k),
                    at.z_peer(ZS - k),
                )
                for k in range(1, ZS)
            ]
        rest = pl.ds(half, ZS - half)
        found = []
        for k in range(1, at.bs):
            if stage == 1:
                src, buf, slot = total.at[:, rest, at.b_at(k)], bufs[1], self.slot_b1
            else:
                src, buf, slot = total.at[at.x, pl.ds(0, half), at.b_at(k)], bufs[3], self.slot_b2
            found.append((src, buf.at[k - 1], slot + k - 1, at.b_peer(k), at.b_peer(at.bs - k)))
        if stage == 1:
            src, buf, slot = total.at[1 - at.x, pl.ds(0, half)], bufs[0], self.slot_x1
        else:
            src, buf, slot = total.at[1 - at.x, rest, at.b], bufs[2], self.slot_x2
        found.append((src, buf, slot, at.x_peer, at.x_peer))
        return found

    def start(self, stage, again):
        for src, buf, slot, to, _ in self.parts(stage):
            if again is not False:

                @pl.when(again)
                def _():
                    pl.semaphore_wait(self.credit.at[slot], 1)

            remote(src, buf, self.send.at[slot], self.recv.at[slot], to).start()

    def land(self, stage, more):
        parts = self.parts(stage)
        for src, buf, slot, to, _ in parts:
            remote(src, buf, self.send.at[slot], self.recv.at[slot], to).wait()
        self.add(stage)
        if more is not False:

            @pl.when(more)
            def _():
                for _, _, slot, _, origin in parts:
                    pl.semaphore_signal(
                        self.credit.at[slot], inc=1, device_id=origin, device_id_type=MESH
                    )

    def add_core(self):
        at, bs, total = self.at, self.at.bs, self.total

        @pl.loop(0, 2 * ZS * bs)
        def _(i):
            z, b = i // bs % ZS, i % bs
            x = i // (ZS * bs)
            total[x, z, b] = self.grads[at.c * 2 + x, z, b] + self.landing[x, z, b]

    def add(self, stage):
        at, half, bs = self.at, self.half, self.at.bs
        total, bufs = self.total, self.bufs
        rest = ZS - half
        if stage == 0:
            self.add_core()
        elif stage == 1:

            @pl.loop(0, half * bs)
            def _(i):
                z, b = i // bs, i % bs
                total[at.x, z, b] = total[at.x, z, b] + bufs[0][z, b]

            @pl.loop(0, 2 * rest)
            def _(i):
                x, z = i // rest, i % rest
                for k in range(bs - 1):
                    total[x, half + z, at.b] = total[x, half + z, at.b] + bufs[1][k, x, z]

        elif stage == 2:

            @pl.loop(0, rest)
            def _(z):
                total[at.x, half + z, at.b] = total[at.x, half + z, at.b] + bufs[2][z]

            @pl.loop(0, half)
            def _(z):
                for k in range(bs - 1):
                    total[at.x, z, at.b] = total[at.x, z, at.b] + bufs[3][k, z]

        else:
            self.finish([bufs[4][k] for k in range(ZS - 1)])

    def finish(self, pieces):
        at = self.at
        done = self.total[at.x, at.z, at.b].astype(jnp.float32)
        for piece in pieces:
            done = done + piece.astype(jnp.float32)
        self.final[...] = done.astype(self.final.dtype)

    def move(self, stage, again, more):
        self.land(stage, more)
        self.start(stage + 1, again)


class FoldCross(Fold):
    @staticmethod
    def slots(bs):
        return 2 * bs + 2 * ZS - 1

    @staticmethod
    def buffers(bs, rows, half):
        nb = max(bs - 1, 1)
        cut = rows // 32 * 16
        rest = rows - cut
        return [
            (nb, 2, ZS, cut, LANES),
            (ZS, bs, rest, LANES),
            (ZS - 1, 2, cut, LANES),
            (ZS - 1, bs, rest, LANES),
            (cut, LANES),
            (nb, rest, LANES),
        ]

    def cuts(self):
        rows = self.total.shape[-2]
        cut = rows // 32 * 16
        return pl.ds(0, cut), pl.ds(cut, rows - cut)

    def parts(self, stage):
        at, total, bufs = self.at, self.total, self.bufs
        if stage == 0:
            return self.core_parts()
        some, rest = self.cuts()
        found = []
        if stage == 2:
            for k in range(1, ZS):
                pair = (at.z_peer(k), at.z_peer(ZS - k))
                z = at.z_at(k)
                found.append((total.at[:, z, at.b, some], bufs[2].at[k - 1], at.bs + k, *pair))
                slot = at.bs + ZS + k - 1
                found.append((total.at[at.x, z, :, rest], bufs[3].at[k - 1], slot, *pair))
            return found
        base = 1 if stage == 1 else at.bs + 2 * ZS - 1
        for k in range(1, at.bs):
            pair = (at.b_peer(k), at.b_peer(at.bs - k))
            if stage == 1:
                src, buf = total.at[:, :, at.b_at(k), some], bufs[0].at[k - 1]
            else:
                src, buf = total.at[at.x, at.z, at.b_at(k), rest], bufs[5].at[k - 1]
            found.append((src, buf, base + k, *pair))
        if stage == 1:
            src, buf = total.at[1 - at.x, :, :, rest], bufs[1]
        else:
            src, buf = total.at[1 - at.x, at.z, at.b, some], bufs[4]
        found.append((src, buf, base, at.x_peer, at.x_peer))
        return found

    def add(self, stage):
        at, bs = self.at, self.at.bs
        total, bufs = self.total, self.bufs
        some, rest = self.cuts()
        if stage == 0:
            self.add_core()
        elif stage == 1:

            @pl.loop(0, 2 * ZS)
            def _(i):
                x, z = i // ZS, i % ZS
                for k in range(bs - 1):
                    total[x, z, at.b, some] = total[x, z, at.b, some] + bufs[0][k, x, z]

            @pl.loop(0, ZS * bs)
            def _(i):
                z, b = i // bs, i % bs
                total[at.x, z, b, rest] = total[at.x, z, b, rest] + bufs[1][z, b]

        elif stage == 2:
            for x in range(2):
                for k in range(ZS - 1):
                    total[x, at.z, at.b, some] = total[x, at.z, at.b, some] + bufs[2][k, x]

            @pl.loop(0, bs)
            def _(b):
                for k in range(ZS - 1):
                    total[at.x, at.z, b, rest] = total[at.x, at.z, b, rest] + bufs[3][k, b]

        else:
            total[at.x, at.z, at.b, some] = total[at.x, at.z, at.b, some] + bufs[4][...]
            for k in range(bs - 1):
                total[at.x, at.z, at.b, rest] = total[at.x, at.z, at.b, rest] + bufs[5][k]
            self.final[...] = total[at.x, at.z, at.b]


HALF = 256
WIDE = 512
QKV_TILE = 768
VEC_ROWS = 16


STEP = 64


def by_rows(fn, *arrays, step=STEP):
    parts = [
        fn(*[array[at : at + step] for array in arrays])
        for at in range(0, arrays[0].shape[0], step)
    ]
    if isinstance(parts[0], tuple):
        return tuple(jnp.concatenate(part, axis=0) for part in zip(*parts))
    return jnp.concatenate(parts, axis=0)


def dot_nt(a, b):
    return lax.dot_general(a, b, (((1,), (1,)), ((), ())), preferred_element_type=jnp.float32)


def dot_nn(a, b):
    return lax.dot_general(a, b, (((1,), (0,)), ((), ())), preferred_element_type=jnp.float32)


def dot_tn(a, b):
    return lax.dot_general(a, b, (((0,), (0,)), ((), ())), preferred_element_type=jnp.float32)


def aligned(index, unit):
    return pl.multiple_of(index, unit)


def rows_of(ref, bs, first, count, start, rows, blocks=range(SECT)):
    parts = []
    for i in range(count):
        d = first + i
        place = (d // bs, d % bs)
        parts.append(
            jnp.concatenate(
                [ref[(lb,) + place + (pl.ds(start, rows), slice(None))] for lb in blocks], axis=1
            )
        )
    return parts[0] if count == 1 else jnp.concatenate(parts, axis=0)


def put_rows(ref, bs, first, count, start, rows, value, block=0):
    value = value.astype(ref.dtype)
    for i in range(count):
        d = first + i
        place = (d // bs, d % bs)
        for lane in range(value.shape[1] // LANES):
            ref[(block + lane,) + place + (pl.ds(start, rows), slice(None))] = value[
                i * rows : (i + 1) * rows, lane * LANES : (lane + 1) * LANES
            ]


def vector_pieces(dps):
    n_gains, n_biases = 2 * WIDE // dps, 10 * WIDE // dps
    starts = [(0, 0), (0, 2), (1, 0), (1, 2), (2, 0), (2, 1), (2, 2), (2, 3), (3, 0), (3, 2)]
    pieces = []
    for d in range(dps):
        at = 0
        while at < n_gains + n_biases:
            if at < n_gains:
                index = d * n_gains + at
                row, column = (1, 3)[index // WIDE], WIDE + index % WIDE
                left = n_gains - at
            else:
                index = d * n_biases + at - n_gains
                row, part = starts[index // WIDE]
                column = part * WIDE + index % WIDE
                left = n_gains + n_biases - at
            size = min(left, LANES - at % LANES, LANES - column % LANES)
            pieces.append((d, at // WIDE, at % WIDE, row, column, size))
            at += size
    return pieces


def read_vectors(ref, table, bs, start):
    dps = ZS * bs
    tiles = {}
    for d, row, lane, to_row, to_lane, size in vector_pieces(dps):
        key = (d, lane // LANES)
        if key not in tiles:
            tile = ref[lane // LANES, d // bs, d % bs, start : start + VEC_ROWS, :]
            tiles[key] = tile.astype(jnp.float32)
        off = lane % LANES
        table[to_row : to_row + 1, to_lane : to_lane + size] = tiles[key][
            row : row + 1, off : off + size
        ]


def write_vectors(ref, table, bs, start):
    dps = ZS * bs
    found = {}
    for d, row, lane, to_row, to_lane, size in vector_pieces(dps):
        piece = table[to_row : to_row + 1, to_lane : to_lane + size]
        found.setdefault((d, lane // LANES), {}).setdefault(row, []).append(piece)
    row_id = lax.broadcasted_iota(jnp.int32, (VEC_ROWS, LANES), 0)
    for d in range(dps):
        for lb in range(SECT):
            tile = jnp.zeros((VEC_ROWS, LANES), jnp.float32)
            for row, pieces in found.get((d, lb), {}).items():
                have = sum(piece.shape[1] for piece in pieces)
                if have < LANES:
                    pieces = pieces + [jnp.zeros((1, LANES - have), jnp.float32)]
                line = pieces[0] if len(pieces) == 1 else jnp.concatenate(pieces, axis=1)
                tile = jnp.where(row_id == row, line, tile)
            ref[lb, d // bs, d % bs, start : start + VEC_ROWS, :] = tile.astype(ref.dtype)


def fold_rows(x):
    total = x[:8]
    for at in range(8, x.shape[0], 8):
        total = total + x[at : at + 8]
    return total


def normalize(x):
    mean = jnp.mean(x, axis=1, keepdims=True)
    centred = x - mean
    scale = lax.rsqrt(jnp.mean(centred * centred, axis=1, keepdims=True) + NORM_EPS)
    return centred * scale, jnp.broadcast_to(scale, (x.shape[0], LANES))


def normalize_back(unit, scale, grad, gain):
    inner = grad * gain
    first = jnp.mean(inner, axis=1, keepdims=True)
    second = jnp.mean(inner * unit, axis=1, keepdims=True)
    out = jnp.concatenate([scale] * (WIDE // LANES), axis=1) * (inner - first - unit * second)
    return out, fold_rows(out), fold_rows(grad * unit), fold_rows(grad)


def gelu_pair(u):
    below = 0.5 + 0.5 * lax.erf(u * math.sqrt(0.5))
    bell = jnp.exp2((-0.5 * math.log2(math.e)) * (u * u))
    return u * below, below + u * (bell * (1.0 / math.sqrt(2.0 * math.pi)))


def head_masks(scale):
    lane = lax.broadcasted_iota(jnp.int32, (1, LANES), 1)
    first = jnp.where(lane < HEAD, scale, 0.0).astype(jnp.bfloat16)
    second = jnp.where(lane < HEAD, 0.0, scale).astype(jnp.bfloat16)
    return first, second


class Sizes:
    def __init__(self, dps):
        self.dps, self.bs = dps, dps // ZS
        self.qkv, self.out, self.up, self.down = (
            3 * WIDE // dps,
            WIDE // dps,
            4 * WIDE // dps,
            WIDE // dps,
        )
        self.att = self.qkv + VEC_ROWS
        self.dense = self.out + self.up
        self.wide = 4 * self.down


def qkv_rows(size, w, tile):
    count = QKV_TILE // size.qkv
    return rows_of(w, size.bs, tile * count, count, 0, size.qkv)


def out_rows(size, w):
    return rows_of(w, size.bs, 0, size.dps, 0, size.out)


def up_rows(size, w, tile):
    count = HALF // size.up
    return rows_of(w, size.bs, tile * count, count, size.out, size.up)


def forward_mix(size, w, table, h, mixed, piece):
    columns = slice(piece * QKV_TILE, (piece + 1) * QKV_TILE)
    shift = table[0:1, columns]
    out = dot_nt(h[...], qkv_rows(size, w, piece))
    mixed[:, columns] = by_rows(lambda part: (part + shift).astype(mixed.dtype), out)


def softmax_columns(scores):
    parts = [scores[at : at + STEP] for at in range(0, scores.shape[0], STEP)]
    top = parts[0]
    for part in parts[1:]:
        top = jnp.maximum(top, part)
    top = jnp.max(top, axis=0, keepdims=True)
    parts = [jnp.exp(part - top) for part in parts]
    total = parts[0]
    for part in parts[1:]:
        total = total + part
    scale = 1.0 / jnp.sum(total, axis=0, keepdims=True)
    return jnp.concatenate([(part * scale).astype(jnp.bfloat16) for part in parts], axis=0)


def forward_attend(mixed, probs, attended, pair):
    lane = pair * LANES
    key_rows = mixed[:, WIDE + lane : WIDE + lane + LANES]
    values = mixed[:, 2 * WIDE + lane : 2 * WIDE + lane + LANES].T

    for part in range(2):
        rows = slice(part * HALF, (part + 1) * HALF)
        queries = mixed[rows, lane : lane + LANES]
        joined = []
        for head, mask in enumerate(head_masks(1.0 / math.sqrt(HEAD))):
            weights = softmax_columns(dot_nt(key_rows, queries * mask))
            probs[2 * pair + head, :, rows] = weights
            joined.append(dot_nn(values[head * HEAD : (head + 1) * HEAD], weights))
        joined = jnp.concatenate(joined, axis=0).T
        attended[rows, lane : lane + LANES] = joined.astype(attended.dtype)


def forward_project(size, w, table, h, attended, first, scale, normed):
    out = dot_nt(attended[...], out_rows(size, w))
    for part in range(WIDE // STEP):
        rows = slice(part * STEP, (part + 1) * STEP)
        total = h[rows, :].astype(jnp.float32) + (out[rows] + table[1:2, 0:WIDE])
        unit, scale[rows, :] = normalize(total)
        first[rows, :] = unit
        normed[rows, :] = (
            unit * table[1:2, WIDE : 2 * WIDE] + table[1:2, 2 * WIDE : 3 * WIDE]
        ).astype(normed.dtype)


def forward_up(size, w, table, normed, slope, hidden, piece):
    for j in (2 * piece, 2 * piece + 1):
        columns = slice(j * HALF, (j + 1) * HALF)
        shift = table[2:3, columns]
        upper = dot_nt(normed[...], up_rows(size, w, j))
        for part in range(WIDE // STEP):
            rows = slice(part * STEP, (part + 1) * STEP)
            value, grad = gelu_pair(upper[rows] + shift)
            hidden[rows, columns] = value.astype(hidden.dtype)
            slope[rows, columns] = grad.astype(slope.dtype)


def forward_down(size, w, table, normed, hidden, second, scale, h, piece):
    columns = slice(piece * HALF, (piece + 1) * HALF)
    count = size.dps // 2
    matrix = jnp.concatenate(
        [
            rows_of(w, size.bs, piece * count, count, j * size.down, size.down)
            for j in range(4)
        ],
        axis=1,
    )
    out = dot_nt(hidden[...], matrix)
    shift = table[3:4, columns]
    for part in range(WIDE // STEP):
        rows = slice(part * STEP, (part + 1) * STEP)
        second[rows, columns] = normed[rows, columns].astype(jnp.float32) + (out[rows] + shift)
    if piece == 1:
        for part in range(WIDE // STEP):
            rows = slice(part * STEP, (part + 1) * STEP)
            unit, scale[rows, :] = normalize(second[rows, :])
            second[rows, :] = unit
            h[rows, :] = (
                unit * table[3:4, WIDE : 2 * WIDE] + table[3:4, 2 * WIDE : 3 * WIDE]
            ).astype(h.dtype)


def backward_norm_two(table, dtable, dy, second, scale, dnormed, dlow, dlow_t):
    dtable[...] = jnp.zeros_like(dtable)
    sums = [jnp.zeros((8, WIDE), jnp.float32)] * 3
    for part in range(WIDE // STEP):
        rows = slice(part * STEP, (part + 1) * STEP)
        grad, *found = normalize_back(
            second[rows, :],
            scale[rows, :],
            dy[rows, :].astype(jnp.float32),
            table[3:4, WIDE : 2 * WIDE],
        )
        dnormed[rows, :] = grad
        dlow[rows, :] = grad.astype(dlow.dtype)
        sums = [total + new for total, new in zip(sums, found)]
    for i, total in enumerate(sums):
        dtable[3:4, i * WIDE : (i + 1) * WIDE] = jnp.sum(total, axis=0, keepdims=True)
    dlow_t[...] = dlow[...].T


def backward_down(size, grads, hidden, dlow_t, piece):
    @pl.loop(2 * piece, 2 * piece + 2)
    def _(i):
        start = aligned(i * size.down, 16)
        for half in range(2):
            columns = pl.ds(aligned(i * WIDE, WIDE) + half * HALF, HALF)
            value = dot_nn(dlow_t[...], hidden[:, columns])
            put_rows(grads, size.bs, 0, size.dps, start, size.down, value, 2 * half)


def backward_gelu(size, w, dtable, slope, dlow, dup, piece):
    @pl.loop(2 * piece, 2 * piece + 2)
    def _(i):
        start = aligned(i * size.down, 16)
        for half in range(2):
            columns = pl.ds(aligned(i * WIDE, WIDE) + half * HALF, HALF)
            blocks = (2 * half, 2 * half + 1)
            matrix = rows_of(w, size.bs, 0, size.dps, start, size.down, blocks)
            dhidden = dot_nn(dlow[...], matrix)
            total = jnp.zeros((8, HALF), jnp.float32)
            for part in range(WIDE // STEP):
                rows = slice(part * STEP, (part + 1) * STEP)
                dupper = dhidden[rows] * slope[rows, columns].astype(jnp.float32)
                total = total + fold_rows(dupper)
                dup[rows, columns] = dupper.astype(dup.dtype)
            dtable[2:3, columns] = jnp.sum(total, axis=0, keepdims=True)


def backward_up(size, grads, normed, dup):
    count = HALF // size.up

    @pl.loop(0, 4)
    def _(i):
        for half in range(2):
            columns = pl.ds(aligned(i * WIDE, WIDE) + half * HALF, HALF)
            value = dot_tn(dup[:, columns], normed[...])
            first = (2 * i + half) * count
            put_rows(grads, size.bs, first, count, size.out, size.up, value)


def backward_normed(size, w, dnormed, dup):
    for half in range(2):
        columns = slice(half * HALF, (half + 1) * HALF)
        blocks = (2 * half, 2 * half + 1)
        matrix = rows_of(w, size.bs, 0, size.dps, size.out, size.up, blocks)
        out = dot_nn(dup[...], matrix)
        for part in range(WIDE // STEP):
            rows = slice(part * STEP, (part + 1) * STEP)
            dnormed[rows, columns] = dnormed[rows, columns] + out[rows]


def backward_norm_one(
    size, w, table, grads, dtable, first, scale, attended, dnormed, dlow, dlow_t, delta
):
    sums = [jnp.zeros((8, WIDE), jnp.float32)] * 3
    for part in range(WIDE // STEP):
        rows = slice(part * STEP, (part + 1) * STEP)
        grad, *found = normalize_back(
            first[rows, :], scale[rows, :], dnormed[rows, :], table[1:2, WIDE : 2 * WIDE]
        )
        dnormed[rows, :] = grad
        dlow[rows, :] = grad.astype(dlow.dtype)
        sums = [total + new for total, new in zip(sums, found)]
    for i, total in enumerate(sums):
        dtable[1:2, i * WIDE : (i + 1) * WIDE] = jnp.sum(total, axis=0, keepdims=True)
    dlow_t[...] = dlow[...].T
    for block in (0, 2):
        columns = slice(block * LANES, (block + 2) * LANES)
        value = dot_nn(dlow_t[...], attended[:, columns])
        put_rows(grads, size.bs, 0, size.dps, 0, size.out, value, block)
    grad = dot_nn(dlow[...], out_rows(size, w)).astype(dlow.dtype)
    dlow[...] = grad
    product = grad.astype(jnp.float32) * attended[...].astype(jnp.float32)
    high = product.astype(jnp.bfloat16)
    rest = (product - high.astype(jnp.float32)).astype(jnp.bfloat16)
    head = lax.broadcasted_iota(jnp.int32, delta.shape, 0)
    lane = lax.broadcasted_iota(jnp.int32, delta.shape, 1)
    inside = (lane >= head * HEAD) & (lane < (head + 1) * HEAD)
    inside = jnp.where(inside, 1.0, 0.0).astype(jnp.bfloat16)
    delta[...] = dot_nt(inside, high) + dot_nt(inside, rest)


def backward_attend(mixed, probs, delta, dtable, dlow, dmixed, pair):
    scale = 1.0 / math.sqrt(HEAD)
    lane = pair * LANES
    columns = slice(lane, lane + LANES)
    key_columns = slice(WIDE + lane, WIDE + lane + LANES)
    value_columns = slice(2 * WIDE + lane, 2 * WIDE + lane + LANES)
    keys_t = mixed[:, key_columns].T
    values = mixed[:, value_columns]
    dkeys = jnp.zeros((WIDE, LANES), jnp.float32)
    dvalues = jnp.zeros((WIDE, LANES), jnp.float32)
    for part in range(2):
        rows = slice(part * HALF, (part + 1) * HALF)
        queries = mixed[rows, columns]
        grad_out = dlow[rows, columns]
        dqueries = []
        for head in range(2):
            query = queries * head_masks(scale)[head]
            grad = grad_out * head_masks(1.0)[head]
            at = 2 * pair + head
            weights = probs[at, :, rows]
            less = delta[at : at + 1, rows]
            dprobs = dot_nt(values, grad)
            dscores = by_rows(
                lambda p, dp: (p.astype(jnp.float32) * (dp - less)).astype(jnp.bfloat16),
                weights,
                dprobs,
            )
            dvalues = dvalues + dot_nn(weights, grad)
            dkeys = dkeys + dot_nn(dscores, query)
            dqueries.append(dot_nn(keys_t[head * HEAD : (head + 1) * HEAD], dscores))
        dquery = jnp.concatenate(dqueries, axis=0).T * scale
        dtable[0:1, columns] += jnp.sum(dquery, axis=0, keepdims=True)
        dmixed[rows, columns] = dquery.astype(dmixed.dtype)
    dmixed[:, key_columns] = dkeys.astype(dmixed.dtype)
    dmixed[:, value_columns] = dvalues.astype(dmixed.dtype)
    dtable[0:1, value_columns] = jnp.sum(dvalues, axis=0, keepdims=True)


def backward_mix(size, grads, h, dmixed, piece):
    count = QKV_TILE // size.qkv
    grad = dmixed[:, piece * QKV_TILE : (piece + 1) * QKV_TILE]
    put_rows(grads, size.bs, piece * count, count, 0, size.qkv, dot_tn(grad, h[...]))


def backward_input(size, w, dnormed, dmixed, dy):
    for half in range(2):
        columns = slice(half * HALF, (half + 1) * HALF)
        blocks = (2 * half, 2 * half + 1)
        matrix = rows_of(w, size.bs, 0, size.dps, 0, size.qkv, blocks)
        out = dot_nn(dmixed[...], matrix)
        for part in range(WIDE // STEP):
            rows = slice(part * STEP, (part + 1) * STEP)
            dy[rows, columns] = (dnormed[rows, columns] + out[rows]).astype(dy.dtype)


WINDOW = 384


def group_rows(group):
    rows = lax.broadcasted_iota(jnp.int32, (16, LANES), 0)
    return jnp.where(rows == group, 1.0, 0.0).astype(jnp.bfloat16)


def pack_mix(piece, qkv, gains, biases):
    low = piece.dtype
    rows = qkv.shape[0]
    flat = jnp.concatenate([gains[...], biases[...]], axis=1)
    flat = jnp.concatenate([flat, jnp.zeros((1, 2 * WIDE - flat.shape[1]), flat.dtype)], axis=1)
    row_id = lax.broadcasted_iota(jnp.int32, (VEC_ROWS, LANES), 0)
    for lb in range(SECT):
        lane = lb * LANES
        piece[lb, :rows] = qkv[:, lane : lane + LANES].astype(low)
        tile = jnp.where(row_id == 0, flat[:, lane : lane + LANES], 0.0)
        lane += WIDE
        tile = jnp.where(row_id == 1, flat[:, lane : lane + LANES], tile)
        piece[lb, rows:] = tile.astype(low)


def pack_up(piece, out, up):
    rows = out.shape[0]
    for lb in range(SECT):
        lanes = slice(lb * LANES, (lb + 1) * LANES)
        piece[lb, :rows] = out[:, lanes].astype(piece.dtype)
        piece[lb, rows:] = up[:, lanes].astype(piece.dtype)


def pack_down(piece, down):
    rows = down.shape[0]
    for lb in range(SECT):
        for j in range(4):
            start = j * WIDE + lb * LANES
            piece[lb, j * rows : (j + 1) * rows] = down[:, start : start + LANES].astype(piece.dtype)


def pack_embedding(piece, weight, shift, square):
    n = weight.shape[0]
    square[...] = jnp.zeros_like(square)
    square[:GROUPS, :n] = shift[...]

    def ending(part, width):
        return jnp.concatenate([jnp.zeros((n, width - part.shape[1]), part.dtype), part], axis=1)

    parts = [
        square[...].T[:n],
        ending(weight[:, L1 + L2 :], 3 * LANES),
        ending(weight[:, L1 : L1 + L2], 2 * LANES),
        ending(weight[:, :L1], 2 * LANES),
    ]
    columns = jnp.concatenate(parts, axis=1).astype(piece.dtype)
    for lb in range(SECT):
        for part in range(2):
            start = part * WIDE + lb * LANES
            piece[lb, part * n : (part + 1) * n] = columns[:, start : start + LANES]


def expand(series, group, x):
    empty = jnp.zeros((WINDOW - series.shape[0], series.shape[1]), series.dtype)
    x[:, :WINDOW] = jnp.concatenate([empty, series[...]], axis=0).T
    lane = lax.broadcasted_iota(jnp.int32, (x.shape[0], LANES), 1)
    x[:, WINDOW:] = jnp.where(lane == group, 1.0, 0.0).astype(x.dtype)


def embed(size, emb, pick, x, wsel, h):
    rows = WIDE // size.dps
    first = rows_of(emb, size.bs, 0, size.dps, 0, rows)
    second = rows_of(emb, size.bs, 0, size.dps, rows, rows)
    long, middle, short = (pick[g : g + 1, :] for g in (2, 1, 0))
    wide = jnp.concatenate(
        [
            first[:, LANES : 2 * LANES] * long,
            first[:, 2 * LANES : 3 * LANES] * long + second[:, :LANES] * middle,
            first[:, 3 * LANES :] * long
            + second[:, LANES : 2 * LANES] * middle
            + second[:, 3 * LANES :] * short,
        ],
        axis=1,
    )
    wsel[...] = wide.T
    matrix = jnp.concatenate([wide, first[:, :LANES]], axis=1)
    h[...] = dot_nt(x[...], matrix).astype(h.dtype)


def embed_back(size, pick, x, wsel, dh, grads, series_grad):
    history = series_grad.shape[0]
    series_grad[...] = dot_nt(wsel[...], dh[...])[WINDOW - history :]
    sums = dot_tn(dh[...], x[...])
    long, middle, short = (pick[g : g + 1, :].astype(jnp.float32) for g in (2, 1, 0))
    parts = [sums[:, i * LANES : (i + 1) * LANES] for i in range(4)]
    parts = [
        parts[3],
        parts[0] * long,
        parts[1] * long,
        parts[2] * long,
        parts[1] * middle,
        parts[2] * middle,
        jnp.zeros_like(parts[0]),
        parts[2] * short,
    ]
    rows = WIDE // (SECT * size.dps)
    for pipe in range(SECT):
        block = (pipe % 2) * 2 + pipe // 2
        for dp in range(size.dps):
            start = (pipe * size.dps + dp) * rows
            piece = jnp.concatenate([part[start : start + rows] for part in parts], axis=0)
            grads[block, dp // size.bs, dp % size.bs] = piece.astype(grads.dtype)


def saved_shapes():
    low, wide = jnp.bfloat16, jnp.float32
    return [
        ((WIDE, WIDE), low),
        ((WIDE, 3 * WIDE), low),
        ((2 * SECT, 1, LANES), wide),
        ((WIDE, WIDE), low),
        ((WIDE, WIDE), wide),
        ((WIDE, WIDE), low),
        ((WIDE, 4 * WIDE), low),
        ((WIDE, 4 * WIDE), low),
        ((WIDE, WIDE), wide),
        ((SECT, 4 * WIDE), wide),
        ((WIDE, LANES), wide),
        ((WIDE, LANES), wide),
        ((2 * SECT, WIDE, WIDE), low),
    ]


def chunk_shape(size, rows):
    return (SECT, ZS, size.bs, rows, LANES)


HALVES = (2, 2, 2, 2)
CROSS = (2,)


def follow(plan, section, act, compute):
    seen = {}
    for step in plan:
        if len(step) == 1:
            piece = seen.get(step[0], 0)
            seen[step[0]] = piece + 1
            compute(step[0], piece)
            continue
        op, kind, offset = step
        where = section + offset
        if isinstance(where, int):
            if 0 <= where < SECT:
                act(op, kind, where)
        elif offset == 0:
            act(op, kind, where)
        else:
            inside = where < SECT if offset > 0 else where >= 0

            @pl.when(inside)
            def _():
                act(op, kind, where)


def forward_kernel(dps, groups, *refs):
    size = Sizes(dps)
    given, refs = refs[:9], refs[9:]
    out, wholes, wsel, x, refs = refs[0], refs[1:5], refs[5], refs[6], refs[7:]
    kept, local, refs = refs[:13], refs[13:26], refs[26:]
    buffers, refs = refs[:4], refs[4:]
    pieces, held, refs = refs[:4], refs[4:13], refs[13:]
    emb_rows, pick, refs = refs[0], refs[1], refs[2:]
    given_sem, w_sem, kept_sem, own_sem, p_send, p_recv, send, recv = refs
    h, mixed, lse, attended, first, normed, slope, hidden, second, table, scale_1, scale_2, probs = local
    at = Place(dps)

    own = [
        pltpu.make_async_copy(
            pieces[kind].at[at.block],
            wholes[kind].at[at.pipe, at.block, at.z, at.b]
            if kind < EMB
            else wholes[kind].at[at.block, at.z, at.b],
            own_sem.at[kind],
        )
        for kind in range(4)
    ]
    def split(kind, back):
        copies = []
        for k in range(1, SECT):
            if back:
                region = wholes[kind].at[at.pipe_at(SECT - k), at.block, at.z, at.b]
                src = region
            else:
                block = at.block_of(at.pipe_at(k))
                region = wholes[kind].at[at.pipe, block, at.z, at.b]
                src = pieces[kind].at[block]
            sems = p_send.at[kind, k - 1], p_recv.at[kind, k - 1]
            copies.append(remote(src, region, *sems, (at.pipe_at(k), at.dp)))
        return copies

    def chunk(kind, section):
        if kind == EMB:
            return Spread(at, wholes[kind], send.at[3 * SECT], recv.at[3 * SECT])
        number = 3 * section + kind
        sort = SpreadCross if kind in CROSS else Spread
        return sort(at, wholes[kind].at[section], send.at[number], recv.at[number], HALVES[kind])

    def load(kind, section, core):
        blocks = pl.ds(core * 2, 2)
        src, dst = wholes[kind], buffers[kind]
        if kind != EMB:
            src, dst = src.at[section], dst.at[section % 2]
        sem = w_sem.at[kind, section % 2, core]
        return pltpu.make_async_copy(src.at[blocks], dst.at[blocks], sem)

    def loaded(kind, section):
        load(kind, section, at.c).wait()
        load(kind, section, 1 - at.c).wait()

    arrived = []

    def act(op, kind, section):
        if op == 0:
            if kind not in arrived:
                arrived.append(kind)
                own[kind].wait()
                if kind == EMB:
                    chunk(kind, section).start(0)
                    return
                for copy in split(kind, True):
                    copy.wait_recv()
                for copy in split(kind, False):
                    copy.wait_send()
                if kind == 0:
                    copies_start(split(1, False))
                    copies_start(split(2, False))
            chunk(kind, section).start(0)
        elif op < 4:
            chunk(kind, section).move(op - 1)
            if op == 3:
                load(kind, section, at.c).start()
        else:
            chunk(kind, section).land(3)
            load(kind, section, 1 - at.c).start()

    def saves(section, early):
        which = (1, 3, 4, 5, 9, 10, 12) if early else (6, 7, 8, 11)
        return [
            pltpu.make_async_copy(local[i], kept[i].at[section], kept_sem.at[i]) for i in which
        ]

    series, embed_weight, embed_bias, qkv, out_w, up_w, down_w, gains, biases = held
    gets = copies_of(zip(given, held), given_sem)
    for i in (3, 7, 8, 1, 2, 4, 5, 6, 0):
        gets[i].start()
    pick[...] = group_rows(groups[0])
    at.greet()
    copies_wait([gets[i] for i in (3, 7, 8)])
    pack_mix(pieces[0], qkv, gains, biases)
    own[0].start()
    at.met()
    copies_start(split(0, False))
    copies_wait(gets[1:3])
    pack_embedding(pieces[EMB], embed_weight, embed_bias, emb_rows)
    own[EMB].start()
    copies_wait(gets[4:7])
    pack_up(pieces[1], out_w, up_w)
    own[1].start()
    pack_down(pieces[2], down_w)
    own[2].start()
    table[...] = jnp.zeros_like(table)
    gets[0].wait()
    expand(series, groups[0], x)

    def before(name, piece):
        loaded(EMB, 0)
        embed(size, buffers[EMB], pick, x, wsel, h)

    follow(FORWARD_START, 0, act, before)

    @pl.loop(0, SECT)
    def _(section):
        att, up, down = (ref.at[section % 2] for ref in buffers[:3])
        keep_h = pltpu.make_async_copy(h, kept[0].at[section], kept_sem.at[0])

        def compute(name, piece):
            if name == "mix":
                if piece == 0:

                    @pl.when(section > 0)
                    def _():
                        copies_wait(saves(section - 1, True))

                    keep_h.start()
                    loaded(0, section)
                    read_vectors(att, table, size.bs, size.qkv)
                forward_mix(size, att, table, h, mixed, piece)
            elif name == "attend":
                forward_attend(mixed, probs, attended, piece)
            elif name == "project":
                loaded(1, section)
                forward_project(size, up, table, h, attended, first, scale_1, normed)
                copies_start(saves(section, True))
            elif name == "up":
                if piece == 0:

                    @pl.when(section > 0)
                    def _():
                        copies_wait(saves(section - 1, False))

                forward_up(size, up, table, normed, slope, hidden, piece)
            else:
                if piece == 0:
                    loaded(2, section)
                    keep_h.wait()
                forward_down(size, down, table, normed, hidden, second, scale_2, h, piece)
                if piece == 1:
                    copies_start(saves(section, False))

        follow(FORWARD_PERIOD, section, act, compute)

    out[...] = h[...]
    copies_wait(saves(SECT - 1, True))
    copies_wait(saves(SECT - 1, False))


def copies_of(pairs, sems):
    return [pltpu.make_async_copy(src, dst, sems.at[i]) for i, (src, dst) in enumerate(pairs)]


def forward_all(groups, given, dps):
    size = Sizes(dps)
    low, wide = jnp.bfloat16, jnp.float32
    shapes = saved_shapes()
    rows = (size.att, size.dense, size.wide, 2 * WIDE // dps)
    chunks = [chunk_shape(size, count) for count in rows]
    anywhere = pl.BlockSpec(memory_space=pl.ANY)
    inside = pl.BlockSpec(memory_space=pltpu.VMEM)
    outs = [((WIDE, WIDE), low)]
    outs += [((SECT,) + shape, low) for shape in chunks[:3]] + [(chunks[3], low)]
    outs += [((WINDOW, WIDE), low), ((WIDE, WIDE), low)]
    outs += [((SECT,) + shape, dtype) for shape, dtype in shapes]
    scratch = shapes + [((2,) + shape, low) for shape in chunks[:3]] + [(chunks[3], low)]
    scratch += [((SECT, count, LANES), low) for count in rows]
    scratch += [(array.shape, array.dtype) for array in given]
    scratch += [((LANES, LANES), wide), ((16, LANES), low)]
    slots = max(Spread.slots(size.bs), SpreadCross.slots(size.bs))
    dma = pltpu.SemaphoreType.DMA
    return pl.pallas_call(
        partial(forward_kernel, dps),
        out_shape=[jax.ShapeDtypeStruct(shape, dtype) for shape, dtype in outs],
        in_specs=[pl.BlockSpec(memory_space=pltpu.SMEM)] + [anywhere] * len(given),
        out_specs=[inside] + [anywhere] * 4 + [inside] * 2 + [anywhere] * len(shapes),
        scratch_shapes=[pltpu.VMEM(shape, dtype) for shape, dtype in scratch]
        + [
            dma((len(given),)),
            dma((4, 2, 2)),
            dma((len(shapes),)),
            dma((4,)),
            dma((3, SECT - 1)),
            dma((3, SECT - 1)),
            dma((1 + 3 * SECT, slots)),
            dma((1 + 3 * SECT, slots)),
        ],
        compiler_params=pltpu.CompilerParams(
            collective_id=0, has_side_effects=True, vmem_limit_bytes=60 * 1024 * 1024
        ),
        name="gather_forward",
    )(groups, *given)


FETCHES = {
    ("norm2", 0): (("second", "scale_2"), ("second", "scale_2")),
    ("down", 0): (("hidden",), ()),
    ("down", 1): ((), ("hidden",)),
    ("gelu", 0): (("slope", 2), ()),
    ("gelu", 1): ((), ("slope", 2)),
    ("up", 0): (("normed",), ("normed",)),
    ("normed", 0): ((1,), ()),
    ("norm1", 0): (("first", "scale_1", "attended"), ("first", "scale_1", "attended", 1)),
    ("attend", 0): (("mixed", "probs"), ()),
    ("attend", 3): ((), ("mixed", "probs")),
    ("mix", 0): (("h",), ()),
    ("mix", 1): ((), ("h",)),
    ("input", 0): ((0,), (0,)),
}


def backward_kernel(dps, groups, att, up, down, cotangent, x_in, wsel_in, *refs):
    size = Sizes(dps)
    kept, refs = refs[:13], refs[13:]
    series_grad, outs, refs = refs[0], refs[1:5], refs[5:]
    local, refs = refs[:12], refs[12:]
    tables, w_att, w_up, w_down, dtable, dy, dnormed, dlow, dlow_t, dmixed, dup = refs[:11]
    x, wsel, pick, delta, refs = *refs[11:15], refs[15:]
    kinds = []
    for kind in range(4):
        count = 6 if kind in CROSS else 5
        kinds.append(refs[:4] + (refs[4 : 4 + count],))
        refs = refs[4 + count :]
    w_sem, kept_sem, table_sem, late_sem, out_sem, p_send, p_recv, send, recv, credit = refs
    h, mixed, lse, attended, first, normed, slope, hidden, second, scale_1, scale_2, probs = local
    at = Place(dps)
    last = SECT - 1

    def weights(kind, section):
        src, dst = ((att, w_att), (up, w_up), (down, w_down))[kind]
        return pltpu.make_async_copy(src.at[section], dst, w_sem.at[kind])

    names = ("h", "mixed", "lse", "attended", "first", "normed", "slope", "hidden", "second")
    names += ("table", "scale_1", "scale_2", "probs")
    held = dict(zip(names[:9] + names[10:], local))

    def fetches(section, *wanted):
        found = []
        for name in wanted:
            if isinstance(name, int):
                found.append(weights(name, section))
            else:
                i = names.index(name)
                dst = held[name]
                found.append(pltpu.make_async_copy(kept[i].at[section], dst, kept_sem.at[i]))
        return found

    def chunk(kind, i):
        grads, totals, finals, landing, bufs = kinds[kind]
        sort = FoldCross if kind in CROSS else Fold
        refs = (grads, totals.at[i % 2], landing, bufs, finals.at[i])
        return sort(at, *refs, send.at[kind], recv.at[kind], credit.at[kind], HALVES[kind])

    def hand_over(kind, i):
        landing = outs[kind].at[at.block]
        final = kinds[kind][2].at[i]
        return (
            pltpu.make_async_copy(final, landing, out_sem.at[kind]),
            remote(final, landing, p_send.at[kind, i], p_recv.at[kind, at.pipe], (last - i, at.dp)),
        )

    def act(op, kind, i):
        again, more = (False, False) if kind == EMB else (i > 0, i < last)
        if op == 0:
            chunk(kind, i).start(0, again)
        elif op < 4:
            chunk(kind, i).move(op - 1, again, more)
        else:
            chunk(kind, i).land(3, more)
            if kind == EMB:
                outs[kind][...] = kinds[kind][2][0]
            else:
                here, away = hand_over(kind, i)

                @pl.when(at.pipe == last - i)
                def _():
                    here.start()

                @pl.when(at.pipe != last - i)
                def _():
                    away.start()

    copies_start(fetches(last, "second", "scale_2", "hidden", "slope", 2, "normed", 1))
    get_tables = pltpu.make_async_copy(kept[9], tables, table_sem)
    get_tables.start()
    copies_start(fetches(last, "first", "scale_1", "attended", "mixed", "probs", "h", 0))
    late = copies_of(((cotangent, dy), (x_in, x), (wsel_in, wsel)), late_sem)
    copies_start(late)
    pick[...] = group_rows(groups[0])
    at.greet()
    at.met()
    get_tables.wait()
    late[0].wait()

    @pl.loop(0, SECT)
    def _(i):
        section = last - i
        table = tables.at[section]

        def compute(name, piece):
            need, free = FETCHES.get((name, piece), ((), ()))
            copies_wait(fetches(section, *need))
            if name == "norm2":
                backward_norm_two(table, dtable, dy, second, scale_2, dnormed, dlow, dlow_t)
            elif name == "down":
                backward_down(size, kinds[2][0], hidden, dlow_t, piece)
            elif name == "gelu":
                backward_gelu(size, w_down, dtable, slope, dlow, dup, piece)
            elif name == "up":
                backward_up(size, kinds[1][0], normed, dup)
            elif name == "normed":
                backward_normed(size, w_up, dnormed, dup)
            elif name == "norm1":
                backward_norm_one(
                    size,
                    w_up,
                    table,
                    kinds[1][0],
                    dtable,
                    first,
                    scale_1,
                    attended,
                    dnormed,
                    dlow,
                    dlow_t,
                    delta,
                )
            elif name == "attend":
                backward_attend(mixed, probs, delta, dtable, dlow, dmixed, piece)
            elif name == "mix":
                backward_mix(size, kinds[0][0], h, dmixed, piece)
                if piece == 1:
                    write_vectors(kinds[0][0], dtable, size.bs, size.qkv)
            else:
                backward_input(size, w_att, dnormed, dmixed, dy)
            if free:

                @pl.when(section > 0)
                def _():
                    copies_start(fetches(section - 1, *free))

        follow(BACKWARD_PERIOD, i, act, compute)

    def after(name, piece):
        copies_wait(late[1:])
        embed_back(size, pick, x, wsel, dy, kinds[EMB][0], series_grad)

    follow(BACKWARD_END, 0, act, after)

    for kind in range(3):
        for i in range(SECT):
            here, away = hand_over(kind, i)

            @pl.when(at.pipe == last - i)
            def _():
                here.wait()

            @pl.when(at.pipe != last - i)
            def _():
                away.wait_send()

        for k in range(1, SECT):
            other = at.pipe_at(k)
            landing = outs[kind].at[at.block_of(other)]
            sems = p_send.at[kind, 0], p_recv.at[kind, other]
            remote(landing, landing, *sems, (other, at.dp)).wait_recv()


def backward_all(groups, weights, cotangent, x, wsel, kept, history, dps):
    size = Sizes(dps)
    low, wide = jnp.bfloat16, jnp.float32
    anywhere = pl.BlockSpec(memory_space=pl.ANY)
    inside = pl.BlockSpec(memory_space=pltpu.VMEM)
    shapes = saved_shapes()
    rows_emb = 8 * WIDE // (SECT * dps)
    kind_rows = (size.att, size.dense, size.wide, rows_emb)
    scratch = shapes[:9] + shapes[10:] + [((SECT,) + shapes[9][0], wide)]
    scratch += [(chunk_shape(size, rows), low) for rows in kind_rows[:3]]
    scratch += [
        (shapes[9][0], wide),
        ((WIDE, WIDE), low),
        ((WIDE, WIDE), wide),
        ((WIDE, WIDE), low),
        ((WIDE, WIDE), low),
        ((WIDE, 3 * WIDE), low),
        ((WIDE, 4 * WIDE), low),
        ((WIDE, WIDE), low),
        ((WINDOW, WIDE), low),
        ((16, LANES), low),
        ((16, WIDE), wide),
    ]
    for kind, rows in enumerate(kind_rows):
        sets, results = (1, 1) if kind == EMB else (2, SECT)
        scratch += [
            (chunk_shape(size, rows), low),
            ((sets, 2, ZS, size.bs, rows, LANES), low),
            ((results, rows, LANES), low),
            ((2, ZS, size.bs, rows, LANES), low),
        ]
        sort = FoldCross if kind in CROSS else Fold
        scratch += [(shape, low) for shape in sort.buffers(size.bs, rows, HALVES[kind])]
    slots = max(Fold.slots(size.bs), FoldCross.slots(size.bs))
    dma = pltpu.SemaphoreType.DMA
    return pl.pallas_call(
        partial(backward_kernel, dps),
        out_shape=[jax.ShapeDtypeStruct((history, WIDE), wide)]
        + [jax.ShapeDtypeStruct((SECT, rows, LANES), low) for rows in kind_rows[:3]]
        + [jax.ShapeDtypeStruct((rows_emb, LANES), low)],
        in_specs=[pl.BlockSpec(memory_space=pltpu.SMEM)] + [anywhere] * (6 + len(kept)),
        out_specs=[inside] + [anywhere] * 3 + [inside],
        scratch_shapes=[pltpu.VMEM(shape, dtype) for shape, dtype in scratch]
        + [
            dma((3,)),
            dma((13,)),
            dma(()),
            dma((3,)),
            dma((3,)),
            dma((3, SECT)),
            dma((3, SECT)),
            dma((4, slots)),
            dma((4, slots)),
            pltpu.SemaphoreType.REGULAR((4, slots)),
        ],
        compiler_params=pltpu.CompilerParams(
            collective_id=1, has_side_effects=True, vmem_limit_bytes=60 * 1024 * 1024
        ),
        name="backward_fold",
    )(groups, *weights, cotangent, x, wsel, *kept)


def finish_kernel(dps, n_gains, n_biases, *refs):
    size = Sizes(dps)
    given, refs = refs[:6], refs[6:]
    block_out, series_out, embed_w, embed_b, qkv, out, up_out, down_out, gains, biases = refs[:10]
    att, up, down, emb, sems = refs[10:]
    copies = copies_of(zip(given, (att, up, down, emb, block_out, series_out)), sems)
    copies_start(copies)
    copies_wait(copies[:4])
    for lb in range(SECT):
        lanes = slice(lb * LANES, (lb + 1) * LANES)
        qkv[:, lanes] = att[lb, : size.qkv].astype(jnp.float32)
        out[:, lanes] = up[lb, : size.out].astype(jnp.float32)
        up_out[:, lanes] = up[lb, size.out :].astype(jnp.float32)
        for j in range(4):
            rows = slice(j * size.down, (j + 1) * size.down)
            start = j * WIDE + lb * LANES
            down_out[:, start : start + LANES] = down[lb, rows].astype(jnp.float32)
    tiles = [att[lb, size.qkv :].astype(jnp.float32) for lb in range(SECT)]
    flat = jnp.concatenate([tile[row : row + 1] for row in range(2) for tile in tiles], axis=1)
    gains[...] = flat[:, :n_gains]
    biases[...] = flat[:, n_gains : n_gains + n_biases]
    rows = emb.shape[0] // 8
    packed = emb[...].astype(jnp.float32)
    packed = [packed[i * rows : (i + 1) * rows] for i in range(8)]
    square = jnp.concatenate([packed[0], jnp.zeros((LANES - rows, LANES), jnp.float32)], axis=0)
    embed_b[...] = square.T[:GROUPS, :rows]
    packed = jnp.concatenate(packed, axis=1)
    ends = ((1024, L1), (768, L2), (512, L3))
    embed_w[...] = jnp.concatenate([packed[:, end - span : end] for end, span in ends], axis=1)
    copies_wait(copies[4:])


def finish_all(sums, block, series, n_gains, n_biases, dps):
    size = Sizes(dps)
    wide = jnp.float32
    columns = WIDE // (SECT * dps)
    outs = [
        (block.shape, block.dtype),
        (series.shape, wide),
        ((columns, L1 + L2 + L3), wide),
        ((GROUPS, columns), wide),
        ((size.qkv, WIDE), wide),
        ((size.out, WIDE), wide),
        ((size.up, WIDE), wide),
        ((size.down, 4 * WIDE), wide),
        ((1, n_gains), wide),
        ((1, n_biases), wide),
    ]
    anywhere = pl.BlockSpec(memory_space=pl.ANY)
    inside = pl.BlockSpec(memory_space=pltpu.VMEM)
    return pl.pallas_call(
        partial(finish_kernel, dps, n_gains, n_biases),
        out_shape=[jax.ShapeDtypeStruct(shape, dtype) for shape, dtype in outs],
        in_specs=[anywhere] * 6,
        out_specs=[inside] * 10,
        scratch_shapes=[pltpu.VMEM(array.shape, array.dtype) for array in sums]
        + [pltpu.SemaphoreType.DMA((6,))],
        compiler_params=pltpu.CompilerParams(vmem_limit_bytes=60 * 1024 * 1024),
        name="finish",
    )(*sums, block, series)


def per_device(
    series,
    groups,
    cotangent,
    embed_weight,
    embed_bias,
    qkv_weight,
    out_weight,
    up_weight,
    down_weight,
    gains,
    biases,
):
    dps = lax.axis_size("dp")
    given = (
        series[0],
        embed_weight.T,
        embed_bias,
        qkv_weight[0],
        out_weight[0],
        up_weight[0],
        down_weight[0],
        gains,
        biases,
    )
    block_output, att, up, down, _, wsel, x, *kept = forward_all(groups, given, dps)
    series_grad, *sums = backward_all(
        groups, (att, up, down), cotangent[0], x, wsel, kept, series.shape[1], dps
    )
    outs = finish_all(sums, block_output, series_grad, gains.shape[1], biases.shape[1], dps)
    block_output, series_grad, embed_w, embed_b, qkv, out, up, down, gain_sum, bias_sum = outs
    return (
        block_output[None],
        series_grad[None],
        embed_w.T,
        embed_b,
        qkv[None],
        out[None],
        up[None],
        down[None],
        gain_sum,
        bias_sum,
    )


def solution(mesh):
    return jax.shard_map(
        per_device,
        mesh=mesh,
        in_specs=(
            P(("pipe", "dp"), None, None),
            P(("pipe", "dp")),
            P(("pipe", "dp"), None, None),
            P(None, "dp"),
            P(None, "dp"),
            P("pipe", "dp", None),
            P("pipe", "dp", None),
            P("pipe", "dp", None),
            P("pipe", "dp", None),
            P("pipe", "dp"),
            P("pipe", "dp"),
        ),
        out_specs=(
            P(("pipe", "dp"), None, None),
            P(("pipe", "dp"), None, None),
            P(None, ("pipe", "dp")),
            P(None, ("pipe", "dp")),
            P("pipe", "dp", None),
            P("pipe", "dp", None),
            P("pipe", "dp", None),
            P("pipe", "dp", None),
            P("pipe", "dp"),
            P("pipe", "dp"),
        ),
        check_vma=False,
    )
```

```python
from functools import partial
import math

import jax
import jax.numpy as jnp
from jax import lax
from jax.experimental import pallas as pl
from jax.experimental.pallas import tpu as pltpu
from jax.sharding import PartitionSpec as P

HEAD = 64
L1 = 96
L2 = 192
L3 = 336
GROUPS = 3


NORM_EPS = 1e-05


MESH = pl.DeviceIdType.MESH
LANES = 128
ZS = 4
SECT = 4
EMB = 3


class Place:
    def __init__(self, dps):
        self.bs = dps // ZS
        pipe = lax.axis_index("pipe")
        dp = lax.axis_index("dp")
        self.pipe, self.dp = pipe, dp
        self.x, self.c = pipe // 2, pipe % 2
        self.z, self.b = dp // self.bs, dp % self.bs
        self.block = self.c * 2 + self.x
        self.x_peer = ((1 - self.x) * 2 + self.c, dp)
        self.core_peer = (self.x * 2 + 1 - self.c, dp)

    def block_of(self, pipe):
        return (pipe % 2) * 2 + pipe // 2

    def pipe_at(self, step):
        return (self.pipe + step) % SECT

    def z_at(self, step):
        return (self.z + step) % ZS

    def b_at(self, step):
        return (self.b + step) % self.bs

    def z_peer(self, step):
        return (self.pipe, self.z_at(step) * self.bs + self.b)

    def b_peer(self, step):
        return (self.pipe, self.z * self.bs + self.b_at(step))

    def greet(self):
        barrier = pltpu.get_barrier_semaphore()
        peers = [(self.pipe_at(k), self.dp) for k in range(1, SECT)]
        peers += [self.z_peer(k) for k in range(1, ZS)]
        peers += [self.b_peer(k) for k in range(1, self.bs)]
        for peer in peers:
            pl.semaphore_signal(barrier, inc=1, device_id=peer, device_id_type=MESH)

    def met(self):
        pl.semaphore_wait(pltpu.get_barrier_semaphore(), SECT + ZS + self.bs - 3)


def remote(src, dst, send, recv, peer):
    return pltpu.make_async_remote_copy(
        src_ref=src, dst_ref=dst, send_sem=send, recv_sem=recv, device_id=peer, device_id_type=MESH
    )


FORWARD_START = (
    (0, 3, 0),
    (0, 0, 0),
    (1, 0, 0),
    (1, 3, 0),
    (0, 2, 0),
    (0, 1, 0),
    (2, 3, 0),
    (2, 0, 0),
    (0, 0, 1),
    (1, 1, 0),
    (1, 2, 0),
    (1, 0, 1),
    (3, 0, 0),
    (2, 1, 0),
    (3, 3, 0),
    (0, 2, 1),
    (4, 0, 0),
    (4, 3, 0),
    ("embed",),
)
FORWARD_PERIOD = (
    (0, 1, 1),
    ("mix",),
    (2, 2, 0),
    ("mix",),
    (3, 1, 0),
    ("attend",),
    ("attend",),
    (2, 0, 1),
    (0, 0, 2),
    ("attend",),
    ("attend",),
    (4, 1, 0),
    (1, 1, 1),
    (1, 2, 1),
    (3, 2, 0),
    ("project",),
    ("up",),
    (1, 0, 2),
    ("up",),
    (3, 0, 1),
    (4, 2, 0),
    (2, 1, 1),
    (0, 2, 2),
    ("up",),
    ("up",),
    ("down",),
    (4, 0, 1),
    ("down",),
)
BACKWARD_PERIOD = (
    ("norm2",),
    ("down",),
    (2, 2, -1),
    ("down",),
    (1, 0, -1),
    (0, 2, 0),
    ("gelu",),
    ("gelu",),
    ("up",),
    (2, 1, -1),
    ("normed",),
    ("norm1",),
    (2, 0, -1),
    (0, 1, 0),
    (4, 1, -2),
    (4, 0, -2),
    ("attend",),
    (3, 1, -1),
    (4, 2, -2),
    (1, 2, 0),
    ("attend",),
    ("attend",),
    ("attend",),
    ("mix",),
    (1, 1, 0),
    (3, 2, -1),
    (3, 0, -1),
    ("mix",),
    (0, 0, 0),
    ("input",),
)
BACKWARD_END = (
    (2, 2, 3),
    (1, 0, 3),
    (2, 1, 3),
    ("embed",),
    (2, 0, 3),
    (4, 1, 2),
    (4, 0, 2),
    (3, 1, 3),
    (0, 3, 0),
    (4, 2, 2),
    (3, 2, 3),
    (1, 3, 0),
    (3, 0, 3),
    (2, 3, 0),
    (4, 1, 3),
    (3, 3, 0),
    (4, 0, 3),
    (4, 2, 3),
    (4, 3, 0),
)


def copies_start(copies):
    for copy in copies:
        copy.start()


def copies_wait(copies):
    for copy in copies:
        copy.wait()


class Spread:
    def __init__(self, at, out, send, recv, half=ZS // 2):
        self.at, self.out, self.send, self.recv = at, out, send, recv
        nb = at.bs - 1
        self.slot_z = 0
        self.slot_b1 = ZS - 1
        self.slot_x1 = self.slot_b1 + nb
        self.slot_x2 = self.slot_x1 + 1
        self.slot_b2 = self.slot_x2 + 1
        self.slot_c = self.slot_b2 + nb
        self.half = half

    @staticmethod
    def slots(bs):
        return ZS - 1 + 2 * (bs - 1) + 3

    def copy(self, region, slot, peer):
        return remote(region, region, self.send.at[slot], self.recv.at[slot], peer)

    def copies(self, stage, back):
        at, out, half = self.at, self.out, self.half
        rest = pl.ds(half, ZS - half)
        x_block = at.c * 2 + 1 - at.x if back else at.block
        if stage == 0:
            return [
                self.copy(
                    out.at[at.block, at.z_at(ZS - k) if back else at.z, at.b],
                    self.slot_z + k - 1,
                    at.z_peer(k),
                )
                for k in range(1, ZS)
            ]
        if stage == 3:
            core = 1 - at.c if back else at.c
            return [self.copy(out.at[pl.ds(core * 2, 2)], self.slot_c, at.core_peer)]
        copies = []
        for k in range(1, at.bs):
            b = at.b_at(at.bs - k) if back else at.b
            if stage == 1:
                region, slot = out.at[at.block, pl.ds(0, half), b], self.slot_b1
            else:
                region, slot = out.at[pl.ds(at.c * 2, 2), rest, b], self.slot_b2
            copies.append(self.copy(region, slot + k - 1, at.b_peer(k)))
        if stage == 1:
            region, slot = out.at[x_block, rest, at.b], self.slot_x1
        else:
            region, slot = out.at[x_block, pl.ds(0, half)], self.slot_x2
        copies.append(self.copy(region, slot, at.x_peer))
        return copies

    def start(self, stage):
        copies_start(self.copies(stage, False))

    def land(self, stage):
        for copy in self.copies(stage, True):
            copy.wait_recv()
        for copy in self.copies(stage, False):
            copy.wait_send()

    def move(self, stage):
        self.land(stage)
        self.start(stage + 1)


class SpreadCross(Spread):
    @staticmethod
    def slots(bs):
        return 2 * bs + 2 * ZS - 1

    def copies(self, stage, back):
        at, out = self.at, self.out
        rows = out.shape[-2]
        cut = rows // 32 * 16
        some, rest = pl.ds(0, cut), pl.ds(cut, rows - cut)
        core = 1 - at.c if back else at.c
        if stage == 3:
            return [self.copy(out.at[pl.ds(core * 2, 2)], 2 * at.bs + 2 * ZS - 2, at.core_peer)]
        both = pl.ds(at.c * 2, 2)
        x_block = at.c * 2 + 1 - at.x if back else at.block
        copies = []
        if stage == 1:
            for k in range(1, ZS):
                z = at.z_at(ZS - k) if back else at.z
                copies.append(self.copy(out.at[both, z, at.b, some], at.bs + k - 1, at.z_peer(k)))
                slot = at.bs + ZS + k - 2
                copies.append(self.copy(out.at[at.block, z, :, rest], slot, at.z_peer(k)))
            return copies
        base = 0 if stage == 0 else at.bs + 2 * ZS - 2
        for k in range(1, at.bs):
            b = at.b_at(at.bs - k) if back else at.b
            region = out.at[at.block, at.z, b, rest] if stage == 0 else out.at[both, :, b, some]
            copies.append(self.copy(region, base + k, at.b_peer(k)))
        if stage == 0:
            region = out.at[x_block, at.z, at.b, some]
        else:
            region = out.at[x_block, :, :, rest]
        copies.append(self.copy(region, base, at.x_peer))
        return copies


class Fold:
    def __init__(self, at, grads, total, landing, bufs, final, send, recv, credit, half):
        self.at, self.grads, self.total = at, grads, total
        self.landing, self.bufs, self.final = landing, bufs, final
        self.send, self.recv, self.credit = send, recv, credit
        self.half = half
        nb = at.bs - 1
        self.slot_x1 = 1
        self.slot_b1 = 2
        self.slot_x2 = 2 + nb
        self.slot_b2 = 3 + nb
        self.slot_z = 3 + 2 * nb

    @staticmethod
    def slots(bs):
        return 3 + 2 * (bs - 1) + ZS - 1

    @staticmethod
    def buffers(bs, rows, half):
        nb = max(bs - 1, 1)
        rest = ZS - half
        return [
            (half, bs, rows, LANES),
            (nb, 2, rest, rows, LANES),
            (rest, rows, LANES),
            (nb, half, rows, LANES),
            (ZS - 1, rows, LANES),
        ]

    def core_parts(self):
        other = self.grads.at[pl.ds((1 - self.at.c) * 2, 2)]
        return [(other, self.landing, 0, self.at.core_peer, self.at.core_peer)]

    def parts(self, stage):
        at, half, total, bufs = self.at, self.half, self.total, self.bufs
        if stage == 0:
            return self.core_parts()
        if stage == 3:
            return [
                (
                    total.at[at.x, at.z_at(k), at.b],
                    bufs[4].at[k - 1],
                    self.slot_z + k - 1,
                    at.z_peer(k),
                    at.z_peer(ZS - k),
                )
                for k in range(1, ZS)
            ]
        rest = pl.ds(half, ZS - half)
        found = []
        for k in range(1, at.bs):
            if stage == 1:
                src, buf, slot = total.at[:, rest, at.b_at(k)], bufs[1], self.slot_b1
            else:
                src, buf, slot = total.at[at.x, pl.ds(0, half), at.b_at(k)], bufs[3], self.slot_b2
            found.append((src, buf.at[k - 1], slot + k - 1, at.b_peer(k), at.b_peer(at.bs - k)))
        if stage == 1:
            src, buf, slot = total.at[1 - at.x, pl.ds(0, half)], bufs[0], self.slot_x1
        else:
            src, buf, slot = total.at[1 - at.x, rest, at.b], bufs[2], self.slot_x2
        found.append((src, buf, slot, at.x_peer, at.x_peer))
        return found

    def start(self, stage, again):
        for src, buf, slot, to, _ in self.parts(stage):
            if again is not False:

                @pl.when(again)
                def _():
                    pl.semaphore_wait(self.credit.at[slot], 1)

            remote(src, buf, self.send.at[slot], self.recv.at[slot], to).start()

    def land(self, stage, more):
        parts = self.parts(stage)
        for src, buf, slot, to, _ in parts:
            remote(src, buf, self.send.at[slot], self.recv.at[slot], to).wait()
        self.add(stage)
        if more is not False:

            @pl.when(more)
            def _():
                for _, _, slot, _, origin in parts:
                    pl.semaphore_signal(
                        self.credit.at[slot], inc=1, device_id=origin, device_id_type=MESH
                    )

    def add_core(self):
        at, bs, total = self.at, self.at.bs, self.total

        @pl.loop(0, 2 * ZS * bs)
        def _(i):
            z, b = i // bs % ZS, i % bs
            x = i // (ZS * bs)
            total[x, z, b] = self.grads[at.c * 2 + x, z, b] + self.landing[x, z, b]

    def add(self, stage):
        at, half, bs = self.at, self.half, self.at.bs
        total, bufs = self.total, self.bufs
        rest = ZS - half
        if stage == 0:
            self.add_core()
        elif stage == 1:

            @pl.loop(0, half * bs)
            def _(i):
                z, b = i // bs, i % bs
                total[at.x, z, b] = total[at.x, z, b] + bufs[0][z, b]

            @pl.loop(0, 2 * rest)
            def _(i):
                x, z = i // rest, i % rest
                for k in range(bs - 1):
                    total[x, half + z, at.b] = total[x, half + z, at.b] + bufs[1][k, x, z]

        elif stage == 2:

            @pl.loop(0, rest)
            def _(z):
                total[at.x, half + z, at.b] = total[at.x, half + z, at.b] + bufs[2][z]

            @pl.loop(0, half)
            def _(z):
                for k in range(bs - 1):
                    total[at.x, z, at.b] = total[at.x, z, at.b] + bufs[3][k, z]

        else:
            self.finish([bufs[4][k] for k in range(ZS - 1)])

    def finish(self, pieces):
        at = self.at
        done = self.total[at.x, at.z, at.b].astype(jnp.float32)
        for piece in pieces:
            done = done + piece.astype(jnp.float32)
        self.final[...] = done.astype(self.final.dtype)

    def move(self, stage, again, more):
        self.land(stage, more)
        self.start(stage + 1, again)


class FoldCross(Fold):
    @staticmethod
    def slots(bs):
        return 2 * bs + 2 * ZS - 1

    @staticmethod
    def buffers(bs, rows, half):
        nb = max(bs - 1, 1)
        cut = rows // 32 * 16
        rest = rows - cut
        return [
            (nb, 2, ZS, cut, LANES),
            (ZS, bs, rest, LANES),
            (ZS - 1, 2, cut, LANES),
            (ZS - 1, bs, rest, LANES),
            (cut, LANES),
            (nb, rest, LANES),
        ]

    def cuts(self):
        rows = self.total.shape[-2]
        cut = rows // 32 * 16
        return pl.ds(0, cut), pl.ds(cut, rows - cut)

    def parts(self, stage):
        at, total, bufs = self.at, self.total, self.bufs
        if stage == 0:
            return self.core_parts()
        some, rest = self.cuts()
        found = []
        if stage == 2:
            for k in range(1, ZS):
                pair = (at.z_peer(k), at.z_peer(ZS - k))
                z = at.z_at(k)
                found.append((total.at[:, z, at.b, some], bufs[2].at[k - 1], at.bs + k, *pair))
                slot = at.bs + ZS + k - 1
                found.append((total.at[at.x, z, :, rest], bufs[3].at[k - 1], slot, *pair))
            return found
        base = 1 if stage == 1 else at.bs + 2 * ZS - 1
        for k in range(1, at.bs):
            pair = (at.b_peer(k), at.b_peer(at.bs - k))
            if stage == 1:
                src, buf = total.at[:, :, at.b_at(k), some], bufs[0].at[k - 1]
            else:
                src, buf = total.at[at.x, at.z, at.b_at(k), rest], bufs[5].at[k - 1]
            found.append((src, buf, base + k, *pair))
        if stage == 1:
            src, buf = total.at[1 - at.x, :, :, rest], bufs[1]
        else:
            src, buf = total.at[1 - at.x, at.z, at.b, some], bufs[4]
        found.append((src, buf, base, at.x_peer, at.x_peer))
        return found

    def add(self, stage):
        at, bs = self.at, self.at.bs
        total, bufs = self.total, self.bufs
        some, rest = self.cuts()
        if stage == 0:
            self.add_core()
        elif stage == 1:

            @pl.loop(0, 2 * ZS)
            def _(i):
                x, z = i // ZS, i % ZS
                for k in range(bs - 1):
                    total[x, z, at.b, some] = total[x, z, at.b, some] + bufs[0][k, x, z]

            @pl.loop(0, ZS * bs)
            def _(i):
                z, b = i // bs, i % bs
                total[at.x, z, b, rest] = total[at.x, z, b, rest] + bufs[1][z, b]

        elif stage == 2:
            for x in range(2):
                for k in range(ZS - 1):
                    total[x, at.z, at.b, some] = total[x, at.z, at.b, some] + bufs[2][k, x]

            @pl.loop(0, bs)
            def _(b):
                for k in range(ZS - 1):
                    total[at.x, at.z, b, rest] = total[at.x, at.z, b, rest] + bufs[3][k, b]

        else:
            total[at.x, at.z, at.b, some] = total[at.x, at.z, at.b, some] + bufs[4][...]
            for k in range(bs - 1):
                total[at.x, at.z, at.b, rest] = total[at.x, at.z, at.b, rest] + bufs[5][k]
            self.final[...] = total[at.x, at.z, at.b]


HALF = 256
WIDE = 512
QKV_TILE = 768
VEC_ROWS = 16


STEP = 64


def by_rows(fn, *arrays, step=STEP):
    parts = [
        fn(*[array[at : at + step] for array in arrays])
        for at in range(0, arrays[0].shape[0], step)
    ]
    if isinstance(parts[0], tuple):
        return tuple(jnp.concatenate(part, axis=0) for part in zip(*parts))
    return jnp.concatenate(parts, axis=0)


def dot_nt(a, b):
    return lax.dot_general(a, b, (((1,), (1,)), ((), ())), preferred_element_type=jnp.float32)


def dot_nn(a, b):
    return lax.dot_general(a, b, (((1,), (0,)), ((), ())), preferred_element_type=jnp.float32)


def dot_tn(a, b):
    return lax.dot_general(a, b, (((0,), (0,)), ((), ())), preferred_element_type=jnp.float32)


def aligned(index, unit):
    return pl.multiple_of(index, unit)


def rows_of(ref, bs, first, count, start, rows, blocks=range(SECT)):
    parts = []
    for i in range(count):
        d = first + i
        place = (d // bs, d % bs)
        parts.append(
            jnp.concatenate(
                [ref[(lb,) + place + (pl.ds(start, rows), slice(None))] for lb in blocks], axis=1
            )
        )
    return parts[0] if count == 1 else jnp.concatenate(parts, axis=0)


def put_rows(ref, bs, first, count, start, rows, value, block=0):
    value = value.astype(ref.dtype)
    for i in range(count):
        d = first + i
        place = (d // bs, d % bs)
        for lane in range(value.shape[1] // LANES):
            ref[(block + lane,) + place + (pl.ds(start, rows), slice(None))] = value[
                i * rows : (i + 1) * rows, lane * LANES : (lane + 1) * LANES
            ]


def vector_pieces(dps):
    n_gains, n_biases = 2 * WIDE // dps, 10 * WIDE // dps
    starts = [(0, 0), (0, 2), (1, 0), (1, 2), (2, 0), (2, 1), (2, 2), (2, 3), (3, 0), (3, 2)]
    pieces = []
    for d in range(dps):
        at = 0
        while at < n_gains + n_biases:
            if at < n_gains:
                index = d * n_gains + at
                row, column = (1, 3)[index // WIDE], WIDE + index % WIDE
                left = n_gains - at
            else:
                index = d * n_biases + at - n_gains
                row, part = starts[index // WIDE]
                column = part * WIDE + index % WIDE
                left = n_gains + n_biases - at
            size = min(left, LANES - at % LANES, LANES - column % LANES)
            pieces.append((d, at // WIDE, at % WIDE, row, column, size))
            at += size
    return pieces


def read_vectors(ref, table, bs, start):
    dps = ZS * bs
    tiles = {}
    for d, row, lane, to_row, to_lane, size in vector_pieces(dps):
        key = (d, lane // LANES)
        if key not in tiles:
            tile = ref[lane // LANES, d // bs, d % bs, start : start + VEC_ROWS, :]
            tiles[key] = tile.astype(jnp.float32)
        off = lane % LANES
        table[to_row : to_row + 1, to_lane : to_lane + size] = tiles[key][
            row : row + 1, off : off + size
        ]


def write_vectors(ref, table, bs, start):
    dps = ZS * bs
    found = {}
    for d, row, lane, to_row, to_lane, size in vector_pieces(dps):
        piece = table[to_row : to_row + 1, to_lane : to_lane + size]
        found.setdefault((d, lane // LANES), {}).setdefault(row, []).append(piece)
    row_id = lax.broadcasted_iota(jnp.int32, (VEC_ROWS, LANES), 0)
    for d in range(dps):
        for lb in range(SECT):
            tile = jnp.zeros((VEC_ROWS, LANES), jnp.float32)
            for row, pieces in found.get((d, lb), {}).items():
                have = sum(piece.shape[1] for piece in pieces)
                if have < LANES:
                    pieces = pieces + [jnp.zeros((1, LANES - have), jnp.float32)]
                line = pieces[0] if len(pieces) == 1 else jnp.concatenate(pieces, axis=1)
                tile = jnp.where(row_id == row, line, tile)
            ref[lb, d // bs, d % bs, start : start + VEC_ROWS, :] = tile.astype(ref.dtype)


def fold_rows(x):
    total = x[:8]
    for at in range(8, x.shape[0], 8):
        total = total + x[at : at + 8]
    return total


def normalize(x):
    mean = jnp.mean(x, axis=1, keepdims=True)
    centred = x - mean
    scale = lax.rsqrt(jnp.mean(centred * centred, axis=1, keepdims=True) + NORM_EPS)
    return centred * scale, jnp.broadcast_to(scale, (x.shape[0], LANES))


def normalize_back(unit, scale, grad, gain):
    inner = grad * gain
    first = jnp.mean(inner, axis=1, keepdims=True)
    second = jnp.mean(inner * unit, axis=1, keepdims=True)
    out = jnp.concatenate([scale] * (WIDE // LANES), axis=1) * (inner - first - unit * second)
    return out, fold_rows(out), fold_rows(grad * unit), fold_rows(grad)


def gelu_pair(u):
    below = 0.5 + 0.5 * lax.erf(u * math.sqrt(0.5))
    bell = jnp.exp2((-0.5 * math.log2(math.e)) * (u * u))
    return u * below, below + u * (bell * (1.0 / math.sqrt(2.0 * math.pi)))


def head_masks(scale):
    lane = lax.broadcasted_iota(jnp.int32, (1, LANES), 1)
    first = jnp.where(lane < HEAD, scale, 0.0).astype(jnp.bfloat16)
    second = jnp.where(lane < HEAD, 0.0, scale).astype(jnp.bfloat16)
    return first, second


class Sizes:
    def __init__(self, dps):
        self.dps, self.bs = dps, dps // ZS
        self.qkv, self.out, self.up, self.down = (
            3 * WIDE // dps,
            WIDE // dps,
            4 * WIDE // dps,
            WIDE // dps,
        )
        self.att = self.qkv + VEC_ROWS
        self.dense = self.out + self.up
        self.wide = 4 * self.down


def qkv_rows(size, w, tile):
    count = QKV_TILE // size.qkv
    return rows_of(w, size.bs, tile * count, count, 0, size.qkv)


def out_rows(size, w):
    return rows_of(w, size.bs, 0, size.dps, 0, size.out)


def up_rows(size, w, tile):
    count = HALF // size.up
    return rows_of(w, size.bs, tile * count, count, size.out, size.up)


def forward_mix(size, w, table, h, mixed, piece):
    columns = slice(piece * QKV_TILE, (piece + 1) * QKV_TILE)
    shift = table[0:1, columns]
    out = dot_nt(h[...], qkv_rows(size, w, piece))
    mixed[:, columns] = by_rows(lambda part: (part + shift).astype(mixed.dtype), out)


def softmax_columns(scores):
    parts = [scores[at : at + STEP] for at in range(0, scores.shape[0], STEP)]
    top = parts[0]
    for part in parts[1:]:
        top = jnp.maximum(top, part)
    top = jnp.max(top, axis=0, keepdims=True)
    parts = [jnp.exp(part - top) for part in parts]
    total = parts[0]
    for part in parts[1:]:
        total = total + part
    scale = 1.0 / jnp.sum(total, axis=0, keepdims=True)
    return jnp.concatenate([(part * scale).astype(jnp.bfloat16) for part in parts], axis=0)


def forward_attend(mixed, probs, attended, pair):
    lane = pair * LANES
    key_rows = mixed[:, WIDE + lane : WIDE + lane + LANES]
    values = mixed[:, 2 * WIDE + lane : 2 * WIDE + lane + LANES].T

    for part in range(2):
        rows = slice(part * HALF, (part + 1) * HALF)
        queries = mixed[rows, lane : lane + LANES]
        joined = []
        for head, mask in enumerate(head_masks(1.0 / math.sqrt(HEAD))):
            weights = softmax_columns(dot_nt(key_rows, queries * mask))
            probs[2 * pair + head, :, rows] = weights
            joined.append(dot_nn(values[head * HEAD : (head + 1) * HEAD], weights))
        joined = jnp.concatenate(joined, axis=0).T
        attended[rows, lane : lane + LANES] = joined.astype(attended.dtype)


def forward_project(size, w, table, h, attended, first, scale, normed):
    out = dot_nt(attended[...], out_rows(size, w))
    for part in range(WIDE // STEP):
        rows = slice(part * STEP, (part + 1) * STEP)
        total = h[rows, :].astype(jnp.float32) + (out[rows] + table[1:2, 0:WIDE])
        unit, scale[rows, :] = normalize(total)
        first[rows, :] = unit
        normed[rows, :] = (
            unit * table[1:2, WIDE : 2 * WIDE] + table[1:2, 2 * WIDE : 3 * WIDE]
        ).astype(normed.dtype)


def forward_up(size, w, table, normed, slope, hidden, piece):
    for j in (2 * piece, 2 * piece + 1):
        columns = slice(j * HALF, (j + 1) * HALF)
        shift = table[2:3, columns]
        upper = dot_nt(normed[...], up_rows(size, w, j))
        for part in range(WIDE // STEP):
            rows = slice(part * STEP, (part + 1) * STEP)
            value, grad = gelu_pair(upper[rows] + shift)
            hidden[rows, columns] = value.astype(hidden.dtype)
            slope[rows, columns] = grad.astype(slope.dtype)


def forward_down(size, w, table, normed, hidden, second, scale, h, piece):
    columns = slice(piece * HALF, (piece + 1) * HALF)
    count = size.dps // 2
    matrix = jnp.concatenate(
        [
            rows_of(w, size.bs, piece * count, count, j * size.down, size.down)
            for j in range(4)
        ],
        axis=1,
    )
    out = dot_nt(hidden[...], matrix)
    shift = table[3:4, columns]
    for part in range(WIDE // STEP):
        rows = slice(part * STEP, (part + 1) * STEP)
        second[rows, columns] = normed[rows, columns].astype(jnp.float32) + (out[rows] + shift)
    if piece == 1:
        for part in range(WIDE // STEP):
            rows = slice(part * STEP, (part + 1) * STEP)
            unit, scale[rows, :] = normalize(second[rows, :])
            second[rows, :] = unit
            h[rows, :] = (
                unit * table[3:4, WIDE : 2 * WIDE] + table[3:4, 2 * WIDE : 3 * WIDE]
            ).astype(h.dtype)


def backward_norm_two(table, dtable, dy, second, scale, dnormed, dlow, dlow_t):
    dtable[...] = jnp.zeros_like(dtable)
    sums = [jnp.zeros((8, WIDE), jnp.float32)] * 3
    for part in range(WIDE // STEP):
        rows = slice(part * STEP, (part + 1) * STEP)
        grad, *found = normalize_back(
            second[rows, :],
            scale[rows, :],
            dy[rows, :].astype(jnp.float32),
            table[3:4, WIDE : 2 * WIDE],
        )
        dnormed[rows, :] = grad
        dlow[rows, :] = grad.astype(dlow.dtype)
        sums = [total + new for total, new in zip(sums, found)]
    for i, total in enumerate(sums):
        dtable[3:4, i * WIDE : (i + 1) * WIDE] = jnp.sum(total, axis=0, keepdims=True)
    dlow_t[...] = dlow[...].T


def backward_down(size, grads, hidden, dlow_t, piece):
    @pl.loop(2 * piece, 2 * piece + 2)
    def _(i):
        start = aligned(i * size.down, 16)
        for half in range(2):
            columns = pl.ds(aligned(i * WIDE, WIDE) + half * HALF, HALF)
            value = dot_nn(dlow_t[...], hidden[:, columns])
            put_rows(grads, size.bs, 0, size.dps, start, size.down, value, 2 * half)


def backward_gelu(size, w, dtable, slope, dlow, dup, piece):
    @pl.loop(2 * piece, 2 * piece + 2)
    def _(i):
        start = aligned(i * size.down, 16)
        for half in range(2):
            columns = pl.ds(aligned(i * WIDE, WIDE) + half * HALF, HALF)
            blocks = (2 * half, 2 * half + 1)
            matrix = rows_of(w, size.bs, 0, size.dps, start, size.down, blocks)
            dhidden = dot_nn(dlow[...], matrix)
            total = jnp.zeros((8, HALF), jnp.float32)
            for part in range(WIDE // STEP):
                rows = slice(part * STEP, (part + 1) * STEP)
                dupper = dhidden[rows] * slope[rows, columns].astype(jnp.float32)
                total = total + fold_rows(dupper)
                dup[rows, columns] = dupper.astype(dup.dtype)
            dtable[2:3, columns] = jnp.sum(total, axis=0, keepdims=True)


def backward_up(size, grads, normed, dup):
    count = HALF // size.up

    @pl.loop(0, 4)
    def _(i):
        for half in range(2):
            columns = pl.ds(aligned(i * WIDE, WIDE) + half * HALF, HALF)
            value = dot_tn(dup[:, columns], normed[...])
            first = (2 * i + half) * count
            put_rows(grads, size.bs, first, count, size.out, size.up, value)


def backward_normed(size, w, dnormed, dup):
    for half in range(2):
        columns = slice(half * HALF, (half + 1) * HALF)
        blocks = (2 * half, 2 * half + 1)
        matrix = rows_of(w, size.bs, 0, size.dps, size.out, size.up, blocks)
        out = dot_nn(dup[...], matrix)
        for part in range(WIDE // STEP):
            rows = slice(part * STEP, (part + 1) * STEP)
            dnormed[rows, columns] = dnormed[rows, columns] + out[rows]


def backward_norm_one(
    size, w, table, grads, dtable, first, scale, attended, dnormed, dlow, dlow_t, delta
):
    sums = [jnp.zeros((8, WIDE), jnp.float32)] * 3
    for part in range(WIDE // STEP):
        rows = slice(part * STEP, (part + 1) * STEP)
        grad, *found = normalize_back(
            first[rows, :], scale[rows, :], dnormed[rows, :], table[1:2, WIDE : 2 * WIDE]
        )
        dnormed[rows, :] = grad
        dlow[rows, :] = grad.astype(dlow.dtype)
        sums = [total + new for total, new in zip(sums, found)]
    for i, total in enumerate(sums):
        dtable[1:2, i * WIDE : (i + 1) * WIDE] = jnp.sum(total, axis=0, keepdims=True)
    dlow_t[...] = dlow[...].T
    for block in (0, 2):
        columns = slice(block * LANES, (block + 2) * LANES)
        value = dot_nn(dlow_t[...], attended[:, columns])
        put_rows(grads, size.bs, 0, size.dps, 0, size.out, value, block)
    grad = dot_nn(dlow[...], out_rows(size, w)).astype(dlow.dtype)
    dlow[...] = grad
    product = grad.astype(jnp.float32) * attended[...].astype(jnp.float32)
    high = product.astype(jnp.bfloat16)
    rest = (product - high.astype(jnp.float32)).astype(jnp.bfloat16)
    head = lax.broadcasted_iota(jnp.int32, delta.shape, 0)
    lane = lax.broadcasted_iota(jnp.int32, delta.shape, 1)
    inside = (lane >= head * HEAD) & (lane < (head + 1) * HEAD)
    inside = jnp.where(inside, 1.0, 0.0).astype(jnp.bfloat16)
    delta[...] = dot_nt(inside, high) + dot_nt(inside, rest)


def backward_attend(mixed, probs, delta, dtable, dlow, dmixed, pair):
    scale = 1.0 / math.sqrt(HEAD)
    lane = pair * LANES
    columns = slice(lane, lane + LANES)
    key_columns = slice(WIDE + lane, WIDE + lane + LANES)
    value_columns = slice(2 * WIDE + lane, 2 * WIDE + lane + LANES)
    keys_t = mixed[:, key_columns].T
    values = mixed[:, value_columns]
    dkeys = jnp.zeros((WIDE, LANES), jnp.float32)
    dvalues = jnp.zeros((WIDE, LANES), jnp.float32)
    for part in range(2):
        rows = slice(part * HALF, (part + 1) * HALF)
        queries = mixed[rows, columns]
        grad_out = dlow[rows, columns]
        dqueries = []
        for head in range(2):
            query = queries * head_masks(scale)[head]
            grad = grad_out * head_masks(1.0)[head]
            at = 2 * pair + head
            weights = probs[at, :, rows]
            less = delta[at : at + 1, rows]
            dprobs = dot_nt(values, grad)
            dscores = by_rows(
                lambda p, dp: (p.astype(jnp.float32) * (dp - less)).astype(jnp.bfloat16),
                weights,
                dprobs,
            )
            dvalues = dvalues + dot_nn(weights, grad)
            dkeys = dkeys + dot_nn(dscores, query)
            dqueries.append(dot_nn(keys_t[head * HEAD : (head + 1) * HEAD], dscores))
        dquery = jnp.concatenate(dqueries, axis=0).T * scale
        dtable[0:1, columns] += jnp.sum(dquery, axis=0, keepdims=True)
        dmixed[rows, columns] = dquery.astype(dmixed.dtype)
    dmixed[:, key_columns] = dkeys.astype(dmixed.dtype)
    dmixed[:, value_columns] = dvalues.astype(dmixed.dtype)
    dtable[0:1, value_columns] = jnp.sum(dvalues, axis=0, keepdims=True)


def backward_mix(size, grads, h, dmixed, piece):
    count = QKV_TILE // size.qkv
    grad = dmixed[:, piece * QKV_TILE : (piece + 1) * QKV_TILE]
    put_rows(grads, size.bs, piece * count, count, 0, size.qkv, dot_tn(grad, h[...]))


def backward_input(size, w, dnormed, dmixed, dy):
    for half in range(2):
        columns = slice(half * HALF, (half + 1) * HALF)
        blocks = (2 * half, 2 * half + 1)
        matrix = rows_of(w, size.bs, 0, size.dps, 0, size.qkv, blocks)
        out = dot_nn(dmixed[...], matrix)
        for part in range(WIDE // STEP):
            rows = slice(part * STEP, (part + 1) * STEP)
            dy[rows, columns] = (dnormed[rows, columns] + out[rows]).astype(dy.dtype)


WINDOW = 384


def group_rows(group):
    rows = lax.broadcasted_iota(jnp.int32, (16, LANES), 0)
    return jnp.where(rows == group, 1.0, 0.0).astype(jnp.bfloat16)


def pack_mix(piece, qkv, gains, biases):
    low = piece.dtype
    rows = qkv.shape[0]
    flat = jnp.concatenate([gains[...], biases[...]], axis=1)
    flat = jnp.concatenate([flat, jnp.zeros((1, 2 * WIDE - flat.shape[1]), flat.dtype)], axis=1)
    row_id = lax.broadcasted_iota(jnp.int32, (VEC_ROWS, LANES), 0)
    for lb in range(SECT):
        lane = lb * LANES
        piece[lb, :rows] = qkv[:, lane : lane + LANES].astype(low)
        tile = jnp.where(row_id == 0, flat[:, lane : lane + LANES], 0.0)
        lane += WIDE
        tile = jnp.where(row_id == 1, flat[:, lane : lane + LANES], tile)
        piece[lb, rows:] = tile.astype(low)


def pack_up(piece, out, up):
    rows = out.shape[0]
    for lb in range(SECT):
        lanes = slice(lb * LANES, (lb + 1) * LANES)
        piece[lb, :rows] = out[:, lanes].astype(piece.dtype)
        piece[lb, rows:] = up[:, lanes].astype(piece.dtype)


def pack_down(piece, down):
    rows = down.shape[0]
    for lb in range(SECT):
        for j in range(4):
            start = j * WIDE + lb * LANES
            piece[lb, j * rows : (j + 1) * rows] = down[:, start : start + LANES].astype(piece.dtype)


def pack_embedding(piece, weight, shift, square):
    n = weight.shape[0]
    square[...] = jnp.zeros_like(square)
    square[:GROUPS, :n] = shift[...]

    def ending(part, width):
        return jnp.concatenate([jnp.zeros((n, width - part.shape[1]), part.dtype), part], axis=1)

    parts = [
        square[...].T[:n],
        ending(weight[:, L1 + L2 :], 3 * LANES),
        ending(weight[:, L1 : L1 + L2], 2 * LANES),
        ending(weight[:, :L1], 2 * LANES),
    ]
    columns = jnp.concatenate(parts, axis=1).astype(piece.dtype)
    for lb in range(SECT):
        for part in range(2):
            start = part * WIDE + lb * LANES
            piece[lb, part * n : (part + 1) * n] = columns[:, start : start + LANES]


def expand(series, group, x):
    empty = jnp.zeros((WINDOW - series.shape[0], series.shape[1]), series.dtype)
    x[:, :WINDOW] = jnp.concatenate([empty, series[...]], axis=0).T
    lane = lax.broadcasted_iota(jnp.int32, (x.shape[0], LANES), 1)
    x[:, WINDOW:] = jnp.where(lane == group, 1.0, 0.0).astype(x.dtype)


def embed(size, emb, pick, x, wsel, h):
    rows = WIDE // size.dps
    first = rows_of(emb, size.bs, 0, size.dps, 0, rows)
    second = rows_of(emb, size.bs, 0, size.dps, rows, rows)
    long, middle, short = (pick[g : g + 1, :] for g in (2, 1, 0))
    wide = jnp.concatenate(
        [
            first[:, LANES : 2 * LANES] * long,
            first[:, 2 * LANES : 3 * LANES] * long + second[:, :LANES] * middle,
            first[:, 3 * LANES :] * long
            + second[:, LANES : 2 * LANES] * middle
            + second[:, 3 * LANES :] * short,
        ],
        axis=1,
    )
    wsel[...] = wide.T
    matrix = jnp.concatenate([wide, first[:, :LANES]], axis=1)
    h[...] = dot_nt(x[...], matrix).astype(h.dtype)


def embed_back(size, pick, x, wsel, dh, grads, series_grad):
    history = series_grad.shape[0]
    series_grad[...] = dot_nt(wsel[...], dh[...])[WINDOW - history :]
    sums = dot_tn(dh[...], x[...])
    long, middle, short = (pick[g : g + 1, :].astype(jnp.float32) for g in (2, 1, 0))
    parts = [sums[:, i * LANES : (i + 1) * LANES] for i in range(4)]
    parts = [
        parts[3],
        parts[0] * long,
        parts[1] * long,
        parts[2] * long,
        parts[1] * middle,
        parts[2] * middle,
        jnp.zeros_like(parts[0]),
        parts[2] * short,
    ]
    rows = WIDE // (SECT * size.dps)
    for pipe in range(SECT):
        block = (pipe % 2) * 2 + pipe // 2
        for dp in range(size.dps):
            start = (pipe * size.dps + dp) * rows
            piece = jnp.concatenate([part[start : start + rows] for part in parts], axis=0)
            grads[block, dp // size.bs, dp % size.bs] = piece.astype(grads.dtype)


def saved_shapes():
    low, wide = jnp.bfloat16, jnp.float32
    return [
        ((WIDE, WIDE), low),
        ((WIDE, 3 * WIDE), low),
        ((2 * SECT, 1, LANES), wide),
        ((WIDE, WIDE), low),
        ((WIDE, WIDE), wide),
        ((WIDE, WIDE), low),
        ((WIDE, 4 * WIDE), low),
        ((WIDE, 4 * WIDE), low),
        ((WIDE, WIDE), wide),
        ((SECT, 4 * WIDE), wide),
        ((WIDE, LANES), wide),
        ((WIDE, LANES), wide),
        ((2 * SECT, WIDE, WIDE), low),
    ]


def chunk_shape(size, rows):
    return (SECT, ZS, size.bs, rows, LANES)


HALVES = (2, 2, 2, 2)
CROSS = (2,)


def follow(plan, section, act, compute):
    seen = {}
    for step in plan:
        if len(step) == 1:
            piece = seen.get(step[0], 0)
            seen[step[0]] = piece + 1
            compute(step[0], piece)
            continue
        op, kind, offset = step
        where = section + offset
        if isinstance(where, int):
            if 0 <= where < SECT:
                act(op, kind, where)
        elif offset == 0:
            act(op, kind, where)
        else:
            inside = where < SECT if offset > 0 else where >= 0

            @pl.when(inside)
            def _():
                act(op, kind, where)


def forward_kernel(dps, groups, *refs):
    size = Sizes(dps)
    given, refs = refs[:9], refs[9:]
    out, wholes, wsel, x, refs = refs[0], refs[1:5], refs[5], refs[6], refs[7:]
    kept, local, refs = refs[:13], refs[13:26], refs[26:]
    buffers, refs = refs[:4], refs[4:]
    pieces, held, refs = refs[:4], refs[4:13], refs[13:]
    emb_rows, pick, refs = refs[0], refs[1], refs[2:]
    given_sem, w_sem, kept_sem, own_sem, p_send, p_recv, send, recv = refs
    h, mixed, lse, attended, first, normed, slope, hidden, second, table, scale_1, scale_2, probs = local
    at = Place(dps)

    own = [
        pltpu.make_async_copy(
            pieces[kind].at[at.block],
            wholes[kind].at[at.pipe, at.block, at.z, at.b]
            if kind < EMB
            else wholes[kind].at[at.block, at.z, at.b],
            own_sem.at[kind],
        )
        for kind in range(4)
    ]
    def split(kind, back):
        copies = []
        for k in range(1, SECT):
            if back:
                region = wholes[kind].at[at.pipe_at(SECT - k), at.block, at.z, at.b]
                src = region
            else:
                block = at.block_of(at.pipe_at(k))
                region = wholes[kind].at[at.pipe, block, at.z, at.b]
                src = pieces[kind].at[block]
            sems = p_send.at[kind, k - 1], p_recv.at[kind, k - 1]
            copies.append(remote(src, region, *sems, (at.pipe_at(k), at.dp)))
        return copies

    def chunk(kind, section):
        if kind == EMB:
            return Spread(at, wholes[kind], send.at[3 * SECT], recv.at[3 * SECT])
        number = 3 * section + kind
        sort = SpreadCross if kind in CROSS else Spread
        return sort(at, wholes[kind].at[section], send.at[number], recv.at[number], HALVES[kind])

    def load(kind, section, core):
        blocks = pl.ds(core * 2, 2)
        src, dst = wholes[kind], buffers[kind]
        if kind != EMB:
            src, dst = src.at[section], dst.at[section % 2]
        sem = w_sem.at[kind, section % 2, core]
        return pltpu.make_async_copy(src.at[blocks], dst.at[blocks], sem)

    def loaded(kind, section):
        load(kind, section, at.c).wait()
        load(kind, section, 1 - at.c).wait()

    arrived = []

    def act(op, kind, section):
        if op == 0:
            if kind not in arrived:
                arrived.append(kind)
                own[kind].wait()
                if kind == EMB:
                    chunk(kind, section).start(0)
                    return
                for copy in split(kind, True):
                    copy.wait_recv()
                for copy in split(kind, False):
                    copy.wait_send()
                if kind == 0:
                    copies_start(split(1, False))
                    copies_start(split(2, False))
            chunk(kind, section).start(0)
        elif op < 4:
            chunk(kind, section).move(op - 1)
            if op == 3:
                load(kind, section, at.c).start()
        else:
            chunk(kind, section).land(3)
            load(kind, section, 1 - at.c).start()

    def saves(section, early):
        which = (1, 3, 4, 5, 9, 10, 12) if early else (6, 7, 8, 11)
        return [
            pltpu.make_async_copy(local[i], kept[i].at[section], kept_sem.at[i]) for i in which
        ]

    series, embed_weight, embed_bias, qkv, out_w, up_w, down_w, gains, biases = held
    gets = copies_of(zip(given, held), given_sem)
    for i in (3, 7, 8, 1, 2, 4, 5, 6, 0):
        gets[i].start()
    pick[...] = group_rows(groups[0])
    at.greet()
    copies_wait([gets[i] for i in (3, 7, 8)])
    pack_mix(pieces[0], qkv, gains, biases)
    own[0].start()
    at.met()
    copies_start(split(0, False))
    copies_wait(gets[1:3])
    pack_embedding(pieces[EMB], embed_weight, embed_bias, emb_rows)
    own[EMB].start()
    copies_wait(gets[4:7])
    pack_up(pieces[1], out_w, up_w)
    own[1].start()
    pack_down(pieces[2], down_w)
    own[2].start()
    table[...] = jnp.zeros_like(table)
    gets[0].wait()
    expand(series, groups[0], x)

    def before(name, piece):
        loaded(EMB, 0)
        embed(size, buffers[EMB], pick, x, wsel, h)

    follow(FORWARD_START, 0, act, before)

    @pl.loop(0, SECT)
    def _(section):
        att, up, down = (ref.at[section % 2] for ref in buffers[:3])
        keep_h = pltpu.make_async_copy(h, kept[0].at[section], kept_sem.at[0])

        def compute(name, piece):
            if name == "mix":
                if piece == 0:

                    @pl.when(section > 0)
                    def _():
                        copies_wait(saves(section - 1, True))

                    keep_h.start()
                    loaded(0, section)
                    read_vectors(att, table, size.bs, size.qkv)
                forward_mix(size, att, table, h, mixed, piece)
            elif name == "attend":
                forward_attend(mixed, probs, attended, piece)
            elif name == "project":
                loaded(1, section)
                forward_project(size, up, table, h, attended, first, scale_1, normed)
                copies_start(saves(section, True))
            elif name == "up":
                if piece == 0:

                    @pl.when(section > 0)
                    def _():
                        copies_wait(saves(section - 1, False))

                forward_up(size, up, table, normed, slope, hidden, piece)
            else:
                if piece == 0:
                    loaded(2, section)
                    keep_h.wait()
                forward_down(size, down, table, normed, hidden, second, scale_2, h, piece)
                if piece == 1:
                    copies_start(saves(section, False))

        follow(FORWARD_PERIOD, section, act, compute)

    out[...] = h[...]
    copies_wait(saves(SECT - 1, True))
    copies_wait(saves(SECT - 1, False))


def copies_of(pairs, sems):
    return [pltpu.make_async_copy(src, dst, sems.at[i]) for i, (src, dst) in enumerate(pairs)]


def forward_all(groups, given, dps):
    size = Sizes(dps)
    low, wide = jnp.bfloat16, jnp.float32
    shapes = saved_shapes()
    rows = (size.att, size.dense, size.wide, 2 * WIDE // dps)
    chunks = [chunk_shape(size, count) for count in rows]
    anywhere = pl.BlockSpec(memory_space=pl.ANY)
    inside = pl.BlockSpec(memory_space=pltpu.VMEM)
    outs = [((WIDE, WIDE), low)]
    outs += [((SECT,) + shape, low) for shape in chunks[:3]] + [(chunks[3], low)]
    outs += [((WINDOW, WIDE), low), ((WIDE, WIDE), low)]
    outs += [((SECT,) + shape, dtype) for shape, dtype in shapes]
    scratch = shapes + [((2,) + shape, low) for shape in chunks[:3]] + [(chunks[3], low)]
    scratch += [((SECT, count, LANES), low) for count in rows]
    scratch += [(array.shape, array.dtype) for array in given]
    scratch += [((LANES, LANES), wide), ((16, LANES), low)]
    slots = max(Spread.slots(size.bs), SpreadCross.slots(size.bs))
    dma = pltpu.SemaphoreType.DMA
    return pl.pallas_call(
        partial(forward_kernel, dps),
        out_shape=[jax.ShapeDtypeStruct(shape, dtype) for shape, dtype in outs],
        in_specs=[pl.BlockSpec(memory_space=pltpu.SMEM)] + [anywhere] * len(given),
        out_specs=[inside] + [anywhere] * 4 + [inside] * 2 + [anywhere] * len(shapes),
        scratch_shapes=[pltpu.VMEM(shape, dtype) for shape, dtype in scratch]
        + [
            dma((len(given),)),
            dma((4, 2, 2)),
            dma((len(shapes),)),
            dma((4,)),
            dma((3, SECT - 1)),
            dma((3, SECT - 1)),
            dma((1 + 3 * SECT, slots)),
            dma((1 + 3 * SECT, slots)),
        ],
        compiler_params=pltpu.CompilerParams(
            collective_id=0, has_side_effects=True, vmem_limit_bytes=60 * 1024 * 1024
        ),
        name="gather_forward",
    )(groups, *given)


FETCHES = {
    ("norm2", 0): (("second", "scale_2"), ("second", "scale_2")),
    ("down", 0): (("hidden",), ()),
    ("down", 1): ((), ("hidden",)),
    ("gelu", 0): (("slope", 2), ()),
    ("gelu", 1): ((), ("slope", 2)),
    ("up", 0): (("normed",), ("normed",)),
    ("normed", 0): ((1,), ()),
    ("norm1", 0): (("first", "scale_1", "attended"), ("first", "scale_1", "attended", 1)),
    ("attend", 0): (("mixed", "probs"), ()),
    ("attend", 3): ((), ("mixed", "probs")),
    ("mix", 0): (("h",), ()),
    ("mix", 1): ((), ("h",)),
    ("input", 0): ((0,), (0,)),
}


def backward_kernel(dps, groups, att, up, down, cotangent, x_in, wsel_in, *refs):
    size = Sizes(dps)
    kept, refs = refs[:13], refs[13:]
    series_grad, outs, refs = refs[0], refs[1:5], refs[5:]
    local, refs = refs[:12], refs[12:]
    tables, w_att, w_up, w_down, dtable, dy, dnormed, dlow, dlow_t, dmixed, dup = refs[:11]
    x, wsel, pick, delta, refs = *refs[11:15], refs[15:]
    kinds = []
    for kind in range(4):
        count = 6 if kind in CROSS else 5
        kinds.append(refs[:4] + (refs[4 : 4 + count],))
        refs = refs[4 + count :]
    w_sem, kept_sem, table_sem, late_sem, out_sem, p_send, p_recv, send, recv, credit = refs
    h, mixed, lse, attended, first, normed, slope, hidden, second, scale_1, scale_2, probs = local
    at = Place(dps)
    last = SECT - 1

    def weights(kind, section):
        src, dst = ((att, w_att), (up, w_up), (down, w_down))[kind]
        return pltpu.make_async_copy(src.at[section], dst, w_sem.at[kind])

    names = ("h", "mixed", "lse", "attended", "first", "normed", "slope", "hidden", "second")
    names += ("table", "scale_1", "scale_2", "probs")
    held = dict(zip(names[:9] + names[10:], local))

    def fetches(section, *wanted):
        found = []
        for name in wanted:
            if isinstance(name, int):
                found.append(weights(name, section))
            else:
                i = names.index(name)
                dst = held[name]
                found.append(pltpu.make_async_copy(kept[i].at[section], dst, kept_sem.at[i]))
        return found

    def chunk(kind, i):
        grads, totals, finals, landing, bufs = kinds[kind]
        sort = FoldCross if kind in CROSS else Fold
        refs = (grads, totals.at[i % 2], landing, bufs, finals.at[i])
        return sort(at, *refs, send.at[kind], recv.at[kind], credit.at[kind], HALVES[kind])

    def hand_over(kind, i):
        landing = outs[kind].at[at.block]
        final = kinds[kind][2].at[i]
        return (
            pltpu.make_async_copy(final, landing, out_sem.at[kind]),
            remote(final, landing, p_send.at[kind, i], p_recv.at[kind, at.pipe], (last - i, at.dp)),
        )

    def act(op, kind, i):
        again, more = (False, False) if kind == EMB else (i > 0, i < last)
        if op == 0:
            chunk(kind, i).start(0, again)
        elif op < 4:
            chunk(kind, i).move(op - 1, again, more)
        else:
            chunk(kind, i).land(3, more)
            if kind == EMB:
                outs[kind][...] = kinds[kind][2][0]
            else:
                here, away = hand_over(kind, i)

                @pl.when(at.pipe == last - i)
                def _():
                    here.start()

                @pl.when(at.pipe != last - i)
                def _():
                    away.start()

    copies_start(fetches(last, "second", "scale_2", "hidden", "slope", 2, "normed", 1))
    get_tables = pltpu.make_async_copy(kept[9], tables, table_sem)
    get_tables.start()
    copies_start(fetches(last, "first", "scale_1", "attended", "mixed", "probs", "h", 0))
    late = copies_of(((cotangent, dy), (x_in, x), (wsel_in, wsel)), late_sem)
    copies_start(late)
    pick[...] = group_rows(groups[0])
    at.greet()
    at.met()
    get_tables.wait()
    late[0].wait()

    @pl.loop(0, SECT)
    def _(i):
        section = last - i
        table = tables.at[section]

        def compute(name, piece):
            need, free = FETCHES.get((name, piece), ((), ()))
            copies_wait(fetches(section, *need))
            if name == "norm2":
                backward_norm_two(table, dtable, dy, second, scale_2, dnormed, dlow, dlow_t)
            elif name == "down":
                backward_down(size, kinds[2][0], hidden, dlow_t, piece)
            elif name == "gelu":
                backward_gelu(size, w_down, dtable, slope, dlow, dup, piece)
            elif name == "up":
                backward_up(size, kinds[1][0], normed, dup)
            elif name == "normed":
                backward_normed(size, w_up, dnormed, dup)
            elif name == "norm1":
                backward_norm_one(
                    size,
                    w_up,
                    table,
                    kinds[1][0],
                    dtable,
                    first,
                    scale_1,
                    attended,
                    dnormed,
                    dlow,
                    dlow_t,
                    delta,
                )
            elif name == "attend":
                backward_attend(mixed, probs, delta, dtable, dlow, dmixed, piece)
            elif name == "mix":
                backward_mix(size, kinds[0][0], h, dmixed, piece)
                if piece == 1:
                    write_vectors(kinds[0][0], dtable, size.bs, size.qkv)
            else:
                backward_input(size, w_att, dnormed, dmixed, dy)
            if free:

                @pl.when(section > 0)
                def _():
                    copies_start(fetches(section - 1, *free))

        follow(BACKWARD_PERIOD, i, act, compute)

    def after(name, piece):
        copies_wait(late[1:])
        embed_back(size, pick, x, wsel, dy, kinds[EMB][0], series_grad)

    follow(BACKWARD_END, 0, act, after)

    for kind in range(3):
        for i in range(SECT):
            here, away = hand_over(kind, i)

            @pl.when(at.pipe == last - i)
            def _():
                here.wait()

            @pl.when(at.pipe != last - i)
            def _():
                away.wait_send()

        for k in range(1, SECT):
            other = at.pipe_at(k)
            landing = outs[kind].at[at.block_of(other)]
            sems = p_send.at[kind, 0], p_recv.at[kind, other]
            remote(landing, landing, *sems, (other, at.dp)).wait_recv()


def backward_all(groups, weights, cotangent, x, wsel, kept, history, dps):
    size = Sizes(dps)
    low, wide = jnp.bfloat16, jnp.float32
    anywhere = pl.BlockSpec(memory_space=pl.ANY)
    inside = pl.BlockSpec(memory_space=pltpu.VMEM)
    shapes = saved_shapes()
    rows_emb = 8 * WIDE // (SECT * dps)
    kind_rows = (size.att, size.dense, size.wide, rows_emb)
    scratch = shapes[:9] + shapes[10:] + [((SECT,) + shapes[9][0], wide)]
    scratch += [(chunk_shape(size, rows), low) for rows in kind_rows[:3]]
    scratch += [
        (shapes[9][0], wide),
        ((WIDE, WIDE), low),
        ((WIDE, WIDE), wide),
        ((WIDE, WIDE), low),
        ((WIDE, WIDE), low),
        ((WIDE, 3 * WIDE), low),
        ((WIDE, 4 * WIDE), low),
        ((WIDE, WIDE), low),
        ((WINDOW, WIDE), low),
        ((16, LANES), low),
        ((16, WIDE), wide),
    ]
    for kind, rows in enumerate(kind_rows):
        sets, results = (1, 1) if kind == EMB else (2, SECT)
        scratch += [
            (chunk_shape(size, rows), low),
            ((sets, 2, ZS, size.bs, rows, LANES), low),
            ((results, rows, LANES), low),
            ((2, ZS, size.bs, rows, LANES), low),
        ]
        sort = FoldCross if kind in CROSS else Fold
        scratch += [(shape, low) for shape in sort.buffers(size.bs, rows, HALVES[kind])]
    slots = max(Fold.slots(size.bs), FoldCross.slots(size.bs))
    dma = pltpu.SemaphoreType.DMA
    return pl.pallas_call(
        partial(backward_kernel, dps),
        out_shape=[jax.ShapeDtypeStruct((history, WIDE), wide)]
        + [jax.ShapeDtypeStruct((SECT, rows, LANES), low) for rows in kind_rows[:3]]
        + [jax.ShapeDtypeStruct((rows_emb, LANES), low)],
        in_specs=[pl.BlockSpec(memory_space=pltpu.SMEM)] + [anywhere] * (6 + len(kept)),
        out_specs=[inside] + [anywhere] * 3 + [inside],
        scratch_shapes=[pltpu.VMEM(shape, dtype) for shape, dtype in scratch]
        + [
            dma((3,)),
            dma((13,)),
            dma(()),
            dma((3,)),
            dma((3,)),
            dma((3, SECT)),
            dma((3, SECT)),
            dma((4, slots)),
            dma((4, slots)),
            pltpu.SemaphoreType.REGULAR((4, slots)),
        ],
        compiler_params=pltpu.CompilerParams(
            collective_id=1, has_side_effects=True, vmem_limit_bytes=60 * 1024 * 1024
        ),
        name="backward_fold",
    )(groups, *weights, cotangent, x, wsel, *kept)


def finish_kernel(dps, n_gains, n_biases, *refs):
    size = Sizes(dps)
    given, refs = refs[:6], refs[6:]
    block_out, series_out, embed_w, embed_b, qkv, out, up_out, down_out, gains, biases = refs[:10]
    att, up, down, emb, sems = refs[10:]
    copies = copies_of(zip(given, (att, up, down, emb, block_out, series_out)), sems)
    copies_start(copies)
    copies_wait(copies[:4])
    for lb in range(SECT):
        lanes = slice(lb * LANES, (lb + 1) * LANES)
        qkv[:, lanes] = att[lb, : size.qkv].astype(jnp.float32)
        out[:, lanes] = up[lb, : size.out].astype(jnp.float32)
        up_out[:, lanes] = up[lb, size.out :].astype(jnp.float32)
        for j in range(4):
            rows = slice(j * size.down, (j + 1) * size.down)
            start = j * WIDE + lb * LANES
            down_out[:, start : start + LANES] = down[lb, rows].astype(jnp.float32)
    tiles = [att[lb, size.qkv :].astype(jnp.float32) for lb in range(SECT)]
    flat = jnp.concatenate([tile[row : row + 1] for row in range(2) for tile in tiles], axis=1)
    gains[...] = flat[:, :n_gains]
    biases[...] = flat[:, n_gains : n_gains + n_biases]
    rows = emb.shape[0] // 8
    packed = emb[...].astype(jnp.float32)
    packed = [packed[i * rows : (i + 1) * rows] for i in range(8)]
    square = jnp.concatenate([packed[0], jnp.zeros((LANES - rows, LANES), jnp.float32)], axis=0)
    embed_b[...] = square.T[:GROUPS, :rows]
    packed = jnp.concatenate(packed, axis=1)
    ends = ((1024, L1), (768, L2), (512, L3))
    embed_w[...] = jnp.concatenate([packed[:, end - span : end] for end, span in ends], axis=1)
    copies_wait(copies[4:])


def finish_all(sums, block, series, n_gains, n_biases, dps):
    size = Sizes(dps)
    wide = jnp.float32
    columns = WIDE // (SECT * dps)
    outs = [
        (block.shape, block.dtype),
        (series.shape, wide),
        ((columns, L1 + L2 + L3), wide),
        ((GROUPS, columns), wide),
        ((size.qkv, WIDE), wide),
        ((size.out, WIDE), wide),
        ((size.up, WIDE), wide),
        ((size.down, 4 * WIDE), wide),
        ((1, n_gains), wide),
        ((1, n_biases), wide),
    ]
    anywhere = pl.BlockSpec(memory_space=pl.ANY)
    inside = pl.BlockSpec(memory_space=pltpu.VMEM)
    return pl.pallas_call(
        partial(finish_kernel, dps, n_gains, n_biases),
        out_shape=[jax.ShapeDtypeStruct(shape, dtype) for shape, dtype in outs],
        in_specs=[anywhere] * 6,
        out_specs=[inside] * 10,
        scratch_shapes=[pltpu.VMEM(array.shape, array.dtype) for array in sums]
        + [pltpu.SemaphoreType.DMA((6,))],
        compiler_params=pltpu.CompilerParams(vmem_limit_bytes=60 * 1024 * 1024),
        name="finish",
    )(*sums, block, series)


def per_device(
    series,
    groups,
    cotangent,
    embed_weight,
    embed_bias,
    qkv_weight,
    out_weight,
    up_weight,
    down_weight,
    gains,
    biases,
):
    dps = lax.axis_size("dp")
    given = (
        series[0],
        embed_weight.T,
        embed_bias,
        qkv_weight[0],
        out_weight[0],
        up_weight[0],
        down_weight[0],
        gains,
        biases,
    )
    block_output, att, up, down, _, wsel, x, *kept = forward_all(groups, given, dps)
    series_grad, *sums = backward_all(
        groups, (att, up, down), cotangent[0], x, wsel, kept, series.shape[1], dps
    )
    outs = finish_all(sums, block_output, series_grad, gains.shape[1], biases.shape[1], dps)
    block_output, series_grad, embed_w, embed_b, qkv, out, up, down, gain_sum, bias_sum = outs
    return (
        block_output[None],
        series_grad[None],
        embed_w.T,
        embed_b,
        qkv[None],
        out[None],
        up[None],
        down[None],
        gain_sum,
        bias_sum,
    )


def solution(mesh):
    return jax.shard_map(
        per_device,
        mesh=mesh,
        in_specs=(
            P(("pipe", "dp"), None, None),
            P(("pipe", "dp")),
            P(("pipe", "dp"), None, None),
            P(None, "dp"),
            P(None, "dp"),
            P("pipe", "dp", None),
            P("pipe", "dp", None),
            P("pipe", "dp", None),
            P("pipe", "dp", None),
            P("pipe", "dp"),
            P("pipe", "dp"),
        ),
        out_specs=(
            P(("pipe", "dp"), None, None),
            P(("pipe", "dp"), None, None),
            P(None, ("pipe", "dp")),
            P(None, ("pipe", "dp")),
            P("pipe", "dp", None),
            P("pipe", "dp", None),
            P("pipe", "dp", None),
            P("pipe", "dp", None),
            P("pipe", "dp"),
            P("pipe", "dp"),
        ),
        check_vma=False,
    )
```

```python
from functools import partial
import math

import jax
import jax.numpy as jnp
from jax import lax
from jax.experimental import pallas as pl
from jax.experimental.pallas import tpu as pltpu
from jax.sharding import PartitionSpec as P

HEAD = 64
L1 = 96
L2 = 192
L3 = 336
GROUPS = 3


NORM_EPS = 1e-05


MESH = pl.DeviceIdType.MESH
LANES = 128
ZS = 4
SECT = 4
EMB = 3


class Place:
    def __init__(self, dps):
        self.bs = dps // ZS
        pipe = lax.axis_index("pipe")
        dp = lax.axis_index("dp")
        self.pipe, self.dp = pipe, dp
        self.x, self.c = pipe // 2, pipe % 2
        self.z, self.b = dp // self.bs, dp % self.bs
        self.block = self.c * 2 + self.x
        self.x_peer = ((1 - self.x) * 2 + self.c, dp)
        self.core_peer = (self.x * 2 + 1 - self.c, dp)

    def block_of(self, pipe):
        return (pipe % 2) * 2 + pipe // 2

    def pipe_at(self, step):
        return (self.pipe + step) % SECT

    def z_at(self, step):
        return (self.z + step) % ZS

    def b_at(self, step):
        return (self.b + step) % self.bs

    def z_peer(self, step):
        return (self.pipe, self.z_at(step) * self.bs + self.b)

    def b_peer(self, step):
        return (self.pipe, self.z * self.bs + self.b_at(step))

    def greet(self):
        barrier = pltpu.get_barrier_semaphore()
        peers = [(self.pipe_at(k), self.dp) for k in range(1, SECT)]
        peers += [self.z_peer(k) for k in range(1, ZS)]
        peers += [self.b_peer(k) for k in range(1, self.bs)]
        for peer in peers:
            pl.semaphore_signal(barrier, inc=1, device_id=peer, device_id_type=MESH)

    def met(self):
        pl.semaphore_wait(pltpu.get_barrier_semaphore(), SECT + ZS + self.bs - 3)


def remote(src, dst, send, recv, peer):
    return pltpu.make_async_remote_copy(
        src_ref=src, dst_ref=dst, send_sem=send, recv_sem=recv, device_id=peer, device_id_type=MESH
    )


FORWARD_START = (
    (0, 3, 0),
    (0, 0, 0),
    (0, 2, 0),
    (1, 0, 0),
    (1, 3, 0),
    (0, 1, 0),
    (2, 3, 0),
    (2, 0, 0),
    (0, 0, 1),
    (0, 2, 1),
    (1, 1, 0),
    (3, 3, 0),
    (1, 2, 0),
    (4, 3, 0),
    (1, 0, 1),
    (3, 0, 0),
    (2, 1, 0),
    (4, 0, 0),
    ("embed",),
)
FORWARD_PERIOD = (
    ("mix",),
    ("mix",),
    ("attend",),
    (0, 1, 1),
    (2, 2, 0),
    (3, 1, 0),
    ("attend",),
    ("attend",),
    ("attend",),
    (4, 1, 0),
    (2, 0, 1),
    (0, 0, 2),
    ("project",),
    (3, 2, 0),
    (0, 2, 2),
    ("up",),
    (1, 1, 1),
    (1, 2, 1),
    ("up",),
    ("up",),
    (1, 0, 2),
    (4, 2, 0),
    (3, 0, 1),
    ("up",),
    (2, 1, 1),
    ("down",),
    (4, 0, 1),
    ("down",),
)
BACKWARD_PERIOD = (
    ("norm2",),
    (1, 0, -1),
    ("down",),
    ("down",),
    ("gelu",),
    ("gelu",),
    (2, 1, -1),
    (0, 2, 0),
    ("up",),
    ("normed",),
    (2, 0, -1),
    ("norm1",),
    (4, 1, -2),
    (4, 2, -2),
    (1, 2, 0),
    (3, 1, -1),
    (0, 1, 0),
    ("attend",),
    ("attend",),
    ("attend",),
    ("attend",),
    (3, 2, -1),
    (1, 1, 0),
    (4, 0, -2),
    (3, 0, -1),
    ("mix",),
    ("mix",),
    (0, 0, 0),
    ("input",),
    (2, 2, 0),
)
BACKWARD_END = (
    ("embed",),
    (1, 0, 3),
    (2, 1, 3),
    (2, 0, 3),
    (4, 1, 2),
    (4, 2, 2),
    (3, 1, 3),
    (0, 3, 0),
    (3, 2, 3),
    (4, 0, 2),
    (1, 3, 0),
    (3, 0, 3),
    (2, 3, 0),
    (3, 3, 0),
    (4, 1, 3),
    (4, 2, 3),
    (4, 0, 3),
    (4, 3, 0),
)


def copies_start(copies):
    for copy in copies:
        copy.start()


def copies_wait(copies):
    for copy in copies:
        copy.wait()


class Spread:
    def __init__(self, at, out, send, recv, half=ZS // 2):
        self.at, self.out, self.send, self.recv = at, out, send, recv
        nb = at.bs - 1
        self.slot_z = 0
        self.slot_b1 = ZS - 1
        self.slot_x1 = self.slot_b1 + nb
        self.slot_x2 = self.slot_x1 + 1
        self.slot_b2 = self.slot_x2 + 1
        self.slot_c = self.slot_b2 + nb
        self.half = half

    @staticmethod
    def slots(bs):
        return ZS - 1 + 2 * (bs - 1) + 3

    def copy(self, region, slot, peer):
        return remote(region, region, self.send.at[slot], self.recv.at[slot], peer)

    def copies(self, stage, back):
        at, out, half = self.at, self.out, self.half
        rest = pl.ds(half, ZS - half)
        x_block = at.c * 2 + 1 - at.x if back else at.block
        if stage == 0:
            return [
                self.copy(
                    out.at[at.block, at.z_at(ZS - k) if back else at.z, at.b],
                    self.slot_z + k - 1,
                    at.z_peer(k),
                )
                for k in range(1, ZS)
            ]
        if stage == 3:
            core = 1 - at.c if back else at.c
            return [self.copy(out.at[pl.ds(core * 2, 2)], self.slot_c, at.core_peer)]
        copies = []
        for k in range(1, at.bs):
            b = at.b_at(at.bs - k) if back else at.b
            if stage == 1:
                region, slot = out.at[at.block, pl.ds(0, half), b], self.slot_b1
            else:
                region, slot = out.at[pl.ds(at.c * 2, 2), rest, b], self.slot_b2
            copies.append(self.copy(region, slot + k - 1, at.b_peer(k)))
        if stage == 1:
            region, slot = out.at[x_block, rest, at.b], self.slot_x1
        else:
            region, slot = out.at[x_block, pl.ds(0, half)], self.slot_x2
        copies.append(self.copy(region, slot, at.x_peer))
        return copies

    def start(self, stage):
        copies_start(self.copies(stage, False))

    def land(self, stage):
        for copy in self.copies(stage, True):
            copy.wait_recv()
        for copy in self.copies(stage, False):
            copy.wait_send()

    def move(self, stage):
        self.land(stage)
        self.start(stage + 1)


class SpreadCross(Spread):
    @staticmethod
    def slots(bs):
        return 2 * bs + 2 * ZS - 1

    def copies(self, stage, back):
        at, out = self.at, self.out
        rows = out.shape[-2]
        cut = rows // 32 * 16
        some, rest = pl.ds(0, cut), pl.ds(cut, rows - cut)
        core = 1 - at.c if back else at.c
        if stage == 3:
            return [self.copy(out.at[pl.ds(core * 2, 2)], 2 * at.bs + 2 * ZS - 2, at.core_peer)]
        both = pl.ds(at.c * 2, 2)
        x_block = at.c * 2 + 1 - at.x if back else at.block
        copies = []
        if stage == 1:
            for k in range(1, ZS):
                z = at.z_at(ZS - k) if back else at.z
                copies.append(self.copy(out.at[both, z, at.b, some], at.bs + k - 1, at.z_peer(k)))
                slot = at.bs + ZS + k - 2
                copies.append(self.copy(out.at[at.block, z, :, rest], slot, at.z_peer(k)))
            return copies
        base = 0 if stage == 0 else at.bs + 2 * ZS - 2
        for k in range(1, at.bs):
            b = at.b_at(at.bs - k) if back else at.b
            region = out.at[at.block, at.z, b, rest] if stage == 0 else out.at[both, :, b, some]
            copies.append(self.copy(region, base + k, at.b_peer(k)))
        if stage == 0:
            region = out.at[x_block, at.z, at.b, some]
        else:
            region = out.at[x_block, :, :, rest]
        copies.append(self.copy(region, base, at.x_peer))
        return copies


class Fold:
    def __init__(self, at, grads, total, landing, bufs, final, send, recv, credit, half):
        self.at, self.grads, self.total = at, grads, total
        self.landing, self.bufs, self.final = landing, bufs, final
        self.send, self.recv, self.credit = send, recv, credit
        self.half = half
        nb = at.bs - 1
        self.slot_x1 = 1
        self.slot_b1 = 2
        self.slot_x2 = 2 + nb
        self.slot_b2 = 3 + nb
        self.slot_z = 3 + 2 * nb

    @staticmethod
    def slots(bs):
        return 3 + 2 * (bs - 1) + ZS - 1

    @staticmethod
    def buffers(bs, rows, half):
        nb = max(bs - 1, 1)
        rest = ZS - half
        return [
            (half, bs, rows, LANES),
            (nb, 2, rest, rows, LANES),
            (rest, rows, LANES),
            (nb, half, rows, LANES),
            (ZS - 1, rows, LANES),
        ]

    def core_parts(self):
        other = self.grads.at[pl.ds((1 - self.at.c) * 2, 2)]
        return [(other, self.landing, 0, self.at.core_peer, self.at.core_peer)]

    def parts(self, stage):
        at, half, total, bufs = self.at, self.half, self.total, self.bufs
        if stage == 0:
            return self.core_parts()
        if stage == 3:
            return [
                (
                    total.at[at.x, at.z_at(k), at.b],
                    bufs[4].at[k - 1],
                    self.slot_z + k - 1,
                    at.z_peer(k),
                    at.z_peer(ZS - k),
                )
                for k in range(1, ZS)
            ]
        rest = pl.ds(half, ZS - half)
        found = []
        for k in range(1, at.bs):
            if stage == 1:
                src, buf, slot = total.at[:, rest, at.b_at(k)], bufs[1], self.slot_b1
            else:
                src, buf, slot = total.at[at.x, pl.ds(0, half), at.b_at(k)], bufs[3], self.slot_b2
            found.append((src, buf.at[k - 1], slot + k - 1, at.b_peer(k), at.b_peer(at.bs - k)))
        if stage == 1:
            src, buf, slot = total.at[1 - at.x, pl.ds(0, half)], bufs[0], self.slot_x1
        else:
            src, buf, slot = total.at[1 - at.x, rest, at.b], bufs[2], self.slot_x2
        found.append((src, buf, slot, at.x_peer, at.x_peer))
        return found

    def start(self, stage, again):
        for src, buf, slot, to, _ in self.parts(stage):
            if again is not False:

                @pl.when(again)
                def _():
                    pl.semaphore_wait(self.credit.at[slot], 1)

            remote(src, buf, self.send.at[slot], self.recv.at[slot], to).start()

    def land(self, stage, more):
        parts = self.parts(stage)
        for src, buf, slot, to, _ in parts:
            remote(src, buf, self.send.at[slot], self.recv.at[slot], to).wait()
        self.add(stage)
        if more is not False:

            @pl.when(more)
            def _():
                for _, _, slot, _, origin in parts:
                    pl.semaphore_signal(
                        self.credit.at[slot], inc=1, device_id=origin, device_id_type=MESH
                    )

    def add_core(self):
        at, bs, total = self.at, self.at.bs, self.total

        @pl.loop(0, 2 * ZS * bs)
        def _(i):
            z, b = i // bs % ZS, i % bs
            x = i // (ZS * bs)
            total[x, z, b] = self.grads[at.c * 2 + x, z, b] + self.landing[x, z, b]

    def add(self, stage):
        at, half, bs = self.at, self.half, self.at.bs
        total, bufs = self.total, self.bufs
        rest = ZS - half
        if stage == 0:
            self.add_core()
        elif stage == 1:

            @pl.loop(0, half * bs)
            def _(i):
                z, b = i // bs, i % bs
                total[at.x, z, b] = total[at.x, z, b] + bufs[0][z, b]

            @pl.loop(0, 2 * rest)
            def _(i):
                x, z = i // rest, i % rest
                for k in range(bs - 1):
                    total[x, half + z, at.b] = total[x, half + z, at.b] + bufs[1][k, x, z]

        elif stage == 2:

            @pl.loop(0, rest)
            def _(z):
                total[at.x, half + z, at.b] = total[at.x, half + z, at.b] + bufs[2][z]

            @pl.loop(0, half)
            def _(z):
                for k in range(bs - 1):
                    total[at.x, z, at.b] = total[at.x, z, at.b] + bufs[3][k, z]

        else:
            self.finish([bufs[4][k] for k in range(ZS - 1)])

    def finish(self, pieces):
        at = self.at
        done = self.total[at.x, at.z, at.b].astype(jnp.float32)
        for piece in pieces:
            done = done + piece.astype(jnp.float32)
        self.final[...] = done.astype(self.final.dtype)

    def move(self, stage, again, more):
        self.land(stage, more)
        self.start(stage + 1, again)


class FoldCross(Fold):
    @staticmethod
    def slots(bs):
        return 2 * bs + 2 * ZS - 1

    @staticmethod
    def buffers(bs, rows, half):
        nb = max(bs - 1, 1)
        cut = rows // 32 * 16
        rest = rows - cut
        return [
            (nb, 2, ZS, cut, LANES),
            (ZS, bs, rest, LANES),
            (ZS - 1, 2, cut, LANES),
            (ZS - 1, bs, rest, LANES),
            (cut, LANES),
            (nb, rest, LANES),
        ]

    def cuts(self):
        rows = self.total.shape[-2]
        cut = rows // 32 * 16
        return pl.ds(0, cut), pl.ds(cut, rows - cut)

    def parts(self, stage):
        at, total, bufs = self.at, self.total, self.bufs
        if stage == 0:
            return self.core_parts()
        some, rest = self.cuts()
        found = []
        if stage == 2:
            for k in range(1, ZS):
                pair = (at.z_peer(k), at.z_peer(ZS - k))
                z = at.z_at(k)
                found.append((total.at[:, z, at.b, some], bufs[2].at[k - 1], at.bs + k, *pair))
                slot = at.bs + ZS + k - 1
                found.append((total.at[at.x, z, :, rest], bufs[3].at[k - 1], slot, *pair))
            return found
        base = 1 if stage == 1 else at.bs + 2 * ZS - 1
        for k in range(1, at.bs):
            pair = (at.b_peer(k), at.b_peer(at.bs - k))
            if stage == 1:
                src, buf = total.at[:, :, at.b_at(k), some], bufs[0].at[k - 1]
            else:
                src, buf = total.at[at.x, at.z, at.b_at(k), rest], bufs[5].at[k - 1]
            found.append((src, buf, base + k, *pair))
        if stage == 1:
            src, buf = total.at[1 - at.x, :, :, rest], bufs[1]
        else:
            src, buf = total.at[1 - at.x, at.z, at.b, some], bufs[4]
        found.append((src, buf, base, at.x_peer, at.x_peer))
        return found

    def add(self, stage):
        at, bs = self.at, self.at.bs
        total, bufs = self.total, self.bufs
        some, rest = self.cuts()
        if stage == 0:
            self.add_core()
        elif stage == 1:

            @pl.loop(0, 2 * ZS)
            def _(i):
                x, z = i // ZS, i % ZS
                for k in range(bs - 1):
                    total[x, z, at.b, some] = total[x, z, at.b, some] + bufs[0][k, x, z]

            @pl.loop(0, ZS * bs)
            def _(i):
                z, b = i // bs, i % bs
                total[at.x, z, b, rest] = total[at.x, z, b, rest] + bufs[1][z, b]

        elif stage == 2:
            for x in range(2):
                for k in range(ZS - 1):
                    total[x, at.z, at.b, some] = total[x, at.z, at.b, some] + bufs[2][k, x]

            @pl.loop(0, bs)
            def _(b):
                for k in range(ZS - 1):
                    total[at.x, at.z, b, rest] = total[at.x, at.z, b, rest] + bufs[3][k, b]

        else:
            total[at.x, at.z, at.b, some] = total[at.x, at.z, at.b, some] + bufs[4][...]
            for k in range(bs - 1):
                total[at.x, at.z, at.b, rest] = total[at.x, at.z, at.b, rest] + bufs[5][k]
            self.final[...] = total[at.x, at.z, at.b]


HALF = 256
WIDE = 512
QKV_TILE = 768
VEC_ROWS = 16


STEP = 64


def by_rows(fn, *arrays, step=STEP):
    parts = [
        fn(*[array[at : at + step] for array in arrays])
        for at in range(0, arrays[0].shape[0], step)
    ]
    if isinstance(parts[0], tuple):
        return tuple(jnp.concatenate(part, axis=0) for part in zip(*parts))
    return jnp.concatenate(parts, axis=0)


def dot_nt(a, b):
    return lax.dot_general(a, b, (((1,), (1,)), ((), ())), preferred_element_type=jnp.float32)


def dot_nn(a, b):
    return lax.dot_general(a, b, (((1,), (0,)), ((), ())), preferred_element_type=jnp.float32)


def dot_tn(a, b):
    return lax.dot_general(a, b, (((0,), (0,)), ((), ())), preferred_element_type=jnp.float32)


def aligned(index, unit):
    return pl.multiple_of(index, unit)


def rows_of(ref, bs, first, count, start, rows, blocks=range(SECT)):
    parts = []
    for i in range(count):
        d = first + i
        place = (d // bs, d % bs)
        parts.append(
            jnp.concatenate(
                [ref[(lb,) + place + (pl.ds(start, rows), slice(None))] for lb in blocks], axis=1
            )
        )
    return parts[0] if count == 1 else jnp.concatenate(parts, axis=0)


def put_rows(ref, bs, first, count, start, rows, value, block=0):
    value = value.astype(ref.dtype)
    for i in range(count):
        d = first + i
        place = (d // bs, d % bs)
        for lane in range(value.shape[1] // LANES):
            ref[(block + lane,) + place + (pl.ds(start, rows), slice(None))] = value[
                i * rows : (i + 1) * rows, lane * LANES : (lane + 1) * LANES
            ]


def vector_pieces(dps):
    n_gains, n_biases = 2 * WIDE // dps, 10 * WIDE // dps
    starts = [(0, 0), (0, 2), (1, 0), (1, 2), (2, 0), (2, 1), (2, 2), (2, 3), (3, 0), (3, 2)]
    pieces = []
    for d in range(dps):
        at = 0
        while at < n_gains + n_biases:
            if at < n_gains:
                index = d * n_gains + at
                row, column = (1, 3)[index // WIDE], WIDE + index % WIDE
                left = n_gains - at
            else:
                index = d * n_biases + at - n_gains
                row, part = starts[index // WIDE]
                column = part * WIDE + index % WIDE
                left = n_gains + n_biases - at
            size = min(left, LANES - at % LANES, LANES - column % LANES)
            pieces.append((d, at // WIDE, at % WIDE, row, column, size))
            at += size
    return pieces


def read_vectors(ref, table, bs, start):
    dps = ZS * bs
    tiles = {}
    for d, row, lane, to_row, to_lane, size in vector_pieces(dps):
        key = (d, lane // LANES)
        if key not in tiles:
            tile = ref[lane // LANES, d // bs, d % bs, start : start + VEC_ROWS, :]
            tiles[key] = tile.astype(jnp.float32)
        off = lane % LANES
        table[to_row : to_row + 1, to_lane : to_lane + size] = tiles[key][
            row : row + 1, off : off + size
        ]


def write_vectors(ref, table, bs, start):
    dps = ZS * bs
    found = {}
    for d, row, lane, to_row, to_lane, size in vector_pieces(dps):
        piece = table[to_row : to_row + 1, to_lane : to_lane + size]
        found.setdefault((d, lane // LANES), {}).setdefault(row, []).append(piece)
    row_id = lax.broadcasted_iota(jnp.int32, (VEC_ROWS, LANES), 0)
    for d in range(dps):
        for lb in range(SECT):
            tile = jnp.zeros((VEC_ROWS, LANES), jnp.float32)
            for row, pieces in found.get((d, lb), {}).items():
                have = sum(piece.shape[1] for piece in pieces)
                if have < LANES:
                    pieces = pieces + [jnp.zeros((1, LANES - have), jnp.float32)]
                line = pieces[0] if len(pieces) == 1 else jnp.concatenate(pieces, axis=1)
                tile = jnp.where(row_id == row, line, tile)
            ref[lb, d // bs, d % bs, start : start + VEC_ROWS, :] = tile.astype(ref.dtype)


def fold_rows(x):
    total = x[:8]
    for at in range(8, x.shape[0], 8):
        total = total + x[at : at + 8]
    return total


def normalize(x):
    mean = jnp.mean(x, axis=1, keepdims=True)
    centred = x - mean
    scale = lax.rsqrt(jnp.mean(centred * centred, axis=1, keepdims=True) + NORM_EPS)
    return centred * scale, jnp.broadcast_to(scale, (x.shape[0], LANES))


def normalize_back(unit, scale, grad, gain):
    inner = grad * gain
    first = jnp.mean(inner, axis=1, keepdims=True)
    second = jnp.mean(inner * unit, axis=1, keepdims=True)
    out = jnp.concatenate([scale] * (WIDE // LANES), axis=1) * (inner - first - unit * second)
    return out, fold_rows(out), fold_rows(grad * unit), fold_rows(grad)


def gelu_pair(u):
    below = 0.5 + 0.5 * lax.erf(u * math.sqrt(0.5))
    bell = jnp.exp2((-0.5 * math.log2(math.e)) * (u * u))
    return u * below, below + u * (bell * (1.0 / math.sqrt(2.0 * math.pi)))


def head_masks(scale):
    lane = lax.broadcasted_iota(jnp.int32, (1, LANES), 1)
    first = jnp.where(lane < HEAD, scale, 0.0).astype(jnp.bfloat16)
    second = jnp.where(lane < HEAD, 0.0, scale).astype(jnp.bfloat16)
    return first, second


class Sizes:
    def __init__(self, dps):
        self.dps, self.bs = dps, dps // ZS
        self.qkv, self.out, self.up, self.down = (
            3 * WIDE // dps,
            WIDE // dps,
            4 * WIDE // dps,
            WIDE // dps,
        )
        self.att = self.qkv + VEC_ROWS
        self.dense = self.out + self.up
        self.wide = 4 * self.down


def qkv_rows(size, w, tile):
    count = QKV_TILE // size.qkv
    return rows_of(w, size.bs, tile * count, count, 0, size.qkv)


def out_rows(size, w):
    return rows_of(w, size.bs, 0, size.dps, 0, size.out)


def up_rows(size, w, tile):
    count = HALF // size.up
    return rows_of(w, size.bs, tile * count, count, size.out, size.up)


def forward_mix(size, w, table, h, mixed, piece):
    columns = slice(piece * QKV_TILE, (piece + 1) * QKV_TILE)
    shift = table[0:1, columns]
    out = dot_nt(h[...], qkv_rows(size, w, piece))
    mixed[:, columns] = by_rows(lambda part: (part + shift).astype(mixed.dtype), out)


def softmax_columns(scores):
    parts = [scores[at : at + STEP] for at in range(0, scores.shape[0], STEP)]
    top = parts[0]
    for part in parts[1:]:
        top = jnp.maximum(top, part)
    top = jnp.max(top, axis=0, keepdims=True)
    parts = [jnp.exp(part - top) for part in parts]
    total = parts[0]
    for part in parts[1:]:
        total = total + part
    scale = 1.0 / jnp.sum(total, axis=0, keepdims=True)
    return jnp.concatenate([(part * scale).astype(jnp.bfloat16) for part in parts], axis=0)


def forward_attend(mixed, probs, attended, pair):
    lane = pair * LANES
    key_rows = mixed[:, WIDE + lane : WIDE + lane + LANES]
    values = mixed[:, 2 * WIDE + lane : 2 * WIDE + lane + LANES].T

    for part in range(2):
        rows = slice(part * HALF, (part + 1) * HALF)
        queries = mixed[rows, lane : lane + LANES]
        joined = []
        for head, mask in enumerate(head_masks(1.0 / math.sqrt(HEAD))):
            weights = softmax_columns(dot_nt(key_rows, queries * mask))
            probs[2 * pair + head, :, rows] = weights
            joined.append(dot_nn(values[head * HEAD : (head + 1) * HEAD], weights))
        joined = jnp.concatenate(joined, axis=0).T
        attended[rows, lane : lane + LANES] = joined.astype(attended.dtype)


def forward_project(size, w, table, h, attended, first, scale, normed):
    out = dot_nt(attended[...], out_rows(size, w))
    for part in range(WIDE // STEP):
        rows = slice(part * STEP, (part + 1) * STEP)
        total = h[rows, :].astype(jnp.float32) + (out[rows] + table[1:2, 0:WIDE])
        unit, scale[rows, :] = normalize(total)
        first[rows, :] = unit
        normed[rows, :] = (
            unit * table[1:2, WIDE : 2 * WIDE] + table[1:2, 2 * WIDE : 3 * WIDE]
        ).astype(normed.dtype)


def forward_up(size, w, table, normed, slope, hidden, piece):
    for j in (2 * piece, 2 * piece + 1):
        columns = slice(j * HALF, (j + 1) * HALF)
        shift = table[2:3, columns]
        upper = dot_nt(normed[...], up_rows(size, w, j))
        for part in range(WIDE // STEP):
            rows = slice(part * STEP, (part + 1) * STEP)
            value, grad = gelu_pair(upper[rows] + shift)
            hidden[rows, columns] = value.astype(hidden.dtype)
            slope[rows, columns] = grad.astype(slope.dtype)


def forward_down(size, w, table, normed, hidden, second, scale, h, piece):
    columns = slice(piece * HALF, (piece + 1) * HALF)
    count = size.dps // 2
    matrix = jnp.concatenate(
        [
            rows_of(w, size.bs, piece * count, count, j * size.down, size.down)
            for j in range(4)
        ],
        axis=1,
    )
    out = dot_nt(hidden[...], matrix)
    shift = table[3:4, columns]
    for part in range(WIDE // STEP):
        rows = slice(part * STEP, (part + 1) * STEP)
        second[rows, columns] = normed[rows, columns].astype(jnp.float32) + (out[rows] + shift)
    if piece == 1:
        for part in range(WIDE // STEP):
            rows = slice(part * STEP, (part + 1) * STEP)
            unit, scale[rows, :] = normalize(second[rows, :])
            second[rows, :] = unit
            h[rows, :] = (
                unit * table[3:4, WIDE : 2 * WIDE] + table[3:4, 2 * WIDE : 3 * WIDE]
            ).astype(h.dtype)


def backward_norm_two(table, dtable, dy, second, scale, dnormed, dlow, dlow_t):
    dtable[...] = jnp.zeros_like(dtable)
    sums = [jnp.zeros((8, WIDE), jnp.float32)] * 3
    for part in range(WIDE // STEP):
        rows = slice(part * STEP, (part + 1) * STEP)
        grad, *found = normalize_back(
            second[rows, :],
            scale[rows, :],
            dy[rows, :].astype(jnp.float32),
            table[3:4, WIDE : 2 * WIDE],
        )
        dnormed[rows, :] = grad
        dlow[rows, :] = grad.astype(dlow.dtype)
        sums = [total + new for total, new in zip(sums, found)]
    for i, total in enumerate(sums):
        dtable[3:4, i * WIDE : (i + 1) * WIDE] = jnp.sum(total, axis=0, keepdims=True)
    dlow_t[...] = dlow[...].T


def backward_down(size, grads, hidden, dlow_t, piece):
    @pl.loop(2 * piece, 2 * piece + 2)
    def _(i):
        start = aligned(i * size.down, 16)
        for half in range(2):
            columns = pl.ds(aligned(i * WIDE, WIDE) + half * HALF, HALF)
            value = dot_nn(dlow_t[...], hidden[:, columns])
            put_rows(grads, size.bs, 0, size.dps, start, size.down, value, 2 * half)


def backward_gelu(size, w, dtable, slope, dlow, dup, piece):
    @pl.loop(2 * piece, 2 * piece + 2)
    def _(i):
        start = aligned(i * size.down, 16)
        for half in range(2):
            columns = pl.ds(aligned(i * WIDE, WIDE) + half * HALF, HALF)
            blocks = (2 * half, 2 * half + 1)
            matrix = rows_of(w, size.bs, 0, size.dps, start, size.down, blocks)
            dhidden = dot_nn(dlow[...], matrix)
            total = jnp.zeros((8, HALF), jnp.float32)
            for part in range(WIDE // STEP):
                rows = slice(part * STEP, (part + 1) * STEP)
                dupper = dhidden[rows] * slope[rows, columns].astype(jnp.float32)
                total = total + fold_rows(dupper)
                dup[rows, columns] = dupper.astype(dup.dtype)
            dtable[2:3, columns] = jnp.sum(total, axis=0, keepdims=True)


def backward_up(size, grads, normed, dup):
    count = HALF // size.up

    @pl.loop(0, 4)
    def _(i):
        for half in range(2):
            columns = pl.ds(aligned(i * WIDE, WIDE) + half * HALF, HALF)
            value = dot_tn(dup[:, columns], normed[...])
            first = (2 * i + half) * count
            put_rows(grads, size.bs, first, count, size.out, size.up, value)


def backward_normed(size, w, dnormed, dup):
    for half in range(2):
        columns = slice(half * HALF, (half + 1) * HALF)
        blocks = (2 * half, 2 * half + 1)
        matrix = rows_of(w, size.bs, 0, size.dps, size.out, size.up, blocks)
        out = dot_nn(dup[...], matrix)
        for part in range(WIDE // STEP):
            rows = slice(part * STEP, (part + 1) * STEP)
            dnormed[rows, columns] = dnormed[rows, columns] + out[rows]


def backward_norm_one(
    size, w, table, grads, dtable, first, scale, attended, dnormed, dlow, dlow_t, delta
):
    sums = [jnp.zeros((8, WIDE), jnp.float32)] * 3
    for part in range(WIDE // STEP):
        rows = slice(part * STEP, (part + 1) * STEP)
        grad, *found = normalize_back(
            first[rows, :], scale[rows, :], dnormed[rows, :], table[1:2, WIDE : 2 * WIDE]
        )
        dnormed[rows, :] = grad
        dlow[rows, :] = grad.astype(dlow.dtype)
        sums = [total + new for total, new in zip(sums, found)]
    for i, total in enumerate(sums):
        dtable[1:2, i * WIDE : (i + 1) * WIDE] = jnp.sum(total, axis=0, keepdims=True)
    dlow_t[...] = dlow[...].T
    for block in (0, 2):
        columns = slice(block * LANES, (block + 2) * LANES)
        value = dot_nn(dlow_t[...], attended[:, columns])
        put_rows(grads, size.bs, 0, size.dps, 0, size.out, value, block)
    grad = dot_nn(dlow[...], out_rows(size, w)).astype(dlow.dtype)
    dlow[...] = grad
    product = grad.astype(jnp.float32) * attended[...].astype(jnp.float32)
    high = product.astype(jnp.bfloat16)
    rest = (product - high.astype(jnp.float32)).astype(jnp.bfloat16)
    head = lax.broadcasted_iota(jnp.int32, delta.shape, 0)
    lane = lax.broadcasted_iota(jnp.int32, delta.shape, 1)
    inside = (lane >= head * HEAD) & (lane < (head + 1) * HEAD)
    inside = jnp.where(inside, 1.0, 0.0).astype(jnp.bfloat16)
    delta[...] = dot_nt(inside, high) + dot_nt(inside, rest)


def backward_attend(mixed, probs, delta, dtable, dlow, dmixed, pair):
    scale = 1.0 / math.sqrt(HEAD)
    lane = pair * LANES
    columns = slice(lane, lane + LANES)
    key_columns = slice(WIDE + lane, WIDE + lane + LANES)
    value_columns = slice(2 * WIDE + lane, 2 * WIDE + lane + LANES)
    keys_t = mixed[:, key_columns].T
    values = mixed[:, value_columns]
    dkeys = jnp.zeros((WIDE, LANES), jnp.float32)
    dvalues = jnp.zeros((WIDE, LANES), jnp.float32)
    for part in range(2):
        rows = slice(part * HALF, (part + 1) * HALF)
        queries = mixed[rows, columns]
        grad_out = dlow[rows, columns]
        dqueries = []
        for head in range(2):
            query = queries * head_masks(scale)[head]
            grad = grad_out * head_masks(1.0)[head]
            at = 2 * pair + head
            weights = probs[at, :, rows]
            less = delta[at : at + 1, rows]
            dprobs = dot_nt(values, grad)
            dscores = by_rows(
                lambda p, dp: (p.astype(jnp.float32) * (dp - less)).astype(jnp.bfloat16),
                weights,
                dprobs,
            )
            dvalues = dvalues + dot_nn(weights, grad)
            dkeys = dkeys + dot_nn(dscores, query)
            dqueries.append(dot_nn(keys_t[head * HEAD : (head + 1) * HEAD], dscores))
        dquery = jnp.concatenate(dqueries, axis=0).T * scale
        dtable[0:1, columns] += jnp.sum(dquery, axis=0, keepdims=True)
        dmixed[rows, columns] = dquery.astype(dmixed.dtype)
    dmixed[:, key_columns] = dkeys.astype(dmixed.dtype)
    dmixed[:, value_columns] = dvalues.astype(dmixed.dtype)
    dtable[0:1, value_columns] = jnp.sum(dvalues, axis=0, keepdims=True)


def backward_mix(size, grads, h, dmixed, piece):
    count = QKV_TILE // size.qkv
    grad = dmixed[:, piece * QKV_TILE : (piece + 1) * QKV_TILE]
    put_rows(grads, size.bs, piece * count, count, 0, size.qkv, dot_tn(grad, h[...]))


def backward_input(size, w, dnormed, dmixed, dy):
    for half in range(2):
        columns = slice(half * HALF, (half + 1) * HALF)
        blocks = (2 * half, 2 * half + 1)
        matrix = rows_of(w, size.bs, 0, size.dps, 0, size.qkv, blocks)
        out = dot_nn(dmixed[...], matrix)
        for part in range(WIDE // STEP):
            rows = slice(part * STEP, (part + 1) * STEP)
            dy[rows, columns] = (dnormed[rows, columns] + out[rows]).astype(dy.dtype)


WINDOW = 384


def group_rows(group):
    rows = lax.broadcasted_iota(jnp.int32, (16, LANES), 0)
    return jnp.where(rows == group, 1.0, 0.0).astype(jnp.bfloat16)


def pack_mix(piece, qkv, gains, biases):
    low = piece.dtype
    rows = qkv.shape[0]
    flat = jnp.concatenate([gains[...], biases[...]], axis=1)
    flat = jnp.concatenate([flat, jnp.zeros((1, 2 * WIDE - flat.shape[1]), flat.dtype)], axis=1)
    row_id = lax.broadcasted_iota(jnp.int32, (VEC_ROWS, LANES), 0)
    for lb in range(SECT):
        lane = lb * LANES
        piece[lb, :rows] = qkv[:, lane : lane + LANES].astype(low)
        tile = jnp.where(row_id == 0, flat[:, lane : lane + LANES], 0.0)
        lane += WIDE
        tile = jnp.where(row_id == 1, flat[:, lane : lane + LANES], tile)
        piece[lb, rows:] = tile.astype(low)


def pack_up(piece, out, up):
    rows = out.shape[0]
    for lb in range(SECT):
        lanes = slice(lb * LANES, (lb + 1) * LANES)
        piece[lb, :rows] = out[:, lanes].astype(piece.dtype)
        piece[lb, rows:] = up[:, lanes].astype(piece.dtype)


def pack_down(piece, down):
    rows = down.shape[0]
    for lb in range(SECT):
        for j in range(4):
            start = j * WIDE + lb * LANES
            piece[lb, j * rows : (j + 1) * rows] = down[:, start : start + LANES].astype(piece.dtype)


def pack_embedding(piece, weight, shift, square):
    n = weight.shape[0]
    square[...] = jnp.zeros_like(square)
    square[:GROUPS, :n] = shift[...]

    def ending(part, width):
        return jnp.concatenate([jnp.zeros((n, width - part.shape[1]), part.dtype), part], axis=1)

    parts = [
        square[...].T[:n],
        ending(weight[:, L1 + L2 :], 3 * LANES),
        ending(weight[:, L1 : L1 + L2], 2 * LANES),
        ending(weight[:, :L1], 2 * LANES),
    ]
    columns = jnp.concatenate(parts, axis=1).astype(piece.dtype)
    for lb in range(SECT):
        for part in range(2):
            start = part * WIDE + lb * LANES
            piece[lb, part * n : (part + 1) * n] = columns[:, start : start + LANES]


def expand(series, group, x):
    empty = jnp.zeros((WINDOW - series.shape[0], series.shape[1]), series.dtype)
    x[:, :WINDOW] = jnp.concatenate([empty, series[...]], axis=0).T
    lane = lax.broadcasted_iota(jnp.int32, (x.shape[0], LANES), 1)
    x[:, WINDOW:] = jnp.where(lane == group, 1.0, 0.0).astype(x.dtype)


def embed(size, emb, pick, x, wsel, h):
    rows = WIDE // size.dps
    first = rows_of(emb, size.bs, 0, size.dps, 0, rows)
    second = rows_of(emb, size.bs, 0, size.dps, rows, rows)
    long, middle, short = (pick[g : g + 1, :] for g in (2, 1, 0))
    wide = jnp.concatenate(
        [
            first[:, LANES : 2 * LANES] * long,
            first[:, 2 * LANES : 3 * LANES] * long + second[:, :LANES] * middle,
            first[:, 3 * LANES :] * long
            + second[:, LANES : 2 * LANES] * middle
            + second[:, 3 * LANES :] * short,
        ],
        axis=1,
    )
    wsel[...] = wide.T
    matrix = jnp.concatenate([wide, first[:, :LANES]], axis=1)
    h[...] = dot_nt(x[...], matrix).astype(h.dtype)


def embed_back(size, pick, x, wsel, dh, grads, series_grad):
    history = series_grad.shape[0]
    series_grad[...] = dot_nt(wsel[...], dh[...])[WINDOW - history :]
    sums = dot_tn(dh[...], x[...])
    long, middle, short = (pick[g : g + 1, :].astype(jnp.float32) for g in (2, 1, 0))
    parts = [sums[:, i * LANES : (i + 1) * LANES] for i in range(4)]
    parts = [
        parts[3],
        parts[0] * long,
        parts[1] * long,
        parts[2] * long,
        parts[1] * middle,
        parts[2] * middle,
        jnp.zeros_like(parts[0]),
        parts[2] * short,
    ]
    rows = WIDE // (SECT * size.dps)
    for pipe in range(SECT):
        block = (pipe % 2) * 2 + pipe // 2
        for dp in range(size.dps):
            start = (pipe * size.dps + dp) * rows
            piece = jnp.concatenate([part[start : start + rows] for part in parts], axis=0)
            grads[block, dp // size.bs, dp % size.bs] = piece.astype(grads.dtype)


def saved_shapes():
    low, wide = jnp.bfloat16, jnp.float32
    return [
        ((WIDE, WIDE), low),
        ((WIDE, 3 * WIDE), low),
        ((2 * SECT, WIDE, WIDE), low),
        ((WIDE, WIDE), low),
        ((WIDE, WIDE), wide),
        ((WIDE, WIDE), low),
        ((WIDE, 4 * WIDE), low),
        ((WIDE, 4 * WIDE), low),
        ((WIDE, WIDE), wide),
        ((SECT, 4 * WIDE), wide),
        ((WIDE, LANES), wide),
        ((WIDE, LANES), wide),
    ]


def chunk_shape(size, rows):
    return (SECT, ZS, size.bs, rows, LANES)


HALVES = (2, 2, 2, 2)
CROSS = (2,)


def follow(plan, section, act, compute):
    seen = {}
    for step in plan:
        if len(step) == 1:
            piece = seen.get(step[0], 0)
            seen[step[0]] = piece + 1
            compute(step[0], piece)
            continue
        op, kind, offset = step
        where = section + offset
        if isinstance(where, int):
            if 0 <= where < SECT:
                act(op, kind, where)
        elif offset == 0:
            act(op, kind, where)
        else:
            inside = where < SECT if offset > 0 else where >= 0

            @pl.when(inside)
            def _():
                act(op, kind, where)


def forward_kernel(dps, groups, *refs):
    size = Sizes(dps)
    given, refs = refs[:9], refs[9:]
    out, wholes, wsel, x, refs = refs[0], refs[1:5], refs[5], refs[6], refs[7:]
    kept, local, refs = refs[:12], refs[12:24], refs[24:]
    buffers, refs = refs[:4], refs[4:]
    pieces, held, refs = refs[:4], refs[4:13], refs[13:]
    emb_rows, pick, refs = refs[0], refs[1], refs[2:]
    given_sem, w_sem, kept_sem, own_sem, p_send, p_recv, send, recv = refs
    h, mixed, probs, attended, first, normed, slope, hidden, second, table, scale_1, scale_2 = local
    at = Place(dps)

    own = [
        pltpu.make_async_copy(
            pieces[kind].at[at.block],
            wholes[kind].at[at.pipe, at.block, at.z, at.b]
            if kind < EMB
            else wholes[kind].at[at.block, at.z, at.b],
            own_sem.at[kind],
        )
        for kind in range(4)
    ]
    def split(kind, back):
        copies = []
        for k in range(1, SECT):
            if back:
                region = wholes[kind].at[at.pipe_at(SECT - k), at.block, at.z, at.b]
                src = region
            else:
                block = at.block_of(at.pipe_at(k))
                region = wholes[kind].at[at.pipe, block, at.z, at.b]
                src = pieces[kind].at[block]
            sems = p_send.at[kind, k - 1], p_recv.at[kind, k - 1]
            copies.append(remote(src, region, *sems, (at.pipe_at(k), at.dp)))
        return copies

    def chunk(kind, section):
        if kind == EMB:
            return Spread(at, wholes[kind], send.at[3 * SECT], recv.at[3 * SECT])
        number = 3 * section + kind
        sort = SpreadCross if kind in CROSS else Spread
        return sort(at, wholes[kind].at[section], send.at[number], recv.at[number], HALVES[kind])

    def load(kind, section, core):
        blocks = pl.ds(core * 2, 2)
        src, dst = wholes[kind], buffers[kind]
        if kind != EMB:
            src, dst = src.at[section], dst.at[section % 2]
        sem = w_sem.at[kind, section % 2, core]
        return pltpu.make_async_copy(src.at[blocks], dst.at[blocks], sem)

    def loaded(kind, section):
        load(kind, section, at.c).wait()
        load(kind, section, 1 - at.c).wait()

    arrived = []

    def act(op, kind, section):
        if op == 0:
            if kind not in arrived:
                arrived.append(kind)
                own[kind].wait()
                if kind == EMB:
                    chunk(kind, section).start(0)
                    return
                for copy in split(kind, True):
                    copy.wait_recv()
                for copy in split(kind, False):
                    copy.wait_send()
                if kind == 0:
                    copies_start(split(1, False))
                    copies_start(split(2, False))
            chunk(kind, section).start(0)
        elif op < 4:
            chunk(kind, section).move(op - 1)
            if op == 3:
                load(kind, section, at.c).start()
        else:
            chunk(kind, section).land(3)
            load(kind, section, 1 - at.c).start()

    def saves(section, early):
        which = (1, 2, 3, 4, 5, 9, 10) if early else (6, 7, 8, 11)
        return [
            pltpu.make_async_copy(local[i], kept[i].at[section], kept_sem.at[i]) for i in which
        ]

    series, embed_weight, embed_bias, qkv, out_w, up_w, down_w, gains, biases = held
    gets = copies_of(zip(given, held), given_sem)
    for i in (3, 7, 8, 1, 2, 4, 5, 6, 0):
        gets[i].start()
    pick[...] = group_rows(groups[0])
    at.greet()
    copies_wait([gets[i] for i in (3, 7, 8)])
    pack_mix(pieces[0], qkv, gains, biases)
    own[0].start()
    at.met()
    copies_start(split(0, False))
    copies_wait(gets[1:3])
    pack_embedding(pieces[EMB], embed_weight, embed_bias, emb_rows)
    own[EMB].start()
    copies_wait(gets[4:7])
    pack_up(pieces[1], out_w, up_w)
    own[1].start()
    pack_down(pieces[2], down_w)
    own[2].start()
    table[...] = jnp.zeros_like(table)
    gets[0].wait()
    expand(series, groups[0], x)

    def before(name, piece):
        loaded(EMB, 0)
        embed(size, buffers[EMB], pick, x, wsel, h)

    follow(FORWARD_START, 0, act, before)

    @pl.loop(0, SECT)
    def _(section):
        att, up, down = (ref.at[section % 2] for ref in buffers[:3])
        keep_h = pltpu.make_async_copy(h, kept[0].at[section], kept_sem.at[0])

        def compute(name, piece):
            if name == "mix":
                if piece == 0:

                    @pl.when(section > 0)
                    def _():
                        copies_wait(saves(section - 1, True))

                    keep_h.start()
                    loaded(0, section)
                    read_vectors(att, table, size.bs, size.qkv)
                forward_mix(size, att, table, h, mixed, piece)
            elif name == "attend":
                forward_attend(mixed, probs, attended, piece)
            elif name == "project":
                loaded(1, section)
                forward_project(size, up, table, h, attended, first, scale_1, normed)
                copies_start(saves(section, True))
            elif name == "up":
                if piece == 0:

                    @pl.when(section > 0)
                    def _():
                        copies_wait(saves(section - 1, False))

                forward_up(size, up, table, normed, slope, hidden, piece)
            else:
                if piece == 0:
                    loaded(2, section)
                    keep_h.wait()
                forward_down(size, down, table, normed, hidden, second, scale_2, h, piece)
                if piece == 1:
                    copies_start(saves(section, False))

        follow(FORWARD_PERIOD, section, act, compute)

    out[...] = h[...]
    copies_wait(saves(SECT - 1, True))
    copies_wait(saves(SECT - 1, False))


def copies_of(pairs, sems):
    return [pltpu.make_async_copy(src, dst, sems.at[i]) for i, (src, dst) in enumerate(pairs)]


def forward_all(groups, given, dps):
    size = Sizes(dps)
    low, wide = jnp.bfloat16, jnp.float32
    shapes = saved_shapes()
    rows = (size.att, size.dense, size.wide, 2 * WIDE // dps)
    chunks = [chunk_shape(size, count) for count in rows]
    anywhere = pl.BlockSpec(memory_space=pl.ANY)
    inside = pl.BlockSpec(memory_space=pltpu.VMEM)
    outs = [((WIDE, WIDE), low)]
    outs += [((SECT,) + shape, low) for shape in chunks[:3]] + [(chunks[3], low)]
    outs += [((WINDOW, WIDE), low), ((WIDE, WIDE), low)]
    outs += [((SECT,) + shape, dtype) for shape, dtype in shapes]
    scratch = shapes + [((2,) + shape, low) for shape in chunks[:3]] + [(chunks[3], low)]
    scratch += [((SECT, count, LANES), low) for count in rows]
    scratch += [(array.shape, array.dtype) for array in given]
    scratch += [((LANES, LANES), wide), ((16, LANES), low)]
    slots = max(Spread.slots(size.bs), SpreadCross.slots(size.bs))
    dma = pltpu.SemaphoreType.DMA
    return pl.pallas_call(
        partial(forward_kernel, dps),
        out_shape=[jax.ShapeDtypeStruct(shape, dtype) for shape, dtype in outs],
        in_specs=[pl.BlockSpec(memory_space=pltpu.SMEM)] + [anywhere] * len(given),
        out_specs=[inside] + [anywhere] * 4 + [inside] * 2 + [anywhere] * len(shapes),
        scratch_shapes=[pltpu.VMEM(shape, dtype) for shape, dtype in scratch]
        + [
            dma((len(given),)),
            dma((4, 2, 2)),
            dma((len(shapes),)),
            dma((4,)),
            dma((3, SECT - 1)),
            dma((3, SECT - 1)),
            dma((1 + 3 * SECT, slots)),
            dma((1 + 3 * SECT, slots)),
        ],
        compiler_params=pltpu.CompilerParams(
            collective_id=0, has_side_effects=True, vmem_limit_bytes=60 * 1024 * 1024
        ),
        name="gather_forward",
    )(groups, *given)


FETCHES = {
    ("norm2", 0): (("second", "scale_2"), ("second", "scale_2")),
    ("down", 0): (("hidden",), ()),
    ("down", 1): ((), ("hidden",)),
    ("gelu", 0): (("slope", 2), ()),
    ("gelu", 1): ((), ("slope", 2)),
    ("up", 0): (("normed",), ("normed",)),
    ("normed", 0): ((1,), ()),
    ("norm1", 0): (("first", "scale_1", "attended"), ("first", "scale_1", "attended", 1)),
    ("attend", 0): (("mixed", "probs"), ()),
    ("attend", 3): ((), ("mixed", "probs")),
    ("mix", 0): (("h",), ()),
    ("mix", 1): ((), ("h",)),
    ("input", 0): ((0,), (0,)),
}


def backward_kernel(dps, groups, att, up, down, cotangent, x_in, wsel_in, *refs):
    size = Sizes(dps)
    kept, refs = refs[:12], refs[12:]
    series_grad, outs, refs = refs[0], refs[1:5], refs[5:]
    local, refs = refs[:11], refs[11:]
    tables, w_att, w_up, w_down, dtable, dy, dnormed, dlow, dlow_t, dmixed, dup = refs[:11]
    x, wsel, pick, delta, refs = *refs[11:15], refs[15:]
    kinds = []
    for kind in range(4):
        count = 6 if kind in CROSS else 5
        kinds.append(refs[:4] + (refs[4 : 4 + count],))
        refs = refs[4 + count :]
    w_sem, kept_sem, table_sem, late_sem, out_sem, p_send, p_recv, send, recv, credit = refs
    h, mixed, probs, attended, first, normed, slope, hidden, second, scale_1, scale_2 = local
    at = Place(dps)
    last = SECT - 1

    def weights(kind, section):
        src, dst = ((att, w_att), (up, w_up), (down, w_down))[kind]
        return pltpu.make_async_copy(src.at[section], dst, w_sem.at[kind])

    names = ("h", "mixed", "probs", "attended", "first", "normed", "slope", "hidden", "second")
    names += ("table", "scale_1", "scale_2")
    held = dict(zip(names[:9] + names[10:], local))

    def fetches(section, *wanted):
        found = []
        for name in wanted:
            if isinstance(name, int):
                found.append(weights(name, section))
            else:
                i = names.index(name)
                dst = held[name]
                found.append(pltpu.make_async_copy(kept[i].at[section], dst, kept_sem.at[i]))
        return found

    def chunk(kind, i):
        grads, totals, finals, landing, bufs = kinds[kind]
        sort = FoldCross if kind in CROSS else Fold
        refs = (grads, totals.at[i % 2], landing, bufs, finals.at[i])
        return sort(at, *refs, send.at[kind], recv.at[kind], credit.at[kind], HALVES[kind])

    def hand_over(kind, i):
        landing = outs[kind].at[at.block]
        final = kinds[kind][2].at[i]
        return (
            pltpu.make_async_copy(final, landing, out_sem.at[kind]),
            remote(final, landing, p_send.at[kind, i], p_recv.at[kind, at.pipe], (last - i, at.dp)),
        )

    def act(op, kind, i):
        again, more = (False, False) if kind == EMB else (i > 0, i < last)
        if op == 0:
            chunk(kind, i).start(0, again)
        elif op < 4:
            chunk(kind, i).move(op - 1, again, more)
        else:
            chunk(kind, i).land(3, more)
            if kind == EMB:
                outs[kind][...] = kinds[kind][2][0]
            else:
                here, away = hand_over(kind, i)

                @pl.when(at.pipe == last - i)
                def _():
                    here.start()

                @pl.when(at.pipe != last - i)
                def _():
                    away.start()

    copies_start(fetches(last, "second", "scale_2", "hidden", "slope", 2, "normed", 1))
    get_tables = pltpu.make_async_copy(kept[9], tables, table_sem)
    get_tables.start()
    copies_start(fetches(last, "first", "scale_1", "attended", "mixed", "probs", "h", 0))
    late = copies_of(((cotangent, dy), (x_in, x), (wsel_in, wsel)), late_sem)
    copies_start(late)
    pick[...] = group_rows(groups[0])
    at.greet()
    at.met()
    get_tables.wait()
    late[0].wait()

    @pl.loop(0, SECT)
    def _(i):
        section = last - i
        table = tables.at[section]

        def compute(name, piece):
            need, free = FETCHES.get((name, piece), ((), ()))
            copies_wait(fetches(section, *need))
            if name == "norm2":
                backward_norm_two(table, dtable, dy, second, scale_2, dnormed, dlow, dlow_t)
            elif name == "down":
                backward_down(size, kinds[2][0], hidden, dlow_t, piece)
            elif name == "gelu":
                backward_gelu(size, w_down, dtable, slope, dlow, dup, piece)
            elif name == "up":
                backward_up(size, kinds[1][0], normed, dup)
            elif name == "normed":
                backward_normed(size, w_up, dnormed, dup)
            elif name == "norm1":
                backward_norm_one(
                    size,
                    w_up,
                    table,
                    kinds[1][0],
                    dtable,
                    first,
                    scale_1,
                    attended,
                    dnormed,
                    dlow,
                    dlow_t,
                    delta,
                )
            elif name == "attend":
                backward_attend(mixed, probs, delta, dtable, dlow, dmixed, piece)
            elif name == "mix":
                backward_mix(size, kinds[0][0], h, dmixed, piece)
                if piece == 1:
                    write_vectors(kinds[0][0], dtable, size.bs, size.qkv)
            else:
                backward_input(size, w_att, dnormed, dmixed, dy)
            if free:

                @pl.when(section > 0)
                def _():
                    copies_start(fetches(section - 1, *free))

        follow(BACKWARD_PERIOD, i, act, compute)

    def after(name, piece):
        copies_wait(late[1:])
        embed_back(size, pick, x, wsel, dy, kinds[EMB][0], series_grad)

    follow(BACKWARD_END, 0, act, after)

    for kind in range(3):
        for i in range(SECT):
            here, away = hand_over(kind, i)

            @pl.when(at.pipe == last - i)
            def _():
                here.wait()

            @pl.when(at.pipe != last - i)
            def _():
                away.wait_send()

        for k in range(1, SECT):
            other = at.pipe_at(k)
            landing = outs[kind].at[at.block_of(other)]
            sems = p_send.at[kind, 0], p_recv.at[kind, other]
            remote(landing, landing, *sems, (other, at.dp)).wait_recv()


def backward_all(groups, weights, cotangent, x, wsel, kept, history, dps):
    size = Sizes(dps)
    low, wide = jnp.bfloat16, jnp.float32
    anywhere = pl.BlockSpec(memory_space=pl.ANY)
    inside = pl.BlockSpec(memory_space=pltpu.VMEM)
    shapes = saved_shapes()
    rows_emb = 8 * WIDE // (SECT * dps)
    kind_rows = (size.att, size.dense, size.wide, rows_emb)
    scratch = shapes[:9] + shapes[10:] + [((SECT,) + shapes[9][0], wide)]
    scratch += [(chunk_shape(size, rows), low) for rows in kind_rows[:3]]
    scratch += [
        (shapes[9][0], wide),
        ((WIDE, WIDE), low),
        ((WIDE, WIDE), wide),
        ((WIDE, WIDE), low),
        ((WIDE, WIDE), low),
        ((WIDE, 3 * WIDE), low),
        ((WIDE, 4 * WIDE), low),
        ((WIDE, WIDE), low),
        ((WINDOW, WIDE), low),
        ((16, LANES), low),
        ((16, WIDE), wide),
    ]
    for kind, rows in enumerate(kind_rows):
        sets, results = (1, 1) if kind == EMB else (2, SECT)
        scratch += [
            (chunk_shape(size, rows), low),
            ((sets, 2, ZS, size.bs, rows, LANES), low),
            ((results, rows, LANES), low),
            ((2, ZS, size.bs, rows, LANES), low),
        ]
        sort = FoldCross if kind in CROSS else Fold
        scratch += [(shape, low) for shape in sort.buffers(size.bs, rows, HALVES[kind])]
    slots = max(Fold.slots(size.bs), FoldCross.slots(size.bs))
    dma = pltpu.SemaphoreType.DMA
    return pl.pallas_call(
        partial(backward_kernel, dps),
        out_shape=[jax.ShapeDtypeStruct((history, WIDE), wide)]
        + [jax.ShapeDtypeStruct((SECT, rows, LANES), low) for rows in kind_rows[:3]]
        + [jax.ShapeDtypeStruct((rows_emb, LANES), low)],
        in_specs=[pl.BlockSpec(memory_space=pltpu.SMEM)] + [anywhere] * (6 + len(kept)),
        out_specs=[inside] + [anywhere] * 3 + [inside],
        scratch_shapes=[pltpu.VMEM(shape, dtype) for shape, dtype in scratch]
        + [
            dma((3,)),
            dma((12,)),
            dma(()),
            dma((3,)),
            dma((3,)),
            dma((3, SECT)),
            dma((3, SECT)),
            dma((4, slots)),
            dma((4, slots)),
            pltpu.SemaphoreType.REGULAR((4, slots)),
        ],
        compiler_params=pltpu.CompilerParams(
            collective_id=1, has_side_effects=True, vmem_limit_bytes=60 * 1024 * 1024
        ),
        name="backward_fold",
    )(groups, *weights, cotangent, x, wsel, *kept)


def finish_kernel(dps, n_gains, n_biases, *refs):
    size = Sizes(dps)
    given, refs = refs[:6], refs[6:]
    block_out, series_out, embed_w, embed_b, qkv, out, up_out, down_out, gains, biases = refs[:10]
    att, up, down, emb, sems = refs[10:]
    copies = copies_of(zip(given, (att, up, down, emb, block_out, series_out)), sems)
    copies_start(copies)
    copies_wait(copies[:4])
    for lb in range(SECT):
        lanes = slice(lb * LANES, (lb + 1) * LANES)
        qkv[:, lanes] = att[lb, : size.qkv].astype(jnp.float32)
        out[:, lanes] = up[lb, : size.out].astype(jnp.float32)
        up_out[:, lanes] = up[lb, size.out :].astype(jnp.float32)
        for j in range(4):
            rows = slice(j * size.down, (j + 1) * size.down)
            start = j * WIDE + lb * LANES
            down_out[:, start : start + LANES] = down[lb, rows].astype(jnp.float32)
    tiles = [att[lb, size.qkv :].astype(jnp.float32) for lb in range(SECT)]
    flat = jnp.concatenate([tile[row : row + 1] for row in range(2) for tile in tiles], axis=1)
    gains[...] = flat[:, :n_gains]
    biases[...] = flat[:, n_gains : n_gains + n_biases]
    rows = emb.shape[0] // 8
    packed = emb[...].astype(jnp.float32)
    packed = [packed[i * rows : (i + 1) * rows] for i in range(8)]
    square = jnp.concatenate([packed[0], jnp.zeros((LANES - rows, LANES), jnp.float32)], axis=0)
    embed_b[...] = square.T[:GROUPS, :rows]
    packed = jnp.concatenate(packed, axis=1)
    ends = ((1024, L1), (768, L2), (512, L3))
    embed_w[...] = jnp.concatenate([packed[:, end - span : end] for end, span in ends], axis=1)
    copies_wait(copies[4:])


def finish_all(sums, block, series, n_gains, n_biases, dps):
    size = Sizes(dps)
    wide = jnp.float32
    columns = WIDE // (SECT * dps)
    outs = [
        (block.shape, block.dtype),
        (series.shape, wide),
        ((columns, L1 + L2 + L3), wide),
        ((GROUPS, columns), wide),
        ((size.qkv, WIDE), wide),
        ((size.out, WIDE), wide),
        ((size.up, WIDE), wide),
        ((size.down, 4 * WIDE), wide),
        ((1, n_gains), wide),
        ((1, n_biases), wide),
    ]
    anywhere = pl.BlockSpec(memory_space=pl.ANY)
    inside = pl.BlockSpec(memory_space=pltpu.VMEM)
    return pl.pallas_call(
        partial(finish_kernel, dps, n_gains, n_biases),
        out_shape=[jax.ShapeDtypeStruct(shape, dtype) for shape, dtype in outs],
        in_specs=[anywhere] * 6,
        out_specs=[inside] * 10,
        scratch_shapes=[pltpu.VMEM(array.shape, array.dtype) for array in sums]
        + [pltpu.SemaphoreType.DMA((6,))],
        compiler_params=pltpu.CompilerParams(vmem_limit_bytes=60 * 1024 * 1024),
        name="finish",
    )(*sums, block, series)


def per_device(
    series,
    groups,
    cotangent,
    embed_weight,
    embed_bias,
    qkv_weight,
    out_weight,
    up_weight,
    down_weight,
    gains,
    biases,
):
    dps = lax.axis_size("dp")
    given = (
        series[0],
        embed_weight.T,
        embed_bias,
        qkv_weight[0],
        out_weight[0],
        up_weight[0],
        down_weight[0],
        gains,
        biases,
    )
    block_output, att, up, down, _, wsel, x, *kept = forward_all(groups, given, dps)
    series_grad, *sums = backward_all(
        groups, (att, up, down), cotangent[0], x, wsel, kept, series.shape[1], dps
    )
    outs = finish_all(sums, block_output, series_grad, gains.shape[1], biases.shape[1], dps)
    block_output, series_grad, embed_w, embed_b, qkv, out, up, down, gain_sum, bias_sum = outs
    return (
        block_output[None],
        series_grad[None],
        embed_w.T,
        embed_b,
        qkv[None],
        out[None],
        up[None],
        down[None],
        gain_sum,
        bias_sum,
    )


def solution(mesh):
    return jax.shard_map(
        per_device,
        mesh=mesh,
        in_specs=(
            P(("pipe", "dp"), None, None),
            P(("pipe", "dp")),
            P(("pipe", "dp"), None, None),
            P(None, "dp"),
            P(None, "dp"),
            P("pipe", "dp", None),
            P("pipe", "dp", None),
            P("pipe", "dp", None),
            P("pipe", "dp", None),
            P("pipe", "dp"),
            P("pipe", "dp"),
        ),
        out_specs=(
            P(("pipe", "dp"), None, None),
            P(("pipe", "dp"), None, None),
            P(None, ("pipe", "dp")),
            P(None, ("pipe", "dp")),
            P("pipe", "dp", None),
            P("pipe", "dp", None),
            P("pipe", "dp", None),
            P("pipe", "dp", None),
            P("pipe", "dp"),
            P("pipe", "dp"),
        ),
        check_vma=False,
    )
```

```python
from functools import partial
import math

import jax
import jax.numpy as jnp
from jax import lax
from jax.experimental import pallas as pl
from jax.experimental.pallas import tpu as pltpu
from jax.sharding import PartitionSpec as P

HEAD = 64
L1 = 96
L2 = 192
L3 = 336
GROUPS = 3


NORM_EPS = 1e-05


MESH = pl.DeviceIdType.MESH
LANES = 128
ZS = 4
SECT = 4
EMB = 3


class Place:
    def __init__(self, dps):
        self.bs = bs = dps // ZS
        pipe = lax.axis_index("pipe")
        dp = lax.axis_index("dp")
        self.pipe, self.dp = pipe, dp
        self.x, self.c = x, c = lax.div(pipe, 2), lax.rem(pipe, 2)
        self.z, self.b = z, b = lax.div(dp, bs), lax.rem(dp, bs)
        self.block = c * 2 + x
        self.other_block = c * 2 + 1 - x
        self.x_peer = ((1 - x) * 2 + c, dp)
        self.core_peer = (x * 2 + 1 - c, dp)
        self.pipes = [lax.rem(pipe + k, SECT) for k in range(SECT)]
        self.blocks = [self.block_of(other) for other in self.pipes]
        self.zs = [lax.rem(z + k, ZS) for k in range(ZS)]
        self.bees = [lax.rem(b + k, bs) for k in range(bs)]
        self.z_peers = [(pipe, other * bs + b) for other in self.zs]
        self.b_peers = [(pipe, z * bs + other) for other in self.bees]

    def block_of(self, pipe):
        return lax.rem(pipe, 2) * 2 + lax.div(pipe, 2)

    def pipe_at(self, step):
        return self.pipes[step % SECT]

    def z_at(self, step):
        return self.zs[step % ZS]

    def b_at(self, step):
        return self.bees[step % self.bs]

    def z_peer(self, step):
        return self.z_peers[step % ZS]

    def b_peer(self, step):
        return self.b_peers[step % self.bs]

    def greet(self):
        barrier = pltpu.get_barrier_semaphore()
        peers = [(self.pipe_at(k), self.dp) for k in range(1, SECT)]
        peers += [self.z_peer(k) for k in range(1, ZS)]
        peers += [self.b_peer(k) for k in range(1, self.bs)]
        for peer in peers:
            pl.semaphore_signal(barrier, inc=1, device_id=peer, device_id_type=MESH)

    def met(self):
        pl.semaphore_wait(pltpu.get_barrier_semaphore(), SECT + ZS + self.bs - 3)


def remote(src, dst, send, recv, peer):
    return pltpu.make_async_remote_copy(
        src_ref=src, dst_ref=dst, send_sem=send, recv_sem=recv, device_id=peer, device_id_type=MESH
    )


FORWARD_START = (
    (0, 3, 0),
    (0, 0, 0),
    (0, 2, 0),
    (1, 3, 0),
    (1, 0, 0),
    (0, 1, 0),
    (2, 3, 0),
    (2, 0, 0),
    (0, 0, 1),
    (1, 1, 0),
    (1, 2, 0),
    (3, 3, 0),
    (0, 2, 1),
    (1, 0, 1),
    (2, 1, 0),
    (4, 3, 0),
    (3, 0, 0),
    ("embed",),
    (4, 0, 0),
)
FORWARD_PERIOD = (
    ("mix",),
    (0, 1, 1),
    (2, 0, 1),
    ("mix",),
    ("attend",),
    (3, 1, 0),
    ("attend",),
    (2, 2, 0),
    ("attend",),
    (0, 0, 2),
    (4, 1, 0),
    ("attend",),
    ("project",),
    (1, 1, 1),
    ("up",),
    (1, 2, 1),
    (0, 2, 2),
    (3, 2, 0),
    ("up",),
    (1, 0, 2),
    ("up",),
    (2, 1, 1),
    (3, 0, 1),
    (4, 2, 0),
    ("up",),
    ("down",),
    (4, 0, 1),
    ("down",),
)
BACKWARD_PERIOD = (
    ("norm2",),
    (1, 0, -1),
    ("down",),
    ("down",),
    ("gelu",),
    ("gelu",),
    (2, 1, -1),
    (0, 2, 0),
    ("up",),
    ("normed",),
    (2, 0, -1),
    ("norm1",),
    (4, 1, -2),
    (4, 2, -2),
    (1, 2, 0),
    (3, 1, -1),
    (0, 1, 0),
    ("attend",),
    ("attend",),
    ("attend",),
    ("attend",),
    (3, 2, -1),
    (1, 1, 0),
    (4, 0, -2),
    (3, 0, -1),
    ("mix",),
    ("mix",),
    (0, 0, 0),
    ("input",),
    (2, 2, 0),
)
BACKWARD_END = (
    ("embed",),
    (1, 0, 3),
    (2, 1, 3),
    (2, 0, 3),
    (4, 1, 2),
    (4, 2, 2),
    (3, 1, 3),
    (0, 3, 0),
    (3, 2, 3),
    (4, 0, 2),
    (1, 3, 0),
    (3, 0, 3),
    (2, 3, 0),
    (3, 3, 0),
    (4, 1, 3),
    (4, 2, 3),
    (4, 0, 3),
    (4, 3, 0),
)


def copies_start(copies):
    for copy in copies:
        copy.start()


def copies_wait(copies):
    for copy in copies:
        copy.wait()


class Spread:
    def __init__(self, at, out, send, recv, half=ZS // 2):
        self.at, self.out, self.send, self.recv = at, out, send, recv
        nb = at.bs - 1
        self.slot_z = 0
        self.slot_b1 = ZS - 1
        self.slot_x1 = self.slot_b1 + nb
        self.slot_x2 = self.slot_x1 + 1
        self.slot_b2 = self.slot_x2 + 1
        self.slot_c = self.slot_b2 + nb
        self.half = half

    @staticmethod
    def slots(bs):
        return ZS - 1 + 2 * (bs - 1) + 3

    def copy(self, region, slot, peer):
        return remote(region, region, self.send.at[slot], self.recv.at[slot], peer)

    def copies(self, stage, back):
        at, out, half = self.at, self.out, self.half
        rest = pl.ds(half, ZS - half)
        x_block = at.other_block if back else at.block
        if stage == 0:
            return [
                self.copy(
                    out.at[at.block, at.z_at(ZS - k) if back else at.z, at.b],
                    self.slot_z + k - 1,
                    at.z_peer(k),
                )
                for k in range(1, ZS)
            ]
        if stage == 3:
            core = 1 - at.c if back else at.c
            return [self.copy(out.at[pl.ds(core * 2, 2)], self.slot_c, at.core_peer)]
        copies = []
        for k in range(1, at.bs):
            b = at.b_at(at.bs - k) if back else at.b
            if stage == 1:
                region, slot = out.at[at.block, pl.ds(0, half), b], self.slot_b1
            else:
                region, slot = out.at[pl.ds(at.c * 2, 2), rest, b], self.slot_b2
            copies.append(self.copy(region, slot + k - 1, at.b_peer(k)))
        if stage == 1:
            region, slot = out.at[x_block, rest, at.b], self.slot_x1
        else:
            region, slot = out.at[x_block, pl.ds(0, half)], self.slot_x2
        copies.append(self.copy(region, slot, at.x_peer))
        return copies

    def start(self, stage):
        copies_start(self.copies(stage, False))

    def land(self, stage):
        for copy in self.copies(stage, True):
            copy.wait_recv()
        for copy in self.copies(stage, False):
            copy.wait_send()

    def move(self, stage):
        self.land(stage)
        self.start(stage + 1)


class SpreadCross(Spread):
    @staticmethod
    def slots(bs):
        return 2 * bs + 2 * ZS - 1

    def copies(self, stage, back):
        at, out = self.at, self.out
        rows = out.shape[-2]
        cut = rows // 32 * 16
        some, rest = pl.ds(0, cut), pl.ds(cut, rows - cut)
        core = 1 - at.c if back else at.c
        if stage == 3:
            return [self.copy(out.at[pl.ds(core * 2, 2)], 2 * at.bs + 2 * ZS - 2, at.core_peer)]
        both = pl.ds(at.c * 2, 2)
        x_block = at.other_block if back else at.block
        copies = []
        if stage == 1:
            for k in range(1, ZS):
                z = at.z_at(ZS - k) if back else at.z
                copies.append(self.copy(out.at[both, z, at.b, some], at.bs + k - 1, at.z_peer(k)))
                slot = at.bs + ZS + k - 2
                copies.append(self.copy(out.at[at.block, z, :, rest], slot, at.z_peer(k)))
            return copies
        base = 0 if stage == 0 else at.bs + 2 * ZS - 2
        for k in range(1, at.bs):
            b = at.b_at(at.bs - k) if back else at.b
            region = out.at[at.block, at.z, b, rest] if stage == 0 else out.at[both, :, b, some]
            copies.append(self.copy(region, base + k, at.b_peer(k)))
        if stage == 0:
            region = out.at[x_block, at.z, at.b, some]
        else:
            region = out.at[x_block, :, :, rest]
        copies.append(self.copy(region, base, at.x_peer))
        return copies


class Fold:
    def __init__(self, at, grads, total, landing, bufs, final, send, recv, credit, half):
        self.at, self.grads, self.total = at, grads, total
        self.landing, self.bufs, self.final = landing, bufs, final
        self.send, self.recv, self.credit = send, recv, credit
        self.half = half
        nb = at.bs - 1
        self.slot_x1 = 1
        self.slot_b1 = 2
        self.slot_x2 = 2 + nb
        self.slot_b2 = 3 + nb
        self.slot_z = 3 + 2 * nb

    @staticmethod
    def slots(bs):
        return 3 + 2 * (bs - 1) + ZS - 1

    @staticmethod
    def buffers(bs, rows, half):
        nb = max(bs - 1, 1)
        rest = ZS - half
        return [
            (half, bs, rows, LANES),
            (nb, 2, rest, rows, LANES),
            (rest, rows, LANES),
            (nb, half, rows, LANES),
            (ZS - 1, rows, LANES),
        ]

    def core_parts(self):
        other = self.grads.at[pl.ds((1 - self.at.c) * 2, 2)]
        return [(other, self.landing, 0, self.at.core_peer, self.at.core_peer)]

    def parts(self, stage):
        at, half, total, bufs = self.at, self.half, self.total, self.bufs
        if stage == 0:
            return self.core_parts()
        if stage == 3:
            return [
                (
                    total.at[at.x, at.z_at(k), at.b],
                    bufs[4].at[k - 1],
                    self.slot_z + k - 1,
                    at.z_peer(k),
                    at.z_peer(ZS - k),
                )
                for k in range(1, ZS)
            ]
        rest = pl.ds(half, ZS - half)
        found = []
        for k in range(1, at.bs):
            if stage == 1:
                src, buf, slot = total.at[:, rest, at.b_at(k)], bufs[1], self.slot_b1
            else:
                src, buf, slot = total.at[at.x, pl.ds(0, half), at.b_at(k)], bufs[3], self.slot_b2
            found.append((src, buf.at[k - 1], slot + k - 1, at.b_peer(k), at.b_peer(at.bs - k)))
        if stage == 1:
            src, buf, slot = total.at[1 - at.x, pl.ds(0, half)], bufs[0], self.slot_x1
        else:
            src, buf, slot = total.at[1 - at.x, rest, at.b], bufs[2], self.slot_x2
        found.append((src, buf, slot, at.x_peer, at.x_peer))
        return found

    def start(self, stage, again):
        for src, buf, slot, to, _ in self.parts(stage):
            if again is not False:

                @pl.when(again)
                def _():
                    pl.semaphore_wait(self.credit.at[slot], 1)

            remote(src, buf, self.send.at[slot], self.recv.at[slot], to).start()

    def land(self, stage, more):
        parts = self.parts(stage)
        for src, buf, slot, to, _ in parts:
            remote(src, buf, self.send.at[slot], self.recv.at[slot], to).wait()
        self.add(stage)
        if more is not False:

            @pl.when(more)
            def _():
                for _, _, slot, _, origin in parts:
                    pl.semaphore_signal(
                        self.credit.at[slot], inc=1, device_id=origin, device_id_type=MESH
                    )

    def add_core(self):
        at, bs, total = self.at, self.at.bs, self.total

        @pl.loop(0, 2 * ZS * bs)
        def _(i):
            z, b = i // bs % ZS, i % bs
            x = i // (ZS * bs)
            total[x, z, b] = self.grads[at.c * 2 + x, z, b] + self.landing[x, z, b]

    def add(self, stage):
        at, half, bs = self.at, self.half, self.at.bs
        total, bufs = self.total, self.bufs
        rest = ZS - half
        if stage == 0:
            self.add_core()
        elif stage == 1:

            @pl.loop(0, half * bs)
            def _(i):
                z, b = i // bs, i % bs
                total[at.x, z, b] = total[at.x, z, b] + bufs[0][z, b]

            @pl.loop(0, 2 * rest)
            def _(i):
                x, z = i // rest, i % rest
                for k in range(bs - 1):
                    total[x, half + z, at.b] = total[x, half + z, at.b] + bufs[1][k, x, z]

        elif stage == 2:

            @pl.loop(0, rest)
            def _(z):
                total[at.x, half + z, at.b] = total[at.x, half + z, at.b] + bufs[2][z]

            @pl.loop(0, half)
            def _(z):
                for k in range(bs - 1):
                    total[at.x, z, at.b] = total[at.x, z, at.b] + bufs[3][k, z]

        else:
            self.finish([bufs[4][k] for k in range(ZS - 1)])

    def finish(self, pieces):
        at = self.at
        done = self.total[at.x, at.z, at.b].astype(jnp.float32)
        for piece in pieces:
            done = done + piece.astype(jnp.float32)
        self.final[...] = done.astype(self.final.dtype)

    def move(self, stage, again, more):
        self.land(stage, more)
        self.start(stage + 1, again)


class FoldCross(Fold):
    @staticmethod
    def slots(bs):
        return 2 * bs + 2 * ZS - 1

    @staticmethod
    def buffers(bs, rows, half):
        nb = max(bs - 1, 1)
        cut = rows // 32 * 16
        rest = rows - cut
        return [
            (nb, 2, ZS, cut, LANES),
            (ZS, bs, rest, LANES),
            (ZS - 1, 2, cut, LANES),
            (ZS - 1, bs, rest, LANES),
            (cut, LANES),
            (nb, rest, LANES),
        ]

    def cuts(self):
        rows = self.total.shape[-2]
        cut = rows // 32 * 16
        return pl.ds(0, cut), pl.ds(cut, rows - cut)

    def parts(self, stage):
        at, total, bufs = self.at, self.total, self.bufs
        if stage == 0:
            return self.core_parts()
        some, rest = self.cuts()
        found = []
        if stage == 2:
            for k in range(1, ZS):
                pair = (at.z_peer(k), at.z_peer(ZS - k))
                z = at.z_at(k)
                found.append((total.at[:, z, at.b, some], bufs[2].at[k - 1], at.bs + k, *pair))
                slot = at.bs + ZS + k - 1
                found.append((total.at[at.x, z, :, rest], bufs[3].at[k - 1], slot, *pair))
            return found
        base = 1 if stage == 1 else at.bs + 2 * ZS - 1
        for k in range(1, at.bs):
            pair = (at.b_peer(k), at.b_peer(at.bs - k))
            if stage == 1:
                src, buf = total.at[:, :, at.b_at(k), some], bufs[0].at[k - 1]
            else:
                src, buf = total.at[at.x, at.z, at.b_at(k), rest], bufs[5].at[k - 1]
            found.append((src, buf, base + k, *pair))
        if stage == 1:
            src, buf = total.at[1 - at.x, :, :, rest], bufs[1]
        else:
            src, buf = total.at[1 - at.x, at.z, at.b, some], bufs[4]
        found.append((src, buf, base, at.x_peer, at.x_peer))
        return found

    def add(self, stage):
        at, bs = self.at, self.at.bs
        total, bufs = self.total, self.bufs
        some, rest = self.cuts()
        if stage == 0:
            self.add_core()
        elif stage == 1:

            @pl.loop(0, 2 * ZS)
            def _(i):
                x, z = i // ZS, i % ZS
                for k in range(bs - 1):
                    total[x, z, at.b, some] = total[x, z, at.b, some] + bufs[0][k, x, z]

            @pl.loop(0, ZS * bs)
            def _(i):
                z, b = i // bs, i % bs
                total[at.x, z, b, rest] = total[at.x, z, b, rest] + bufs[1][z, b]

        elif stage == 2:
            for x in range(2):
                for k in range(ZS - 1):
                    total[x, at.z, at.b, some] = total[x, at.z, at.b, some] + bufs[2][k, x]

            @pl.loop(0, bs)
            def _(b):
                for k in range(ZS - 1):
                    total[at.x, at.z, b, rest] = total[at.x, at.z, b, rest] + bufs[3][k, b]

        else:
            total[at.x, at.z, at.b, some] = total[at.x, at.z, at.b, some] + bufs[4][...]
            for k in range(bs - 1):
                total[at.x, at.z, at.b, rest] = total[at.x, at.z, at.b, rest] + bufs[5][k]
            self.final[...] = total[at.x, at.z, at.b]


HALF = 256
WIDE = 512
QKV_TILE = 768
VEC_ROWS = 16


STEP = 64


def by_rows(fn, *arrays, step=STEP):
    parts = [
        fn(*[array[at : at + step] for array in arrays])
        for at in range(0, arrays[0].shape[0], step)
    ]
    if isinstance(parts[0], tuple):
        return tuple(jnp.concatenate(part, axis=0) for part in zip(*parts))
    return jnp.concatenate(parts, axis=0)


def dot_nt(a, b):
    return lax.dot_general(a, b, (((1,), (1,)), ((), ())), preferred_element_type=jnp.float32)


def dot_nn(a, b):
    return lax.dot_general(a, b, (((1,), (0,)), ((), ())), preferred_element_type=jnp.float32)


def dot_tn(a, b):
    return lax.dot_general(a, b, (((0,), (0,)), ((), ())), preferred_element_type=jnp.float32)


def aligned(index, unit):
    return pl.multiple_of(index, unit)


def rows_of(ref, bs, first, count, start, rows, blocks=range(SECT)):
    parts = []
    for i in range(count):
        d = first + i
        place = (d // bs, d % bs)
        parts.append(
            jnp.concatenate(
                [ref[(lb,) + place + (pl.ds(start, rows), slice(None))] for lb in blocks], axis=1
            )
        )
    return parts[0] if count == 1 else jnp.concatenate(parts, axis=0)


def put_rows(ref, bs, first, count, start, rows, value, block=0):
    value = value.astype(ref.dtype)
    for i in range(count):
        d = first + i
        place = (d // bs, d % bs)
        for lane in range(value.shape[1] // LANES):
            ref[(block + lane,) + place + (pl.ds(start, rows), slice(None))] = value[
                i * rows : (i + 1) * rows, lane * LANES : (lane + 1) * LANES
            ]


def vector_pieces(dps):
    n_gains, n_biases = 2 * WIDE // dps, 10 * WIDE // dps
    starts = [(0, 0), (0, 2), (1, 0), (1, 2), (2, 0), (2, 1), (2, 2), (2, 3), (3, 0), (3, 2)]
    pieces = []
    for d in range(dps):
        at = 0
        while at < n_gains + n_biases:
            if at < n_gains:
                index = d * n_gains + at
                row, column = (1, 3)[index // WIDE], WIDE + index % WIDE
                left = n_gains - at
            else:
                index = d * n_biases + at - n_gains
                row, part = starts[index // WIDE]
                column = part * WIDE + index % WIDE
                left = n_gains + n_biases - at
            size = min(left, LANES - at % LANES, LANES - column % LANES)
            pieces.append((d, at // WIDE, at % WIDE, row, column, size))
            at += size
    return pieces


def read_vectors(ref, table, bs, start):
    dps = ZS * bs
    tiles = {}
    for d, row, lane, to_row, to_lane, size in vector_pieces(dps):
        key = (d, lane // LANES)
        if key not in tiles:
            tile = ref[lane // LANES, d // bs, d % bs, start : start + VEC_ROWS, :]
            tiles[key] = tile.astype(jnp.float32)
        off = lane % LANES
        table[to_row : to_row + 1, to_lane : to_lane + size] = tiles[key][
            row : row + 1, off : off + size
        ]


def write_vectors(ref, table, bs, start):
    dps = ZS * bs
    found = {}
    for d, row, lane, to_row, to_lane, size in vector_pieces(dps):
        piece = table[to_row : to_row + 1, to_lane : to_lane + size]
        found.setdefault((d, lane // LANES), {}).setdefault(row, []).append(piece)
    row_id = lax.broadcasted_iota(jnp.int32, (VEC_ROWS, LANES), 0)
    for d in range(dps):
        for lb in range(SECT):
            tile = jnp.zeros((VEC_ROWS, LANES), jnp.float32)
            for row, pieces in found.get((d, lb), {}).items():
                have = sum(piece.shape[1] for piece in pieces)
                if have < LANES:
                    pieces = pieces + [jnp.zeros((1, LANES - have), jnp.float32)]
                line = pieces[0] if len(pieces) == 1 else jnp.concatenate(pieces, axis=1)
                tile = jnp.where(row_id == row, line, tile)
            ref[lb, d // bs, d % bs, start : start + VEC_ROWS, :] = tile.astype(ref.dtype)


def fold_rows(x):
    total = x[:8]
    for at in range(8, x.shape[0], 8):
        total = total + x[at : at + 8]
    return total


def normalize(x):
    mean = jnp.mean(x, axis=1, keepdims=True)
    centred = x - mean
    scale = lax.rsqrt(jnp.mean(centred * centred, axis=1, keepdims=True) + NORM_EPS)
    return centred * scale, jnp.broadcast_to(scale, (x.shape[0], LANES))


def normalize_back(unit, scale, grad, gain):
    inner = grad * gain
    first = jnp.mean(inner, axis=1, keepdims=True)
    second = jnp.mean(inner * unit, axis=1, keepdims=True)
    out = jnp.concatenate([scale] * (WIDE // LANES), axis=1) * (inner - first - unit * second)
    return out, fold_rows(out), fold_rows(grad * unit), fold_rows(grad)


def gelu_pair(u):
    below = 0.5 + 0.5 * lax.erf(u * math.sqrt(0.5))
    bell = jnp.exp2((-0.5 * math.log2(math.e)) * (u * u))
    return u * below, below + u * (bell * (1.0 / math.sqrt(2.0 * math.pi)))


def head_masks(scale):
    lane = lax.broadcasted_iota(jnp.int32, (1, LANES), 1)
    first = jnp.where(lane < HEAD, scale, 0.0).astype(jnp.bfloat16)
    second = jnp.where(lane < HEAD, 0.0, scale).astype(jnp.bfloat16)
    return first, second


class Sizes:
    def __init__(self, dps):
        self.dps, self.bs = dps, dps // ZS
        self.qkv, self.out, self.up, self.down = (
            3 * WIDE // dps,
            WIDE // dps,
            4 * WIDE // dps,
            WIDE // dps,
        )
        self.att = self.qkv + VEC_ROWS
        self.dense = self.out + self.up
        self.wide = 4 * self.down


def qkv_rows(size, w, tile):
    count = QKV_TILE // size.qkv
    return rows_of(w, size.bs, tile * count, count, 0, size.qkv)


def out_rows(size, w):
    return rows_of(w, size.bs, 0, size.dps, 0, size.out)


def up_rows(size, w, tile):
    count = HALF // size.up
    return rows_of(w, size.bs, tile * count, count, size.out, size.up)


def forward_mix(size, w, table, h, mixed, piece):
    columns = slice(piece * QKV_TILE, (piece + 1) * QKV_TILE)
    shift = table[0:1, columns]
    out = dot_nt(h[...], qkv_rows(size, w, piece))
    mixed[:, columns] = by_rows(lambda part: (part + shift).astype(mixed.dtype), out)


def softmax_columns(scores):
    parts = [scores[at : at + STEP] for at in range(0, scores.shape[0], STEP)]
    top = parts[0]
    for part in parts[1:]:
        top = jnp.maximum(top, part)
    top = jnp.max(top, axis=0, keepdims=True)
    parts = [jnp.exp(part - top) for part in parts]
    total = parts[0]
    for part in parts[1:]:
        total = total + part
    scale = 1.0 / jnp.sum(total, axis=0, keepdims=True)
    return jnp.concatenate([(part * scale).astype(jnp.bfloat16) for part in parts], axis=0)


def forward_attend(mixed, probs, attended, pair):
    lane = pair * LANES
    key_rows = mixed[:, WIDE + lane : WIDE + lane + LANES]
    values = mixed[:, 2 * WIDE + lane : 2 * WIDE + lane + LANES].T

    for part in range(2):
        rows = slice(part * HALF, (part + 1) * HALF)
        queries = mixed[rows, lane : lane + LANES]
        joined = []
        for head, mask in enumerate(head_masks(1.0 / math.sqrt(HEAD))):
            weights = softmax_columns(dot_nt(key_rows, queries * mask))
            probs[2 * pair + head, :, rows] = weights
            joined.append(dot_nn(values[head * HEAD : (head + 1) * HEAD], weights))
        joined = jnp.concatenate(joined, axis=0).T
        attended[rows, lane : lane + LANES] = joined.astype(attended.dtype)


def forward_project(size, w, table, h, attended, first, scale, normed):
    out = dot_nt(attended[...], out_rows(size, w))
    for part in range(WIDE // STEP):
        rows = slice(part * STEP, (part + 1) * STEP)
        total = h[rows, :].astype(jnp.float32) + (out[rows] + table[1:2, 0:WIDE])
        unit, scale[rows, :] = normalize(total)
        first[rows, :] = unit
        normed[rows, :] = (
            unit * table[1:2, WIDE : 2 * WIDE] + table[1:2, 2 * WIDE : 3 * WIDE]
        ).astype(normed.dtype)


def forward_up(size, w, table, normed, slope, hidden, piece):
    for j in (2 * piece, 2 * piece + 1):
        columns = slice(j * HALF, (j + 1) * HALF)
        shift = table[2:3, columns]
        upper = dot_nt(normed[...], up_rows(size, w, j))
        for part in range(WIDE // STEP):
            rows = slice(part * STEP, (part + 1) * STEP)
            value, grad = gelu_pair(upper[rows] + shift)
            hidden[rows, columns] = value.astype(hidden.dtype)
            slope[rows, columns] = grad.astype(slope.dtype)


def forward_down(size, w, table, normed, hidden, second, scale, h, piece):
    columns = slice(piece * HALF, (piece + 1) * HALF)
    count = size.dps // 2
    matrix = jnp.concatenate(
        [
            rows_of(w, size.bs, piece * count, count, j * size.down, size.down)
            for j in range(4)
        ],
        axis=1,
    )
    out = dot_nt(hidden[...], matrix)
    shift = table[3:4, columns]
    for part in range(WIDE // STEP):
        rows = slice(part * STEP, (part + 1) * STEP)
        second[rows, columns] = normed[rows, columns].astype(jnp.float32) + (out[rows] + shift)
    if piece == 1:
        for part in range(WIDE // STEP):
            rows = slice(part * STEP, (part + 1) * STEP)
            unit, scale[rows, :] = normalize(second[rows, :])
            second[rows, :] = unit
            h[rows, :] = (
                unit * table[3:4, WIDE : 2 * WIDE] + table[3:4, 2 * WIDE : 3 * WIDE]
            ).astype(h.dtype)


def backward_norm_two(table, dtable, dy, second, scale, dnormed, dlow, dlow_t):
    dtable[...] = jnp.zeros_like(dtable)
    sums = [jnp.zeros((8, WIDE), jnp.float32)] * 3
    for part in range(WIDE // STEP):
        rows = slice(part * STEP, (part + 1) * STEP)
        grad, *found = normalize_back(
            second[rows, :],
            scale[rows, :],
            dy[rows, :].astype(jnp.float32),
            table[3:4, WIDE : 2 * WIDE],
        )
        dnormed[rows, :] = grad
        dlow[rows, :] = grad.astype(dlow.dtype)
        sums = [total + new for total, new in zip(sums, found)]
    for i, total in enumerate(sums):
        dtable[3:4, i * WIDE : (i + 1) * WIDE] = jnp.sum(total, axis=0, keepdims=True)
    dlow_t[...] = dlow[...].T


def backward_down(size, grads, hidden, dlow_t, piece):
    @pl.loop(2 * piece, 2 * piece + 2)
    def _(i):
        start = aligned(i * size.down, 16)
        for half in range(2):
            columns = pl.ds(aligned(i * WIDE, WIDE) + half * HALF, HALF)
            value = dot_nn(dlow_t[...], hidden[:, columns])
            put_rows(grads, size.bs, 0, size.dps, start, size.down, value, 2 * half)


def backward_gelu(size, w, dtable, slope, dlow, dup, piece):
    @pl.loop(2 * piece, 2 * piece + 2)
    def _(i):
        start = aligned(i * size.down, 16)
        for half in range(2):
            columns = pl.ds(aligned(i * WIDE, WIDE) + half * HALF, HALF)
            blocks = (2 * half, 2 * half + 1)
            matrix = rows_of(w, size.bs, 0, size.dps, start, size.down, blocks)
            dhidden = dot_nn(dlow[...], matrix)
            total = jnp.zeros((8, HALF), jnp.float32)
            for part in range(WIDE // STEP):
                rows = slice(part * STEP, (part + 1) * STEP)
                dupper = dhidden[rows] * slope[rows, columns].astype(jnp.float32)
                total = total + fold_rows(dupper)
                dup[rows, columns] = dupper.astype(dup.dtype)
            dtable[2:3, columns] = jnp.sum(total, axis=0, keepdims=True)


def backward_up(size, grads, normed, dup):
    count = HALF // size.up

    @pl.loop(0, 4)
    def _(i):
        for half in range(2):
            columns = pl.ds(aligned(i * WIDE, WIDE) + half * HALF, HALF)
            value = dot_tn(dup[:, columns], normed[...])
            first = (2 * i + half) * count
            put_rows(grads, size.bs, first, count, size.out, size.up, value)


def backward_normed(size, w, dnormed, dup):
    for half in range(2):
        columns = slice(half * HALF, (half + 1) * HALF)
        blocks = (2 * half, 2 * half + 1)
        matrix = rows_of(w, size.bs, 0, size.dps, size.out, size.up, blocks)
        out = dot_nn(dup[...], matrix)
        for part in range(WIDE // STEP):
            rows = slice(part * STEP, (part + 1) * STEP)
            dnormed[rows, columns] = dnormed[rows, columns] + out[rows]


def backward_norm_one(
    size, w, table, grads, dtable, first, scale, attended, dnormed, dlow, dlow_t, delta
):
    sums = [jnp.zeros((8, WIDE), jnp.float32)] * 3
    for part in range(WIDE // STEP):
        rows = slice(part * STEP, (part + 1) * STEP)
        grad, *found = normalize_back(
            first[rows, :], scale[rows, :], dnormed[rows, :], table[1:2, WIDE : 2 * WIDE]
        )
        dnormed[rows, :] = grad
        dlow[rows, :] = grad.astype(dlow.dtype)
        sums = [total + new for total, new in zip(sums, found)]
    for i, total in enumerate(sums):
        dtable[1:2, i * WIDE : (i + 1) * WIDE] = jnp.sum(total, axis=0, keepdims=True)
    dlow_t[...] = dlow[...].T
    for block in (0, 2):
        columns = slice(block * LANES, (block + 2) * LANES)
        value = dot_nn(dlow_t[...], attended[:, columns])
        put_rows(grads, size.bs, 0, size.dps, 0, size.out, value, block)
    grad = dot_nn(dlow[...], out_rows(size, w)).astype(dlow.dtype)
    dlow[...] = grad
    product = grad.astype(jnp.float32) * attended[...].astype(jnp.float32)
    high = product.astype(jnp.bfloat16)
    rest = (product - high.astype(jnp.float32)).astype(jnp.bfloat16)
    head = lax.broadcasted_iota(jnp.int32, delta.shape, 0)
    lane = lax.broadcasted_iota(jnp.int32, delta.shape, 1)
    inside = (lane >= head * HEAD) & (lane < (head + 1) * HEAD)
    inside = jnp.where(inside, 1.0, 0.0).astype(jnp.bfloat16)
    delta[...] = dot_nt(inside, high) + dot_nt(inside, rest)


def backward_attend(mixed, probs, delta, dtable, dlow, dmixed, pair):
    scale = 1.0 / math.sqrt(HEAD)
    lane = pair * LANES
    columns = slice(lane, lane + LANES)
    key_columns = slice(WIDE + lane, WIDE + lane + LANES)
    value_columns = slice(2 * WIDE + lane, 2 * WIDE + lane + LANES)
    keys_t = mixed[:, key_columns].T
    values = mixed[:, value_columns]
    dkeys = jnp.zeros((WIDE, LANES), jnp.float32)
    dvalues = jnp.zeros((WIDE, LANES), jnp.float32)
    for part in range(2):
        rows = slice(part * HALF, (part + 1) * HALF)
        queries = mixed[rows, columns]
        grad_out = dlow[rows, columns]
        dqueries = []
        for head in range(2):
            query = queries * head_masks(scale)[head]
            grad = grad_out * head_masks(1.0)[head]
            at = 2 * pair + head
            weights = probs[at, :, rows]
            less = delta[at : at + 1, rows]
            dprobs = dot_nt(values, grad)
            dscores = by_rows(
                lambda p, dp: (p.astype(jnp.float32) * (dp - less)).astype(jnp.bfloat16),
                weights,
                dprobs,
            )
            dvalues = dvalues + dot_nn(weights, grad)
            dkeys = dkeys + dot_nn(dscores, query)
            dqueries.append(dot_nn(keys_t[head * HEAD : (head + 1) * HEAD], dscores))
        dquery = jnp.concatenate(dqueries, axis=0).T * scale
        dtable[0:1, columns] += jnp.sum(dquery, axis=0, keepdims=True)
        dmixed[rows, columns] = dquery.astype(dmixed.dtype)
    dmixed[:, key_columns] = dkeys.astype(dmixed.dtype)
    dmixed[:, value_columns] = dvalues.astype(dmixed.dtype)
    dtable[0:1, value_columns] = jnp.sum(dvalues, axis=0, keepdims=True)


def backward_mix(size, grads, h, dmixed, piece):
    count = QKV_TILE // size.qkv
    grad = dmixed[:, piece * QKV_TILE : (piece + 1) * QKV_TILE]
    put_rows(grads, size.bs, piece * count, count, 0, size.qkv, dot_tn(grad, h[...]))


def backward_input(size, w, dnormed, dmixed, dy):
    for half in range(2):
        columns = slice(half * HALF, (half + 1) * HALF)
        blocks = (2 * half, 2 * half + 1)
        matrix = rows_of(w, size.bs, 0, size.dps, 0, size.qkv, blocks)
        out = dot_nn(dmixed[...], matrix)
        for part in range(WIDE // STEP):
            rows = slice(part * STEP, (part + 1) * STEP)
            dy[rows, columns] = (dnormed[rows, columns] + out[rows]).astype(dy.dtype)


WINDOW = 384


def group_rows(group):
    rows = lax.broadcasted_iota(jnp.int32, (16, LANES), 0)
    return jnp.where(rows == group, 1.0, 0.0).astype(jnp.bfloat16)


def pack_mix(piece, qkv, gains, biases):
    low = piece.dtype
    rows = qkv.shape[0]
    flat = jnp.concatenate([gains[...], biases[...]], axis=1)
    flat = jnp.concatenate([flat, jnp.zeros((1, 2 * WIDE - flat.shape[1]), flat.dtype)], axis=1)
    row_id = lax.broadcasted_iota(jnp.int32, (VEC_ROWS, LANES), 0)
    for lb in range(SECT):
        lane = lb * LANES
        piece[lb, :rows] = qkv[:, lane : lane + LANES].astype(low)
        tile = jnp.where(row_id == 0, flat[:, lane : lane + LANES], 0.0)
        lane += WIDE
        tile = jnp.where(row_id == 1, flat[:, lane : lane + LANES], tile)
        piece[lb, rows:] = tile.astype(low)


def pack_up(piece, out, up):
    rows = out.shape[0]
    for lb in range(SECT):
        lanes = slice(lb * LANES, (lb + 1) * LANES)
        piece[lb, :rows] = out[:, lanes].astype(piece.dtype)
        piece[lb, rows:] = up[:, lanes].astype(piece.dtype)


def pack_down(piece, down):
    rows = down.shape[0]
    for lb in range(SECT):
        for j in range(4):
            start = j * WIDE + lb * LANES
            piece[lb, j * rows : (j + 1) * rows] = down[:, start : start + LANES].astype(piece.dtype)


def pack_embedding(piece, weight, shift, square):
    n = weight.shape[0]
    square[...] = jnp.zeros_like(square)
    square[:GROUPS, :n] = shift[...]

    def ending(part, width):
        return jnp.concatenate([jnp.zeros((n, width - part.shape[1]), part.dtype), part], axis=1)

    parts = [
        square[...].T[:n],
        ending(weight[:, L1 + L2 :], 3 * LANES),
        ending(weight[:, L1 : L1 + L2], 2 * LANES),
        ending(weight[:, :L1], 2 * LANES),
    ]
    columns = jnp.concatenate(parts, axis=1).astype(piece.dtype)
    for lb in range(SECT):
        for part in range(2):
            start = part * WIDE + lb * LANES
            piece[lb, part * n : (part + 1) * n] = columns[:, start : start + LANES]


def expand(series, group, x):
    empty = jnp.zeros((WINDOW - series.shape[0], series.shape[1]), series.dtype)
    x[:, :WINDOW] = jnp.concatenate([empty, series[...]], axis=0).T
    lane = lax.broadcasted_iota(jnp.int32, (x.shape[0], LANES), 1)
    x[:, WINDOW:] = jnp.where(lane == group, 1.0, 0.0).astype(x.dtype)


def embed(size, emb, pick, x, wsel, h):
    rows = WIDE // size.dps
    first = rows_of(emb, size.bs, 0, size.dps, 0, rows)
    second = rows_of(emb, size.bs, 0, size.dps, rows, rows)
    long, middle, short = (pick[g : g + 1, :] for g in (2, 1, 0))
    wide = jnp.concatenate(
        [
            first[:, LANES : 2 * LANES] * long,
            first[:, 2 * LANES : 3 * LANES] * long + second[:, :LANES] * middle,
            first[:, 3 * LANES :] * long
            + second[:, LANES : 2 * LANES] * middle
            + second[:, 3 * LANES :] * short,
        ],
        axis=1,
    )
    wsel[...] = wide.T
    matrix = jnp.concatenate([wide, first[:, :LANES]], axis=1)
    h[...] = dot_nt(x[...], matrix).astype(h.dtype)


def embed_back(size, pick, x, wsel, dh, grads, series_grad):
    history = series_grad.shape[0]
    series_grad[...] = dot_nt(wsel[...], dh[...])[WINDOW - history :]
    sums = dot_tn(dh[...], x[...])
    long, middle, short = (pick[g : g + 1, :].astype(jnp.float32) for g in (2, 1, 0))
    parts = [sums[:, i * LANES : (i + 1) * LANES] for i in range(4)]
    parts = [
        parts[3],
        parts[0] * long,
        parts[1] * long,
        parts[2] * long,
        parts[1] * middle,
        parts[2] * middle,
        jnp.zeros_like(parts[0]),
        parts[2] * short,
    ]
    rows = WIDE // (SECT * size.dps)
    for pipe in range(SECT):
        block = (pipe % 2) * 2 + pipe // 2
        for dp in range(size.dps):
            start = (pipe * size.dps + dp) * rows
            piece = jnp.concatenate([part[start : start + rows] for part in parts], axis=0)
            grads[block, dp // size.bs, dp % size.bs] = piece.astype(grads.dtype)


def saved_shapes():
    low, wide = jnp.bfloat16, jnp.float32
    return [
        ((WIDE, WIDE), low),
        ((WIDE, 3 * WIDE), low),
        ((2 * SECT, WIDE, WIDE), low),
        ((WIDE, WIDE), low),
        ((WIDE, WIDE), wide),
        ((WIDE, WIDE), low),
        ((WIDE, 4 * WIDE), low),
        ((WIDE, 4 * WIDE), low),
        ((WIDE, WIDE), wide),
        ((SECT, 4 * WIDE), wide),
        ((WIDE, LANES), wide),
        ((WIDE, LANES), wide),
    ]


def chunk_shape(size, rows):
    return (SECT, ZS, size.bs, rows, LANES)


HALVES = (2, 2, 2, 2)
CROSS = (2,)


def follow(plan, section, act, compute):
    seen = {}
    for step in plan:
        if len(step) == 1:
            piece = seen.get(step[0], 0)
            seen[step[0]] = piece + 1
            compute(step[0], piece)
            continue
        op, kind, offset = step
        where = section + offset
        if isinstance(where, int):
            if 0 <= where < SECT:
                act(op, kind, where)
        elif offset == 0:
            act(op, kind, where)
        else:
            inside = where < SECT if offset > 0 else where >= 0

            @pl.when(inside)
            def _():
                act(op, kind, where)


def forward_kernel(dps, groups, *refs):
    size = Sizes(dps)
    given, refs = refs[:9], refs[9:]
    out, wholes, wsel, x, refs = refs[0], refs[1:5], refs[5], refs[6], refs[7:]
    kept, local, refs = refs[:12], refs[12:24], refs[24:]
    buffers, refs = refs[:4], refs[4:]
    pieces, held, refs = refs[:4], refs[4:13], refs[13:]
    emb_rows, pick, refs = refs[0], refs[1], refs[2:]
    given_sem, w_sem, kept_sem, own_sem, p_send, p_recv, send, recv = refs
    h, mixed, probs, attended, first, normed, slope, hidden, second, table, scale_1, scale_2 = local
    at = Place(dps)

    own = [
        pltpu.make_async_copy(
            pieces[kind].at[at.block],
            wholes[kind].at[at.pipe, at.block, at.z, at.b]
            if kind < EMB
            else wholes[kind].at[at.block, at.z, at.b],
            own_sem.at[kind],
        )
        for kind in range(4)
    ]
    def split(kind, back):
        copies = []
        for k in range(1, SECT):
            if back:
                region = wholes[kind].at[at.pipe_at(SECT - k), at.block, at.z, at.b]
                src = region
            else:
                block = at.blocks[k]
                region = wholes[kind].at[at.pipe, block, at.z, at.b]
                src = pieces[kind].at[block]
            sems = p_send.at[kind, k - 1], p_recv.at[kind, k - 1]
            copies.append(remote(src, region, *sems, (at.pipe_at(k), at.dp)))
        return copies

    def chunk(kind, section):
        if kind == EMB:
            return Spread(at, wholes[kind], send.at[3 * SECT], recv.at[3 * SECT])
        number = 3 * section + kind
        sort = SpreadCross if kind in CROSS else Spread
        return sort(at, wholes[kind].at[section], send.at[number], recv.at[number], HALVES[kind])

    def load(kind, section, core):
        blocks = pl.ds(core * 2, 2)
        src, dst = wholes[kind], buffers[kind]
        if kind != EMB:
            src, dst = src.at[section], dst.at[section % 2]
        sem = w_sem.at[kind, section % 2, core]
        return pltpu.make_async_copy(src.at[blocks], dst.at[blocks], sem)

    def loaded(kind, section):
        load(kind, section, at.c).wait()
        load(kind, section, 1 - at.c).wait()

    arrived = []

    def act(op, kind, section):
        if op == 0:
            if kind not in arrived:
                arrived.append(kind)
                own[kind].wait()
                if kind == EMB:
                    chunk(kind, section).start(0)
                    return
                for copy in split(kind, True):
                    copy.wait_recv()
                for copy in split(kind, False):
                    copy.wait_send()
                if kind == 0:
                    copies_start(split(1, False))
                    copies_start(split(2, False))
            chunk(kind, section).start(0)
        elif op < 4:
            chunk(kind, section).move(op - 1)
            if op == 1 and kind == EMB:
                gets[0].wait()
                expand(series, groups[0], x)
            if op == 3:
                load(kind, section, at.c).start()
        else:
            chunk(kind, section).land(3)
            load(kind, section, 1 - at.c).start()

    def saves(section, early):
        which = (1, 2, 3, 4, 5, 9, 10) if early else (6, 7, 8, 11)
        return [
            pltpu.make_async_copy(local[i], kept[i].at[section], kept_sem.at[i]) for i in which
        ]

    series, embed_weight, embed_bias, qkv, out_w, up_w, down_w, gains, biases = held
    gets = copies_of(zip(given, held), given_sem)
    for i in (3, 7, 8, 1, 2, 4, 5, 6, 0):
        gets[i].start()
    pick[...] = group_rows(groups[0])
    at.greet()
    copies_wait([gets[i] for i in (3, 7, 8)])
    pack_mix(pieces[0], qkv, gains, biases)
    own[0].start()
    at.met()
    copies_start(split(0, False))
    copies_wait(gets[1:3])
    pack_embedding(pieces[EMB], embed_weight, embed_bias, emb_rows)
    own[EMB].start()
    copies_wait(gets[4:7])
    pack_up(pieces[1], out_w, up_w)
    own[1].start()
    pack_down(pieces[2], down_w)
    own[2].start()
    table[...] = jnp.zeros_like(table)

    def before(name, piece):
        loaded(EMB, 0)
        embed(size, buffers[EMB], pick, x, wsel, h)

    follow(FORWARD_START, 0, act, before)

    @pl.loop(0, SECT)
    def _(section):
        att, up, down = (ref.at[section % 2] for ref in buffers[:3])
        keep_h = pltpu.make_async_copy(h, kept[0].at[section], kept_sem.at[0])

        def compute(name, piece):
            if name == "mix":
                if piece == 0:

                    @pl.when(section > 0)
                    def _():
                        copies_wait(saves(section - 1, True))

                    keep_h.start()
                    loaded(0, section)
                    read_vectors(att, table, size.bs, size.qkv)
                forward_mix(size, att, table, h, mixed, piece)
            elif name == "attend":
                forward_attend(mixed, probs, attended, piece)
            elif name == "project":
                loaded(1, section)
                forward_project(size, up, table, h, attended, first, scale_1, normed)
                copies_start(saves(section, True))
            elif name == "up":
                if piece == 0:

                    @pl.when(section > 0)
                    def _():
                        copies_wait(saves(section - 1, False))

                forward_up(size, up, table, normed, slope, hidden, piece)
            else:
                if piece == 0:
                    loaded(2, section)
                    keep_h.wait()
                forward_down(size, down, table, normed, hidden, second, scale_2, h, piece)
                if piece == 1:
                    copies_start(saves(section, False))

        follow(FORWARD_PERIOD, section, act, compute)

    out[...] = h[...]
    copies_wait(saves(SECT - 1, True))
    copies_wait(saves(SECT - 1, False))


def copies_of(pairs, sems):
    return [pltpu.make_async_copy(src, dst, sems.at[i]) for i, (src, dst) in enumerate(pairs)]


def forward_all(groups, given, dps):
    size = Sizes(dps)
    low, wide = jnp.bfloat16, jnp.float32
    shapes = saved_shapes()
    rows = (size.att, size.dense, size.wide, 2 * WIDE // dps)
    chunks = [chunk_shape(size, count) for count in rows]
    anywhere = pl.BlockSpec(memory_space=pl.ANY)
    inside = pl.BlockSpec(memory_space=pltpu.VMEM)
    outs = [((WIDE, WIDE), low)]
    outs += [((SECT,) + shape, low) for shape in chunks[:3]] + [(chunks[3], low)]
    outs += [((WINDOW, WIDE), low), ((WIDE, WIDE), low)]
    outs += [((SECT,) + shape, dtype) for shape, dtype in shapes]
    scratch = shapes + [((2,) + shape, low) for shape in chunks[:3]] + [(chunks[3], low)]
    scratch += [((SECT, count, LANES), low) for count in rows]
    scratch += [(array.shape, array.dtype) for array in given]
    scratch += [((LANES, LANES), wide), ((16, LANES), low)]
    slots = max(Spread.slots(size.bs), SpreadCross.slots(size.bs))
    dma = pltpu.SemaphoreType.DMA
    return pl.pallas_call(
        partial(forward_kernel, dps),
        out_shape=[jax.ShapeDtypeStruct(shape, dtype) for shape, dtype in outs],
        in_specs=[pl.BlockSpec(memory_space=pltpu.SMEM)] + [anywhere] * len(given),
        out_specs=[inside] + [anywhere] * 4 + [inside] * 2 + [anywhere] * len(shapes),
        scratch_shapes=[pltpu.VMEM(shape, dtype) for shape, dtype in scratch]
        + [
            dma((len(given),)),
            dma((4, 2, 2)),
            dma((len(shapes),)),
            dma((4,)),
            dma((3, SECT - 1)),
            dma((3, SECT - 1)),
            dma((1 + 3 * SECT, slots)),
            dma((1 + 3 * SECT, slots)),
        ],
        compiler_params=pltpu.CompilerParams(
            collective_id=0, has_side_effects=True, vmem_limit_bytes=60 * 1024 * 1024
        ),
        name="gather_forward",
    )(groups, *given)


FETCHES = {
    ("norm2", 0): (("second", "scale_2"), ("second", "scale_2")),
    ("down", 0): (("hidden",), ()),
    ("down", 1): ((), ("hidden",)),
    ("gelu", 0): (("slope", 2), ()),
    ("gelu", 1): ((), ("slope", 2)),
    ("up", 0): (("normed",), ("normed",)),
    ("normed", 0): ((1,), ()),
    ("norm1", 0): (("first", "scale_1", "attended"), ("first", "scale_1", "attended", 1)),
    ("attend", 0): (("mixed", "probs"), ()),
    ("attend", 3): ((), ("mixed", "probs")),
    ("mix", 0): (("h",), ()),
    ("mix", 1): ((), ("h",)),
    ("input", 0): ((0,), (0,)),
}


def backward_kernel(dps, groups, att, up, down, cotangent, x_in, wsel_in, *refs):
    size = Sizes(dps)
    kept, refs = refs[:12], refs[12:]
    series_grad, outs, refs = refs[0], refs[1:5], refs[5:]
    local, refs = refs[:11], refs[11:]
    tables, w_att, w_up, w_down, dtable, dy, dnormed, dlow, dlow_t, dmixed, dup = refs[:11]
    x, wsel, pick, delta, refs = *refs[11:15], refs[15:]
    kinds = []
    for kind in range(4):
        count = 6 if kind in CROSS else 5
        kinds.append(refs[:4] + (refs[4 : 4 + count],))
        refs = refs[4 + count :]
    w_sem, kept_sem, table_sem, late_sem, out_sem, p_send, p_recv, send, recv, credit = refs
    h, mixed, probs, attended, first, normed, slope, hidden, second, scale_1, scale_2 = local
    at = Place(dps)
    last = SECT - 1

    def weights(kind, section):
        src, dst = ((att, w_att), (up, w_up), (down, w_down))[kind]
        return pltpu.make_async_copy(src.at[section], dst, w_sem.at[kind])

    names = ("h", "mixed", "probs", "attended", "first", "normed", "slope", "hidden", "second")
    names += ("table", "scale_1", "scale_2")
    held = dict(zip(names[:9] + names[10:], local))

    def fetches(section, *wanted):
        found = []
        for name in wanted:
            if isinstance(name, int):
                found.append(weights(name, section))
            else:
                i = names.index(name)
                dst = held[name]
                found.append(pltpu.make_async_copy(kept[i].at[section], dst, kept_sem.at[i]))
        return found

    def chunk(kind, i):
        grads, totals, finals, landing, bufs = kinds[kind]
        sort = FoldCross if kind in CROSS else Fold
        refs = (grads, totals.at[i % 2], landing, bufs, finals.at[i])
        return sort(at, *refs, send.at[kind], recv.at[kind], credit.at[kind], HALVES[kind])

    def hand_over(kind, i):
        landing = outs[kind].at[at.block]
        final = kinds[kind][2].at[i]
        return (
            pltpu.make_async_copy(final, landing, out_sem.at[kind]),
            remote(final, landing, p_send.at[kind, i], p_recv.at[kind, at.pipe], (last - i, at.dp)),
        )

    def act(op, kind, i):
        again, more = (False, False) if kind == EMB else (i > 0, i < last)
        if op == 0:
            chunk(kind, i).start(0, again)
        elif op < 4:
            chunk(kind, i).move(op - 1, again, more)
        else:
            chunk(kind, i).land(3, more)
            if kind == EMB:
                outs[kind][...] = kinds[kind][2][0]
            else:
                here, away = hand_over(kind, i)

                @pl.when(at.pipe == last - i)
                def _():
                    here.start()

                @pl.when(at.pipe != last - i)
                def _():
                    away.start()

    copies_start(fetches(last, "second", "scale_2", "hidden", "slope", 2, "normed", 1))
    get_tables = pltpu.make_async_copy(kept[9], tables, table_sem)
    get_tables.start()
    copies_start(fetches(last, "first", "scale_1", "attended", "mixed", "probs", "h", 0))
    late = copies_of(((cotangent, dy), (x_in, x), (wsel_in, wsel)), late_sem)
    copies_start(late)
    pick[...] = group_rows(groups[0])
    at.greet()
    at.met()
    get_tables.wait()
    late[0].wait()

    @pl.loop(0, SECT)
    def _(i):
        section = last - i
        table = tables.at[section]

        def compute(name, piece):
            need, free = FETCHES.get((name, piece), ((), ()))
            copies_wait(fetches(section, *need))
            if name == "norm2":
                backward_norm_two(table, dtable, dy, second, scale_2, dnormed, dlow, dlow_t)
            elif name == "down":
                backward_down(size, kinds[2][0], hidden, dlow_t, piece)
            elif name == "gelu":
                backward_gelu(size, w_down, dtable, slope, dlow, dup, piece)
            elif name == "up":
                backward_up(size, kinds[1][0], normed, dup)
            elif name == "normed":
                backward_normed(size, w_up, dnormed, dup)
            elif name == "norm1":
                backward_norm_one(
                    size,
                    w_up,
                    table,
                    kinds[1][0],
                    dtable,
                    first,
                    scale_1,
                    attended,
                    dnormed,
                    dlow,
                    dlow_t,
                    delta,
                )
            elif name == "attend":
                backward_attend(mixed, probs, delta, dtable, dlow, dmixed, piece)
            elif name == "mix":
                backward_mix(size, kinds[0][0], h, dmixed, piece)
                if piece == 1:
                    write_vectors(kinds[0][0], dtable, size.bs, size.qkv)
            else:
                backward_input(size, w_att, dnormed, dmixed, dy)
            if free:

                @pl.when(section > 0)
                def _():
                    copies_start(fetches(section - 1, *free))

        follow(BACKWARD_PERIOD, i, act, compute)

    def after(name, piece):
        copies_wait(late[1:])
        embed_back(size, pick, x, wsel, dy, kinds[EMB][0], series_grad)

    follow(BACKWARD_END, 0, act, after)

    for kind in range(3):
        for i in range(SECT):
            here, away = hand_over(kind, i)

            @pl.when(at.pipe == last - i)
            def _():
                here.wait()

            @pl.when(at.pipe != last - i)
            def _():
                away.wait_send()

        for k in range(1, SECT):
            other = at.pipe_at(k)
            landing = outs[kind].at[at.blocks[k]]
            sems = p_send.at[kind, 0], p_recv.at[kind, other]
            remote(landing, landing, *sems, (other, at.dp)).wait_recv()


def backward_all(groups, weights, cotangent, x, wsel, kept, history, dps):
    size = Sizes(dps)
    low, wide = jnp.bfloat16, jnp.float32
    anywhere = pl.BlockSpec(memory_space=pl.ANY)
    inside = pl.BlockSpec(memory_space=pltpu.VMEM)
    shapes = saved_shapes()
    rows_emb = 8 * WIDE // (SECT * dps)
    kind_rows = (size.att, size.dense, size.wide, rows_emb)
    scratch = shapes[:9] + shapes[10:] + [((SECT,) + shapes[9][0], wide)]
    scratch += [(chunk_shape(size, rows), low) for rows in kind_rows[:3]]
    scratch += [
        (shapes[9][0], wide),
        ((WIDE, WIDE), low),
        ((WIDE, WIDE), wide),
        ((WIDE, WIDE), low),
        ((WIDE, WIDE), low),
        ((WIDE, 3 * WIDE), low),
        ((WIDE, 4 * WIDE), low),
        ((WIDE, WIDE), low),
        ((WINDOW, WIDE), low),
        ((16, LANES), low),
        ((16, WIDE), wide),
    ]
    for kind, rows in enumerate(kind_rows):
        sets, results = (1, 1) if kind == EMB else (2, SECT)
        scratch += [
            (chunk_shape(size, rows), low),
            ((sets, 2, ZS, size.bs, rows, LANES), low),
            ((results, rows, LANES), low),
            ((2, ZS, size.bs, rows, LANES), low),
        ]
        sort = FoldCross if kind in CROSS else Fold
        scratch += [(shape, low) for shape in sort.buffers(size.bs, rows, HALVES[kind])]
    slots = max(Fold.slots(size.bs), FoldCross.slots(size.bs))
    dma = pltpu.SemaphoreType.DMA
    return pl.pallas_call(
        partial(backward_kernel, dps),
        out_shape=[jax.ShapeDtypeStruct((history, WIDE), wide)]
        + [jax.ShapeDtypeStruct((SECT, rows, LANES), low) for rows in kind_rows[:3]]
        + [jax.ShapeDtypeStruct((rows_emb, LANES), low)],
        in_specs=[pl.BlockSpec(memory_space=pltpu.SMEM)] + [anywhere] * (6 + len(kept)),
        out_specs=[inside] + [anywhere] * 3 + [inside],
        scratch_shapes=[pltpu.VMEM(shape, dtype) for shape, dtype in scratch]
        + [
            dma((3,)),
            dma((12,)),
            dma(()),
            dma((3,)),
            dma((3,)),
            dma((3, SECT)),
            dma((3, SECT)),
            dma((4, slots)),
            dma((4, slots)),
            pltpu.SemaphoreType.REGULAR((4, slots)),
        ],
        compiler_params=pltpu.CompilerParams(
            collective_id=1, has_side_effects=True, vmem_limit_bytes=60 * 1024 * 1024
        ),
        name="backward_fold",
    )(groups, *weights, cotangent, x, wsel, *kept)


def finish_kernel(dps, n_gains, n_biases, *refs):
    size = Sizes(dps)
    given, refs = refs[:6], refs[6:]
    block_out, series_out, embed_w, embed_b, qkv, out, up_out, down_out, gains, biases = refs[:10]
    att, up, down, emb, sems = refs[10:]
    copies = copies_of(zip(given, (att, up, down, emb, block_out, series_out)), sems)
    copies_start(copies)
    copies_wait(copies[:4])
    for lb in range(SECT):
        lanes = slice(lb * LANES, (lb + 1) * LANES)
        qkv[:, lanes] = att[lb, : size.qkv].astype(jnp.float32)
        out[:, lanes] = up[lb, : size.out].astype(jnp.float32)
        up_out[:, lanes] = up[lb, size.out :].astype(jnp.float32)
        for j in range(4):
            rows = slice(j * size.down, (j + 1) * size.down)
            start = j * WIDE + lb * LANES
            down_out[:, start : start + LANES] = down[lb, rows].astype(jnp.float32)
    tiles = [att[lb, size.qkv :].astype(jnp.float32) for lb in range(SECT)]
    flat = jnp.concatenate([tile[row : row + 1] for row in range(2) for tile in tiles], axis=1)
    gains[...] = flat[:, :n_gains]
    biases[...] = flat[:, n_gains : n_gains + n_biases]
    rows = emb.shape[0] // 8
    packed = emb[...].astype(jnp.float32)
    packed = [packed[i * rows : (i + 1) * rows] for i in range(8)]
    square = jnp.concatenate([packed[0], jnp.zeros((LANES - rows, LANES), jnp.float32)], axis=0)
    embed_b[...] = square.T[:GROUPS, :rows]
    packed = jnp.concatenate(packed, axis=1)
    ends = ((1024, L1), (768, L2), (512, L3))
    embed_w[...] = jnp.concatenate([packed[:, end - span : end] for end, span in ends], axis=1)
    copies_wait(copies[4:])


def finish_all(sums, block, series, n_gains, n_biases, dps):
    size = Sizes(dps)
    wide = jnp.float32
    columns = WIDE // (SECT * dps)
    outs = [
        (block.shape, block.dtype),
        (series.shape, wide),
        ((columns, L1 + L2 + L3), wide),
        ((GROUPS, columns), wide),
        ((size.qkv, WIDE), wide),
        ((size.out, WIDE), wide),
        ((size.up, WIDE), wide),
        ((size.down, 4 * WIDE), wide),
        ((1, n_gains), wide),
        ((1, n_biases), wide),
    ]
    anywhere = pl.BlockSpec(memory_space=pl.ANY)
    inside = pl.BlockSpec(memory_space=pltpu.VMEM)
    return pl.pallas_call(
        partial(finish_kernel, dps, n_gains, n_biases),
        out_shape=[jax.ShapeDtypeStruct(shape, dtype) for shape, dtype in outs],
        in_specs=[anywhere] * 6,
        out_specs=[inside] * 10,
        scratch_shapes=[pltpu.VMEM(array.shape, array.dtype) for array in sums]
        + [pltpu.SemaphoreType.DMA((6,))],
        compiler_params=pltpu.CompilerParams(vmem_limit_bytes=60 * 1024 * 1024),
        name="finish",
    )(*sums, block, series)


def per_device(
    series,
    groups,
    cotangent,
    embed_weight,
    embed_bias,
    qkv_weight,
    out_weight,
    up_weight,
    down_weight,
    gains,
    biases,
):
    dps = lax.axis_size("dp")
    given = (
        series[0],
        embed_weight.T,
        embed_bias,
        qkv_weight[0],
        out_weight[0],
        up_weight[0],
        down_weight[0],
        gains,
        biases,
    )
    block_output, att, up, down, _, wsel, x, *kept = forward_all(groups, given, dps)
    series_grad, *sums = backward_all(
        groups, (att, up, down), cotangent[0], x, wsel, kept, series.shape[1], dps
    )
    outs = finish_all(sums, block_output, series_grad, gains.shape[1], biases.shape[1], dps)
    block_output, series_grad, embed_w, embed_b, qkv, out, up, down, gain_sum, bias_sum = outs
    return (
        block_output[None],
        series_grad[None],
        embed_w.T,
        embed_b,
        qkv[None],
        out[None],
        up[None],
        down[None],
        gain_sum,
        bias_sum,
    )


def solution(mesh):
    return jax.shard_map(
        per_device,
        mesh=mesh,
        in_specs=(
            P(("pipe", "dp"), None, None),
            P(("pipe", "dp")),
            P(("pipe", "dp"), None, None),
            P(None, "dp"),
            P(None, "dp"),
            P("pipe", "dp", None),
            P("pipe", "dp", None),
            P("pipe", "dp", None),
            P("pipe", "dp", None),
            P("pipe", "dp"),
            P("pipe", "dp"),
        ),
        out_specs=(
            P(("pipe", "dp"), None, None),
            P(("pipe", "dp"), None, None),
            P(None, ("pipe", "dp")),
            P(None, ("pipe", "dp")),
            P("pipe", "dp", None),
            P("pipe", "dp", None),
            P("pipe", "dp", None),
            P("pipe", "dp", None),
            P("pipe", "dp"),
            P("pipe", "dp"),
        ),
        check_vma=False,
    )
```

```python
from functools import partial
import math

import jax
import jax.numpy as jnp
from jax import lax
from jax.experimental import pallas as pl
from jax.experimental.pallas import tpu as pltpu
from jax.sharding import PartitionSpec as P

HEAD = 64
L1 = 96
L2 = 192
L3 = 336
GROUPS = 3


NORM_EPS = 1e-05


MESH = pl.DeviceIdType.MESH
LANES = 128
ZS = 4
SECT = 4
EMB = 3


class Place:
    def __init__(self, dps):
        self.bs = bs = dps // ZS
        pipe = lax.axis_index("pipe")
        dp = lax.axis_index("dp")
        self.pipe, self.dp = pipe, dp
        self.x, self.c = x, c = lax.div(pipe, 2), lax.rem(pipe, 2)
        self.z, self.b = z, b = lax.div(dp, bs), lax.rem(dp, bs)
        self.block = c * 2 + x
        self.other_block = c * 2 + 1 - x
        self.x_peer = ((1 - x) * 2 + c, dp)
        self.core_peer = (x * 2 + 1 - c, dp)
        self.pipes = [lax.rem(pipe + k, SECT) for k in range(SECT)]
        self.blocks = [self.block_of(other) for other in self.pipes]
        self.zs = [lax.rem(z + k, ZS) for k in range(ZS)]
        self.bees = [lax.rem(b + k, bs) for k in range(bs)]
        self.z_peers = [(pipe, other * bs + b) for other in self.zs]
        self.b_peers = [(pipe, z * bs + other) for other in self.bees]

    def block_of(self, pipe):
        return lax.rem(pipe, 2) * 2 + lax.div(pipe, 2)

    def pipe_at(self, step):
        return self.pipes[step % SECT]

    def z_at(self, step):
        return self.zs[step % ZS]

    def b_at(self, step):
        return self.bees[step % self.bs]

    def z_peer(self, step):
        return self.z_peers[step % ZS]

    def b_peer(self, step):
        return self.b_peers[step % self.bs]

    def greet(self):
        barrier = pltpu.get_barrier_semaphore()
        peers = [(self.pipe_at(k), self.dp) for k in range(1, SECT)]
        peers += [self.z_peer(k) for k in range(1, ZS)]
        peers += [self.b_peer(k) for k in range(1, self.bs)]
        for peer in peers:
            pl.semaphore_signal(barrier, inc=1, device_id=peer, device_id_type=MESH)

    def met(self):
        pl.semaphore_wait(pltpu.get_barrier_semaphore(), SECT + ZS + self.bs - 3)


def remote(src, dst, send, recv, peer):
    return pltpu.make_async_remote_copy(
        src_ref=src, dst_ref=dst, send_sem=send, recv_sem=recv, device_id=peer, device_id_type=MESH
    )


FORWARD_START = (
    (0, 3, 0),
    (0, 0, 0),
    (0, 2, 0),
    (1, 3, 0),
    (1, 0, 0),
    (0, 1, 0),
    (2, 3, 0),
    (2, 0, 0),
    (0, 0, 1),
    (1, 1, 0),
    (1, 2, 0),
    (3, 3, 0),
    (0, 2, 1),
    (1, 0, 1),
    (2, 1, 0),
    (4, 3, 0),
    (3, 0, 0),
    ("embed",),
    (4, 0, 0),
)
FORWARD_PERIOD = (
    ("mix",),
    (0, 1, 1),
    (2, 0, 1),
    ("mix",),
    ("attend",),
    (3, 1, 0),
    ("attend",),
    (2, 2, 0),
    ("attend",),
    (0, 0, 2),
    (4, 1, 0),
    ("attend",),
    ("project",),
    (1, 1, 1),
    ("up",),
    (1, 2, 1),
    (0, 2, 2),
    (3, 2, 0),
    ("up",),
    (1, 0, 2),
    ("up",),
    (2, 1, 1),
    (3, 0, 1),
    (4, 2, 0),
    ("up",),
    ("down",),
    (4, 0, 1),
    ("down",),
)
BACKWARD_PERIOD = (
    ("norm2",),
    (1, 0, -1),
    ("down",),
    ("down",),
    ("gelu",),
    ("gelu",),
    (2, 1, -1),
    (0, 2, 0),
    ("up",),
    ("normed",),
    (2, 0, -1),
    ("norm1",),
    (4, 1, -2),
    (4, 2, -2),
    (1, 2, 0),
    (3, 1, -1),
    (0, 1, 0),
    ("attend",),
    ("attend",),
    ("attend",),
    ("attend",),
    (3, 2, -1),
    (1, 1, 0),
    (4, 0, -2),
    (3, 0, -1),
    ("mix",),
    ("mix",),
    (0, 0, 0),
    ("input",),
    (2, 2, 0),
)
BACKWARD_END = (
    ("embed",),
    (1, 0, 3),
    (2, 1, 3),
    (2, 0, 3),
    (4, 1, 2),
    (4, 2, 2),
    (3, 1, 3),
    (0, 3, 0),
    (3, 2, 3),
    (4, 0, 2),
    (1, 3, 0),
    (3, 0, 3),
    (2, 3, 0),
    (3, 3, 0),
    (4, 1, 3),
    (4, 2, 3),
    (4, 0, 3),
    (4, 3, 0),
)


def copies_start(copies):
    for copy in copies:
        copy.start()


def copies_wait(copies):
    for copy in copies:
        copy.wait()


class Spread:
    def __init__(self, at, out, send, recv, half=ZS // 2):
        self.at, self.out, self.send, self.recv = at, out, send, recv
        nb = at.bs - 1
        self.slot_z = 0
        self.slot_b1 = ZS - 1
        self.slot_x1 = self.slot_b1 + nb
        self.slot_x2 = self.slot_x1 + 1
        self.slot_b2 = self.slot_x2 + 1
        self.slot_c = self.slot_b2 + nb
        self.half = half

    @staticmethod
    def slots(bs):
        return ZS - 1 + 2 * (bs - 1) + 3

    def copy(self, region, slot, peer):
        return remote(region, region, self.send.at[slot], self.recv.at[slot], peer)

    def copies(self, stage, back):
        at, out, half = self.at, self.out, self.half
        rest = pl.ds(half, ZS - half)
        x_block = at.other_block if back else at.block
        if stage == 0:
            return [
                self.copy(
                    out.at[at.block, at.z_at(ZS - k) if back else at.z, at.b],
                    self.slot_z + k - 1,
                    at.z_peer(k),
                )
                for k in range(1, ZS)
            ]
        if stage == 3:
            core = 1 - at.c if back else at.c
            return [self.copy(out.at[pl.ds(core * 2, 2)], self.slot_c, at.core_peer)]
        copies = []
        for k in range(1, at.bs):
            b = at.b_at(at.bs - k) if back else at.b
            if stage == 1:
                region, slot = out.at[at.block, pl.ds(0, half), b], self.slot_b1
            else:
                region, slot = out.at[pl.ds(at.c * 2, 2), rest, b], self.slot_b2
            copies.append(self.copy(region, slot + k - 1, at.b_peer(k)))
        if stage == 1:
            region, slot = out.at[x_block, rest, at.b], self.slot_x1
        else:
            region, slot = out.at[x_block, pl.ds(0, half)], self.slot_x2
        copies.append(self.copy(region, slot, at.x_peer))
        return copies

    def start(self, stage):
        copies_start(self.copies(stage, False))

    def land(self, stage):
        for copy in self.copies(stage, True):
            copy.wait_recv()
        for copy in self.copies(stage, False):
            copy.wait_send()

    def move(self, stage):
        self.land(stage)
        self.start(stage + 1)


class SpreadCross(Spread):
    @staticmethod
    def slots(bs):
        return 2 * bs + 2 * ZS - 1

    def copies(self, stage, back):
        at, out = self.at, self.out
        rows = out.shape[-2]
        cut = rows // 32 * 16
        some, rest = pl.ds(0, cut), pl.ds(cut, rows - cut)
        core = 1 - at.c if back else at.c
        if stage == 3:
            return [self.copy(out.at[pl.ds(core * 2, 2)], 2 * at.bs + 2 * ZS - 2, at.core_peer)]
        both = pl.ds(at.c * 2, 2)
        x_block = at.other_block if back else at.block
        copies = []
        if stage == 1:
            for k in range(1, ZS):
                z = at.z_at(ZS - k) if back else at.z
                copies.append(self.copy(out.at[both, z, at.b, some], at.bs + k - 1, at.z_peer(k)))
                slot = at.bs + ZS + k - 2
                copies.append(self.copy(out.at[at.block, z, :, rest], slot, at.z_peer(k)))
            return copies
        base = 0 if stage == 0 else at.bs + 2 * ZS - 2
        for k in range(1, at.bs):
            b = at.b_at(at.bs - k) if back else at.b
            region = out.at[at.block, at.z, b, rest] if stage == 0 else out.at[both, :, b, some]
            copies.append(self.copy(region, base + k, at.b_peer(k)))
        if stage == 0:
            region = out.at[x_block, at.z, at.b, some]
        else:
            region = out.at[x_block, :, :, rest]
        copies.append(self.copy(region, base, at.x_peer))
        return copies


class Fold:
    def __init__(self, at, grads, total, landing, bufs, final, send, recv, credit, half):
        self.at, self.grads, self.total = at, grads, total
        self.landing, self.bufs, self.final = landing, bufs, final
        self.send, self.recv, self.credit = send, recv, credit
        self.half = half
        nb = at.bs - 1
        self.slot_x1 = 1
        self.slot_b1 = 2
        self.slot_x2 = 2 + nb
        self.slot_b2 = 3 + nb
        self.slot_z = 3 + 2 * nb

    @staticmethod
    def slots(bs):
        return 3 + 2 * (bs - 1) + ZS - 1

    @staticmethod
    def buffers(bs, rows, half):
        nb = max(bs - 1, 1)
        rest = ZS - half
        return [
            (half, bs, rows, LANES),
            (nb, 2, rest, rows, LANES),
            (rest, rows, LANES),
            (nb, half, rows, LANES),
            (ZS - 1, rows, LANES),
        ]

    def core_parts(self):
        other = self.grads.at[pl.ds((1 - self.at.c) * 2, 2)]
        return [(other, self.landing, 0, self.at.core_peer, self.at.core_peer)]

    def parts(self, stage):
        at, half, total, bufs = self.at, self.half, self.total, self.bufs
        if stage == 0:
            return self.core_parts()
        if stage == 3:
            return [
                (
                    total.at[at.x, at.z_at(k), at.b],
                    bufs[4].at[k - 1],
                    self.slot_z + k - 1,
                    at.z_peer(k),
                    at.z_peer(ZS - k),
                )
                for k in range(1, ZS)
            ]
        rest = pl.ds(half, ZS - half)
        found = []
        for k in range(1, at.bs):
            if stage == 1:
                src, buf, slot = total.at[:, rest, at.b_at(k)], bufs[1], self.slot_b1
            else:
                src, buf, slot = total.at[at.x, pl.ds(0, half), at.b_at(k)], bufs[3], self.slot_b2
            found.append((src, buf.at[k - 1], slot + k - 1, at.b_peer(k), at.b_peer(at.bs - k)))
        if stage == 1:
            src, buf, slot = total.at[1 - at.x, pl.ds(0, half)], bufs[0], self.slot_x1
        else:
            src, buf, slot = total.at[1 - at.x, rest, at.b], bufs[2], self.slot_x2
        found.append((src, buf, slot, at.x_peer, at.x_peer))
        return found

    def start(self, stage, again):
        for src, buf, slot, to, _ in self.parts(stage):
            if again is not False:

                @pl.when(again)
                def _():
                    pl.semaphore_wait(self.credit.at[slot], 1)

            remote(src, buf, self.send.at[slot], self.recv.at[slot], to).start()

    def land(self, stage, more):
        parts = self.parts(stage)
        for src, buf, slot, to, _ in parts:
            remote(src, buf, self.send.at[slot], self.recv.at[slot], to).wait()
        self.add(stage)
        if more is not False:

            @pl.when(more)
            def _():
                for _, _, slot, _, origin in parts:
                    pl.semaphore_signal(
                        self.credit.at[slot], inc=1, device_id=origin, device_id_type=MESH
                    )

    def add_core(self):
        at, bs, total = self.at, self.at.bs, self.total

        @pl.loop(0, 2 * ZS * bs)
        def _(i):
            z, b = i // bs % ZS, i % bs
            x = i // (ZS * bs)
            total[x, z, b] = self.grads[at.c * 2 + x, z, b] + self.landing[x, z, b]

    def add(self, stage):
        at, half, bs = self.at, self.half, self.at.bs
        total, bufs = self.total, self.bufs
        rest = ZS - half
        if stage == 0:
            self.add_core()
        elif stage == 1:

            @pl.loop(0, half * bs)
            def _(i):
                z, b = i // bs, i % bs
                total[at.x, z, b] = total[at.x, z, b] + bufs[0][z, b]

            @pl.loop(0, 2 * rest)
            def _(i):
                x, z = i // rest, i % rest
                for k in range(bs - 1):
                    total[x, half + z, at.b] = total[x, half + z, at.b] + bufs[1][k, x, z]

        elif stage == 2:

            @pl.loop(0, rest)
            def _(z):
                total[at.x, half + z, at.b] = total[at.x, half + z, at.b] + bufs[2][z]

            @pl.loop(0, half)
            def _(z):
                for k in range(bs - 1):
                    total[at.x, z, at.b] = total[at.x, z, at.b] + bufs[3][k, z]

        else:
            self.finish([bufs[4][k] for k in range(ZS - 1)])

    def finish(self, pieces):
        at = self.at
        done = self.total[at.x, at.z, at.b].astype(jnp.float32)
        for piece in pieces:
            done = done + piece.astype(jnp.float32)
        self.final[...] = done.astype(self.final.dtype)

    def move(self, stage, again, more):
        self.land(stage, more)
        self.start(stage + 1, again)


class FoldCross(Fold):
    @staticmethod
    def slots(bs):
        return 2 * bs + 2 * ZS - 1

    @staticmethod
    def buffers(bs, rows, half):
        nb = max(bs - 1, 1)
        cut = rows // 32 * 16
        rest = rows - cut
        return [
            (nb, 2, ZS, cut, LANES),
            (ZS, bs, rest, LANES),
            (ZS - 1, 2, cut, LANES),
            (ZS - 1, bs, rest, LANES),
            (cut, LANES),
            (nb, rest, LANES),
        ]

    def cuts(self):
        rows = self.total.shape[-2]
        cut = rows // 32 * 16
        return pl.ds(0, cut), pl.ds(cut, rows - cut)

    def parts(self, stage):
        at, total, bufs = self.at, self.total, self.bufs
        if stage == 0:
            return self.core_parts()
        some, rest = self.cuts()
        found = []
        if stage == 2:
            for k in range(1, ZS):
                pair = (at.z_peer(k), at.z_peer(ZS - k))
                z = at.z_at(k)
                found.append((total.at[:, z, at.b, some], bufs[2].at[k - 1], at.bs + k, *pair))
                slot = at.bs + ZS + k - 1
                found.append((total.at[at.x, z, :, rest], bufs[3].at[k - 1], slot, *pair))
            return found
        base = 1 if stage == 1 else at.bs + 2 * ZS - 1
        for k in range(1, at.bs):
            pair = (at.b_peer(k), at.b_peer(at.bs - k))
            if stage == 1:
                src, buf = total.at[:, :, at.b_at(k), some], bufs[0].at[k - 1]
            else:
                src, buf = total.at[at.x, at.z, at.b_at(k), rest], bufs[5].at[k - 1]
            found.append((src, buf, base + k, *pair))
        if stage == 1:
            src, buf = total.at[1 - at.x, :, :, rest], bufs[1]
        else:
            src, buf = total.at[1 - at.x, at.z, at.b, some], bufs[4]
        found.append((src, buf, base, at.x_peer, at.x_peer))
        return found

    def add(self, stage):
        at, bs = self.at, self.at.bs
        total, bufs = self.total, self.bufs
        some, rest = self.cuts()
        if stage == 0:
            self.add_core()
        elif stage == 1:

            @pl.loop(0, 2 * ZS)
            def _(i):
                x, z = i // ZS, i % ZS
                for k in range(bs - 1):
                    total[x, z, at.b, some] = total[x, z, at.b, some] + bufs[0][k, x, z]

            @pl.loop(0, ZS * bs)
            def _(i):
                z, b = i // bs, i % bs
                total[at.x, z, b, rest] = total[at.x, z, b, rest] + bufs[1][z, b]

        elif stage == 2:
            for x in range(2):
                for k in range(ZS - 1):
                    total[x, at.z, at.b, some] = total[x, at.z, at.b, some] + bufs[2][k, x]

            @pl.loop(0, bs)
            def _(b):
                for k in range(ZS - 1):
                    total[at.x, at.z, b, rest] = total[at.x, at.z, b, rest] + bufs[3][k, b]

        else:
            total[at.x, at.z, at.b, some] = total[at.x, at.z, at.b, some] + bufs[4][...]
            for k in range(bs - 1):
                total[at.x, at.z, at.b, rest] = total[at.x, at.z, at.b, rest] + bufs[5][k]
            self.final[...] = total[at.x, at.z, at.b]


HALF = 256
WIDE = 512
QKV_TILE = 768
VEC_ROWS = 16


STEP = 64


def by_rows(fn, *arrays, step=STEP):
    parts = [
        fn(*[array[at : at + step] for array in arrays])
        for at in range(0, arrays[0].shape[0], step)
    ]
    if isinstance(parts[0], tuple):
        return tuple(jnp.concatenate(part, axis=0) for part in zip(*parts))
    return jnp.concatenate(parts, axis=0)


def dot_nt(a, b):
    return lax.dot_general(a, b, (((1,), (1,)), ((), ())), preferred_element_type=jnp.float32)


def dot_nn(a, b):
    return lax.dot_general(a, b, (((1,), (0,)), ((), ())), preferred_element_type=jnp.float32)


def dot_tn(a, b):
    return lax.dot_general(a, b, (((0,), (0,)), ((), ())), preferred_element_type=jnp.float32)


def aligned(index, unit):
    return pl.multiple_of(index, unit)


def rows_of(ref, bs, first, count, start, rows, blocks=range(SECT)):
    parts = []
    for i in range(count):
        d = first + i
        place = (d // bs, d % bs)
        parts.append(
            jnp.concatenate(
                [ref[(lb,) + place + (pl.ds(start, rows), slice(None))] for lb in blocks], axis=1
            )
        )
    return parts[0] if count == 1 else jnp.concatenate(parts, axis=0)


def put_rows(ref, bs, first, count, start, rows, value, block=0):
    value = value.astype(ref.dtype)
    for i in range(count):
        d = first + i
        place = (d // bs, d % bs)
        for lane in range(value.shape[1] // LANES):
            ref[(block + lane,) + place + (pl.ds(start, rows), slice(None))] = value[
                i * rows : (i + 1) * rows, lane * LANES : (lane + 1) * LANES
            ]


def vector_pieces(dps):
    n_gains, n_biases = 2 * WIDE // dps, 10 * WIDE // dps
    starts = [(0, 0), (0, 2), (1, 0), (1, 2), (2, 0), (2, 1), (2, 2), (2, 3), (3, 0), (3, 2)]
    pieces = []
    for d in range(dps):
        at = 0
        while at < n_gains + n_biases:
            if at < n_gains:
                index = d * n_gains + at
                row, column = (1, 3)[index // WIDE], WIDE + index % WIDE
                left = n_gains - at
            else:
                index = d * n_biases + at - n_gains
                row, part = starts[index // WIDE]
                column = part * WIDE + index % WIDE
                left = n_gains + n_biases - at
            size = min(left, LANES - at % LANES, LANES - column % LANES)
            pieces.append((d, at // LANES, at % LANES, row, column, size))
            at += size
    return pieces


def read_vectors(ref, table, bs, start, block):
    tiles = {}
    for d, row, lane, to_row, to_lane, size in vector_pieces(ZS * bs):
        if d not in tiles:
            tile = ref[block, d // bs, d % bs, start : start + VEC_ROWS, :]
            tiles[d] = tile.astype(jnp.float32)
        table[to_row : to_row + 1, to_lane : to_lane + size] = tiles[d][
            row : row + 1, lane : lane + size
        ]


def rows_tile(lines):
    row_id = lax.broadcasted_iota(jnp.int32, (VEC_ROWS, LANES), 0)
    tile = jnp.zeros((VEC_ROWS, LANES), jnp.float32)
    for row, pieces in enumerate(lines):
        have = sum(piece.shape[1] for piece in pieces)
        if have < LANES:
            pieces = pieces + [jnp.zeros((1, LANES - have), jnp.float32)]
        line = pieces[0] if len(pieces) == 1 else jnp.concatenate(pieces, axis=1)
        tile = jnp.where(row_id == row, line, tile)
    return tile


def vector_tile(table, dps, place):
    lines = []
    for d, row, lane, to_row, to_lane, size in vector_pieces(dps):
        if d == place:
            if row == len(lines):
                lines.append([])
            lines[row].append(table[to_row : to_row + 1, to_lane : to_lane + size])
    return rows_tile(lines)


def fold_rows(x):
    total = x[:8]
    for at in range(8, x.shape[0], 8):
        total = total + x[at : at + 8]
    return total


def normalize(x):
    mean = jnp.mean(x, axis=1, keepdims=True)
    centred = x - mean
    scale = lax.rsqrt(jnp.mean(centred * centred, axis=1, keepdims=True) + NORM_EPS)
    return centred * scale, jnp.broadcast_to(scale, (x.shape[0], LANES))


def normalize_back(unit, scale, grad, gain):
    inner = grad * gain
    first = jnp.mean(inner, axis=1, keepdims=True)
    second = jnp.mean(inner * unit, axis=1, keepdims=True)
    out = jnp.concatenate([scale] * (WIDE // LANES), axis=1) * (inner - first - unit * second)
    return out, fold_rows(out), fold_rows(grad * unit), fold_rows(grad)


def gelu_pair(u):
    below = 0.5 + 0.5 * lax.erf(u * math.sqrt(0.5))
    bell = jnp.exp2((-0.5 * math.log2(math.e)) * (u * u))
    return u * below, below + u * (bell * (1.0 / math.sqrt(2.0 * math.pi)))


def head_masks(scale):
    lane = lax.broadcasted_iota(jnp.int32, (1, LANES), 1)
    first = jnp.where(lane < HEAD, scale, 0.0).astype(jnp.bfloat16)
    second = jnp.where(lane < HEAD, 0.0, scale).astype(jnp.bfloat16)
    return first, second


class Sizes:
    def __init__(self, dps):
        self.dps, self.bs = dps, dps // ZS
        self.qkv, self.out, self.up, self.down = (
            3 * WIDE // dps,
            WIDE // dps,
            4 * WIDE // dps,
            WIDE // dps,
        )
        self.lookback = -(-6 * WIDE // (SECT * dps) // VEC_ROWS) * VEC_ROWS
        self.emb = self.lookback + VEC_ROWS
        self.dense = self.out + self.up
        self.wide = 4 * self.down


def qkv_rows(size, w, tile):
    count = QKV_TILE // size.qkv
    return rows_of(w, size.bs, tile * count, count, 0, size.qkv)


def out_rows(size, w):
    return rows_of(w, size.bs, 0, size.dps, 0, size.out)


def up_rows(size, w, tile):
    count = HALF // size.up
    return rows_of(w, size.bs, tile * count, count, size.out, size.up)


def forward_mix(size, w, table, h, mixed, piece):
    columns = slice(piece * QKV_TILE, (piece + 1) * QKV_TILE)
    shift = table[0:1, columns]
    out = dot_nt(h[...], qkv_rows(size, w, piece))
    mixed[:, columns] = by_rows(lambda part: (part + shift).astype(mixed.dtype), out)


def softmax_columns(scores):
    parts = [scores[at : at + STEP] for at in range(0, scores.shape[0], STEP)]
    top = parts[0]
    for part in parts[1:]:
        top = jnp.maximum(top, part)
    top = jnp.max(top, axis=0, keepdims=True)
    parts = [jnp.exp(part - top) for part in parts]
    total = parts[0]
    for part in parts[1:]:
        total = total + part
    scale = 1.0 / jnp.sum(total, axis=0, keepdims=True)
    return jnp.concatenate([(part * scale).astype(jnp.bfloat16) for part in parts], axis=0)


def forward_attend(mixed, probs, attended, pair):
    lane = pair * LANES
    key_rows = mixed[:, WIDE + lane : WIDE + lane + LANES]
    values = mixed[:, 2 * WIDE + lane : 2 * WIDE + lane + LANES].T

    for part in range(2):
        rows = slice(part * HALF, (part + 1) * HALF)
        queries = mixed[rows, lane : lane + LANES]
        joined = []
        for head, mask in enumerate(head_masks(1.0 / math.sqrt(HEAD))):
            weights = softmax_columns(dot_nt(key_rows, queries * mask))
            probs[2 * pair + head, :, rows] = weights
            joined.append(dot_nn(values[head * HEAD : (head + 1) * HEAD], weights))
        joined = jnp.concatenate(joined, axis=0).T
        attended[rows, lane : lane + LANES] = joined.astype(attended.dtype)


def forward_project(size, w, table, h, attended, first, scale, normed):
    out = dot_nt(attended[...], out_rows(size, w))
    for part in range(WIDE // STEP):
        rows = slice(part * STEP, (part + 1) * STEP)
        total = h[rows, :].astype(jnp.float32) + (out[rows] + table[1:2, 0:WIDE])
        unit, scale[rows, :] = normalize(total)
        first[rows, :] = unit
        normed[rows, :] = (
            unit * table[1:2, WIDE : 2 * WIDE] + table[1:2, 2 * WIDE : 3 * WIDE]
        ).astype(normed.dtype)


def forward_up(size, w, table, normed, slope, hidden, piece):
    for j in (2 * piece, 2 * piece + 1):
        columns = slice(j * HALF, (j + 1) * HALF)
        shift = table[2:3, columns]
        upper = dot_nt(normed[...], up_rows(size, w, j))
        for part in range(WIDE // STEP):
            rows = slice(part * STEP, (part + 1) * STEP)
            value, grad = gelu_pair(upper[rows] + shift)
            hidden[rows, columns] = value.astype(hidden.dtype)
            slope[rows, columns] = grad.astype(slope.dtype)


def forward_down(size, w, table, normed, hidden, second, scale, h, piece):
    columns = slice(piece * HALF, (piece + 1) * HALF)
    count = size.dps // 2
    matrix = jnp.concatenate(
        [
            rows_of(w, size.bs, piece * count, count, j * size.down, size.down)
            for j in range(4)
        ],
        axis=1,
    )
    out = dot_nt(hidden[...], matrix)
    shift = table[3:4, columns]
    for part in range(WIDE // STEP):
        rows = slice(part * STEP, (part + 1) * STEP)
        second[rows, columns] = normed[rows, columns].astype(jnp.float32) + (out[rows] + shift)
    if piece == 1:
        for part in range(WIDE // STEP):
            rows = slice(part * STEP, (part + 1) * STEP)
            unit, scale[rows, :] = normalize(second[rows, :])
            second[rows, :] = unit
            h[rows, :] = (
                unit * table[3:4, WIDE : 2 * WIDE] + table[3:4, 2 * WIDE : 3 * WIDE]
            ).astype(h.dtype)


def backward_norm_two(table, dtable, dy, second, scale, dnormed, dlow, dlow_t):
    dtable[...] = jnp.zeros_like(dtable)
    sums = [jnp.zeros((8, WIDE), jnp.float32)] * 3
    for part in range(WIDE // STEP):
        rows = slice(part * STEP, (part + 1) * STEP)
        grad, *found = normalize_back(
            second[rows, :],
            scale[rows, :],
            dy[rows, :].astype(jnp.float32),
            table[3:4, WIDE : 2 * WIDE],
        )
        dnormed[rows, :] = grad
        dlow[rows, :] = grad.astype(dlow.dtype)
        sums = [total + new for total, new in zip(sums, found)]
    for i, total in enumerate(sums):
        dtable[3:4, i * WIDE : (i + 1) * WIDE] = jnp.sum(total, axis=0, keepdims=True)
    dlow_t[...] = dlow[...].T


def backward_down(size, grads, hidden, dlow_t, piece):
    @pl.loop(2 * piece, 2 * piece + 2)
    def _(i):
        start = aligned(i * size.down, 16)
        for half in range(2):
            columns = pl.ds(aligned(i * WIDE, WIDE) + half * HALF, HALF)
            value = dot_nn(dlow_t[...], hidden[:, columns])
            put_rows(grads, size.bs, 0, size.dps, start, size.down, value, 2 * half)


def backward_gelu(size, w, dtable, slope, dlow, dup, piece):
    @pl.loop(2 * piece, 2 * piece + 2)
    def _(i):
        start = aligned(i * size.down, 16)
        for half in range(2):
            columns = pl.ds(aligned(i * WIDE, WIDE) + half * HALF, HALF)
            blocks = (2 * half, 2 * half + 1)
            matrix = rows_of(w, size.bs, 0, size.dps, start, size.down, blocks)
            dhidden = dot_nn(dlow[...], matrix)
            total = jnp.zeros((8, HALF), jnp.float32)
            for part in range(WIDE // STEP):
                rows = slice(part * STEP, (part + 1) * STEP)
                dupper = dhidden[rows] * slope[rows, columns].astype(jnp.float32)
                total = total + fold_rows(dupper)
                dup[rows, columns] = dupper.astype(dup.dtype)
            dtable[2:3, columns] = jnp.sum(total, axis=0, keepdims=True)


def backward_up(size, grads, normed, dup):
    count = HALF // size.up

    @pl.loop(0, 4)
    def _(i):
        for half in range(2):
            columns = pl.ds(aligned(i * WIDE, WIDE) + half * HALF, HALF)
            value = dot_tn(dup[:, columns], normed[...])
            first = (2 * i + half) * count
            put_rows(grads, size.bs, first, count, size.out, size.up, value)


def backward_normed(size, w, dnormed, dup):
    for half in range(2):
        columns = slice(half * HALF, (half + 1) * HALF)
        blocks = (2 * half, 2 * half + 1)
        matrix = rows_of(w, size.bs, 0, size.dps, size.out, size.up, blocks)
        out = dot_nn(dup[...], matrix)
        for part in range(WIDE // STEP):
            rows = slice(part * STEP, (part + 1) * STEP)
            dnormed[rows, columns] = dnormed[rows, columns] + out[rows]


def backward_norm_one(
    size, w, table, grads, dtable, first, scale, attended, dnormed, dlow, dlow_t, delta
):
    sums = [jnp.zeros((8, WIDE), jnp.float32)] * 3
    for part in range(WIDE // STEP):
        rows = slice(part * STEP, (part + 1) * STEP)
        grad, *found = normalize_back(
            first[rows, :], scale[rows, :], dnormed[rows, :], table[1:2, WIDE : 2 * WIDE]
        )
        dnormed[rows, :] = grad
        dlow[rows, :] = grad.astype(dlow.dtype)
        sums = [total + new for total, new in zip(sums, found)]
    for i, total in enumerate(sums):
        dtable[1:2, i * WIDE : (i + 1) * WIDE] = jnp.sum(total, axis=0, keepdims=True)
    dlow_t[...] = dlow[...].T
    for block in (0, 2):
        columns = slice(block * LANES, (block + 2) * LANES)
        value = dot_nn(dlow_t[...], attended[:, columns])
        put_rows(grads, size.bs, 0, size.dps, 0, size.out, value, block)
    grad = dot_nn(dlow[...], out_rows(size, w)).astype(dlow.dtype)
    dlow[...] = grad
    product = grad.astype(jnp.float32) * attended[...].astype(jnp.float32)
    high = product.astype(jnp.bfloat16)
    rest = (product - high.astype(jnp.float32)).astype(jnp.bfloat16)
    head = lax.broadcasted_iota(jnp.int32, delta.shape, 0)
    lane = lax.broadcasted_iota(jnp.int32, delta.shape, 1)
    inside = (lane >= head * HEAD) & (lane < (head + 1) * HEAD)
    inside = jnp.where(inside, 1.0, 0.0).astype(jnp.bfloat16)
    delta[...] = dot_nt(inside, high) + dot_nt(inside, rest)


def backward_attend(mixed, probs, delta, dtable, dlow, dmixed, pair):
    scale = 1.0 / math.sqrt(HEAD)
    lane = pair * LANES
    columns = slice(lane, lane + LANES)
    key_columns = slice(WIDE + lane, WIDE + lane + LANES)
    value_columns = slice(2 * WIDE + lane, 2 * WIDE + lane + LANES)
    keys_t = mixed[:, key_columns].T
    values = mixed[:, value_columns]
    dkeys = jnp.zeros((WIDE, LANES), jnp.float32)
    dvalues = jnp.zeros((WIDE, LANES), jnp.float32)
    for part in range(2):
        rows = slice(part * HALF, (part + 1) * HALF)
        queries = mixed[rows, columns]
        grad_out = dlow[rows, columns]
        dqueries = []
        for head in range(2):
            query = queries * head_masks(scale)[head]
            grad = grad_out * head_masks(1.0)[head]
            at = 2 * pair + head
            weights = probs[at, :, rows]
            less = delta[at : at + 1, rows]
            dprobs = dot_nt(values, grad)
            dscores = by_rows(
                lambda p, dp: (p.astype(jnp.float32) * (dp - less)).astype(jnp.bfloat16),
                weights,
                dprobs,
            )
            dvalues = dvalues + dot_nn(weights, grad)
            dkeys = dkeys + dot_nn(dscores, query)
            dqueries.append(dot_nn(keys_t[head * HEAD : (head + 1) * HEAD], dscores))
        dquery = jnp.concatenate(dqueries, axis=0).T * scale
        dtable[0:1, columns] += jnp.sum(dquery, axis=0, keepdims=True)
        dmixed[rows, columns] = dquery.astype(dmixed.dtype)
    dmixed[:, key_columns] = dkeys.astype(dmixed.dtype)
    dmixed[:, value_columns] = dvalues.astype(dmixed.dtype)
    dtable[0:1, value_columns] = jnp.sum(dvalues, axis=0, keepdims=True)


def backward_mix(size, grads, h, dmixed, piece):
    count = QKV_TILE // size.qkv
    grad = dmixed[:, piece * QKV_TILE : (piece + 1) * QKV_TILE]
    put_rows(grads, size.bs, piece * count, count, 0, size.qkv, dot_tn(grad, h[...]))


def backward_input(size, w, dnormed, dmixed, dy):
    for half in range(2):
        columns = slice(half * HALF, (half + 1) * HALF)
        blocks = (2 * half, 2 * half + 1)
        matrix = rows_of(w, size.bs, 0, size.dps, 0, size.qkv, blocks)
        out = dot_nn(dmixed[...], matrix)
        for part in range(WIDE // STEP):
            rows = slice(part * STEP, (part + 1) * STEP)
            dy[rows, columns] = (dnormed[rows, columns] + out[rows]).astype(dy.dtype)


WINDOW = 384


def group_rows(group):
    rows = lax.broadcasted_iota(jnp.int32, (16, LANES), 0)
    return jnp.where(rows == group, 1.0, 0.0).astype(jnp.bfloat16)


def pack_mix(piece, qkv):
    for lb in range(SECT):
        piece[lb] = qkv[:, lb * LANES : (lb + 1) * LANES].astype(piece.dtype)


def pack_up(piece, out, up):
    rows = out.shape[0]
    for lb in range(SECT):
        lanes = slice(lb * LANES, (lb + 1) * LANES)
        piece[lb, :rows] = out[:, lanes].astype(piece.dtype)
        piece[lb, rows:] = up[:, lanes].astype(piece.dtype)


def pack_down(piece, down):
    rows = down.shape[0]
    for lb in range(SECT):
        for j in range(4):
            start = j * WIDE + lb * LANES
            piece[lb, j * rows : (j + 1) * rows] = down[:, start : start + LANES].astype(piece.dtype)


def pack_embedding(piece, weight, shift, gains, biases, square, block):
    n = weight.shape[0]
    square[...] = jnp.zeros_like(square)
    square[:GROUPS, :n] = shift[...]

    def ending(part, width):
        return jnp.concatenate([jnp.zeros((n, width - part.shape[1]), part.dtype), part], axis=1)

    third = ending(weight[:, L1 + L2 :], 3 * LANES)
    second = ending(weight[:, L1 : L1 + L2], 2 * LANES)
    blocks = [third[:, :LANES] + square[...].T[:n]]
    blocks += [third[:, LANES : 2 * LANES], third[:, 2 * LANES :]]
    blocks += [second[:, :LANES], second[:, LANES:], ending(weight[:, :L1], LANES)]
    rows = piece.shape[1] - VEC_ROWS
    if SECT * rows > 6 * n:
        blocks.append(jnp.zeros((SECT * rows - 6 * n, LANES), jnp.float32))
    flat = jnp.concatenate(blocks, axis=0).astype(piece.dtype)
    for lb in range(SECT):
        piece[lb, :rows] = flat[lb * rows : (lb + 1) * rows]
    line = jnp.concatenate([gains[...], biases[...]], axis=1)
    lines = [[line[:, at : at + LANES]] for at in range(0, line.shape[1], LANES)]
    piece[block, rows:] = rows_tile(lines).astype(piece.dtype)


def expand(series, group, x):
    empty = jnp.zeros((WINDOW - series.shape[0], series.shape[1]), series.dtype)
    x[:, :WINDOW] = jnp.concatenate([empty, series[...]], axis=0).T
    lane = lax.broadcasted_iota(jnp.int32, (x.shape[0], LANES), 1)
    x[:, WINDOW:] = jnp.where(lane == group, 1.0, 0.0).astype(x.dtype)


def embed(size, emb, pick, x, wsel, h):
    n = WIDE // size.dps
    flat = []
    for d in range(size.dps):
        place = (d // size.bs, d % size.bs, slice(0, size.lookback), slice(None))
        flat.append(jnp.concatenate([emb[(lb,) + place] for lb in range(SECT)], axis=0))
    blocks = [
        jnp.concatenate([rows[j * n : (j + 1) * n] for rows in flat], axis=0) for j in range(6)
    ]
    long, middle, short = (pick[g : g + 1, :] for g in (2, 1, 0))
    wide = jnp.concatenate(
        [
            blocks[0] * long,
            blocks[1] * long + blocks[3] * middle,
            blocks[2] * long + blocks[4] * middle + blocks[5] * short,
        ],
        axis=1,
    )
    wsel[...] = wide.T
    h[...] = dot_nt(x[...], jnp.concatenate([wide, blocks[0]], axis=1)).astype(h.dtype)


def embed_back(size, pick, x, wsel, dh, tables, grads, series_grad):
    history = series_grad.shape[0]
    series_grad[...] = dot_nt(wsel[...], dh[...])[WINDOW - history :]
    sums = dot_tn(dh[...], x[...])
    long, middle, short = (pick[g : g + 1, :].astype(jnp.float32) for g in (2, 1, 0))
    parts = [sums[:, i * LANES : (i + 1) * LANES] for i in range(4)]
    parts = [
        parts[0] * long + parts[3],
        parts[1] * long,
        parts[2] * long,
        parts[1] * middle,
        parts[2] * middle,
        parts[2] * short,
    ]
    rows = WIDE // (SECT * size.dps)
    spare = size.lookback - 6 * rows
    for pipe in range(SECT):
        block = (pipe % 2) * 2 + pipe // 2
        for dp in range(size.dps):
            start = (pipe * size.dps + dp) * rows
            pieces = [part[start : start + rows] for part in parts]
            if spare:
                pieces.append(jnp.zeros((spare, LANES), jnp.float32))
            pieces.append(vector_tile(tables.at[pipe], size.dps, dp))
            piece = jnp.concatenate(pieces, axis=0)
            grads[block, dp // size.bs, dp % size.bs] = piece.astype(grads.dtype)


def saved_shapes():
    low, wide = jnp.bfloat16, jnp.float32
    return [
        ((WIDE, WIDE), low),
        ((WIDE, 3 * WIDE), low),
        ((2 * SECT, WIDE, WIDE), low),
        ((WIDE, WIDE), low),
        ((WIDE, WIDE), wide),
        ((WIDE, WIDE), low),
        ((WIDE, 4 * WIDE), low),
        ((WIDE, 4 * WIDE), low),
        ((WIDE, WIDE), wide),
        ((SECT, 4 * WIDE), wide),
        ((WIDE, LANES), wide),
        ((WIDE, LANES), wide),
    ]


def chunk_shape(size, rows):
    return (SECT, ZS, size.bs, rows, LANES)


HALVES = (2, 2, 2, 2)
CROSS = (2,)


def follow(plan, section, act, compute):
    seen = {}
    for step in plan:
        if len(step) == 1:
            piece = seen.get(step[0], 0)
            seen[step[0]] = piece + 1
            compute(step[0], piece)
            continue
        op, kind, offset = step
        where = section + offset
        if isinstance(where, int):
            if 0 <= where < SECT:
                act(op, kind, where)
        elif offset == 0:
            act(op, kind, where)
        else:
            inside = where < SECT if offset > 0 else where >= 0

            @pl.when(inside)
            def _():
                act(op, kind, where)


def forward_kernel(dps, groups, *refs):
    size = Sizes(dps)
    given, refs = refs[:9], refs[9:]
    out, wholes, wsel, x, refs = refs[0], refs[1:5], refs[5], refs[6], refs[7:]
    kept, local, refs = refs[:12], refs[12:24], refs[24:]
    buffers, refs = refs[:4], refs[4:]
    pieces, held, refs = refs[:4], refs[4:13], refs[13:]
    emb_rows, pick, refs = refs[0], refs[1], refs[2:]
    given_sem, w_sem, kept_sem, own_sem, p_send, p_recv, send, recv = refs
    h, mixed, probs, attended, first, normed, slope, hidden, second, table, scale_1, scale_2 = local
    at = Place(dps)

    own = [
        pltpu.make_async_copy(
            pieces[kind].at[at.block],
            wholes[kind].at[at.pipe, at.block, at.z, at.b]
            if kind < EMB
            else wholes[kind].at[at.block, at.z, at.b],
            own_sem.at[kind],
        )
        for kind in range(4)
    ]
    def split(kind, back):
        copies = []
        for k in range(1, SECT):
            if back:
                region = wholes[kind].at[at.pipe_at(SECT - k), at.block, at.z, at.b]
                src = region
            else:
                block = at.blocks[k]
                region = wholes[kind].at[at.pipe, block, at.z, at.b]
                src = pieces[kind].at[block]
            sems = p_send.at[kind, k - 1], p_recv.at[kind, k - 1]
            copies.append(remote(src, region, *sems, (at.pipe_at(k), at.dp)))
        return copies

    def chunk(kind, section):
        if kind == EMB:
            return Spread(at, wholes[kind], send.at[3 * SECT], recv.at[3 * SECT])
        number = 3 * section + kind
        sort = SpreadCross if kind in CROSS else Spread
        return sort(at, wholes[kind].at[section], send.at[number], recv.at[number], HALVES[kind])

    def load(kind, section, core):
        blocks = pl.ds(core * 2, 2)
        src, dst = wholes[kind], buffers[kind]
        if kind != EMB:
            src, dst = src.at[section], dst.at[section % 2]
        sem = w_sem.at[kind, section % 2, core]
        return pltpu.make_async_copy(src.at[blocks], dst.at[blocks], sem)

    def loaded(kind, section):
        load(kind, section, at.c).wait()
        load(kind, section, 1 - at.c).wait()

    arrived = []

    def act(op, kind, section):
        if op == 0:
            if kind not in arrived:
                arrived.append(kind)
                own[kind].wait()
                if kind == EMB:
                    chunk(kind, section).start(0)
                    return
                for copy in split(kind, True):
                    copy.wait_recv()
                for copy in split(kind, False):
                    copy.wait_send()
                if kind == 0:
                    copies_start(split(1, False))
                    copies_start(split(2, False))
            chunk(kind, section).start(0)
        elif op < 4:
            chunk(kind, section).move(op - 1)
            if op == 1 and kind == EMB:
                gets[0].wait()
                expand(series, groups[0], x)
            if op == 3:
                load(kind, section, at.c).start()
        else:
            chunk(kind, section).land(3)
            load(kind, section, 1 - at.c).start()

    def saves(section, early):
        which = (1, 2, 3, 4, 5, 9, 10) if early else (6, 7, 8, 11)
        return [
            pltpu.make_async_copy(local[i], kept[i].at[section], kept_sem.at[i]) for i in which
        ]

    series, embed_weight, embed_bias, qkv, out_w, up_w, down_w, gains, biases = held
    gets = copies_of(zip(given, held), given_sem)
    for i in (3, 7, 8, 1, 2, 4, 5, 6, 0):
        gets[i].start()
    pick[...] = group_rows(groups[0])
    at.greet()
    gets[3].wait()
    pack_mix(pieces[0], qkv)
    own[0].start()
    at.met()
    copies_start(split(0, False))
    copies_wait(gets[1:3] + gets[7:9])
    pack_embedding(
        pieces[EMB], embed_weight, embed_bias, gains, biases, emb_rows, at.block
    )
    own[EMB].start()
    copies_wait(gets[4:7])
    pack_up(pieces[1], out_w, up_w)
    own[1].start()
    pack_down(pieces[2], down_w)
    own[2].start()
    table[...] = jnp.zeros_like(table)

    def before(name, piece):
        loaded(EMB, 0)
        embed(size, buffers[EMB], pick, x, wsel, h)

    follow(FORWARD_START, 0, act, before)

    @pl.loop(0, SECT)
    def _(section):
        att, up, down = (ref.at[section % 2] for ref in buffers[:3])
        keep_h = pltpu.make_async_copy(h, kept[0].at[section], kept_sem.at[0])

        def compute(name, piece):
            if name == "mix":
                if piece == 0:

                    @pl.when(section > 0)
                    def _():
                        copies_wait(saves(section - 1, True))

                    keep_h.start()
                    loaded(0, section)
                    block = section % 2 * 2 + section // 2
                    read_vectors(buffers[EMB], table, size.bs, size.lookback, block)
                forward_mix(size, att, table, h, mixed, piece)
            elif name == "attend":
                forward_attend(mixed, probs, attended, piece)
            elif name == "project":
                loaded(1, section)
                forward_project(size, up, table, h, attended, first, scale_1, normed)
                copies_start(saves(section, True))
            elif name == "up":
                if piece == 0:

                    @pl.when(section > 0)
                    def _():
                        copies_wait(saves(section - 1, False))

                forward_up(size, up, table, normed, slope, hidden, piece)
            else:
                if piece == 0:
                    loaded(2, section)
                    keep_h.wait()
                forward_down(size, down, table, normed, hidden, second, scale_2, h, piece)
                if piece == 1:
                    copies_start(saves(section, False))

        follow(FORWARD_PERIOD, section, act, compute)

    out[...] = h[...]
    copies_wait(saves(SECT - 1, True))
    copies_wait(saves(SECT - 1, False))


def copies_of(pairs, sems):
    return [pltpu.make_async_copy(src, dst, sems.at[i]) for i, (src, dst) in enumerate(pairs)]


def forward_all(groups, given, dps):
    size = Sizes(dps)
    low, wide = jnp.bfloat16, jnp.float32
    shapes = saved_shapes()
    rows = (size.qkv, size.dense, size.wide, size.emb)
    chunks = [chunk_shape(size, count) for count in rows]
    anywhere = pl.BlockSpec(memory_space=pl.ANY)
    inside = pl.BlockSpec(memory_space=pltpu.VMEM)
    outs = [((WIDE, WIDE), low)]
    outs += [((SECT,) + shape, low) for shape in chunks[:3]] + [(chunks[3], low)]
    outs += [((WINDOW, WIDE), low), ((WIDE, WIDE), low)]
    outs += [((SECT,) + shape, dtype) for shape, dtype in shapes]
    scratch = shapes + [((2,) + shape, low) for shape in chunks[:3]] + [(chunks[3], low)]
    scratch += [((SECT, count, LANES), low) for count in rows]
    scratch += [(array.shape, array.dtype) for array in given]
    scratch += [((LANES, LANES), wide), ((16, LANES), low)]
    slots = max(Spread.slots(size.bs), SpreadCross.slots(size.bs))
    dma = pltpu.SemaphoreType.DMA
    return pl.pallas_call(
        partial(forward_kernel, dps),
        out_shape=[jax.ShapeDtypeStruct(shape, dtype) for shape, dtype in outs],
        in_specs=[pl.BlockSpec(memory_space=pltpu.SMEM)] + [anywhere] * len(given),
        out_specs=[inside] + [anywhere] * 4 + [inside] * 2 + [anywhere] * len(shapes),
        scratch_shapes=[pltpu.VMEM(shape, dtype) for shape, dtype in scratch]
        + [
            dma((len(given),)),
            dma((4, 2, 2)),
            dma((len(shapes),)),
            dma((4,)),
            dma((3, SECT - 1)),
            dma((3, SECT - 1)),
            dma((1 + 3 * SECT, slots)),
            dma((1 + 3 * SECT, slots)),
        ],
        compiler_params=pltpu.CompilerParams(
            collective_id=0, has_side_effects=True, vmem_limit_bytes=60 * 1024 * 1024
        ),
        name="gather_forward",
    )(groups, *given)


FETCHES = {
    ("norm2", 0): (("second", "scale_2"), ("second", "scale_2")),
    ("down", 0): (("hidden",), ()),
    ("down", 1): ((), ("hidden",)),
    ("gelu", 0): (("slope", 2), ()),
    ("gelu", 1): ((), ("slope", 2)),
    ("up", 0): (("normed",), ("normed",)),
    ("normed", 0): ((1,), ()),
    ("norm1", 0): (("first", "scale_1", "attended"), ("first", "scale_1", "attended", 1)),
    ("attend", 0): (("mixed", "probs"), ()),
    ("attend", 3): ((), ("mixed", "probs")),
    ("mix", 0): (("h",), ()),
    ("mix", 1): ((), ("h",)),
    ("input", 0): ((0,), (0,)),
}


def backward_kernel(dps, groups, att, up, down, cotangent, x_in, wsel_in, *refs):
    size = Sizes(dps)
    kept, refs = refs[:12], refs[12:]
    series_grad, outs, refs = refs[0], refs[1:5], refs[5:]
    local, refs = refs[:11], refs[11:]
    tables, w_att, w_up, w_down, dtables, dy, dnormed, dlow, dlow_t, dmixed, dup = refs[:11]
    x, wsel, pick, delta, refs = *refs[11:15], refs[15:]
    kinds = []
    for kind in range(4):
        count = 6 if kind in CROSS else 5
        kinds.append(refs[:4] + (refs[4 : 4 + count],))
        refs = refs[4 + count :]
    w_sem, kept_sem, table_sem, late_sem, out_sem, p_send, p_recv, send, recv, credit = refs
    h, mixed, probs, attended, first, normed, slope, hidden, second, scale_1, scale_2 = local
    at = Place(dps)
    last = SECT - 1

    def weights(kind, section):
        src, dst = ((att, w_att), (up, w_up), (down, w_down))[kind]
        return pltpu.make_async_copy(src.at[section], dst, w_sem.at[kind])

    names = ("h", "mixed", "probs", "attended", "first", "normed", "slope", "hidden", "second")
    names += ("table", "scale_1", "scale_2")
    held = dict(zip(names[:9] + names[10:], local))

    def fetches(section, *wanted):
        found = []
        for name in wanted:
            if isinstance(name, int):
                found.append(weights(name, section))
            else:
                i = names.index(name)
                dst = held[name]
                found.append(pltpu.make_async_copy(kept[i].at[section], dst, kept_sem.at[i]))
        return found

    def chunk(kind, i):
        grads, totals, finals, landing, bufs = kinds[kind]
        sort = FoldCross if kind in CROSS else Fold
        refs = (grads, totals.at[i % 2], landing, bufs, finals.at[i])
        return sort(at, *refs, send.at[kind], recv.at[kind], credit.at[kind], HALVES[kind])

    def hand_over(kind, i):
        landing = outs[kind].at[at.block]
        final = kinds[kind][2].at[i]
        return (
            pltpu.make_async_copy(final, landing, out_sem.at[kind]),
            remote(final, landing, p_send.at[kind, i], p_recv.at[kind, at.pipe], (last - i, at.dp)),
        )

    def act(op, kind, i):
        again, more = (False, False) if kind == EMB else (i > 0, i < last)
        if op == 0:
            chunk(kind, i).start(0, again)
        elif op < 4:
            chunk(kind, i).move(op - 1, again, more)
        else:
            chunk(kind, i).land(3, more)
            if kind == EMB:
                outs[kind][...] = kinds[kind][2][0]
            else:
                here, away = hand_over(kind, i)

                @pl.when(at.pipe == last - i)
                def _():
                    here.start()

                @pl.when(at.pipe != last - i)
                def _():
                    away.start()

    copies_start(fetches(last, "second", "scale_2", "hidden", "slope", 2, "normed", 1))
    get_tables = pltpu.make_async_copy(kept[9], tables, table_sem)
    get_tables.start()
    copies_start(fetches(last, "first", "scale_1", "attended", "mixed", "probs", "h", 0))
    late = copies_of(((cotangent, dy), (x_in, x), (wsel_in, wsel)), late_sem)
    copies_start(late)
    pick[...] = group_rows(groups[0])
    at.greet()
    at.met()
    get_tables.wait()
    late[0].wait()

    @pl.loop(0, SECT)
    def _(i):
        section = last - i
        table, dtable = tables.at[section], dtables.at[section]

        def compute(name, piece):
            need, free = FETCHES.get((name, piece), ((), ()))
            copies_wait(fetches(section, *need))
            if name == "norm2":
                backward_norm_two(table, dtable, dy, second, scale_2, dnormed, dlow, dlow_t)
            elif name == "down":
                backward_down(size, kinds[2][0], hidden, dlow_t, piece)
            elif name == "gelu":
                backward_gelu(size, w_down, dtable, slope, dlow, dup, piece)
            elif name == "up":
                backward_up(size, kinds[1][0], normed, dup)
            elif name == "normed":
                backward_normed(size, w_up, dnormed, dup)
            elif name == "norm1":
                backward_norm_one(
                    size,
                    w_up,
                    table,
                    kinds[1][0],
                    dtable,
                    first,
                    scale_1,
                    attended,
                    dnormed,
                    dlow,
                    dlow_t,
                    delta,
                )
            elif name == "attend":
                backward_attend(mixed, probs, delta, dtable, dlow, dmixed, piece)
            elif name == "mix":
                backward_mix(size, kinds[0][0], h, dmixed, piece)
            else:
                backward_input(size, w_att, dnormed, dmixed, dy)
            if free:

                @pl.when(section > 0)
                def _():
                    copies_start(fetches(section - 1, *free))

        follow(BACKWARD_PERIOD, i, act, compute)

    def after(name, piece):
        copies_wait(late[1:])
        embed_back(size, pick, x, wsel, dy, dtables, kinds[EMB][0], series_grad)

    follow(BACKWARD_END, 0, act, after)

    for kind in range(3):
        for i in range(SECT):
            here, away = hand_over(kind, i)

            @pl.when(at.pipe == last - i)
            def _():
                here.wait()

            @pl.when(at.pipe != last - i)
            def _():
                away.wait_send()

        for k in range(1, SECT):
            other = at.pipe_at(k)
            landing = outs[kind].at[at.blocks[k]]
            sems = p_send.at[kind, 0], p_recv.at[kind, other]
            remote(landing, landing, *sems, (other, at.dp)).wait_recv()


def backward_all(groups, weights, cotangent, x, wsel, kept, history, dps):
    size = Sizes(dps)
    low, wide = jnp.bfloat16, jnp.float32
    anywhere = pl.BlockSpec(memory_space=pl.ANY)
    inside = pl.BlockSpec(memory_space=pltpu.VMEM)
    shapes = saved_shapes()
    kind_rows = (size.qkv, size.dense, size.wide, size.emb)
    scratch = shapes[:9] + shapes[10:] + [((SECT,) + shapes[9][0], wide)]
    scratch += [(chunk_shape(size, rows), low) for rows in kind_rows[:3]]
    scratch += [
        ((SECT,) + shapes[9][0], wide),
        ((WIDE, WIDE), low),
        ((WIDE, WIDE), wide),
        ((WIDE, WIDE), low),
        ((WIDE, WIDE), low),
        ((WIDE, 3 * WIDE), low),
        ((WIDE, 4 * WIDE), low),
        ((WIDE, WIDE), low),
        ((WINDOW, WIDE), low),
        ((16, LANES), low),
        ((16, WIDE), wide),
    ]
    for kind, rows in enumerate(kind_rows):
        sets, results = (1, 1) if kind == EMB else (2, SECT)
        scratch += [
            (chunk_shape(size, rows), low),
            ((sets, 2, ZS, size.bs, rows, LANES), low),
            ((results, rows, LANES), low),
            ((2, ZS, size.bs, rows, LANES), low),
        ]
        sort = FoldCross if kind in CROSS else Fold
        scratch += [(shape, low) for shape in sort.buffers(size.bs, rows, HALVES[kind])]
    slots = max(Fold.slots(size.bs), FoldCross.slots(size.bs))
    dma = pltpu.SemaphoreType.DMA
    return pl.pallas_call(
        partial(backward_kernel, dps),
        out_shape=[jax.ShapeDtypeStruct((history, WIDE), wide)]
        + [jax.ShapeDtypeStruct((SECT, rows, LANES), low) for rows in kind_rows[:3]]
        + [jax.ShapeDtypeStruct((size.emb, LANES), low)],
        in_specs=[pl.BlockSpec(memory_space=pltpu.SMEM)] + [anywhere] * (6 + len(kept)),
        out_specs=[inside] + [anywhere] * 3 + [inside],
        scratch_shapes=[pltpu.VMEM(shape, dtype) for shape, dtype in scratch]
        + [
            dma((3,)),
            dma((12,)),
            dma(()),
            dma((3,)),
            dma((3,)),
            dma((3, SECT)),
            dma((3, SECT)),
            dma((4, slots)),
            dma((4, slots)),
            pltpu.SemaphoreType.REGULAR((4, slots)),
        ],
        compiler_params=pltpu.CompilerParams(
            collective_id=1, has_side_effects=True, vmem_limit_bytes=60 * 1024 * 1024
        ),
        name="backward_fold",
    )(groups, *weights, cotangent, x, wsel, *kept)


def finish_kernel(dps, n_gains, n_biases, *refs):
    size = Sizes(dps)
    given, refs = refs[:6], refs[6:]
    block_out, series_out, embed_w, embed_b, qkv, out, up_out, down_out, gains, biases = refs[:10]
    att, up, down, emb, sems = refs[10:]
    copies = copies_of(zip(given, (att, up, down, emb, block_out, series_out)), sems)
    copies_start(copies)
    copies_wait(copies[:4])
    for lb in range(SECT):
        lanes = slice(lb * LANES, (lb + 1) * LANES)
        qkv[:, lanes] = att[lb].astype(jnp.float32)
        out[:, lanes] = up[lb, : size.out].astype(jnp.float32)
        up_out[:, lanes] = up[lb, size.out :].astype(jnp.float32)
        for j in range(4):
            rows = slice(j * size.down, (j + 1) * size.down)
            start = j * WIDE + lb * LANES
            down_out[:, start : start + LANES] = down[lb, rows].astype(jnp.float32)
    vectors = emb[size.lookback :].astype(jnp.float32)
    count = -(-(n_gains + n_biases) // LANES)
    flat = jnp.concatenate([vectors[row : row + 1] for row in range(count)], axis=1)
    gains[...] = flat[:, :n_gains]
    biases[...] = flat[:, n_gains : n_gains + n_biases]
    rows = WIDE // (SECT * dps)
    packed = emb[: size.lookback].astype(jnp.float32)
    packed = [packed[i * rows : (i + 1) * rows] for i in range(6)]
    square = jnp.concatenate([packed[0], jnp.zeros((LANES - rows, LANES), jnp.float32)], axis=0)
    embed_b[...] = square.T[:GROUPS, :rows]
    packed = jnp.concatenate(packed, axis=1)
    ends = ((6 * LANES, L1), (5 * LANES, L2), (3 * LANES, L3))
    embed_w[...] = jnp.concatenate([packed[:, end - span : end] for end, span in ends], axis=1)
    copies_wait(copies[4:])


def finish_all(sums, block, series, n_gains, n_biases, dps):
    size = Sizes(dps)
    wide = jnp.float32
    columns = WIDE // (SECT * dps)
    outs = [
        (block.shape, block.dtype),
        (series.shape, wide),
        ((columns, L1 + L2 + L3), wide),
        ((GROUPS, columns), wide),
        ((size.qkv, WIDE), wide),
        ((size.out, WIDE), wide),
        ((size.up, WIDE), wide),
        ((size.down, 4 * WIDE), wide),
        ((1, n_gains), wide),
        ((1, n_biases), wide),
    ]
    anywhere = pl.BlockSpec(memory_space=pl.ANY)
    inside = pl.BlockSpec(memory_space=pltpu.VMEM)
    return pl.pallas_call(
        partial(finish_kernel, dps, n_gains, n_biases),
        out_shape=[jax.ShapeDtypeStruct(shape, dtype) for shape, dtype in outs],
        in_specs=[anywhere] * 6,
        out_specs=[inside] * 10,
        scratch_shapes=[pltpu.VMEM(array.shape, array.dtype) for array in sums]
        + [pltpu.SemaphoreType.DMA((6,))],
        compiler_params=pltpu.CompilerParams(vmem_limit_bytes=60 * 1024 * 1024),
        name="finish",
    )(*sums, block, series)


def per_device(
    series,
    groups,
    cotangent,
    embed_weight,
    embed_bias,
    qkv_weight,
    out_weight,
    up_weight,
    down_weight,
    gains,
    biases,
):
    dps = lax.axis_size("dp")
    given = (
        series[0],
        embed_weight.T,
        embed_bias,
        qkv_weight[0],
        out_weight[0],
        up_weight[0],
        down_weight[0],
        gains,
        biases,
    )
    block_output, att, up, down, _, wsel, x, *kept = forward_all(groups, given, dps)
    series_grad, *sums = backward_all(
        groups, (att, up, down), cotangent[0], x, wsel, kept, series.shape[1], dps
    )
    outs = finish_all(sums, block_output, series_grad, gains.shape[1], biases.shape[1], dps)
    block_output, series_grad, embed_w, embed_b, qkv, out, up, down, gain_sum, bias_sum = outs
    return (
        block_output[None],
        series_grad[None],
        embed_w.T,
        embed_b,
        qkv[None],
        out[None],
        up[None],
        down[None],
        gain_sum,
        bias_sum,
    )


def solution(mesh):
    return jax.shard_map(
        per_device,
        mesh=mesh,
        in_specs=(
            P(("pipe", "dp"), None, None),
            P(("pipe", "dp")),
            P(("pipe", "dp"), None, None),
            P(None, "dp"),
            P(None, "dp"),
            P("pipe", "dp", None),
            P("pipe", "dp", None),
            P("pipe", "dp", None),
            P("pipe", "dp", None),
            P("pipe", "dp"),
            P("pipe", "dp"),
        ),
        out_specs=(
            P(("pipe", "dp"), None, None),
            P(("pipe", "dp"), None, None),
            P(None, ("pipe", "dp")),
            P(None, ("pipe", "dp")),
            P("pipe", "dp", None),
            P("pipe", "dp", None),
            P("pipe", "dp", None),
            P("pipe", "dp", None),
            P("pipe", "dp"),
            P("pipe", "dp"),
        ),
        check_vma=False,
    )
```

```python
from functools import partial
import math

import jax
import jax.numpy as jnp
from jax import lax
from jax.experimental import pallas as pl
from jax.experimental.pallas import tpu as pltpu
from jax.sharding import PartitionSpec as P

HEAD = 64
L1 = 96
L2 = 192
L3 = 336
GROUPS = 3


NORM_EPS = 1e-05


MESH = pl.DeviceIdType.MESH
LANES = 128
ZS = 4
SECT = 4
EMB = 3


class Place:
    def __init__(self, dps):
        self.bs = bs = dps // ZS
        pipe = lax.axis_index("pipe")
        dp = lax.axis_index("dp")
        self.pipe, self.dp = pipe, dp
        self.x, self.c = x, c = lax.div(pipe, 2), lax.rem(pipe, 2)
        self.z, self.b = z, b = lax.div(dp, bs), lax.rem(dp, bs)
        self.block = c * 2 + x
        self.other_block = c * 2 + 1 - x
        self.x_peer = ((1 - x) * 2 + c, dp)
        self.core_peer = (x * 2 + 1 - c, dp)
        self.pipes = [lax.rem(pipe + k, SECT) for k in range(SECT)]
        self.blocks = [self.block_of(other) for other in self.pipes]
        self.zs = [lax.rem(z + k, ZS) for k in range(ZS)]
        self.bees = [lax.rem(b + k, bs) for k in range(bs)]
        self.z_peers = [(pipe, other * bs + b) for other in self.zs]
        self.b_peers = [(pipe, z * bs + other) for other in self.bees]

    def block_of(self, pipe):
        return lax.rem(pipe, 2) * 2 + lax.div(pipe, 2)

    def pipe_at(self, step):
        return self.pipes[step % SECT]

    def z_at(self, step):
        return self.zs[step % ZS]

    def b_at(self, step):
        return self.bees[step % self.bs]

    def z_peer(self, step):
        return self.z_peers[step % ZS]

    def b_peer(self, step):
        return self.b_peers[step % self.bs]

    def greet(self):
        barrier = pltpu.get_barrier_semaphore()
        peers = [(self.pipe_at(k), self.dp) for k in range(1, SECT)]
        peers += [self.z_peer(k) for k in range(1, ZS)]
        peers += [self.b_peer(k) for k in range(1, self.bs)]
        for peer in peers:
            pl.semaphore_signal(barrier, inc=1, device_id=peer, device_id_type=MESH)

    def met(self):
        pl.semaphore_wait(pltpu.get_barrier_semaphore(), SECT + ZS + self.bs - 3)


def remote(src, dst, send, recv, peer):
    return pltpu.make_async_remote_copy(
        src_ref=src, dst_ref=dst, send_sem=send, recv_sem=recv, device_id=peer, device_id_type=MESH
    )


FORWARD_START = (
    (0, 3, 0),
    (0, 0, 0),
    (0, 2, 0),
    (1, 3, 0),
    (1, 0, 0),
    (0, 1, 0),
    (2, 3, 0),
    (2, 0, 0),
    (0, 0, 1),
    (1, 1, 0),
    (1, 2, 0),
    (3, 3, 0),
    (0, 2, 1),
    (1, 0, 1),
    (2, 1, 0),
    (4, 3, 0),
    (3, 0, 0),
    ("embed",),
    (4, 0, 0),
)
FORWARD_PERIOD = (
    ("mix",),
    (0, 1, 1),
    (2, 0, 1),
    ("mix",),
    ("attend",),
    (3, 1, 0),
    ("attend",),
    (2, 2, 0),
    ("attend",),
    (0, 0, 2),
    (4, 1, 0),
    ("attend",),
    ("project",),
    (1, 1, 1),
    ("up",),
    (1, 2, 1),
    (0, 2, 2),
    (3, 2, 0),
    ("up",),
    (1, 0, 2),
    ("up",),
    (2, 1, 1),
    (3, 0, 1),
    (4, 2, 0),
    ("up",),
    ("down",),
    (4, 0, 1),
    ("down",),
)
BACKWARD_PERIOD = (
    ("norm2",),
    (1, 0, -1),
    ("down",),
    ("down",),
    ("gelu",),
    ("gelu",),
    (2, 1, -1),
    (0, 2, 0),
    ("up",),
    ("normed",),
    (2, 0, -1),
    ("norm1",),
    (4, 1, -2),
    (4, 2, -2),
    (1, 2, 0),
    (3, 1, -1),
    (0, 1, 0),
    ("attend",),
    ("attend",),
    ("attend",),
    ("attend",),
    (3, 2, -1),
    (1, 1, 0),
    (4, 0, -2),
    (3, 0, -1),
    ("mix",),
    ("mix",),
    (0, 0, 0),
    ("input",),
    (2, 2, 0),
)
BACKWARD_END = (
    ("embed",),
    (1, 0, 3),
    (2, 1, 3),
    (2, 0, 3),
    (4, 1, 2),
    (4, 2, 2),
    (3, 1, 3),
    (0, 3, 0),
    (3, 2, 3),
    (4, 0, 2),
    (1, 3, 0),
    (3, 0, 3),
    (2, 3, 0),
    (3, 3, 0),
    (4, 1, 3),
    (4, 2, 3),
    (4, 0, 3),
    (4, 3, 0),
)


def copies_start(copies):
    for copy in copies:
        copy.start()


def copies_wait(copies):
    for copy in copies:
        copy.wait()


class Spread:
    def __init__(self, at, out, send, recv, half=ZS // 2):
        self.at, self.out, self.send, self.recv = at, out, send, recv
        nb = at.bs - 1
        self.slot_z = 0
        self.slot_b1 = ZS - 1
        self.slot_x1 = self.slot_b1 + nb
        self.slot_x2 = self.slot_x1 + 1
        self.slot_b2 = self.slot_x2 + 1
        self.slot_c = self.slot_b2 + nb
        self.half = half

    @staticmethod
    def slots(bs):
        return ZS - 1 + 2 * (bs - 1) + 3

    def copy(self, region, slot, peer):
        return remote(region, region, self.send.at[slot], self.recv.at[slot], peer)

    def copies(self, stage, back):
        at, out, half = self.at, self.out, self.half
        rest = pl.ds(half, ZS - half)
        x_block = at.other_block if back else at.block
        if stage == 0:
            return [
                self.copy(
                    out.at[at.block, at.z_at(ZS - k) if back else at.z, at.b],
                    self.slot_z + k - 1,
                    at.z_peer(k),
                )
                for k in range(1, ZS)
            ]
        if stage == 3:
            core = 1 - at.c if back else at.c
            return [self.copy(out.at[pl.ds(core * 2, 2)], self.slot_c, at.core_peer)]
        copies = []
        for k in range(1, at.bs):
            b = at.b_at(at.bs - k) if back else at.b
            if stage == 1:
                region, slot = out.at[at.block, pl.ds(0, half), b], self.slot_b1
            else:
                region, slot = out.at[pl.ds(at.c * 2, 2), rest, b], self.slot_b2
            copies.append(self.copy(region, slot + k - 1, at.b_peer(k)))
        if stage == 1:
            region, slot = out.at[x_block, rest, at.b], self.slot_x1
        else:
            region, slot = out.at[x_block, pl.ds(0, half)], self.slot_x2
        copies.append(self.copy(region, slot, at.x_peer))
        return copies

    def start(self, stage):
        copies_start(self.copies(stage, False))

    def land(self, stage):
        for copy in self.copies(stage, True):
            copy.wait_recv()
        for copy in self.copies(stage, False):
            copy.wait_send()

    def move(self, stage):
        self.land(stage)
        self.start(stage + 1)


class SpreadCross(Spread):
    @staticmethod
    def slots(bs):
        return 2 * bs + 2 * ZS - 1

    def copies(self, stage, back):
        at, out = self.at, self.out
        rows = out.shape[-2]
        cut = rows // 32 * 16
        some, rest = pl.ds(0, cut), pl.ds(cut, rows - cut)
        core = 1 - at.c if back else at.c
        if stage == 3:
            return [self.copy(out.at[pl.ds(core * 2, 2)], 2 * at.bs + 2 * ZS - 2, at.core_peer)]
        both = pl.ds(at.c * 2, 2)
        x_block = at.other_block if back else at.block
        copies = []
        if stage == 1:
            for k in range(1, ZS):
                z = at.z_at(ZS - k) if back else at.z
                copies.append(self.copy(out.at[both, z, at.b, some], at.bs + k - 1, at.z_peer(k)))
                slot = at.bs + ZS + k - 2
                copies.append(self.copy(out.at[at.block, z, :, rest], slot, at.z_peer(k)))
            return copies
        base = 0 if stage == 0 else at.bs + 2 * ZS - 2
        for k in range(1, at.bs):
            b = at.b_at(at.bs - k) if back else at.b
            region = out.at[at.block, at.z, b, rest] if stage == 0 else out.at[both, :, b, some]
            copies.append(self.copy(region, base + k, at.b_peer(k)))
        if stage == 0:
            region = out.at[x_block, at.z, at.b, some]
        else:
            region = out.at[x_block, :, :, rest]
        copies.append(self.copy(region, base, at.x_peer))
        return copies


class Fold:
    def __init__(self, at, grads, total, landing, bufs, final, send, recv, credit, half):
        self.at, self.grads, self.total = at, grads, total
        self.landing, self.bufs, self.final = landing, bufs, final
        self.send, self.recv, self.credit = send, recv, credit
        self.half = half
        nb = at.bs - 1
        self.slot_x1 = 1
        self.slot_b1 = 2
        self.slot_x2 = 2 + nb
        self.slot_b2 = 3 + nb
        self.slot_z = 3 + 2 * nb

    @staticmethod
    def slots(bs):
        return 3 + 2 * (bs - 1) + ZS - 1

    @staticmethod
    def buffers(bs, rows, half):
        nb = max(bs - 1, 1)
        rest = ZS - half
        return [
            (half, bs, rows, LANES),
            (nb, 2, rest, rows, LANES),
            (rest, rows, LANES),
            (nb, half, rows, LANES),
            (ZS - 1, rows, LANES),
        ]

    def core_parts(self):
        other = self.grads.at[pl.ds((1 - self.at.c) * 2, 2)]
        return [(other, self.landing, 0, self.at.core_peer, self.at.core_peer)]

    def parts(self, stage):
        at, half, total, bufs = self.at, self.half, self.total, self.bufs
        if stage == 0:
            return self.core_parts()
        if stage == 3:
            return [
                (
                    total.at[at.x, at.z_at(k), at.b],
                    bufs[4].at[k - 1],
                    self.slot_z + k - 1,
                    at.z_peer(k),
                    at.z_peer(ZS - k),
                )
                for k in range(1, ZS)
            ]
        rest = pl.ds(half, ZS - half)
        found = []
        for k in range(1, at.bs):
            if stage == 1:
                src, buf, slot = total.at[:, rest, at.b_at(k)], bufs[1], self.slot_b1
            else:
                src, buf, slot = total.at[at.x, pl.ds(0, half), at.b_at(k)], bufs[3], self.slot_b2
            found.append((src, buf.at[k - 1], slot + k - 1, at.b_peer(k), at.b_peer(at.bs - k)))
        if stage == 1:
            src, buf, slot = total.at[1 - at.x, pl.ds(0, half)], bufs[0], self.slot_x1
        else:
            src, buf, slot = total.at[1 - at.x, rest, at.b], bufs[2], self.slot_x2
        found.append((src, buf, slot, at.x_peer, at.x_peer))
        return found

    def start(self, stage, again):
        for src, buf, slot, to, _ in self.parts(stage):
            if again is not False:

                @pl.when(again)
                def _():
                    pl.semaphore_wait(self.credit.at[slot], 1)

            remote(src, buf, self.send.at[slot], self.recv.at[slot], to).start()

    def land(self, stage, more):
        parts = self.parts(stage)
        for src, buf, slot, to, _ in parts:
            remote(src, buf, self.send.at[slot], self.recv.at[slot], to).wait()
        self.add(stage)
        if more is not False:

            @pl.when(more)
            def _():
                for _, _, slot, _, origin in parts:
                    pl.semaphore_signal(
                        self.credit.at[slot], inc=1, device_id=origin, device_id_type=MESH
                    )

    def add_core(self):
        at, bs, total = self.at, self.at.bs, self.total

        @pl.loop(0, 2 * ZS * bs)
        def _(i):
            z, b = i // bs % ZS, i % bs
            x = i // (ZS * bs)
            total[x, z, b] = self.grads[at.c * 2 + x, z, b] + self.landing[x, z, b]

    def add(self, stage):
        at, half, bs = self.at, self.half, self.at.bs
        total, bufs = self.total, self.bufs
        rest = ZS - half
        if stage == 0:
            self.add_core()
        elif stage == 1:

            @pl.loop(0, half * bs)
            def _(i):
                z, b = i // bs, i % bs
                total[at.x, z, b] = total[at.x, z, b] + bufs[0][z, b]

            @pl.loop(0, 2 * rest)
            def _(i):
                x, z = i // rest, i % rest
                for k in range(bs - 1):
                    total[x, half + z, at.b] = total[x, half + z, at.b] + bufs[1][k, x, z]

        elif stage == 2:

            @pl.loop(0, rest)
            def _(z):
                total[at.x, half + z, at.b] = total[at.x, half + z, at.b] + bufs[2][z]

            @pl.loop(0, half)
            def _(z):
                for k in range(bs - 1):
                    total[at.x, z, at.b] = total[at.x, z, at.b] + bufs[3][k, z]

        else:
            self.finish([bufs[4][k] for k in range(ZS - 1)])

    def finish(self, pieces):
        at = self.at
        done = self.total[at.x, at.z, at.b].astype(jnp.float32)
        for piece in pieces:
            done = done + piece.astype(jnp.float32)
        self.final[...] = done.astype(self.final.dtype)

    def move(self, stage, again, more):
        self.land(stage, more)
        self.start(stage + 1, again)


class FoldCross(Fold):
    @staticmethod
    def slots(bs):
        return 2 * bs + 2 * ZS - 1

    @staticmethod
    def buffers(bs, rows, half):
        nb = max(bs - 1, 1)
        cut = rows // 32 * 16
        rest = rows - cut
        return [
            (nb, 2, ZS, cut, LANES),
            (ZS, bs, rest, LANES),
            (ZS - 1, 2, cut, LANES),
            (ZS - 1, bs, rest, LANES),
            (cut, LANES),
            (nb, rest, LANES),
        ]

    def cuts(self):
        rows = self.total.shape[-2]
        cut = rows // 32 * 16
        return pl.ds(0, cut), pl.ds(cut, rows - cut)

    def parts(self, stage):
        at, total, bufs = self.at, self.total, self.bufs
        if stage == 0:
            return self.core_parts()
        some, rest = self.cuts()
        found = []
        if stage == 2:
            for k in range(1, ZS):
                pair = (at.z_peer(k), at.z_peer(ZS - k))
                z = at.z_at(k)
                found.append((total.at[:, z, at.b, some], bufs[2].at[k - 1], at.bs + k, *pair))
                slot = at.bs + ZS + k - 1
                found.append((total.at[at.x, z, :, rest], bufs[3].at[k - 1], slot, *pair))
            return found
        base = 1 if stage == 1 else at.bs + 2 * ZS - 1
        for k in range(1, at.bs):
            pair = (at.b_peer(k), at.b_peer(at.bs - k))
            if stage == 1:
                src, buf = total.at[:, :, at.b_at(k), some], bufs[0].at[k - 1]
            else:
                src, buf = total.at[at.x, at.z, at.b_at(k), rest], bufs[5].at[k - 1]
            found.append((src, buf, base + k, *pair))
        if stage == 1:
            src, buf = total.at[1 - at.x, :, :, rest], bufs[1]
        else:
            src, buf = total.at[1 - at.x, at.z, at.b, some], bufs[4]
        found.append((src, buf, base, at.x_peer, at.x_peer))
        return found

    def add(self, stage):
        at, bs = self.at, self.at.bs
        total, bufs = self.total, self.bufs
        some, rest = self.cuts()
        if stage == 0:
            self.add_core()
        elif stage == 1:

            @pl.loop(0, 2 * ZS)
            def _(i):
                x, z = i // ZS, i % ZS
                for k in range(bs - 1):
                    total[x, z, at.b, some] = total[x, z, at.b, some] + bufs[0][k, x, z]

            @pl.loop(0, ZS * bs)
            def _(i):
                z, b = i // bs, i % bs
                total[at.x, z, b, rest] = total[at.x, z, b, rest] + bufs[1][z, b]

        elif stage == 2:
            for x in range(2):
                for k in range(ZS - 1):
                    total[x, at.z, at.b, some] = total[x, at.z, at.b, some] + bufs[2][k, x]

            @pl.loop(0, bs)
            def _(b):
                for k in range(ZS - 1):
                    total[at.x, at.z, b, rest] = total[at.x, at.z, b, rest] + bufs[3][k, b]

        else:
            total[at.x, at.z, at.b, some] = total[at.x, at.z, at.b, some] + bufs[4][...]
            for k in range(bs - 1):
                total[at.x, at.z, at.b, rest] = total[at.x, at.z, at.b, rest] + bufs[5][k]
            self.final[...] = total[at.x, at.z, at.b]


HALF = 256
WIDE = 512
QKV_TILE = 768
VEC_ROWS = 16


STEP = 64


def by_rows(fn, *arrays, step=STEP):
    parts = [
        fn(*[array[at : at + step] for array in arrays])
        for at in range(0, arrays[0].shape[0], step)
    ]
    if isinstance(parts[0], tuple):
        return tuple(jnp.concatenate(part, axis=0) for part in zip(*parts))
    return jnp.concatenate(parts, axis=0)


def dot_nt(a, b):
    return lax.dot_general(a, b, (((1,), (1,)), ((), ())), preferred_element_type=jnp.float32)


def dot_nn(a, b):
    return lax.dot_general(a, b, (((1,), (0,)), ((), ())), preferred_element_type=jnp.float32)


def dot_tn(a, b):
    return lax.dot_general(a, b, (((0,), (0,)), ((), ())), preferred_element_type=jnp.float32)


def aligned(index, unit):
    return pl.multiple_of(index, unit)


def rows_of(ref, bs, first, count, start, rows, blocks=range(SECT)):
    parts = []
    for i in range(count):
        d = first + i
        place = (d // bs, d % bs)
        parts.append(
            jnp.concatenate(
                [ref[(lb,) + place + (pl.ds(start, rows), slice(None))] for lb in blocks], axis=1
            )
        )
    return parts[0] if count == 1 else jnp.concatenate(parts, axis=0)


def put_rows(ref, bs, first, count, start, rows, value, block=0):
    value = value.astype(ref.dtype)
    for i in range(count):
        d = first + i
        place = (d // bs, d % bs)
        for lane in range(value.shape[1] // LANES):
            ref[(block + lane,) + place + (pl.ds(start, rows), slice(None))] = value[
                i * rows : (i + 1) * rows, lane * LANES : (lane + 1) * LANES
            ]


def vector_pieces(dps):
    n_gains, n_biases = 2 * WIDE // dps, 10 * WIDE // dps
    starts = [(0, 0), (0, 2), (1, 0), (1, 2), (2, 0), (2, 1), (2, 2), (2, 3), (3, 0), (3, 2)]
    pieces = []
    for d in range(dps):
        at = 0
        while at < n_gains + n_biases:
            if at < n_gains:
                index = d * n_gains + at
                row, column = (1, 3)[index // WIDE], WIDE + index % WIDE
                left = n_gains - at
            else:
                index = d * n_biases + at - n_gains
                row, part = starts[index // WIDE]
                column = part * WIDE + index % WIDE
                left = n_gains + n_biases - at
            size = min(left, LANES - at % LANES, LANES - column % LANES)
            pieces.append((d, at // LANES, at % LANES, row, column, size))
            at += size
    return pieces


def read_vectors(ref, table, bs, start, block):
    tiles = {}
    for d, row, lane, to_row, to_lane, size in vector_pieces(ZS * bs):
        if d not in tiles:
            tile = ref[block, d // bs, d % bs, start : start + VEC_ROWS, :]
            tiles[d] = tile.astype(jnp.float32)
        table[to_row : to_row + 1, to_lane : to_lane + size] = tiles[d][
            row : row + 1, lane : lane + size
        ]


def rows_tile(lines):
    row_id = lax.broadcasted_iota(jnp.int32, (VEC_ROWS, LANES), 0)
    tile = jnp.zeros((VEC_ROWS, LANES), jnp.float32)
    for row, pieces in enumerate(lines):
        have = sum(piece.shape[1] for piece in pieces)
        if have < LANES:
            pieces = pieces + [jnp.zeros((1, LANES - have), jnp.float32)]
        line = pieces[0] if len(pieces) == 1 else jnp.concatenate(pieces, axis=1)
        tile = jnp.where(row_id == row, line, tile)
    return tile


def vector_tile(table, dps, place):
    lines = []
    for d, row, lane, to_row, to_lane, size in vector_pieces(dps):
        if d == place:
            if row == len(lines):
                lines.append([])
            lines[row].append(table[to_row : to_row + 1, to_lane : to_lane + size])
    return rows_tile(lines)


def fold_rows(x):
    total = x[:8]
    for at in range(8, x.shape[0], 8):
        total = total + x[at : at + 8]
    return total


def normalize(x):
    mean = jnp.mean(x, axis=1, keepdims=True)
    centred = x - mean
    scale = lax.rsqrt(jnp.mean(centred * centred, axis=1, keepdims=True) + NORM_EPS)
    return centred * scale, jnp.broadcast_to(scale, (x.shape[0], LANES))


def normalize_back(unit, scale, grad, gain):
    inner = grad * gain
    first = jnp.mean(inner, axis=1, keepdims=True)
    second = jnp.mean(inner * unit, axis=1, keepdims=True)
    out = jnp.concatenate([scale] * (WIDE // LANES), axis=1) * (inner - first - unit * second)
    return out, fold_rows(out), fold_rows(grad * unit), fold_rows(grad)


def gelu_pair(u):
    below = 0.5 + 0.5 * lax.erf(u * math.sqrt(0.5))
    bell = jnp.exp2((-0.5 * math.log2(math.e)) * (u * u))
    return u * below, below + u * (bell * (1.0 / math.sqrt(2.0 * math.pi)))


def head_masks(scale):
    lane = lax.broadcasted_iota(jnp.int32, (1, LANES), 1)
    first = jnp.where(lane < HEAD, scale, 0.0).astype(jnp.bfloat16)
    second = jnp.where(lane < HEAD, 0.0, scale).astype(jnp.bfloat16)
    return first, second


class Sizes:
    def __init__(self, dps):
        self.dps, self.bs = dps, dps // ZS
        self.qkv, self.out, self.up, self.down = (
            3 * WIDE // dps,
            WIDE // dps,
            4 * WIDE // dps,
            WIDE // dps,
        )
        self.lookback = -(-6 * WIDE // (SECT * dps) // VEC_ROWS) * VEC_ROWS
        self.emb = self.lookback + VEC_ROWS
        self.dense = self.out + self.up
        self.wide = 4 * self.down


def qkv_rows(size, w, tile):
    count = QKV_TILE // size.qkv
    return rows_of(w, size.bs, tile * count, count, 0, size.qkv)


def out_rows(size, w):
    return rows_of(w, size.bs, 0, size.dps, 0, size.out)


def up_rows(size, w, tile):
    count = HALF // size.up
    return rows_of(w, size.bs, tile * count, count, size.out, size.up)


def forward_mix(size, w, table, h, mixed, piece):
    columns = slice(piece * QKV_TILE, (piece + 1) * QKV_TILE)
    shift = table[0:1, columns]
    out = dot_nt(h[...], qkv_rows(size, w, piece))
    mixed[:, columns] = by_rows(lambda part: (part + shift).astype(mixed.dtype), out)


def softmax_columns(scores):
    parts = [scores[at : at + STEP] for at in range(0, scores.shape[0], STEP)]
    top = parts[0]
    for part in parts[1:]:
        top = jnp.maximum(top, part)
    top = jnp.max(top, axis=0, keepdims=True)
    parts = [jnp.exp(part - top) for part in parts]
    total = parts[0]
    for part in parts[1:]:
        total = total + part
    scale = 1.0 / jnp.sum(total, axis=0, keepdims=True)
    return jnp.concatenate([(part * scale).astype(jnp.bfloat16) for part in parts], axis=0)


def forward_attend(mixed, probs, attended, pair):
    lane = pair * LANES
    key_rows = mixed[:, WIDE + lane : WIDE + lane + LANES]
    values = mixed[:, 2 * WIDE + lane : 2 * WIDE + lane + LANES].T

    for part in range(2):
        rows = slice(part * HALF, (part + 1) * HALF)
        queries = mixed[rows, lane : lane + LANES]
        joined = []
        for head, mask in enumerate(head_masks(1.0 / math.sqrt(HEAD))):
            weights = softmax_columns(dot_nt(key_rows, queries * mask))
            probs[2 * pair + head, :, rows] = weights
            joined.append(dot_nn(values[head * HEAD : (head + 1) * HEAD], weights))
        joined = jnp.concatenate(joined, axis=0).T
        attended[rows, lane : lane + LANES] = joined.astype(attended.dtype)


def forward_project(size, w, table, h, attended, first, scale, normed):
    out = dot_nt(attended[...], out_rows(size, w))
    for part in range(WIDE // STEP):
        rows = slice(part * STEP, (part + 1) * STEP)
        total = h[rows, :].astype(jnp.float32) + (out[rows] + table[1:2, 0:WIDE])
        unit, scale[rows, :] = normalize(total)
        first[rows, :] = unit
        normed[rows, :] = (
            unit * table[1:2, WIDE : 2 * WIDE] + table[1:2, 2 * WIDE : 3 * WIDE]
        ).astype(normed.dtype)


def forward_up(size, w, table, normed, slope, hidden, piece):
    for j in (2 * piece, 2 * piece + 1):
        columns = slice(j * HALF, (j + 1) * HALF)
        shift = table[2:3, columns]
        upper = dot_nt(normed[...], up_rows(size, w, j))
        for part in range(WIDE // STEP):
            rows = slice(part * STEP, (part + 1) * STEP)
            value, grad = gelu_pair(upper[rows] + shift)
            hidden[rows, columns] = value.astype(hidden.dtype)
            slope[rows, columns] = grad.astype(slope.dtype)


def forward_down(size, w, table, normed, hidden, second, scale, h, piece):
    columns = slice(piece * HALF, (piece + 1) * HALF)
    count = size.dps // 2
    matrix = jnp.concatenate(
        [
            rows_of(w, size.bs, piece * count, count, j * size.down, size.down)
            for j in range(4)
        ],
        axis=1,
    )
    out = dot_nt(hidden[...], matrix)
    shift = table[3:4, columns]
    for part in range(WIDE // STEP):
        rows = slice(part * STEP, (part + 1) * STEP)
        second[rows, columns] = normed[rows, columns].astype(jnp.float32) + (out[rows] + shift)
    if piece == 1:
        for part in range(WIDE // STEP):
            rows = slice(part * STEP, (part + 1) * STEP)
            unit, scale[rows, :] = normalize(second[rows, :])
            second[rows, :] = unit
            h[rows, :] = (
                unit * table[3:4, WIDE : 2 * WIDE] + table[3:4, 2 * WIDE : 3 * WIDE]
            ).astype(h.dtype)


def backward_norm_two(table, dtable, dy, second, scale, dnormed, dlow, dlow_t):
    dtable[...] = jnp.zeros_like(dtable)
    sums = [jnp.zeros((8, WIDE), jnp.float32)] * 3
    for part in range(WIDE // STEP):
        rows = slice(part * STEP, (part + 1) * STEP)
        grad, *found = normalize_back(
            second[rows, :],
            scale[rows, :],
            dy[rows, :].astype(jnp.float32),
            table[3:4, WIDE : 2 * WIDE],
        )
        dnormed[rows, :] = grad
        dlow[rows, :] = grad.astype(dlow.dtype)
        sums = [total + new for total, new in zip(sums, found)]
    for i, total in enumerate(sums):
        dtable[3:4, i * WIDE : (i + 1) * WIDE] = jnp.sum(total, axis=0, keepdims=True)
    dlow_t[...] = dlow[...].T


def backward_down(size, grads, hidden, dlow_t, piece):
    @pl.loop(2 * piece, 2 * piece + 2)
    def _(i):
        start = aligned(i * size.down, 16)
        for half in range(2):
            columns = pl.ds(aligned(i * WIDE, WIDE) + half * HALF, HALF)
            value = dot_nn(dlow_t[...], hidden[:, columns])
            put_rows(grads, size.bs, 0, size.dps, start, size.down, value, 2 * half)


def backward_gelu(size, w, dtable, slope, dlow, dup, piece):
    @pl.loop(2 * piece, 2 * piece + 2)
    def _(i):
        start = aligned(i * size.down, 16)
        for half in range(2):
            columns = pl.ds(aligned(i * WIDE, WIDE) + half * HALF, HALF)
            blocks = (2 * half, 2 * half + 1)
            matrix = rows_of(w, size.bs, 0, size.dps, start, size.down, blocks)
            dhidden = dot_nn(dlow[...], matrix)
            total = jnp.zeros((8, HALF), jnp.float32)
            for part in range(WIDE // STEP):
                rows = slice(part * STEP, (part + 1) * STEP)
                dupper = dhidden[rows] * slope[rows, columns].astype(jnp.float32)
                total = total + fold_rows(dupper)
                dup[rows, columns] = dupper.astype(dup.dtype)
            dtable[2:3, columns] = jnp.sum(total, axis=0, keepdims=True)


def backward_up(size, grads, normed, dup):
    count = HALF // size.up

    @pl.loop(0, 4)
    def _(i):
        for half in range(2):
            columns = pl.ds(aligned(i * WIDE, WIDE) + half * HALF, HALF)
            value = dot_tn(dup[:, columns], normed[...])
            first = (2 * i + half) * count
            put_rows(grads, size.bs, first, count, size.out, size.up, value)


def backward_normed(size, w, dnormed, dup):
    for half in range(2):
        columns = slice(half * HALF, (half + 1) * HALF)
        blocks = (2 * half, 2 * half + 1)
        matrix = rows_of(w, size.bs, 0, size.dps, size.out, size.up, blocks)
        out = dot_nn(dup[...], matrix)
        for part in range(WIDE // STEP):
            rows = slice(part * STEP, (part + 1) * STEP)
            dnormed[rows, columns] = dnormed[rows, columns] + out[rows]


def backward_norm_one(
    size, w, table, grads, dtable, first, scale, attended, dnormed, dlow, dlow_t, delta
):
    sums = [jnp.zeros((8, WIDE), jnp.float32)] * 3
    for part in range(WIDE // STEP):
        rows = slice(part * STEP, (part + 1) * STEP)
        grad, *found = normalize_back(
            first[rows, :], scale[rows, :], dnormed[rows, :], table[1:2, WIDE : 2 * WIDE]
        )
        dnormed[rows, :] = grad
        dlow[rows, :] = grad.astype(dlow.dtype)
        sums = [total + new for total, new in zip(sums, found)]
    for i, total in enumerate(sums):
        dtable[1:2, i * WIDE : (i + 1) * WIDE] = jnp.sum(total, axis=0, keepdims=True)
    dlow_t[...] = dlow[...].T
    for block in (0, 2):
        columns = slice(block * LANES, (block + 2) * LANES)
        value = dot_nn(dlow_t[...], attended[:, columns])
        put_rows(grads, size.bs, 0, size.dps, 0, size.out, value, block)
    grad = dot_nn(dlow[...], out_rows(size, w)).astype(dlow.dtype)
    dlow[...] = grad
    product = grad.astype(jnp.float32) * attended[...].astype(jnp.float32)
    high = product.astype(jnp.bfloat16)
    rest = (product - high.astype(jnp.float32)).astype(jnp.bfloat16)
    head = lax.broadcasted_iota(jnp.int32, delta.shape, 0)
    lane = lax.broadcasted_iota(jnp.int32, delta.shape, 1)
    inside = (lane >= head * HEAD) & (lane < (head + 1) * HEAD)
    inside = jnp.where(inside, 1.0, 0.0).astype(jnp.bfloat16)
    delta[...] = dot_nt(inside, high) + dot_nt(inside, rest)


def backward_attend(mixed, probs, delta, dtable, dlow, dmixed, pair):
    scale = 1.0 / math.sqrt(HEAD)
    lane = pair * LANES
    columns = slice(lane, lane + LANES)
    key_columns = slice(WIDE + lane, WIDE + lane + LANES)
    value_columns = slice(2 * WIDE + lane, 2 * WIDE + lane + LANES)
    keys_t = mixed[:, key_columns].T
    values = mixed[:, value_columns]
    dkeys = jnp.zeros((WIDE, LANES), jnp.float32)
    dvalues = jnp.zeros((WIDE, LANES), jnp.float32)
    for part in range(2):
        rows = slice(part * HALF, (part + 1) * HALF)
        queries = mixed[rows, columns]
        grad_out = dlow[rows, columns]
        dqueries = []
        for head in range(2):
            query = queries * head_masks(scale)[head]
            grad = grad_out * head_masks(1.0)[head]
            at = 2 * pair + head
            weights = probs[at, :, rows]
            less = delta[at : at + 1, rows]
            dprobs = dot_nt(values, grad)
            dscores = by_rows(
                lambda p, dp: (p.astype(jnp.float32) * (dp - less)).astype(jnp.bfloat16),
                weights,
                dprobs,
            )
            dvalues = dvalues + dot_nn(weights, grad)
            dkeys = dkeys + dot_nn(dscores, query)
            dqueries.append(dot_nn(keys_t[head * HEAD : (head + 1) * HEAD], dscores))
        dquery = jnp.concatenate(dqueries, axis=0).T * scale
        dtable[0:1, columns] += jnp.sum(dquery, axis=0, keepdims=True)
        dmixed[rows, columns] = dquery.astype(dmixed.dtype)
    dmixed[:, key_columns] = dkeys.astype(dmixed.dtype)
    dmixed[:, value_columns] = dvalues.astype(dmixed.dtype)
    dtable[0:1, value_columns] = jnp.sum(dvalues, axis=0, keepdims=True)


def backward_mix(size, grads, h, dmixed, piece):
    count = QKV_TILE // size.qkv
    grad = dmixed[:, piece * QKV_TILE : (piece + 1) * QKV_TILE]
    put_rows(grads, size.bs, piece * count, count, 0, size.qkv, dot_tn(grad, h[...]))


def backward_input(size, w, dnormed, dmixed, dy):
    for half in range(2):
        columns = slice(half * HALF, (half + 1) * HALF)
        blocks = (2 * half, 2 * half + 1)
        matrix = rows_of(w, size.bs, 0, size.dps, 0, size.qkv, blocks)
        out = dot_nn(dmixed[...], matrix)
        for part in range(WIDE // STEP):
            rows = slice(part * STEP, (part + 1) * STEP)
            dy[rows, columns] = (dnormed[rows, columns] + out[rows]).astype(dy.dtype)


WINDOW = 384


def group_rows(group):
    rows = lax.broadcasted_iota(jnp.int32, (16, LANES), 0)
    return jnp.where(rows == group, 1.0, 0.0).astype(jnp.bfloat16)


def pack_mix(piece, qkv):
    for lb in range(SECT):
        piece[lb] = qkv[:, lb * LANES : (lb + 1) * LANES].astype(piece.dtype)


def pack_up(piece, out, up):
    rows = out.shape[0]
    for lb in range(SECT):
        lanes = slice(lb * LANES, (lb + 1) * LANES)
        piece[lb, :rows] = out[:, lanes].astype(piece.dtype)
        piece[lb, rows:] = up[:, lanes].astype(piece.dtype)


def pack_down(piece, down):
    rows = down.shape[0]
    for lb in range(SECT):
        for j in range(4):
            start = j * WIDE + lb * LANES
            piece[lb, j * rows : (j + 1) * rows] = down[:, start : start + LANES].astype(piece.dtype)


def pack_embedding(piece, weight, shift, gains, biases, square, block):
    n = weight.shape[0]
    square[...] = jnp.zeros_like(square)
    square[:GROUPS, :n] = shift[...]

    def ending(part, width):
        return jnp.concatenate([jnp.zeros((n, width - part.shape[1]), part.dtype), part], axis=1)

    third = ending(weight[:, L1 + L2 :], 3 * LANES)
    second = ending(weight[:, L1 : L1 + L2], 2 * LANES)
    blocks = [third[:, :LANES] + square[...].T[:n]]
    blocks += [third[:, LANES : 2 * LANES], third[:, 2 * LANES :]]
    blocks += [second[:, :LANES], second[:, LANES:], ending(weight[:, :L1], LANES)]
    rows = piece.shape[1] - VEC_ROWS
    if SECT * rows > 6 * n:
        blocks.append(jnp.zeros((SECT * rows - 6 * n, LANES), jnp.float32))
    flat = jnp.concatenate(blocks, axis=0).astype(piece.dtype)
    for lb in range(SECT):
        piece[lb, :rows] = flat[lb * rows : (lb + 1) * rows]
    line = jnp.concatenate([gains[...], biases[...]], axis=1)
    lines = [[line[:, at : at + LANES]] for at in range(0, line.shape[1], LANES)]
    piece[block, rows:] = rows_tile(lines).astype(piece.dtype)


def expand(series, group, x):
    empty = jnp.zeros((WINDOW - series.shape[0], series.shape[1]), series.dtype)
    x[:, :WINDOW] = jnp.concatenate([empty, series[...]], axis=0).T
    lane = lax.broadcasted_iota(jnp.int32, (x.shape[0], LANES), 1)
    x[:, WINDOW:] = jnp.where(lane == group, 1.0, 0.0).astype(x.dtype)


def embed(size, emb, pick, x, wsel, h):
    n = WIDE // size.dps
    flat = []
    for d in range(size.dps):
        place = (d // size.bs, d % size.bs, slice(0, size.lookback), slice(None))
        flat.append(jnp.concatenate([emb[(lb,) + place] for lb in range(SECT)], axis=0))
    blocks = [
        jnp.concatenate([rows[j * n : (j + 1) * n] for rows in flat], axis=0) for j in range(6)
    ]
    long, middle, short = (pick[g : g + 1, :] for g in (2, 1, 0))
    wide = jnp.concatenate(
        [
            blocks[0] * long,
            blocks[1] * long + blocks[3] * middle,
            blocks[2] * long + blocks[4] * middle + blocks[5] * short,
        ],
        axis=1,
    )
    wsel[...] = wide.T
    h[...] = dot_nt(x[...], jnp.concatenate([wide, blocks[0]], axis=1)).astype(h.dtype)


def embed_back(size, pick, x, wsel, dh, tables, grads, series_grad):
    history = series_grad.shape[0]
    series_grad[...] = dot_nt(wsel[...], dh[...])[WINDOW - history :]
    sums = dot_tn(dh[...], x[...])
    long, middle, short = (pick[g : g + 1, :].astype(jnp.float32) for g in (2, 1, 0))
    parts = [sums[:, i * LANES : (i + 1) * LANES] for i in range(4)]
    parts = [
        parts[0] * long + parts[3],
        parts[1] * long,
        parts[2] * long,
        parts[1] * middle,
        parts[2] * middle,
        parts[2] * short,
    ]
    rows = WIDE // (SECT * size.dps)
    spare = size.lookback - 6 * rows
    for pipe in range(SECT):
        block = (pipe % 2) * 2 + pipe // 2
        for dp in range(size.dps):
            start = (pipe * size.dps + dp) * rows
            pieces = [part[start : start + rows] for part in parts]
            if spare:
                pieces.append(jnp.zeros((spare, LANES), jnp.float32))
            pieces.append(vector_tile(tables.at[pipe], size.dps, dp))
            piece = jnp.concatenate(pieces, axis=0)
            grads[block, dp // size.bs, dp % size.bs] = piece.astype(grads.dtype)


def saved_shapes():
    low, wide = jnp.bfloat16, jnp.float32
    return [
        ((WIDE, WIDE), low),
        ((WIDE, 3 * WIDE), low),
        ((2 * SECT, WIDE, WIDE), low),
        ((WIDE, WIDE), low),
        ((WIDE, WIDE), wide),
        ((WIDE, WIDE), low),
        ((WIDE, 4 * WIDE), low),
        ((WIDE, 4 * WIDE), low),
        ((WIDE, WIDE), wide),
        ((SECT, 4 * WIDE), wide),
        ((WIDE, LANES), wide),
        ((WIDE, LANES), wide),
    ]


def chunk_shape(size, rows):
    return (SECT, ZS, size.bs, rows, LANES)


HALVES = (2, 2, 2, 2)
CROSS = (2,)


def follow(plan, section, act, compute):
    seen = {}
    for step in plan:
        if len(step) == 1:
            piece = seen.get(step[0], 0)
            seen[step[0]] = piece + 1
            compute(step[0], piece)
            continue
        op, kind, offset = step
        where = section + offset
        if isinstance(where, int):
            if 0 <= where < SECT:
                act(op, kind, where)
        elif offset == 0:
            act(op, kind, where)
        else:
            inside = where < SECT if offset > 0 else where >= 0

            @pl.when(inside)
            def _():
                act(op, kind, where)


def forward_kernel(dps, groups, *refs):
    size = Sizes(dps)
    given, refs = refs[:9], refs[9:]
    out, wholes, wsel, x, refs = refs[0], refs[1:5], refs[5], refs[6], refs[7:]
    kept, local, refs = refs[:12], refs[12:24], refs[24:]
    buffers, refs = refs[:4], refs[4:]
    pieces, held, refs = refs[:4], refs[4:13], refs[13:]
    emb_rows, pick, refs = refs[0], refs[1], refs[2:]
    given_sem, w_sem, kept_sem, own_sem, p_send, p_recv, send, recv = refs
    h, mixed, probs, attended, first, normed, slope, hidden, second, table, scale_1, scale_2 = local
    at = Place(dps)

    own = [
        pltpu.make_async_copy(
            pieces[kind].at[at.block],
            wholes[kind].at[at.pipe, at.block, at.z, at.b]
            if kind < EMB
            else wholes[kind].at[at.block, at.z, at.b],
            own_sem.at[kind],
        )
        for kind in range(4)
    ]
    def split(kind, back):
        copies = []
        for k in range(1, SECT):
            if back:
                region = wholes[kind].at[at.pipe_at(SECT - k), at.block, at.z, at.b]
                src = region
            else:
                block = at.blocks[k]
                region = wholes[kind].at[at.pipe, block, at.z, at.b]
                src = pieces[kind].at[block]
            sems = p_send.at[kind, k - 1], p_recv.at[kind, k - 1]
            copies.append(remote(src, region, *sems, (at.pipe_at(k), at.dp)))
        return copies

    def chunk(kind, section):
        if kind == EMB:
            return Spread(at, wholes[kind], send.at[3 * SECT], recv.at[3 * SECT])
        number = 3 * section + kind
        sort = SpreadCross if kind in CROSS else Spread
        return sort(at, wholes[kind].at[section], send.at[number], recv.at[number], HALVES[kind])

    def load(kind, section, core):
        blocks = pl.ds(core * 2, 2)
        src, dst = wholes[kind], buffers[kind]
        if kind != EMB:
            src, dst = src.at[section], dst.at[section % 2]
        sem = w_sem.at[kind, section % 2, core]
        return pltpu.make_async_copy(src.at[blocks], dst.at[blocks], sem)

    def loaded(kind, section):
        load(kind, section, at.c).wait()
        load(kind, section, 1 - at.c).wait()

    arrived = []

    def act(op, kind, section):
        if op == 0:
            if kind not in arrived:
                arrived.append(kind)
                own[kind].wait()
                if kind == EMB:
                    chunk(kind, section).start(0)
                    return
                for copy in split(kind, True):
                    copy.wait_recv()
                for copy in split(kind, False):
                    copy.wait_send()
                if kind == 0:
                    copies_start(split(1, False))
                    copies_start(split(2, False))
            chunk(kind, section).start(0)
        elif op < 4:
            chunk(kind, section).move(op - 1)
            if op == 1 and kind == EMB:
                gets[0].wait()
                expand(series, groups[0], x)
            if op == 3:
                load(kind, section, at.c).start()
        else:
            chunk(kind, section).land(3)
            load(kind, section, 1 - at.c).start()

    def saves(section, early):
        which = (1, 2, 3, 4, 5, 9, 10) if early else (6, 7, 8, 11)
        return [
            pltpu.make_async_copy(local[i], kept[i].at[section], kept_sem.at[i]) for i in which
        ]

    series, embed_weight, embed_bias, qkv, out_w, up_w, down_w, gains, biases = held
    gets = copies_of(zip(given, held), given_sem)
    for i in (3, 7, 8, 1, 2, 4, 5, 6, 0):
        gets[i].start()
    pick[...] = group_rows(groups[0])
    at.greet()
    gets[3].wait()
    pack_mix(pieces[0], qkv)
    own[0].start()
    at.met()
    copies_start(split(0, False))
    copies_wait(gets[1:3] + gets[7:9])
    pack_embedding(
        pieces[EMB], embed_weight, embed_bias, gains, biases, emb_rows, at.block
    )
    own[EMB].start()
    copies_wait(gets[4:7])
    pack_up(pieces[1], out_w, up_w)
    own[1].start()
    pack_down(pieces[2], down_w)
    own[2].start()
    table[...] = jnp.zeros_like(table)

    def before(name, piece):
        loaded(EMB, 0)
        embed(size, buffers[EMB], pick, x, wsel, h)

    follow(FORWARD_START, 0, act, before)

    @pl.loop(0, SECT)
    def _(section):
        att, up, down = (ref.at[section % 2] for ref in buffers[:3])
        keep_h = pltpu.make_async_copy(h, kept[0].at[section], kept_sem.at[0])

        def compute(name, piece):
            if name == "mix":
                if piece == 0:

                    @pl.when(section > 0)
                    def _():
                        copies_wait(saves(section - 1, True))

                    keep_h.start()
                    loaded(0, section)
                    block = section % 2 * 2 + section // 2
                    read_vectors(buffers[EMB], table, size.bs, size.lookback, block)
                forward_mix(size, att, table, h, mixed, piece)
            elif name == "attend":
                forward_attend(mixed, probs, attended, piece)
            elif name == "project":
                loaded(1, section)
                forward_project(size, up, table, h, attended, first, scale_1, normed)
                copies_start(saves(section, True))
            elif name == "up":
                if piece == 0:

                    @pl.when(section > 0)
                    def _():
                        copies_wait(saves(section - 1, False))

                forward_up(size, up, table, normed, slope, hidden, piece)
            else:
                if piece == 0:
                    loaded(2, section)
                    keep_h.wait()
                forward_down(size, down, table, normed, hidden, second, scale_2, h, piece)
                if piece == 1:
                    copies_start(saves(section, False))

        follow(FORWARD_PERIOD, section, act, compute)

    out[...] = h[...]
    copies_wait(saves(SECT - 1, True))
    copies_wait(saves(SECT - 1, False))


def copies_of(pairs, sems):
    return [pltpu.make_async_copy(src, dst, sems.at[i]) for i, (src, dst) in enumerate(pairs)]


def forward_all(groups, given, dps):
    size = Sizes(dps)
    low, wide = jnp.bfloat16, jnp.float32
    shapes = saved_shapes()
    rows = (size.qkv, size.dense, size.wide, size.emb)
    chunks = [chunk_shape(size, count) for count in rows]
    anywhere = pl.BlockSpec(memory_space=pl.ANY)
    inside = pl.BlockSpec(memory_space=pltpu.VMEM)
    outs = [((WIDE, WIDE), low)]
    outs += [((SECT,) + shape, low) for shape in chunks[:3]] + [(chunks[3], low)]
    outs += [((WINDOW, WIDE), low), ((WIDE, WIDE), low)]
    outs += [((SECT,) + shape, dtype) for shape, dtype in shapes]
    scratch = shapes + [((2,) + shape, low) for shape in chunks[:3]] + [(chunks[3], low)]
    scratch += [((SECT, count, LANES), low) for count in rows]
    scratch += [(array.shape, array.dtype) for array in given]
    scratch += [((LANES, LANES), wide), ((16, LANES), low)]
    slots = max(Spread.slots(size.bs), SpreadCross.slots(size.bs))
    dma = pltpu.SemaphoreType.DMA
    return pl.pallas_call(
        partial(forward_kernel, dps),
        out_shape=[jax.ShapeDtypeStruct(shape, dtype) for shape, dtype in outs],
        in_specs=[pl.BlockSpec(memory_space=pltpu.SMEM)] + [anywhere] * len(given),
        out_specs=[inside] + [anywhere] * 4 + [inside] * 2 + [anywhere] * len(shapes),
        scratch_shapes=[pltpu.VMEM(shape, dtype) for shape, dtype in scratch]
        + [
            dma((len(given),)),
            dma((4, 2, 2)),
            dma((len(shapes),)),
            dma((4,)),
            dma((3, SECT - 1)),
            dma((3, SECT - 1)),
            dma((1 + 3 * SECT, slots)),
            dma((1 + 3 * SECT, slots)),
        ],
        compiler_params=pltpu.CompilerParams(
            collective_id=0, has_side_effects=True, vmem_limit_bytes=60 * 1024 * 1024
        ),
        name="gather_forward",
    )(groups, *given)


FETCHES = {
    ("norm2", 0): (("second", "scale_2"), ("second", "scale_2")),
    ("down", 0): (("hidden",), ()),
    ("down", 1): ((), ("hidden",)),
    ("gelu", 0): (("slope", 2), ()),
    ("gelu", 1): ((), ("slope", 2)),
    ("up", 0): (("normed",), ("normed",)),
    ("normed", 0): ((1,), ()),
    ("norm1", 0): (("first", "scale_1", "attended"), ("first", "scale_1", "attended", 1)),
    ("attend", 0): (("mixed", "probs"), ()),
    ("attend", 3): ((), ("mixed", "probs")),
    ("mix", 0): (("h",), ()),
    ("mix", 1): ((), ("h",)),
    ("input", 0): ((0,), (0,)),
}


def backward_kernel(dps, groups, att, up, down, cotangent, x_in, wsel_in, *refs):
    size = Sizes(dps)
    kept, refs = refs[:12], refs[12:]
    series_grad, outs, refs = refs[0], refs[1:5], refs[5:]
    local, refs = refs[:11], refs[11:]
    tables, w_att, w_up, w_down, dtables, dy, dnormed, dlow, dlow_t, dmixed, dup = refs[:11]
    x, wsel, pick, delta, refs = *refs[11:15], refs[15:]
    kinds = []
    for kind in range(4):
        count = 6 if kind in CROSS else 5
        kinds.append(refs[:4] + (refs[4 : 4 + count],))
        refs = refs[4 + count :]
    w_sem, kept_sem, table_sem, late_sem, out_sem, p_send, p_recv, send, recv, credit = refs
    h, mixed, probs, attended, first, normed, slope, hidden, second, scale_1, scale_2 = local
    at = Place(dps)
    last = SECT - 1

    def weights(kind, section):
        src, dst = ((att, w_att), (up, w_up), (down, w_down))[kind]
        return pltpu.make_async_copy(src.at[section], dst, w_sem.at[kind])

    names = ("h", "mixed", "probs", "attended", "first", "normed", "slope", "hidden", "second")
    names += ("table", "scale_1", "scale_2")
    held = dict(zip(names[:9] + names[10:], local))

    def fetches(section, *wanted):
        found = []
        for name in wanted:
            if isinstance(name, int):
                found.append(weights(name, section))
            else:
                i = names.index(name)
                dst = held[name]
                found.append(pltpu.make_async_copy(kept[i].at[section], dst, kept_sem.at[i]))
        return found

    def chunk(kind, i):
        grads, totals, finals, landing, bufs = kinds[kind]
        sort = FoldCross if kind in CROSS else Fold
        refs = (grads, totals.at[i % 2], landing, bufs, finals.at[i])
        return sort(at, *refs, send.at[kind], recv.at[kind], credit.at[kind], HALVES[kind])

    def hand_over(kind, i):
        landing = outs[kind].at[at.block]
        final = kinds[kind][2].at[i]
        return (
            pltpu.make_async_copy(final, landing, out_sem.at[kind]),
            remote(final, landing, p_send.at[kind, i], p_recv.at[kind, at.pipe], (last - i, at.dp)),
        )

    def act(op, kind, i):
        again, more = (False, False) if kind == EMB else (i > 0, i < last)
        if op == 0:
            chunk(kind, i).start(0, again)
        elif op < 4:
            chunk(kind, i).move(op - 1, again, more)
        else:
            chunk(kind, i).land(3, more)
            if kind == EMB:
                outs[kind][...] = kinds[kind][2][0]
            else:
                here, away = hand_over(kind, i)

                @pl.when(at.pipe == last - i)
                def _():
                    here.start()

                @pl.when(at.pipe != last - i)
                def _():
                    away.start()

    at.greet()
    get_tables = pltpu.make_async_copy(kept[9], tables, table_sem)
    late = copies_of(((cotangent, dy), (x_in, x), (wsel_in, wsel)), late_sem)
    copies_start([late[0], get_tables] + fetches(last, "second", "scale_2", "hidden"))
    copies_start(fetches(last, "slope", 2, "normed", 1, "first", "scale_1", "attended"))
    copies_start(fetches(last, "mixed", "probs", "h", 0) + late[1:])
    pick[...] = group_rows(groups[0])
    copies_wait([late[0], get_tables])

    @pl.loop(0, SECT)
    def _(i):
        section = last - i
        table, dtable = tables.at[section], dtables.at[section]

        def compute(name, piece):
            need, free = FETCHES.get((name, piece), ((), ()))
            copies_wait(fetches(section, *need))
            if name == "norm2":
                backward_norm_two(table, dtable, dy, second, scale_2, dnormed, dlow, dlow_t)
                pl.when(i == 0)(at.met)
            elif name == "down":
                backward_down(size, kinds[2][0], hidden, dlow_t, piece)
            elif name == "gelu":
                backward_gelu(size, w_down, dtable, slope, dlow, dup, piece)
            elif name == "up":
                backward_up(size, kinds[1][0], normed, dup)
            elif name == "normed":
                backward_normed(size, w_up, dnormed, dup)
            elif name == "norm1":
                backward_norm_one(
                    size,
                    w_up,
                    table,
                    kinds[1][0],
                    dtable,
                    first,
                    scale_1,
                    attended,
                    dnormed,
                    dlow,
                    dlow_t,
                    delta,
                )
            elif name == "attend":
                backward_attend(mixed, probs, delta, dtable, dlow, dmixed, piece)
            elif name == "mix":
                backward_mix(size, kinds[0][0], h, dmixed, piece)
            else:
                backward_input(size, w_att, dnormed, dmixed, dy)
            if free:

                @pl.when(section > 0)
                def _():
                    copies_start(fetches(section - 1, *free))

        follow(BACKWARD_PERIOD, i, act, compute)

    def after(name, piece):
        copies_wait(late[1:])
        embed_back(size, pick, x, wsel, dy, dtables, kinds[EMB][0], series_grad)

    follow(BACKWARD_END, 0, act, after)

    for kind in range(3):
        for i in range(SECT):
            here, away = hand_over(kind, i)

            @pl.when(at.pipe == last - i)
            def _():
                here.wait()

            @pl.when(at.pipe != last - i)
            def _():
                away.wait_send()

        for k in range(1, SECT):
            other = at.pipe_at(k)
            landing = outs[kind].at[at.blocks[k]]
            sems = p_send.at[kind, 0], p_recv.at[kind, other]
            remote(landing, landing, *sems, (other, at.dp)).wait_recv()


def backward_all(groups, weights, cotangent, x, wsel, kept, history, dps):
    size = Sizes(dps)
    low, wide = jnp.bfloat16, jnp.float32
    anywhere = pl.BlockSpec(memory_space=pl.ANY)
    inside = pl.BlockSpec(memory_space=pltpu.VMEM)
    shapes = saved_shapes()
    kind_rows = (size.qkv, size.dense, size.wide, size.emb)
    scratch = shapes[:9] + shapes[10:] + [((SECT,) + shapes[9][0], wide)]
    scratch += [(chunk_shape(size, rows), low) for rows in kind_rows[:3]]
    scratch += [
        ((SECT,) + shapes[9][0], wide),
        ((WIDE, WIDE), low),
        ((WIDE, WIDE), wide),
        ((WIDE, WIDE), low),
        ((WIDE, WIDE), low),
        ((WIDE, 3 * WIDE), low),
        ((WIDE, 4 * WIDE), low),
        ((WIDE, WIDE), low),
        ((WINDOW, WIDE), low),
        ((16, LANES), low),
        ((16, WIDE), wide),
    ]
    for kind, rows in enumerate(kind_rows):
        sets, results = (1, 1) if kind == EMB else (2, SECT)
        scratch += [
            (chunk_shape(size, rows), low),
            ((sets, 2, ZS, size.bs, rows, LANES), low),
            ((results, rows, LANES), low),
            ((2, ZS, size.bs, rows, LANES), low),
        ]
        sort = FoldCross if kind in CROSS else Fold
        scratch += [(shape, low) for shape in sort.buffers(size.bs, rows, HALVES[kind])]
    slots = max(Fold.slots(size.bs), FoldCross.slots(size.bs))
    dma = pltpu.SemaphoreType.DMA
    return pl.pallas_call(
        partial(backward_kernel, dps),
        out_shape=[jax.ShapeDtypeStruct((history, WIDE), wide)]
        + [jax.ShapeDtypeStruct((SECT, rows, LANES), low) for rows in kind_rows[:3]]
        + [jax.ShapeDtypeStruct((size.emb, LANES), low)],
        in_specs=[pl.BlockSpec(memory_space=pltpu.SMEM)] + [anywhere] * (6 + len(kept)),
        out_specs=[inside] + [anywhere] * 3 + [inside],
        scratch_shapes=[pltpu.VMEM(shape, dtype) for shape, dtype in scratch]
        + [
            dma((3,)),
            dma((12,)),
            dma(()),
            dma((3,)),
            dma((3,)),
            dma((3, SECT)),
            dma((3, SECT)),
            dma((4, slots)),
            dma((4, slots)),
            pltpu.SemaphoreType.REGULAR((4, slots)),
        ],
        compiler_params=pltpu.CompilerParams(
            collective_id=1, has_side_effects=True, vmem_limit_bytes=60 * 1024 * 1024
        ),
        name="backward_fold",
    )(groups, *weights, cotangent, x, wsel, *kept)


def finish_kernel(dps, n_gains, n_biases, *refs):
    size = Sizes(dps)
    given, refs = refs[:6], refs[6:]
    block_out, series_out, embed_w, embed_b, qkv, out, up_out, down_out, gains, biases = refs[:10]
    att, up, down, emb, sems = refs[10:]
    copies = copies_of(zip(given, (att, up, down, emb, block_out, series_out)), sems)
    copies_start(copies)
    copies_wait(copies[:4])
    for lb in range(SECT):
        lanes = slice(lb * LANES, (lb + 1) * LANES)
        qkv[:, lanes] = att[lb].astype(jnp.float32)
        out[:, lanes] = up[lb, : size.out].astype(jnp.float32)
        up_out[:, lanes] = up[lb, size.out :].astype(jnp.float32)
        for j in range(4):
            rows = slice(j * size.down, (j + 1) * size.down)
            start = j * WIDE + lb * LANES
            down_out[:, start : start + LANES] = down[lb, rows].astype(jnp.float32)
    vectors = emb[size.lookback :].astype(jnp.float32)
    count = -(-(n_gains + n_biases) // LANES)
    flat = jnp.concatenate([vectors[row : row + 1] for row in range(count)], axis=1)
    gains[...] = flat[:, :n_gains]
    biases[...] = flat[:, n_gains : n_gains + n_biases]
    rows = WIDE // (SECT * dps)
    packed = emb[: size.lookback].astype(jnp.float32)
    packed = [packed[i * rows : (i + 1) * rows] for i in range(6)]
    square = jnp.concatenate([packed[0], jnp.zeros((LANES - rows, LANES), jnp.float32)], axis=0)
    embed_b[...] = square.T[:GROUPS, :rows]
    packed = jnp.concatenate(packed, axis=1)
    ends = ((6 * LANES, L1), (5 * LANES, L2), (3 * LANES, L3))
    embed_w[...] = jnp.concatenate([packed[:, end - span : end] for end, span in ends], axis=1)
    copies_wait(copies[4:])


def finish_all(sums, block, series, n_gains, n_biases, dps):
    size = Sizes(dps)
    wide = jnp.float32
    columns = WIDE // (SECT * dps)
    outs = [
        (block.shape, block.dtype),
        (series.shape, wide),
        ((columns, L1 + L2 + L3), wide),
        ((GROUPS, columns), wide),
        ((size.qkv, WIDE), wide),
        ((size.out, WIDE), wide),
        ((size.up, WIDE), wide),
        ((size.down, 4 * WIDE), wide),
        ((1, n_gains), wide),
        ((1, n_biases), wide),
    ]
    anywhere = pl.BlockSpec(memory_space=pl.ANY)
    inside = pl.BlockSpec(memory_space=pltpu.VMEM)
    return pl.pallas_call(
        partial(finish_kernel, dps, n_gains, n_biases),
        out_shape=[jax.ShapeDtypeStruct(shape, dtype) for shape, dtype in outs],
        in_specs=[anywhere] * 6,
        out_specs=[inside] * 10,
        scratch_shapes=[pltpu.VMEM(array.shape, array.dtype) for array in sums]
        + [pltpu.SemaphoreType.DMA((6,))],
        compiler_params=pltpu.CompilerParams(vmem_limit_bytes=60 * 1024 * 1024),
        name="finish",
    )(*sums, block, series)


def per_device(
    series,
    groups,
    cotangent,
    embed_weight,
    embed_bias,
    qkv_weight,
    out_weight,
    up_weight,
    down_weight,
    gains,
    biases,
):
    dps = lax.axis_size("dp")
    given = (
        series[0],
        embed_weight.T,
        embed_bias,
        qkv_weight[0],
        out_weight[0],
        up_weight[0],
        down_weight[0],
        gains,
        biases,
    )
    block_output, att, up, down, _, wsel, x, *kept = forward_all(groups, given, dps)
    series_grad, *sums = backward_all(
        groups, (att, up, down), cotangent[0], x, wsel, kept, series.shape[1], dps
    )
    outs = finish_all(sums, block_output, series_grad, gains.shape[1], biases.shape[1], dps)
    block_output, series_grad, embed_w, embed_b, qkv, out, up, down, gain_sum, bias_sum = outs
    return (
        block_output[None],
        series_grad[None],
        embed_w.T,
        embed_b,
        qkv[None],
        out[None],
        up[None],
        down[None],
        gain_sum,
        bias_sum,
    )


def solution(mesh):
    return jax.shard_map(
        per_device,
        mesh=mesh,
        in_specs=(
            P(("pipe", "dp"), None, None),
            P(("pipe", "dp")),
            P(("pipe", "dp"), None, None),
            P(None, "dp"),
            P(None, "dp"),
            P("pipe", "dp", None),
            P("pipe", "dp", None),
            P("pipe", "dp", None),
            P("pipe", "dp", None),
            P("pipe", "dp"),
            P("pipe", "dp"),
        ),
        out_specs=(
            P(("pipe", "dp"), None, None),
            P(("pipe", "dp"), None, None),
            P(None, ("pipe", "dp")),
            P(None, ("pipe", "dp")),
            P("pipe", "dp", None),
            P("pipe", "dp", None),
            P("pipe", "dp", None),
            P("pipe", "dp", None),
            P("pipe", "dp"),
            P("pipe", "dp"),
        ),
        check_vma=False,
    )
```

```python
from functools import partial
import math

import jax
import jax.numpy as jnp
from jax import lax
from jax.experimental import pallas as pl
from jax.experimental.pallas import tpu as pltpu
from jax.sharding import PartitionSpec as P

HEAD = 64
L1 = 96
L2 = 192
L3 = 336
GROUPS = 3


NORM_EPS = 1e-05


MESH = pl.DeviceIdType.MESH
LANES = 128
ZS = 4
SECT = 4
EMB = 3


class Place:
    def __init__(self, dps):
        self.bs = bs = dps // ZS
        pipe = lax.axis_index("pipe")
        dp = lax.axis_index("dp")
        self.pipe, self.dp = pipe, dp
        self.x, self.c = x, c = lax.div(pipe, 2), lax.rem(pipe, 2)
        self.z, self.b = z, b = lax.div(dp, bs), lax.rem(dp, bs)
        self.block = c * 2 + x
        self.other_block = c * 2 + 1 - x
        self.x_peer = ((1 - x) * 2 + c, dp)
        self.core_peer = (x * 2 + 1 - c, dp)
        self.pipes = [lax.rem(pipe + k, SECT) for k in range(SECT)]
        self.blocks = [self.block_of(other) for other in self.pipes]
        self.zs = [lax.rem(z + k, ZS) for k in range(ZS)]
        self.bees = [lax.rem(b + k, bs) for k in range(bs)]
        self.z_peers = [(pipe, other * bs + b) for other in self.zs]
        self.b_peers = [(pipe, z * bs + other) for other in self.bees]

    def block_of(self, pipe):
        return lax.rem(pipe, 2) * 2 + lax.div(pipe, 2)

    def pipe_at(self, step):
        return self.pipes[step % SECT]

    def z_at(self, step):
        return self.zs[step % ZS]

    def b_at(self, step):
        return self.bees[step % self.bs]

    def z_peer(self, step):
        return self.z_peers[step % ZS]

    def b_peer(self, step):
        return self.b_peers[step % self.bs]

    def greet(self):
        barrier = pltpu.get_barrier_semaphore()
        peers = [(self.pipe_at(k), self.dp) for k in range(1, SECT)]
        peers += [self.z_peer(k) for k in range(1, ZS)]
        peers += [self.b_peer(k) for k in range(1, self.bs)]
        for peer in peers:
            pl.semaphore_signal(barrier, inc=1, device_id=peer, device_id_type=MESH)

    def met(self):
        pl.semaphore_wait(pltpu.get_barrier_semaphore(), SECT + ZS + self.bs - 3)


def remote(src, dst, send, recv, peer):
    return pltpu.make_async_remote_copy(
        src_ref=src, dst_ref=dst, send_sem=send, recv_sem=recv, device_id=peer, device_id_type=MESH
    )


FORWARD_START = (
    (0, 3, 0),
    (0, 0, 0),
    (0, 2, 0),
    (1, 3, 0),
    (1, 0, 0),
    (0, 1, 0),
    (2, 3, 0),
    (2, 0, 0),
    (0, 0, 1),
    (1, 1, 0),
    (1, 2, 0),
    (3, 3, 0),
    (0, 2, 1),
    (1, 0, 1),
    (2, 1, 0),
    (4, 3, 0),
    (3, 0, 0),
    ("embed",),
    (4, 0, 0),
)
FORWARD_PERIOD = (
    ("mix",),
    (0, 1, 1),
    (2, 0, 1),
    ("mix",),
    ("attend",),
    (3, 1, 0),
    ("attend",),
    (2, 2, 0),
    ("attend",),
    (0, 0, 2),
    (4, 1, 0),
    ("attend",),
    ("project",),
    (1, 1, 1),
    ("up",),
    (1, 2, 1),
    (0, 2, 2),
    (3, 2, 0),
    ("up",),
    (1, 0, 2),
    ("up",),
    (2, 1, 1),
    (3, 0, 1),
    (4, 2, 0),
    ("up",),
    ("down",),
    (4, 0, 1),
    ("down",),
)
BACKWARD_PERIOD = (
    ("norm2",),
    (1, 0, -1),
    ("down",),
    ("down",),
    ("gelu",),
    ("gelu",),
    (2, 1, -1),
    (0, 2, 0),
    ("up",),
    ("normed",),
    (2, 0, -1),
    ("norm1",),
    (4, 1, -2),
    (4, 2, -2),
    (1, 2, 0),
    (3, 1, -1),
    (0, 1, 0),
    ("attend",),
    ("attend",),
    ("attend",),
    ("attend",),
    (3, 2, -1),
    (1, 1, 0),
    (4, 0, -2),
    (3, 0, -1),
    ("mix",),
    ("mix",),
    (0, 0, 0),
    ("input",),
    (2, 2, 0),
)
BACKWARD_END = (
    ("embed",),
    (1, 0, 3),
    (2, 1, 3),
    (2, 0, 3),
    (4, 1, 2),
    (4, 2, 2),
    (3, 1, 3),
    (0, 3, 0),
    (3, 2, 3),
    (4, 0, 2),
    (1, 3, 0),
    (3, 0, 3),
    (2, 3, 0),
    (3, 3, 0),
    (4, 1, 3),
    (4, 2, 3),
    (4, 0, 3),
    (4, 3, 0),
)


def copies_start(copies):
    for copy in copies:
        copy.start()


def copies_begin(copies):
    for copy in copies:
        copy.start(priority=1)


def copies_wait(copies):
    for copy in copies:
        copy.wait()


class Spread:
    def __init__(self, at, out, send, recv, half=ZS // 2):
        self.at, self.out, self.send, self.recv = at, out, send, recv
        nb = at.bs - 1
        self.slot_z = 0
        self.slot_b1 = ZS - 1
        self.slot_x1 = self.slot_b1 + nb
        self.slot_x2 = self.slot_x1 + 1
        self.slot_b2 = self.slot_x2 + 1
        self.slot_c = self.slot_b2 + nb
        self.half = half

    @staticmethod
    def slots(bs):
        return ZS - 1 + 2 * (bs - 1) + 3

    def copy(self, region, slot, peer):
        return remote(region, region, self.send.at[slot], self.recv.at[slot], peer)

    def copies(self, stage, back):
        at, out, half = self.at, self.out, self.half
        rest = pl.ds(half, ZS - half)
        x_block = at.other_block if back else at.block
        if stage == 0:
            return [
                self.copy(
                    out.at[at.block, at.z_at(ZS - k) if back else at.z, at.b],
                    self.slot_z + k - 1,
                    at.z_peer(k),
                )
                for k in range(1, ZS)
            ]
        if stage == 3:
            core = 1 - at.c if back else at.c
            return [self.copy(out.at[pl.ds(core * 2, 2)], self.slot_c, at.core_peer)]
        copies = []
        for k in range(1, at.bs):
            b = at.b_at(at.bs - k) if back else at.b
            if stage == 1:
                region, slot = out.at[at.block, pl.ds(0, half), b], self.slot_b1
            else:
                region, slot = out.at[pl.ds(at.c * 2, 2), rest, b], self.slot_b2
            copies.append(self.copy(region, slot + k - 1, at.b_peer(k)))
        if stage == 1:
            region, slot = out.at[x_block, rest, at.b], self.slot_x1
        else:
            region, slot = out.at[x_block, pl.ds(0, half)], self.slot_x2
        copies.append(self.copy(region, slot, at.x_peer))
        return copies

    def start(self, stage):
        copies_start(self.copies(stage, False))

    def land(self, stage):
        for copy in self.copies(stage, True):
            copy.wait_recv()
        for copy in self.copies(stage, False):
            copy.wait_send()

    def move(self, stage):
        self.land(stage)
        self.start(stage + 1)


class SpreadCross(Spread):
    @staticmethod
    def slots(bs):
        return 2 * bs + 2 * ZS - 1

    def copies(self, stage, back):
        at, out = self.at, self.out
        rows = out.shape[-2]
        cut = rows // 32 * 16
        some, rest = pl.ds(0, cut), pl.ds(cut, rows - cut)
        core = 1 - at.c if back else at.c
        if stage == 3:
            return [self.copy(out.at[pl.ds(core * 2, 2)], 2 * at.bs + 2 * ZS - 2, at.core_peer)]
        both = pl.ds(at.c * 2, 2)
        x_block = at.other_block if back else at.block
        copies = []
        if stage == 1:
            for k in range(1, ZS):
                z = at.z_at(ZS - k) if back else at.z
                copies.append(self.copy(out.at[both, z, at.b, some], at.bs + k - 1, at.z_peer(k)))
                slot = at.bs + ZS + k - 2
                copies.append(self.copy(out.at[at.block, z, :, rest], slot, at.z_peer(k)))
            return copies
        base = 0 if stage == 0 else at.bs + 2 * ZS - 2
        for k in range(1, at.bs):
            b = at.b_at(at.bs - k) if back else at.b
            region = out.at[at.block, at.z, b, rest] if stage == 0 else out.at[both, :, b, some]
            copies.append(self.copy(region, base + k, at.b_peer(k)))
        if stage == 0:
            region = out.at[x_block, at.z, at.b, some]
        else:
            region = out.at[x_block, :, :, rest]
        copies.append(self.copy(region, base, at.x_peer))
        return copies


class Fold:
    def __init__(self, at, grads, total, landing, bufs, final, send, recv, credit, half):
        self.at, self.grads, self.total = at, grads, total
        self.landing, self.bufs, self.final = landing, bufs, final
        self.send, self.recv, self.credit = send, recv, credit
        self.half = half
        nb = at.bs - 1
        self.slot_x1 = 1
        self.slot_b1 = 2
        self.slot_x2 = 2 + nb
        self.slot_b2 = 3 + nb
        self.slot_z = 3 + 2 * nb

    @staticmethod
    def slots(bs):
        return 3 + 2 * (bs - 1) + ZS - 1

    @staticmethod
    def buffers(bs, rows, half):
        nb = max(bs - 1, 1)
        rest = ZS - half
        return [
            (half, bs, rows, LANES),
            (nb, 2, rest, rows, LANES),
            (rest, rows, LANES),
            (nb, half, rows, LANES),
            (ZS - 1, rows, LANES),
        ]

    def core_parts(self):
        other = self.grads.at[pl.ds((1 - self.at.c) * 2, 2)]
        return [(other, self.landing, 0, self.at.core_peer, self.at.core_peer)]

    def parts(self, stage):
        at, half, total, bufs = self.at, self.half, self.total, self.bufs
        if stage == 0:
            return self.core_parts()
        if stage == 3:
            return [
                (
                    total.at[at.x, at.z_at(k), at.b],
                    bufs[4].at[k - 1],
                    self.slot_z + k - 1,
                    at.z_peer(k),
                    at.z_peer(ZS - k),
                )
                for k in range(1, ZS)
            ]
        rest = pl.ds(half, ZS - half)
        found = []
        for k in range(1, at.bs):
            if stage == 1:
                src, buf, slot = total.at[:, rest, at.b_at(k)], bufs[1], self.slot_b1
            else:
                src, buf, slot = total.at[at.x, pl.ds(0, half), at.b_at(k)], bufs[3], self.slot_b2
            found.append((src, buf.at[k - 1], slot + k - 1, at.b_peer(k), at.b_peer(at.bs - k)))
        if stage == 1:
            src, buf, slot = total.at[1 - at.x, pl.ds(0, half)], bufs[0], self.slot_x1
        else:
            src, buf, slot = total.at[1 - at.x, rest, at.b], bufs[2], self.slot_x2
        found.append((src, buf, slot, at.x_peer, at.x_peer))
        return found

    def start(self, stage, again):
        for src, buf, slot, to, _ in self.parts(stage):
            if again is not False:

                @pl.when(again)
                def _():
                    pl.semaphore_wait(self.credit.at[slot], 1)

            remote(src, buf, self.send.at[slot], self.recv.at[slot], to).start()

    def land(self, stage, more):
        parts = self.parts(stage)
        for src, buf, slot, to, _ in parts:
            remote(src, buf, self.send.at[slot], self.recv.at[slot], to).wait()
        self.add(stage)
        if more is not False:

            @pl.when(more)
            def _():
                for _, _, slot, _, origin in parts:
                    pl.semaphore_signal(
                        self.credit.at[slot], inc=1, device_id=origin, device_id_type=MESH
                    )

    def add_core(self):
        at, bs, total = self.at, self.at.bs, self.total

        @pl.loop(0, 2 * ZS * bs)
        def _(i):
            z, b = i // bs % ZS, i % bs
            x = i // (ZS * bs)
            total[x, z, b] = self.grads[at.c * 2 + x, z, b] + self.landing[x, z, b]

    def add(self, stage):
        at, half, bs = self.at, self.half, self.at.bs
        total, bufs = self.total, self.bufs
        rest = ZS - half
        if stage == 0:
            self.add_core()
        elif stage == 1:

            @pl.loop(0, half * bs)
            def _(i):
                z, b = i // bs, i % bs
                total[at.x, z, b] = total[at.x, z, b] + bufs[0][z, b]

            @pl.loop(0, 2 * rest)
            def _(i):
                x, z = i // rest, i % rest
                for k in range(bs - 1):
                    total[x, half + z, at.b] = total[x, half + z, at.b] + bufs[1][k, x, z]

        elif stage == 2:

            @pl.loop(0, rest)
            def _(z):
                total[at.x, half + z, at.b] = total[at.x, half + z, at.b] + bufs[2][z]

            @pl.loop(0, half)
            def _(z):
                for k in range(bs - 1):
                    total[at.x, z, at.b] = total[at.x, z, at.b] + bufs[3][k, z]

        else:
            self.finish([bufs[4][k] for k in range(ZS - 1)])

    def finish(self, pieces):
        at = self.at
        done = self.total[at.x, at.z, at.b].astype(jnp.float32)
        for piece in pieces:
            done = done + piece.astype(jnp.float32)
        self.final[...] = done.astype(self.final.dtype)

    def move(self, stage, again, more):
        self.land(stage, more)
        self.start(stage + 1, again)


class FoldCross(Fold):
    @staticmethod
    def slots(bs):
        return 2 * bs + 2 * ZS - 1

    @staticmethod
    def buffers(bs, rows, half):
        nb = max(bs - 1, 1)
        cut = rows // 32 * 16
        rest = rows - cut
        return [
            (nb, 2, ZS, cut, LANES),
            (ZS, bs, rest, LANES),
            (ZS - 1, 2, cut, LANES),
            (ZS - 1, bs, rest, LANES),
            (cut, LANES),
            (nb, rest, LANES),
        ]

    def cuts(self):
        rows = self.total.shape[-2]
        cut = rows // 32 * 16
        return pl.ds(0, cut), pl.ds(cut, rows - cut)

    def parts(self, stage):
        at, total, bufs = self.at, self.total, self.bufs
        if stage == 0:
            return self.core_parts()
        some, rest = self.cuts()
        found = []
        if stage == 2:
            for k in range(1, ZS):
                pair = (at.z_peer(k), at.z_peer(ZS - k))
                z = at.z_at(k)
                found.append((total.at[:, z, at.b, some], bufs[2].at[k - 1], at.bs + k, *pair))
                slot = at.bs + ZS + k - 1
                found.append((total.at[at.x, z, :, rest], bufs[3].at[k - 1], slot, *pair))
            return found
        base = 1 if stage == 1 else at.bs + 2 * ZS - 1
        for k in range(1, at.bs):
            pair = (at.b_peer(k), at.b_peer(at.bs - k))
            if stage == 1:
                src, buf = total.at[:, :, at.b_at(k), some], bufs[0].at[k - 1]
            else:
                src, buf = total.at[at.x, at.z, at.b_at(k), rest], bufs[5].at[k - 1]
            found.append((src, buf, base + k, *pair))
        if stage == 1:
            src, buf = total.at[1 - at.x, :, :, rest], bufs[1]
        else:
            src, buf = total.at[1 - at.x, at.z, at.b, some], bufs[4]
        found.append((src, buf, base, at.x_peer, at.x_peer))
        return found

    def add(self, stage):
        at, bs = self.at, self.at.bs
        total, bufs = self.total, self.bufs
        some, rest = self.cuts()
        if stage == 0:
            self.add_core()
        elif stage == 1:

            @pl.loop(0, 2 * ZS)
            def _(i):
                x, z = i // ZS, i % ZS
                for k in range(bs - 1):
                    total[x, z, at.b, some] = total[x, z, at.b, some] + bufs[0][k, x, z]

            @pl.loop(0, ZS * bs)
            def _(i):
                z, b = i // bs, i % bs
                total[at.x, z, b, rest] = total[at.x, z, b, rest] + bufs[1][z, b]

        elif stage == 2:
            for x in range(2):
                for k in range(ZS - 1):
                    total[x, at.z, at.b, some] = total[x, at.z, at.b, some] + bufs[2][k, x]

            @pl.loop(0, bs)
            def _(b):
                for k in range(ZS - 1):
                    total[at.x, at.z, b, rest] = total[at.x, at.z, b, rest] + bufs[3][k, b]

        else:
            total[at.x, at.z, at.b, some] = total[at.x, at.z, at.b, some] + bufs[4][...]
            for k in range(bs - 1):
                total[at.x, at.z, at.b, rest] = total[at.x, at.z, at.b, rest] + bufs[5][k]
            self.final[...] = total[at.x, at.z, at.b]


HALF = 256
WIDE = 512
QKV_TILE = 768
VEC_ROWS = 16


STEP = 64


def by_rows(fn, *arrays, step=STEP):
    parts = [
        fn(*[array[at : at + step] for array in arrays])
        for at in range(0, arrays[0].shape[0], step)
    ]
    if isinstance(parts[0], tuple):
        return tuple(jnp.concatenate(part, axis=0) for part in zip(*parts))
    return jnp.concatenate(parts, axis=0)


def dot_nt(a, b):
    return lax.dot_general(a, b, (((1,), (1,)), ((), ())), preferred_element_type=jnp.float32)


def dot_nn(a, b):
    return lax.dot_general(a, b, (((1,), (0,)), ((), ())), preferred_element_type=jnp.float32)


def dot_tn(a, b):
    return lax.dot_general(a, b, (((0,), (0,)), ((), ())), preferred_element_type=jnp.float32)


def aligned(index, unit):
    return pl.multiple_of(index, unit)


def rows_of(ref, bs, first, count, start, rows, blocks=range(SECT)):
    parts = []
    for i in range(count):
        d = first + i
        place = (d // bs, d % bs)
        parts.append(
            jnp.concatenate(
                [ref[(lb,) + place + (pl.ds(start, rows), slice(None))] for lb in blocks], axis=1
            )
        )
    return parts[0] if count == 1 else jnp.concatenate(parts, axis=0)


def put_rows(ref, bs, first, count, start, rows, value, block=0):
    value = value.astype(ref.dtype)
    for i in range(count):
        d = first + i
        place = (d // bs, d % bs)
        for lane in range(value.shape[1] // LANES):
            ref[(block + lane,) + place + (pl.ds(start, rows), slice(None))] = value[
                i * rows : (i + 1) * rows, lane * LANES : (lane + 1) * LANES
            ]


def vector_pieces(dps):
    n_gains, n_biases = 2 * WIDE // dps, 10 * WIDE // dps
    starts = [(0, 0), (0, 2), (1, 0), (1, 2), (2, 0), (2, 1), (2, 2), (2, 3), (3, 0), (3, 2)]
    pieces = []
    for d in range(dps):
        at = 0
        while at < n_gains + n_biases:
            if at < n_gains:
                index = d * n_gains + at
                row, column = (1, 3)[index // WIDE], WIDE + index % WIDE
                left = n_gains - at
            else:
                index = d * n_biases + at - n_gains
                row, part = starts[index // WIDE]
                column = part * WIDE + index % WIDE
                left = n_gains + n_biases - at
            size = min(left, LANES - at % LANES, LANES - column % LANES)
            pieces.append((d, at // LANES, at % LANES, row, column, size))
            at += size
    return pieces


def read_vectors(ref, table, bs, start, block):
    tiles = {}
    for d, row, lane, to_row, to_lane, size in vector_pieces(ZS * bs):
        if d not in tiles:
            tile = ref[block, d // bs, d % bs, start : start + VEC_ROWS, :]
            tiles[d] = tile.astype(jnp.float32)
        table[to_row : to_row + 1, to_lane : to_lane + size] = tiles[d][
            row : row + 1, lane : lane + size
        ]


def rows_tile(lines):
    row_id = lax.broadcasted_iota(jnp.int32, (VEC_ROWS, LANES), 0)
    tile = jnp.zeros((VEC_ROWS, LANES), jnp.float32)
    for row, pieces in enumerate(lines):
        have = sum(piece.shape[1] for piece in pieces)
        if have < LANES:
            pieces = pieces + [jnp.zeros((1, LANES - have), jnp.float32)]
        line = pieces[0] if len(pieces) == 1 else jnp.concatenate(pieces, axis=1)
        tile = jnp.where(row_id == row, line, tile)
    return tile


def vector_tile(table, dps, place):
    lines = []
    for d, row, lane, to_row, to_lane, size in vector_pieces(dps):
        if d == place:
            if row == len(lines):
                lines.append([])
            lines[row].append(table[to_row : to_row + 1, to_lane : to_lane + size])
    return rows_tile(lines)


def fold_rows(x):
    total = x[:8]
    for at in range(8, x.shape[0], 8):
        total = total + x[at : at + 8]
    return total


def normalize(x):
    mean = jnp.mean(x, axis=1, keepdims=True)
    centred = x - mean
    scale = lax.rsqrt(jnp.mean(centred * centred, axis=1, keepdims=True) + NORM_EPS)
    return centred * scale, jnp.broadcast_to(scale, (x.shape[0], LANES))


def normalize_back(unit, scale, grad, gain):
    inner = grad * gain
    first = jnp.mean(inner, axis=1, keepdims=True)
    second = jnp.mean(inner * unit, axis=1, keepdims=True)
    out = jnp.concatenate([scale] * (WIDE // LANES), axis=1) * (inner - first - unit * second)
    return out, fold_rows(out), fold_rows(grad * unit), fold_rows(grad)


def gelu_pair(u):
    below = 0.5 + 0.5 * lax.erf(u * math.sqrt(0.5))
    bell = jnp.exp2((-0.5 * math.log2(math.e)) * (u * u))
    return u * below, below + u * (bell * (1.0 / math.sqrt(2.0 * math.pi)))


def head_masks(scale):
    lane = lax.broadcasted_iota(jnp.int32, (1, LANES), 1)
    first = jnp.where(lane < HEAD, scale, 0.0).astype(jnp.bfloat16)
    second = jnp.where(lane < HEAD, 0.0, scale).astype(jnp.bfloat16)
    return first, second


class Sizes:
    def __init__(self, dps):
        self.dps, self.bs = dps, dps // ZS
        self.qkv, self.out, self.up, self.down = (
            3 * WIDE // dps,
            WIDE // dps,
            4 * WIDE // dps,
            WIDE // dps,
        )
        self.lookback = -(-6 * WIDE // (SECT * dps) // VEC_ROWS) * VEC_ROWS
        self.emb = self.lookback + VEC_ROWS
        self.dense = self.out + self.up
        self.wide = 4 * self.down


def qkv_rows(size, w, tile):
    count = QKV_TILE // size.qkv
    return rows_of(w, size.bs, tile * count, count, 0, size.qkv)


def out_rows(size, w):
    return rows_of(w, size.bs, 0, size.dps, 0, size.out)


def up_rows(size, w, tile):
    count = HALF // size.up
    return rows_of(w, size.bs, tile * count, count, size.out, size.up)


def forward_mix(size, w, table, h, mixed, piece):
    columns = slice(piece * QKV_TILE, (piece + 1) * QKV_TILE)
    shift = table[0:1, columns]
    out = dot_nt(h[...], qkv_rows(size, w, piece))
    mixed[:, columns] = by_rows(lambda part: (part + shift).astype(mixed.dtype), out)


def softmax_columns(scores):
    parts = [scores[at : at + STEP] for at in range(0, scores.shape[0], STEP)]
    top = parts[0]
    for part in parts[1:]:
        top = jnp.maximum(top, part)
    top = jnp.max(top, axis=0, keepdims=True)
    parts = [jnp.exp(part - top) for part in parts]
    total = parts[0]
    for part in parts[1:]:
        total = total + part
    scale = 1.0 / jnp.sum(total, axis=0, keepdims=True)
    return jnp.concatenate([(part * scale).astype(jnp.bfloat16) for part in parts], axis=0)


def forward_attend(mixed, probs, attended, pair):
    lane = pair * LANES
    key_rows = mixed[:, WIDE + lane : WIDE + lane + LANES]
    values = mixed[:, 2 * WIDE + lane : 2 * WIDE + lane + LANES].T

    for part in range(2):
        rows = slice(part * HALF, (part + 1) * HALF)
        queries = mixed[rows, lane : lane + LANES]
        joined = []
        for head, mask in enumerate(head_masks(1.0 / math.sqrt(HEAD))):
            weights = softmax_columns(dot_nt(key_rows, queries * mask))
            probs[2 * pair + head, :, rows] = weights
            joined.append(dot_nn(values[head * HEAD : (head + 1) * HEAD], weights))
        joined = jnp.concatenate(joined, axis=0).T
        attended[rows, lane : lane + LANES] = joined.astype(attended.dtype)


def forward_project(size, w, table, h, attended, first, scale, normed):
    out = dot_nt(attended[...], out_rows(size, w))
    for part in range(WIDE // STEP):
        rows = slice(part * STEP, (part + 1) * STEP)
        total = h[rows, :].astype(jnp.float32) + (out[rows] + table[1:2, 0:WIDE])
        unit, scale[rows, :] = normalize(total)
        first[rows, :] = unit
        normed[rows, :] = (
            unit * table[1:2, WIDE : 2 * WIDE] + table[1:2, 2 * WIDE : 3 * WIDE]
        ).astype(normed.dtype)


def forward_up(size, w, table, normed, slope, hidden, piece):
    for j in (2 * piece, 2 * piece + 1):
        columns = slice(j * HALF, (j + 1) * HALF)
        shift = table[2:3, columns]
        upper = dot_nt(normed[...], up_rows(size, w, j))
        for part in range(WIDE // STEP):
            rows = slice(part * STEP, (part + 1) * STEP)
            value, grad = gelu_pair(upper[rows] + shift)
            hidden[rows, columns] = value.astype(hidden.dtype)
            slope[rows, columns] = grad.astype(slope.dtype)


def forward_down(size, w, table, normed, hidden, second, scale, h, piece):
    columns = slice(piece * HALF, (piece + 1) * HALF)
    count = size.dps // 2
    matrix = jnp.concatenate(
        [
            rows_of(w, size.bs, piece * count, count, j * size.down, size.down)
            for j in range(4)
        ],
        axis=1,
    )
    out = dot_nt(hidden[...], matrix)
    shift = table[3:4, columns]
    for part in range(WIDE // STEP):
        rows = slice(part * STEP, (part + 1) * STEP)
        second[rows, columns] = normed[rows, columns].astype(jnp.float32) + (out[rows] + shift)
    if piece == 1:
        for part in range(WIDE // STEP):
            rows = slice(part * STEP, (part + 1) * STEP)
            unit, scale[rows, :] = normalize(second[rows, :])
            second[rows, :] = unit
            h[rows, :] = (
                unit * table[3:4, WIDE : 2 * WIDE] + table[3:4, 2 * WIDE : 3 * WIDE]
            ).astype(h.dtype)


def backward_norm_two(table, dtable, dy, second, scale, dnormed, dlow, dlow_t):
    dtable[...] = jnp.zeros_like(dtable)
    sums = [jnp.zeros((8, WIDE), jnp.float32)] * 3
    for part in range(WIDE // STEP):
        rows = slice(part * STEP, (part + 1) * STEP)
        grad, *found = normalize_back(
            second[rows, :],
            scale[rows, :],
            dy[rows, :].astype(jnp.float32),
            table[3:4, WIDE : 2 * WIDE],
        )
        dnormed[rows, :] = grad
        dlow[rows, :] = grad.astype(dlow.dtype)
        sums = [total + new for total, new in zip(sums, found)]
    for i, total in enumerate(sums):
        dtable[3:4, i * WIDE : (i + 1) * WIDE] = jnp.sum(total, axis=0, keepdims=True)
    dlow_t[...] = dlow[...].T


def backward_down(size, grads, hidden, dlow_t, piece):
    @pl.loop(2 * piece, 2 * piece + 2)
    def _(i):
        start = aligned(i * size.down, 16)
        for half in range(2):
            columns = pl.ds(aligned(i * WIDE, WIDE) + half * HALF, HALF)
            value = dot_nn(dlow_t[...], hidden[:, columns])
            put_rows(grads, size.bs, 0, size.dps, start, size.down, value, 2 * half)


def backward_gelu(size, w, dtable, slope, dlow, dup, piece):
    @pl.loop(2 * piece, 2 * piece + 2)
    def _(i):
        start = aligned(i * size.down, 16)
        for half in range(2):
            columns = pl.ds(aligned(i * WIDE, WIDE) + half * HALF, HALF)
            blocks = (2 * half, 2 * half + 1)
            matrix = rows_of(w, size.bs, 0, size.dps, start, size.down, blocks)
            dhidden = dot_nn(dlow[...], matrix)
            total = jnp.zeros((8, HALF), jnp.float32)
            for part in range(WIDE // STEP):
                rows = slice(part * STEP, (part + 1) * STEP)
                dupper = dhidden[rows] * slope[rows, columns].astype(jnp.float32)
                total = total + fold_rows(dupper)
                dup[rows, columns] = dupper.astype(dup.dtype)
            dtable[2:3, columns] = jnp.sum(total, axis=0, keepdims=True)


def backward_up(size, grads, normed, dup):
    count = HALF // size.up

    @pl.loop(0, 4)
    def _(i):
        for half in range(2):
            columns = pl.ds(aligned(i * WIDE, WIDE) + half * HALF, HALF)
            value = dot_tn(dup[:, columns], normed[...])
            first = (2 * i + half) * count
            put_rows(grads, size.bs, first, count, size.out, size.up, value)


def backward_normed(size, w, dnormed, dup):
    for half in range(2):
        columns = slice(half * HALF, (half + 1) * HALF)
        blocks = (2 * half, 2 * half + 1)
        matrix = rows_of(w, size.bs, 0, size.dps, size.out, size.up, blocks)
        out = dot_nn(dup[...], matrix)
        for part in range(WIDE // STEP):
            rows = slice(part * STEP, (part + 1) * STEP)
            dnormed[rows, columns] = dnormed[rows, columns] + out[rows]


def backward_norm_one(
    size, w, table, grads, dtable, first, scale, attended, dnormed, dlow, dlow_t, delta
):
    sums = [jnp.zeros((8, WIDE), jnp.float32)] * 3
    for part in range(WIDE // STEP):
        rows = slice(part * STEP, (part + 1) * STEP)
        grad, *found = normalize_back(
            first[rows, :], scale[rows, :], dnormed[rows, :], table[1:2, WIDE : 2 * WIDE]
        )
        dnormed[rows, :] = grad
        dlow[rows, :] = grad.astype(dlow.dtype)
        sums = [total + new for total, new in zip(sums, found)]
    for i, total in enumerate(sums):
        dtable[1:2, i * WIDE : (i + 1) * WIDE] = jnp.sum(total, axis=0, keepdims=True)
    dlow_t[...] = dlow[...].T
    for block in (0, 2):
        columns = slice(block * LANES, (block + 2) * LANES)
        value = dot_nn(dlow_t[...], attended[:, columns])
        put_rows(grads, size.bs, 0, size.dps, 0, size.out, value, block)
    grad = dot_nn(dlow[...], out_rows(size, w)).astype(dlow.dtype)
    dlow[...] = grad
    product = grad.astype(jnp.float32) * attended[...].astype(jnp.float32)
    high = product.astype(jnp.bfloat16)
    rest = (product - high.astype(jnp.float32)).astype(jnp.bfloat16)
    head = lax.broadcasted_iota(jnp.int32, delta.shape, 0)
    lane = lax.broadcasted_iota(jnp.int32, delta.shape, 1)
    inside = (lane >= head * HEAD) & (lane < (head + 1) * HEAD)
    inside = jnp.where(inside, 1.0, 0.0).astype(jnp.bfloat16)
    delta[...] = dot_nt(inside, high) + dot_nt(inside, rest)


def backward_attend(mixed, probs, delta, dtable, dlow, dmixed, pair):
    scale = 1.0 / math.sqrt(HEAD)
    lane = pair * LANES
    columns = slice(lane, lane + LANES)
    key_columns = slice(WIDE + lane, WIDE + lane + LANES)
    value_columns = slice(2 * WIDE + lane, 2 * WIDE + lane + LANES)
    keys_t = mixed[:, key_columns].T
    values = mixed[:, value_columns]
    dkeys = jnp.zeros((WIDE, LANES), jnp.float32)
    dvalues = jnp.zeros((WIDE, LANES), jnp.float32)
    for part in range(2):
        rows = slice(part * HALF, (part + 1) * HALF)
        queries = mixed[rows, columns]
        grad_out = dlow[rows, columns]
        dqueries = []
        for head in range(2):
            query = queries * head_masks(scale)[head]
            grad = grad_out * head_masks(1.0)[head]
            at = 2 * pair + head
            weights = probs[at, :, rows]
            less = delta[at : at + 1, rows]
            dprobs = dot_nt(values, grad)
            dscores = by_rows(
                lambda p, dp: (p.astype(jnp.float32) * (dp - less)).astype(jnp.bfloat16),
                weights,
                dprobs,
            )
            dvalues = dvalues + dot_nn(weights, grad)
            dkeys = dkeys + dot_nn(dscores, query)
            dqueries.append(dot_nn(keys_t[head * HEAD : (head + 1) * HEAD], dscores))
        dquery = jnp.concatenate(dqueries, axis=0).T * scale
        dtable[0:1, columns] += jnp.sum(dquery, axis=0, keepdims=True)
        dmixed[rows, columns] = dquery.astype(dmixed.dtype)
    dmixed[:, key_columns] = dkeys.astype(dmixed.dtype)
    dmixed[:, value_columns] = dvalues.astype(dmixed.dtype)
    dtable[0:1, value_columns] = jnp.sum(dvalues, axis=0, keepdims=True)


def backward_mix(size, grads, h, dmixed, piece):
    count = QKV_TILE // size.qkv
    grad = dmixed[:, piece * QKV_TILE : (piece + 1) * QKV_TILE]
    put_rows(grads, size.bs, piece * count, count, 0, size.qkv, dot_tn(grad, h[...]))


def backward_input(size, w, dnormed, dmixed, dy):
    for half in range(2):
        columns = slice(half * HALF, (half + 1) * HALF)
        blocks = (2 * half, 2 * half + 1)
        matrix = rows_of(w, size.bs, 0, size.dps, 0, size.qkv, blocks)
        out = dot_nn(dmixed[...], matrix)
        for part in range(WIDE // STEP):
            rows = slice(part * STEP, (part + 1) * STEP)
            dy[rows, columns] = (dnormed[rows, columns] + out[rows]).astype(dy.dtype)


WINDOW = 384


def group_rows(group):
    rows = lax.broadcasted_iota(jnp.int32, (16, LANES), 0)
    return jnp.where(rows == group, 1.0, 0.0).astype(jnp.bfloat16)


def pack_mix(piece, qkv):
    for lb in range(SECT):
        piece[lb] = qkv[:, lb * LANES : (lb + 1) * LANES].astype(piece.dtype)


def pack_up(piece, out, up):
    rows = out.shape[0]
    for lb in range(SECT):
        lanes = slice(lb * LANES, (lb + 1) * LANES)
        piece[lb, :rows] = out[:, lanes].astype(piece.dtype)
        piece[lb, rows:] = up[:, lanes].astype(piece.dtype)


def pack_down(piece, down):
    rows = down.shape[0]
    for lb in range(SECT):
        for j in range(4):
            start = j * WIDE + lb * LANES
            piece[lb, j * rows : (j + 1) * rows] = down[:, start : start + LANES].astype(piece.dtype)


def pack_embedding(piece, weight, shift, gains, biases, square, block):
    n = weight.shape[0]
    square[...] = jnp.zeros_like(square)
    square[:GROUPS, :n] = shift[...]

    def ending(part, width):
        return jnp.concatenate([jnp.zeros((n, width - part.shape[1]), part.dtype), part], axis=1)

    third = ending(weight[:, L1 + L2 :], 3 * LANES)
    second = ending(weight[:, L1 : L1 + L2], 2 * LANES)
    blocks = [third[:, :LANES] + square[...].T[:n]]
    blocks += [third[:, LANES : 2 * LANES], third[:, 2 * LANES :]]
    blocks += [second[:, :LANES], second[:, LANES:], ending(weight[:, :L1], LANES)]
    rows = piece.shape[1] - VEC_ROWS
    if SECT * rows > 6 * n:
        blocks.append(jnp.zeros((SECT * rows - 6 * n, LANES), jnp.float32))
    flat = jnp.concatenate(blocks, axis=0).astype(piece.dtype)
    for lb in range(SECT):
        piece[lb, :rows] = flat[lb * rows : (lb + 1) * rows]
    line = jnp.concatenate([gains[...], biases[...]], axis=1)
    lines = [[line[:, at : at + LANES]] for at in range(0, line.shape[1], LANES)]
    piece[block, rows:] = rows_tile(lines).astype(piece.dtype)


def expand(series, group, x):
    empty = jnp.zeros((WINDOW - series.shape[0], series.shape[1]), series.dtype)
    x[:, :WINDOW] = jnp.concatenate([empty, series[...]], axis=0).T
    lane = lax.broadcasted_iota(jnp.int32, (x.shape[0], LANES), 1)
    x[:, WINDOW:] = jnp.where(lane == group, 1.0, 0.0).astype(x.dtype)


def embed(size, emb, pick, x, wsel, h):
    n = WIDE // size.dps
    flat = []
    for d in range(size.dps):
        place = (d // size.bs, d % size.bs, slice(0, size.lookback), slice(None))
        flat.append(jnp.concatenate([emb[(lb,) + place] for lb in range(SECT)], axis=0))
    blocks = [
        jnp.concatenate([rows[j * n : (j + 1) * n] for rows in flat], axis=0) for j in range(6)
    ]
    long, middle, short = (pick[g : g + 1, :] for g in (2, 1, 0))
    wide = jnp.concatenate(
        [
            blocks[0] * long,
            blocks[1] * long + blocks[3] * middle,
            blocks[2] * long + blocks[4] * middle + blocks[5] * short,
        ],
        axis=1,
    )
    wsel[...] = wide.T
    h[...] = dot_nt(x[...], jnp.concatenate([wide, blocks[0]], axis=1)).astype(h.dtype)


def embed_back(size, pick, x, wsel, dh, tables, grads, series_grad):
    history = series_grad.shape[0]
    series_grad[...] = dot_nt(wsel[...], dh[...])[WINDOW - history :]
    sums = dot_tn(dh[...], x[...])
    long, middle, short = (pick[g : g + 1, :].astype(jnp.float32) for g in (2, 1, 0))
    parts = [sums[:, i * LANES : (i + 1) * LANES] for i in range(4)]
    parts = [
        parts[0] * long + parts[3],
        parts[1] * long,
        parts[2] * long,
        parts[1] * middle,
        parts[2] * middle,
        parts[2] * short,
    ]
    rows = WIDE // (SECT * size.dps)
    spare = size.lookback - 6 * rows
    for pipe in range(SECT):
        block = (pipe % 2) * 2 + pipe // 2
        for dp in range(size.dps):
            start = (pipe * size.dps + dp) * rows
            pieces = [part[start : start + rows] for part in parts]
            if spare:
                pieces.append(jnp.zeros((spare, LANES), jnp.float32))
            pieces.append(vector_tile(tables.at[pipe], size.dps, dp))
            piece = jnp.concatenate(pieces, axis=0)
            grads[block, dp // size.bs, dp % size.bs] = piece.astype(grads.dtype)


def saved_shapes():
    low, wide = jnp.bfloat16, jnp.float32
    return [
        ((WIDE, WIDE), low),
        ((WIDE, 3 * WIDE), low),
        ((2 * SECT, WIDE, WIDE), low),
        ((WIDE, WIDE), low),
        ((WIDE, WIDE), wide),
        ((WIDE, WIDE), low),
        ((WIDE, 4 * WIDE), low),
        ((WIDE, 4 * WIDE), low),
        ((WIDE, WIDE), wide),
        ((SECT, 4 * WIDE), wide),
        ((WIDE, LANES), wide),
        ((WIDE, LANES), wide),
    ]


def chunk_shape(size, rows):
    return (SECT, ZS, size.bs, rows, LANES)


HALVES = (2, 2, 2, 2)
CROSS = (2,)


def follow(plan, section, act, compute):
    seen = {}
    for step in plan:
        if len(step) == 1:
            piece = seen.get(step[0], 0)
            seen[step[0]] = piece + 1
            compute(step[0], piece)
            continue
        op, kind, offset = step
        where = section + offset
        if isinstance(where, int):
            if 0 <= where < SECT:
                act(op, kind, where)
        elif offset == 0:
            act(op, kind, where)
        else:
            inside = where < SECT if offset > 0 else where >= 0

            @pl.when(inside)
            def _():
                act(op, kind, where)


def forward_kernel(dps, groups, *refs):
    size = Sizes(dps)
    given, refs = refs[:9], refs[9:]
    out, wholes, wsel, x, refs = refs[0], refs[1:5], refs[5], refs[6], refs[7:]
    kept, local, refs = refs[:12], refs[12:24], refs[24:]
    buffers, refs = refs[:4], refs[4:]
    pieces, held, refs = refs[:4], refs[4:13], refs[13:]
    emb_rows, pick, refs = refs[0], refs[1], refs[2:]
    given_sem, w_sem, kept_sem, own_sem, p_send, p_recv, send, recv = refs
    h, mixed, probs, attended, first, normed, slope, hidden, second, table, scale_1, scale_2 = local
    at = Place(dps)

    own = [
        pltpu.make_async_copy(
            pieces[kind].at[at.block],
            wholes[kind].at[at.pipe, at.block, at.z, at.b]
            if kind < EMB
            else wholes[kind].at[at.block, at.z, at.b],
            own_sem.at[kind],
        )
        for kind in range(4)
    ]
    def split(kind, back):
        copies = []
        for k in range(1, SECT):
            if back:
                region = wholes[kind].at[at.pipe_at(SECT - k), at.block, at.z, at.b]
                src = region
            else:
                block = at.blocks[k]
                region = wholes[kind].at[at.pipe, block, at.z, at.b]
                src = pieces[kind].at[block]
            sems = p_send.at[kind, k - 1], p_recv.at[kind, k - 1]
            copies.append(remote(src, region, *sems, (at.pipe_at(k), at.dp)))
        return copies

    def chunk(kind, section):
        if kind == EMB:
            return Spread(at, wholes[kind], send.at[3 * SECT], recv.at[3 * SECT])
        number = 3 * section + kind
        sort = SpreadCross if kind in CROSS else Spread
        return sort(at, wholes[kind].at[section], send.at[number], recv.at[number], HALVES[kind])

    def load(kind, section, core):
        blocks = pl.ds(core * 2, 2)
        src, dst = wholes[kind], buffers[kind]
        if kind != EMB:
            src, dst = src.at[section], dst.at[section % 2]
        sem = w_sem.at[kind, section % 2, core]
        return pltpu.make_async_copy(src.at[blocks], dst.at[blocks], sem)

    def loaded(kind, section):
        load(kind, section, at.c).wait()
        load(kind, section, 1 - at.c).wait()

    arrived = []

    def act(op, kind, section):
        if op == 0:
            if kind not in arrived:
                arrived.append(kind)
                own[kind].wait()
                if kind == EMB:
                    chunk(kind, section).start(0)
                    return
                for copy in split(kind, True):
                    copy.wait_recv()
                for copy in split(kind, False):
                    copy.wait_send()
                if kind == 0:
                    copies_start(split(1, False))
                    copies_start(split(2, False))
            chunk(kind, section).start(0)
        elif op < 4:
            chunk(kind, section).move(op - 1)
            if op == 1 and kind == EMB:
                gets[0].wait()
                expand(series, groups[0], x)
            if op == 3:
                load(kind, section, at.c).start(priority=1)
        else:
            chunk(kind, section).land(3)
            load(kind, section, 1 - at.c).start(priority=1)

    def saves(section, early):
        which = (1, 2, 3, 4, 5, 9, 10) if early else (6, 7, 8, 11)
        return [
            pltpu.make_async_copy(local[i], kept[i].at[section], kept_sem.at[i]) for i in which
        ]

    series, embed_weight, embed_bias, qkv, out_w, up_w, down_w, gains, biases = held
    gets = copies_of(zip(given, held), given_sem)
    for i in (3, 7, 8, 1, 2, 4, 5, 6, 0):
        gets[i].start(priority=1)
    pick[...] = group_rows(groups[0])
    at.greet()
    gets[3].wait()
    pack_mix(pieces[0], qkv)
    own[0].start(priority=1)
    at.met()
    copies_start(split(0, False))
    copies_wait(gets[1:3] + gets[7:9])
    pack_embedding(
        pieces[EMB], embed_weight, embed_bias, gains, biases, emb_rows, at.block
    )
    own[EMB].start(priority=1)
    copies_wait(gets[4:7])
    pack_up(pieces[1], out_w, up_w)
    own[1].start(priority=1)
    pack_down(pieces[2], down_w)
    own[2].start(priority=1)
    table[...] = jnp.zeros_like(table)

    def before(name, piece):
        loaded(EMB, 0)
        embed(size, buffers[EMB], pick, x, wsel, h)

    follow(FORWARD_START, 0, act, before)

    @pl.loop(0, SECT)
    def _(section):
        att, up, down = (ref.at[section % 2] for ref in buffers[:3])
        keep_h = pltpu.make_async_copy(h, kept[0].at[section], kept_sem.at[0])

        def compute(name, piece):
            if name == "mix":
                if piece == 0:

                    @pl.when(section > 0)
                    def _():
                        copies_wait(saves(section - 1, True))

                    keep_h.start(priority=1)
                    loaded(0, section)
                    block = section % 2 * 2 + section // 2
                    read_vectors(buffers[EMB], table, size.bs, size.lookback, block)
                forward_mix(size, att, table, h, mixed, piece)
            elif name == "attend":
                forward_attend(mixed, probs, attended, piece)
            elif name == "project":
                loaded(1, section)
                forward_project(size, up, table, h, attended, first, scale_1, normed)
                copies_begin(saves(section, True))
            elif name == "up":
                if piece == 0:

                    @pl.when(section > 0)
                    def _():
                        copies_wait(saves(section - 1, False))

                forward_up(size, up, table, normed, slope, hidden, piece)
            else:
                if piece == 0:
                    loaded(2, section)
                    keep_h.wait()
                forward_down(size, down, table, normed, hidden, second, scale_2, h, piece)
                if piece == 1:
                    copies_begin(saves(section, False))

        follow(FORWARD_PERIOD, section, act, compute)

    out[...] = h[...]
    copies_wait(saves(SECT - 1, True))
    copies_wait(saves(SECT - 1, False))


def copies_of(pairs, sems):
    return [pltpu.make_async_copy(src, dst, sems.at[i]) for i, (src, dst) in enumerate(pairs)]


def forward_all(groups, given, dps):
    size = Sizes(dps)
    low, wide = jnp.bfloat16, jnp.float32
    shapes = saved_shapes()
    rows = (size.qkv, size.dense, size.wide, size.emb)
    chunks = [chunk_shape(size, count) for count in rows]
    anywhere = pl.BlockSpec(memory_space=pl.ANY)
    inside = pl.BlockSpec(memory_space=pltpu.VMEM)
    outs = [((WIDE, WIDE), low)]
    outs += [((SECT,) + shape, low) for shape in chunks[:3]] + [(chunks[3], low)]
    outs += [((WINDOW, WIDE), low), ((WIDE, WIDE), low)]
    outs += [((SECT,) + shape, dtype) for shape, dtype in shapes]
    scratch = shapes + [((2,) + shape, low) for shape in chunks[:3]] + [(chunks[3], low)]
    scratch += [((SECT, count, LANES), low) for count in rows]
    scratch += [(array.shape, array.dtype) for array in given]
    scratch += [((LANES, LANES), wide), ((16, LANES), low)]
    slots = max(Spread.slots(size.bs), SpreadCross.slots(size.bs))
    dma = pltpu.SemaphoreType.DMA
    return pl.pallas_call(
        partial(forward_kernel, dps),
        out_shape=[jax.ShapeDtypeStruct(shape, dtype) for shape, dtype in outs],
        in_specs=[pl.BlockSpec(memory_space=pltpu.SMEM)] + [anywhere] * len(given),
        out_specs=[inside] + [anywhere] * 4 + [inside] * 2 + [anywhere] * len(shapes),
        scratch_shapes=[pltpu.VMEM(shape, dtype) for shape, dtype in scratch]
        + [
            dma((len(given),)),
            dma((4, 2, 2)),
            dma((len(shapes),)),
            dma((4,)),
            dma((3, SECT - 1)),
            dma((3, SECT - 1)),
            dma((1 + 3 * SECT, slots)),
            dma((1 + 3 * SECT, slots)),
        ],
        compiler_params=pltpu.CompilerParams(
            collective_id=0, has_side_effects=True, vmem_limit_bytes=60 * 1024 * 1024
        ),
        name="gather_forward",
    )(groups, *given)


FETCHES = {
    ("norm2", 0): (("second", "scale_2"), ("second", "scale_2")),
    ("down", 0): (("hidden",), ()),
    ("down", 1): ((), ("hidden",)),
    ("gelu", 0): (("slope", 2), ()),
    ("gelu", 1): ((), ("slope", 2)),
    ("up", 0): (("normed",), ("normed",)),
    ("normed", 0): ((1,), ()),
    ("norm1", 0): (("first", "scale_1", "attended"), ("first", "scale_1", "attended", 1)),
    ("attend", 0): (("mixed", "probs"), ()),
    ("attend", 3): ((), ("mixed", "probs")),
    ("mix", 0): (("h",), ()),
    ("mix", 1): ((), ("h",)),
    ("input", 0): ((0,), (0,)),
}


def backward_kernel(dps, groups, att, up, down, cotangent, x_in, wsel_in, *refs):
    size = Sizes(dps)
    kept, refs = refs[:12], refs[12:]
    series_grad, outs, refs = refs[0], refs[1:5], refs[5:]
    local, refs = refs[:11], refs[11:]
    tables, w_att, w_up, w_down, dtables, dy, dnormed, dlow, dlow_t, dmixed, dup = refs[:11]
    x, wsel, pick, delta, refs = *refs[11:15], refs[15:]
    kinds = []
    for kind in range(4):
        count = 6 if kind in CROSS else 5
        kinds.append(refs[:4] + (refs[4 : 4 + count],))
        refs = refs[4 + count :]
    w_sem, kept_sem, table_sem, late_sem, out_sem, p_send, p_recv, send, recv, credit = refs
    h, mixed, probs, attended, first, normed, slope, hidden, second, scale_1, scale_2 = local
    at = Place(dps)
    last = SECT - 1

    def weights(kind, section):
        src, dst = ((att, w_att), (up, w_up), (down, w_down))[kind]
        return pltpu.make_async_copy(src.at[section], dst, w_sem.at[kind])

    names = ("h", "mixed", "probs", "attended", "first", "normed", "slope", "hidden", "second")
    names += ("table", "scale_1", "scale_2")
    held = dict(zip(names[:9] + names[10:], local))

    def fetches(section, *wanted):
        found = []
        for name in wanted:
            if isinstance(name, int):
                found.append(weights(name, section))
            else:
                i = names.index(name)
                dst = held[name]
                found.append(pltpu.make_async_copy(kept[i].at[section], dst, kept_sem.at[i]))
        return found

    def chunk(kind, i):
        grads, totals, finals, landing, bufs = kinds[kind]
        sort = FoldCross if kind in CROSS else Fold
        refs = (grads, totals.at[i % 2], landing, bufs, finals.at[i])
        return sort(at, *refs, send.at[kind], recv.at[kind], credit.at[kind], HALVES[kind])

    def hand_over(kind, i):
        landing = outs[kind].at[at.block]
        final = kinds[kind][2].at[i]
        return (
            pltpu.make_async_copy(final, landing, out_sem.at[kind]),
            remote(final, landing, p_send.at[kind, i], p_recv.at[kind, at.pipe], (last - i, at.dp)),
        )

    def act(op, kind, i):
        again, more = (False, False) if kind == EMB else (i > 0, i < last)
        if op == 0:
            chunk(kind, i).start(0, again)
        elif op < 4:
            chunk(kind, i).move(op - 1, again, more)
        else:
            chunk(kind, i).land(3, more)
            if kind == EMB:
                outs[kind][...] = kinds[kind][2][0]
            else:
                here, away = hand_over(kind, i)

                @pl.when(at.pipe == last - i)
                def _():
                    here.start(priority=1)

                @pl.when(at.pipe != last - i)
                def _():
                    away.start()

    at.greet()
    get_tables = pltpu.make_async_copy(kept[9], tables, table_sem)
    late = copies_of(((cotangent, dy), (x_in, x), (wsel_in, wsel)), late_sem)
    copies_begin([late[0], get_tables] + fetches(last, "second", "scale_2", "hidden"))
    copies_begin(fetches(last, "slope", 2, "normed", 1, "first", "scale_1", "attended"))
    copies_begin(fetches(last, "mixed", "probs", "h", 0) + late[1:])
    pick[...] = group_rows(groups[0])
    copies_wait([late[0], get_tables])

    @pl.loop(0, SECT)
    def _(i):
        section = last - i
        table, dtable = tables.at[section], dtables.at[section]

        def compute(name, piece):
            need, free = FETCHES.get((name, piece), ((), ()))
            copies_wait(fetches(section, *need))
            if name == "norm2":
                backward_norm_two(table, dtable, dy, second, scale_2, dnormed, dlow, dlow_t)
                pl.when(i == 0)(at.met)
            elif name == "down":
                backward_down(size, kinds[2][0], hidden, dlow_t, piece)
            elif name == "gelu":
                backward_gelu(size, w_down, dtable, slope, dlow, dup, piece)
            elif name == "up":
                backward_up(size, kinds[1][0], normed, dup)
            elif name == "normed":
                backward_normed(size, w_up, dnormed, dup)
            elif name == "norm1":
                backward_norm_one(
                    size,
                    w_up,
                    table,
                    kinds[1][0],
                    dtable,
                    first,
                    scale_1,
                    attended,
                    dnormed,
                    dlow,
                    dlow_t,
                    delta,
                )
            elif name == "attend":
                backward_attend(mixed, probs, delta, dtable, dlow, dmixed, piece)
            elif name == "mix":
                backward_mix(size, kinds[0][0], h, dmixed, piece)
            else:
                backward_input(size, w_att, dnormed, dmixed, dy)
            if free:

                @pl.when(section > 0)
                def _():
                    copies_begin(fetches(section - 1, *free))

        follow(BACKWARD_PERIOD, i, act, compute)

    def after(name, piece):
        copies_wait(late[1:])
        embed_back(size, pick, x, wsel, dy, dtables, kinds[EMB][0], series_grad)

    follow(BACKWARD_END, 0, act, after)

    for kind in range(3):
        for i in range(SECT):
            here, away = hand_over(kind, i)

            @pl.when(at.pipe == last - i)
            def _():
                here.wait()

            @pl.when(at.pipe != last - i)
            def _():
                away.wait_send()

        for k in range(1, SECT):
            other = at.pipe_at(k)
            landing = outs[kind].at[at.blocks[k]]
            sems = p_send.at[kind, 0], p_recv.at[kind, other]
            remote(landing, landing, *sems, (other, at.dp)).wait_recv()


def backward_all(groups, weights, cotangent, x, wsel, kept, history, dps):
    size = Sizes(dps)
    low, wide = jnp.bfloat16, jnp.float32
    anywhere = pl.BlockSpec(memory_space=pl.ANY)
    inside = pl.BlockSpec(memory_space=pltpu.VMEM)
    shapes = saved_shapes()
    kind_rows = (size.qkv, size.dense, size.wide, size.emb)
    scratch = shapes[:9] + shapes[10:] + [((SECT,) + shapes[9][0], wide)]
    scratch += [(chunk_shape(size, rows), low) for rows in kind_rows[:3]]
    scratch += [
        ((SECT,) + shapes[9][0], wide),
        ((WIDE, WIDE), low),
        ((WIDE, WIDE), wide),
        ((WIDE, WIDE), low),
        ((WIDE, WIDE), low),
        ((WIDE, 3 * WIDE), low),
        ((WIDE, 4 * WIDE), low),
        ((WIDE, WIDE), low),
        ((WINDOW, WIDE), low),
        ((16, LANES), low),
        ((16, WIDE), wide),
    ]
    for kind, rows in enumerate(kind_rows):
        sets, results = (1, 1) if kind == EMB else (2, SECT)
        scratch += [
            (chunk_shape(size, rows), low),
            ((sets, 2, ZS, size.bs, rows, LANES), low),
            ((results, rows, LANES), low),
            ((2, ZS, size.bs, rows, LANES), low),
        ]
        sort = FoldCross if kind in CROSS else Fold
        scratch += [(shape, low) for shape in sort.buffers(size.bs, rows, HALVES[kind])]
    slots = max(Fold.slots(size.bs), FoldCross.slots(size.bs))
    dma = pltpu.SemaphoreType.DMA
    return pl.pallas_call(
        partial(backward_kernel, dps),
        out_shape=[jax.ShapeDtypeStruct((history, WIDE), wide)]
        + [jax.ShapeDtypeStruct((SECT, rows, LANES), low) for rows in kind_rows[:3]]
        + [jax.ShapeDtypeStruct((size.emb, LANES), low)],
        in_specs=[pl.BlockSpec(memory_space=pltpu.SMEM)] + [anywhere] * (6 + len(kept)),
        out_specs=[inside] + [anywhere] * 3 + [inside],
        scratch_shapes=[pltpu.VMEM(shape, dtype) for shape, dtype in scratch]
        + [
            dma((3,)),
            dma((12,)),
            dma(()),
            dma((3,)),
            dma((3,)),
            dma((3, SECT)),
            dma((3, SECT)),
            dma((4, slots)),
            dma((4, slots)),
            pltpu.SemaphoreType.REGULAR((4, slots)),
        ],
        compiler_params=pltpu.CompilerParams(
            collective_id=1, has_side_effects=True, vmem_limit_bytes=60 * 1024 * 1024
        ),
        name="backward_fold",
    )(groups, *weights, cotangent, x, wsel, *kept)


def finish_kernel(dps, n_gains, n_biases, *refs):
    size = Sizes(dps)
    given, refs = refs[:6], refs[6:]
    block_out, series_out, embed_w, embed_b, qkv, out, up_out, down_out, gains, biases = refs[:10]
    att, up, down, emb, sems = refs[10:]
    copies = copies_of(zip(given, (att, up, down, emb, block_out, series_out)), sems)
    copies_start(copies)
    copies_wait(copies[:4])
    for lb in range(SECT):
        lanes = slice(lb * LANES, (lb + 1) * LANES)
        qkv[:, lanes] = att[lb].astype(jnp.float32)
        out[:, lanes] = up[lb, : size.out].astype(jnp.float32)
        up_out[:, lanes] = up[lb, size.out :].astype(jnp.float32)
        for j in range(4):
            rows = slice(j * size.down, (j + 1) * size.down)
            start = j * WIDE + lb * LANES
            down_out[:, start : start + LANES] = down[lb, rows].astype(jnp.float32)
    vectors = emb[size.lookback :].astype(jnp.float32)
    count = -(-(n_gains + n_biases) // LANES)
    flat = jnp.concatenate([vectors[row : row + 1] for row in range(count)], axis=1)
    gains[...] = flat[:, :n_gains]
    biases[...] = flat[:, n_gains : n_gains + n_biases]
    rows = WIDE // (SECT * dps)
    packed = emb[: size.lookback].astype(jnp.float32)
    packed = [packed[i * rows : (i + 1) * rows] for i in range(6)]
    square = jnp.concatenate([packed[0], jnp.zeros((LANES - rows, LANES), jnp.float32)], axis=0)
    embed_b[...] = square.T[:GROUPS, :rows]
    packed = jnp.concatenate(packed, axis=1)
    ends = ((6 * LANES, L1), (5 * LANES, L2), (3 * LANES, L3))
    embed_w[...] = jnp.concatenate([packed[:, end - span : end] for end, span in ends], axis=1)
    copies_wait(copies[4:])


def finish_all(sums, block, series, n_gains, n_biases, dps):
    size = Sizes(dps)
    wide = jnp.float32
    columns = WIDE // (SECT * dps)
    outs = [
        (block.shape, block.dtype),
        (series.shape, wide),
        ((columns, L1 + L2 + L3), wide),
        ((GROUPS, columns), wide),
        ((size.qkv, WIDE), wide),
        ((size.out, WIDE), wide),
        ((size.up, WIDE), wide),
        ((size.down, 4 * WIDE), wide),
        ((1, n_gains), wide),
        ((1, n_biases), wide),
    ]
    anywhere = pl.BlockSpec(memory_space=pl.ANY)
    inside = pl.BlockSpec(memory_space=pltpu.VMEM)
    return pl.pallas_call(
        partial(finish_kernel, dps, n_gains, n_biases),
        out_shape=[jax.ShapeDtypeStruct(shape, dtype) for shape, dtype in outs],
        in_specs=[anywhere] * 6,
        out_specs=[inside] * 10,
        scratch_shapes=[pltpu.VMEM(array.shape, array.dtype) for array in sums]
        + [pltpu.SemaphoreType.DMA((6,))],
        compiler_params=pltpu.CompilerParams(vmem_limit_bytes=60 * 1024 * 1024),
        name="finish",
    )(*sums, block, series)


def per_device(
    series,
    groups,
    cotangent,
    embed_weight,
    embed_bias,
    qkv_weight,
    out_weight,
    up_weight,
    down_weight,
    gains,
    biases,
):
    dps = lax.axis_size("dp")
    given = (
        series[0],
        embed_weight.T,
        embed_bias,
        qkv_weight[0],
        out_weight[0],
        up_weight[0],
        down_weight[0],
        gains,
        biases,
    )
    block_output, att, up, down, _, wsel, x, *kept = forward_all(groups, given, dps)
    series_grad, *sums = backward_all(
        groups, (att, up, down), cotangent[0], x, wsel, kept, series.shape[1], dps
    )
    outs = finish_all(sums, block_output, series_grad, gains.shape[1], biases.shape[1], dps)
    block_output, series_grad, embed_w, embed_b, qkv, out, up, down, gain_sum, bias_sum = outs
    return (
        block_output[None],
        series_grad[None],
        embed_w.T,
        embed_b,
        qkv[None],
        out[None],
        up[None],
        down[None],
        gain_sum,
        bias_sum,
    )


def solution(mesh):
    return jax.shard_map(
        per_device,
        mesh=mesh,
        in_specs=(
            P(("pipe", "dp"), None, None),
            P(("pipe", "dp")),
            P(("pipe", "dp"), None, None),
            P(None, "dp"),
            P(None, "dp"),
            P("pipe", "dp", None),
            P("pipe", "dp", None),
            P("pipe", "dp", None),
            P("pipe", "dp", None),
            P("pipe", "dp"),
            P("pipe", "dp"),
        ),
        out_specs=(
            P(("pipe", "dp"), None, None),
            P(("pipe", "dp"), None, None),
            P(None, ("pipe", "dp")),
            P(None, ("pipe", "dp")),
            P("pipe", "dp", None),
            P("pipe", "dp", None),
            P("pipe", "dp", None),
            P("pipe", "dp", None),
            P("pipe", "dp"),
            P("pipe", "dp"),
        ),
        check_vma=False,
    )
```

```python
from functools import partial
import math

import jax
import jax.numpy as jnp
from jax import lax
from jax.experimental import pallas as pl
from jax.experimental.pallas import tpu as pltpu
from jax.sharding import PartitionSpec as P

HEAD = 64
L1 = 96
L2 = 192
L3 = 336
GROUPS = 3


NORM_EPS = 1e-05


MESH = pl.DeviceIdType.MESH
LANES = 128
ZS = 4
SECT = 4
EMB = 3


class Place:
    def __init__(self, dps):
        self.bs = bs = dps // ZS
        pipe = lax.axis_index("pipe")
        dp = lax.axis_index("dp")
        self.pipe, self.dp = pipe, dp
        self.x, self.c = x, c = lax.div(pipe, 2), lax.rem(pipe, 2)
        self.z, self.b = z, b = lax.div(dp, bs), lax.rem(dp, bs)
        self.block = c * 2 + x
        self.other_block = c * 2 + 1 - x
        self.x_peer = ((1 - x) * 2 + c, dp)
        self.core_peer = (x * 2 + 1 - c, dp)
        self.pipes = [lax.rem(pipe + k, SECT) for k in range(SECT)]
        self.blocks = [self.block_of(other) for other in self.pipes]
        self.zs = [lax.rem(z + k, ZS) for k in range(ZS)]
        self.bees = [lax.rem(b + k, bs) for k in range(bs)]
        self.z_peers = [(pipe, other * bs + b) for other in self.zs]
        self.b_peers = [(pipe, z * bs + other) for other in self.bees]

    def block_of(self, pipe):
        return lax.rem(pipe, 2) * 2 + lax.div(pipe, 2)

    def pipe_at(self, step):
        return self.pipes[step % SECT]

    def z_at(self, step):
        return self.zs[step % ZS]

    def b_at(self, step):
        return self.bees[step % self.bs]

    def z_peer(self, step):
        return self.z_peers[step % ZS]

    def b_peer(self, step):
        return self.b_peers[step % self.bs]

    def greet(self):
        barrier = pltpu.get_barrier_semaphore()
        peers = [(self.pipe_at(k), self.dp) for k in range(1, SECT)]
        peers += [self.z_peer(k) for k in range(1, ZS)]
        peers += [self.b_peer(k) for k in range(1, self.bs)]
        for peer in peers:
            pl.semaphore_signal(barrier, inc=1, device_id=peer, device_id_type=MESH)

    def met(self):
        pl.semaphore_wait(pltpu.get_barrier_semaphore(), SECT + ZS + self.bs - 3)


def remote(src, dst, send, recv, peer):
    return pltpu.make_async_remote_copy(
        src_ref=src, dst_ref=dst, send_sem=send, recv_sem=recv, device_id=peer, device_id_type=MESH
    )


FORWARD_START = (
    (0, 3, 0),
    (0, 0, 0),
    (0, 2, 0),
    (1, 3, 0),
    (1, 0, 0),
    (0, 1, 0),
    (2, 3, 0),
    (2, 0, 0),
    (0, 0, 1),
    (1, 1, 0),
    (1, 2, 0),
    (3, 3, 0),
    (0, 2, 1),
    (1, 0, 1),
    (2, 1, 0),
    (4, 3, 0),
    (3, 0, 0),
    ("embed",),
    (4, 0, 0),
)
FORWARD_PERIOD = (
    ("mix",),
    (0, 1, 1),
    (2, 0, 1),
    ("mix",),
    ("attend",),
    (3, 1, 0),
    ("attend",),
    (2, 2, 0),
    ("attend",),
    (0, 0, 2),
    (4, 1, 0),
    ("attend",),
    ("project",),
    (1, 1, 1),
    ("up",),
    (1, 2, 1),
    (0, 2, 2),
    (3, 2, 0),
    ("up",),
    (1, 0, 2),
    ("up",),
    (2, 1, 1),
    (3, 0, 1),
    (4, 2, 0),
    ("up",),
    ("down",),
    (4, 0, 1),
    ("down",),
)
BACKWARD_PERIOD = (
    ("norm2",),
    (2, 2, -1),
    ("down",),
    ("down",),
    (0, 2, 0),
    (1, 0, -1),
    ("gelu",),
    ("gelu",),
    ("up",),
    (2, 1, -1),
    ("normed",),
    ("norm1",),
    (2, 0, -1),
    (0, 1, 0),
    (4, 2, -2),
    (1, 2, 0),
    ("attend",),
    ("attend",),
    (4, 1, -2),
    (3, 1, -1),
    ("attend",),
    ("attend",),
    ("mix",),
    (1, 1, 0),
    ("mix",),
    (0, 0, 0),
    (4, 0, -2),
    (3, 0, -1),
    (3, 2, -1),
    ("input",),
)
BACKWARD_END = (
    (2, 2, 3),
    ("embed",),
    (1, 0, 3),
    (0, 3, 0),
    (2, 1, 3),
    (2, 0, 3),
    (4, 2, 2),
    (4, 1, 2),
    (3, 1, 3),
    (4, 0, 2),
    (1, 3, 0),
    (3, 0, 3),
    (3, 2, 3),
    (2, 3, 0),
    (4, 2, 3),
    (3, 3, 0),
    (4, 1, 3),
    (4, 0, 3),
    (4, 3, 0),
)


def copies_start(copies):
    for copy in copies:
        copy.start()


def copies_begin(copies):
    for copy in copies:
        copy.start(priority=1)


def copies_wait(copies):
    for copy in copies:
        copy.wait()


class Spread:
    def __init__(self, at, out, send, recv, half=ZS // 2):
        self.at, self.out, self.send, self.recv = at, out, send, recv
        nb = at.bs - 1
        self.slot_z = 0
        self.slot_b1 = ZS - 1
        self.slot_x1 = self.slot_b1 + nb
        self.slot_x2 = self.slot_x1 + 1
        self.slot_b2 = self.slot_x2 + 1
        self.slot_c = self.slot_b2 + nb
        self.half = half

    @staticmethod
    def slots(bs):
        return ZS - 1 + 2 * (bs - 1) + 3

    def copy(self, region, slot, peer):
        return remote(region, region, self.send.at[slot], self.recv.at[slot], peer)

    def copies(self, stage, back):
        at, out, half = self.at, self.out, self.half
        rest = pl.ds(half, ZS - half)
        x_block = at.other_block if back else at.block
        if stage == 0:
            return [
                self.copy(
                    out.at[at.block, at.z_at(ZS - k) if back else at.z, at.b],
                    self.slot_z + k - 1,
                    at.z_peer(k),
                )
                for k in range(1, ZS)
            ]
        if stage == 3:
            core = 1 - at.c if back else at.c
            return [self.copy(out.at[pl.ds(core * 2, 2)], self.slot_c, at.core_peer)]
        copies = []
        for k in range(1, at.bs):
            b = at.b_at(at.bs - k) if back else at.b
            if stage == 1:
                region, slot = out.at[at.block, pl.ds(0, half), b], self.slot_b1
            else:
                region, slot = out.at[pl.ds(at.c * 2, 2), rest, b], self.slot_b2
            copies.append(self.copy(region, slot + k - 1, at.b_peer(k)))
        if stage == 1:
            region, slot = out.at[x_block, rest, at.b], self.slot_x1
        else:
            region, slot = out.at[x_block, pl.ds(0, half)], self.slot_x2
        copies.append(self.copy(region, slot, at.x_peer))
        return copies

    def start(self, stage):
        copies_start(self.copies(stage, False))

    def land(self, stage):
        for copy in self.copies(stage, True):
            copy.wait_recv()
        for copy in self.copies(stage, False):
            copy.wait_send()

    def move(self, stage):
        self.land(stage)
        self.start(stage + 1)


class SpreadCross(Spread):
    @staticmethod
    def slots(bs):
        return 2 * bs + 2 * ZS - 1

    def copies(self, stage, back):
        at, out = self.at, self.out
        rows = out.shape[-2]
        cut = rows // 32 * 16
        some, rest = pl.ds(0, cut), pl.ds(cut, rows - cut)
        core = 1 - at.c if back else at.c
        if stage == 3:
            return [self.copy(out.at[pl.ds(core * 2, 2)], 2 * at.bs + 2 * ZS - 2, at.core_peer)]
        both = pl.ds(at.c * 2, 2)
        x_block = at.other_block if back else at.block
        copies = []
        if stage == 1:
            for k in range(1, ZS):
                z = at.z_at(ZS - k) if back else at.z
                copies.append(self.copy(out.at[both, z, at.b, some], at.bs + k - 1, at.z_peer(k)))
                slot = at.bs + ZS + k - 2
                copies.append(self.copy(out.at[at.block, z, :, rest], slot, at.z_peer(k)))
            return copies
        base = 0 if stage == 0 else at.bs + 2 * ZS - 2
        for k in range(1, at.bs):
            b = at.b_at(at.bs - k) if back else at.b
            region = out.at[at.block, at.z, b, rest] if stage == 0 else out.at[both, :, b, some]
            copies.append(self.copy(region, base + k, at.b_peer(k)))
        if stage == 0:
            region = out.at[x_block, at.z, at.b, some]
        else:
            region = out.at[x_block, :, :, rest]
        copies.append(self.copy(region, base, at.x_peer))
        return copies


class Fold:
    def __init__(self, at, grads, total, landing, bufs, final, send, recv, credit, half):
        self.at, self.grads, self.total = at, grads, total
        self.landing, self.bufs, self.final = landing, bufs, final
        self.send, self.recv, self.credit = send, recv, credit
        self.half = half
        nb = at.bs - 1
        self.slot_x1 = 1
        self.slot_b1 = 2
        self.slot_x2 = 2 + nb
        self.slot_b2 = 3 + nb
        self.slot_z = 3 + 2 * nb

    @staticmethod
    def slots(bs):
        return 3 + 2 * (bs - 1) + ZS - 1

    @staticmethod
    def buffers(bs, rows, half):
        nb = max(bs - 1, 1)
        rest = ZS - half
        return [
            (half, bs, rows, LANES),
            (nb, 2, rest, rows, LANES),
            (rest, rows, LANES),
            (nb, half, rows, LANES),
            (ZS - 1, rows, LANES),
        ]

    def core_parts(self):
        other = self.grads.at[pl.ds((1 - self.at.c) * 2, 2)]
        return [(other, self.landing, 0, self.at.core_peer, self.at.core_peer)]

    def parts(self, stage):
        at, half, total, bufs = self.at, self.half, self.total, self.bufs
        if stage == 0:
            return self.core_parts()
        if stage == 3:
            return [
                (
                    total.at[at.x, at.z_at(k), at.b],
                    bufs[4].at[k - 1],
                    self.slot_z + k - 1,
                    at.z_peer(k),
                    at.z_peer(ZS - k),
                )
                for k in range(1, ZS)
            ]
        rest = pl.ds(half, ZS - half)
        found = []
        for k in range(1, at.bs):
            if stage == 1:
                src, buf, slot = total.at[:, rest, at.b_at(k)], bufs[1], self.slot_b1
            else:
                src, buf, slot = total.at[at.x, pl.ds(0, half), at.b_at(k)], bufs[3], self.slot_b2
            found.append((src, buf.at[k - 1], slot + k - 1, at.b_peer(k), at.b_peer(at.bs - k)))
        if stage == 1:
            src, buf, slot = total.at[1 - at.x, pl.ds(0, half)], bufs[0], self.slot_x1
        else:
            src, buf, slot = total.at[1 - at.x, rest, at.b], bufs[2], self.slot_x2
        found.append((src, buf, slot, at.x_peer, at.x_peer))
        return found

    def start(self, stage, again):
        for src, buf, slot, to, _ in self.parts(stage):
            if again is not False:

                @pl.when(again)
                def _():
                    pl.semaphore_wait(self.credit.at[slot], 1)

            remote(src, buf, self.send.at[slot], self.recv.at[slot], to).start()

    def land(self, stage, more):
        parts = self.parts(stage)
        for src, buf, slot, to, _ in parts:
            remote(src, buf, self.send.at[slot], self.recv.at[slot], to).wait()
        self.add(stage)
        if more is not False:

            @pl.when(more)
            def _():
                for _, _, slot, _, origin in parts:
                    pl.semaphore_signal(
                        self.credit.at[slot], inc=1, device_id=origin, device_id_type=MESH
                    )

    def add_core(self):
        at, bs, total = self.at, self.at.bs, self.total

        @pl.loop(0, 2 * ZS * bs)
        def _(i):
            z, b = i // bs % ZS, i % bs
            x = i // (ZS * bs)
            total[x, z, b] = self.grads[at.c * 2 + x, z, b] + self.landing[x, z, b]

    def add(self, stage):
        at, half, bs = self.at, self.half, self.at.bs
        total, bufs = self.total, self.bufs
        rest = ZS - half
        if stage == 0:
            self.add_core()
        elif stage == 1:

            @pl.loop(0, half * bs)
            def _(i):
                z, b = i // bs, i % bs
                total[at.x, z, b] = total[at.x, z, b] + bufs[0][z, b]

            @pl.loop(0, 2 * rest)
            def _(i):
                x, z = i // rest, i % rest
                for k in range(bs - 1):
                    total[x, half + z, at.b] = total[x, half + z, at.b] + bufs[1][k, x, z]

        elif stage == 2:

            @pl.loop(0, rest)
            def _(z):
                total[at.x, half + z, at.b] = total[at.x, half + z, at.b] + bufs[2][z]

            @pl.loop(0, half)
            def _(z):
                for k in range(bs - 1):
                    total[at.x, z, at.b] = total[at.x, z, at.b] + bufs[3][k, z]

        else:
            self.finish([bufs[4][k] for k in range(ZS - 1)])

    def finish(self, pieces):
        at = self.at
        done = self.total[at.x, at.z, at.b].astype(jnp.float32)
        for piece in pieces:
            done = done + piece.astype(jnp.float32)
        self.final[...] = done.astype(self.final.dtype)

    def move(self, stage, again, more):
        self.land(stage, more)
        self.start(stage + 1, again)


class FoldCross(Fold):
    @staticmethod
    def slots(bs):
        return 2 * bs + 2 * ZS - 1

    @staticmethod
    def buffers(bs, rows, half):
        nb = max(bs - 1, 1)
        cut = rows // 32 * 16
        rest = rows - cut
        return [
            (nb, 2, ZS, cut, LANES),
            (ZS, bs, rest, LANES),
            (ZS - 1, 2, cut, LANES),
            (ZS - 1, bs, rest, LANES),
            (cut, LANES),
            (nb, rest, LANES),
        ]

    def cuts(self):
        rows = self.total.shape[-2]
        cut = rows // 32 * 16
        return pl.ds(0, cut), pl.ds(cut, rows - cut)

    def parts(self, stage):
        at, total, bufs = self.at, self.total, self.bufs
        if stage == 0:
            return self.core_parts()
        some, rest = self.cuts()
        found = []
        if stage == 2:
            for k in range(1, ZS):
                pair = (at.z_peer(k), at.z_peer(ZS - k))
                z = at.z_at(k)
                found.append((total.at[:, z, at.b, some], bufs[2].at[k - 1], at.bs + k, *pair))
                slot = at.bs + ZS + k - 1
                found.append((total.at[at.x, z, :, rest], bufs[3].at[k - 1], slot, *pair))
            return found
        base = 1 if stage == 1 else at.bs + 2 * ZS - 1
        for k in range(1, at.bs):
            pair = (at.b_peer(k), at.b_peer(at.bs - k))
            if stage == 1:
                src, buf = total.at[:, :, at.b_at(k), some], bufs[0].at[k - 1]
            else:
                src, buf = total.at[at.x, at.z, at.b_at(k), rest], bufs[5].at[k - 1]
            found.append((src, buf, base + k, *pair))
        if stage == 1:
            src, buf = total.at[1 - at.x, :, :, rest], bufs[1]
        else:
            src, buf = total.at[1 - at.x, at.z, at.b, some], bufs[4]
        found.append((src, buf, base, at.x_peer, at.x_peer))
        return found

    def add(self, stage):
        at, bs = self.at, self.at.bs
        total, bufs = self.total, self.bufs
        some, rest = self.cuts()
        if stage == 0:
            self.add_core()
        elif stage == 1:

            @pl.loop(0, 2 * ZS)
            def _(i):
                x, z = i // ZS, i % ZS
                for k in range(bs - 1):
                    total[x, z, at.b, some] = total[x, z, at.b, some] + bufs[0][k, x, z]

            @pl.loop(0, ZS * bs)
            def _(i):
                z, b = i // bs, i % bs
                total[at.x, z, b, rest] = total[at.x, z, b, rest] + bufs[1][z, b]

        elif stage == 2:
            for x in range(2):
                for k in range(ZS - 1):
                    total[x, at.z, at.b, some] = total[x, at.z, at.b, some] + bufs[2][k, x]

            @pl.loop(0, bs)
            def _(b):
                for k in range(ZS - 1):
                    total[at.x, at.z, b, rest] = total[at.x, at.z, b, rest] + bufs[3][k, b]

        else:
            total[at.x, at.z, at.b, some] = total[at.x, at.z, at.b, some] + bufs[4][...]
            for k in range(bs - 1):
                total[at.x, at.z, at.b, rest] = total[at.x, at.z, at.b, rest] + bufs[5][k]
            self.final[...] = total[at.x, at.z, at.b]


HALF = 256
WIDE = 512
QKV_TILE = 768
VEC_ROWS = 16


STEP = 64


def by_rows(fn, *arrays, step=STEP):
    parts = [
        fn(*[array[at : at + step] for array in arrays])
        for at in range(0, arrays[0].shape[0], step)
    ]
    if isinstance(parts[0], tuple):
        return tuple(jnp.concatenate(part, axis=0) for part in zip(*parts))
    return jnp.concatenate(parts, axis=0)


def dot_nt(a, b):
    return lax.dot_general(a, b, (((1,), (1,)), ((), ())), preferred_element_type=jnp.float32)


def dot_nn(a, b):
    return lax.dot_general(a, b, (((1,), (0,)), ((), ())), preferred_element_type=jnp.float32)


def dot_tn(a, b):
    return lax.dot_general(a, b, (((0,), (0,)), ((), ())), preferred_element_type=jnp.float32)


def aligned(index, unit):
    return pl.multiple_of(index, unit)


def rows_of(ref, bs, first, count, start, rows, blocks=range(SECT)):
    parts = []
    for i in range(count):
        d = first + i
        place = (d // bs, d % bs)
        parts.append(
            jnp.concatenate(
                [ref[(lb,) + place + (pl.ds(start, rows), slice(None))] for lb in blocks], axis=1
            )
        )
    return parts[0] if count == 1 else jnp.concatenate(parts, axis=0)


def put_rows(ref, bs, first, count, start, rows, value, block=0):
    value = value.astype(ref.dtype)
    for i in range(count):
        d = first + i
        place = (d // bs, d % bs)
        for lane in range(value.shape[1] // LANES):
            ref[(block + lane,) + place + (pl.ds(start, rows), slice(None))] = value[
                i * rows : (i + 1) * rows, lane * LANES : (lane + 1) * LANES
            ]


def vector_pieces(dps):
    n_gains, n_biases = 2 * WIDE // dps, 10 * WIDE // dps
    starts = [(0, 0), (0, 2), (1, 0), (1, 2), (2, 0), (2, 1), (2, 2), (2, 3), (3, 0), (3, 2)]
    pieces = []
    for d in range(dps):
        at = 0
        while at < n_gains + n_biases:
            if at < n_gains:
                index = d * n_gains + at
                row, column = (1, 3)[index // WIDE], WIDE + index % WIDE
                left = n_gains - at
            else:
                index = d * n_biases + at - n_gains
                row, part = starts[index // WIDE]
                column = part * WIDE + index % WIDE
                left = n_gains + n_biases - at
            size = min(left, LANES - at % LANES, LANES - column % LANES)
            pieces.append((d, at // LANES, at % LANES, row, column, size))
            at += size
    return pieces


def read_vectors(ref, table, bs, start, block):
    tiles = {}
    for d, row, lane, to_row, to_lane, size in vector_pieces(ZS * bs):
        if d not in tiles:
            tile = ref[block, d // bs, d % bs, start : start + VEC_ROWS, :]
            tiles[d] = tile.astype(jnp.float32)
        table[to_row : to_row + 1, to_lane : to_lane + size] = tiles[d][
            row : row + 1, lane : lane + size
        ]


def rows_tile(lines):
    row_id = lax.broadcasted_iota(jnp.int32, (VEC_ROWS, LANES), 0)
    tile = jnp.zeros((VEC_ROWS, LANES), jnp.float32)
    for row, pieces in enumerate(lines):
        have = sum(piece.shape[1] for piece in pieces)
        if have < LANES:
            pieces = pieces + [jnp.zeros((1, LANES - have), jnp.float32)]
        line = pieces[0] if len(pieces) == 1 else jnp.concatenate(pieces, axis=1)
        tile = jnp.where(row_id == row, line, tile)
    return tile


def vector_tile(table, dps, place):
    lines = []
    for d, row, lane, to_row, to_lane, size in vector_pieces(dps):
        if d == place:
            if row == len(lines):
                lines.append([])
            lines[row].append(table[to_row : to_row + 1, to_lane : to_lane + size])
    return rows_tile(lines)


def fold_rows(x):
    total = x[:8]
    for at in range(8, x.shape[0], 8):
        total = total + x[at : at + 8]
    return total


def normalize(x):
    mean = jnp.mean(x, axis=1, keepdims=True)
    centred = x - mean
    scale = lax.rsqrt(jnp.mean(centred * centred, axis=1, keepdims=True) + NORM_EPS)
    return centred * scale, jnp.broadcast_to(scale, (x.shape[0], LANES))


def normalize_back(unit, scale, grad, gain):
    inner = grad * gain
    first = jnp.mean(inner, axis=1, keepdims=True)
    second = jnp.mean(inner * unit, axis=1, keepdims=True)
    out = jnp.concatenate([scale] * (WIDE // LANES), axis=1) * (inner - first - unit * second)
    return out, fold_rows(out), fold_rows(grad * unit), fold_rows(grad)


def gelu_pair(u):
    below = 0.5 + 0.5 * lax.erf(u * math.sqrt(0.5))
    bell = jnp.exp2((-0.5 * math.log2(math.e)) * (u * u))
    return u * below, below + u * (bell * (1.0 / math.sqrt(2.0 * math.pi)))


def head_masks(scale):
    lane = lax.broadcasted_iota(jnp.int32, (1, LANES), 1)
    first = jnp.where(lane < HEAD, scale, 0.0).astype(jnp.bfloat16)
    second = jnp.where(lane < HEAD, 0.0, scale).astype(jnp.bfloat16)
    return first, second


class Sizes:
    def __init__(self, dps):
        self.dps, self.bs = dps, dps // ZS
        self.qkv, self.out, self.up, self.down = (
            3 * WIDE // dps,
            WIDE // dps,
            4 * WIDE // dps,
            WIDE // dps,
        )
        self.lookback = -(-6 * WIDE // (SECT * dps) // VEC_ROWS) * VEC_ROWS
        self.emb = self.lookback + VEC_ROWS
        self.dense = self.out + self.up
        self.wide = 4 * self.down


def qkv_rows(size, w, tile):
    count = QKV_TILE // size.qkv
    return rows_of(w, size.bs, tile * count, count, 0, size.qkv)


def out_rows(size, w):
    return rows_of(w, size.bs, 0, size.dps, 0, size.out)


def up_rows(size, w, tile):
    count = HALF // size.up
    return rows_of(w, size.bs, tile * count, count, size.out, size.up)


def forward_mix(size, w, table, h, mixed, piece):
    columns = slice(piece * QKV_TILE, (piece + 1) * QKV_TILE)
    shift = table[0:1, columns]
    out = dot_nt(h[...], qkv_rows(size, w, piece))
    mixed[:, columns] = by_rows(lambda part: (part + shift).astype(mixed.dtype), out)


def softmax_columns(scores):
    parts = [scores[at : at + STEP] for at in range(0, scores.shape[0], STEP)]
    top = parts[0]
    for part in parts[1:]:
        top = jnp.maximum(top, part)
    top = jnp.max(top, axis=0, keepdims=True)
    parts = [jnp.exp(part - top) for part in parts]
    total = parts[0]
    for part in parts[1:]:
        total = total + part
    scale = 1.0 / jnp.sum(total, axis=0, keepdims=True)
    return jnp.concatenate([(part * scale).astype(jnp.bfloat16) for part in parts], axis=0)


def forward_attend(mixed, probs, attended, pair):
    lane = pair * LANES
    key_rows = mixed[:, WIDE + lane : WIDE + lane + LANES]
    values = mixed[:, 2 * WIDE + lane : 2 * WIDE + lane + LANES].T

    for part in range(2):
        rows = slice(part * HALF, (part + 1) * HALF)
        queries = mixed[rows, lane : lane + LANES]
        joined = []
        for head, mask in enumerate(head_masks(1.0 / math.sqrt(HEAD))):
            weights = softmax_columns(dot_nt(key_rows, queries * mask))
            probs[2 * pair + head, :, rows] = weights
            joined.append(dot_nn(values[head * HEAD : (head + 1) * HEAD], weights))
        joined = jnp.concatenate(joined, axis=0).T
        attended[rows, lane : lane + LANES] = joined.astype(attended.dtype)


def forward_project(size, w, table, h, attended, first, scale, normed):
    out = dot_nt(attended[...], out_rows(size, w))
    for part in range(WIDE // STEP):
        rows = slice(part * STEP, (part + 1) * STEP)
        total = h[rows, :].astype(jnp.float32) + (out[rows] + table[1:2, 0:WIDE])
        unit, scale[rows, :] = normalize(total)
        first[rows, :] = unit
        normed[rows, :] = (
            unit * table[1:2, WIDE : 2 * WIDE] + table[1:2, 2 * WIDE : 3 * WIDE]
        ).astype(normed.dtype)


def forward_up(size, w, table, normed, slope, hidden, piece):
    for j in (2 * piece, 2 * piece + 1):
        columns = slice(j * HALF, (j + 1) * HALF)
        shift = table[2:3, columns]
        upper = dot_nt(normed[...], up_rows(size, w, j))
        for part in range(WIDE // STEP):
            rows = slice(part * STEP, (part + 1) * STEP)
            value, grad = gelu_pair(upper[rows] + shift)
            hidden[rows, columns] = value.astype(hidden.dtype)
            slope[rows, columns] = grad.astype(slope.dtype)


def forward_down(size, w, table, normed, hidden, second, scale, h, piece):
    columns = slice(piece * HALF, (piece + 1) * HALF)
    count = size.dps // 2
    matrix = jnp.concatenate(
        [
            rows_of(w, size.bs, piece * count, count, j * size.down, size.down)
            for j in range(4)
        ],
        axis=1,
    )
    out = dot_nt(hidden[...], matrix)
    shift = table[3:4, columns]
    for part in range(WIDE // STEP):
        rows = slice(part * STEP, (part + 1) * STEP)
        second[rows, columns] = normed[rows, columns].astype(jnp.float32) + (out[rows] + shift)
    if piece == 1:
        for part in range(WIDE // STEP):
            rows = slice(part * STEP, (part + 1) * STEP)
            unit, scale[rows, :] = normalize(second[rows, :])
            second[rows, :] = unit
            h[rows, :] = (
                unit * table[3:4, WIDE : 2 * WIDE] + table[3:4, 2 * WIDE : 3 * WIDE]
            ).astype(h.dtype)


def backward_norm_two(table, dtable, dy, second, scale, dnormed, dlow, dlow_t):
    dtable[...] = jnp.zeros_like(dtable)
    sums = [jnp.zeros((8, WIDE), jnp.float32)] * 3
    for part in range(WIDE // STEP):
        rows = slice(part * STEP, (part + 1) * STEP)
        grad, *found = normalize_back(
            second[rows, :],
            scale[rows, :],
            dy[rows, :].astype(jnp.float32),
            table[3:4, WIDE : 2 * WIDE],
        )
        dnormed[rows, :] = grad
        dlow[rows, :] = grad.astype(dlow.dtype)
        sums = [total + new for total, new in zip(sums, found)]
    for i, total in enumerate(sums):
        dtable[3:4, i * WIDE : (i + 1) * WIDE] = jnp.sum(total, axis=0, keepdims=True)
    dlow_t[...] = dlow[...].T


def backward_down(size, grads, hidden, dlow_t, piece):
    @pl.loop(2 * piece, 2 * piece + 2)
    def _(i):
        start = aligned(i * size.down, 16)
        for half in range(2):
            columns = pl.ds(aligned(i * WIDE, WIDE) + half * HALF, HALF)
            value = dot_nn(dlow_t[...], hidden[:, columns])
            put_rows(grads, size.bs, 0, size.dps, start, size.down, value, 2 * half)


def backward_gelu(size, w, dtable, slope, dlow, dup, piece):
    @pl.loop(2 * piece, 2 * piece + 2)
    def _(i):
        start = aligned(i * size.down, 16)
        for half in range(2):
            columns = pl.ds(aligned(i * WIDE, WIDE) + half * HALF, HALF)
            blocks = (2 * half, 2 * half + 1)
            matrix = rows_of(w, size.bs, 0, size.dps, start, size.down, blocks)
            dhidden = dot_nn(dlow[...], matrix)
            total = jnp.zeros((8, HALF), jnp.float32)
            for part in range(WIDE // STEP):
                rows = slice(part * STEP, (part + 1) * STEP)
                dupper = dhidden[rows] * slope[rows, columns].astype(jnp.float32)
                total = total + fold_rows(dupper)
                dup[rows, columns] = dupper.astype(dup.dtype)
            dtable[2:3, columns] = jnp.sum(total, axis=0, keepdims=True)


def backward_up(size, grads, normed, dup):
    count = HALF // size.up

    @pl.loop(0, 4)
    def _(i):
        for half in range(2):
            columns = pl.ds(aligned(i * WIDE, WIDE) + half * HALF, HALF)
            value = dot_tn(dup[:, columns], normed[...])
            first = (2 * i + half) * count
            put_rows(grads, size.bs, first, count, size.out, size.up, value)


def backward_normed(size, w, dnormed, dup):
    for half in range(2):
        columns = slice(half * HALF, (half + 1) * HALF)
        blocks = (2 * half, 2 * half + 1)
        matrix = rows_of(w, size.bs, 0, size.dps, size.out, size.up, blocks)
        out = dot_nn(dup[...], matrix)
        for part in range(WIDE // STEP):
            rows = slice(part * STEP, (part + 1) * STEP)
            dnormed[rows, columns] = dnormed[rows, columns] + out[rows]


def backward_norm_one(
    size, w, table, grads, dtable, first, scale, attended, dnormed, dlow, dlow_t, delta
):
    sums = [jnp.zeros((8, WIDE), jnp.float32)] * 3
    for part in range(WIDE // STEP):
        rows = slice(part * STEP, (part + 1) * STEP)
        grad, *found = normalize_back(
            first[rows, :], scale[rows, :], dnormed[rows, :], table[1:2, WIDE : 2 * WIDE]
        )
        dnormed[rows, :] = grad
        dlow[rows, :] = grad.astype(dlow.dtype)
        sums = [total + new for total, new in zip(sums, found)]
    for i, total in enumerate(sums):
        dtable[1:2, i * WIDE : (i + 1) * WIDE] = jnp.sum(total, axis=0, keepdims=True)
    dlow_t[...] = dlow[...].T
    for block in (0, 2):
        columns = slice(block * LANES, (block + 2) * LANES)
        value = dot_nn(dlow_t[...], attended[:, columns])
        put_rows(grads, size.bs, 0, size.dps, 0, size.out, value, block)
    grad = dot_nn(dlow[...], out_rows(size, w)).astype(dlow.dtype)
    dlow[...] = grad
    product = grad.astype(jnp.float32) * attended[...].astype(jnp.float32)
    high = product.astype(jnp.bfloat16)
    rest = (product - high.astype(jnp.float32)).astype(jnp.bfloat16)
    head = lax.broadcasted_iota(jnp.int32, delta.shape, 0)
    lane = lax.broadcasted_iota(jnp.int32, delta.shape, 1)
    inside = (lane >= head * HEAD) & (lane < (head + 1) * HEAD)
    inside = jnp.where(inside, 1.0, 0.0).astype(jnp.bfloat16)
    delta[...] = dot_nt(inside, high) + dot_nt(inside, rest)


def backward_attend(mixed, probs, delta, dtable, dlow, dmixed, pair):
    scale = 1.0 / math.sqrt(HEAD)
    lane = pair * LANES
    columns = slice(lane, lane + LANES)
    key_columns = slice(WIDE + lane, WIDE + lane + LANES)
    value_columns = slice(2 * WIDE + lane, 2 * WIDE + lane + LANES)
    keys_t = mixed[:, key_columns].T
    values = mixed[:, value_columns]
    dkeys = jnp.zeros((WIDE, LANES), jnp.float32)
    dvalues = jnp.zeros((WIDE, LANES), jnp.float32)
    for part in range(2):
        rows = slice(part * HALF, (part + 1) * HALF)
        queries = mixed[rows, columns]
        grad_out = dlow[rows, columns]
        dqueries = []
        for head in range(2):
            query = queries * head_masks(scale)[head]
            grad = grad_out * head_masks(1.0)[head]
            at = 2 * pair + head
            weights = probs[at, :, rows]
            less = delta[at : at + 1, rows]
            dprobs = dot_nt(values, grad)
            dscores = by_rows(
                lambda p, dp: (p.astype(jnp.float32) * (dp - less)).astype(jnp.bfloat16),
                weights,
                dprobs,
            )
            dvalues = dvalues + dot_nn(weights, grad)
            dkeys = dkeys + dot_nn(dscores, query)
            dqueries.append(dot_nn(keys_t[head * HEAD : (head + 1) * HEAD], dscores))
        dquery = jnp.concatenate(dqueries, axis=0).T * scale
        dtable[0:1, columns] += jnp.sum(dquery, axis=0, keepdims=True)
        dmixed[rows, columns] = dquery.astype(dmixed.dtype)
    dmixed[:, key_columns] = dkeys.astype(dmixed.dtype)
    dmixed[:, value_columns] = dvalues.astype(dmixed.dtype)
    dtable[0:1, value_columns] = jnp.sum(dvalues, axis=0, keepdims=True)


def backward_mix(size, grads, h, dmixed, piece):
    count = QKV_TILE // size.qkv
    grad = dmixed[:, piece * QKV_TILE : (piece + 1) * QKV_TILE]
    put_rows(grads, size.bs, piece * count, count, 0, size.qkv, dot_tn(grad, h[...]))


def backward_input(size, w, dnormed, dmixed, dy):
    for half in range(2):
        columns = slice(half * HALF, (half + 1) * HALF)
        blocks = (2 * half, 2 * half + 1)
        matrix = rows_of(w, size.bs, 0, size.dps, 0, size.qkv, blocks)
        out = dot_nn(dmixed[...], matrix)
        for part in range(WIDE // STEP):
            rows = slice(part * STEP, (part + 1) * STEP)
            dy[rows, columns] = (dnormed[rows, columns] + out[rows]).astype(dy.dtype)


WINDOW = 384


def group_rows(group):
    rows = lax.broadcasted_iota(jnp.int32, (16, LANES), 0)
    return jnp.where(rows == group, 1.0, 0.0).astype(jnp.bfloat16)


def pack_mix(piece, qkv):
    for lb in range(SECT):
        piece[lb] = qkv[:, lb * LANES : (lb + 1) * LANES].astype(piece.dtype)


def pack_up(piece, out, up):
    rows = out.shape[0]
    for lb in range(SECT):
        lanes = slice(lb * LANES, (lb + 1) * LANES)
        piece[lb, :rows] = out[:, lanes].astype(piece.dtype)
        piece[lb, rows:] = up[:, lanes].astype(piece.dtype)


def pack_down(piece, down):
    rows = down.shape[0]
    for lb in range(SECT):
        for j in range(4):
            start = j * WIDE + lb * LANES
            piece[lb, j * rows : (j + 1) * rows] = down[:, start : start + LANES].astype(piece.dtype)


def pack_embedding(piece, weight, shift, gains, biases, square, block):
    n = weight.shape[0]
    square[...] = jnp.zeros_like(square)
    square[:GROUPS, :n] = shift[...]

    def ending(part, width):
        return jnp.concatenate([jnp.zeros((n, width - part.shape[1]), part.dtype), part], axis=1)

    third = ending(weight[:, L1 + L2 :], 3 * LANES)
    second = ending(weight[:, L1 : L1 + L2], 2 * LANES)
    blocks = [third[:, :LANES] + square[...].T[:n]]
    blocks += [third[:, LANES : 2 * LANES], third[:, 2 * LANES :]]
    blocks += [second[:, :LANES], second[:, LANES:], ending(weight[:, :L1], LANES)]
    rows = piece.shape[1] - VEC_ROWS
    if SECT * rows > 6 * n:
        blocks.append(jnp.zeros((SECT * rows - 6 * n, LANES), jnp.float32))
    flat = jnp.concatenate(blocks, axis=0).astype(piece.dtype)
    for lb in range(SECT):
        piece[lb, :rows] = flat[lb * rows : (lb + 1) * rows]
    line = jnp.concatenate([gains[...], biases[...]], axis=1)
    lines = [[line[:, at : at + LANES]] for at in range(0, line.shape[1], LANES)]
    piece[block, rows:] = rows_tile(lines).astype(piece.dtype)


def expand(series, group, x):
    empty = jnp.zeros((WINDOW - series.shape[0], series.shape[1]), series.dtype)
    x[:, :WINDOW] = jnp.concatenate([empty, series[...]], axis=0).T
    lane = lax.broadcasted_iota(jnp.int32, (x.shape[0], LANES), 1)
    x[:, WINDOW:] = jnp.where(lane == group, 1.0, 0.0).astype(x.dtype)


def embed(size, emb, pick, x, wsel, h):
    n = WIDE // size.dps
    flat = []
    for d in range(size.dps):
        place = (d // size.bs, d % size.bs, slice(0, size.lookback), slice(None))
        flat.append(jnp.concatenate([emb[(lb,) + place] for lb in range(SECT)], axis=0))
    blocks = [
        jnp.concatenate([rows[j * n : (j + 1) * n] for rows in flat], axis=0) for j in range(6)
    ]
    long, middle, short = (pick[g : g + 1, :] for g in (2, 1, 0))
    wide = jnp.concatenate(
        [
            blocks[0] * long,
            blocks[1] * long + blocks[3] * middle,
            blocks[2] * long + blocks[4] * middle + blocks[5] * short,
        ],
        axis=1,
    )
    wsel[...] = wide.T
    h[...] = dot_nt(x[...], jnp.concatenate([wide, blocks[0]], axis=1)).astype(h.dtype)


def embed_back(size, pick, x, wsel, dh, tables, grads, series_grad):
    history = series_grad.shape[0]
    series_grad[...] = dot_nt(wsel[...], dh[...])[WINDOW - history :]
    sums = dot_tn(dh[...], x[...])
    long, middle, short = (pick[g : g + 1, :].astype(jnp.float32) for g in (2, 1, 0))
    parts = [sums[:, i * LANES : (i + 1) * LANES] for i in range(4)]
    parts = [
        parts[0] * long + parts[3],
        parts[1] * long,
        parts[2] * long,
        parts[1] * middle,
        parts[2] * middle,
        parts[2] * short,
    ]
    rows = WIDE // (SECT * size.dps)
    spare = size.lookback - 6 * rows
    for pipe in range(SECT):
        block = (pipe % 2) * 2 + pipe // 2
        for dp in range(size.dps):
            start = (pipe * size.dps + dp) * rows
            pieces = [part[start : start + rows] for part in parts]
            if spare:
                pieces.append(jnp.zeros((spare, LANES), jnp.float32))
            pieces.append(vector_tile(tables.at[pipe], size.dps, dp))
            piece = jnp.concatenate(pieces, axis=0)
            grads[block, dp // size.bs, dp % size.bs] = piece.astype(grads.dtype)


def saved_shapes():
    low, wide = jnp.bfloat16, jnp.float32
    return [
        ((WIDE, WIDE), low),
        ((WIDE, 3 * WIDE), low),
        ((2 * SECT, WIDE, WIDE), low),
        ((WIDE, WIDE), low),
        ((WIDE, WIDE), wide),
        ((WIDE, WIDE), low),
        ((WIDE, 4 * WIDE), low),
        ((WIDE, 4 * WIDE), low),
        ((WIDE, WIDE), wide),
        ((SECT, 4 * WIDE), wide),
        ((WIDE, LANES), wide),
        ((WIDE, LANES), wide),
    ]


def chunk_shape(size, rows):
    return (SECT, ZS, size.bs, rows, LANES)


HALVES = (2, 2, 2, 2)
CROSS = (2,)


def follow(plan, section, act, compute):
    seen = {}
    for step in plan:
        if len(step) == 1:
            piece = seen.get(step[0], 0)
            seen[step[0]] = piece + 1
            compute(step[0], piece)
            continue
        op, kind, offset = step
        where = section + offset
        if isinstance(where, int):
            if 0 <= where < SECT:
                act(op, kind, where)
        elif offset == 0:
            act(op, kind, where)
        else:
            inside = where < SECT if offset > 0 else where >= 0

            @pl.when(inside)
            def _():
                act(op, kind, where)


def forward_kernel(dps, groups, *refs):
    size = Sizes(dps)
    given, refs = refs[:9], refs[9:]
    out, copies_out, wsel, x, refs = refs[0], refs[1:4], refs[4], refs[5], refs[6:]
    kept, local, refs = refs[:12], refs[12:24], refs[24:]
    wholes, refs = refs[:4], refs[4:]
    pieces, held, refs = refs[:4], refs[4:13], refs[13:]
    emb_rows, pick, refs = refs[0], refs[1], refs[2:]
    given_sem, out_sem, kept_sem, own_sem, p_send, p_recv, send, recv = refs
    h, mixed, probs, attended, first, normed, slope, hidden, second, table, scale_1, scale_2 = local
    at = Place(dps)

    own = [
        pltpu.make_async_copy(
            pieces[kind].at[at.block],
            wholes[kind].at[at.pipe, at.block, at.z, at.b]
            if kind < EMB
            else wholes[kind].at[at.block, at.z, at.b],
            own_sem.at[kind],
        )
        for kind in range(4)
    ]
    def split(kind, back):
        copies = []
        for k in range(1, SECT):
            if back:
                region = wholes[kind].at[at.pipe_at(SECT - k), at.block, at.z, at.b]
                src = region
            else:
                block = at.blocks[k]
                region = wholes[kind].at[at.pipe, block, at.z, at.b]
                src = pieces[kind].at[block]
            sems = p_send.at[kind, k - 1], p_recv.at[kind, k - 1]
            copies.append(remote(src, region, *sems, (at.pipe_at(k), at.dp)))
        return copies

    def chunk(kind, section):
        if kind == EMB:
            return Spread(at, wholes[kind], send.at[3 * SECT], recv.at[3 * SECT])
        number = 3 * section + kind
        sort = SpreadCross if kind in CROSS else Spread
        return sort(at, wholes[kind].at[section], send.at[number], recv.at[number], HALVES[kind])

    def keep(kind, section):
        src, dst = wholes[kind].at[section], copies_out[kind].at[section]
        return pltpu.make_async_copy(src, dst, out_sem.at[kind, section])

    arrived = []

    def act(op, kind, section):
        if op == 0:
            if kind not in arrived:
                arrived.append(kind)
                own[kind].wait()
                if kind == EMB:
                    chunk(kind, section).start(0)
                    return
                for copy in split(kind, True):
                    copy.wait_recv()
                for copy in split(kind, False):
                    copy.wait_send()
                if kind == 0:
                    copies_start(split(1, False))
                    copies_start(split(2, False))
            chunk(kind, section).start(0)
        elif op < 4:
            chunk(kind, section).move(op - 1)
            if op == 1 and kind == EMB:
                gets[0].wait()
                expand(series, groups[0], x)
        else:
            chunk(kind, section).land(3)
            if kind != EMB:
                keep(kind, section).start(priority=1)

    def saves(section, early):
        which = (1, 2, 3, 4, 5, 9, 10) if early else (6, 7, 8, 11)
        return [
            pltpu.make_async_copy(local[i], kept[i].at[section], kept_sem.at[i]) for i in which
        ]

    series, embed_weight, embed_bias, qkv, out_w, up_w, down_w, gains, biases = held
    gets = copies_of(zip(given, held), given_sem)
    for i in (3, 7, 8, 1, 2, 4, 5, 6, 0):
        gets[i].start(priority=1)
    pick[...] = group_rows(groups[0])
    at.greet()
    gets[3].wait()
    pack_mix(pieces[0], qkv)
    own[0].start(priority=1)
    at.met()
    copies_start(split(0, False))
    copies_wait(gets[1:3] + gets[7:9])
    pack_embedding(
        pieces[EMB], embed_weight, embed_bias, gains, biases, emb_rows, at.block
    )
    own[EMB].start(priority=1)
    copies_wait(gets[4:7])
    pack_up(pieces[1], out_w, up_w)
    own[1].start(priority=1)
    pack_down(pieces[2], down_w)
    own[2].start(priority=1)
    table[...] = jnp.zeros_like(table)

    def before(name, piece):
        embed(size, wholes[EMB], pick, x, wsel, h)

    follow(FORWARD_START, 0, act, before)

    @pl.loop(0, SECT)
    def _(section):
        att, up, down = (ref.at[section] for ref in wholes[:3])
        keep_h = pltpu.make_async_copy(h, kept[0].at[section], kept_sem.at[0])

        def compute(name, piece):
            if name == "mix":
                if piece == 0:

                    @pl.when(section > 0)
                    def _():
                        copies_wait(saves(section - 1, True))

                    keep_h.start(priority=1)
                    block = section % 2 * 2 + section // 2
                    read_vectors(wholes[EMB], table, size.bs, size.lookback, block)
                forward_mix(size, att, table, h, mixed, piece)
            elif name == "attend":
                forward_attend(mixed, probs, attended, piece)
            elif name == "project":
                forward_project(size, up, table, h, attended, first, scale_1, normed)
                copies_begin(saves(section, True))
            elif name == "up":
                if piece == 0:

                    @pl.when(section > 0)
                    def _():
                        copies_wait(saves(section - 1, False))

                forward_up(size, up, table, normed, slope, hidden, piece)
            else:
                if piece == 0:
                    keep_h.wait()
                forward_down(size, down, table, normed, hidden, second, scale_2, h, piece)
                if piece == 1:
                    copies_begin(saves(section, False))

        follow(FORWARD_PERIOD, section, act, compute)

    out[...] = h[...]
    copies_wait(saves(SECT - 1, True))
    copies_wait(saves(SECT - 1, False))
    for kind in range(3):
        copies_wait([keep(kind, section) for section in range(SECT)])


def copies_of(pairs, sems):
    return [pltpu.make_async_copy(src, dst, sems.at[i]) for i, (src, dst) in enumerate(pairs)]


def forward_all(groups, given, dps):
    size = Sizes(dps)
    low, wide = jnp.bfloat16, jnp.float32
    shapes = saved_shapes()
    rows = (size.qkv, size.dense, size.wide, size.emb)
    chunks = [chunk_shape(size, count) for count in rows]
    anywhere = pl.BlockSpec(memory_space=pl.ANY)
    inside = pl.BlockSpec(memory_space=pltpu.VMEM)
    outs = [((WIDE, WIDE), low)]
    outs += [((SECT,) + shape, low) for shape in chunks[:3]]
    outs += [((WINDOW, WIDE), low), ((WIDE, WIDE), low)]
    outs += [((SECT,) + shape, dtype) for shape, dtype in shapes]
    scratch = shapes + [((SECT,) + shape, low) for shape in chunks[:3]] + [(chunks[3], low)]
    scratch += [((SECT, count, LANES), low) for count in rows]
    scratch += [(array.shape, array.dtype) for array in given]
    scratch += [((LANES, LANES), wide), ((16, LANES), low)]
    slots = max(Spread.slots(size.bs), SpreadCross.slots(size.bs))
    dma = pltpu.SemaphoreType.DMA
    return pl.pallas_call(
        partial(forward_kernel, dps),
        out_shape=[jax.ShapeDtypeStruct(shape, dtype) for shape, dtype in outs],
        in_specs=[pl.BlockSpec(memory_space=pltpu.SMEM)] + [anywhere] * len(given),
        out_specs=[inside] + [anywhere] * 3 + [inside] * 2 + [anywhere] * len(shapes),
        scratch_shapes=[pltpu.VMEM(shape, dtype) for shape, dtype in scratch]
        + [
            dma((len(given),)),
            dma((3, SECT)),
            dma((len(shapes),)),
            dma((4,)),
            dma((3, SECT - 1)),
            dma((3, SECT - 1)),
            dma((1 + 3 * SECT, slots)),
            dma((1 + 3 * SECT, slots)),
        ],
        compiler_params=pltpu.CompilerParams(
            collective_id=0, has_side_effects=True, vmem_limit_bytes=60 * 1024 * 1024
        ),
        name="gather_forward",
    )(groups, *given)


FETCHES = {
    ("norm2", 0): (("second", "scale_2"), ("second", "scale_2")),
    ("down", 0): (("hidden",), ()),
    ("down", 1): ((), ("hidden",)),
    ("gelu", 0): (("slope", 2), ()),
    ("gelu", 1): ((), ("slope", 2)),
    ("up", 0): (("normed",), ("normed",)),
    ("normed", 0): ((1,), ()),
    ("norm1", 0): (("first", "scale_1", "attended"), ("first", "scale_1", "attended", 1)),
    ("attend", 0): (("mixed", "probs"), ()),
    ("attend", 3): ((), ("mixed", "probs")),
    ("mix", 0): (("h",), ()),
    ("mix", 1): ((), ("h",)),
    ("input", 0): ((0,), (0,)),
}


def backward_kernel(dps, groups, att, up, down, cotangent, x_in, wsel_in, *refs):
    size = Sizes(dps)
    kept, refs = refs[:12], refs[12:]
    series_grad, outs, refs = refs[0], refs[1:5], refs[5:]
    local, refs = refs[:11], refs[11:]
    tables, w_att, w_up, w_down, dtables, dy, dnormed, dlow, dlow_t, dmixed, dup = refs[:11]
    x, wsel, pick, delta, refs = *refs[11:15], refs[15:]
    kinds = []
    for kind in range(4):
        count = 6 if kind in CROSS else 5
        kinds.append(refs[:4] + (refs[4 : 4 + count],))
        refs = refs[4 + count :]
    w_sem, kept_sem, table_sem, late_sem, out_sem, p_send, p_recv, send, recv, credit = refs
    h, mixed, probs, attended, first, normed, slope, hidden, second, scale_1, scale_2 = local
    at = Place(dps)
    last = SECT - 1

    def weights(kind, section):
        src, dst = ((att, w_att), (up, w_up), (down, w_down))[kind]
        return pltpu.make_async_copy(src.at[section], dst, w_sem.at[kind])

    names = ("h", "mixed", "probs", "attended", "first", "normed", "slope", "hidden", "second")
    names += ("table", "scale_1", "scale_2")
    held = dict(zip(names[:9] + names[10:], local))

    def fetches(section, *wanted):
        found = []
        for name in wanted:
            if isinstance(name, int):
                found.append(weights(name, section))
            else:
                i = names.index(name)
                dst = held[name]
                found.append(pltpu.make_async_copy(kept[i].at[section], dst, kept_sem.at[i]))
        return found

    def chunk(kind, i):
        grads, totals, finals, landing, bufs = kinds[kind]
        sort = FoldCross if kind in CROSS else Fold
        refs = (grads, totals.at[i % 2], landing, bufs, finals.at[i])
        return sort(at, *refs, send.at[kind], recv.at[kind], credit.at[kind], HALVES[kind])

    def hand_over(kind, i):
        landing = outs[kind].at[at.block]
        final = kinds[kind][2].at[i]
        return (
            pltpu.make_async_copy(final, landing, out_sem.at[kind]),
            remote(final, landing, p_send.at[kind, i], p_recv.at[kind, at.pipe], (last - i, at.dp)),
        )

    def act(op, kind, i):
        again, more = (False, False) if kind == EMB else (i > 0, i < last)
        if op == 0:
            chunk(kind, i).start(0, again)
        elif op < 4:
            chunk(kind, i).move(op - 1, again, more)
        else:
            chunk(kind, i).land(3, more)
            if kind == EMB:
                outs[kind][...] = kinds[kind][2][0]
            else:
                here, away = hand_over(kind, i)

                @pl.when(at.pipe == last - i)
                def _():
                    here.start(priority=1)

                @pl.when(at.pipe != last - i)
                def _():
                    away.start()

    at.greet()
    get_tables = pltpu.make_async_copy(kept[9], tables, table_sem)
    late = copies_of(((cotangent, dy), (x_in, x), (wsel_in, wsel)), late_sem)
    copies_begin([late[0], get_tables] + fetches(last, "second", "scale_2", "hidden"))
    copies_begin(fetches(last, "slope", 2, "normed", 1, "first", "scale_1", "attended"))
    copies_begin(fetches(last, "mixed", "probs", "h", 0) + late[1:])
    pick[...] = group_rows(groups[0])
    copies_wait([late[0], get_tables])

    @pl.loop(0, SECT)
    def _(i):
        section = last - i
        table, dtable = tables.at[section], dtables.at[section]

        def compute(name, piece):
            need, free = FETCHES.get((name, piece), ((), ()))
            copies_wait(fetches(section, *need))
            if name == "norm2":
                backward_norm_two(table, dtable, dy, second, scale_2, dnormed, dlow, dlow_t)
                pl.when(i == 0)(at.met)
            elif name == "down":
                backward_down(size, kinds[2][0], hidden, dlow_t, piece)
            elif name == "gelu":
                backward_gelu(size, w_down, dtable, slope, dlow, dup, piece)
            elif name == "up":
                backward_up(size, kinds[1][0], normed, dup)
            elif name == "normed":
                backward_normed(size, w_up, dnormed, dup)
            elif name == "norm1":
                backward_norm_one(
                    size,
                    w_up,
                    table,
                    kinds[1][0],
                    dtable,
                    first,
                    scale_1,
                    attended,
                    dnormed,
                    dlow,
                    dlow_t,
                    delta,
                )
            elif name == "attend":
                backward_attend(mixed, probs, delta, dtable, dlow, dmixed, piece)
            elif name == "mix":
                backward_mix(size, kinds[0][0], h, dmixed, piece)
            else:
                backward_input(size, w_att, dnormed, dmixed, dy)
            if free:

                @pl.when(section > 0)
                def _():
                    copies_begin(fetches(section - 1, *free))

        follow(BACKWARD_PERIOD, i, act, compute)

    def after(name, piece):
        copies_wait(late[1:])
        embed_back(size, pick, x, wsel, dy, dtables, kinds[EMB][0], series_grad)

    follow(BACKWARD_END, 0, act, after)

    for kind in range(3):
        for i in range(SECT):
            here, away = hand_over(kind, i)

            @pl.when(at.pipe == last - i)
            def _():
                here.wait()

            @pl.when(at.pipe != last - i)
            def _():
                away.wait_send()

        for k in range(1, SECT):
            other = at.pipe_at(k)
            landing = outs[kind].at[at.blocks[k]]
            sems = p_send.at[kind, 0], p_recv.at[kind, other]
            remote(landing, landing, *sems, (other, at.dp)).wait_recv()


def backward_all(groups, weights, cotangent, x, wsel, kept, history, dps):
    size = Sizes(dps)
    low, wide = jnp.bfloat16, jnp.float32
    anywhere = pl.BlockSpec(memory_space=pl.ANY)
    inside = pl.BlockSpec(memory_space=pltpu.VMEM)
    shapes = saved_shapes()
    kind_rows = (size.qkv, size.dense, size.wide, size.emb)
    scratch = shapes[:9] + shapes[10:] + [((SECT,) + shapes[9][0], wide)]
    scratch += [(chunk_shape(size, rows), low) for rows in kind_rows[:3]]
    scratch += [
        ((SECT,) + shapes[9][0], wide),
        ((WIDE, WIDE), low),
        ((WIDE, WIDE), wide),
        ((WIDE, WIDE), low),
        ((WIDE, WIDE), low),
        ((WIDE, 3 * WIDE), low),
        ((WIDE, 4 * WIDE), low),
        ((WIDE, WIDE), low),
        ((WINDOW, WIDE), low),
        ((16, LANES), low),
        ((16, WIDE), wide),
    ]
    for kind, rows in enumerate(kind_rows):
        sets, results = (1, 1) if kind == EMB else (2, SECT)
        scratch += [
            (chunk_shape(size, rows), low),
            ((sets, 2, ZS, size.bs, rows, LANES), low),
            ((results, rows, LANES), low),
            ((2, ZS, size.bs, rows, LANES), low),
        ]
        sort = FoldCross if kind in CROSS else Fold
        scratch += [(shape, low) for shape in sort.buffers(size.bs, rows, HALVES[kind])]
    slots = max(Fold.slots(size.bs), FoldCross.slots(size.bs))
    dma = pltpu.SemaphoreType.DMA
    return pl.pallas_call(
        partial(backward_kernel, dps),
        out_shape=[jax.ShapeDtypeStruct((history, WIDE), wide)]
        + [jax.ShapeDtypeStruct((SECT, rows, LANES), low) for rows in kind_rows[:3]]
        + [jax.ShapeDtypeStruct((size.emb, LANES), low)],
        in_specs=[pl.BlockSpec(memory_space=pltpu.SMEM)] + [anywhere] * (6 + len(kept)),
        out_specs=[inside] + [anywhere] * 3 + [inside],
        scratch_shapes=[pltpu.VMEM(shape, dtype) for shape, dtype in scratch]
        + [
            dma((3,)),
            dma((12,)),
            dma(()),
            dma((3,)),
            dma((3,)),
            dma((3, SECT)),
            dma((3, SECT)),
            dma((4, slots)),
            dma((4, slots)),
            pltpu.SemaphoreType.REGULAR((4, slots)),
        ],
        compiler_params=pltpu.CompilerParams(
            collective_id=1, has_side_effects=True, vmem_limit_bytes=60 * 1024 * 1024
        ),
        name="backward_fold",
    )(groups, *weights, cotangent, x, wsel, *kept)


def finish_kernel(dps, n_gains, n_biases, *refs):
    size = Sizes(dps)
    given, refs = refs[:6], refs[6:]
    block_out, series_out, embed_w, embed_b, qkv, out, up_out, down_out, gains, biases = refs[:10]
    att, up, down, emb, sems = refs[10:]
    copies = copies_of(zip(given, (att, up, down, emb, block_out, series_out)), sems)
    copies_start(copies)
    copies_wait(copies[:4])
    for lb in range(SECT):
        lanes = slice(lb * LANES, (lb + 1) * LANES)
        qkv[:, lanes] = att[lb].astype(jnp.float32)
        out[:, lanes] = up[lb, : size.out].astype(jnp.float32)
        up_out[:, lanes] = up[lb, size.out :].astype(jnp.float32)
        for j in range(4):
            rows = slice(j * size.down, (j + 1) * size.down)
            start = j * WIDE + lb * LANES
            down_out[:, start : start + LANES] = down[lb, rows].astype(jnp.float32)
    vectors = emb[size.lookback :].astype(jnp.float32)
    count = -(-(n_gains + n_biases) // LANES)
    flat = jnp.concatenate([vectors[row : row + 1] for row in range(count)], axis=1)
    gains[...] = flat[:, :n_gains]
    biases[...] = flat[:, n_gains : n_gains + n_biases]
    rows = WIDE // (SECT * dps)
    packed = emb[: size.lookback].astype(jnp.float32)
    packed = [packed[i * rows : (i + 1) * rows] for i in range(6)]
    square = jnp.concatenate([packed[0], jnp.zeros((LANES - rows, LANES), jnp.float32)], axis=0)
    embed_b[...] = square.T[:GROUPS, :rows]
    packed = jnp.concatenate(packed, axis=1)
    ends = ((6 * LANES, L1), (5 * LANES, L2), (3 * LANES, L3))
    embed_w[...] = jnp.concatenate([packed[:, end - span : end] for end, span in ends], axis=1)
    copies_wait(copies[4:])


def finish_all(sums, block, series, n_gains, n_biases, dps):
    size = Sizes(dps)
    wide = jnp.float32
    columns = WIDE // (SECT * dps)
    outs = [
        (block.shape, block.dtype),
        (series.shape, wide),
        ((columns, L1 + L2 + L3), wide),
        ((GROUPS, columns), wide),
        ((size.qkv, WIDE), wide),
        ((size.out, WIDE), wide),
        ((size.up, WIDE), wide),
        ((size.down, 4 * WIDE), wide),
        ((1, n_gains), wide),
        ((1, n_biases), wide),
    ]
    anywhere = pl.BlockSpec(memory_space=pl.ANY)
    inside = pl.BlockSpec(memory_space=pltpu.VMEM)
    return pl.pallas_call(
        partial(finish_kernel, dps, n_gains, n_biases),
        out_shape=[jax.ShapeDtypeStruct(shape, dtype) for shape, dtype in outs],
        in_specs=[anywhere] * 6,
        out_specs=[inside] * 10,
        scratch_shapes=[pltpu.VMEM(array.shape, array.dtype) for array in sums]
        + [pltpu.SemaphoreType.DMA((6,))],
        compiler_params=pltpu.CompilerParams(vmem_limit_bytes=60 * 1024 * 1024),
        name="finish",
    )(*sums, block, series)


def per_device(
    series,
    groups,
    cotangent,
    embed_weight,
    embed_bias,
    qkv_weight,
    out_weight,
    up_weight,
    down_weight,
    gains,
    biases,
):
    dps = lax.axis_size("dp")
    given = (
        series[0],
        embed_weight.T,
        embed_bias,
        qkv_weight[0],
        out_weight[0],
        up_weight[0],
        down_weight[0],
        gains,
        biases,
    )
    block_output, att, up, down, wsel, x, *kept = forward_all(groups, given, dps)
    series_grad, *sums = backward_all(
        groups, (att, up, down), cotangent[0], x, wsel, kept, series.shape[1], dps
    )
    outs = finish_all(sums, block_output, series_grad, gains.shape[1], biases.shape[1], dps)
    block_output, series_grad, embed_w, embed_b, qkv, out, up, down, gain_sum, bias_sum = outs
    return (
        block_output[None],
        series_grad[None],
        embed_w.T,
        embed_b,
        qkv[None],
        out[None],
        up[None],
        down[None],
        gain_sum,
        bias_sum,
    )


def solution(mesh):
    return jax.shard_map(
        per_device,
        mesh=mesh,
        in_specs=(
            P(("pipe", "dp"), None, None),
            P(("pipe", "dp")),
            P(("pipe", "dp"), None, None),
            P(None, "dp"),
            P(None, "dp"),
            P("pipe", "dp", None),
            P("pipe", "dp", None),
            P("pipe", "dp", None),
            P("pipe", "dp", None),
            P("pipe", "dp"),
            P("pipe", "dp"),
        ),
        out_specs=(
            P(("pipe", "dp"), None, None),
            P(("pipe", "dp"), None, None),
            P(None, ("pipe", "dp")),
            P(None, ("pipe", "dp")),
            P("pipe", "dp", None),
            P("pipe", "dp", None),
            P("pipe", "dp", None),
            P("pipe", "dp", None),
            P("pipe", "dp"),
            P("pipe", "dp"),
        ),
        check_vma=False,
    )
```

```python
from functools import partial
import math

import jax
import jax.numpy as jnp
from jax import lax
from jax.experimental import pallas as pl
from jax.experimental.pallas import tpu as pltpu
from jax.sharding import PartitionSpec as P

HEAD = 64
L1 = 96
L2 = 192
L3 = 336
GROUPS = 3


NORM_EPS = 1e-05


MESH = pl.DeviceIdType.MESH
LANES = 128
ZS = 4
SECT = 4
EMB = 3


class Place:
    def __init__(self, dps):
        self.bs = bs = dps // ZS
        pipe = lax.axis_index("pipe")
        dp = lax.axis_index("dp")
        self.pipe, self.dp = pipe, dp
        self.x, self.c = x, c = lax.div(pipe, 2), lax.rem(pipe, 2)
        self.z, self.b = z, b = lax.div(dp, bs), lax.rem(dp, bs)
        self.block = c * 2 + x
        self.other_block = c * 2 + 1 - x
        self.x_peer = ((1 - x) * 2 + c, dp)
        self.core_peer = (x * 2 + 1 - c, dp)
        self.pipes = [lax.rem(pipe + k, SECT) for k in range(SECT)]
        self.blocks = [self.block_of(other) for other in self.pipes]
        self.zs = [lax.rem(z + k, ZS) for k in range(ZS)]
        self.bees = [lax.rem(b + k, bs) for k in range(bs)]
        self.z_peers = [(pipe, other * bs + b) for other in self.zs]
        self.b_peers = [(pipe, z * bs + other) for other in self.bees]

    def block_of(self, pipe):
        return lax.rem(pipe, 2) * 2 + lax.div(pipe, 2)

    def pipe_at(self, step):
        return self.pipes[step % SECT]

    def z_at(self, step):
        return self.zs[step % ZS]

    def b_at(self, step):
        return self.bees[step % self.bs]

    def z_peer(self, step):
        return self.z_peers[step % ZS]

    def b_peer(self, step):
        return self.b_peers[step % self.bs]

    def greet(self):
        barrier = pltpu.get_barrier_semaphore()
        peers = [(self.pipe_at(k), self.dp) for k in range(1, SECT)]
        peers += [self.z_peer(k) for k in range(1, ZS)]
        peers += [self.b_peer(k) for k in range(1, self.bs)]
        for peer in peers:
            pl.semaphore_signal(barrier, inc=1, device_id=peer, device_id_type=MESH)

    def met(self):
        pl.semaphore_wait(pltpu.get_barrier_semaphore(), SECT + ZS + self.bs - 3)


def remote(src, dst, send, recv, peer):
    return pltpu.make_async_remote_copy(
        src_ref=src, dst_ref=dst, send_sem=send, recv_sem=recv, device_id=peer, device_id_type=MESH
    )


FORWARD_START = (
    (0, 3, 0),
    (0, 0, 0),
    (0, 2, 0),
    (1, 3, 0),
    (1, 0, 0),
    (0, 1, 0),
    (2, 3, 0),
    (2, 0, 0),
    (0, 0, 1),
    (1, 1, 0),
    (1, 2, 0),
    (3, 3, 0),
    (0, 2, 1),
    (1, 0, 1),
    (2, 1, 0),
    (4, 3, 0),
    (3, 0, 0),
    ("embed",),
    (4, 0, 0),
)
FORWARD_PERIOD = (
    ("mix",),
    (0, 1, 1),
    (2, 0, 1),
    ("mix",),
    ("attend",),
    (3, 1, 0),
    ("attend",),
    (2, 2, 0),
    ("attend",),
    (0, 0, 2),
    (4, 1, 0),
    ("attend",),
    ("project",),
    (1, 1, 1),
    ("up",),
    (1, 2, 1),
    (0, 2, 2),
    (3, 2, 0),
    ("up",),
    (1, 0, 2),
    ("up",),
    (2, 1, 1),
    (3, 0, 1),
    (4, 2, 0),
    ("up",),
    ("down",),
    (4, 0, 1),
    ("down",),
)
BACKWARD_PERIOD = (
    ("norm2",),
    (1, 0, -1),
    ("down",),
    ("down",),
    ("gelu",),
    ("gelu",),
    (2, 1, -1),
    (0, 2, 0),
    ("up",),
    ("normed",),
    (2, 0, -1),
    ("norm1",),
    (4, 1, -2),
    (4, 2, -2),
    (1, 2, 0),
    (3, 1, -1),
    (0, 1, 0),
    ("attend",),
    ("attend",),
    ("attend",),
    ("attend",),
    (3, 2, -1),
    (1, 1, 0),
    (4, 0, -2),
    (3, 0, -1),
    ("mix",),
    ("mix",),
    (0, 0, 0),
    ("input",),
    (2, 2, 0),
)
BACKWARD_END = (
    ("embed",),
    (1, 0, 3),
    (2, 1, 3),
    (2, 0, 3),
    (4, 1, 2),
    (4, 2, 2),
    (3, 1, 3),
    (0, 3, 0),
    (3, 2, 3),
    (4, 0, 2),
    (1, 3, 0),
    (3, 0, 3),
    (2, 3, 0),
    (3, 3, 0),
    (4, 1, 3),
    (4, 2, 3),
    (4, 0, 3),
    (4, 3, 0),
)


def copies_start(copies):
    for copy in copies:
        copy.start()


def copies_begin(copies):
    for copy in copies:
        copy.start(priority=1)


def copies_wait(copies):
    for copy in copies:
        copy.wait()


class Spread:
    def __init__(self, at, out, send, recv, half=ZS // 2):
        self.at, self.out, self.send, self.recv = at, out, send, recv
        nb = at.bs - 1
        self.slot_z = 0
        self.slot_b1 = ZS - 1
        self.slot_x1 = self.slot_b1 + nb
        self.slot_x2 = self.slot_x1 + 1
        self.slot_b2 = self.slot_x2 + 1
        self.slot_c = self.slot_b2 + nb
        self.half = half

    @staticmethod
    def slots(bs):
        return ZS - 1 + 2 * (bs - 1) + 3

    def copy(self, region, slot, peer):
        return remote(region, region, self.send.at[slot], self.recv.at[slot], peer)

    def copies(self, stage, back):
        at, out, half = self.at, self.out, self.half
        rest = pl.ds(half, ZS - half)
        x_block = at.other_block if back else at.block
        if stage == 0:
            return [
                self.copy(
                    out.at[at.block, at.z_at(ZS - k) if back else at.z, at.b],
                    self.slot_z + k - 1,
                    at.z_peer(k),
                )
                for k in range(1, ZS)
            ]
        if stage == 3:
            core = 1 - at.c if back else at.c
            return [self.copy(out.at[pl.ds(core * 2, 2)], self.slot_c, at.core_peer)]
        copies = []
        for k in range(1, at.bs):
            b = at.b_at(at.bs - k) if back else at.b
            if stage == 1:
                region, slot = out.at[at.block, pl.ds(0, half), b], self.slot_b1
            else:
                region, slot = out.at[pl.ds(at.c * 2, 2), rest, b], self.slot_b2
            copies.append(self.copy(region, slot + k - 1, at.b_peer(k)))
        if stage == 1:
            region, slot = out.at[x_block, rest, at.b], self.slot_x1
        else:
            region, slot = out.at[x_block, pl.ds(0, half)], self.slot_x2
        copies.append(self.copy(region, slot, at.x_peer))
        return copies

    def start(self, stage):
        copies_start(self.copies(stage, False))

    def land(self, stage):
        for copy in self.copies(stage, True):
            copy.wait_recv()
        for copy in self.copies(stage, False):
            copy.wait_send()

    def move(self, stage):
        self.land(stage)
        self.start(stage + 1)


class SpreadCross(Spread):
    @staticmethod
    def slots(bs):
        return 2 * bs + 2 * ZS - 1

    def copies(self, stage, back):
        at, out = self.at, self.out
        rows = out.shape[-2]
        cut = rows // 32 * 16
        some, rest = pl.ds(0, cut), pl.ds(cut, rows - cut)
        core = 1 - at.c if back else at.c
        if stage == 3:
            return [self.copy(out.at[pl.ds(core * 2, 2)], 2 * at.bs + 2 * ZS - 2, at.core_peer)]
        both = pl.ds(at.c * 2, 2)
        x_block = at.other_block if back else at.block
        copies = []
        if stage == 1:
            for k in range(1, ZS):
                z = at.z_at(ZS - k) if back else at.z
                copies.append(self.copy(out.at[both, z, at.b, some], at.bs + k - 1, at.z_peer(k)))
                slot = at.bs + ZS + k - 2
                copies.append(self.copy(out.at[at.block, z, :, rest], slot, at.z_peer(k)))
            return copies
        base = 0 if stage == 0 else at.bs + 2 * ZS - 2
        for k in range(1, at.bs):
            b = at.b_at(at.bs - k) if back else at.b
            region = out.at[at.block, at.z, b, rest] if stage == 0 else out.at[both, :, b, some]
            copies.append(self.copy(region, base + k, at.b_peer(k)))
        if stage == 0:
            region = out.at[x_block, at.z, at.b, some]
        else:
            region = out.at[x_block, :, :, rest]
        copies.append(self.copy(region, base, at.x_peer))
        return copies


class Fold:
    def __init__(self, at, grads, total, landing, bufs, final, send, recv, credit, half):
        self.at, self.grads, self.total = at, grads, total
        self.landing, self.bufs, self.final = landing, bufs, final
        self.send, self.recv, self.credit = send, recv, credit
        self.half = half
        nb = at.bs - 1
        self.slot_x1 = 1
        self.slot_b1 = 2
        self.slot_x2 = 2 + nb
        self.slot_b2 = 3 + nb
        self.slot_z = 3 + 2 * nb

    @staticmethod
    def slots(bs):
        return 3 + 2 * (bs - 1) + ZS - 1

    @staticmethod
    def buffers(bs, rows, half):
        nb = max(bs - 1, 1)
        rest = ZS - half
        return [
            (half, bs, rows, LANES),
            (nb, 2, rest, rows, LANES),
            (rest, rows, LANES),
            (nb, half, rows, LANES),
            (ZS - 1, rows, LANES),
        ]

    def core_parts(self):
        other = self.grads.at[pl.ds((1 - self.at.c) * 2, 2)]
        return [(other, self.landing, 0, self.at.core_peer, self.at.core_peer)]

    def parts(self, stage):
        at, half, total, bufs = self.at, self.half, self.total, self.bufs
        if stage == 0:
            return self.core_parts()
        if stage == 3:
            return [
                (
                    total.at[at.x, at.z_at(k), at.b],
                    bufs[4].at[k - 1],
                    self.slot_z + k - 1,
                    at.z_peer(k),
                    at.z_peer(ZS - k),
                )
                for k in range(1, ZS)
            ]
        rest = pl.ds(half, ZS - half)
        found = []
        for k in range(1, at.bs):
            if stage == 1:
                src, buf, slot = total.at[:, rest, at.b_at(k)], bufs[1], self.slot_b1
            else:
                src, buf, slot = total.at[at.x, pl.ds(0, half), at.b_at(k)], bufs[3], self.slot_b2
            found.append((src, buf.at[k - 1], slot + k - 1, at.b_peer(k), at.b_peer(at.bs - k)))
        if stage == 1:
            src, buf, slot = total.at[1 - at.x, pl.ds(0, half)], bufs[0], self.slot_x1
        else:
            src, buf, slot = total.at[1 - at.x, rest, at.b], bufs[2], self.slot_x2
        found.append((src, buf, slot, at.x_peer, at.x_peer))
        return found

    def start(self, stage, again):
        for src, buf, slot, to, _ in self.parts(stage):
            if again is not False:

                @pl.when(again)
                def _():
                    pl.semaphore_wait(self.credit.at[slot], 1)

            remote(src, buf, self.send.at[slot], self.recv.at[slot], to).start()

    def land(self, stage, more):
        parts = self.parts(stage)
        for src, buf, slot, to, _ in parts:
            remote(src, buf, self.send.at[slot], self.recv.at[slot], to).wait()
        self.add(stage)
        if more is not False:

            @pl.when(more)
            def _():
                for _, _, slot, _, origin in parts:
                    pl.semaphore_signal(
                        self.credit.at[slot], inc=1, device_id=origin, device_id_type=MESH
                    )

    def add_core(self):
        at, bs, total = self.at, self.at.bs, self.total

        @pl.loop(0, 2 * ZS * bs)
        def _(i):
            z, b = i // bs % ZS, i % bs
            x = i // (ZS * bs)
            total[x, z, b] = self.grads[at.c * 2 + x, z, b] + self.landing[x, z, b]

    def add(self, stage):
        at, half, bs = self.at, self.half, self.at.bs
        total, bufs = self.total, self.bufs
        rest = ZS - half
        if stage == 0:
            self.add_core()
        elif stage == 1:

            @pl.loop(0, half * bs)
            def _(i):
                z, b = i // bs, i % bs
                total[at.x, z, b] = total[at.x, z, b] + bufs[0][z, b]

            @pl.loop(0, 2 * rest)
            def _(i):
                x, z = i // rest, i % rest
                for k in range(bs - 1):
                    total[x, half + z, at.b] = total[x, half + z, at.b] + bufs[1][k, x, z]

        elif stage == 2:

            @pl.loop(0, rest)
            def _(z):
                total[at.x, half + z, at.b] = total[at.x, half + z, at.b] + bufs[2][z]

            @pl.loop(0, half)
            def _(z):
                for k in range(bs - 1):
                    total[at.x, z, at.b] = total[at.x, z, at.b] + bufs[3][k, z]

        else:
            self.finish([bufs[4][k] for k in range(ZS - 1)])

    def finish(self, pieces):
        at = self.at
        done = self.total[at.x, at.z, at.b].astype(jnp.float32)
        for piece in pieces:
            done = done + piece.astype(jnp.float32)
        self.final[...] = done.astype(self.final.dtype)

    def move(self, stage, again, more):
        self.land(stage, more)
        self.start(stage + 1, again)


class FoldCross(Fold):
    @staticmethod
    def slots(bs):
        return 2 * bs + 2 * ZS - 1

    @staticmethod
    def buffers(bs, rows, half):
        nb = max(bs - 1, 1)
        cut = rows // 32 * 16
        rest = rows - cut
        return [
            (nb, 2, ZS, cut, LANES),
            (ZS, bs, rest, LANES),
            (ZS - 1, 2, cut, LANES),
            (ZS - 1, bs, rest, LANES),
            (cut, LANES),
            (nb, rest, LANES),
        ]

    def cuts(self):
        rows = self.total.shape[-2]
        cut = rows // 32 * 16
        return pl.ds(0, cut), pl.ds(cut, rows - cut)

    def parts(self, stage):
        at, total, bufs = self.at, self.total, self.bufs
        if stage == 0:
            return self.core_parts()
        some, rest = self.cuts()
        found = []
        if stage == 2:
            for k in range(1, ZS):
                pair = (at.z_peer(k), at.z_peer(ZS - k))
                z = at.z_at(k)
                found.append((total.at[:, z, at.b, some], bufs[2].at[k - 1], at.bs + k, *pair))
                slot = at.bs + ZS + k - 1
                found.append((total.at[at.x, z, :, rest], bufs[3].at[k - 1], slot, *pair))
            return found
        base = 1 if stage == 1 else at.bs + 2 * ZS - 1
        for k in range(1, at.bs):
            pair = (at.b_peer(k), at.b_peer(at.bs - k))
            if stage == 1:
                src, buf = total.at[:, :, at.b_at(k), some], bufs[0].at[k - 1]
            else:
                src, buf = total.at[at.x, at.z, at.b_at(k), rest], bufs[5].at[k - 1]
            found.append((src, buf, base + k, *pair))
        if stage == 1:
            src, buf = total.at[1 - at.x, :, :, rest], bufs[1]
        else:
            src, buf = total.at[1 - at.x, at.z, at.b, some], bufs[4]
        found.append((src, buf, base, at.x_peer, at.x_peer))
        return found

    def add(self, stage):
        at, bs = self.at, self.at.bs
        total, bufs = self.total, self.bufs
        some, rest = self.cuts()
        if stage == 0:
            self.add_core()
        elif stage == 1:

            @pl.loop(0, 2 * ZS)
            def _(i):
                x, z = i // ZS, i % ZS
                for k in range(bs - 1):
                    total[x, z, at.b, some] = total[x, z, at.b, some] + bufs[0][k, x, z]

            @pl.loop(0, ZS * bs)
            def _(i):
                z, b = i // bs, i % bs
                total[at.x, z, b, rest] = total[at.x, z, b, rest] + bufs[1][z, b]

        elif stage == 2:
            for x in range(2):
                for k in range(ZS - 1):
                    total[x, at.z, at.b, some] = total[x, at.z, at.b, some] + bufs[2][k, x]

            @pl.loop(0, bs)
            def _(b):
                for k in range(ZS - 1):
                    total[at.x, at.z, b, rest] = total[at.x, at.z, b, rest] + bufs[3][k, b]

        else:
            total[at.x, at.z, at.b, some] = total[at.x, at.z, at.b, some] + bufs[4][...]
            for k in range(bs - 1):
                total[at.x, at.z, at.b, rest] = total[at.x, at.z, at.b, rest] + bufs[5][k]
            self.final[...] = total[at.x, at.z, at.b]


HALF = 256
WIDE = 512
QKV_TILE = 768
VEC_ROWS = 16


STEP = 64


def by_rows(fn, *arrays, step=STEP):
    parts = [
        fn(*[array[at : at + step] for array in arrays])
        for at in range(0, arrays[0].shape[0], step)
    ]
    if isinstance(parts[0], tuple):
        return tuple(jnp.concatenate(part, axis=0) for part in zip(*parts))
    return jnp.concatenate(parts, axis=0)


def dot_nt(a, b):
    return lax.dot_general(a, b, (((1,), (1,)), ((), ())), preferred_element_type=jnp.float32)


def dot_nn(a, b):
    return lax.dot_general(a, b, (((1,), (0,)), ((), ())), preferred_element_type=jnp.float32)


def dot_tn(a, b):
    return lax.dot_general(a, b, (((0,), (0,)), ((), ())), preferred_element_type=jnp.float32)


def aligned(index, unit):
    return pl.multiple_of(index, unit)


def rows_of(ref, bs, first, count, start, rows, blocks=range(SECT)):
    parts = []
    for i in range(count):
        d = first + i
        place = (d // bs, d % bs)
        parts.append(
            jnp.concatenate(
                [ref[(lb,) + place + (pl.ds(start, rows), slice(None))] for lb in blocks], axis=1
            )
        )
    return parts[0] if count == 1 else jnp.concatenate(parts, axis=0)


def put_rows(ref, bs, first, count, start, rows, value, block=0):
    value = value.astype(ref.dtype)
    for i in range(count):
        d = first + i
        place = (d // bs, d % bs)
        for lane in range(value.shape[1] // LANES):
            ref[(block + lane,) + place + (pl.ds(start, rows), slice(None))] = value[
                i * rows : (i + 1) * rows, lane * LANES : (lane + 1) * LANES
            ]


def vector_pieces(dps):
    n_gains, n_biases = 2 * WIDE // dps, 10 * WIDE // dps
    starts = [(0, 0), (0, 2), (1, 0), (1, 2), (2, 0), (2, 1), (2, 2), (2, 3), (3, 0), (3, 2)]
    pieces = []
    for d in range(dps):
        at = 0
        while at < n_gains + n_biases:
            if at < n_gains:
                index = d * n_gains + at
                row, column = (1, 3)[index // WIDE], WIDE + index % WIDE
                left = n_gains - at
            else:
                index = d * n_biases + at - n_gains
                row, part = starts[index // WIDE]
                column = part * WIDE + index % WIDE
                left = n_gains + n_biases - at
            size = min(left, LANES - at % LANES, LANES - column % LANES)
            pieces.append((d, at // LANES, at % LANES, row, column, size))
            at += size
    return pieces


def read_vectors(ref, table, bs, start, block):
    tiles = {}
    for d, row, lane, to_row, to_lane, size in vector_pieces(ZS * bs):
        if d not in tiles:
            tile = ref[block, d // bs, d % bs, start : start + VEC_ROWS, :]
            tiles[d] = tile.astype(jnp.float32)
        table[to_row : to_row + 1, to_lane : to_lane + size] = tiles[d][
            row : row + 1, lane : lane + size
        ]


def rows_tile(lines):
    row_id = lax.broadcasted_iota(jnp.int32, (VEC_ROWS, LANES), 0)
    tile = jnp.zeros((VEC_ROWS, LANES), jnp.float32)
    for row, pieces in enumerate(lines):
        have = sum(piece.shape[1] for piece in pieces)
        if have < LANES:
            pieces = pieces + [jnp.zeros((1, LANES - have), jnp.float32)]
        line = pieces[0] if len(pieces) == 1 else jnp.concatenate(pieces, axis=1)
        tile = jnp.where(row_id == row, line, tile)
    return tile


def vector_tile(table, dps, place):
    lines = []
    for d, row, lane, to_row, to_lane, size in vector_pieces(dps):
        if d == place:
            if row == len(lines):
                lines.append([])
            lines[row].append(table[to_row : to_row + 1, to_lane : to_lane + size])
    return rows_tile(lines)


def fold_rows(x):
    total = x[:8]
    for at in range(8, x.shape[0], 8):
        total = total + x[at : at + 8]
    return total


def normalize(x):
    mean = jnp.mean(x, axis=1, keepdims=True)
    centred = x - mean
    scale = lax.rsqrt(jnp.mean(centred * centred, axis=1, keepdims=True) + NORM_EPS)
    return centred * scale, jnp.broadcast_to(scale, (x.shape[0], LANES))


def normalize_back(unit, scale, grad, gain):
    inner = grad * gain
    first = jnp.mean(inner, axis=1, keepdims=True)
    second = jnp.mean(inner * unit, axis=1, keepdims=True)
    out = jnp.concatenate([scale] * (WIDE // LANES), axis=1) * (inner - first - unit * second)
    return out, fold_rows(out), fold_rows(grad * unit), fold_rows(grad)


def gelu_pair(u):
    below = 0.5 + 0.5 * lax.erf(u * math.sqrt(0.5))
    bell = jnp.exp2((-0.5 * math.log2(math.e)) * (u * u))
    return u * below, below + u * (bell * (1.0 / math.sqrt(2.0 * math.pi)))


def head_masks(scale):
    lane = lax.broadcasted_iota(jnp.int32, (1, LANES), 1)
    first = jnp.where(lane < HEAD, scale, 0.0).astype(jnp.bfloat16)
    second = jnp.where(lane < HEAD, 0.0, scale).astype(jnp.bfloat16)
    return first, second


class Sizes:
    def __init__(self, dps):
        self.dps, self.bs = dps, dps // ZS
        self.qkv, self.out, self.up, self.down = (
            3 * WIDE // dps,
            WIDE // dps,
            4 * WIDE // dps,
            WIDE // dps,
        )
        self.lookback = -(-6 * WIDE // (SECT * dps) // VEC_ROWS) * VEC_ROWS
        self.emb = self.lookback + VEC_ROWS
        self.dense = self.out + self.up
        self.wide = 4 * self.down


def qkv_rows(size, w, tile):
    count = QKV_TILE // size.qkv
    return rows_of(w, size.bs, tile * count, count, 0, size.qkv)


def out_rows(size, w):
    return rows_of(w, size.bs, 0, size.dps, 0, size.out)


def up_rows(size, w, tile):
    count = HALF // size.up
    return rows_of(w, size.bs, tile * count, count, size.out, size.up)


def forward_mix(size, w, table, h, mixed, piece):
    columns = slice(piece * QKV_TILE, (piece + 1) * QKV_TILE)
    shift = table[0:1, columns]
    out = dot_nt(h[...], qkv_rows(size, w, piece))
    mixed[:, columns] = by_rows(lambda part: (part + shift).astype(mixed.dtype), out)


def softmax_columns(scores):
    parts = [scores[at : at + STEP] for at in range(0, scores.shape[0], STEP)]
    top = parts[0]
    for part in parts[1:]:
        top = jnp.maximum(top, part)
    top = jnp.max(top, axis=0, keepdims=True)
    parts = [jnp.exp(part - top) for part in parts]
    total = parts[0]
    for part in parts[1:]:
        total = total + part
    scale = 1.0 / jnp.sum(total, axis=0, keepdims=True)
    return jnp.concatenate([(part * scale).astype(jnp.bfloat16) for part in parts], axis=0)


def forward_attend(mixed, probs, attended, pair):
    lane = pair * LANES
    key_rows = mixed[:, WIDE + lane : WIDE + lane + LANES]
    values = mixed[:, 2 * WIDE + lane : 2 * WIDE + lane + LANES].T

    for part in range(2):
        rows = slice(part * HALF, (part + 1) * HALF)
        queries = mixed[rows, lane : lane + LANES]
        joined = []
        for head, mask in enumerate(head_masks(1.0 / math.sqrt(HEAD))):
            weights = softmax_columns(dot_nt(key_rows, queries * mask))
            probs[2 * pair + head, :, rows] = weights
            joined.append(dot_nn(values[head * HEAD : (head + 1) * HEAD], weights))
        joined = jnp.concatenate(joined, axis=0).T
        attended[rows, lane : lane + LANES] = joined.astype(attended.dtype)


def forward_project(size, w, table, h, attended, first, scale, normed):
    out = dot_nt(attended[...], out_rows(size, w))
    for part in range(WIDE // STEP):
        rows = slice(part * STEP, (part + 1) * STEP)
        total = h[rows, :].astype(jnp.float32) + (out[rows] + table[1:2, 0:WIDE])
        unit, scale[rows, :] = normalize(total)
        first[rows, :] = unit
        normed[rows, :] = (
            unit * table[1:2, WIDE : 2 * WIDE] + table[1:2, 2 * WIDE : 3 * WIDE]
        ).astype(normed.dtype)


def forward_up(size, w, table, normed, slope, hidden, piece):
    for j in (2 * piece, 2 * piece + 1):
        columns = slice(j * HALF, (j + 1) * HALF)
        shift = table[2:3, columns]
        upper = dot_nt(normed[...], up_rows(size, w, j))
        for part in range(WIDE // STEP):
            rows = slice(part * STEP, (part + 1) * STEP)
            value, grad = gelu_pair(upper[rows] + shift)
            hidden[rows, columns] = value.astype(hidden.dtype)
            slope[rows, columns] = grad.astype(slope.dtype)


def forward_down(size, w, table, normed, hidden, second, scale, h, piece):
    columns = slice(piece * HALF, (piece + 1) * HALF)
    count = size.dps // 2
    matrix = jnp.concatenate(
        [
            rows_of(w, size.bs, piece * count, count, j * size.down, size.down)
            for j in range(4)
        ],
        axis=1,
    )
    out = dot_nt(hidden[...], matrix)
    shift = table[3:4, columns]
    for part in range(WIDE // STEP):
        rows = slice(part * STEP, (part + 1) * STEP)
        second[rows, columns] = normed[rows, columns].astype(jnp.float32) + (out[rows] + shift)
    if piece == 1:
        for part in range(WIDE // STEP):
            rows = slice(part * STEP, (part + 1) * STEP)
            unit, scale[rows, :] = normalize(second[rows, :])
            second[rows, :] = unit
            h[rows, :] = (
                unit * table[3:4, WIDE : 2 * WIDE] + table[3:4, 2 * WIDE : 3 * WIDE]
            ).astype(h.dtype)


def backward_norm_two(table, dtable, dy, second, scale, dnormed, dlow, dlow_t):
    dtable[...] = jnp.zeros_like(dtable)
    sums = [jnp.zeros((8, WIDE), jnp.float32)] * 3
    for part in range(WIDE // STEP):
        rows = slice(part * STEP, (part + 1) * STEP)
        grad, *found = normalize_back(
            second[rows, :],
            scale[rows, :],
            dy[rows, :].astype(jnp.float32),
            table[3:4, WIDE : 2 * WIDE],
        )
        dnormed[rows, :] = grad
        dlow[rows, :] = grad.astype(dlow.dtype)
        sums = [total + new for total, new in zip(sums, found)]
    for i, total in enumerate(sums):
        dtable[3:4, i * WIDE : (i + 1) * WIDE] = jnp.sum(total, axis=0, keepdims=True)
    dlow_t[...] = dlow[...].T


def backward_down(size, grads, hidden, dlow_t, piece):
    @pl.loop(2 * piece, 2 * piece + 2)
    def _(i):
        start = aligned(i * size.down, 16)
        for half in range(2):
            columns = pl.ds(aligned(i * WIDE, WIDE) + half * HALF, HALF)
            value = dot_nn(dlow_t[...], hidden[:, columns])
            put_rows(grads, size.bs, 0, size.dps, start, size.down, value, 2 * half)


def backward_gelu(size, w, dtable, slope, dlow, dup, piece):
    @pl.loop(2 * piece, 2 * piece + 2)
    def _(i):
        start = aligned(i * size.down, 16)
        for half in range(2):
            columns = pl.ds(aligned(i * WIDE, WIDE) + half * HALF, HALF)
            blocks = (2 * half, 2 * half + 1)
            matrix = rows_of(w, size.bs, 0, size.dps, start, size.down, blocks)
            dhidden = dot_nn(dlow[...], matrix)
            total = jnp.zeros((8, HALF), jnp.float32)
            for part in range(WIDE // STEP):
                rows = slice(part * STEP, (part + 1) * STEP)
                dupper = dhidden[rows] * slope[rows, columns].astype(jnp.float32)
                total = total + fold_rows(dupper)
                dup[rows, columns] = dupper.astype(dup.dtype)
            dtable[2:3, columns] = jnp.sum(total, axis=0, keepdims=True)


def backward_up(size, grads, normed, dup):
    count = HALF // size.up

    @pl.loop(0, 4)
    def _(i):
        for half in range(2):
            columns = pl.ds(aligned(i * WIDE, WIDE) + half * HALF, HALF)
            value = dot_tn(dup[:, columns], normed[...])
            first = (2 * i + half) * count
            put_rows(grads, size.bs, first, count, size.out, size.up, value)


def backward_normed(size, w, dnormed, dup):
    for half in range(2):
        columns = slice(half * HALF, (half + 1) * HALF)
        blocks = (2 * half, 2 * half + 1)
        matrix = rows_of(w, size.bs, 0, size.dps, size.out, size.up, blocks)
        out = dot_nn(dup[...], matrix)
        for part in range(WIDE // STEP):
            rows = slice(part * STEP, (part + 1) * STEP)
            dnormed[rows, columns] = dnormed[rows, columns] + out[rows]


def backward_norm_one(
    size, w, table, grads, dtable, first, scale, attended, dnormed, dlow, dlow_t, delta
):
    sums = [jnp.zeros((8, WIDE), jnp.float32)] * 3
    for part in range(WIDE // STEP):
        rows = slice(part * STEP, (part + 1) * STEP)
        grad, *found = normalize_back(
            first[rows, :], scale[rows, :], dnormed[rows, :], table[1:2, WIDE : 2 * WIDE]
        )
        dnormed[rows, :] = grad
        dlow[rows, :] = grad.astype(dlow.dtype)
        sums = [total + new for total, new in zip(sums, found)]
    for i, total in enumerate(sums):
        dtable[1:2, i * WIDE : (i + 1) * WIDE] = jnp.sum(total, axis=0, keepdims=True)
    dlow_t[...] = dlow[...].T
    for block in (0, 2):
        columns = slice(block * LANES, (block + 2) * LANES)
        value = dot_nn(dlow_t[...], attended[:, columns])
        put_rows(grads, size.bs, 0, size.dps, 0, size.out, value, block)
    grad = dot_nn(dlow[...], out_rows(size, w)).astype(dlow.dtype)
    dlow[...] = grad
    product = grad.astype(jnp.float32) * attended[...].astype(jnp.float32)
    high = product.astype(jnp.bfloat16)
    rest = (product - high.astype(jnp.float32)).astype(jnp.bfloat16)
    head = lax.broadcasted_iota(jnp.int32, delta.shape, 0)
    lane = lax.broadcasted_iota(jnp.int32, delta.shape, 1)
    inside = (lane >= head * HEAD) & (lane < (head + 1) * HEAD)
    inside = jnp.where(inside, 1.0, 0.0).astype(jnp.bfloat16)
    delta[...] = dot_nt(inside, high) + dot_nt(inside, rest)


def backward_attend(mixed, probs, delta, dtable, dlow, dmixed, pair):
    scale = 1.0 / math.sqrt(HEAD)
    lane = pair * LANES
    columns = slice(lane, lane + LANES)
    key_columns = slice(WIDE + lane, WIDE + lane + LANES)
    value_columns = slice(2 * WIDE + lane, 2 * WIDE + lane + LANES)
    keys_t = mixed[:, key_columns].T
    values = mixed[:, value_columns]
    dkeys = jnp.zeros((WIDE, LANES), jnp.float32)
    dvalues = jnp.zeros((WIDE, LANES), jnp.float32)
    for part in range(2):
        rows = slice(part * HALF, (part + 1) * HALF)
        queries = mixed[rows, columns]
        grad_out = dlow[rows, columns]
        dqueries = []
        for head in range(2):
            query = queries * head_masks(scale)[head]
            grad = grad_out * head_masks(1.0)[head]
            at = 2 * pair + head
            weights = probs[at, :, rows]
            less = delta[at : at + 1, rows]
            dprobs = dot_nt(values, grad)
            dscores = by_rows(
                lambda p, dp: (p.astype(jnp.float32) * (dp - less)).astype(jnp.bfloat16),
                weights,
                dprobs,
            )
            dvalues = dvalues + dot_nn(weights, grad)
            dkeys = dkeys + dot_nn(dscores, query)
            dqueries.append(dot_nn(keys_t[head * HEAD : (head + 1) * HEAD], dscores))
        dquery = jnp.concatenate(dqueries, axis=0).T * scale
        dtable[0:1, columns] += jnp.sum(dquery, axis=0, keepdims=True)
        dmixed[rows, columns] = dquery.astype(dmixed.dtype)
    dmixed[:, key_columns] = dkeys.astype(dmixed.dtype)
    dmixed[:, value_columns] = dvalues.astype(dmixed.dtype)
    dtable[0:1, value_columns] = jnp.sum(dvalues, axis=0, keepdims=True)


def backward_mix(size, grads, h, dmixed, piece):
    count = QKV_TILE // size.qkv
    grad = dmixed[:, piece * QKV_TILE : (piece + 1) * QKV_TILE]
    put_rows(grads, size.bs, piece * count, count, 0, size.qkv, dot_tn(grad, h[...]))


def backward_input(size, w, dnormed, dmixed, dy):
    for half in range(2):
        columns = slice(half * HALF, (half + 1) * HALF)
        blocks = (2 * half, 2 * half + 1)
        matrix = rows_of(w, size.bs, 0, size.dps, 0, size.qkv, blocks)
        out = dot_nn(dmixed[...], matrix)
        for part in range(WIDE // STEP):
            rows = slice(part * STEP, (part + 1) * STEP)
            dy[rows, columns] = (dnormed[rows, columns] + out[rows]).astype(dy.dtype)


WINDOW = 384


def group_rows(group):
    rows = lax.broadcasted_iota(jnp.int32, (16, LANES), 0)
    return jnp.where(rows == group, 1.0, 0.0).astype(jnp.bfloat16)


def pack_mix(piece, qkv):
    for lb in range(SECT):
        piece[lb] = qkv[:, lb * LANES : (lb + 1) * LANES].astype(piece.dtype)


def pack_up(piece, out, up):
    rows = out.shape[0]
    for lb in range(SECT):
        lanes = slice(lb * LANES, (lb + 1) * LANES)
        piece[lb, :rows] = out[:, lanes].astype(piece.dtype)
        piece[lb, rows:] = up[:, lanes].astype(piece.dtype)


def pack_down(piece, down):
    rows = down.shape[0]
    for lb in range(SECT):
        for j in range(4):
            start = j * WIDE + lb * LANES
            piece[lb, j * rows : (j + 1) * rows] = down[:, start : start + LANES].astype(piece.dtype)


def pack_embedding(piece, weight, shift, gains, biases, square, block):
    n = weight.shape[0]
    square[...] = jnp.zeros_like(square)
    square[:GROUPS, :n] = shift[...]

    def ending(part, width):
        return jnp.concatenate([jnp.zeros((n, width - part.shape[1]), part.dtype), part], axis=1)

    third = ending(weight[:, L1 + L2 :], 3 * LANES)
    second = ending(weight[:, L1 : L1 + L2], 2 * LANES)
    blocks = [third[:, :LANES] + square[...].T[:n]]
    blocks += [third[:, LANES : 2 * LANES], third[:, 2 * LANES :]]
    blocks += [second[:, :LANES], second[:, LANES:], ending(weight[:, :L1], LANES)]
    rows = piece.shape[1] - VEC_ROWS
    if SECT * rows > 6 * n:
        blocks.append(jnp.zeros((SECT * rows - 6 * n, LANES), jnp.float32))
    flat = jnp.concatenate(blocks, axis=0).astype(piece.dtype)
    for lb in range(SECT):
        piece[lb, :rows] = flat[lb * rows : (lb + 1) * rows]
    line = jnp.concatenate([gains[...], biases[...]], axis=1)
    lines = [[line[:, at : at + LANES]] for at in range(0, line.shape[1], LANES)]
    piece[block, rows:] = rows_tile(lines).astype(piece.dtype)


def expand(series, group, x):
    empty = jnp.zeros((WINDOW - series.shape[0], series.shape[1]), series.dtype)
    x[:, :WINDOW] = jnp.concatenate([empty, series[...]], axis=0).T
    lane = lax.broadcasted_iota(jnp.int32, (x.shape[0], LANES), 1)
    x[:, WINDOW:] = jnp.where(lane == group, 1.0, 0.0).astype(x.dtype)


def embed(size, emb, pick, x, wsel, h):
    n = WIDE // size.dps
    flat = []
    for d in range(size.dps):
        place = (d // size.bs, d % size.bs, slice(0, size.lookback), slice(None))
        flat.append(jnp.concatenate([emb[(lb,) + place] for lb in range(SECT)], axis=0))
    blocks = [
        jnp.concatenate([rows[j * n : (j + 1) * n] for rows in flat], axis=0) for j in range(6)
    ]
    long, middle, short = (pick[g : g + 1, :] for g in (2, 1, 0))
    wide = jnp.concatenate(
        [
            blocks[0] * long,
            blocks[1] * long + blocks[3] * middle,
            blocks[2] * long + blocks[4] * middle + blocks[5] * short,
        ],
        axis=1,
    )
    wsel[...] = wide.T
    h[...] = dot_nt(x[...], jnp.concatenate([wide, blocks[0]], axis=1)).astype(h.dtype)


def embed_back(size, pick, x, wsel, dh, tables, grads, series_grad):
    history = series_grad.shape[0]
    series_grad[...] = dot_nt(wsel[...], dh[...])[WINDOW - history :]
    sums = dot_tn(dh[...], x[...])
    long, middle, short = (pick[g : g + 1, :].astype(jnp.float32) for g in (2, 1, 0))
    parts = [sums[:, i * LANES : (i + 1) * LANES] for i in range(4)]
    parts = [
        parts[0] * long + parts[3],
        parts[1] * long,
        parts[2] * long,
        parts[1] * middle,
        parts[2] * middle,
        parts[2] * short,
    ]
    rows = WIDE // (SECT * size.dps)
    spare = size.lookback - 6 * rows
    for pipe in range(SECT):
        block = (pipe % 2) * 2 + pipe // 2
        for dp in range(size.dps):
            start = (pipe * size.dps + dp) * rows
            pieces = [part[start : start + rows] for part in parts]
            if spare:
                pieces.append(jnp.zeros((spare, LANES), jnp.float32))
            pieces.append(vector_tile(tables.at[pipe], size.dps, dp))
            piece = jnp.concatenate(pieces, axis=0)
            grads[block, dp // size.bs, dp % size.bs] = piece.astype(grads.dtype)


def saved_shapes():
    low, wide = jnp.bfloat16, jnp.float32
    return [
        ((WIDE, WIDE), low),
        ((WIDE, 3 * WIDE), low),
        ((2 * SECT, WIDE, WIDE), low),
        ((WIDE, WIDE), low),
        ((WIDE, WIDE), wide),
        ((WIDE, WIDE), low),
        ((WIDE, 4 * WIDE), low),
        ((WIDE, 4 * WIDE), low),
        ((WIDE, WIDE), wide),
        ((SECT, 4 * WIDE), wide),
        ((WIDE, LANES), wide),
        ((WIDE, LANES), wide),
    ]


def chunk_shape(size, rows):
    return (SECT, ZS, size.bs, rows, LANES)


HALVES = (2, 2, 2, 2)
CROSS = (2,)


def follow(plan, section, act, compute):
    seen = {}
    for step in plan:
        if len(step) == 1:
            piece = seen.get(step[0], 0)
            seen[step[0]] = piece + 1
            compute(step[0], piece)
            continue
        op, kind, offset = step
        where = section + offset
        if isinstance(where, int):
            if 0 <= where < SECT:
                act(op, kind, where)
        elif offset == 0:
            act(op, kind, where)
        else:
            inside = where < SECT if offset > 0 else where >= 0

            @pl.when(inside)
            def _():
                act(op, kind, where)


def forward_kernel(dps, groups, *refs):
    size = Sizes(dps)
    given, refs = refs[:9], refs[9:]
    out, copies_out, wsel, x, refs = refs[0], refs[1:4], refs[4], refs[5], refs[6:]
    kept, local, refs = refs[:12], refs[12:24], refs[24:]
    wholes, refs = refs[:4], refs[4:]
    pieces, held, refs = refs[:4], refs[4:13], refs[13:]
    emb_rows, pick, refs = refs[0], refs[1], refs[2:]
    given_sem, out_sem, kept_sem, own_sem, p_send, p_recv, send, recv = refs
    h, mixed, probs, attended, first, normed, slope, hidden, second, table, scale_1, scale_2 = local
    at = Place(dps)

    own = [
        pltpu.make_async_copy(
            pieces[kind].at[at.block],
            wholes[kind].at[at.pipe, at.block, at.z, at.b]
            if kind < EMB
            else wholes[kind].at[at.block, at.z, at.b],
            own_sem.at[kind],
        )
        for kind in range(4)
    ]
    def split(kind, back):
        copies = []
        for k in range(1, SECT):
            if back:
                region = wholes[kind].at[at.pipe_at(SECT - k), at.block, at.z, at.b]
                src = region
            else:
                block = at.blocks[k]
                region = wholes[kind].at[at.pipe, block, at.z, at.b]
                src = pieces[kind].at[block]
            sems = p_send.at[kind, k - 1], p_recv.at[kind, k - 1]
            copies.append(remote(src, region, *sems, (at.pipe_at(k), at.dp)))
        return copies

    def chunk(kind, section):
        if kind == EMB:
            return Spread(at, wholes[kind], send.at[3 * SECT], recv.at[3 * SECT])
        number = 3 * section + kind
        sort = SpreadCross if kind in CROSS else Spread
        return sort(at, wholes[kind].at[section], send.at[number], recv.at[number], HALVES[kind])

    def keep(kind, section):
        src, dst = wholes[kind].at[section], copies_out[kind].at[section]
        return pltpu.make_async_copy(src, dst, out_sem.at[kind, section])

    arrived = []

    def act(op, kind, section):
        if op == 0:
            if kind not in arrived:
                arrived.append(kind)
                own[kind].wait()
                if kind == EMB:
                    chunk(kind, section).start(0)
                    return
                for copy in split(kind, True):
                    copy.wait_recv()
                for copy in split(kind, False):
                    copy.wait_send()
                if kind == 0:
                    copies_start(split(1, False))
                    copies_start(split(2, False))
            chunk(kind, section).start(0)
        elif op < 4:
            chunk(kind, section).move(op - 1)
            if op == 1 and kind == EMB:
                gets[0].wait()
                expand(series, groups[0], x)
        else:
            chunk(kind, section).land(3)
            if kind != EMB:
                keep(kind, section).start(priority=1)

    def saves(section, early):
        which = (1, 2, 3, 4, 5, 9, 10) if early else (6, 7, 8, 11)
        return [
            pltpu.make_async_copy(local[i], kept[i].at[section], kept_sem.at[i]) for i in which
        ]

    series, embed_weight, embed_bias, qkv, out_w, up_w, down_w, gains, biases = held
    gets = copies_of(zip(given, held), given_sem)
    for i in (3, 7, 8, 1, 2, 4, 5, 6, 0):
        gets[i].start(priority=1)
    pick[...] = group_rows(groups[0])
    at.greet()
    gets[3].wait()
    pack_mix(pieces[0], qkv)
    own[0].start(priority=1)
    at.met()
    copies_start(split(0, False))
    copies_wait(gets[1:3] + gets[7:9])
    pack_embedding(
        pieces[EMB], embed_weight, embed_bias, gains, biases, emb_rows, at.block
    )
    own[EMB].start(priority=1)
    copies_wait(gets[4:7])
    pack_up(pieces[1], out_w, up_w)
    own[1].start(priority=1)
    pack_down(pieces[2], down_w)
    own[2].start(priority=1)
    table[...] = jnp.zeros_like(table)

    def before(name, piece):
        embed(size, wholes[EMB], pick, x, wsel, h)

    follow(FORWARD_START, 0, act, before)

    @pl.loop(0, SECT)
    def _(section):
        att, up, down = (ref.at[section] for ref in wholes[:3])
        keep_h = pltpu.make_async_copy(h, kept[0].at[section], kept_sem.at[0])

        def compute(name, piece):
            if name == "mix":
                if piece == 0:

                    @pl.when(section > 0)
                    def _():
                        copies_wait(saves(section - 1, True))

                    keep_h.start(priority=1)
                    block = section % 2 * 2 + section // 2
                    read_vectors(wholes[EMB], table, size.bs, size.lookback, block)
                forward_mix(size, att, table, h, mixed, piece)
            elif name == "attend":
                forward_attend(mixed, probs, attended, piece)
            elif name == "project":
                forward_project(size, up, table, h, attended, first, scale_1, normed)
                copies_begin(saves(section, True))
            elif name == "up":
                if piece == 0:

                    @pl.when(section > 0)
                    def _():
                        copies_wait(saves(section - 1, False))

                forward_up(size, up, table, normed, slope, hidden, piece)
            else:
                if piece == 0:
                    keep_h.wait()
                forward_down(size, down, table, normed, hidden, second, scale_2, h, piece)
                if piece == 1:
                    copies_begin(saves(section, False))

        follow(FORWARD_PERIOD, section, act, compute)

    out[...] = h[...]
    copies_wait(saves(SECT - 1, True))
    copies_wait(saves(SECT - 1, False))
    for kind in range(3):
        copies_wait([keep(kind, section) for section in range(SECT)])


def copies_of(pairs, sems):
    return [pltpu.make_async_copy(src, dst, sems.at[i]) for i, (src, dst) in enumerate(pairs)]


def forward_all(groups, given, dps):
    size = Sizes(dps)
    low, wide = jnp.bfloat16, jnp.float32
    shapes = saved_shapes()
    rows = (size.qkv, size.dense, size.wide, size.emb)
    chunks = [chunk_shape(size, count) for count in rows]
    anywhere = pl.BlockSpec(memory_space=pl.ANY)
    inside = pl.BlockSpec(memory_space=pltpu.VMEM)
    outs = [((WIDE, WIDE), low)]
    outs += [((SECT,) + shape, low) for shape in chunks[:3]]
    outs += [((WINDOW, WIDE), low), ((WIDE, WIDE), low)]
    outs += [((SECT,) + shape, dtype) for shape, dtype in shapes]
    scratch = shapes + [((SECT,) + shape, low) for shape in chunks[:3]] + [(chunks[3], low)]
    scratch += [((SECT, count, LANES), low) for count in rows]
    scratch += [(array.shape, array.dtype) for array in given]
    scratch += [((LANES, LANES), wide), ((16, LANES), low)]
    slots = max(Spread.slots(size.bs), SpreadCross.slots(size.bs))
    dma = pltpu.SemaphoreType.DMA
    return pl.pallas_call(
        partial(forward_kernel, dps),
        out_shape=[jax.ShapeDtypeStruct(shape, dtype) for shape, dtype in outs],
        in_specs=[pl.BlockSpec(memory_space=pltpu.SMEM)] + [anywhere] * len(given),
        out_specs=[inside] + [anywhere] * 3 + [inside] * 2 + [anywhere] * len(shapes),
        scratch_shapes=[pltpu.VMEM(shape, dtype) for shape, dtype in scratch]
        + [
            dma((len(given),)),
            dma((3, SECT)),
            dma((len(shapes),)),
            dma((4,)),
            dma((3, SECT - 1)),
            dma((3, SECT - 1)),
            dma((1 + 3 * SECT, slots)),
            dma((1 + 3 * SECT, slots)),
        ],
        compiler_params=pltpu.CompilerParams(
            collective_id=0, has_side_effects=True, vmem_limit_bytes=60 * 1024 * 1024
        ),
        name="gather_forward",
    )(groups, *given)


FETCHES = {
    ("norm2", 0): (("second", "scale_2"), ("second", "scale_2")),
    ("down", 0): (("hidden",), ()),
    ("down", 1): ((), ("hidden",)),
    ("gelu", 0): (("slope", 2), ()),
    ("gelu", 1): ((), ("slope", 2)),
    ("up", 0): (("normed",), ("normed",)),
    ("normed", 0): ((1,), ()),
    ("norm1", 0): (("first", "scale_1", "attended"), ("first", "scale_1", "attended", 1)),
    ("attend", 0): (("mixed", "probs"), ()),
    ("attend", 3): ((), ("mixed", "probs")),
    ("mix", 0): (("h",), ()),
    ("mix", 1): ((), ("h",)),
    ("input", 0): ((0,), (0,)),
}


def backward_kernel(dps, groups, att, up, down, cotangent, x_in, wsel_in, *refs):
    size = Sizes(dps)
    kept, refs = refs[:12], refs[12:]
    series_grad, outs, refs = refs[0], refs[1:5], refs[5:]
    local, refs = refs[:11], refs[11:]
    tables, w_att, w_up, w_down, dtables, dy, dnormed, dlow, dlow_t, dmixed, dup = refs[:11]
    x, wsel, pick, delta, refs = *refs[11:15], refs[15:]
    kinds = []
    for kind in range(4):
        count = 6 if kind in CROSS else 5
        kinds.append(refs[:4] + (refs[4 : 4 + count],))
        refs = refs[4 + count :]
    w_sem, kept_sem, table_sem, late_sem, out_sem, p_send, p_recv, send, recv, credit = refs
    h, mixed, probs, attended, first, normed, slope, hidden, second, scale_1, scale_2 = local
    at = Place(dps)
    last = SECT - 1

    def weights(kind, section):
        src, dst = ((att, w_att), (up, w_up), (down, w_down))[kind]
        return pltpu.make_async_copy(src.at[section], dst, w_sem.at[kind])

    names = ("h", "mixed", "probs", "attended", "first", "normed", "slope", "hidden", "second")
    names += ("table", "scale_1", "scale_2")
    held = dict(zip(names[:9] + names[10:], local))

    def fetches(section, *wanted):
        found = []
        for name in wanted:
            if isinstance(name, int):
                found.append(weights(name, section))
            else:
                i = names.index(name)
                dst = held[name]
                found.append(pltpu.make_async_copy(kept[i].at[section], dst, kept_sem.at[i]))
        return found

    def chunk(kind, i):
        grads, totals, finals, landing, bufs = kinds[kind]
        sort = FoldCross if kind in CROSS else Fold
        refs = (grads, totals.at[i % 2], landing, bufs, finals.at[i])
        return sort(at, *refs, send.at[kind], recv.at[kind], credit.at[kind], HALVES[kind])

    def hand_over(kind, i):
        landing = outs[kind].at[at.block]
        final = kinds[kind][2].at[i]
        return (
            pltpu.make_async_copy(final, landing, out_sem.at[kind]),
            remote(final, landing, p_send.at[kind, i], p_recv.at[kind, at.pipe], (last - i, at.dp)),
        )

    def act(op, kind, i):
        again, more = (False, False) if kind == EMB else (i > 0, i < last)
        if op == 0:
            chunk(kind, i).start(0, again)
        elif op < 4:
            chunk(kind, i).move(op - 1, again, more)
        else:
            chunk(kind, i).land(3, more)
            if kind == EMB:
                outs[kind][...] = kinds[kind][2][0]
            else:
                here, away = hand_over(kind, i)

                @pl.when(at.pipe == last - i)
                def _():
                    here.start(priority=1)

                @pl.when(at.pipe != last - i)
                def _():
                    away.start()

    at.greet()
    get_tables = pltpu.make_async_copy(kept[9], tables, table_sem)
    late = copies_of(((cotangent, dy), (x_in, x), (wsel_in, wsel)), late_sem)
    copies_begin([late[0], get_tables] + fetches(last, "second", "scale_2", "hidden"))
    copies_begin(fetches(last, "slope", 2, "normed", 1, "first", "scale_1", "attended"))
    copies_begin(fetches(last, "mixed", "probs", "h", 0) + late[1:])
    pick[...] = group_rows(groups[0])
    copies_wait([late[0], get_tables])

    @pl.loop(0, SECT)
    def _(i):
        section = last - i
        table, dtable = tables.at[section], dtables.at[section]

        def compute(name, piece):
            need, free = FETCHES.get((name, piece), ((), ()))
            copies_wait(fetches(section, *need))
            if name == "norm2":
                backward_norm_two(table, dtable, dy, second, scale_2, dnormed, dlow, dlow_t)
                pl.when(i == 0)(at.met)
            elif name == "down":
                backward_down(size, kinds[2][0], hidden, dlow_t, piece)
            elif name == "gelu":
                backward_gelu(size, w_down, dtable, slope, dlow, dup, piece)
            elif name == "up":
                backward_up(size, kinds[1][0], normed, dup)
            elif name == "normed":
                backward_normed(size, w_up, dnormed, dup)
            elif name == "norm1":
                backward_norm_one(
                    size,
                    w_up,
                    table,
                    kinds[1][0],
                    dtable,
                    first,
                    scale_1,
                    attended,
                    dnormed,
                    dlow,
                    dlow_t,
                    delta,
                )
            elif name == "attend":
                backward_attend(mixed, probs, delta, dtable, dlow, dmixed, piece)
            elif name == "mix":
                backward_mix(size, kinds[0][0], h, dmixed, piece)
            else:
                backward_input(size, w_att, dnormed, dmixed, dy)
            if free:

                @pl.when(section > 0)
                def _():
                    copies_begin(fetches(section - 1, *free))

        follow(BACKWARD_PERIOD, i, act, compute)

    def after(name, piece):
        copies_wait(late[1:])
        embed_back(size, pick, x, wsel, dy, dtables, kinds[EMB][0], series_grad)

    follow(BACKWARD_END, 0, act, after)

    for kind in range(3):
        for i in range(SECT):
            here, away = hand_over(kind, i)

            @pl.when(at.pipe == last - i)
            def _():
                here.wait()

            @pl.when(at.pipe != last - i)
            def _():
                away.wait_send()

        for k in range(1, SECT):
            other = at.pipe_at(k)
            landing = outs[kind].at[at.blocks[k]]
            sems = p_send.at[kind, 0], p_recv.at[kind, other]
            remote(landing, landing, *sems, (other, at.dp)).wait_recv()


def backward_all(groups, weights, cotangent, x, wsel, kept, history, dps):
    size = Sizes(dps)
    low, wide = jnp.bfloat16, jnp.float32
    anywhere = pl.BlockSpec(memory_space=pl.ANY)
    inside = pl.BlockSpec(memory_space=pltpu.VMEM)
    shapes = saved_shapes()
    kind_rows = (size.qkv, size.dense, size.wide, size.emb)
    scratch = shapes[:9] + shapes[10:] + [((SECT,) + shapes[9][0], wide)]
    scratch += [(chunk_shape(size, rows), low) for rows in kind_rows[:3]]
    scratch += [
        ((SECT,) + shapes[9][0], wide),
        ((WIDE, WIDE), low),
        ((WIDE, WIDE), wide),
        ((WIDE, WIDE), low),
        ((WIDE, WIDE), low),
        ((WIDE, 3 * WIDE), low),
        ((WIDE, 4 * WIDE), low),
        ((WIDE, WIDE), low),
        ((WINDOW, WIDE), low),
        ((16, LANES), low),
        ((16, WIDE), wide),
    ]
    for kind, rows in enumerate(kind_rows):
        sets, results = (1, 1) if kind == EMB else (2, SECT)
        scratch += [
            (chunk_shape(size, rows), low),
            ((sets, 2, ZS, size.bs, rows, LANES), low),
            ((results, rows, LANES), low),
            ((2, ZS, size.bs, rows, LANES), low),
        ]
        sort = FoldCross if kind in CROSS else Fold
        scratch += [(shape, low) for shape in sort.buffers(size.bs, rows, HALVES[kind])]
    slots = max(Fold.slots(size.bs), FoldCross.slots(size.bs))
    dma = pltpu.SemaphoreType.DMA
    return pl.pallas_call(
        partial(backward_kernel, dps),
        out_shape=[jax.ShapeDtypeStruct((history, WIDE), wide)]
        + [jax.ShapeDtypeStruct((SECT, rows, LANES), low) for rows in kind_rows[:3]]
        + [jax.ShapeDtypeStruct((size.emb, LANES), low)],
        in_specs=[pl.BlockSpec(memory_space=pltpu.SMEM)] + [anywhere] * (6 + len(kept)),
        out_specs=[inside] + [anywhere] * 3 + [inside],
        scratch_shapes=[pltpu.VMEM(shape, dtype) for shape, dtype in scratch]
        + [
            dma((3,)),
            dma((12,)),
            dma(()),
            dma((3,)),
            dma((3,)),
            dma((3, SECT)),
            dma((3, SECT)),
            dma((4, slots)),
            dma((4, slots)),
            pltpu.SemaphoreType.REGULAR((4, slots)),
        ],
        compiler_params=pltpu.CompilerParams(
            collective_id=1, has_side_effects=True, vmem_limit_bytes=60 * 1024 * 1024
        ),
        name="backward_fold",
    )(groups, *weights, cotangent, x, wsel, *kept)


def finish_kernel(dps, n_gains, n_biases, *refs):
    size = Sizes(dps)
    given, refs = refs[:6], refs[6:]
    block_out, series_out, embed_w, embed_b, qkv, out, up_out, down_out, gains, biases = refs[:10]
    att, up, down, emb, sems = refs[10:]
    copies = copies_of(zip(given, (att, up, down, emb, block_out, series_out)), sems)
    copies_start(copies)
    copies_wait(copies[:4])
    for lb in range(SECT):
        lanes = slice(lb * LANES, (lb + 1) * LANES)
        qkv[:, lanes] = att[lb].astype(jnp.float32)
        out[:, lanes] = up[lb, : size.out].astype(jnp.float32)
        up_out[:, lanes] = up[lb, size.out :].astype(jnp.float32)
        for j in range(4):
            rows = slice(j * size.down, (j + 1) * size.down)
            start = j * WIDE + lb * LANES
            down_out[:, start : start + LANES] = down[lb, rows].astype(jnp.float32)
    vectors = emb[size.lookback :].astype(jnp.float32)
    count = -(-(n_gains + n_biases) // LANES)
    flat = jnp.concatenate([vectors[row : row + 1] for row in range(count)], axis=1)
    gains[...] = flat[:, :n_gains]
    biases[...] = flat[:, n_gains : n_gains + n_biases]
    rows = WIDE // (SECT * dps)
    packed = emb[: size.lookback].astype(jnp.float32)
    packed = [packed[i * rows : (i + 1) * rows] for i in range(6)]
    square = jnp.concatenate([packed[0], jnp.zeros((LANES - rows, LANES), jnp.float32)], axis=0)
    embed_b[...] = square.T[:GROUPS, :rows]
    packed = jnp.concatenate(packed, axis=1)
    ends = ((6 * LANES, L1), (5 * LANES, L2), (3 * LANES, L3))
    embed_w[...] = jnp.concatenate([packed[:, end - span : end] for end, span in ends], axis=1)
    copies_wait(copies[4:])


def finish_all(sums, block, series, n_gains, n_biases, dps):
    size = Sizes(dps)
    wide = jnp.float32
    columns = WIDE // (SECT * dps)
    outs = [
        (block.shape, block.dtype),
        (series.shape, wide),
        ((columns, L1 + L2 + L3), wide),
        ((GROUPS, columns), wide),
        ((size.qkv, WIDE), wide),
        ((size.out, WIDE), wide),
        ((size.up, WIDE), wide),
        ((size.down, 4 * WIDE), wide),
        ((1, n_gains), wide),
        ((1, n_biases), wide),
    ]
    anywhere = pl.BlockSpec(memory_space=pl.ANY)
    inside = pl.BlockSpec(memory_space=pltpu.VMEM)
    return pl.pallas_call(
        partial(finish_kernel, dps, n_gains, n_biases),
        out_shape=[jax.ShapeDtypeStruct(shape, dtype) for shape, dtype in outs],
        in_specs=[anywhere] * 6,
        out_specs=[inside] * 10,
        scratch_shapes=[pltpu.VMEM(array.shape, array.dtype) for array in sums]
        + [pltpu.SemaphoreType.DMA((6,))],
        compiler_params=pltpu.CompilerParams(vmem_limit_bytes=60 * 1024 * 1024),
        name="finish",
    )(*sums, block, series)


def per_device(
    series,
    groups,
    cotangent,
    embed_weight,
    embed_bias,
    qkv_weight,
    out_weight,
    up_weight,
    down_weight,
    gains,
    biases,
):
    dps = lax.axis_size("dp")
    given = (
        series[0],
        embed_weight.T,
        embed_bias,
        qkv_weight[0],
        out_weight[0],
        up_weight[0],
        down_weight[0],
        gains,
        biases,
    )
    block_output, att, up, down, wsel, x, *kept = forward_all(groups, given, dps)
    series_grad, *sums = backward_all(
        groups, (att, up, down), cotangent[0], x, wsel, kept, series.shape[1], dps
    )
    outs = finish_all(sums, block_output, series_grad, gains.shape[1], biases.shape[1], dps)
    block_output, series_grad, embed_w, embed_b, qkv, out, up, down, gain_sum, bias_sum = outs
    return (
        block_output[None],
        series_grad[None],
        embed_w.T,
        embed_b,
        qkv[None],
        out[None],
        up[None],
        down[None],
        gain_sum,
        bias_sum,
    )


def solution(mesh):
    return jax.shard_map(
        per_device,
        mesh=mesh,
        in_specs=(
            P(("pipe", "dp"), None, None),
            P(("pipe", "dp")),
            P(("pipe", "dp"), None, None),
            P(None, "dp"),
            P(None, "dp"),
            P("pipe", "dp", None),
            P("pipe", "dp", None),
            P("pipe", "dp", None),
            P("pipe", "dp", None),
            P("pipe", "dp"),
            P("pipe", "dp"),
        ),
        out_specs=(
            P(("pipe", "dp"), None, None),
            P(("pipe", "dp"), None, None),
            P(None, ("pipe", "dp")),
            P(None, ("pipe", "dp")),
            P("pipe", "dp", None),
            P("pipe", "dp", None),
            P("pipe", "dp", None),
            P("pipe", "dp", None),
            P("pipe", "dp"),
            P("pipe", "dp"),
        ),
        check_vma=False,
    )
```

```python
from functools import partial
import math

import jax
import jax.numpy as jnp
from jax import lax
from jax.experimental import pallas as pl
from jax.experimental.pallas import tpu as pltpu
from jax.sharding import PartitionSpec as P

HEAD = 64
L1 = 96
L2 = 192
L3 = 336
GROUPS = 3


NORM_EPS = 1e-05


MESH = pl.DeviceIdType.MESH
LANES = 128
ZS = 4
SECT = 4
EMB = 3


class Place:
    def __init__(self, dps):
        self.bs = bs = dps // ZS
        pipe = lax.axis_index("pipe")
        dp = lax.axis_index("dp")
        self.pipe, self.dp = pipe, dp
        self.x, self.c = x, c = lax.div(pipe, 2), lax.rem(pipe, 2)
        self.z, self.b = z, b = lax.div(dp, bs), lax.rem(dp, bs)
        self.block = c * 2 + x
        self.other_block = c * 2 + 1 - x
        self.x_peer = ((1 - x) * 2 + c, dp)
        self.core_peer = (x * 2 + 1 - c, dp)
        self.pipes = [lax.rem(pipe + k, SECT) for k in range(SECT)]
        self.blocks = [self.block_of(other) for other in self.pipes]
        self.zs = [lax.rem(z + k, ZS) for k in range(ZS)]
        self.bees = [lax.rem(b + k, bs) for k in range(bs)]
        self.z_peers = [(pipe, other * bs + b) for other in self.zs]
        self.b_peers = [(pipe, z * bs + other) for other in self.bees]

    def block_of(self, pipe):
        return lax.rem(pipe, 2) * 2 + lax.div(pipe, 2)

    def pipe_at(self, step):
        return self.pipes[step % SECT]

    def z_at(self, step):
        return self.zs[step % ZS]

    def b_at(self, step):
        return self.bees[step % self.bs]

    def z_peer(self, step):
        return self.z_peers[step % ZS]

    def b_peer(self, step):
        return self.b_peers[step % self.bs]

    def greet(self):
        barrier = pltpu.get_barrier_semaphore()
        peers = [(self.pipe_at(k), self.dp) for k in range(1, SECT)]
        peers += [self.z_peer(k) for k in range(1, ZS)]
        peers += [self.b_peer(k) for k in range(1, self.bs)]
        for peer in peers:
            pl.semaphore_signal(barrier, inc=1, device_id=peer, device_id_type=MESH)

    def met(self):
        pl.semaphore_wait(pltpu.get_barrier_semaphore(), SECT + ZS + self.bs - 3)


def remote(src, dst, send, recv, peer):
    return pltpu.make_async_remote_copy(
        src_ref=src, dst_ref=dst, send_sem=send, recv_sem=recv, device_id=peer, device_id_type=MESH
    )


FORWARD_START = (
    (0, 3, 0),
    (0, 0, 0),
    (0, 2, 0),
    (1, 3, 0),
    (1, 0, 0),
    (0, 1, 0),
    (2, 3, 0),
    (2, 0, 0),
    (0, 0, 1),
    (1, 1, 0),
    (1, 2, 0),
    (3, 3, 0),
    (0, 2, 1),
    (1, 0, 1),
    (2, 1, 0),
    (4, 3, 0),
    (3, 0, 0),
    ("embed",),
    (4, 0, 0),
)
FORWARD_PERIOD = (
    ("mix",),
    (0, 1, 1),
    (2, 0, 1),
    ("mix",),
    ("attend",),
    (3, 1, 0),
    ("attend",),
    (2, 2, 0),
    ("attend",),
    (0, 0, 2),
    (4, 1, 0),
    ("attend",),
    ("project",),
    (1, 1, 1),
    ("up",),
    (1, 2, 1),
    (0, 2, 2),
    (3, 2, 0),
    ("up",),
    (1, 0, 2),
    ("up",),
    (2, 1, 1),
    (3, 0, 1),
    (4, 2, 0),
    ("up",),
    ("down",),
    (4, 0, 1),
    ("down",),
)
BACKWARD_PERIOD = (
    ("norm2",),
    (1, 0, -1),
    ("down",),
    ("down",),
    ("gelu",),
    ("gelu",),
    (2, 1, -1),
    (0, 2, 0),
    ("up",),
    ("normed",),
    (2, 0, -1),
    ("norm1",),
    (4, 1, -2),
    (4, 2, -2),
    (1, 2, 0),
    (3, 1, -1),
    (0, 1, 0),
    ("attend",),
    ("attend",),
    ("attend",),
    ("attend",),
    (3, 2, -1),
    (1, 1, 0),
    (4, 0, -2),
    (3, 0, -1),
    ("mix",),
    ("mix",),
    (0, 0, 0),
    ("input",),
    (2, 2, 0),
)
BACKWARD_END = (
    ("embed",),
    (1, 0, 3),
    (2, 1, 3),
    (2, 0, 3),
    (4, 1, 2),
    (4, 2, 2),
    (3, 1, 3),
    (0, 3, 0),
    (3, 2, 3),
    (4, 0, 2),
    (1, 3, 0),
    (3, 0, 3),
    (2, 3, 0),
    (3, 3, 0),
    (4, 1, 3),
    (4, 2, 3),
    (4, 0, 3),
    (4, 3, 0),
)


def copies_start(copies):
    for copy in copies:
        copy.start()


def copies_begin(copies):
    for copy in copies:
        copy.start(priority=1)


def copies_wait(copies):
    for copy in copies:
        copy.wait()


class Spread:
    def __init__(self, at, out, send, recv, half=ZS // 2):
        self.at, self.out, self.send, self.recv = at, out, send, recv
        nb = at.bs - 1
        self.slot_z = 0
        self.slot_b1 = ZS - 1
        self.slot_x1 = self.slot_b1 + nb
        self.slot_x2 = self.slot_x1 + 1
        self.slot_b2 = self.slot_x2 + 1
        self.slot_c = self.slot_b2 + nb
        self.half = half

    @staticmethod
    def slots(bs):
        return ZS - 1 + 3 * (bs - 1) + 5

    def copy(self, region, slot, peer):
        return remote(region, region, self.send.at[slot], self.recv.at[slot], peer)

    def core_regions(self, core):
        at, out = self.at, self.out
        some, rest = pl.ds(0, self.half), pl.ds(self.half, ZS - self.half)
        both = pl.ds(core * 2, 2)
        late = [out.at[core * 2 + 1 - at.x, some]]
        late += [out.at[both, rest, at.b_at(k)] for k in range(1, at.bs)]
        return [out.at[core * 2 + at.x, some], out.at[both, rest, at.b]], late

    def core_copies(self, back, early, late):
        groups = self.core_regions(1 - self.at.c if back else self.at.c)
        regions = [(i, region) for i, region in enumerate(groups[0])] if early else []
        if late:
            regions += [(2 + i, region) for i, region in enumerate(groups[1])]
        return [self.copy(region, self.slot_c + i, self.at.core_peer) for i, region in regions]

    def copies(self, stage, back):
        at, out, half = self.at, self.out, self.half
        rest = pl.ds(half, ZS - half)
        x_block = at.other_block if back else at.block
        if stage == 0:
            return [
                self.copy(
                    out.at[at.block, at.z_at(ZS - k) if back else at.z, at.b],
                    self.slot_z + k - 1,
                    at.z_peer(k),
                )
                for k in range(1, ZS)
            ]
        copies = []
        for k in range(1, at.bs):
            b = at.b_at(at.bs - k) if back else at.b
            if stage == 1:
                region, slot = out.at[at.block, pl.ds(0, half), b], self.slot_b1
            else:
                region, slot = out.at[pl.ds(at.c * 2, 2), rest, b], self.slot_b2
            copies.append(self.copy(region, slot + k - 1, at.b_peer(k)))
        if stage == 1:
            region, slot = out.at[x_block, rest, at.b], self.slot_x1
        else:
            region, slot = out.at[x_block, pl.ds(0, half)], self.slot_x2
        copies.append(self.copy(region, slot, at.x_peer))
        return copies

    def start(self, stage):
        if stage < 3:
            copies_start(self.copies(stage, False))
        if stage >= 2:
            copies_start(self.core_copies(False, stage == 2, stage == 3))

    def land(self, stage):
        if stage < 3:
            here, away = self.copies(stage, True), self.copies(stage, False)
        else:
            here, away = (self.core_copies(back, True, True) for back in (True, False))
        for copy in here:
            copy.wait_recv()
        for copy in away:
            copy.wait_send()

    def move(self, stage):
        self.land(stage)
        self.start(stage + 1)


class SpreadCross(Spread):
    @staticmethod
    def slots(bs):
        return 3 * bs + 2 * ZS

    def __init__(self, *args):
        super().__init__(*args)
        self.slot_c = 2 * self.at.bs + 2 * ZS - 2

    def cuts(self):
        rows = self.out.shape[-2]
        cut = rows // 32 * 16
        return pl.ds(0, cut), pl.ds(cut, rows - cut)

    def core_regions(self, core):
        at, out = self.at, self.out
        some, rest = self.cuts()
        both = pl.ds(core * 2, 2)
        late = [out.at[core * 2 + 1 - at.x, :, :, rest]]
        late += [out.at[both, :, at.b_at(k), some] for k in range(1, at.bs)]
        return [out.at[both, :, at.b, some], out.at[core * 2 + at.x, :, :, rest]], late

    def copies(self, stage, back):
        at, out = self.at, self.out
        some, rest = self.cuts()
        both = pl.ds(at.c * 2, 2)
        x_block = at.other_block if back else at.block
        copies = []
        if stage == 1:
            for k in range(1, ZS):
                z = at.z_at(ZS - k) if back else at.z
                copies.append(self.copy(out.at[both, z, at.b, some], at.bs + k - 1, at.z_peer(k)))
                slot = at.bs + ZS + k - 2
                copies.append(self.copy(out.at[at.block, z, :, rest], slot, at.z_peer(k)))
            return copies
        base = 0 if stage == 0 else at.bs + 2 * ZS - 2
        for k in range(1, at.bs):
            b = at.b_at(at.bs - k) if back else at.b
            region = out.at[at.block, at.z, b, rest] if stage == 0 else out.at[both, :, b, some]
            copies.append(self.copy(region, base + k, at.b_peer(k)))
        if stage == 0:
            region = out.at[x_block, at.z, at.b, some]
        else:
            region = out.at[x_block, :, :, rest]
        copies.append(self.copy(region, base, at.x_peer))
        return copies


class Fold:
    def __init__(self, at, grads, total, landing, bufs, final, send, recv, credit, half):
        self.at, self.grads, self.total = at, grads, total
        self.landing, self.bufs, self.final = landing, bufs, final
        self.send, self.recv, self.credit = send, recv, credit
        self.half = half
        nb = at.bs - 1
        self.slot_x1 = 1
        self.slot_b1 = 2
        self.slot_x2 = 2 + nb
        self.slot_b2 = 3 + nb
        self.slot_z = 3 + 2 * nb

    @staticmethod
    def slots(bs):
        return 3 + 2 * (bs - 1) + ZS - 1

    @staticmethod
    def buffers(bs, rows, half):
        nb = max(bs - 1, 1)
        rest = ZS - half
        return [
            (half, bs, rows, LANES),
            (nb, 2, rest, rows, LANES),
            (rest, rows, LANES),
            (nb, half, rows, LANES),
            (ZS - 1, rows, LANES),
        ]

    def core_parts(self):
        other = self.grads.at[pl.ds((1 - self.at.c) * 2, 2)]
        return [(other, self.landing, 0, self.at.core_peer, self.at.core_peer)]

    def parts(self, stage):
        at, half, total, bufs = self.at, self.half, self.total, self.bufs
        if stage == 0:
            return self.core_parts()
        if stage == 3:
            return [
                (
                    total.at[at.x, at.z_at(k), at.b],
                    bufs[4].at[k - 1],
                    self.slot_z + k - 1,
                    at.z_peer(k),
                    at.z_peer(ZS - k),
                )
                for k in range(1, ZS)
            ]
        rest = pl.ds(half, ZS - half)
        found = []
        for k in range(1, at.bs):
            if stage == 1:
                src, buf, slot = total.at[:, rest, at.b_at(k)], bufs[1], self.slot_b1
            else:
                src, buf, slot = total.at[at.x, pl.ds(0, half), at.b_at(k)], bufs[3], self.slot_b2
            found.append((src, buf.at[k - 1], slot + k - 1, at.b_peer(k), at.b_peer(at.bs - k)))
        if stage == 1:
            src, buf, slot = total.at[1 - at.x, pl.ds(0, half)], bufs[0], self.slot_x1
        else:
            src, buf, slot = total.at[1 - at.x, rest, at.b], bufs[2], self.slot_x2
        found.append((src, buf, slot, at.x_peer, at.x_peer))
        return found

    def start(self, stage, again):
        for src, buf, slot, to, _ in self.parts(stage):
            if again is not False:

                @pl.when(again)
                def _():
                    pl.semaphore_wait(self.credit.at[slot], 1)

            remote(src, buf, self.send.at[slot], self.recv.at[slot], to).start()

    def land(self, stage, more):
        parts = self.parts(stage)
        for src, buf, slot, to, _ in parts:
            remote(src, buf, self.send.at[slot], self.recv.at[slot], to).wait()
        self.add(stage)
        if more is not False:

            @pl.when(more)
            def _():
                for _, _, slot, _, origin in parts:
                    pl.semaphore_signal(
                        self.credit.at[slot], inc=1, device_id=origin, device_id_type=MESH
                    )

    def add_core(self):
        at, bs, total = self.at, self.at.bs, self.total

        @pl.loop(0, 2 * ZS * bs)
        def _(i):
            z, b = i // bs % ZS, i % bs
            x = i // (ZS * bs)
            total[x, z, b] = self.grads[at.c * 2 + x, z, b] + self.landing[x, z, b]

    def add(self, stage):
        at, half, bs = self.at, self.half, self.at.bs
        total, bufs = self.total, self.bufs
        rest = ZS - half
        if stage == 0:
            self.add_core()
        elif stage == 1:

            @pl.loop(0, half * bs)
            def _(i):
                z, b = i // bs, i % bs
                total[at.x, z, b] = total[at.x, z, b] + bufs[0][z, b]

            @pl.loop(0, 2 * rest)
            def _(i):
                x, z = i // rest, i % rest
                for k in range(bs - 1):
                    total[x, half + z, at.b] = total[x, half + z, at.b] + bufs[1][k, x, z]

        elif stage == 2:

            @pl.loop(0, rest)
            def _(z):
                total[at.x, half + z, at.b] = total[at.x, half + z, at.b] + bufs[2][z]

            @pl.loop(0, half)
            def _(z):
                for k in range(bs - 1):
                    total[at.x, z, at.b] = total[at.x, z, at.b] + bufs[3][k, z]

        else:
            self.finish([bufs[4][k] for k in range(ZS - 1)])

    def finish(self, pieces):
        at = self.at
        done = self.total[at.x, at.z, at.b].astype(jnp.float32)
        for piece in pieces:
            done = done + piece.astype(jnp.float32)
        self.final[...] = done.astype(self.final.dtype)

    def move(self, stage, again, more):
        self.land(stage, more)
        self.start(stage + 1, again)


class FoldCross(Fold):
    @staticmethod
    def slots(bs):
        return 2 * bs + 2 * ZS - 1

    @staticmethod
    def buffers(bs, rows, half):
        nb = max(bs - 1, 1)
        cut = rows // 32 * 16
        rest = rows - cut
        return [
            (nb, 2, ZS, cut, LANES),
            (ZS, bs, rest, LANES),
            (ZS - 1, 2, cut, LANES),
            (ZS - 1, bs, rest, LANES),
            (cut, LANES),
            (nb, rest, LANES),
        ]

    def cuts(self):
        rows = self.total.shape[-2]
        cut = rows // 32 * 16
        return pl.ds(0, cut), pl.ds(cut, rows - cut)

    def parts(self, stage):
        at, total, bufs = self.at, self.total, self.bufs
        if stage == 0:
            return self.core_parts()
        some, rest = self.cuts()
        found = []
        if stage == 2:
            for k in range(1, ZS):
                pair = (at.z_peer(k), at.z_peer(ZS - k))
                z = at.z_at(k)
                found.append((total.at[:, z, at.b, some], bufs[2].at[k - 1], at.bs + k, *pair))
                slot = at.bs + ZS + k - 1
                found.append((total.at[at.x, z, :, rest], bufs[3].at[k - 1], slot, *pair))
            return found
        base = 1 if stage == 1 else at.bs + 2 * ZS - 1
        for k in range(1, at.bs):
            pair = (at.b_peer(k), at.b_peer(at.bs - k))
            if stage == 1:
                src, buf = total.at[:, :, at.b_at(k), some], bufs[0].at[k - 1]
            else:
                src, buf = total.at[at.x, at.z, at.b_at(k), rest], bufs[5].at[k - 1]
            found.append((src, buf, base + k, *pair))
        if stage == 1:
            src, buf = total.at[1 - at.x, :, :, rest], bufs[1]
        else:
            src, buf = total.at[1 - at.x, at.z, at.b, some], bufs[4]
        found.append((src, buf, base, at.x_peer, at.x_peer))
        return found

    def add(self, stage):
        at, bs = self.at, self.at.bs
        total, bufs = self.total, self.bufs
        some, rest = self.cuts()
        if stage == 0:
            self.add_core()
        elif stage == 1:

            @pl.loop(0, 2 * ZS)
            def _(i):
                x, z = i // ZS, i % ZS
                for k in range(bs - 1):
                    total[x, z, at.b, some] = total[x, z, at.b, some] + bufs[0][k, x, z]

            @pl.loop(0, ZS * bs)
            def _(i):
                z, b = i // bs, i % bs
                total[at.x, z, b, rest] = total[at.x, z, b, rest] + bufs[1][z, b]

        elif stage == 2:
            for x in range(2):
                for k in range(ZS - 1):
                    total[x, at.z, at.b, some] = total[x, at.z, at.b, some] + bufs[2][k, x]

            @pl.loop(0, bs)
            def _(b):
                for k in range(ZS - 1):
                    total[at.x, at.z, b, rest] = total[at.x, at.z, b, rest] + bufs[3][k, b]

        else:
            total[at.x, at.z, at.b, some] = total[at.x, at.z, at.b, some] + bufs[4][...]
            for k in range(bs - 1):
                total[at.x, at.z, at.b, rest] = total[at.x, at.z, at.b, rest] + bufs[5][k]
            self.final[...] = total[at.x, at.z, at.b]


HALF = 256
WIDE = 512
QKV_TILE = 768
VEC_ROWS = 16


STEP = 64


def by_rows(fn, *arrays, step=STEP):
    parts = [
        fn(*[array[at : at + step] for array in arrays])
        for at in range(0, arrays[0].shape[0], step)
    ]
    if isinstance(parts[0], tuple):
        return tuple(jnp.concatenate(part, axis=0) for part in zip(*parts))
    return jnp.concatenate(parts, axis=0)


def dot_nt(a, b):
    return lax.dot_general(a, b, (((1,), (1,)), ((), ())), preferred_element_type=jnp.float32)


def dot_nn(a, b):
    return lax.dot_general(a, b, (((1,), (0,)), ((), ())), preferred_element_type=jnp.float32)


def dot_tn(a, b):
    return lax.dot_general(a, b, (((0,), (0,)), ((), ())), preferred_element_type=jnp.float32)


def aligned(index, unit):
    return pl.multiple_of(index, unit)


def rows_of(ref, bs, first, count, start, rows, blocks=range(SECT)):
    parts = []
    for i in range(count):
        d = first + i
        place = (d // bs, d % bs)
        parts.append(
            jnp.concatenate(
                [ref[(lb,) + place + (pl.ds(start, rows), slice(None))] for lb in blocks], axis=1
            )
        )
    return parts[0] if count == 1 else jnp.concatenate(parts, axis=0)


def put_rows(ref, bs, first, count, start, rows, value, block=0):
    value = value.astype(ref.dtype)
    for i in range(count):
        d = first + i
        place = (d // bs, d % bs)
        for lane in range(value.shape[1] // LANES):
            ref[(block + lane,) + place + (pl.ds(start, rows), slice(None))] = value[
                i * rows : (i + 1) * rows, lane * LANES : (lane + 1) * LANES
            ]


def vector_pieces(dps):
    n_gains, n_biases = 2 * WIDE // dps, 10 * WIDE // dps
    starts = [(0, 0), (0, 2), (1, 0), (1, 2), (2, 0), (2, 1), (2, 2), (2, 3), (3, 0), (3, 2)]
    pieces = []
    for d in range(dps):
        at = 0
        while at < n_gains + n_biases:
            if at < n_gains:
                index = d * n_gains + at
                row, column = (1, 3)[index // WIDE], WIDE + index % WIDE
                left = n_gains - at
            else:
                index = d * n_biases + at - n_gains
                row, part = starts[index // WIDE]
                column = part * WIDE + index % WIDE
                left = n_gains + n_biases - at
            size = min(left, LANES - at % LANES, LANES - column % LANES)
            pieces.append((d, at // LANES, at % LANES, row, column, size))
            at += size
    return pieces


def read_vectors(ref, table, bs, start, block):
    tiles = {}
    for d, row, lane, to_row, to_lane, size in vector_pieces(ZS * bs):
        if d not in tiles:
            tile = ref[block, d // bs, d % bs, start : start + VEC_ROWS, :]
            tiles[d] = tile.astype(jnp.float32)
        table[to_row : to_row + 1, to_lane : to_lane + size] = tiles[d][
            row : row + 1, lane : lane + size
        ]


def rows_tile(lines):
    row_id = lax.broadcasted_iota(jnp.int32, (VEC_ROWS, LANES), 0)
    tile = jnp.zeros((VEC_ROWS, LANES), jnp.float32)
    for row, pieces in enumerate(lines):
        have = sum(piece.shape[1] for piece in pieces)
        if have < LANES:
            pieces = pieces + [jnp.zeros((1, LANES - have), jnp.float32)]
        line = pieces[0] if len(pieces) == 1 else jnp.concatenate(pieces, axis=1)
        tile = jnp.where(row_id == row, line, tile)
    return tile


def vector_tile(table, dps, place):
    lines = []
    for d, row, lane, to_row, to_lane, size in vector_pieces(dps):
        if d == place:
            if row == len(lines):
                lines.append([])
            lines[row].append(table[to_row : to_row + 1, to_lane : to_lane + size])
    return rows_tile(lines)


def fold_rows(x):
    total = x[:8]
    for at in range(8, x.shape[0], 8):
        total = total + x[at : at + 8]
    return total


def normalize(x):
    mean = jnp.mean(x, axis=1, keepdims=True)
    centred = x - mean
    scale = lax.rsqrt(jnp.mean(centred * centred, axis=1, keepdims=True) + NORM_EPS)
    return centred * scale, jnp.broadcast_to(scale, (x.shape[0], LANES))


def normalize_back(unit, scale, grad, gain):
    inner = grad * gain
    first = jnp.mean(inner, axis=1, keepdims=True)
    second = jnp.mean(inner * unit, axis=1, keepdims=True)
    out = jnp.concatenate([scale] * (WIDE // LANES), axis=1) * (inner - first - unit * second)
    return out, fold_rows(out), fold_rows(grad * unit), fold_rows(grad)


def gelu_pair(u):
    below = 0.5 + 0.5 * lax.erf(u * math.sqrt(0.5))
    bell = jnp.exp2((-0.5 * math.log2(math.e)) * (u * u))
    return u * below, below + u * (bell * (1.0 / math.sqrt(2.0 * math.pi)))


def head_masks(scale):
    lane = lax.broadcasted_iota(jnp.int32, (1, LANES), 1)
    first = jnp.where(lane < HEAD, scale, 0.0).astype(jnp.bfloat16)
    second = jnp.where(lane < HEAD, 0.0, scale).astype(jnp.bfloat16)
    return first, second


class Sizes:
    def __init__(self, dps):
        self.dps, self.bs = dps, dps // ZS
        self.qkv, self.out, self.up, self.down = (
            3 * WIDE // dps,
            WIDE // dps,
            4 * WIDE // dps,
            WIDE // dps,
        )
        self.lookback = -(-6 * WIDE // (SECT * dps) // VEC_ROWS) * VEC_ROWS
        self.emb = self.lookback + VEC_ROWS
        self.dense = self.out + self.up
        self.wide = 4 * self.down


def qkv_rows(size, w, tile):
    count = QKV_TILE // size.qkv
    return rows_of(w, size.bs, tile * count, count, 0, size.qkv)


def out_rows(size, w):
    return rows_of(w, size.bs, 0, size.dps, 0, size.out)


def up_rows(size, w, tile):
    count = HALF // size.up
    return rows_of(w, size.bs, tile * count, count, size.out, size.up)


def forward_mix(size, w, table, h, mixed, piece):
    columns = slice(piece * QKV_TILE, (piece + 1) * QKV_TILE)
    shift = table[0:1, columns]
    out = dot_nt(h[...], qkv_rows(size, w, piece))
    mixed[:, columns] = by_rows(lambda part: (part + shift).astype(mixed.dtype), out)


def softmax_columns(scores):
    parts = [scores[at : at + STEP] for at in range(0, scores.shape[0], STEP)]
    top = parts[0]
    for part in parts[1:]:
        top = jnp.maximum(top, part)
    top = jnp.max(top, axis=0, keepdims=True)
    parts = [jnp.exp(part - top) for part in parts]
    total = parts[0]
    for part in parts[1:]:
        total = total + part
    scale = 1.0 / jnp.sum(total, axis=0, keepdims=True)
    return jnp.concatenate([(part * scale).astype(jnp.bfloat16) for part in parts], axis=0)


def forward_attend(mixed, probs, attended, pair):
    lane = pair * LANES
    key_rows = mixed[:, WIDE + lane : WIDE + lane + LANES]
    values = mixed[:, 2 * WIDE + lane : 2 * WIDE + lane + LANES].T

    for part in range(2):
        rows = slice(part * HALF, (part + 1) * HALF)
        queries = mixed[rows, lane : lane + LANES]
        joined = []
        for head, mask in enumerate(head_masks(1.0 / math.sqrt(HEAD))):
            weights = softmax_columns(dot_nt(key_rows, queries * mask))
            probs[2 * pair + head, :, rows] = weights
            joined.append(dot_nn(values[head * HEAD : (head + 1) * HEAD], weights))
        joined = jnp.concatenate(joined, axis=0).T
        attended[rows, lane : lane + LANES] = joined.astype(attended.dtype)


def forward_project(size, w, table, h, attended, first, scale, normed):
    out = dot_nt(attended[...], out_rows(size, w))
    for part in range(WIDE // STEP):
        rows = slice(part * STEP, (part + 1) * STEP)
        total = h[rows, :].astype(jnp.float32) + (out[rows] + table[1:2, 0:WIDE])
        unit, scale[rows, :] = normalize(total)
        first[rows, :] = unit
        normed[rows, :] = (
            unit * table[1:2, WIDE : 2 * WIDE] + table[1:2, 2 * WIDE : 3 * WIDE]
        ).astype(normed.dtype)


def forward_up(size, w, table, normed, slope, hidden, piece):
    for j in (2 * piece, 2 * piece + 1):
        columns = slice(j * HALF, (j + 1) * HALF)
        shift = table[2:3, columns]
        upper = dot_nt(normed[...], up_rows(size, w, j))
        for part in range(WIDE // STEP):
            rows = slice(part * STEP, (part + 1) * STEP)
            value, grad = gelu_pair(upper[rows] + shift)
            hidden[rows, columns] = value.astype(hidden.dtype)
            slope[rows, columns] = grad.astype(slope.dtype)


def forward_down(size, w, table, normed, hidden, second, scale, h, piece):
    columns = slice(piece * HALF, (piece + 1) * HALF)
    count = size.dps // 2
    matrix = jnp.concatenate(
        [
            rows_of(w, size.bs, piece * count, count, j * size.down, size.down)
            for j in range(4)
        ],
        axis=1,
    )
    out = dot_nt(hidden[...], matrix)
    shift = table[3:4, columns]
    for part in range(WIDE // STEP):
        rows = slice(part * STEP, (part + 1) * STEP)
        second[rows, columns] = normed[rows, columns].astype(jnp.float32) + (out[rows] + shift)
    if piece == 1:
        for part in range(WIDE // STEP):
            rows = slice(part * STEP, (part + 1) * STEP)
            unit, scale[rows, :] = normalize(second[rows, :])
            second[rows, :] = unit
            h[rows, :] = (
                unit * table[3:4, WIDE : 2 * WIDE] + table[3:4, 2 * WIDE : 3 * WIDE]
            ).astype(h.dtype)


def backward_norm_two(table, dtable, dy, second, scale, dnormed, dlow, dlow_t):
    dtable[...] = jnp.zeros_like(dtable)
    sums = [jnp.zeros((8, WIDE), jnp.float32)] * 3
    for part in range(WIDE // STEP):
        rows = slice(part * STEP, (part + 1) * STEP)
        grad, *found = normalize_back(
            second[rows, :],
            scale[rows, :],
            dy[rows, :].astype(jnp.float32),
            table[3:4, WIDE : 2 * WIDE],
        )
        dnormed[rows, :] = grad
        dlow[rows, :] = grad.astype(dlow.dtype)
        sums = [total + new for total, new in zip(sums, found)]
    for i, total in enumerate(sums):
        dtable[3:4, i * WIDE : (i + 1) * WIDE] = jnp.sum(total, axis=0, keepdims=True)
    dlow_t[...] = dlow[...].T


def backward_down(size, grads, hidden, dlow_t, piece):
    @pl.loop(2 * piece, 2 * piece + 2)
    def _(i):
        start = aligned(i * size.down, 16)
        for half in range(2):
            columns = pl.ds(aligned(i * WIDE, WIDE) + half * HALF, HALF)
            value = dot_nn(dlow_t[...], hidden[:, columns])
            put_rows(grads, size.bs, 0, size.dps, start, size.down, value, 2 * half)


def backward_gelu(size, w, dtable, slope, dlow, dup, piece):
    @pl.loop(2 * piece, 2 * piece + 2)
    def _(i):
        start = aligned(i * size.down, 16)
        for half in range(2):
            columns = pl.ds(aligned(i * WIDE, WIDE) + half * HALF, HALF)
            blocks = (2 * half, 2 * half + 1)
            matrix = rows_of(w, size.bs, 0, size.dps, start, size.down, blocks)
            dhidden = dot_nn(dlow[...], matrix)
            total = jnp.zeros((8, HALF), jnp.float32)
            for part in range(WIDE // STEP):
                rows = slice(part * STEP, (part + 1) * STEP)
                dupper = dhidden[rows] * slope[rows, columns].astype(jnp.float32)
                total = total + fold_rows(dupper)
                dup[rows, columns] = dupper.astype(dup.dtype)
            dtable[2:3, columns] = jnp.sum(total, axis=0, keepdims=True)


def backward_up(size, grads, normed, dup):
    count = HALF // size.up

    @pl.loop(0, 4)
    def _(i):
        for half in range(2):
            columns = pl.ds(aligned(i * WIDE, WIDE) + half * HALF, HALF)
            value = dot_tn(dup[:, columns], normed[...])
            first = (2 * i + half) * count
            put_rows(grads, size.bs, first, count, size.out, size.up, value)


def backward_normed(size, w, dnormed, dup):
    for half in range(2):
        columns = slice(half * HALF, (half + 1) * HALF)
        blocks = (2 * half, 2 * half + 1)
        matrix = rows_of(w, size.bs, 0, size.dps, size.out, size.up, blocks)
        out = dot_nn(dup[...], matrix)
        for part in range(WIDE // STEP):
            rows = slice(part * STEP, (part + 1) * STEP)
            dnormed[rows, columns] = dnormed[rows, columns] + out[rows]


def backward_norm_one(
    size, w, table, grads, dtable, first, scale, attended, dnormed, dlow, dlow_t, delta
):
    sums = [jnp.zeros((8, WIDE), jnp.float32)] * 3
    for part in range(WIDE // STEP):
        rows = slice(part * STEP, (part + 1) * STEP)
        grad, *found = normalize_back(
            first[rows, :], scale[rows, :], dnormed[rows, :], table[1:2, WIDE : 2 * WIDE]
        )
        dnormed[rows, :] = grad
        dlow[rows, :] = grad.astype(dlow.dtype)
        sums = [total + new for total, new in zip(sums, found)]
    for i, total in enumerate(sums):
        dtable[1:2, i * WIDE : (i + 1) * WIDE] = jnp.sum(total, axis=0, keepdims=True)
    dlow_t[...] = dlow[...].T
    for block in (0, 2):
        columns = slice(block * LANES, (block + 2) * LANES)
        value = dot_nn(dlow_t[...], attended[:, columns])
        put_rows(grads, size.bs, 0, size.dps, 0, size.out, value, block)
    grad = dot_nn(dlow[...], out_rows(size, w)).astype(dlow.dtype)
    dlow[...] = grad
    product = grad.astype(jnp.float32) * attended[...].astype(jnp.float32)
    high = product.astype(jnp.bfloat16)
    rest = (product - high.astype(jnp.float32)).astype(jnp.bfloat16)
    head = lax.broadcasted_iota(jnp.int32, delta.shape, 0)
    lane = lax.broadcasted_iota(jnp.int32, delta.shape, 1)
    inside = (lane >= head * HEAD) & (lane < (head + 1) * HEAD)
    inside = jnp.where(inside, 1.0, 0.0).astype(jnp.bfloat16)
    delta[...] = dot_nt(inside, high) + dot_nt(inside, rest)


def backward_attend(mixed, probs, delta, dtable, dlow, dmixed, pair):
    scale = 1.0 / math.sqrt(HEAD)
    lane = pair * LANES
    columns = slice(lane, lane + LANES)
    key_columns = slice(WIDE + lane, WIDE + lane + LANES)
    value_columns = slice(2 * WIDE + lane, 2 * WIDE + lane + LANES)
    keys_t = mixed[:, key_columns].T
    values = mixed[:, value_columns]
    dkeys = jnp.zeros((WIDE, LANES), jnp.float32)
    dvalues = jnp.zeros((WIDE, LANES), jnp.float32)
    for part in range(2):
        rows = slice(part * HALF, (part + 1) * HALF)
        queries = mixed[rows, columns]
        grad_out = dlow[rows, columns]
        dqueries = []
        for head in range(2):
            query = queries * head_masks(scale)[head]
            grad = grad_out * head_masks(1.0)[head]
            at = 2 * pair + head
            weights = probs[at, :, rows]
            less = delta[at : at + 1, rows]
            dprobs = dot_nt(values, grad)
            dscores = by_rows(
                lambda p, dp: (p.astype(jnp.float32) * (dp - less)).astype(jnp.bfloat16),
                weights,
                dprobs,
            )
            dvalues = dvalues + dot_nn(weights, grad)
            dkeys = dkeys + dot_nn(dscores, query)
            dqueries.append(dot_nn(keys_t[head * HEAD : (head + 1) * HEAD], dscores))
        dquery = jnp.concatenate(dqueries, axis=0).T * scale
        dtable[0:1, columns] += jnp.sum(dquery, axis=0, keepdims=True)
        dmixed[rows, columns] = dquery.astype(dmixed.dtype)
    dmixed[:, key_columns] = dkeys.astype(dmixed.dtype)
    dmixed[:, value_columns] = dvalues.astype(dmixed.dtype)
    dtable[0:1, value_columns] = jnp.sum(dvalues, axis=0, keepdims=True)


def backward_mix(size, grads, h, dmixed, piece):
    count = QKV_TILE // size.qkv
    grad = dmixed[:, piece * QKV_TILE : (piece + 1) * QKV_TILE]
    put_rows(grads, size.bs, piece * count, count, 0, size.qkv, dot_tn(grad, h[...]))


def backward_input(size, w, dnormed, dmixed, dy):
    for half in range(2):
        columns = slice(half * HALF, (half + 1) * HALF)
        blocks = (2 * half, 2 * half + 1)
        matrix = rows_of(w, size.bs, 0, size.dps, 0, size.qkv, blocks)
        out = dot_nn(dmixed[...], matrix)
        for part in range(WIDE // STEP):
            rows = slice(part * STEP, (part + 1) * STEP)
            dy[rows, columns] = (dnormed[rows, columns] + out[rows]).astype(dy.dtype)


WINDOW = 384


def group_rows(group):
    rows = lax.broadcasted_iota(jnp.int32, (16, LANES), 0)
    return jnp.where(rows == group, 1.0, 0.0).astype(jnp.bfloat16)


def pack_mix(piece, qkv):
    for lb in range(SECT):
        piece[lb] = qkv[:, lb * LANES : (lb + 1) * LANES].astype(piece.dtype)


def pack_up(piece, out, up):
    rows = out.shape[0]
    for lb in range(SECT):
        lanes = slice(lb * LANES, (lb + 1) * LANES)
        piece[lb, :rows] = out[:, lanes].astype(piece.dtype)
        piece[lb, rows:] = up[:, lanes].astype(piece.dtype)


def pack_down(piece, down):
    rows = down.shape[0]
    for lb in range(SECT):
        for j in range(4):
            start = j * WIDE + lb * LANES
            piece[lb, j * rows : (j + 1) * rows] = down[:, start : start + LANES].astype(piece.dtype)


def pack_embedding(piece, weight, shift, gains, biases, square, block):
    n = weight.shape[0]
    square[...] = jnp.zeros_like(square)
    square[:GROUPS, :n] = shift[...]

    def ending(part, width):
        return jnp.concatenate([jnp.zeros((n, width - part.shape[1]), part.dtype), part], axis=1)

    third = ending(weight[:, L1 + L2 :], 3 * LANES)
    second = ending(weight[:, L1 : L1 + L2], 2 * LANES)
    blocks = [third[:, :LANES] + square[...].T[:n]]
    blocks += [third[:, LANES : 2 * LANES], third[:, 2 * LANES :]]
    blocks += [second[:, :LANES], second[:, LANES:], ending(weight[:, :L1], LANES)]
    rows = piece.shape[1] - VEC_ROWS
    if SECT * rows > 6 * n:
        blocks.append(jnp.zeros((SECT * rows - 6 * n, LANES), jnp.float32))
    flat = jnp.concatenate(blocks, axis=0).astype(piece.dtype)
    for lb in range(SECT):
        piece[lb, :rows] = flat[lb * rows : (lb + 1) * rows]
    line = jnp.concatenate([gains[...], biases[...]], axis=1)
    lines = [[line[:, at : at + LANES]] for at in range(0, line.shape[1], LANES)]
    piece[block, rows:] = rows_tile(lines).astype(piece.dtype)


def expand(series, group, x):
    empty = jnp.zeros((WINDOW - series.shape[0], series.shape[1]), series.dtype)
    x[:, :WINDOW] = jnp.concatenate([empty, series[...]], axis=0).T
    lane = lax.broadcasted_iota(jnp.int32, (x.shape[0], LANES), 1)
    x[:, WINDOW:] = jnp.where(lane == group, 1.0, 0.0).astype(x.dtype)


def embed(size, emb, pick, x, wsel, h):
    n = WIDE // size.dps
    flat = []
    for d in range(size.dps):
        place = (d // size.bs, d % size.bs, slice(0, size.lookback), slice(None))
        flat.append(jnp.concatenate([emb[(lb,) + place] for lb in range(SECT)], axis=0))
    blocks = [
        jnp.concatenate([rows[j * n : (j + 1) * n] for rows in flat], axis=0) for j in range(6)
    ]
    long, middle, short = (pick[g : g + 1, :] for g in (2, 1, 0))
    wide = jnp.concatenate(
        [
            blocks[0] * long,
            blocks[1] * long + blocks[3] * middle,
            blocks[2] * long + blocks[4] * middle + blocks[5] * short,
        ],
        axis=1,
    )
    wsel[...] = wide.T
    h[...] = dot_nt(x[...], jnp.concatenate([wide, blocks[0]], axis=1)).astype(h.dtype)


def embed_back(size, pick, x, wsel, dh, tables, grads, series_grad):
    history = series_grad.shape[0]
    series_grad[...] = dot_nt(wsel[...], dh[...])[WINDOW - history :]
    sums = dot_tn(dh[...], x[...])
    long, middle, short = (pick[g : g + 1, :].astype(jnp.float32) for g in (2, 1, 0))
    parts = [sums[:, i * LANES : (i + 1) * LANES] for i in range(4)]
    parts = [
        parts[0] * long + parts[3],
        parts[1] * long,
        parts[2] * long,
        parts[1] * middle,
        parts[2] * middle,
        parts[2] * short,
    ]
    rows = WIDE // (SECT * size.dps)
    spare = size.lookback - 6 * rows
    for pipe in range(SECT):
        block = (pipe % 2) * 2 + pipe // 2
        for dp in range(size.dps):
            start = (pipe * size.dps + dp) * rows
            pieces = [part[start : start + rows] for part in parts]
            if spare:
                pieces.append(jnp.zeros((spare, LANES), jnp.float32))
            pieces.append(vector_tile(tables.at[pipe], size.dps, dp))
            piece = jnp.concatenate(pieces, axis=0)
            grads[block, dp // size.bs, dp % size.bs] = piece.astype(grads.dtype)


def saved_shapes():
    low, wide = jnp.bfloat16, jnp.float32
    return [
        ((WIDE, WIDE), low),
        ((WIDE, 3 * WIDE), low),
        ((2 * SECT, WIDE, WIDE), low),
        ((WIDE, WIDE), low),
        ((WIDE, WIDE), wide),
        ((WIDE, WIDE), low),
        ((WIDE, 4 * WIDE), low),
        ((WIDE, 4 * WIDE), low),
        ((WIDE, WIDE), wide),
        ((SECT, 4 * WIDE), wide),
        ((WIDE, LANES), wide),
        ((WIDE, LANES), wide),
    ]


def chunk_shape(size, rows):
    return (SECT, ZS, size.bs, rows, LANES)


HALVES = (2, 2, 2, 2)
CROSS = (2,)


def follow(plan, section, act, compute):
    seen = {}
    for step in plan:
        if len(step) == 1:
            piece = seen.get(step[0], 0)
            seen[step[0]] = piece + 1
            compute(step[0], piece)
            continue
        op, kind, offset = step
        where = section + offset
        if isinstance(where, int):
            if 0 <= where < SECT:
                act(op, kind, where)
        elif offset == 0:
            act(op, kind, where)
        else:
            inside = where < SECT if offset > 0 else where >= 0

            @pl.when(inside)
            def _():
                act(op, kind, where)


def forward_kernel(dps, groups, *refs):
    size = Sizes(dps)
    given, refs = refs[:9], refs[9:]
    out, copies_out, wsel, x, refs = refs[0], refs[1:4], refs[4], refs[5], refs[6:]
    kept, local, refs = refs[:12], refs[12:24], refs[24:]
    wholes, refs = refs[:4], refs[4:]
    pieces, held, refs = refs[:4], refs[4:13], refs[13:]
    emb_rows, pick, refs = refs[0], refs[1], refs[2:]
    given_sem, out_sem, kept_sem, own_sem, p_send, p_recv, send, recv = refs
    h, mixed, probs, attended, first, normed, slope, hidden, second, table, scale_1, scale_2 = local
    at = Place(dps)

    own = [
        pltpu.make_async_copy(
            pieces[kind].at[at.block],
            wholes[kind].at[at.pipe, at.block, at.z, at.b]
            if kind < EMB
            else wholes[kind].at[at.block, at.z, at.b],
            own_sem.at[kind],
        )
        for kind in range(4)
    ]
    def split(kind, back):
        copies = []
        for k in range(1, SECT):
            if back:
                region = wholes[kind].at[at.pipe_at(SECT - k), at.block, at.z, at.b]
                src = region
            else:
                block = at.blocks[k]
                region = wholes[kind].at[at.pipe, block, at.z, at.b]
                src = pieces[kind].at[block]
            sems = p_send.at[kind, k - 1], p_recv.at[kind, k - 1]
            copies.append(remote(src, region, *sems, (at.pipe_at(k), at.dp)))
        return copies

    def chunk(kind, section):
        if kind == EMB:
            return Spread(at, wholes[kind], send.at[3 * SECT], recv.at[3 * SECT])
        number = 3 * section + kind
        sort = SpreadCross if kind in CROSS else Spread
        return sort(at, wholes[kind].at[section], send.at[number], recv.at[number], HALVES[kind])

    def keep(kind, section):
        src, dst = wholes[kind].at[section], copies_out[kind].at[section]
        return pltpu.make_async_copy(src, dst, out_sem.at[kind, section])

    arrived = []

    def act(op, kind, section):
        if op == 0:
            if kind not in arrived:
                arrived.append(kind)
                own[kind].wait()
                if kind == EMB:
                    chunk(kind, section).start(0)
                    return
                for copy in split(kind, True):
                    copy.wait_recv()
                for copy in split(kind, False):
                    copy.wait_send()
                if kind == 0:
                    copies_start(split(1, False))
                    copies_start(split(2, False))
            chunk(kind, section).start(0)
        elif op < 4:
            chunk(kind, section).move(op - 1)
            if op == 1 and kind == EMB:
                gets[0].wait()
                expand(series, groups[0], x)
        else:
            chunk(kind, section).land(3)
            if kind != EMB:
                keep(kind, section).start(priority=1)

    def saves(section, early):
        which = (1, 2, 3, 4, 5, 9, 10) if early else (6, 7, 8, 11)
        return [
            pltpu.make_async_copy(local[i], kept[i].at[section], kept_sem.at[i]) for i in which
        ]

    series, embed_weight, embed_bias, qkv, out_w, up_w, down_w, gains, biases = held
    gets = copies_of(zip(given, held), given_sem)
    for i in (3, 7, 8, 1, 2, 4, 5, 6, 0):
        gets[i].start(priority=1)
    pick[...] = group_rows(groups[0])
    at.greet()
    gets[3].wait()
    pack_mix(pieces[0], qkv)
    own[0].start(priority=1)
    at.met()
    copies_start(split(0, False))
    copies_wait(gets[1:3] + gets[7:9])
    pack_embedding(
        pieces[EMB], embed_weight, embed_bias, gains, biases, emb_rows, at.block
    )
    own[EMB].start(priority=1)
    copies_wait(gets[4:7])
    pack_up(pieces[1], out_w, up_w)
    own[1].start(priority=1)
    pack_down(pieces[2], down_w)
    own[2].start(priority=1)
    table[...] = jnp.zeros_like(table)

    def before(name, piece):
        embed(size, wholes[EMB], pick, x, wsel, h)

    follow(FORWARD_START, 0, act, before)

    @pl.loop(0, SECT)
    def _(section):
        att, up, down = (ref.at[section] for ref in wholes[:3])
        keep_h = pltpu.make_async_copy(h, kept[0].at[section], kept_sem.at[0])

        def compute(name, piece):
            if name == "mix":
                if piece == 0:

                    @pl.when(section > 0)
                    def _():
                        copies_wait(saves(section - 1, True))

                    keep_h.start(priority=1)
                    block = section % 2 * 2 + section // 2
                    read_vectors(wholes[EMB], table, size.bs, size.lookback, block)
                forward_mix(size, att, table, h, mixed, piece)
            elif name == "attend":
                forward_attend(mixed, probs, attended, piece)
            elif name == "project":
                forward_project(size, up, table, h, attended, first, scale_1, normed)
                copies_begin(saves(section, True))
            elif name == "up":
                if piece == 0:

                    @pl.when(section > 0)
                    def _():
                        copies_wait(saves(section - 1, False))

                forward_up(size, up, table, normed, slope, hidden, piece)
            else:
                if piece == 0:
                    keep_h.wait()
                forward_down(size, down, table, normed, hidden, second, scale_2, h, piece)
                if piece == 1:
                    copies_begin(saves(section, False))

        follow(FORWARD_PERIOD, section, act, compute)

    out[...] = h[...]
    copies_wait(saves(SECT - 1, True))
    copies_wait(saves(SECT - 1, False))
    for kind in range(3):
        copies_wait([keep(kind, section) for section in range(SECT)])


def copies_of(pairs, sems):
    return [pltpu.make_async_copy(src, dst, sems.at[i]) for i, (src, dst) in enumerate(pairs)]


def forward_all(groups, given, dps):
    size = Sizes(dps)
    low, wide = jnp.bfloat16, jnp.float32
    shapes = saved_shapes()
    rows = (size.qkv, size.dense, size.wide, size.emb)
    chunks = [chunk_shape(size, count) for count in rows]
    anywhere = pl.BlockSpec(memory_space=pl.ANY)
    inside = pl.BlockSpec(memory_space=pltpu.VMEM)
    outs = [((WIDE, WIDE), low)]
    outs += [((SECT,) + shape, low) for shape in chunks[:3]]
    outs += [((WINDOW, WIDE), low), ((WIDE, WIDE), low)]
    outs += [((SECT,) + shape, dtype) for shape, dtype in shapes]
    scratch = shapes + [((SECT,) + shape, low) for shape in chunks[:3]] + [(chunks[3], low)]
    scratch += [((SECT, count, LANES), low) for count in rows]
    scratch += [(array.shape, array.dtype) for array in given]
    scratch += [((LANES, LANES), wide), ((16, LANES), low)]
    slots = max(Spread.slots(size.bs), SpreadCross.slots(size.bs))
    dma = pltpu.SemaphoreType.DMA
    return pl.pallas_call(
        partial(forward_kernel, dps),
        out_shape=[jax.ShapeDtypeStruct(shape, dtype) for shape, dtype in outs],
        in_specs=[pl.BlockSpec(memory_space=pltpu.SMEM)] + [anywhere] * len(given),
        out_specs=[inside] + [anywhere] * 3 + [inside] * 2 + [anywhere] * len(shapes),
        scratch_shapes=[pltpu.VMEM(shape, dtype) for shape, dtype in scratch]
        + [
            dma((len(given),)),
            dma((3, SECT)),
            dma((len(shapes),)),
            dma((4,)),
            dma((3, SECT - 1)),
            dma((3, SECT - 1)),
            dma((1 + 3 * SECT, slots)),
            dma((1 + 3 * SECT, slots)),
        ],
        compiler_params=pltpu.CompilerParams(
            collective_id=0, has_side_effects=True, vmem_limit_bytes=60 * 1024 * 1024
        ),
        name="gather_forward",
    )(groups, *given)


FETCHES = {
    ("norm2", 0): (("second", "scale_2"), ("second", "scale_2")),
    ("down", 0): (("hidden",), ()),
    ("down", 1): ((), ("hidden",)),
    ("gelu", 0): (("slope", 2), ()),
    ("gelu", 1): ((), ("slope", 2)),
    ("up", 0): (("normed",), ("normed",)),
    ("normed", 0): ((1,), ()),
    ("norm1", 0): (("first", "scale_1", "attended"), ("first", "scale_1", "attended", 1)),
    ("attend", 0): (("mixed", "probs"), ()),
    ("attend", 3): ((), ("mixed", "probs")),
    ("mix", 0): (("h",), ()),
    ("mix", 1): ((), ("h",)),
    ("input", 0): ((0,), (0,)),
}


def backward_kernel(dps, groups, att, up, down, cotangent, x_in, wsel_in, *refs):
    size = Sizes(dps)
    kept, refs = refs[:12], refs[12:]
    series_grad, outs, refs = refs[0], refs[1:5], refs[5:]
    local, refs = refs[:11], refs[11:]
    tables, w_att, w_up, w_down, dtables, dy, dnormed, dlow, dlow_t, dmixed, dup = refs[:11]
    x, wsel, pick, delta, refs = *refs[11:15], refs[15:]
    kinds = []
    for kind in range(4):
        count = 6 if kind in CROSS else 5
        kinds.append(refs[:4] + (refs[4 : 4 + count],))
        refs = refs[4 + count :]
    w_sem, kept_sem, table_sem, late_sem, out_sem, p_send, p_recv, send, recv, credit = refs
    h, mixed, probs, attended, first, normed, slope, hidden, second, scale_1, scale_2 = local
    at = Place(dps)
    last = SECT - 1

    def weights(kind, section):
        src, dst = ((att, w_att), (up, w_up), (down, w_down))[kind]
        return pltpu.make_async_copy(src.at[section], dst, w_sem.at[kind])

    names = ("h", "mixed", "probs", "attended", "first", "normed", "slope", "hidden", "second")
    names += ("table", "scale_1", "scale_2")
    held = dict(zip(names[:9] + names[10:], local))

    def fetches(section, *wanted):
        found = []
        for name in wanted:
            if isinstance(name, int):
                found.append(weights(name, section))
            else:
                i = names.index(name)
                dst = held[name]
                found.append(pltpu.make_async_copy(kept[i].at[section], dst, kept_sem.at[i]))
        return found

    def chunk(kind, i):
        grads, totals, finals, landing, bufs = kinds[kind]
        sort = FoldCross if kind in CROSS else Fold
        refs = (grads, totals.at[i % 2], landing, bufs, finals.at[i])
        return sort(at, *refs, send.at[kind], recv.at[kind], credit.at[kind], HALVES[kind])

    def hand_over(kind, i):
        landing = outs[kind].at[at.block]
        final = kinds[kind][2].at[i]
        return (
            pltpu.make_async_copy(final, landing, out_sem.at[kind]),
            remote(final, landing, p_send.at[kind, i], p_recv.at[kind, at.pipe], (last - i, at.dp)),
        )

    def act(op, kind, i):
        again, more = (False, False) if kind == EMB else (i > 0, i < last)
        if op == 0:
            chunk(kind, i).start(0, again)
        elif op < 4:
            chunk(kind, i).move(op - 1, again, more)
        else:
            chunk(kind, i).land(3, more)
            if kind == EMB:
                outs[kind][...] = kinds[kind][2][0]
            else:
                here, away = hand_over(kind, i)

                @pl.when(at.pipe == last - i)
                def _():
                    here.start(priority=1)

                @pl.when(at.pipe != last - i)
                def _():
                    away.start()

    at.greet()
    get_tables = pltpu.make_async_copy(kept[9], tables, table_sem)
    late = copies_of(((cotangent, dy), (x_in, x), (wsel_in, wsel)), late_sem)
    copies_begin([late[0], get_tables] + fetches(last, "second", "scale_2", "hidden"))
    copies_begin(fetches(last, "slope", 2, "normed", 1, "first", "scale_1", "attended"))
    copies_begin(fetches(last, "mixed", "probs", "h", 0) + late[1:])
    pick[...] = group_rows(groups[0])
    copies_wait([late[0], get_tables])

    @pl.loop(0, SECT)
    def _(i):
        section = last - i
        table, dtable = tables.at[section], dtables.at[section]

        def compute(name, piece):
            need, free = FETCHES.get((name, piece), ((), ()))
            copies_wait(fetches(section, *need))
            if name == "norm2":
                backward_norm_two(table, dtable, dy, second, scale_2, dnormed, dlow, dlow_t)
                pl.when(i == 0)(at.met)
            elif name == "down":
                backward_down(size, kinds[2][0], hidden, dlow_t, piece)
            elif name == "gelu":
                backward_gelu(size, w_down, dtable, slope, dlow, dup, piece)
            elif name == "up":
                backward_up(size, kinds[1][0], normed, dup)
            elif name == "normed":
                backward_normed(size, w_up, dnormed, dup)
            elif name == "norm1":
                backward_norm_one(
                    size,
                    w_up,
                    table,
                    kinds[1][0],
                    dtable,
                    first,
                    scale_1,
                    attended,
                    dnormed,
                    dlow,
                    dlow_t,
                    delta,
                )
            elif name == "attend":
                backward_attend(mixed, probs, delta, dtable, dlow, dmixed, piece)
            elif name == "mix":
                backward_mix(size, kinds[0][0], h, dmixed, piece)
            else:
                backward_input(size, w_att, dnormed, dmixed, dy)
            if free:

                @pl.when(section > 0)
                def _():
                    copies_begin(fetches(section - 1, *free))

        follow(BACKWARD_PERIOD, i, act, compute)

    def after(name, piece):
        copies_wait(late[1:])
        embed_back(size, pick, x, wsel, dy, dtables, kinds[EMB][0], series_grad)

    follow(BACKWARD_END, 0, act, after)

    for kind in range(3):
        for i in range(SECT):
            here, away = hand_over(kind, i)

            @pl.when(at.pipe == last - i)
            def _():
                here.wait()

            @pl.when(at.pipe != last - i)
            def _():
                away.wait_send()

        for k in range(1, SECT):
            other = at.pipe_at(k)
            landing = outs[kind].at[at.blocks[k]]
            sems = p_send.at[kind, 0], p_recv.at[kind, other]
            remote(landing, landing, *sems, (other, at.dp)).wait_recv()


def backward_all(groups, weights, cotangent, x, wsel, kept, history, dps):
    size = Sizes(dps)
    low, wide = jnp.bfloat16, jnp.float32
    anywhere = pl.BlockSpec(memory_space=pl.ANY)
    inside = pl.BlockSpec(memory_space=pltpu.VMEM)
    shapes = saved_shapes()
    kind_rows = (size.qkv, size.dense, size.wide, size.emb)
    scratch = shapes[:9] + shapes[10:] + [((SECT,) + shapes[9][0], wide)]
    scratch += [(chunk_shape(size, rows), low) for rows in kind_rows[:3]]
    scratch += [
        ((SECT,) + shapes[9][0], wide),
        ((WIDE, WIDE), low),
        ((WIDE, WIDE), wide),
        ((WIDE, WIDE), low),
        ((WIDE, WIDE), low),
        ((WIDE, 3 * WIDE), low),
        ((WIDE, 4 * WIDE), low),
        ((WIDE, WIDE), low),
        ((WINDOW, WIDE), low),
        ((16, LANES), low),
        ((16, WIDE), wide),
    ]
    for kind, rows in enumerate(kind_rows):
        sets, results = (1, 1) if kind == EMB else (2, SECT)
        scratch += [
            (chunk_shape(size, rows), low),
            ((sets, 2, ZS, size.bs, rows, LANES), low),
            ((results, rows, LANES), low),
            ((2, ZS, size.bs, rows, LANES), low),
        ]
        sort = FoldCross if kind in CROSS else Fold
        scratch += [(shape, low) for shape in sort.buffers(size.bs, rows, HALVES[kind])]
    slots = max(Fold.slots(size.bs), FoldCross.slots(size.bs))
    dma = pltpu.SemaphoreType.DMA
    return pl.pallas_call(
        partial(backward_kernel, dps),
        out_shape=[jax.ShapeDtypeStruct((history, WIDE), wide)]
        + [jax.ShapeDtypeStruct((SECT, rows, LANES), low) for rows in kind_rows[:3]]
        + [jax.ShapeDtypeStruct((size.emb, LANES), low)],
        in_specs=[pl.BlockSpec(memory_space=pltpu.SMEM)] + [anywhere] * (6 + len(kept)),
        out_specs=[inside] + [anywhere] * 3 + [inside],
        scratch_shapes=[pltpu.VMEM(shape, dtype) for shape, dtype in scratch]
        + [
            dma((3,)),
            dma((12,)),
            dma(()),
            dma((3,)),
            dma((3,)),
            dma((3, SECT)),
            dma((3, SECT)),
            dma((4, slots)),
            dma((4, slots)),
            pltpu.SemaphoreType.REGULAR((4, slots)),
        ],
        compiler_params=pltpu.CompilerParams(
            collective_id=1, has_side_effects=True, vmem_limit_bytes=60 * 1024 * 1024
        ),
        name="backward_fold",
    )(groups, *weights, cotangent, x, wsel, *kept)


def finish_kernel(dps, n_gains, n_biases, *refs):
    size = Sizes(dps)
    given, refs = refs[:6], refs[6:]
    block_out, series_out, embed_w, embed_b, qkv, out, up_out, down_out, gains, biases = refs[:10]
    att, up, down, emb, sems = refs[10:]
    copies = copies_of(zip(given, (att, up, down, emb, block_out, series_out)), sems)
    copies_start(copies)
    copies_wait(copies[:4])
    for lb in range(SECT):
        lanes = slice(lb * LANES, (lb + 1) * LANES)
        qkv[:, lanes] = att[lb].astype(jnp.float32)
        out[:, lanes] = up[lb, : size.out].astype(jnp.float32)
        up_out[:, lanes] = up[lb, size.out :].astype(jnp.float32)
        for j in range(4):
            rows = slice(j * size.down, (j + 1) * size.down)
            start = j * WIDE + lb * LANES
            down_out[:, start : start + LANES] = down[lb, rows].astype(jnp.float32)
    vectors = emb[size.lookback :].astype(jnp.float32)
    count = -(-(n_gains + n_biases) // LANES)
    flat = jnp.concatenate([vectors[row : row + 1] for row in range(count)], axis=1)
    gains[...] = flat[:, :n_gains]
    biases[...] = flat[:, n_gains : n_gains + n_biases]
    rows = WIDE // (SECT * dps)
    packed = emb[: size.lookback].astype(jnp.float32)
    packed = [packed[i * rows : (i + 1) * rows] for i in range(6)]
    square = jnp.concatenate([packed[0], jnp.zeros((LANES - rows, LANES), jnp.float32)], axis=0)
    embed_b[...] = square.T[:GROUPS, :rows]
    packed = jnp.concatenate(packed, axis=1)
    ends = ((6 * LANES, L1), (5 * LANES, L2), (3 * LANES, L3))
    embed_w[...] = jnp.concatenate([packed[:, end - span : end] for end, span in ends], axis=1)
    copies_wait(copies[4:])


def finish_all(sums, block, series, n_gains, n_biases, dps):
    size = Sizes(dps)
    wide = jnp.float32
    columns = WIDE // (SECT * dps)
    outs = [
        (block.shape, block.dtype),
        (series.shape, wide),
        ((columns, L1 + L2 + L3), wide),
        ((GROUPS, columns), wide),
        ((size.qkv, WIDE), wide),
        ((size.out, WIDE), wide),
        ((size.up, WIDE), wide),
        ((size.down, 4 * WIDE), wide),
        ((1, n_gains), wide),
        ((1, n_biases), wide),
    ]
    anywhere = pl.BlockSpec(memory_space=pl.ANY)
    inside = pl.BlockSpec(memory_space=pltpu.VMEM)
    return pl.pallas_call(
        partial(finish_kernel, dps, n_gains, n_biases),
        out_shape=[jax.ShapeDtypeStruct(shape, dtype) for shape, dtype in outs],
        in_specs=[anywhere] * 6,
        out_specs=[inside] * 10,
        scratch_shapes=[pltpu.VMEM(array.shape, array.dtype) for array in sums]
        + [pltpu.SemaphoreType.DMA((6,))],
        compiler_params=pltpu.CompilerParams(vmem_limit_bytes=60 * 1024 * 1024),
        name="finish",
    )(*sums, block, series)


def per_device(
    series,
    groups,
    cotangent,
    embed_weight,
    embed_bias,
    qkv_weight,
    out_weight,
    up_weight,
    down_weight,
    gains,
    biases,
):
    dps = lax.axis_size("dp")
    given = (
        series[0],
        embed_weight.T,
        embed_bias,
        qkv_weight[0],
        out_weight[0],
        up_weight[0],
        down_weight[0],
        gains,
        biases,
    )
    block_output, att, up, down, wsel, x, *kept = forward_all(groups, given, dps)
    series_grad, *sums = backward_all(
        groups, (att, up, down), cotangent[0], x, wsel, kept, series.shape[1], dps
    )
    outs = finish_all(sums, block_output, series_grad, gains.shape[1], biases.shape[1], dps)
    block_output, series_grad, embed_w, embed_b, qkv, out, up, down, gain_sum, bias_sum = outs
    return (
        block_output[None],
        series_grad[None],
        embed_w.T,
        embed_b,
        qkv[None],
        out[None],
        up[None],
        down[None],
        gain_sum,
        bias_sum,
    )


def solution(mesh):
    return jax.shard_map(
        per_device,
        mesh=mesh,
        in_specs=(
            P(("pipe", "dp"), None, None),
            P(("pipe", "dp")),
            P(("pipe", "dp"), None, None),
            P(None, "dp"),
            P(None, "dp"),
            P("pipe", "dp", None),
            P("pipe", "dp", None),
            P("pipe", "dp", None),
            P("pipe", "dp", None),
            P("pipe", "dp"),
            P("pipe", "dp"),
        ),
        out_specs=(
            P(("pipe", "dp"), None, None),
            P(("pipe", "dp"), None, None),
            P(None, ("pipe", "dp")),
            P(None, ("pipe", "dp")),
            P("pipe", "dp", None),
            P("pipe", "dp", None),
            P("pipe", "dp", None),
            P("pipe", "dp", None),
            P("pipe", "dp"),
            P("pipe", "dp"),
        ),
        check_vma=False,
    )
```

```python
from functools import partial
import math

import jax
import jax.numpy as jnp
from jax import lax
from jax.experimental import pallas as pl
from jax.experimental.pallas import tpu as pltpu
from jax.sharding import PartitionSpec as P

HEAD = 64
L1 = 96
L2 = 192
L3 = 336
GROUPS = 3


NORM_EPS = 1e-05


MESH = pl.DeviceIdType.MESH
LANES = 128
ZS = 4
SECT = 4
EMB = 3


class Place:
    def __init__(self, dps):
        self.bs = bs = dps // ZS
        pipe = lax.axis_index("pipe")
        dp = lax.axis_index("dp")
        self.pipe, self.dp = pipe, dp
        self.x, self.c = x, c = lax.div(pipe, 2), lax.rem(pipe, 2)
        self.z, self.b = z, b = lax.div(dp, bs), lax.rem(dp, bs)
        self.block = c * 2 + x
        self.other_block = c * 2 + 1 - x
        self.x_peer = ((1 - x) * 2 + c, dp)
        self.core_peer = (x * 2 + 1 - c, dp)
        self.pipes = [lax.rem(pipe + k, SECT) for k in range(SECT)]
        self.blocks = [self.block_of(other) for other in self.pipes]
        self.zs = [lax.rem(z + k, ZS) for k in range(ZS)]
        self.bees = [lax.rem(b + k, bs) for k in range(bs)]
        self.z_peers = [(pipe, other * bs + b) for other in self.zs]
        self.b_peers = [(pipe, z * bs + other) for other in self.bees]

    def block_of(self, pipe):
        return lax.rem(pipe, 2) * 2 + lax.div(pipe, 2)

    def pipe_at(self, step):
        return self.pipes[step % SECT]

    def z_at(self, step):
        return self.zs[step % ZS]

    def b_at(self, step):
        return self.bees[step % self.bs]

    def z_peer(self, step):
        return self.z_peers[step % ZS]

    def b_peer(self, step):
        return self.b_peers[step % self.bs]

    def greet(self):
        barrier = pltpu.get_barrier_semaphore()
        peers = [(self.pipe_at(k), self.dp) for k in range(1, SECT)]
        peers += [self.z_peer(k) for k in range(1, ZS)]
        peers += [self.b_peer(k) for k in range(1, self.bs)]
        for peer in peers:
            pl.semaphore_signal(barrier, inc=1, device_id=peer, device_id_type=MESH)

    def met(self):
        pl.semaphore_wait(pltpu.get_barrier_semaphore(), SECT + ZS + self.bs - 3)


def remote(src, dst, send, recv, peer):
    return pltpu.make_async_remote_copy(
        src_ref=src, dst_ref=dst, send_sem=send, recv_sem=recv, device_id=peer, device_id_type=MESH
    )


FORWARD_START = (
    (0, 3, 0),
    (0, 0, 0),
    (0, 2, 0),
    (1, 3, 0),
    (1, 0, 0),
    (0, 1, 0),
    (2, 3, 0),
    (2, 0, 0),
    (0, 0, 1),
    (1, 1, 0),
    (1, 2, 0),
    (3, 3, 0),
    (0, 2, 1),
    (1, 0, 1),
    (2, 1, 0),
    (4, 3, 0),
    (3, 0, 0),
    ("embed",),
    (4, 0, 0),
)
FORWARD_PERIOD = (
    ("mix",),
    (0, 1, 1),
    (2, 0, 1),
    ("mix",),
    ("attend",),
    (3, 1, 0),
    ("attend",),
    (2, 2, 0),
    ("attend",),
    (0, 0, 2),
    (4, 1, 0),
    ("attend",),
    ("project",),
    (1, 1, 1),
    ("up",),
    (1, 2, 1),
    (0, 2, 2),
    (3, 2, 0),
    ("up",),
    (1, 0, 2),
    ("up",),
    (2, 1, 1),
    (3, 0, 1),
    (4, 2, 0),
    ("up",),
    ("down",),
    (4, 0, 1),
    ("down",),
)
BACKWARD_PERIOD = (
    ("norm2",),
    (1, 0, -1),
    ("down",),
    ("down",),
    ("gelu",),
    ("gelu",),
    (2, 1, -1),
    (0, 2, 0),
    ("up",),
    ("normed",),
    (2, 0, -1),
    ("norm1",),
    (4, 1, -2),
    (4, 2, -2),
    (1, 2, 0),
    (3, 1, -1),
    (0, 1, 0),
    ("attend",),
    ("attend",),
    ("attend",),
    ("attend",),
    (3, 2, -1),
    (1, 1, 0),
    (4, 0, -2),
    (3, 0, -1),
    ("mix",),
    ("mix",),
    (0, 0, 0),
    ("input",),
    (2, 2, 0),
)
BACKWARD_END = (
    ("embed",),
    (1, 0, 3),
    (2, 1, 3),
    (2, 0, 3),
    (4, 1, 2),
    (4, 2, 2),
    (3, 1, 3),
    (0, 3, 0),
    (3, 2, 3),
    (4, 0, 2),
    (1, 3, 0),
    (3, 0, 3),
    (2, 3, 0),
    (3, 3, 0),
    (4, 1, 3),
    (4, 2, 3),
    (4, 0, 3),
    (4, 3, 0),
)


def copies_start(copies):
    for copy in copies:
        copy.start()


def copies_begin(copies):
    for copy in copies:
        copy.start(priority=1)


def copies_wait(copies):
    for copy in copies:
        copy.wait()


class Spread:
    def __init__(self, at, out, send, recv, half=ZS // 2):
        self.at, self.out, self.send, self.recv = at, out, send, recv
        nb = at.bs - 1
        self.slot_z = 0
        self.slot_b1 = ZS - 1
        self.slot_x1 = self.slot_b1 + nb
        self.slot_x2 = self.slot_x1 + 1
        self.slot_b2 = self.slot_x2 + 1
        self.slot_c = self.slot_b2 + nb
        self.half = half

    @staticmethod
    def slots(bs):
        return ZS - 1 + 2 * (bs - 1) + 3

    def copy(self, region, slot, peer):
        return remote(region, region, self.send.at[slot], self.recv.at[slot], peer)

    def copies(self, stage, back):
        at, out, half = self.at, self.out, self.half
        rest = pl.ds(half, ZS - half)
        x_block = at.other_block if back else at.block
        if stage == 0:
            return [
                self.copy(
                    out.at[at.block, at.z_at(ZS - k) if back else at.z, at.b],
                    self.slot_z + k - 1,
                    at.z_peer(k),
                )
                for k in range(1, ZS)
            ]
        if stage == 3:
            core = 1 - at.c if back else at.c
            return [self.copy(out.at[pl.ds(core * 2, 2)], self.slot_c, at.core_peer)]
        copies = []
        for k in range(1, at.bs):
            b = at.b_at(at.bs - k) if back else at.b
            if stage == 1:
                region, slot = out.at[at.block, pl.ds(0, half), b], self.slot_b1
            else:
                region, slot = out.at[pl.ds(at.c * 2, 2), rest, b], self.slot_b2
            copies.append(self.copy(region, slot + k - 1, at.b_peer(k)))
        if stage == 1:
            region, slot = out.at[x_block, rest, at.b], self.slot_x1
        else:
            region, slot = out.at[x_block, pl.ds(0, half)], self.slot_x2
        copies.append(self.copy(region, slot, at.x_peer))
        return copies

    def start(self, stage):
        copies_start(self.copies(stage, False))

    def land(self, stage):
        for copy in self.copies(stage, True):
            copy.wait_recv()
        for copy in self.copies(stage, False):
            copy.wait_send()

    def move(self, stage):
        self.land(stage)
        self.start(stage + 1)


class SpreadCross(Spread):
    @staticmethod
    def slots(bs):
        return 2 * bs + 2 * ZS - 1

    def copies(self, stage, back):
        at, out = self.at, self.out
        rows = out.shape[-2]
        cut = rows // 32 * 16
        some, rest = pl.ds(0, cut), pl.ds(cut, rows - cut)
        core = 1 - at.c if back else at.c
        if stage == 3:
            return [self.copy(out.at[pl.ds(core * 2, 2)], 2 * at.bs + 2 * ZS - 2, at.core_peer)]
        both = pl.ds(at.c * 2, 2)
        x_block = at.other_block if back else at.block
        copies = []
        if stage == 1:
            for k in range(1, ZS):
                z = at.z_at(ZS - k) if back else at.z
                copies.append(self.copy(out.at[both, z, at.b, some], at.bs + k - 1, at.z_peer(k)))
                slot = at.bs + ZS + k - 2
                copies.append(self.copy(out.at[at.block, z, :, rest], slot, at.z_peer(k)))
            return copies
        base = 0 if stage == 0 else at.bs + 2 * ZS - 2
        for k in range(1, at.bs):
            b = at.b_at(at.bs - k) if back else at.b
            region = out.at[at.block, at.z, b, rest] if stage == 0 else out.at[both, :, b, some]
            copies.append(self.copy(region, base + k, at.b_peer(k)))
        if stage == 0:
            region = out.at[x_block, at.z, at.b, some]
        else:
            region = out.at[x_block, :, :, rest]
        copies.append(self.copy(region, base, at.x_peer))
        return copies


class Fold:
    def __init__(self, at, grads, total, landing, bufs, final, send, recv, credit, half):
        self.at, self.grads, self.total = at, grads, total
        self.landing, self.bufs, self.final = landing, bufs, final
        self.send, self.recv, self.credit = send, recv, credit
        self.half = half
        nb = at.bs - 1
        self.slot_x1 = 1
        self.slot_b1 = 2
        self.slot_x2 = 2 + nb
        self.slot_b2 = 3 + nb
        self.slot_z = 3 + 2 * nb

    @staticmethod
    def slots(bs):
        return 3 + 2 * (bs - 1) + ZS - 1

    @staticmethod
    def buffers(bs, rows, half):
        nb = max(bs - 1, 1)
        rest = ZS - half
        return [
            (half, bs, rows, LANES),
            (nb, 2, rest, rows, LANES),
            (rest, rows, LANES),
            (nb, half, rows, LANES),
            (ZS - 1, rows, LANES),
        ]

    def core_parts(self):
        other = self.grads.at[pl.ds((1 - self.at.c) * 2, 2)]
        return [(other, self.landing, 0, self.at.core_peer, self.at.core_peer)]

    def parts(self, stage):
        at, half, total, bufs = self.at, self.half, self.total, self.bufs
        if stage == 0:
            return self.core_parts()
        if stage == 3:
            return [
                (
                    total.at[at.x, at.z_at(k), at.b],
                    bufs[4].at[k - 1],
                    self.slot_z + k - 1,
                    at.z_peer(k),
                    at.z_peer(ZS - k),
                )
                for k in range(1, ZS)
            ]
        rest = pl.ds(half, ZS - half)
        found = []
        for k in range(1, at.bs):
            if stage == 1:
                src, buf, slot = total.at[:, rest, at.b_at(k)], bufs[1], self.slot_b1
            else:
                src, buf, slot = total.at[at.x, pl.ds(0, half), at.b_at(k)], bufs[3], self.slot_b2
            found.append((src, buf.at[k - 1], slot + k - 1, at.b_peer(k), at.b_peer(at.bs - k)))
        if stage == 1:
            src, buf, slot = total.at[1 - at.x, pl.ds(0, half)], bufs[0], self.slot_x1
        else:
            src, buf, slot = total.at[1 - at.x, rest, at.b], bufs[2], self.slot_x2
        found.append((src, buf, slot, at.x_peer, at.x_peer))
        return found

    def start(self, stage, again):
        for src, buf, slot, to, _ in self.parts(stage):
            if again is not False:

                @pl.when(again)
                def _():
                    pl.semaphore_wait(self.credit.at[slot], 1)

            remote(src, buf, self.send.at[slot], self.recv.at[slot], to).start()

    def land(self, stage, more):
        parts = self.parts(stage)
        for src, buf, slot, to, _ in parts:
            remote(src, buf, self.send.at[slot], self.recv.at[slot], to).wait()
        self.add(stage)
        if more is not False:

            @pl.when(more)
            def _():
                for _, _, slot, _, origin in parts:
                    pl.semaphore_signal(
                        self.credit.at[slot], inc=1, device_id=origin, device_id_type=MESH
                    )

    def add_core(self):
        at, bs, total = self.at, self.at.bs, self.total

        @pl.loop(0, 2 * ZS * bs)
        def _(i):
            z, b = i // bs % ZS, i % bs
            x = i // (ZS * bs)
            total[x, z, b] = self.grads[at.c * 2 + x, z, b] + self.landing[x, z, b]

    def add(self, stage):
        at, half, bs = self.at, self.half, self.at.bs
        total, bufs = self.total, self.bufs
        rest = ZS - half
        if stage == 0:
            self.add_core()
        elif stage == 1:

            @pl.loop(0, half * bs)
            def _(i):
                z, b = i // bs, i % bs
                total[at.x, z, b] = total[at.x, z, b] + bufs[0][z, b]

            @pl.loop(0, 2 * rest)
            def _(i):
                x, z = i // rest, i % rest
                for k in range(bs - 1):
                    total[x, half + z, at.b] = total[x, half + z, at.b] + bufs[1][k, x, z]

        elif stage == 2:

            @pl.loop(0, rest)
            def _(z):
                total[at.x, half + z, at.b] = total[at.x, half + z, at.b] + bufs[2][z]

            @pl.loop(0, half)
            def _(z):
                for k in range(bs - 1):
                    total[at.x, z, at.b] = total[at.x, z, at.b] + bufs[3][k, z]

        else:
            self.finish([bufs[4][k] for k in range(ZS - 1)])

    def finish(self, pieces):
        at = self.at
        done = self.total[at.x, at.z, at.b].astype(jnp.float32)
        for piece in pieces:
            done = done + piece.astype(jnp.float32)
        self.final[...] = done.astype(self.final.dtype)

    def move(self, stage, again, more):
        self.land(stage, more)
        self.start(stage + 1, again)


class FoldCross(Fold):
    @staticmethod
    def slots(bs):
        return 2 * bs + 2 * ZS - 1

    @staticmethod
    def buffers(bs, rows, half):
        nb = max(bs - 1, 1)
        cut = rows // 32 * 16
        rest = rows - cut
        return [
            (nb, 2, ZS, cut, LANES),
            (ZS, bs, rest, LANES),
            (ZS - 1, 2, cut, LANES),
            (ZS - 1, bs, rest, LANES),
            (cut, LANES),
            (nb, rest, LANES),
        ]

    def cuts(self):
        rows = self.total.shape[-2]
        cut = rows // 32 * 16
        return pl.ds(0, cut), pl.ds(cut, rows - cut)

    def parts(self, stage):
        at, total, bufs = self.at, self.total, self.bufs
        if stage == 0:
            return self.core_parts()
        some, rest = self.cuts()
        found = []
        if stage == 2:
            for k in range(1, ZS):
                pair = (at.z_peer(k), at.z_peer(ZS - k))
                z = at.z_at(k)
                found.append((total.at[:, z, at.b, some], bufs[2].at[k - 1], at.bs + k, *pair))
                slot = at.bs + ZS + k - 1
                found.append((total.at[at.x, z, :, rest], bufs[3].at[k - 1], slot, *pair))
            return found
        base = 1 if stage == 1 else at.bs + 2 * ZS - 1
        for k in range(1, at.bs):
            pair = (at.b_peer(k), at.b_peer(at.bs - k))
            if stage == 1:
                src, buf = total.at[:, :, at.b_at(k), some], bufs[0].at[k - 1]
            else:
                src, buf = total.at[at.x, at.z, at.b_at(k), rest], bufs[5].at[k - 1]
            found.append((src, buf, base + k, *pair))
        if stage == 1:
            src, buf = total.at[1 - at.x, :, :, rest], bufs[1]
        else:
            src, buf = total.at[1 - at.x, at.z, at.b, some], bufs[4]
        found.append((src, buf, base, at.x_peer, at.x_peer))
        return found

    def add(self, stage):
        at, bs = self.at, self.at.bs
        total, bufs = self.total, self.bufs
        some, rest = self.cuts()
        if stage == 0:
            self.add_core()
        elif stage == 1:

            @pl.loop(0, 2 * ZS)
            def _(i):
                x, z = i // ZS, i % ZS
                for k in range(bs - 1):
                    total[x, z, at.b, some] = total[x, z, at.b, some] + bufs[0][k, x, z]

            @pl.loop(0, ZS * bs)
            def _(i):
                z, b = i // bs, i % bs
                total[at.x, z, b, rest] = total[at.x, z, b, rest] + bufs[1][z, b]

        elif stage == 2:
            for x in range(2):
                for k in range(ZS - 1):
                    total[x, at.z, at.b, some] = total[x, at.z, at.b, some] + bufs[2][k, x]

            @pl.loop(0, bs)
            def _(b):
                for k in range(ZS - 1):
                    total[at.x, at.z, b, rest] = total[at.x, at.z, b, rest] + bufs[3][k, b]

        else:
            total[at.x, at.z, at.b, some] = total[at.x, at.z, at.b, some] + bufs[4][...]
            for k in range(bs - 1):
                total[at.x, at.z, at.b, rest] = total[at.x, at.z, at.b, rest] + bufs[5][k]
            self.final[...] = total[at.x, at.z, at.b]


HALF = 256
WIDE = 512
QKV_TILE = 768
VEC_ROWS = 16


STEP = 64


def by_rows(fn, *arrays, step=STEP):
    parts = [
        fn(*[array[at : at + step] for array in arrays])
        for at in range(0, arrays[0].shape[0], step)
    ]
    if isinstance(parts[0], tuple):
        return tuple(jnp.concatenate(part, axis=0) for part in zip(*parts))
    return jnp.concatenate(parts, axis=0)


def dot_nt(a, b):
    return lax.dot_general(a, b, (((1,), (1,)), ((), ())), preferred_element_type=jnp.float32)


def dot_nn(a, b):
    return lax.dot_general(a, b, (((1,), (0,)), ((), ())), preferred_element_type=jnp.float32)


def dot_tn(a, b):
    return lax.dot_general(a, b, (((0,), (0,)), ((), ())), preferred_element_type=jnp.float32)


def aligned(index, unit):
    return pl.multiple_of(index, unit)


def rows_of(ref, bs, first, count, start, rows, blocks=range(SECT)):
    parts = []
    for i in range(count):
        d = first + i
        place = (d // bs, d % bs)
        parts.append(
            jnp.concatenate(
                [ref[(lb,) + place + (pl.ds(start, rows), slice(None))] for lb in blocks], axis=1
            )
        )
    return parts[0] if count == 1 else jnp.concatenate(parts, axis=0)


def put_rows(ref, bs, first, count, start, rows, value, block=0):
    value = value.astype(ref.dtype)
    for i in range(count):
        d = first + i
        place = (d // bs, d % bs)
        for lane in range(value.shape[1] // LANES):
            ref[(block + lane,) + place + (pl.ds(start, rows), slice(None))] = value[
                i * rows : (i + 1) * rows, lane * LANES : (lane + 1) * LANES
            ]


def vector_pieces(dps):
    n_gains, n_biases = 2 * WIDE // dps, 10 * WIDE // dps
    starts = [(0, 0), (0, 2), (1, 0), (1, 2), (2, 0), (2, 1), (2, 2), (2, 3), (3, 0), (3, 2)]
    pieces = []
    for d in range(dps):
        at = 0
        while at < n_gains + n_biases:
            if at < n_gains:
                index = d * n_gains + at
                row, column = (1, 3)[index // WIDE], WIDE + index % WIDE
                left = n_gains - at
            else:
                index = d * n_biases + at - n_gains
                row, part = starts[index // WIDE]
                column = part * WIDE + index % WIDE
                left = n_gains + n_biases - at
            size = min(left, LANES - at % LANES, LANES - column % LANES)
            pieces.append((d, at // LANES, at % LANES, row, column, size))
            at += size
    return pieces


def read_vectors(ref, table, bs, start, block):
    tiles = {}
    for d, row, lane, to_row, to_lane, size in vector_pieces(ZS * bs):
        if d not in tiles:
            tile = ref[block, d // bs, d % bs, start : start + VEC_ROWS, :]
            tiles[d] = tile.astype(jnp.float32)
        table[to_row : to_row + 1, to_lane : to_lane + size] = tiles[d][
            row : row + 1, lane : lane + size
        ]


def rows_tile(lines):
    row_id = lax.broadcasted_iota(jnp.int32, (VEC_ROWS, LANES), 0)
    tile = jnp.zeros((VEC_ROWS, LANES), jnp.float32)
    for row, pieces in enumerate(lines):
        have = sum(piece.shape[1] for piece in pieces)
        if have < LANES:
            pieces = pieces + [jnp.zeros((1, LANES - have), jnp.float32)]
        line = pieces[0] if len(pieces) == 1 else jnp.concatenate(pieces, axis=1)
        tile = jnp.where(row_id == row, line, tile)
    return tile


def vector_tile(table, dps, place):
    lines = []
    for d, row, lane, to_row, to_lane, size in vector_pieces(dps):
        if d == place:
            if row == len(lines):
                lines.append([])
            lines[row].append(table[to_row : to_row + 1, to_lane : to_lane + size])
    return rows_tile(lines)


def fold_rows(x):
    total = x[:8]
    for at in range(8, x.shape[0], 8):
        total = total + x[at : at + 8]
    return total


def normalize(x):
    mean = jnp.mean(x, axis=1, keepdims=True)
    centred = x - mean
    scale = lax.rsqrt(jnp.mean(centred * centred, axis=1, keepdims=True) + NORM_EPS)
    return centred * scale, jnp.broadcast_to(scale, (x.shape[0], LANES))


def normalize_back(unit, scale, grad, gain):
    inner = grad * gain
    first = jnp.mean(inner, axis=1, keepdims=True)
    second = jnp.mean(inner * unit, axis=1, keepdims=True)
    out = jnp.concatenate([scale] * (WIDE // LANES), axis=1) * (inner - first - unit * second)
    return out, fold_rows(out), fold_rows(grad * unit), fold_rows(grad)


def gelu_pair(u):
    below = 0.5 + 0.5 * lax.erf(u * math.sqrt(0.5))
    bell = jnp.exp2((-0.5 * math.log2(math.e)) * (u * u))
    return u * below, below + u * (bell * (1.0 / math.sqrt(2.0 * math.pi)))


def head_masks(scale):
    lane = lax.broadcasted_iota(jnp.int32, (1, LANES), 1)
    first = jnp.where(lane < HEAD, scale, 0.0).astype(jnp.bfloat16)
    second = jnp.where(lane < HEAD, 0.0, scale).astype(jnp.bfloat16)
    return first, second


class Sizes:
    def __init__(self, dps):
        self.dps, self.bs = dps, dps // ZS
        self.qkv, self.out, self.up, self.down = (
            3 * WIDE // dps,
            WIDE // dps,
            4 * WIDE // dps,
            WIDE // dps,
        )
        self.lookback = -(-6 * WIDE // (SECT * dps) // VEC_ROWS) * VEC_ROWS
        self.emb = self.lookback + VEC_ROWS
        self.dense = self.out + self.up
        self.wide = 4 * self.down


def qkv_rows(size, w, tile):
    count = QKV_TILE // size.qkv
    return rows_of(w, size.bs, tile * count, count, 0, size.qkv)


def out_rows(size, w):
    return rows_of(w, size.bs, 0, size.dps, 0, size.out)


def up_rows(size, w, tile):
    count = HALF // size.up
    return rows_of(w, size.bs, tile * count, count, size.out, size.up)


def forward_mix(size, w, table, h, mixed, piece):
    columns = slice(piece * QKV_TILE, (piece + 1) * QKV_TILE)
    shift = table[0:1, columns]
    out = dot_nt(h[...], qkv_rows(size, w, piece))
    mixed[:, columns] = by_rows(lambda part: (part + shift).astype(mixed.dtype), out)


def softmax_columns(scores):
    parts = [scores[at : at + STEP] for at in range(0, scores.shape[0], STEP)]
    top = parts[0]
    for part in parts[1:]:
        top = jnp.maximum(top, part)
    top = jnp.max(top, axis=0, keepdims=True)
    parts = [jnp.exp(part - top) for part in parts]
    total = parts[0]
    for part in parts[1:]:
        total = total + part
    scale = 1.0 / jnp.sum(total, axis=0, keepdims=True)
    return jnp.concatenate([(part * scale).astype(jnp.bfloat16) for part in parts], axis=0)


def forward_attend(mixed, probs, attended, pair):
    lane = pair * LANES
    key_rows = mixed[:, WIDE + lane : WIDE + lane + LANES]
    values = mixed[:, 2 * WIDE + lane : 2 * WIDE + lane + LANES].T

    for part in range(2):
        rows = slice(part * HALF, (part + 1) * HALF)
        queries = mixed[rows, lane : lane + LANES]
        joined = []
        for head, mask in enumerate(head_masks(1.0 / math.sqrt(HEAD))):
            weights = softmax_columns(dot_nt(key_rows, queries * mask))
            probs[2 * pair + head, :, rows] = weights
            joined.append(dot_nn(values[head * HEAD : (head + 1) * HEAD], weights))
        joined = jnp.concatenate(joined, axis=0).T
        attended[rows, lane : lane + LANES] = joined.astype(attended.dtype)


def forward_project(size, w, table, h, attended, first, scale, normed):
    out = dot_nt(attended[...], out_rows(size, w))
    for part in range(WIDE // STEP):
        rows = slice(part * STEP, (part + 1) * STEP)
        total = h[rows, :].astype(jnp.float32) + (out[rows] + table[1:2, 0:WIDE])
        unit, scale[rows, :] = normalize(total)
        first[rows, :] = unit
        normed[rows, :] = (
            unit * table[1:2, WIDE : 2 * WIDE] + table[1:2, 2 * WIDE : 3 * WIDE]
        ).astype(normed.dtype)


def forward_up(size, w, table, normed, slope, hidden, piece):
    for j in (2 * piece, 2 * piece + 1):
        columns = slice(j * HALF, (j + 1) * HALF)
        shift = table[2:3, columns]
        upper = dot_nt(normed[...], up_rows(size, w, j))
        for part in range(WIDE // STEP):
            rows = slice(part * STEP, (part + 1) * STEP)
            value, grad = gelu_pair(upper[rows] + shift)
            hidden[rows, columns] = value.astype(hidden.dtype)
            slope[rows, columns] = grad.astype(slope.dtype)


def forward_down(size, w, table, normed, hidden, second, scale, h, piece):
    columns = slice(piece * HALF, (piece + 1) * HALF)
    count = size.dps // 2
    matrix = jnp.concatenate(
        [
            rows_of(w, size.bs, piece * count, count, j * size.down, size.down)
            for j in range(4)
        ],
        axis=1,
    )
    out = dot_nt(hidden[...], matrix)
    shift = table[3:4, columns]
    for part in range(WIDE // STEP):
        rows = slice(part * STEP, (part + 1) * STEP)
        second[rows, columns] = normed[rows, columns].astype(jnp.float32) + (out[rows] + shift)
    if piece == 1:
        for part in range(WIDE // STEP):
            rows = slice(part * STEP, (part + 1) * STEP)
            unit, scale[rows, :] = normalize(second[rows, :])
            second[rows, :] = unit
            h[rows, :] = (
                unit * table[3:4, WIDE : 2 * WIDE] + table[3:4, 2 * WIDE : 3 * WIDE]
            ).astype(h.dtype)


def backward_norm_two(table, dtable, dy, second, scale, dnormed, dlow, dlow_t):
    dtable[...] = jnp.zeros_like(dtable)
    sums = [jnp.zeros((8, WIDE), jnp.float32)] * 3
    for part in range(WIDE // STEP):
        rows = slice(part * STEP, (part + 1) * STEP)
        grad, *found = normalize_back(
            second[rows, :],
            scale[rows, :],
            dy[rows, :].astype(jnp.float32),
            table[3:4, WIDE : 2 * WIDE],
        )
        dnormed[rows, :] = grad
        dlow[rows, :] = grad.astype(dlow.dtype)
        sums = [total + new for total, new in zip(sums, found)]
    for i, total in enumerate(sums):
        dtable[3:4, i * WIDE : (i + 1) * WIDE] = jnp.sum(total, axis=0, keepdims=True)
    dlow_t[...] = dlow[...].T


def backward_down(size, grads, hidden, dlow_t, piece):
    @pl.loop(2 * piece, 2 * piece + 2)
    def _(i):
        start = aligned(i * size.down, 16)
        for half in range(2):
            columns = pl.ds(aligned(i * WIDE, WIDE) + half * HALF, HALF)
            value = dot_nn(dlow_t[...], hidden[:, columns])
            put_rows(grads, size.bs, 0, size.dps, start, size.down, value, 2 * half)


def backward_gelu(size, w, dtable, slope, dlow, dup, piece):
    @pl.loop(2 * piece, 2 * piece + 2)
    def _(i):
        start = aligned(i * size.down, 16)
        for half in range(2):
            columns = pl.ds(aligned(i * WIDE, WIDE) + half * HALF, HALF)
            blocks = (2 * half, 2 * half + 1)
            matrix = rows_of(w, size.bs, 0, size.dps, start, size.down, blocks)
            dhidden = dot_nn(dlow[...], matrix)
            total = jnp.zeros((8, HALF), jnp.float32)
            for part in range(WIDE // STEP):
                rows = slice(part * STEP, (part + 1) * STEP)
                dupper = dhidden[rows] * slope[rows, columns].astype(jnp.float32)
                total = total + fold_rows(dupper)
                dup[rows, columns] = dupper.astype(dup.dtype)
            dtable[2:3, columns] = jnp.sum(total, axis=0, keepdims=True)


def backward_up(size, grads, normed, dup):
    count = HALF // size.up

    @pl.loop(0, 4)
    def _(i):
        for half in range(2):
            columns = pl.ds(aligned(i * WIDE, WIDE) + half * HALF, HALF)
            value = dot_tn(dup[:, columns], normed[...])
            first = (2 * i + half) * count
            put_rows(grads, size.bs, first, count, size.out, size.up, value)


def backward_normed(size, w, dnormed, dup):
    for half in range(2):
        columns = slice(half * HALF, (half + 1) * HALF)
        blocks = (2 * half, 2 * half + 1)
        matrix = rows_of(w, size.bs, 0, size.dps, size.out, size.up, blocks)
        out = dot_nn(dup[...], matrix)
        for part in range(WIDE // STEP):
            rows = slice(part * STEP, (part + 1) * STEP)
            dnormed[rows, columns] = dnormed[rows, columns] + out[rows]


def backward_norm_one(
    size, w, table, grads, dtable, first, scale, attended, dnormed, dlow, dlow_t, delta
):
    sums = [jnp.zeros((8, WIDE), jnp.float32)] * 3
    for part in range(WIDE // STEP):
        rows = slice(part * STEP, (part + 1) * STEP)
        grad, *found = normalize_back(
            first[rows, :], scale[rows, :], dnormed[rows, :], table[1:2, WIDE : 2 * WIDE]
        )
        dnormed[rows, :] = grad
        dlow[rows, :] = grad.astype(dlow.dtype)
        sums = [total + new for total, new in zip(sums, found)]
    for i, total in enumerate(sums):
        dtable[1:2, i * WIDE : (i + 1) * WIDE] = jnp.sum(total, axis=0, keepdims=True)
    dlow_t[...] = dlow[...].T
    for block in (0, 2):
        columns = slice(block * LANES, (block + 2) * LANES)
        value = dot_nn(dlow_t[...], attended[:, columns])
        put_rows(grads, size.bs, 0, size.dps, 0, size.out, value, block)
    grad = dot_nn(dlow[...], out_rows(size, w)).astype(dlow.dtype)
    dlow[...] = grad
    product = grad.astype(jnp.float32) * attended[...].astype(jnp.float32)
    high = product.astype(jnp.bfloat16)
    rest = (product - high.astype(jnp.float32)).astype(jnp.bfloat16)
    head = lax.broadcasted_iota(jnp.int32, delta.shape, 0)
    lane = lax.broadcasted_iota(jnp.int32, delta.shape, 1)
    inside = (lane >= head * HEAD) & (lane < (head + 1) * HEAD)
    inside = jnp.where(inside, 1.0, 0.0).astype(jnp.bfloat16)
    delta[...] = dot_nt(inside, high) + dot_nt(inside, rest)


def backward_attend(mixed, probs, delta, dtable, dlow, dmixed, pair):
    scale = 1.0 / math.sqrt(HEAD)
    lane = pair * LANES
    columns = slice(lane, lane + LANES)
    key_columns = slice(WIDE + lane, WIDE + lane + LANES)
    value_columns = slice(2 * WIDE + lane, 2 * WIDE + lane + LANES)
    keys_t = mixed[:, key_columns].T
    values = mixed[:, value_columns]
    dkeys = jnp.zeros((WIDE, LANES), jnp.float32)
    dvalues = jnp.zeros((WIDE, LANES), jnp.float32)
    for part in range(2):
        rows = slice(part * HALF, (part + 1) * HALF)
        queries = mixed[rows, columns]
        grad_out = dlow[rows, columns]
        dqueries = []
        for head in range(2):
            query = queries * head_masks(scale)[head]
            grad = grad_out * head_masks(1.0)[head]
            at = 2 * pair + head
            weights = probs[at, :, rows]
            less = delta[at : at + 1, rows]
            dprobs = dot_nt(values, grad)
            dscores = by_rows(
                lambda p, dp: (p.astype(jnp.float32) * (dp - less)).astype(jnp.bfloat16),
                weights,
                dprobs,
            )
            dvalues = dvalues + dot_nn(weights, grad)
            dkeys = dkeys + dot_nn(dscores, query)
            dqueries.append(dot_nn(keys_t[head * HEAD : (head + 1) * HEAD], dscores))
        dquery = jnp.concatenate(dqueries, axis=0).T * scale
        dtable[0:1, columns] += jnp.sum(dquery, axis=0, keepdims=True)
        dmixed[rows, columns] = dquery.astype(dmixed.dtype)
    dmixed[:, key_columns] = dkeys.astype(dmixed.dtype)
    dmixed[:, value_columns] = dvalues.astype(dmixed.dtype)
    dtable[0:1, value_columns] = jnp.sum(dvalues, axis=0, keepdims=True)


def backward_mix(size, grads, h, dmixed, piece):
    count = QKV_TILE // size.qkv
    grad = dmixed[:, piece * QKV_TILE : (piece + 1) * QKV_TILE]
    put_rows(grads, size.bs, piece * count, count, 0, size.qkv, dot_tn(grad, h[...]))


def backward_input(size, w, dnormed, dmixed, dy):
    for half in range(2):
        columns = slice(half * HALF, (half + 1) * HALF)
        blocks = (2 * half, 2 * half + 1)
        matrix = rows_of(w, size.bs, 0, size.dps, 0, size.qkv, blocks)
        out = dot_nn(dmixed[...], matrix)
        for part in range(WIDE // STEP):
            rows = slice(part * STEP, (part + 1) * STEP)
            dy[rows, columns] = (dnormed[rows, columns] + out[rows]).astype(dy.dtype)


WINDOW = 384


def group_rows(group):
    rows = lax.broadcasted_iota(jnp.int32, (16, LANES), 0)
    return jnp.where(rows == group, 1.0, 0.0)


def pack_mix(piece, qkv):
    for lb in range(SECT):
        piece[lb] = qkv[:, lb * LANES : (lb + 1) * LANES].astype(piece.dtype)


def pack_up(piece, out, up):
    rows = out.shape[0]
    for lb in range(SECT):
        lanes = slice(lb * LANES, (lb + 1) * LANES)
        piece[lb, :rows] = out[:, lanes].astype(piece.dtype)
        piece[lb, rows:] = up[:, lanes].astype(piece.dtype)


def pack_down(piece, down):
    rows = down.shape[0]
    for lb in range(SECT):
        for j in range(4):
            start = j * WIDE + lb * LANES
            piece[lb, j * rows : (j + 1) * rows] = down[:, start : start + LANES].astype(piece.dtype)


def pack_embedding(piece, weight, shift, gains, biases, square, block):
    n = weight.shape[0]
    square[...] = jnp.zeros_like(square)
    square[:GROUPS, :n] = shift[...]

    def ending(part, width):
        return jnp.concatenate([jnp.zeros((n, width - part.shape[1]), part.dtype), part], axis=1)

    third = ending(weight[:, L1 + L2 :], 3 * LANES)
    second = ending(weight[:, L1 : L1 + L2], 2 * LANES)
    blocks = [third[:, :LANES] + square[...].T[:n]]
    blocks += [third[:, LANES : 2 * LANES], third[:, 2 * LANES :]]
    blocks += [second[:, :LANES], second[:, LANES:], ending(weight[:, :L1], LANES)]
    rows = piece.shape[1] - VEC_ROWS
    if SECT * rows > 6 * n:
        blocks.append(jnp.zeros((SECT * rows - 6 * n, LANES), jnp.float32))
    flat = jnp.concatenate(blocks, axis=0).astype(piece.dtype)
    for lb in range(SECT):
        piece[lb, :rows] = flat[lb * rows : (lb + 1) * rows]
    line = jnp.concatenate([gains[...], biases[...]], axis=1)
    lines = [[line[:, at : at + LANES]] for at in range(0, line.shape[1], LANES)]
    piece[block, rows:] = rows_tile(lines).astype(piece.dtype)


def expand(series, group, x):
    empty = jnp.zeros((WINDOW - series.shape[0], series.shape[1]), series.dtype)
    x[:, :WINDOW] = jnp.concatenate([empty, series[...]], axis=0).T
    lane = lax.broadcasted_iota(jnp.int32, (x.shape[0], LANES), 1)
    x[:, WINDOW:] = jnp.where(lane == group, 1.0, 0.0).astype(x.dtype)


def embed(size, emb, pick, x, wsel, h):
    n = WIDE // size.dps
    flat = []
    for d in range(size.dps):
        place = (d // size.bs, d % size.bs, slice(0, size.lookback), slice(None))
        flat.append(jnp.concatenate([emb[(lb,) + place] for lb in range(SECT)], axis=0))
    blocks = [
        jnp.concatenate([rows[j * n : (j + 1) * n] for rows in flat], axis=0) for j in range(6)
    ]
    parts = [block.astype(jnp.float32) for block in blocks]
    long, middle, short = (pick[g : g + 1, :] for g in (2, 1, 0))
    wide = jnp.concatenate(
        [
            parts[0] * long,
            parts[1] * long + parts[3] * middle,
            parts[2] * long + parts[4] * middle + parts[5] * short,
        ],
        axis=1,
    ).astype(jnp.bfloat16)
    wsel[...] = wide.T
    h[...] = dot_nt(x[...], jnp.concatenate([wide, blocks[0]], axis=1)).astype(h.dtype)


def embed_back(size, pick, x, wsel, dh, tables, grads, series_grad):
    history = series_grad.shape[0]
    series_grad[...] = dot_nt(wsel[...], dh[...])[WINDOW - history :]
    sums = dot_tn(dh[...], x[...])
    long, middle, short = (pick[g : g + 1, :] for g in (2, 1, 0))
    parts = [sums[:, i * LANES : (i + 1) * LANES] for i in range(4)]
    parts = [
        parts[0] * long + parts[3],
        parts[1] * long,
        parts[2] * long,
        parts[1] * middle,
        parts[2] * middle,
        parts[2] * short,
    ]
    rows = WIDE // (SECT * size.dps)
    spare = size.lookback - 6 * rows
    for pipe in range(SECT):
        block = (pipe % 2) * 2 + pipe // 2
        for dp in range(size.dps):
            start = (pipe * size.dps + dp) * rows
            pieces = [part[start : start + rows] for part in parts]
            if spare:
                pieces.append(jnp.zeros((spare, LANES), jnp.float32))
            pieces.append(vector_tile(tables.at[pipe], size.dps, dp))
            piece = jnp.concatenate(pieces, axis=0)
            grads[block, dp // size.bs, dp % size.bs] = piece.astype(grads.dtype)


def saved_shapes():
    low, wide = jnp.bfloat16, jnp.float32
    return [
        ((WIDE, WIDE), low),
        ((WIDE, 3 * WIDE), low),
        ((2 * SECT, WIDE, WIDE), low),
        ((WIDE, WIDE), low),
        ((WIDE, WIDE), wide),
        ((WIDE, WIDE), low),
        ((WIDE, 4 * WIDE), low),
        ((WIDE, 4 * WIDE), low),
        ((WIDE, WIDE), wide),
        ((SECT, 4 * WIDE), wide),
        ((WIDE, LANES), wide),
        ((WIDE, LANES), wide),
    ]


def chunk_shape(size, rows):
    return (SECT, ZS, size.bs, rows, LANES)


HALVES = (2, 2, 2, 2)
CROSS = (2,)


def follow(plan, section, act, compute):
    seen = {}
    for step in plan:
        if len(step) == 1:
            piece = seen.get(step[0], 0)
            seen[step[0]] = piece + 1
            compute(step[0], piece)
            continue
        op, kind, offset = step
        where = section + offset
        if isinstance(where, int):
            if 0 <= where < SECT:
                act(op, kind, where)
        elif offset == 0:
            act(op, kind, where)
        else:
            inside = where < SECT if offset > 0 else where >= 0

            @pl.when(inside)
            def _():
                act(op, kind, where)


def forward_kernel(dps, groups, *refs):
    size = Sizes(dps)
    given, refs = refs[:9], refs[9:]
    out, copies_out, wsel, x, refs = refs[0], refs[1:4], refs[4], refs[5], refs[6:]
    kept, local, refs = refs[:12], refs[12:24], refs[24:]
    wholes, refs = refs[:4], refs[4:]
    pieces, held, refs = refs[:4], refs[4:13], refs[13:]
    emb_rows, pick, refs = refs[0], refs[1], refs[2:]
    given_sem, out_sem, kept_sem, own_sem, p_send, p_recv, send, recv = refs
    h, mixed, probs, attended, first, normed, slope, hidden, second, table, scale_1, scale_2 = local
    at = Place(dps)

    own = [
        pltpu.make_async_copy(
            pieces[kind].at[at.block],
            wholes[kind].at[at.pipe, at.block, at.z, at.b]
            if kind < EMB
            else wholes[kind].at[at.block, at.z, at.b],
            own_sem.at[kind],
        )
        for kind in range(4)
    ]
    def split(kind, back):
        copies = []
        for k in range(1, SECT):
            if back:
                region = wholes[kind].at[at.pipe_at(SECT - k), at.block, at.z, at.b]
                src = region
            else:
                block = at.blocks[k]
                region = wholes[kind].at[at.pipe, block, at.z, at.b]
                src = pieces[kind].at[block]
            sems = p_send.at[kind, k - 1], p_recv.at[kind, k - 1]
            copies.append(remote(src, region, *sems, (at.pipe_at(k), at.dp)))
        return copies

    def chunk(kind, section):
        if kind == EMB:
            return Spread(at, wholes[kind], send.at[3 * SECT], recv.at[3 * SECT])
        number = 3 * section + kind
        sort = SpreadCross if kind in CROSS else Spread
        return sort(at, wholes[kind].at[section], send.at[number], recv.at[number], HALVES[kind])

    def keep(kind, section):
        src, dst = wholes[kind].at[section], copies_out[kind].at[section]
        return pltpu.make_async_copy(src, dst, out_sem.at[kind, section])

    arrived = []

    def act(op, kind, section):
        if op == 0:
            if kind not in arrived:
                arrived.append(kind)
                own[kind].wait()
                if kind == EMB:
                    chunk(kind, section).start(0)
                    return
                for copy in split(kind, True):
                    copy.wait_recv()
                for copy in split(kind, False):
                    copy.wait_send()
                if kind == 0:
                    copies_start(split(1, False))
                    copies_start(split(2, False))
            chunk(kind, section).start(0)
        elif op < 4:
            chunk(kind, section).move(op - 1)
            if op == 1 and kind == EMB:
                gets[0].wait()
                expand(series, groups[0], x)
        else:
            chunk(kind, section).land(3)
            if kind != EMB:
                keep(kind, section).start(priority=1)

    def saves(section, early):
        which = (1, 2, 3, 4, 5, 9, 10) if early else (6, 7, 8, 11)
        return [
            pltpu.make_async_copy(local[i], kept[i].at[section], kept_sem.at[i]) for i in which
        ]

    series, embed_weight, embed_bias, qkv, out_w, up_w, down_w, gains, biases = held
    gets = copies_of(zip(given, held), given_sem)
    for i in (3, 7, 8, 1, 2, 4, 5, 6, 0):
        gets[i].start(priority=1)
    pick[...] = group_rows(groups[0])
    at.greet()
    gets[3].wait()
    pack_mix(pieces[0], qkv)
    own[0].start(priority=1)
    at.met()
    copies_start(split(0, False))
    copies_wait(gets[1:3] + gets[7:9])
    pack_embedding(
        pieces[EMB], embed_weight, embed_bias, gains, biases, emb_rows, at.block
    )
    own[EMB].start(priority=1)
    copies_wait(gets[4:7])
    pack_up(pieces[1], out_w, up_w)
    own[1].start(priority=1)
    pack_down(pieces[2], down_w)
    own[2].start(priority=1)
    table[...] = jnp.zeros_like(table)

    def before(name, piece):
        embed(size, wholes[EMB], pick, x, wsel, h)

    follow(FORWARD_START, 0, act, before)

    @pl.loop(0, SECT)
    def _(section):
        att, up, down = (ref.at[section] for ref in wholes[:3])
        keep_h = pltpu.make_async_copy(h, kept[0].at[section], kept_sem.at[0])

        def compute(name, piece):
            if name == "mix":
                if piece == 0:

                    @pl.when(section > 0)
                    def _():
                        copies_wait(saves(section - 1, True))

                    keep_h.start(priority=1)
                    block = section % 2 * 2 + section // 2
                    read_vectors(wholes[EMB], table, size.bs, size.lookback, block)
                forward_mix(size, att, table, h, mixed, piece)
            elif name == "attend":
                forward_attend(mixed, probs, attended, piece)
            elif name == "project":
                forward_project(size, up, table, h, attended, first, scale_1, normed)
                copies_begin(saves(section, True))
            elif name == "up":
                if piece == 0:

                    @pl.when(section > 0)
                    def _():
                        copies_wait(saves(section - 1, False))

                forward_up(size, up, table, normed, slope, hidden, piece)
            else:
                if piece == 0:
                    keep_h.wait()
                forward_down(size, down, table, normed, hidden, second, scale_2, h, piece)
                if piece == 1:
                    copies_begin(saves(section, False))

        follow(FORWARD_PERIOD, section, act, compute)

    out[...] = h[...]
    copies_wait(saves(SECT - 1, True))
    copies_wait(saves(SECT - 1, False))
    for kind in range(3):
        copies_wait([keep(kind, section) for section in range(SECT)])


def copies_of(pairs, sems):
    return [pltpu.make_async_copy(src, dst, sems.at[i]) for i, (src, dst) in enumerate(pairs)]


def forward_all(groups, given, dps):
    size = Sizes(dps)
    low, wide = jnp.bfloat16, jnp.float32
    shapes = saved_shapes()
    rows = (size.qkv, size.dense, size.wide, size.emb)
    chunks = [chunk_shape(size, count) for count in rows]
    anywhere = pl.BlockSpec(memory_space=pl.ANY)
    inside = pl.BlockSpec(memory_space=pltpu.VMEM)
    outs = [((WIDE, WIDE), low)]
    outs += [((SECT,) + shape, low) for shape in chunks[:3]]
    outs += [((WINDOW, WIDE), low), ((WIDE, WIDE), low)]
    outs += [((SECT,) + shape, dtype) for shape, dtype in shapes]
    scratch = shapes + [((SECT,) + shape, low) for shape in chunks[:3]] + [(chunks[3], low)]
    scratch += [((SECT, count, LANES), low) for count in rows]
    scratch += [(array.shape, array.dtype) for array in given]
    scratch += [((LANES, LANES), wide), ((16, LANES), wide)]
    slots = max(Spread.slots(size.bs), SpreadCross.slots(size.bs))
    dma = pltpu.SemaphoreType.DMA
    return pl.pallas_call(
        partial(forward_kernel, dps),
        out_shape=[jax.ShapeDtypeStruct(shape, dtype) for shape, dtype in outs],
        in_specs=[pl.BlockSpec(memory_space=pltpu.SMEM)] + [anywhere] * len(given),
        out_specs=[inside] + [anywhere] * 3 + [inside] * 2 + [anywhere] * len(shapes),
        scratch_shapes=[pltpu.VMEM(shape, dtype) for shape, dtype in scratch]
        + [
            dma((len(given),)),
            dma((3, SECT)),
            dma((len(shapes),)),
            dma((4,)),
            dma((3, SECT - 1)),
            dma((3, SECT - 1)),
            dma((1 + 3 * SECT, slots)),
            dma((1 + 3 * SECT, slots)),
        ],
        compiler_params=pltpu.CompilerParams(
            collective_id=0, has_side_effects=True, vmem_limit_bytes=60 * 1024 * 1024
        ),
        name="gather_forward",
    )(groups, *given)


FETCHES = {
    ("norm2", 0): (("second", "scale_2"), ("second", "scale_2")),
    ("down", 0): (("hidden",), ()),
    ("down", 1): ((), ("hidden",)),
    ("gelu", 0): (("slope", 2), ()),
    ("gelu", 1): ((), ("slope", 2)),
    ("up", 0): (("normed",), ("normed",)),
    ("normed", 0): ((1,), ()),
    ("norm1", 0): (("first", "scale_1", "attended"), ("first", "scale_1", "attended", 1)),
    ("attend", 0): (("mixed", "probs"), ()),
    ("attend", 3): ((), ("mixed", "probs")),
    ("mix", 0): (("h",), ()),
    ("mix", 1): ((), ("h",)),
    ("input", 0): ((0,), (0,)),
}


def backward_kernel(dps, groups, att, up, down, cotangent, x_in, wsel_in, *refs):
    size = Sizes(dps)
    kept, refs = refs[:12], refs[12:]
    series_grad, outs, refs = refs[0], refs[1:5], refs[5:]
    local, refs = refs[:11], refs[11:]
    tables, w_att, w_up, w_down, dtables, dy, dnormed, dlow, dlow_t, dmixed, dup = refs[:11]
    x, wsel, pick, delta, refs = *refs[11:15], refs[15:]
    kinds = []
    for kind in range(4):
        count = 6 if kind in CROSS else 5
        kinds.append(refs[:4] + (refs[4 : 4 + count],))
        refs = refs[4 + count :]
    w_sem, kept_sem, table_sem, late_sem, out_sem, p_send, p_recv, send, recv, credit = refs
    h, mixed, probs, attended, first, normed, slope, hidden, second, scale_1, scale_2 = local
    at = Place(dps)
    last = SECT - 1

    def weights(kind, section):
        src, dst = ((att, w_att), (up, w_up), (down, w_down))[kind]
        return pltpu.make_async_copy(src.at[section], dst, w_sem.at[kind])

    names = ("h", "mixed", "probs", "attended", "first", "normed", "slope", "hidden", "second")
    names += ("table", "scale_1", "scale_2")
    held = dict(zip(names[:9] + names[10:], local))

    def fetches(section, *wanted):
        found = []
        for name in wanted:
            if isinstance(name, int):
                found.append(weights(name, section))
            else:
                i = names.index(name)
                dst = held[name]
                found.append(pltpu.make_async_copy(kept[i].at[section], dst, kept_sem.at[i]))
        return found

    def chunk(kind, i):
        grads, totals, finals, landing, bufs = kinds[kind]
        sort = FoldCross if kind in CROSS else Fold
        refs = (grads, totals.at[i % 2], landing, bufs, finals.at[i])
        return sort(at, *refs, send.at[kind], recv.at[kind], credit.at[kind], HALVES[kind])

    def hand_over(kind, i):
        landing = outs[kind].at[at.block]
        final = kinds[kind][2].at[i]
        return (
            pltpu.make_async_copy(final, landing, out_sem.at[kind]),
            remote(final, landing, p_send.at[kind, i], p_recv.at[kind, at.pipe], (last - i, at.dp)),
        )

    def act(op, kind, i):
        again, more = (False, False) if kind == EMB else (i > 0, i < last)
        if op == 0:
            chunk(kind, i).start(0, again)
        elif op < 4:
            chunk(kind, i).move(op - 1, again, more)
        else:
            chunk(kind, i).land(3, more)
            if kind == EMB:
                outs[kind][...] = kinds[kind][2][0]
            else:
                here, away = hand_over(kind, i)

                @pl.when(at.pipe == last - i)
                def _():
                    here.start(priority=1)

                @pl.when(at.pipe != last - i)
                def _():
                    away.start()

    at.greet()
    get_tables = pltpu.make_async_copy(kept[9], tables, table_sem)
    late = copies_of(((cotangent, dy), (x_in, x), (wsel_in, wsel)), late_sem)
    copies_begin([late[0], get_tables] + fetches(last, "second", "scale_2", "hidden"))
    copies_begin(fetches(last, "slope", 2, "normed", 1, "first", "scale_1", "attended"))
    copies_begin(fetches(last, "mixed", "probs", "h", 0) + late[1:])
    pick[...] = group_rows(groups[0])
    copies_wait([late[0], get_tables])

    @pl.loop(0, SECT)
    def _(i):
        section = last - i
        table, dtable = tables.at[section], dtables.at[section]

        def compute(name, piece):
            need, free = FETCHES.get((name, piece), ((), ()))
            copies_wait(fetches(section, *need))
            if name == "norm2":
                backward_norm_two(table, dtable, dy, second, scale_2, dnormed, dlow, dlow_t)
                pl.when(i == 0)(at.met)
            elif name == "down":
                backward_down(size, kinds[2][0], hidden, dlow_t, piece)
            elif name == "gelu":
                backward_gelu(size, w_down, dtable, slope, dlow, dup, piece)
            elif name == "up":
                backward_up(size, kinds[1][0], normed, dup)
            elif name == "normed":
                backward_normed(size, w_up, dnormed, dup)
            elif name == "norm1":
                backward_norm_one(
                    size,
                    w_up,
                    table,
                    kinds[1][0],
                    dtable,
                    first,
                    scale_1,
                    attended,
                    dnormed,
                    dlow,
                    dlow_t,
                    delta,
                )
            elif name == "attend":
                backward_attend(mixed, probs, delta, dtable, dlow, dmixed, piece)
            elif name == "mix":
                backward_mix(size, kinds[0][0], h, dmixed, piece)
            else:
                backward_input(size, w_att, dnormed, dmixed, dy)
            if free:

                @pl.when(section > 0)
                def _():
                    copies_begin(fetches(section - 1, *free))

        follow(BACKWARD_PERIOD, i, act, compute)

    def after(name, piece):
        copies_wait(late[1:])
        embed_back(size, pick, x, wsel, dy, dtables, kinds[EMB][0], series_grad)

    follow(BACKWARD_END, 0, act, after)

    for kind in range(3):
        for i in range(SECT):
            here, away = hand_over(kind, i)

            @pl.when(at.pipe == last - i)
            def _():
                here.wait()

            @pl.when(at.pipe != last - i)
            def _():
                away.wait_send()

        for k in range(1, SECT):
            other = at.pipe_at(k)
            landing = outs[kind].at[at.blocks[k]]
            sems = p_send.at[kind, 0], p_recv.at[kind, other]
            remote(landing, landing, *sems, (other, at.dp)).wait_recv()


def backward_all(groups, weights, cotangent, x, wsel, kept, history, dps):
    size = Sizes(dps)
    low, wide = jnp.bfloat16, jnp.float32
    anywhere = pl.BlockSpec(memory_space=pl.ANY)
    inside = pl.BlockSpec(memory_space=pltpu.VMEM)
    shapes = saved_shapes()
    kind_rows = (size.qkv, size.dense, size.wide, size.emb)
    scratch = shapes[:9] + shapes[10:] + [((SECT,) + shapes[9][0], wide)]
    scratch += [(chunk_shape(size, rows), low) for rows in kind_rows[:3]]
    scratch += [
        ((SECT,) + shapes[9][0], wide),
        ((WIDE, WIDE), low),
        ((WIDE, WIDE), wide),
        ((WIDE, WIDE), low),
        ((WIDE, WIDE), low),
        ((WIDE, 3 * WIDE), low),
        ((WIDE, 4 * WIDE), low),
        ((WIDE, WIDE), low),
        ((WINDOW, WIDE), low),
        ((16, LANES), wide),
        ((16, WIDE), wide),
    ]
    for kind, rows in enumerate(kind_rows):
        sets, results = (1, 1) if kind == EMB else (2, SECT)
        scratch += [
            (chunk_shape(size, rows), low),
            ((sets, 2, ZS, size.bs, rows, LANES), low),
            ((results, rows, LANES), low),
            ((2, ZS, size.bs, rows, LANES), low),
        ]
        sort = FoldCross if kind in CROSS else Fold
        scratch += [(shape, low) for shape in sort.buffers(size.bs, rows, HALVES[kind])]
    slots = max(Fold.slots(size.bs), FoldCross.slots(size.bs))
    dma = pltpu.SemaphoreType.DMA
    return pl.pallas_call(
        partial(backward_kernel, dps),
        out_shape=[jax.ShapeDtypeStruct((history, WIDE), wide)]
        + [jax.ShapeDtypeStruct((SECT, rows, LANES), low) for rows in kind_rows[:3]]
        + [jax.ShapeDtypeStruct((size.emb, LANES), low)],
        in_specs=[pl.BlockSpec(memory_space=pltpu.SMEM)] + [anywhere] * (6 + len(kept)),
        out_specs=[inside] + [anywhere] * 3 + [inside],
        scratch_shapes=[pltpu.VMEM(shape, dtype) for shape, dtype in scratch]
        + [
            dma((3,)),
            dma((12,)),
            dma(()),
            dma((3,)),
            dma((3,)),
            dma((3, SECT)),
            dma((3, SECT)),
            dma((4, slots)),
            dma((4, slots)),
            pltpu.SemaphoreType.REGULAR((4, slots)),
        ],
        compiler_params=pltpu.CompilerParams(
            collective_id=1, has_side_effects=True, vmem_limit_bytes=60 * 1024 * 1024
        ),
        name="backward_fold",
    )(groups, *weights, cotangent, x, wsel, *kept)


def finish_kernel(dps, n_gains, n_biases, *refs):
    size = Sizes(dps)
    given, refs = refs[:6], refs[6:]
    block_out, series_out, embed_w, embed_b, qkv, out, up_out, down_out, gains, biases = refs[:10]
    att, up, down, emb, sems = refs[10:]
    copies = copies_of(zip(given, (att, up, down, emb, block_out, series_out)), sems)
    copies_start(copies)
    copies_wait(copies[:4])
    for lb in range(SECT):
        lanes = slice(lb * LANES, (lb + 1) * LANES)
        qkv[:, lanes] = att[lb].astype(jnp.float32)
        out[:, lanes] = up[lb, : size.out].astype(jnp.float32)
        up_out[:, lanes] = up[lb, size.out :].astype(jnp.float32)
        for j in range(4):
            rows = slice(j * size.down, (j + 1) * size.down)
            start = j * WIDE + lb * LANES
            down_out[:, start : start + LANES] = down[lb, rows].astype(jnp.float32)
    vectors = emb[size.lookback :].astype(jnp.float32)
    count = -(-(n_gains + n_biases) // LANES)
    flat = jnp.concatenate([vectors[row : row + 1] for row in range(count)], axis=1)
    gains[...] = flat[:, :n_gains]
    biases[...] = flat[:, n_gains : n_gains + n_biases]
    rows = WIDE // (SECT * dps)
    packed = emb[: size.lookback].astype(jnp.float32)
    packed = [packed[i * rows : (i + 1) * rows] for i in range(6)]
    square = jnp.concatenate([packed[0], jnp.zeros((LANES - rows, LANES), jnp.float32)], axis=0)
    embed_b[...] = square.T[:GROUPS, :rows]
    packed = jnp.concatenate(packed, axis=1)
    ends = ((6 * LANES, L1), (5 * LANES, L2), (3 * LANES, L3))
    embed_w[...] = jnp.concatenate([packed[:, end - span : end] for end, span in ends], axis=1)
    copies_wait(copies[4:])


def finish_all(sums, block, series, n_gains, n_biases, dps):
    size = Sizes(dps)
    wide = jnp.float32
    columns = WIDE // (SECT * dps)
    outs = [
        (block.shape, block.dtype),
        (series.shape, wide),
        ((columns, L1 + L2 + L3), wide),
        ((GROUPS, columns), wide),
        ((size.qkv, WIDE), wide),
        ((size.out, WIDE), wide),
        ((size.up, WIDE), wide),
        ((size.down, 4 * WIDE), wide),
        ((1, n_gains), wide),
        ((1, n_biases), wide),
    ]
    anywhere = pl.BlockSpec(memory_space=pl.ANY)
    inside = pl.BlockSpec(memory_space=pltpu.VMEM)
    return pl.pallas_call(
        partial(finish_kernel, dps, n_gains, n_biases),
        out_shape=[jax.ShapeDtypeStruct(shape, dtype) for shape, dtype in outs],
        in_specs=[anywhere] * 6,
        out_specs=[inside] * 10,
        scratch_shapes=[pltpu.VMEM(array.shape, array.dtype) for array in sums]
        + [pltpu.SemaphoreType.DMA((6,))],
        compiler_params=pltpu.CompilerParams(vmem_limit_bytes=60 * 1024 * 1024),
        name="finish",
    )(*sums, block, series)


def per_device(
    series,
    groups,
    cotangent,
    embed_weight,
    embed_bias,
    qkv_weight,
    out_weight,
    up_weight,
    down_weight,
    gains,
    biases,
):
    dps = lax.axis_size("dp")
    given = (
        series[0],
        embed_weight.T,
        embed_bias,
        qkv_weight[0],
        out_weight[0],
        up_weight[0],
        down_weight[0],
        gains,
        biases,
    )
    block_output, att, up, down, wsel, x, *kept = forward_all(groups, given, dps)
    series_grad, *sums = backward_all(
        groups, (att, up, down), cotangent[0], x, wsel, kept, series.shape[1], dps
    )
    outs = finish_all(sums, block_output, series_grad, gains.shape[1], biases.shape[1], dps)
    block_output, series_grad, embed_w, embed_b, qkv, out, up, down, gain_sum, bias_sum = outs
    return (
        block_output[None],
        series_grad[None],
        embed_w.T,
        embed_b,
        qkv[None],
        out[None],
        up[None],
        down[None],
        gain_sum,
        bias_sum,
    )


def solution(mesh):
    return jax.shard_map(
        per_device,
        mesh=mesh,
        in_specs=(
            P(("pipe", "dp"), None, None),
            P(("pipe", "dp")),
            P(("pipe", "dp"), None, None),
            P(None, "dp"),
            P(None, "dp"),
            P("pipe", "dp", None),
            P("pipe", "dp", None),
            P("pipe", "dp", None),
            P("pipe", "dp", None),
            P("pipe", "dp"),
            P("pipe", "dp"),
        ),
        out_specs=(
            P(("pipe", "dp"), None, None),
            P(("pipe", "dp"), None, None),
            P(None, ("pipe", "dp")),
            P(None, ("pipe", "dp")),
            P("pipe", "dp", None),
            P("pipe", "dp", None),
            P("pipe", "dp", None),
            P("pipe", "dp", None),
            P("pipe", "dp"),
            P("pipe", "dp"),
        ),
        check_vma=False,
    )
```
